32 devices in a mesh: batch: 8 (over z, y), tensor: 4 (over x, core).
Axes of the slice: x: 2, y: 2, z: 4, core: 2. Of those that a mesh axis runs over, the one named last changes fastest.
Arguments:
- features: bfloat16 [8, 24, 24, 1024], P('batch', None, None, 'tensor'), may hold values from -6 to 6
- labels: int32 [8, 24, 24], P('batch'), may hold values from 0 to 149
- valid: int32 [8, 24, 24], P('batch'), may hold values 0 or 1
- sizes: int32 [8, 2], P('batch'), may hold values from 12 to 24, as said below
- params: float32 [4, 7897088], P('tensor', 'batch'), as said below
- first_moment: float32 [4, 7897088], P('tensor', 'batch'), may hold values from -5e-05 to 5e-05
- squared_mean: float32 [4, 7897088], P('tensor', 'batch'), may hold values from 8e-11 to 3.2e-10
- average: float32 [4, 7897088], P('tensor', 'batch')
Outputs:
- new_params: float32 [4, 7897088], P('tensor', 'batch')
- new_first: float32 [4, 7897088], P('tensor', 'batch')
- new_second: float32 [4, 7897088], P('tensor', 'batch')
- new_average: float32 [4, 7897088], P('tensor', 'batch')
- param_copy: bfloat16 [4, 7897088], P('tensor', 'batch')
- grad_norm: float32 [], replicated
- loss_sum: float32 [], replicated
- loss_weight: float32 [], replicated
- unite_shift_grad: float32 [512], P('tensor')
The draws below stay inside these ranges and needn't reach their ends.
Inputs may be any that keep to these rules, and one draw needn't show every extreme that they name: `sizes`: every image spans at least half the map in each direction, and some image fills the whole map. `params`: gammas lie near one and are positive.
All inputs are finite; a program needn't handle non-finite values. No bound on the sum of `valid` on one device may be relied on, other than what follows from the above.
Results may differ from the reference program's by a relative error of at most 0.028.
Values may be sent and summed in bfloat16 or wider, within the bound.
A program may use at most 256 MiB of HBM per device.

```python
import math
import jax
import jax.numpy as jnp
from jax import lax

C_IN = 1024
MID = 512
C_OUT = 2048
PPM = 512
AUXW = 256
NCLS = 150
MAP = 24
STEP = 3
IMAGES = 8
FLAT = 7897088
N_BATCH = 8
N_TENSOR = 4


def field_scales():
    splits = N_TENSOR
    shapes = [(C_IN, MID // splits), (C_IN, C_OUT // splits), (9, MID, MID // splits), (MID, C_OUT // splits), (4, C_OUT // splits, PPM), (9, C_OUT + 4 * PPM, PPM // splits), (PPM // splits, NCLS), (9, C_IN, AUXW // splits), (AUXW // splits, NCLS)]
    fans = [C_IN, C_IN, 9 * MID, MID, C_OUT, 9 * (C_OUT + 4 * PPM), PPM, 9 * C_IN, AUXW]
    scales = []
    offsets = []
    for shape, fan in zip(shapes, fans):
        count = 1
        for extent in shape:
            count = count * extent
        count = count // N_BATCH
        scales.append(jnp.full((N_BATCH, count), fan ** (-0.5), jnp.float32))
        offsets.append(jnp.zeros((N_BATCH, count), jnp.float32))
    gain_count = (2 * MID + 2 * C_OUT + 5 * PPM + AUXW) // splits
    place = jnp.arange(2 * gain_count, dtype=jnp.int32).reshape(N_BATCH, -1)
    scales.append(jnp.where(place < gain_count, 0.1, 0.3).astype(jnp.float32))
    offsets.append(jnp.where(place < gain_count, 1.0, 0.0).astype(jnp.float32))
    return (jnp.concatenate(scales, axis=1), jnp.concatenate(offsets, axis=1))


def shaped(noise):
    scales, offsets = field_scales()
    values = noise.reshape(N_TENSOR, N_BATCH, -1) * scales[None] + offsets[None]
    return values.reshape(N_TENSOR, -1)


def draw_params(key, part):
    key = jax.random.fold_in(key, 11)
    noise = jnp.clip(jax.random.normal(key, (N_TENSOR, FLAT), jnp.float32), -4.0, 4.0)
    return shaped(noise)


def draw_average(key, part):
    key = jax.random.fold_in(key, 12)
    noise = jnp.clip(jax.random.normal(key, (N_TENSOR, FLAT), jnp.float32), -4.0, 4.0)
    return shaped(noise) * (1.0 - 0.999 ** STEP)


def draw_sizes(key, part):
    key = jax.random.fold_in(key, 13)
    values = jax.random.randint(key, (IMAGES, 2), MAP // 2, MAP + 1)
    return values.at[0].set(MAP)


def set_ends(entries, key, least, top_value):
    spot = [jax.random.randint(jax.random.fold_in(key, axis), (), 0, length) for axis, length in enumerate(entries.shape)]
    longest = entries.shape.index(max(entries.shape))
    neighbour = spot[:longest] + [(spot[longest] + 1) % entries.shape[longest]] + spot[longest + 1:]
    return entries.at[tuple(spot)].set(least).at[tuple(neighbour)].set(top_value)


def levels(own_key, dims, cuts, smallest, top_value):
    gain, own = 1.0, jax.random.fold_in(own_key, 6)
    for dim, shards_of in cuts:
        draws = jnp.exp(jax.random.uniform(jax.random.fold_in(own, dim), (shards_of,), jnp.float32, smallest / len(cuts), top_value / len(cuts)))
        gain = gain * jnp.repeat(draws, dims[dim] // shards_of).reshape([-1 if axis == dim else 1 for axis in range(len(dims))])
    return gain


def bell_draw(rng, shape, scale, limit, split=(), kind=jnp.bfloat16):
    values = scale * jax.random.normal(rng, shape, jnp.float32)
    if split:
        values = values * levels(rng, shape, split, -0.22, 0.18)
    return jnp.clip(values, -limit, limit).astype(kind)


def setup_inputs(seed: int = 0) -> dict:
    key_list = jax.random.split(jax.random.key(seed), 9)
    features = bell_draw(key_list[0], (IMAGES, MAP, MAP, C_IN), 1.0, 6.0, ((0, 8), (3, 4)))
    labels = set_ends(jax.random.randint(key_list[1], (IMAGES, MAP, MAP), 0, NCLS), jax.random.fold_in(key_list[1], 1), 0, NCLS - 1).astype(jnp.int32)
    valid = set_ends((jax.random.randint(key_list[2], (IMAGES, MAP, MAP), 0, 10) < 9).astype(jnp.int32), jax.random.fold_in(key_list[2], 1), 0, 1)
    sizes = draw_sizes(jax.random.fold_in(key_list[8], 71), 0)
    params = draw_params(jax.random.fold_in(key_list[8], 71), 0)
    first_moment = bell_draw(key_list[5], (N_TENSOR, FLAT), 0.000009, 4.999999873689376e-05, ((0, 4), (1, 8)), jnp.float32)
    squared_mean = jnp.clip(jnp.exp(math.log(3.199999987213431e-10) - 1.3862944 * jax.random.uniform(key_list[6], (N_TENSOR, FLAT), jnp.float32) ** levels(key_list[6], (N_TENSOR, FLAT), ((0, 4), (1, 8)), -0.2, 0.2)), 7.999999968033578e-11, 3.199999987213431e-10)
    average = draw_average(jax.random.fold_in(key_list[8], 71), 0)
    return dict(features=features, labels=labels, valid=valid, sizes=sizes, params=params, first_moment=first_moment, squared_mean=squared_mean, average=average)


HIGH = lax.Precision.HIGHEST
BIN_COUNTS = (1, 2, 3, 6)

@jax.custom_vjp
def low(v):
    return lax.optimization_barrier(v.astype(jnp.bfloat16)).astype(jnp.float32)

@jax.custom_vjp
def low_back(v):
    return v

def low_keep(v):
    return (low(v), None)

def low_pass(kept, grad):
    return (grad,)

def back_keep(v):
    return (v, None)

def back_low(kept, grad):
    return (low(grad),)
low.defvjp(low_keep, low_pass)
low_back.defvjp(back_keep, back_low)

def segment_shapes(splits):
    return [(C_IN, MID // splits), (C_IN, C_OUT // splits), (9, MID, MID // splits), (MID, C_OUT // splits), (4, C_OUT // splits, PPM), (9, C_OUT + 4 * PPM, PPM // splits), (PPM // splits, NCLS), (9, C_IN, AUXW // splits), (AUXW // splits, NCLS), (2, (2 * MID + 2 * C_OUT + 5 * PPM + AUXW) // splits)]

def unflatten(rows, splits):
    split_parts = []
    start = 0
    for shape in segment_shapes(splits):
        count = 1
        for extent in shape:
            count = count * extent
        count = count // rows.shape[0]
        split_parts.append(rows[:, start:start + count].reshape(shape))
        start = start + count
    return split_parts

def gain_pieces(gains, splits):
    widths = [MID, C_OUT, MID, C_OUT, PPM, PPM, PPM, PPM, PPM, AUXW]
    split_parts = []
    start = 0
    for width in widths:
        step_width = width // splits
        split_parts.append(gains[:, start:start + step_width])
        start = start + step_width
    return split_parts

def whole_weights(flat):
    shards = [unflatten(flat[row].reshape(N_BATCH, -1), N_TENSOR) for row in range(N_TENSOR)]
    joins = [1, 1, 2, 1, 1, 2, 0, 2, 0]
    weights = [jnp.concatenate([piece[k] for piece in shards], axis=joins[k]) for k in range(9)]
    gain_shards = [gain_pieces(piece[9], N_TENSOR) for piece in shards]
    norms = [jnp.concatenate([g[k] for g in gain_shards], axis=1) for k in range(10)]
    return (weights, norms)

def shifted(field, down, right):
    image_height, width = (field.shape[1], field.shape[2])
    rows_pad, cols_pad = (abs(down), abs(right))
    padded = jnp.pad(field, ((0, 0), (rows_pad, rows_pad), (cols_pad, cols_pad), (0, 0)))
    return padded[:, rows_pad + down:rows_pad + down + image_height, cols_pad + right:cols_pad + right + width, :]

def matmul(field, weight):
    return jnp.dot(field, weight, precision=HIGH)

def conv_apply(field, kernel, spacing):
    total = jnp.zeros(field.shape[:-1] + (kernel.shape[2],), jnp.float32)
    for tap in range(9):
        total = total + matmul(shifted(field, (tap // 3 - 1) * spacing, (tap % 3 - 1) * spacing), kernel[tap])
    return total

def batch_norm(value, mask, norm):
    count = jnp.sum(mask * jnp.ones((1,) * (value.ndim - 1) + (1,), jnp.float32))
    axes = tuple(range(value.ndim - 1))
    mean = lax.optimization_barrier(jnp.sum(value * mask, axis=axes)) / count
    spread = lax.optimization_barrier(jnp.sum(value * value * mask, axis=axes)) / count - mean * mean
    return norm[0] * (value - mean) * lax.rsqrt(spread + 1e-05) + norm[1]

def bin_tables(extent, bins, length):
    which = jnp.arange(bins, dtype=jnp.int32)[None, :, None]
    place = jnp.arange(length, dtype=jnp.int32)[None, None, :]
    edge = extent.astype(jnp.int32)[:, None, None]
    lower = which * edge // bins
    upper = ((which + 1) * edge + bins - 1) // bins
    member = ((place >= lower) & (place < upper)).astype(jnp.float32)
    target = jnp.minimum(place * bins // edge, bins - 1)
    chosen = (target == which).astype(jnp.float32)
    return (member, chosen)

def forward(flat, features, labels_hot, cell_weight, inside, sizes):
    weights, norms = whole_weights(low(flat))
    w_reduce, w_short, w_middle, w_expand, w_branch, w_unite, w_classes, w_aux, w_aux_classes = weights
    field = features.astype(jnp.float32)
    pre_reduce = low_back(matmul(field, w_reduce))
    pre_short = low_back(matmul(field, w_short))
    pre_aux = low_back(conv_apply(field, w_aux, 1))
    hidden_one = low(jax.nn.silu(batch_norm(pre_reduce, inside, norms[0])))
    aux_act = low(jax.nn.silu(batch_norm(pre_aux, inside, norms[9])))
    pre_middle = low_back(conv_apply(hidden_one, w_middle, 4))
    hidden_two = low(jax.nn.silu(batch_norm(pre_middle, inside, norms[2])))
    pre_expand = low_back(matmul(hidden_two, w_expand))
    merged = low(jax.nn.silu(batch_norm(pre_expand, inside, norms[3]) + batch_norm(pre_short, inside, norms[1])))
    joined = [merged]
    for group, bins in enumerate(BIN_COUNTS):
        rows_in, rows_pick = bin_tables(sizes[:, 0], bins, MAP)
        cols_in, cols_pick = bin_tables(sizes[:, 1], bins, MAP)
        rows_in = rows_in / lax.optimization_barrier(jnp.sum(rows_in, axis=2, keepdims=True))
        cols_in = cols_in / lax.optimization_barrier(jnp.sum(cols_in, axis=2, keepdims=True))
        pooled = low(jnp.einsum('ikh,ilw,ihwc->iklc', rows_in, cols_in, merged, precision=HIGH))
        branch_pre = low_back(jnp.einsum('iklc,cd->ikld', pooled, w_branch[group], precision=HIGH))
        ones = jnp.ones(branch_pre.shape[:-1] + (1,), jnp.float32)
        branch_act = low(jax.nn.silu(batch_norm(branch_pre, ones, norms[4 + group])))
        joined.append(jnp.einsum('ikh,ilw,iklc->ihwc', rows_pick, cols_pick, branch_act, precision=HIGH))
    pre_unite = low_back(conv_apply(jnp.concatenate(joined, axis=-1), w_unite, 1))
    united = low(jax.nn.silu(batch_norm(pre_unite, inside, norms[8])))
    logit_main = low_back(matmul(united, w_classes))
    logit_aux = low_back(matmul(aux_act, w_aux_classes))
    loss_main = -lax.optimization_barrier(jnp.sum(labels_hot * jax.nn.log_softmax(logit_main, axis=-1), axis=-1, keepdims=True))
    loss_aux = -lax.optimization_barrier(jnp.sum(labels_hot * jax.nn.log_softmax(logit_aux, axis=-1), axis=-1, keepdims=True))
    return jnp.sum(cell_weight * (loss_main + 0.4 * loss_aux))

def reference(features, labels, valid, sizes, params, first_moment, squared_mean, average):
    rows_at = jnp.arange(MAP, dtype=jnp.int32)
    inside = (rows_at[None, :, None] < sizes[:, 0][:, None, None]) & (rows_at[None, None, :] < sizes[:, 1][:, None, None])
    inside = inside.astype(jnp.float32)[..., None]
    counted = inside * valid.astype(jnp.float32)[..., None]
    labels_hot = (labels[..., None] == jnp.arange(NCLS, dtype=jnp.int32)).astype(jnp.float32)
    class_pixel_counts = lax.optimization_barrier(jnp.sum(labels_hot * counted, axis=(0, 1, 2)))
    total = jnp.sum(class_pixel_counts)
    class_weight = total / (NCLS * class_pixel_counts + total)
    loss_weight = jnp.sum(class_pixel_counts * class_weight)
    cell_weight = lax.optimization_barrier(jnp.sum(labels_hot * class_weight, axis=-1, keepdims=True)) * counted

    def objective(flat):
        summed = forward(flat, features, labels_hot, cell_weight, inside, sizes)
        return (summed / loss_weight, summed)
    loss, pull, loss_sum = jax.vjp(objective, params, has_aux=True)
    grad = pull(jnp.ones((), jnp.float32))[0]
    unite_shift_grad = whole_weights(grad)[1][8][1]
    grad_norm = jnp.sqrt(jnp.sum(grad * grad))
    clipped = grad * jnp.minimum(1.0, 0.05 / (grad_norm + 1e-06))
    new_first = 0.5 * first_moment + 0.5 * clipped
    new_second = 0.5 * squared_mean + 0.5 * clipped * clipped
    keep = 1.0 - 0.5 ** STEP
    new_params = params - 0.01 * (new_first / keep / (jnp.sqrt(new_second / keep) + 1e-08) + 0.01 * params)
    new_average = 0.999 * average + 0.001 * new_params
    return (new_params, new_first, new_second, new_average, new_params.astype(jnp.bfloat16), grad_norm, loss_sum, loss_weight, unite_shift_grad)
```

```python
import functools

import jax
import jax.numpy as jnp
from jax import lax
from jax.experimental import pallas as pl
from jax.experimental.pallas import tpu as pltpu
from jax.sharding import PartitionSpec as P

C_IN = 1024
MID = 512
C_OUT = 2048
PPM = 512
AUXW = 256
NCLS = 150
MAP = 24
STEP = 3


BIN_COUNTS = (1, 2, 3, 6)
BIN_STARTS = (0, 1, 5, 14)


def segment_shapes(splits):
    return [
        (C_IN, MID // splits),
        (C_IN, C_OUT // splits),
        (9, MID, MID // splits),
        (MID, C_OUT // splits),
        (4, C_OUT // splits, PPM),
        (9, C_OUT + 4 * PPM, PPM // splits),
        (PPM // splits, NCLS),
        (9, C_IN, AUXW // splits),
        (AUXW // splits, NCLS),
        (2, (2 * MID + 2 * C_OUT + 5 * PPM + AUXW) // splits),
    ]


def unflatten(rows, splits):
    split_parts = []
    start = 0
    for shape in segment_shapes(splits):
        count = 1
        for extent in shape:
            count = count * extent
        count = count // rows.shape[0]
        split_parts.append(rows[:, start : start + count].reshape(shape))
        start = start + count
    return split_parts


def gain_pieces(gains, splits):
    widths = [MID, C_OUT, MID, C_OUT, PPM, PPM, PPM, PPM, PPM, AUXW]
    split_parts = []
    start = 0
    for width in widths:
        step_width = width // splits
        split_parts.append(gains[:, start : start + step_width])
        start = start + step_width
    return split_parts


def shifted(field, down, right):
    image_height, width = (field.shape[1], field.shape[2])
    rows_pad, cols_pad = (abs(down), abs(right))
    padded = jnp.pad(field, ((0, 0), (rows_pad, rows_pad), (cols_pad, cols_pad), (0, 0)))
    return padded[
        :,
        rows_pad + down : rows_pad + down + image_height,
        cols_pad + right : cols_pad + right + width,
        :,
    ]


def conv_forward(field, kernel, spacing):
    total = jnp.zeros(field.shape[:-1] + (kernel.shape[2],), jnp.float32)
    for tap in range(9):
        moved = shifted(field, (tap // 3 - 1) * spacing, (tap % 3 - 1) * spacing)
        total = total + jnp.dot(moved, kernel[tap], preferred_element_type=jnp.float32)
    return total


def conv_input_back(grad, kernel, spacing):
    total = jnp.zeros(grad.shape[:-1] + (kernel.shape[1],), jnp.float32)
    for tap in range(9):
        product = jnp.dot(grad, kernel[tap].T, preferred_element_type=jnp.float32)
        total = total + shifted(product, -(tap // 3 - 1) * spacing, -(tap % 3 - 1) * spacing)
    return total


def conv_kernel_back(field, grad, spacing):
    return jnp.stack(
        [
            jnp.einsum(
                "ihwc,ihwd->cd",
                shifted(field, (tap // 3 - 1) * spacing, (tap % 3 - 1) * spacing),
                grad,
                preferred_element_type=jnp.float32,
            )
            for tap in range(9)
        ]
    )


def silu_slope(value):
    gate = jax.nn.sigmoid(value)
    return gate * (1.0 + value * (1.0 - gate))


def channel_sums(values):
    return values.reshape(-1, values.shape[-1]).sum(0)


def masked_norm_apply(items, extra):
    sends = []
    for value, mask, norm in items:
        sends = sends + [
            channel_sums(value * mask),
            channel_sums(value * value * mask),
            jnp.sum(mask) * jnp.ones((1,), jnp.float32),
        ]
    totals = lax.psum(tuple(sends + extra), "batch")
    results = []
    for index, (value, mask, norm) in enumerate(items):
        count = totals[3 * index + 2]
        mean = totals[3 * index] / count
        spread = totals[3 * index + 1] / count - mean * mean
        scaling = lax.rsqrt(spread + 1e-05)
        normed = (value - mean) * scaling
        results.append((norm[0] * normed + norm[1], normed, scaling, count, mask, norm[0]))
    return (results, totals[3 * len(items) :])


def norm_backward(items):
    sends = []
    for grad, kept in items:
        sends = sends + [channel_sums(grad), channel_sums(grad * kept[1])]
    totals = lax.psum(tuple(sends), "batch")
    results = []
    for index, (grad, kept) in enumerate(items):
        outcome, normed, scaling, count, mask, gamma = kept
        first_sum, second_sum = (totals[2 * index], totals[2 * index + 1])
        inner = grad - mask * (first_sum + normed * second_sum) / count
        results.append(gamma * scaling * inner)
    return (results, sends, totals)


def bin_tables(extent, bins, length):
    which = jnp.arange(bins, dtype=jnp.int32)[None, :, None]
    place = jnp.arange(length, dtype=jnp.int32)[None, None, :]
    edge = extent[:, None, None]
    lower = which * edge // bins
    upper = ((which + 1) * edge + bins - 1) // bins
    member = ((place >= lower) & (place < upper)).astype(jnp.float32)
    target = jnp.minimum(place * bins // edge, bins - 1)
    chosen = (target == which).astype(jnp.float32)
    return (member, chosen)


def spread_bins(merged, branch, tables, images):
    joined = [merged]
    for group, bins in enumerate(BIN_COUNTS):
        rows_in, cols_in, rows_pick, cols_pick, cell_count = tables[group]
        piece = branch[:, BIN_STARTS[group] : BIN_STARTS[group] + bins * bins].reshape(
            images, bins, bins, -1
        )
        joined.append(
            jnp.einsum(
                "ikh,ilw,iklc->ihwc",
                rows_pick.astype(jnp.bfloat16),
                cols_pick.astype(jnp.bfloat16),
                piece,
                preferred_element_type=jnp.float32,
            ).astype(jnp.bfloat16)
        )
    return jnp.concatenate(joined, axis=-1)


def pick_bins(d_joined, width, tables, images):
    branch_width = (d_joined.shape[-1] - width) // 4
    d_up = []
    for group, bins in enumerate(BIN_COUNTS):
        rows_in, cols_in, rows_pick, cols_pick, cell_count = tables[group]
        piece = d_joined[..., width + group * branch_width : width + (group + 1) * branch_width]
        d_up.append(
            jnp.einsum("ikh,ilw,ihwc->iklc", rows_pick, cols_pick, piece).reshape(
                images, bins * bins, -1
            )
        )
    return (d_joined[..., :width], jnp.concatenate(d_up, axis=1))


def gather_channels(field):
    return lax.all_gather(field, "tensor", axis=3, tiled=True)


def scatter_channels(field):
    return lax.psum_scatter(
        field.astype(jnp.bfloat16), "tensor", scatter_dimension=3, tiled=True
    ).astype(jnp.float32)


def local(features, labels, valid, sizes, params, first_moment, squared_mean, average):
    splits = lax.axis_size("tensor")
    owners = lax.axis_size("batch")
    images = features.shape[0]
    gathered = lax.all_gather(params.astype(jnp.bfloat16), "batch", axis=0, tiled=True)
    (
        w_reduce,
        w_short,
        w_middle,
        w_expand,
        w_branch,
        w_unite,
        w_classes,
        w_aux,
        w_aux_classes,
        gains,
    ) = unflatten(gathered, splits)
    norms = [(piece[0], piece[1]) for piece in gain_pieces(gains.astype(jnp.float32), splits)]
    rows_at = jnp.arange(MAP, dtype=jnp.int32)
    inside = (rows_at[None, :, None] < sizes[:, 0][:, None, None]) & (
        rows_at[None, None, :] < sizes[:, 1][:, None, None]
    )
    inside = inside.astype(jnp.float32)[..., None]
    counted = inside * valid.astype(jnp.float32)[..., None]
    labels_hot = (labels[..., None] == jnp.arange(NCLS, dtype=jnp.int32)).astype(jnp.float32)
    class_local = channel_sums(labels_hot * counted)
    whole = lax.all_gather(features, "tensor", axis=3, tiled=True)
    pre_reduce = jnp.dot(whole, w_reduce, preferred_element_type=jnp.float32)
    pre_short = jnp.dot(whole, w_short, preferred_element_type=jnp.float32)
    pre_aux = conv_forward(whole, w_aux, 1)
    leading_part, label_tally = masked_norm_apply(
        [
            (pre_reduce, inside, norms[0]),
            (pre_short, inside, norms[1]),
            (pre_aux, inside, norms[9]),
        ],
        [class_local],
    )
    class_pixel_counts = label_tally[0]
    hidden_one = jax.nn.silu(leading_part[0][0]).astype(jnp.bfloat16)
    aux_act = jax.nn.silu(leading_part[2][0]).astype(jnp.bfloat16)
    hidden_full = gather_channels(hidden_one)
    pre_middle = conv_forward(hidden_full, w_middle, 4)
    second, unused = masked_norm_apply([(pre_middle, inside, norms[2])], [])
    hidden_two = jax.nn.silu(second[0][0]).astype(jnp.bfloat16)
    hidden_two_full = gather_channels(hidden_two)
    pre_expand = jnp.dot(hidden_two_full, w_expand, preferred_element_type=jnp.float32)
    third, unused = masked_norm_apply([(pre_expand, inside, norms[3])], [])
    summed = third[0][0] + leading_part[1][0]
    merged = jax.nn.silu(summed).astype(jnp.bfloat16)
    tables = []
    pooled_list = []
    partial_list = []
    for group, bins in enumerate(BIN_COUNTS):
        rows_in, rows_pick = bin_tables(sizes[:, 0], bins, MAP)
        cols_in, cols_pick = bin_tables(sizes[:, 1], bins, MAP)
        cell_count = (
            jnp.sum(rows_in, axis=2)[:, :, None, None] * jnp.sum(cols_in, axis=2)[:, None, :, None]
        )
        tables.append((rows_in, cols_in, rows_pick, cols_pick, cell_count))
        pooled = (
            jnp.einsum(
                "ikh,ilw,ihwc->iklc",
                rows_in.astype(jnp.bfloat16),
                cols_in.astype(jnp.bfloat16),
                merged,
                preferred_element_type=jnp.float32,
            )
            / cell_count
        )
        pooled = pooled.astype(jnp.bfloat16).reshape(images, bins * bins, -1)
        pooled_list.append(pooled)
        partial_list.append(
            jnp.einsum("ipc,cd->ipd", pooled, w_branch[group], preferred_element_type=jnp.float32)
        )
    branch_pre = lax.psum_scatter(
        jnp.concatenate(partial_list, axis=1).astype(jnp.bfloat16),
        "tensor",
        scatter_dimension=2,
        tiled=True,
    ).astype(jnp.float32)
    branch_items = []
    for group, bins in enumerate(BIN_COUNTS):
        piece = branch_pre[:, BIN_STARTS[group] : BIN_STARTS[group] + bins * bins]
        branch_items.append(
            (piece, jnp.ones(piece.shape[:-1] + (1,), jnp.float32), norms[4 + group])
        )
    fourth, unused = masked_norm_apply(branch_items, [])
    branch_act = jnp.concatenate([jax.nn.silu(kept[0]) for kept in fourth], axis=1).astype(
        jnp.bfloat16
    )
    merged_full, branch_full = (
        lax.all_gather(merged, "tensor", axis=3, tiled=True),
        lax.all_gather(branch_act, "tensor", axis=2, tiled=True),
    )
    joined = spread_bins(merged_full, branch_full, tables, images)
    pre_unite = conv_forward(joined, w_unite, 1)
    fifth, unused = masked_norm_apply([(pre_unite, inside, norms[8])], [])
    united = jax.nn.silu(fifth[0][0]).astype(jnp.bfloat16)
    logit_main, logit_aux = (
        lax.psum_scatter(
            jnp.dot(united, w_classes, preferred_element_type=jnp.float32).astype(jnp.bfloat16),
            "tensor",
            scatter_dimension=1,
            tiled=True,
        ).astype(jnp.float32),
        lax.psum_scatter(
            jnp.dot(aux_act, w_aux_classes, preferred_element_type=jnp.float32).astype(
                jnp.bfloat16
            ),
            "tensor",
            scatter_dimension=1,
            tiled=True,
        ).astype(jnp.float32),
    )
    total_valid = jnp.sum(class_pixel_counts)
    class_weight = total_valid / (NCLS * class_pixel_counts + total_valid)
    loss_weight = jnp.sum(class_pixel_counts * class_weight)
    cell_weight = jnp.sum(labels_hot * class_weight, axis=-1, keepdims=True) * counted
    band_rows = labels.shape[1] // splits
    band_start = lax.axis_index("tensor") * band_rows
    hot_band = lax.dynamic_slice_in_dim(labels_hot, band_start, band_rows, 1)
    weight_band = lax.dynamic_slice_in_dim(cell_weight, band_start, band_rows, 1)
    log_main = jax.nn.log_softmax(logit_main, axis=-1)
    log_aux = jax.nn.log_softmax(logit_aux, axis=-1)
    loss_cells = -jnp.sum(hot_band * (log_main + 0.4 * log_aux), axis=-1, keepdims=True)
    loss_local = jnp.sum(weight_band * loss_cells)
    band_main = (weight_band * (jnp.exp(log_main) - hot_band) / loss_weight).astype(jnp.bfloat16)
    band_aux = (0.4 * weight_band * (jnp.exp(log_aux) - hot_band) / loss_weight).astype(
        jnp.bfloat16
    )
    grad_main, grad_aux = (
        lax.all_gather(band_main, "tensor", axis=1, tiled=True),
        lax.all_gather(band_aux, "tensor", axis=1, tiled=True),
    )
    reduced = {}

    def settle(index, value):
        reduced[index] = value

    settle(6, jnp.einsum("ihwc,ihwk->ck", united, grad_main, preferred_element_type=jnp.float32))
    settle(8, jnp.einsum("ihwc,ihwk->ck", aux_act, grad_aux, preferred_element_type=jnp.float32))
    d_united = jnp.dot(grad_main, w_classes.T, preferred_element_type=jnp.float32) * silu_slope(
        fifth[0][0]
    )
    d_aux = jnp.dot(grad_aux, w_aux_classes.T, preferred_element_type=jnp.float32) * silu_slope(
        leading_part[2][0]
    )
    back_one, sums_one, totals_one = norm_backward([(d_united, fifth[0]), (d_aux, leading_part[2])])
    unite_shift_grad = totals_one[0]
    d_unite_pre = back_one[0].astype(jnp.bfloat16)
    d_aux_pre = back_one[1].astype(jnp.bfloat16)
    settle(5, conv_kernel_back(joined, d_unite_pre, 1))
    d_merged, d_branch = pick_bins(conv_input_back(d_unite_pre, w_unite, 1), C_OUT, tables, images)
    d_merged, d_branch = (
        lax.psum_scatter(
            d_merged.astype(jnp.bfloat16), "tensor", scatter_dimension=3, tiled=True
        ).astype(jnp.float32),
        lax.psum_scatter(
            d_branch.astype(jnp.bfloat16), "tensor", scatter_dimension=2, tiled=True
        ).astype(jnp.float32),
    )
    settle(7, conv_kernel_back(whole, d_aux_pre, 1))
    branch_back = []
    for group, bins in enumerate(BIN_COUNTS):
        piece = d_branch[:, BIN_STARTS[group] : BIN_STARTS[group] + bins * bins]
        branch_back.append((piece * silu_slope(fourth[group][0]), fourth[group]))
    back_two, sums_two, unused = norm_backward(branch_back)
    d_branch_pre = jnp.concatenate(back_two, axis=1).astype(jnp.bfloat16)
    d_branch_full = lax.all_gather(d_branch_pre, "tensor", axis=2, tiled=True)
    branch_grads = []
    for group, bins in enumerate(BIN_COUNTS):
        rows_in, cols_in, rows_pick, cols_pick, cell_count = tables[group]
        piece = d_branch_full[:, BIN_STARTS[group] : BIN_STARTS[group] + bins * bins]
        branch_grads.append(
            jnp.einsum("ipc,ipd->cd", pooled_list[group], piece, preferred_element_type=jnp.float32)
        )
        d_pooled = jnp.dot(piece, w_branch[group].T, preferred_element_type=jnp.float32).reshape(
            images, bins, bins, -1
        )
        d_merged = d_merged + jnp.einsum(
            "ikh,ilw,iklc->ihwc", rows_in, cols_in, d_pooled / cell_count
        )
    settle(4, jnp.stack(branch_grads))
    d_summed = d_merged * silu_slope(summed)
    back_three, sums_three, unused = norm_backward(
        [(d_summed, third[0]), (d_summed, leading_part[1])]
    )
    d_expand_pre = back_three[0].astype(jnp.bfloat16)
    d_short_pre = back_three[1].astype(jnp.bfloat16)
    settle(
        3,
        jnp.einsum(
            "ihwc,ihwd->cd", hidden_two_full, d_expand_pre, preferred_element_type=jnp.float32
        ),
    )
    settle(1, jnp.einsum("ihwc,ihwd->cd", whole, d_short_pre, preferred_element_type=jnp.float32))
    d_two = scatter_channels(jnp.dot(d_expand_pre, w_expand.T, preferred_element_type=jnp.float32))
    back_four, sums_four, unused = norm_backward([(d_two * silu_slope(second[0][0]), second[0])])
    d_middle_pre = back_four[0].astype(jnp.bfloat16)
    settle(2, conv_kernel_back(hidden_full, d_middle_pre, 4))
    d_one = scatter_channels(conv_input_back(d_middle_pre, w_middle, 4))
    back_five, sums_five, unused = norm_backward(
        [(d_one * silu_slope(leading_part[0][0]), leading_part[0])]
    )
    settle(
        0,
        jnp.einsum(
            "ihwc,ihwd->cd",
            whole,
            back_five[0].astype(jnp.bfloat16),
            preferred_element_type=jnp.float32,
        ),
    )
    beta_grads = (
        [sums_five[0], sums_three[2], sums_four[0], sums_three[0]]
        + [sums_two[2 * g] for g in range(4)]
        + [sums_one[0], sums_one[2]]
    )
    gamma_grads = (
        [sums_five[1], sums_three[3], sums_four[1], sums_three[1]]
        + [sums_two[2 * g + 1] for g in range(4)]
        + [sums_one[1], sums_one[3]]
    )
    settle(9, jnp.stack([jnp.concatenate(gamma_grads), jnp.concatenate(beta_grads)]))
    ordered = [reduced[index] for index in range(10)]
    grad_share = lax.psum_scatter(
        jnp.concatenate([part.reshape(owners, -1) for part in ordered], axis=1),
        "batch",
        scatter_dimension=0,
        tiled=True,
    )
    square_all, loss_sum = lax.psum(
        (jnp.sum(grad_share * grad_share), loss_local), ("batch", "tensor")
    )
    grad_norm = jnp.sqrt(square_all)
    clipped = grad_share * jnp.minimum(1.0, 0.05 / (grad_norm + 1e-06))
    new_first = 0.5 * first_moment + 0.5 * clipped
    new_second = 0.5 * squared_mean + 0.5 * clipped * clipped
    keep = 1.0 - 0.5**STEP
    new_params = params - 0.01 * (
        new_first / keep / (jnp.sqrt(new_second / keep) + 1e-08) + 0.01 * params
    )
    new_average = 0.999 * average + 0.001 * new_params
    return (
        new_params,
        new_first,
        new_second,
        new_average,
        new_params.astype(jnp.bfloat16),
        grad_norm,
        loss_sum,
        loss_weight,
        unite_shift_grad,
    )


MESH = pl.DeviceIdType.MESH
ANY = pl.BlockSpec(memory_space=pl.ANY)


def gather_kernel(owners, count, order, *refs):
    pieces, fulls = refs[:count], refs[count : 2 * count]
    near_send, far_send, pass_send, recv, keep = refs[2 * count :]
    me = lax.axis_index("batch")
    half = owners // 2
    partner = me + 1 - 2 * lax.rem(me, 2)

    def peer_of(base, step):
        return lax.rem(base + 2 * step, owners)

    barrier = pltpu.get_barrier_semaphore()
    pl.semaphore_signal(barrier, inc=1, device_id={"batch": partner}, device_id_type=MESH)
    for step in range(1, half):
        pl.semaphore_signal(
            barrier, inc=1, device_id={"batch": peer_of(me, step)}, device_id_type=MESH
        )
    pl.semaphore_wait(barrier, half)

    def near(seg):
        return pltpu.make_async_remote_copy(
            src_ref=pieces[seg],
            dst_ref=fulls[seg].at[me],
            send_sem=near_send.at[seg],
            recv_sem=recv.at[seg, me],
            device_id={"batch": partner},
            device_id_type=MESH,
        )

    def far(seg, step):
        return pltpu.make_async_remote_copy(
            src_ref=pieces[seg],
            dst_ref=fulls[seg].at[me],
            send_sem=far_send.at[seg, step],
            recv_sem=recv.at[seg, me],
            device_id={"batch": peer_of(me, step)},
            device_id_type=MESH,
        )

    def passed(seg, step, base):
        source = peer_of(base, step)
        return pltpu.make_async_remote_copy(
            src_ref=fulls[seg].at[source],
            dst_ref=fulls[seg].at[source],
            send_sem=pass_send.at[seg, step],
            recv_sem=recv.at[seg, source],
            device_id={"batch": partner},
            device_id_type=MESH,
        )

    for seg in order:
        pltpu.make_async_copy(pieces[seg], fulls[seg].at[me], keep.at[seg]).start()
        for step in range(1, half):
            far(seg, step).start()
        near(seg).start()
    for seg in order:
        for step in range(1, half):
            passed(seg, step, me).wait_recv()
            passed(seg, step, me).start()
    for seg in order:
        for step in range(half):
            passed(seg, step, partner).wait_recv()
    for seg in order:
        pltpu.make_async_copy(pieces[seg], fulls[seg].at[me], keep.at[seg]).wait()
        near(seg).wait_send()
        for step in range(1, half):
            far(seg, step).wait_send()
            passed(seg, step, me).wait_send()


def gather_weights(pieces, owners, order):
    count = len(pieces)
    half = owners // 2
    return pl.pallas_call(
        functools.partial(gather_kernel, owners, count, order),
        out_shape=[jax.ShapeDtypeStruct((owners,) + p.shape, p.dtype) for p in pieces],
        in_specs=[ANY] * count,
        out_specs=[ANY] * count,
        scratch_shapes=[
            pltpu.SemaphoreType.DMA((count,)),
            pltpu.SemaphoreType.DMA((count, half)),
            pltpu.SemaphoreType.DMA((count, half)),
            pltpu.SemaphoreType.DMA((count, owners)),
            pltpu.SemaphoreType.DMA((count,)),
        ],
        compiler_params=pltpu.CompilerParams(collective_id=0, has_side_effects=True),
        name="gather_weights",
    )(*pieces)


def scatter_kernel(owners, count, order, *refs):
    half = owners // 2
    parts, outs = refs[:count], refs[count : 2 * count]
    first, second = refs[2 * count : 3 * count], refs[3 * count : 4 * count]
    near_send, near_recv, far_send, far_recv = refs[4 * count :]
    me = lax.axis_index("batch")
    side = lax.rem(me, 2)
    partner = me + 1 - 2 * side

    def peer_of(base, step):
        return lax.rem(base + 2 * step, owners)

    barrier = pltpu.get_barrier_semaphore()
    pl.semaphore_signal(barrier, inc=1, device_id={"batch": partner}, device_id_type=MESH)
    for step in range(1, half):
        pl.semaphore_signal(
            barrier, inc=1, device_id={"batch": peer_of(me, step)}, device_id_type=MESH
        )
    pl.semaphore_wait(barrier, half)

    def near(seg, step):
        return pltpu.make_async_remote_copy(
            src_ref=parts[seg].at[peer_of(partner, step)],
            dst_ref=first[seg].at[step],
            send_sem=near_send.at[seg, step],
            recv_sem=near_recv.at[seg, step],
            device_id={"batch": partner},
            device_id_type=MESH,
        )

    def far(seg, step):
        return pltpu.make_async_remote_copy(
            src_ref=first[seg].at[step],
            dst_ref=second[seg].at[step],
            send_sem=far_send.at[seg, step],
            recv_sem=far_recv.at[seg, step],
            device_id={"batch": peer_of(me, step)},
            device_id_type=MESH,
        )

    def rows_of(seg):
        return min(64, parts[seg].shape[1])

    steps = list(range(1, half)) + [0]
    for seg in order:
        for step in steps:
            near(seg, step).start()
    for seg in order:
        rows = rows_of(seg)
        for step in steps:
            near(seg, step).wait_recv()
            mine = peer_of(me, step)

            def add(k, carry, seg=seg, step=step, mine=mine, rows=rows):
                at = pl.ds(pl.multiple_of(k * rows, rows), rows)
                total = parts[seg][mine, at, :].astype(jnp.float32) + first[seg][
                    step, at, :
                ].astype(jnp.float32)
                if step == 0:
                    outs[seg][at, :] = total
                else:
                    first[seg][step, at, :] = total.astype(jnp.bfloat16)
                return carry

            lax.fori_loop(0, parts[seg].shape[1] // rows, add, 0)
            if step:
                far(seg, step).start()
    for seg in order:
        rows = rows_of(seg)
        for step in range(1, half):
            far(seg, step).wait_recv()

        def add_far(k, carry, seg=seg, rows=rows):
            at = pl.ds(pl.multiple_of(k * rows, rows), rows)
            total = outs[seg][at, :]
            for step in range(1, half):
                total = total + second[seg][step, at, :].astype(jnp.float32)
            outs[seg][at, :] = total
            return carry

        lax.fori_loop(0, parts[seg].shape[1] // rows, add_far, 0)
    for seg in order:
        for step in steps:
            near(seg, step).wait_send()
            if step:
                far(seg, step).wait_send()


def scatter_grads(parts, order):
    count = len(parts)
    owners = parts[0].shape[0]
    half = owners // 2
    buffers = [pltpu.VMEM((half,) + p.shape[1:], jnp.bfloat16) for p in parts]
    vmem = pl.BlockSpec(memory_space=pltpu.VMEM)
    return pl.pallas_call(
        functools.partial(scatter_kernel, owners, count, order),
        out_shape=[jax.ShapeDtypeStruct(p.shape[1:], jnp.float32) for p in parts],
        in_specs=[vmem] * count,
        out_specs=[vmem] * count,
        scratch_shapes=buffers
        + buffers
        + [pltpu.SemaphoreType.DMA((count, half)) for _ in range(4)],
        compiler_params=pltpu.CompilerParams(
            collective_id=1, has_side_effects=True, vmem_limit_bytes=60 * 1024 * 1024
        ),
        name="scatter_grads",
    )(*parts)


def update_kernel(scale, grad, param, first, second, average, o_param, o_first, o_second, o_average):
    clipped = grad[...] * scale[0]
    new_first = 0.5 * first[...] + 0.5 * clipped
    new_second = 0.5 * second[...] + 0.5 * clipped * clipped
    keep = 1.0 - 0.5**STEP
    old = param[...]
    new = old - 0.01 * (new_first / keep / (jnp.sqrt(new_second / keep) + 1e-08) + 0.01 * old)
    o_param[...] = new
    o_first[...] = new_first
    o_second[...] = new_second
    o_average[...] = 0.999 * average[...] + 0.001 * new


def update(scale, grad, param, first, second, average):
    rows = grad.shape[0]
    block = pl.BlockSpec((512, 128), lambda i: (i, 0))
    return pl.pallas_call(
        update_kernel,
        grid=(pl.cdiv(rows, 512),),
        out_shape=[jax.ShapeDtypeStruct((rows, 128), jnp.float32)] * 4,
        in_specs=[pl.BlockSpec(memory_space=pltpu.SMEM)] + [block] * 5,
        out_specs=[block] * 4,
        name="update",
    )(scale.reshape(1), grad, param, first, second, average)


PIECES = (0, 1, 2, 3, 4, 5, 7)
SMALL = (6, 8, 9)


def piece_shapes(splits, owners):
    shapes = []
    for shape in segment_shapes(splits):
        count = 1
        for extent in shape:
            count = count * extent
        lanes = shape[-1] if shape[-1] % 128 == 0 else 128
        shapes.append((count // owners // lanes, lanes, count // owners))
    return shapes


def fits(splits, owners):
    shapes = piece_shapes(splits, owners)
    return owners % 2 == 0 and all(
        rows * lanes == count and (rows % 64 == 0 or rows in (16, 32))
        for rows, lanes, count in [shapes[k] for k in PIECES]
    ) and sum(shapes[k][2] for k in SMALL) % 2048 == 0


def local_fast(features, labels, valid, sizes, params, first_moment, squared_mean, average):
    splits = lax.axis_size("tensor")
    owners = lax.axis_size("batch")
    images = features.shape[0]
    shapes = piece_shapes(splits, owners)
    low = params.reshape(-1, 128).astype(jnp.bfloat16)
    starts = [0]
    for rows, lanes, count in shapes:
        starts.append(starts[-1] + count)
    tail = starts[6] // 128
    flat_tail = low[tail:].reshape(-1)
    pieces = []
    for k in range(6):
        pieces.append(low[starts[k] // 128 : starts[k + 1] // 128].reshape(shapes[k][:2]))
    cut = [
        flat_tail[starts[k] - starts[6] : starts[k + 1] - starts[6]] for k in range(6, 10)
    ]
    pieces.append(cut[1].reshape(shapes[7][:2]))
    pieces.append(jnp.concatenate([cut[0], cut[2], cut[3]]).reshape(-1, 128))
    full = gather_weights(pieces, owners, (0, 1, 6, 7, 2, 3, 4, 5))
    whole_shapes = segment_shapes(splits)
    small = full[7].reshape(owners, -1)
    ends = [shapes[6][2], shapes[6][2] + shapes[8][2]]
    parts_of = [
        full[0],
        full[1],
        full[2],
        full[3],
        full[4],
        full[5],
        small[:, : ends[0]],
        full[6],
        small[:, ends[0] : ends[1]],
        small[:, ends[1] :],
    ]
    unpacked = [part.reshape(shape) for part, shape in zip(parts_of, whole_shapes)]
    (
        w_reduce,
        w_short,
        w_middle,
        w_expand,
        w_branch,
        w_unite,
        w_classes,
        w_aux,
        w_aux_classes,
        gains,
    ) = unpacked
    norms = [(piece[0], piece[1]) for piece in gain_pieces(gains.astype(jnp.float32), splits)]
    rows_at = jnp.arange(MAP, dtype=jnp.int32)
    inside = (rows_at[None, :, None] < sizes[:, 0][:, None, None]) & (
        rows_at[None, None, :] < sizes[:, 1][:, None, None]
    )
    inside = inside.astype(jnp.float32)[..., None]
    counted = inside * valid.astype(jnp.float32)[..., None]
    labels_hot = (labels[..., None] == jnp.arange(NCLS, dtype=jnp.int32)).astype(jnp.float32)
    class_local = channel_sums(labels_hot * counted)
    whole = lax.all_gather(features, "tensor", axis=3, tiled=True)
    pre_reduce = jnp.dot(whole, w_reduce, preferred_element_type=jnp.float32)
    pre_short = jnp.dot(whole, w_short, preferred_element_type=jnp.float32)
    pre_aux = conv_forward(whole, w_aux, 1)
    leading_part, label_tally = masked_norm_apply(
        [
            (pre_reduce, inside, norms[0]),
            (pre_short, inside, norms[1]),
            (pre_aux, inside, norms[9]),
        ],
        [class_local],
    )
    class_pixel_counts = label_tally[0]
    hidden_one = jax.nn.silu(leading_part[0][0]).astype(jnp.bfloat16)
    aux_act = jax.nn.silu(leading_part[2][0]).astype(jnp.bfloat16)
    hidden_full = gather_channels(hidden_one)
    pre_middle = conv_forward(hidden_full, w_middle, 4)
    second, unused = masked_norm_apply([(pre_middle, inside, norms[2])], [])
    hidden_two = jax.nn.silu(second[0][0]).astype(jnp.bfloat16)
    hidden_two_full = gather_channels(hidden_two)
    pre_expand = jnp.dot(hidden_two_full, w_expand, preferred_element_type=jnp.float32)
    third, unused = masked_norm_apply([(pre_expand, inside, norms[3])], [])
    summed = third[0][0] + leading_part[1][0]
    merged = jax.nn.silu(summed).astype(jnp.bfloat16)
    tables = []
    pooled_list = []
    partial_list = []
    for group, bins in enumerate(BIN_COUNTS):
        rows_in, rows_pick = bin_tables(sizes[:, 0], bins, MAP)
        cols_in, cols_pick = bin_tables(sizes[:, 1], bins, MAP)
        cell_count = (
            jnp.sum(rows_in, axis=2)[:, :, None, None] * jnp.sum(cols_in, axis=2)[:, None, :, None]
        )
        tables.append((rows_in, cols_in, rows_pick, cols_pick, cell_count))
        pooled = (
            jnp.einsum(
                "ikh,ilw,ihwc->iklc",
                rows_in.astype(jnp.bfloat16),
                cols_in.astype(jnp.bfloat16),
                merged,
                preferred_element_type=jnp.float32,
            )
            / cell_count
        )
        pooled = pooled.astype(jnp.bfloat16).reshape(images, bins * bins, -1)
        pooled_list.append(pooled)
        partial_list.append(
            jnp.einsum("ipc,cd->ipd", pooled, w_branch[group], preferred_element_type=jnp.float32)
        )
    branch_pre = lax.psum_scatter(
        jnp.concatenate(partial_list, axis=1).astype(jnp.bfloat16),
        "tensor",
        scatter_dimension=2,
        tiled=True,
    ).astype(jnp.float32)
    branch_items = []
    for group, bins in enumerate(BIN_COUNTS):
        piece = branch_pre[:, BIN_STARTS[group] : BIN_STARTS[group] + bins * bins]
        branch_items.append(
            (piece, jnp.ones(piece.shape[:-1] + (1,), jnp.float32), norms[4 + group])
        )
    fourth, unused = masked_norm_apply(branch_items, [])
    branch_act = jnp.concatenate([jax.nn.silu(kept[0]) for kept in fourth], axis=1).astype(
        jnp.bfloat16
    )
    merged_full, branch_full = (
        lax.all_gather(merged, "tensor", axis=3, tiled=True),
        lax.all_gather(branch_act, "tensor", axis=2, tiled=True),
    )
    joined = spread_bins(merged_full, branch_full, tables, images)
    pre_unite = conv_forward(joined, w_unite, 1)
    fifth, unused = masked_norm_apply([(pre_unite, inside, norms[8])], [])
    united = jax.nn.silu(fifth[0][0]).astype(jnp.bfloat16)
    logit_main, logit_aux = (
        lax.psum_scatter(
            jnp.dot(united, w_classes, preferred_element_type=jnp.float32).astype(jnp.bfloat16),
            "tensor",
            scatter_dimension=1,
            tiled=True,
        ).astype(jnp.float32),
        lax.psum_scatter(
            jnp.dot(aux_act, w_aux_classes, preferred_element_type=jnp.float32).astype(
                jnp.bfloat16
            ),
            "tensor",
            scatter_dimension=1,
            tiled=True,
        ).astype(jnp.float32),
    )
    total_valid = jnp.sum(class_pixel_counts)
    class_weight = total_valid / (NCLS * class_pixel_counts + total_valid)
    loss_weight = jnp.sum(class_pixel_counts * class_weight)
    cell_weight = jnp.sum(labels_hot * class_weight, axis=-1, keepdims=True) * counted
    band_rows = labels.shape[1] // splits
    band_start = lax.axis_index("tensor") * band_rows
    hot_band = lax.dynamic_slice_in_dim(labels_hot, band_start, band_rows, 1)
    weight_band = lax.dynamic_slice_in_dim(cell_weight, band_start, band_rows, 1)
    log_main = jax.nn.log_softmax(logit_main, axis=-1)
    log_aux = jax.nn.log_softmax(logit_aux, axis=-1)
    loss_cells = -jnp.sum(hot_band * (log_main + 0.4 * log_aux), axis=-1, keepdims=True)
    loss_local = jnp.sum(weight_band * loss_cells)
    band_main = (weight_band * (jnp.exp(log_main) - hot_band) / loss_weight).astype(jnp.bfloat16)
    band_aux = (0.4 * weight_band * (jnp.exp(log_aux) - hot_band) / loss_weight).astype(
        jnp.bfloat16
    )
    grad_main, grad_aux = (
        lax.all_gather(band_main, "tensor", axis=1, tiled=True),
        lax.all_gather(band_aux, "tensor", axis=1, tiled=True),
    )
    reduced = {}

    def settle(index, value):
        reduced[index] = value

    settle(6, jnp.einsum("ihwc,ihwk->ck", united, grad_main, preferred_element_type=jnp.float32))
    settle(8, jnp.einsum("ihwc,ihwk->ck", aux_act, grad_aux, preferred_element_type=jnp.float32))
    d_united = jnp.dot(grad_main, w_classes.T, preferred_element_type=jnp.float32) * silu_slope(
        fifth[0][0]
    )
    d_aux = jnp.dot(grad_aux, w_aux_classes.T, preferred_element_type=jnp.float32) * silu_slope(
        leading_part[2][0]
    )
    back_one, sums_one, totals_one = norm_backward([(d_united, fifth[0]), (d_aux, leading_part[2])])
    unite_shift_grad = totals_one[0]
    d_unite_pre = back_one[0].astype(jnp.bfloat16)
    d_aux_pre = back_one[1].astype(jnp.bfloat16)
    settle(5, conv_kernel_back(joined, d_unite_pre, 1))
    d_merged, d_branch = pick_bins(conv_input_back(d_unite_pre, w_unite, 1), C_OUT, tables, images)
    d_merged, d_branch = (
        lax.psum_scatter(
            d_merged.astype(jnp.bfloat16), "tensor", scatter_dimension=3, tiled=True
        ).astype(jnp.float32),
        lax.psum_scatter(
            d_branch.astype(jnp.bfloat16), "tensor", scatter_dimension=2, tiled=True
        ).astype(jnp.float32),
    )
    settle(7, conv_kernel_back(whole, d_aux_pre, 1))
    branch_back = []
    for group, bins in enumerate(BIN_COUNTS):
        piece = d_branch[:, BIN_STARTS[group] : BIN_STARTS[group] + bins * bins]
        branch_back.append((piece * silu_slope(fourth[group][0]), fourth[group]))
    back_two, sums_two, unused = norm_backward(branch_back)
    d_branch_pre = jnp.concatenate(back_two, axis=1).astype(jnp.bfloat16)
    d_branch_full = lax.all_gather(d_branch_pre, "tensor", axis=2, tiled=True)
    branch_grads = []
    for group, bins in enumerate(BIN_COUNTS):
        rows_in, cols_in, rows_pick, cols_pick, cell_count = tables[group]
        piece = d_branch_full[:, BIN_STARTS[group] : BIN_STARTS[group] + bins * bins]
        branch_grads.append(
            jnp.einsum("ipc,ipd->cd", pooled_list[group], piece, preferred_element_type=jnp.float32)
        )
        d_pooled = jnp.dot(piece, w_branch[group].T, preferred_element_type=jnp.float32).reshape(
            images, bins, bins, -1
        )
        d_merged = d_merged + jnp.einsum(
            "ikh,ilw,iklc->ihwc", rows_in, cols_in, d_pooled / cell_count
        )
    settle(4, jnp.stack(branch_grads))
    d_summed = d_merged * silu_slope(summed)
    back_three, sums_three, unused = norm_backward(
        [(d_summed, third[0]), (d_summed, leading_part[1])]
    )
    d_expand_pre = back_three[0].astype(jnp.bfloat16)
    d_short_pre = back_three[1].astype(jnp.bfloat16)
    settle(
        3,
        jnp.einsum(
            "ihwc,ihwd->cd", hidden_two_full, d_expand_pre, preferred_element_type=jnp.float32
        ),
    )
    settle(1, jnp.einsum("ihwc,ihwd->cd", whole, d_short_pre, preferred_element_type=jnp.float32))
    d_two = scatter_channels(jnp.dot(d_expand_pre, w_expand.T, preferred_element_type=jnp.float32))
    back_four, sums_four, unused = norm_backward([(d_two * silu_slope(second[0][0]), second[0])])
    d_middle_pre = back_four[0].astype(jnp.bfloat16)
    settle(2, conv_kernel_back(hidden_full, d_middle_pre, 4))
    d_one = scatter_channels(conv_input_back(d_middle_pre, w_middle, 4))
    back_five, sums_five, unused = norm_backward(
        [(d_one * silu_slope(leading_part[0][0]), leading_part[0])]
    )
    settle(
        0,
        jnp.einsum(
            "ihwc,ihwd->cd",
            whole,
            back_five[0].astype(jnp.bfloat16),
            preferred_element_type=jnp.float32,
        ),
    )
    beta_grads = (
        [sums_five[0], sums_three[2], sums_four[0], sums_three[0]]
        + [sums_two[2 * g] for g in range(4)]
        + [sums_one[0], sums_one[2]]
    )
    gamma_grads = (
        [sums_five[1], sums_three[3], sums_four[1], sums_three[1]]
        + [sums_two[2 * g + 1] for g in range(4)]
        + [sums_one[1], sums_one[3]]
    )
    settle(9, jnp.stack([jnp.concatenate(gamma_grads), jnp.concatenate(beta_grads)]))
    rounded = [reduced[index].astype(jnp.bfloat16) for index in range(10)]
    sends = [
        rounded[k].reshape((owners,) + shapes[k][:2]) for k in PIECES
    ]
    sends.append(
        jnp.concatenate([rounded[k].reshape(owners, -1) for k in SMALL], axis=1).reshape(
            owners, -1, 128
        )
    )
    own = scatter_grads(sends, (5, 4, 6, 7, 3, 1, 2, 0))
    own_small = own[7].reshape(-1)
    grad_share = jnp.concatenate(
        [own[k].reshape(-1, 128) for k in range(6)]
        + [
            jnp.concatenate(
                [own_small[: ends[0]], own[6].reshape(-1), own_small[ends[0] :]]
            ).reshape(-1, 128)
        ]
    )
    square_all, loss_sum = lax.psum(
        (jnp.sum(grad_share * grad_share), loss_local), ("batch", "tensor")
    )
    grad_norm = jnp.sqrt(square_all)
    scale = jnp.minimum(1.0, 0.05 / (grad_norm + 1e-06))
    new_params, new_first, new_second, new_average = [
        item.reshape(params.shape)
        for item in update(
            scale,
            grad_share,
            params.reshape(-1, 128),
            first_moment.reshape(-1, 128),
            squared_mean.reshape(-1, 128),
            average.reshape(-1, 128),
        )
    ]
    return (
        new_params,
        new_first,
        new_second,
        new_average,
        new_params.astype(jnp.bfloat16),
        grad_norm,
        loss_sum,
        loss_weight,
        unite_shift_grad,
    )


def solution(mesh):
    chosen = local_fast if fits(mesh.shape["tensor"], mesh.shape["batch"]) else local
    return jax.shard_map(
        chosen,
        mesh=mesh,
        in_specs=(
            P("batch", None, None, "tensor"),
            P("batch", None, None),
            P("batch", None, None),
            P("batch", None),
            P("tensor", "batch"),
            P("tensor", "batch"),
            P("tensor", "batch"),
            P("tensor", "batch"),
        ),
        out_specs=(
            P("tensor", "batch"),
            P("tensor", "batch"),
            P("tensor", "batch"),
            P("tensor", "batch"),
            P("tensor", "batch"),
            P(),
            P(),
            P(),
            P("tensor"),
        ),
        check_vma=False,
    )
```

```python
import functools

import jax
import jax.numpy as jnp
from jax import lax
from jax.experimental import pallas as pl
from jax.experimental.pallas import tpu as pltpu
from jax.sharding import PartitionSpec as P

C_IN = 1024
MID = 512
C_OUT = 2048
PPM = 512
AUXW = 256
NCLS = 150
MAP = 24
STEP = 3


BIN_COUNTS = (1, 2, 3, 6)
BIN_STARTS = (0, 1, 5, 14)


def segment_shapes(splits):
    return [
        (C_IN, MID // splits),
        (C_IN, C_OUT // splits),
        (9, MID, MID // splits),
        (MID, C_OUT // splits),
        (4, C_OUT // splits, PPM),
        (9, C_OUT + 4 * PPM, PPM // splits),
        (PPM // splits, NCLS),
        (9, C_IN, AUXW // splits),
        (AUXW // splits, NCLS),
        (2, (2 * MID + 2 * C_OUT + 5 * PPM + AUXW) // splits),
    ]


def unflatten(rows, splits):
    split_parts = []
    start = 0
    for shape in segment_shapes(splits):
        count = 1
        for extent in shape:
            count = count * extent
        count = count // rows.shape[0]
        split_parts.append(rows[:, start : start + count].reshape(shape))
        start = start + count
    return split_parts


def gain_pieces(gains, splits):
    widths = [MID, C_OUT, MID, C_OUT, PPM, PPM, PPM, PPM, PPM, AUXW]
    split_parts = []
    start = 0
    for width in widths:
        step_width = width // splits
        split_parts.append(gains[:, start : start + step_width])
        start = start + step_width
    return split_parts


def shifted(field, down, right):
    image_height, width = (field.shape[1], field.shape[2])
    rows_pad, cols_pad = (abs(down), abs(right))
    padded = jnp.pad(field, ((0, 0), (rows_pad, rows_pad), (cols_pad, cols_pad), (0, 0)))
    return padded[
        :,
        rows_pad + down : rows_pad + down + image_height,
        cols_pad + right : cols_pad + right + width,
        :,
    ]


def conv_forward(field, kernel, spacing):
    total = jnp.zeros(field.shape[:-1] + (kernel.shape[2],), jnp.float32)
    for tap in range(9):
        moved = shifted(field, (tap // 3 - 1) * spacing, (tap % 3 - 1) * spacing)
        total = total + jnp.dot(moved, kernel[tap], preferred_element_type=jnp.float32)
    return total


def conv_input_back(grad, kernel, spacing):
    total = jnp.zeros(grad.shape[:-1] + (kernel.shape[1],), jnp.float32)
    for tap in range(9):
        product = jnp.dot(grad, kernel[tap].T, preferred_element_type=jnp.float32)
        total = total + shifted(product, -(tap // 3 - 1) * spacing, -(tap % 3 - 1) * spacing)
    return total


def conv_kernel_back(field, grad, spacing):
    return jnp.stack(
        [
            jnp.einsum(
                "ihwc,ihwd->cd",
                shifted(field, (tap // 3 - 1) * spacing, (tap % 3 - 1) * spacing),
                grad,
                preferred_element_type=jnp.float32,
            )
            for tap in range(9)
        ]
    )


def silu_slope(value):
    gate = jax.nn.sigmoid(value)
    return gate * (1.0 + value * (1.0 - gate))


def channel_sums(values):
    return values.reshape(-1, values.shape[-1]).sum(0)


def masked_norm_apply(items, extra):
    sends = []
    for value, mask, norm in items:
        sends = sends + [
            channel_sums(value * mask),
            channel_sums(value * value * mask),
            jnp.sum(mask) * jnp.ones((1,), jnp.float32),
        ]
    totals = lax.psum(tuple(sends + extra), "batch")
    results = []
    for index, (value, mask, norm) in enumerate(items):
        count = totals[3 * index + 2]
        mean = totals[3 * index] / count
        spread = totals[3 * index + 1] / count - mean * mean
        scaling = lax.rsqrt(spread + 1e-05)
        normed = (value - mean) * scaling
        results.append((norm[0] * normed + norm[1], normed, scaling, count, mask, norm[0]))
    return (results, totals[3 * len(items) :])


def norm_backward(items):
    sends = []
    for grad, kept in items:
        sends = sends + [channel_sums(grad), channel_sums(grad * kept[1])]
    totals = lax.psum(tuple(sends), "batch")
    results = []
    for index, (grad, kept) in enumerate(items):
        outcome, normed, scaling, count, mask, gamma = kept
        first_sum, second_sum = (totals[2 * index], totals[2 * index + 1])
        inner = grad - mask * (first_sum + normed * second_sum) / count
        results.append(gamma * scaling * inner)
    return (results, sends, totals)


def bin_tables(extent, bins, length):
    which = jnp.arange(bins, dtype=jnp.int32)[None, :, None]
    place = jnp.arange(length, dtype=jnp.int32)[None, None, :]
    edge = extent[:, None, None]
    lower = which * edge // bins
    upper = ((which + 1) * edge + bins - 1) // bins
    member = ((place >= lower) & (place < upper)).astype(jnp.float32)
    target = jnp.minimum(place * bins // edge, bins - 1)
    chosen = (target == which).astype(jnp.float32)
    return (member, chosen)


def spread_bins(merged, branch, tables, images):
    joined = [merged]
    for group, bins in enumerate(BIN_COUNTS):
        rows_in, cols_in, rows_pick, cols_pick, cell_count = tables[group]
        piece = branch[:, BIN_STARTS[group] : BIN_STARTS[group] + bins * bins].reshape(
            images, bins, bins, -1
        )
        joined.append(
            jnp.einsum(
                "ikh,ilw,iklc->ihwc",
                rows_pick.astype(jnp.bfloat16),
                cols_pick.astype(jnp.bfloat16),
                piece,
                preferred_element_type=jnp.float32,
            ).astype(jnp.bfloat16)
        )
    return jnp.concatenate(joined, axis=-1)


def pick_bins(d_joined, width, tables, images):
    branch_width = (d_joined.shape[-1] - width) // 4
    d_up = []
    for group, bins in enumerate(BIN_COUNTS):
        rows_in, cols_in, rows_pick, cols_pick, cell_count = tables[group]
        piece = d_joined[..., width + group * branch_width : width + (group + 1) * branch_width]
        d_up.append(
            jnp.einsum("ikh,ilw,ihwc->iklc", rows_pick, cols_pick, piece).reshape(
                images, bins * bins, -1
            )
        )
    return (d_joined[..., :width], jnp.concatenate(d_up, axis=1))


def gather_channels(field):
    return lax.all_gather(field, "tensor", axis=3, tiled=True)


def scatter_channels(field):
    return lax.psum_scatter(
        field.astype(jnp.bfloat16), "tensor", scatter_dimension=3, tiled=True
    ).astype(jnp.float32)


def local(features, labels, valid, sizes, params, first_moment, squared_mean, average):
    splits = lax.axis_size("tensor")
    owners = lax.axis_size("batch")
    images = features.shape[0]
    gathered = lax.all_gather(params.astype(jnp.bfloat16), "batch", axis=0, tiled=True)
    (
        w_reduce,
        w_short,
        w_middle,
        w_expand,
        w_branch,
        w_unite,
        w_classes,
        w_aux,
        w_aux_classes,
        gains,
    ) = unflatten(gathered, splits)
    norms = [(piece[0], piece[1]) for piece in gain_pieces(gains.astype(jnp.float32), splits)]
    rows_at = jnp.arange(MAP, dtype=jnp.int32)
    inside = (rows_at[None, :, None] < sizes[:, 0][:, None, None]) & (
        rows_at[None, None, :] < sizes[:, 1][:, None, None]
    )
    inside = inside.astype(jnp.float32)[..., None]
    counted = inside * valid.astype(jnp.float32)[..., None]
    labels_hot = (labels[..., None] == jnp.arange(NCLS, dtype=jnp.int32)).astype(jnp.float32)
    class_local = channel_sums(labels_hot * counted)
    whole = lax.all_gather(features, "tensor", axis=3, tiled=True)
    pre_reduce = jnp.dot(whole, w_reduce, preferred_element_type=jnp.float32)
    pre_short = jnp.dot(whole, w_short, preferred_element_type=jnp.float32)
    pre_aux = conv_forward(whole, w_aux, 1)
    leading_part, label_tally = masked_norm_apply(
        [
            (pre_reduce, inside, norms[0]),
            (pre_short, inside, norms[1]),
            (pre_aux, inside, norms[9]),
        ],
        [class_local],
    )
    class_pixel_counts = label_tally[0]
    hidden_one = jax.nn.silu(leading_part[0][0]).astype(jnp.bfloat16)
    aux_act = jax.nn.silu(leading_part[2][0]).astype(jnp.bfloat16)
    hidden_full = gather_channels(hidden_one)
    pre_middle = conv_forward(hidden_full, w_middle, 4)
    second, unused = masked_norm_apply([(pre_middle, inside, norms[2])], [])
    hidden_two = jax.nn.silu(second[0][0]).astype(jnp.bfloat16)
    hidden_two_full = gather_channels(hidden_two)
    pre_expand = jnp.dot(hidden_two_full, w_expand, preferred_element_type=jnp.float32)
    third, unused = masked_norm_apply([(pre_expand, inside, norms[3])], [])
    summed = third[0][0] + leading_part[1][0]
    merged = jax.nn.silu(summed).astype(jnp.bfloat16)
    tables = []
    pooled_list = []
    partial_list = []
    for group, bins in enumerate(BIN_COUNTS):
        rows_in, rows_pick = bin_tables(sizes[:, 0], bins, MAP)
        cols_in, cols_pick = bin_tables(sizes[:, 1], bins, MAP)
        cell_count = (
            jnp.sum(rows_in, axis=2)[:, :, None, None] * jnp.sum(cols_in, axis=2)[:, None, :, None]
        )
        tables.append((rows_in, cols_in, rows_pick, cols_pick, cell_count))
        pooled = (
            jnp.einsum(
                "ikh,ilw,ihwc->iklc",
                rows_in.astype(jnp.bfloat16),
                cols_in.astype(jnp.bfloat16),
                merged,
                preferred_element_type=jnp.float32,
            )
            / cell_count
        )
        pooled = pooled.astype(jnp.bfloat16).reshape(images, bins * bins, -1)
        pooled_list.append(pooled)
        partial_list.append(
            jnp.einsum("ipc,cd->ipd", pooled, w_branch[group], preferred_element_type=jnp.float32)
        )
    branch_pre = lax.psum_scatter(
        jnp.concatenate(partial_list, axis=1).astype(jnp.bfloat16),
        "tensor",
        scatter_dimension=2,
        tiled=True,
    ).astype(jnp.float32)
    branch_items = []
    for group, bins in enumerate(BIN_COUNTS):
        piece = branch_pre[:, BIN_STARTS[group] : BIN_STARTS[group] + bins * bins]
        branch_items.append(
            (piece, jnp.ones(piece.shape[:-1] + (1,), jnp.float32), norms[4 + group])
        )
    fourth, unused = masked_norm_apply(branch_items, [])
    branch_act = jnp.concatenate([jax.nn.silu(kept[0]) for kept in fourth], axis=1).astype(
        jnp.bfloat16
    )
    merged_full, branch_full = (
        lax.all_gather(merged, "tensor", axis=3, tiled=True),
        lax.all_gather(branch_act, "tensor", axis=2, tiled=True),
    )
    joined = spread_bins(merged_full, branch_full, tables, images)
    pre_unite = conv_forward(joined, w_unite, 1)
    fifth, unused = masked_norm_apply([(pre_unite, inside, norms[8])], [])
    united = jax.nn.silu(fifth[0][0]).astype(jnp.bfloat16)
    logit_main, logit_aux = (
        lax.psum_scatter(
            jnp.dot(united, w_classes, preferred_element_type=jnp.float32).astype(jnp.bfloat16),
            "tensor",
            scatter_dimension=1,
            tiled=True,
        ).astype(jnp.float32),
        lax.psum_scatter(
            jnp.dot(aux_act, w_aux_classes, preferred_element_type=jnp.float32).astype(
                jnp.bfloat16
            ),
            "tensor",
            scatter_dimension=1,
            tiled=True,
        ).astype(jnp.float32),
    )
    total_valid = jnp.sum(class_pixel_counts)
    class_weight = total_valid / (NCLS * class_pixel_counts + total_valid)
    loss_weight = jnp.sum(class_pixel_counts * class_weight)
    cell_weight = jnp.sum(labels_hot * class_weight, axis=-1, keepdims=True) * counted
    band_rows = labels.shape[1] // splits
    band_start = lax.axis_index("tensor") * band_rows
    hot_band = lax.dynamic_slice_in_dim(labels_hot, band_start, band_rows, 1)
    weight_band = lax.dynamic_slice_in_dim(cell_weight, band_start, band_rows, 1)
    log_main = jax.nn.log_softmax(logit_main, axis=-1)
    log_aux = jax.nn.log_softmax(logit_aux, axis=-1)
    loss_cells = -jnp.sum(hot_band * (log_main + 0.4 * log_aux), axis=-1, keepdims=True)
    loss_local = jnp.sum(weight_band * loss_cells)
    band_main = (weight_band * (jnp.exp(log_main) - hot_band) / loss_weight).astype(jnp.bfloat16)
    band_aux = (0.4 * weight_band * (jnp.exp(log_aux) - hot_band) / loss_weight).astype(
        jnp.bfloat16
    )
    grad_main, grad_aux = (
        lax.all_gather(band_main, "tensor", axis=1, tiled=True),
        lax.all_gather(band_aux, "tensor", axis=1, tiled=True),
    )
    reduced = {}

    def settle(index, value):
        reduced[index] = value

    settle(6, jnp.einsum("ihwc,ihwk->ck", united, grad_main, preferred_element_type=jnp.float32))
    settle(8, jnp.einsum("ihwc,ihwk->ck", aux_act, grad_aux, preferred_element_type=jnp.float32))
    d_united = jnp.dot(grad_main, w_classes.T, preferred_element_type=jnp.float32) * silu_slope(
        fifth[0][0]
    )
    d_aux = jnp.dot(grad_aux, w_aux_classes.T, preferred_element_type=jnp.float32) * silu_slope(
        leading_part[2][0]
    )
    back_one, sums_one, totals_one = norm_backward([(d_united, fifth[0]), (d_aux, leading_part[2])])
    unite_shift_grad = totals_one[0]
    d_unite_pre = back_one[0].astype(jnp.bfloat16)
    d_aux_pre = back_one[1].astype(jnp.bfloat16)
    settle(5, conv_kernel_back(joined, d_unite_pre, 1))
    d_merged, d_branch = pick_bins(conv_input_back(d_unite_pre, w_unite, 1), C_OUT, tables, images)
    d_merged, d_branch = (
        lax.psum_scatter(
            d_merged.astype(jnp.bfloat16), "tensor", scatter_dimension=3, tiled=True
        ).astype(jnp.float32),
        lax.psum_scatter(
            d_branch.astype(jnp.bfloat16), "tensor", scatter_dimension=2, tiled=True
        ).astype(jnp.float32),
    )
    settle(7, conv_kernel_back(whole, d_aux_pre, 1))
    branch_back = []
    for group, bins in enumerate(BIN_COUNTS):
        piece = d_branch[:, BIN_STARTS[group] : BIN_STARTS[group] + bins * bins]
        branch_back.append((piece * silu_slope(fourth[group][0]), fourth[group]))
    back_two, sums_two, unused = norm_backward(branch_back)
    d_branch_pre = jnp.concatenate(back_two, axis=1).astype(jnp.bfloat16)
    d_branch_full = lax.all_gather(d_branch_pre, "tensor", axis=2, tiled=True)
    branch_grads = []
    for group, bins in enumerate(BIN_COUNTS):
        rows_in, cols_in, rows_pick, cols_pick, cell_count = tables[group]
        piece = d_branch_full[:, BIN_STARTS[group] : BIN_STARTS[group] + bins * bins]
        branch_grads.append(
            jnp.einsum("ipc,ipd->cd", pooled_list[group], piece, preferred_element_type=jnp.float32)
        )
        d_pooled = jnp.dot(piece, w_branch[group].T, preferred_element_type=jnp.float32).reshape(
            images, bins, bins, -1
        )
        d_merged = d_merged + jnp.einsum(
            "ikh,ilw,iklc->ihwc", rows_in, cols_in, d_pooled / cell_count
        )
    settle(4, jnp.stack(branch_grads))
    d_summed = d_merged * silu_slope(summed)
    back_three, sums_three, unused = norm_backward(
        [(d_summed, third[0]), (d_summed, leading_part[1])]
    )
    d_expand_pre = back_three[0].astype(jnp.bfloat16)
    d_short_pre = back_three[1].astype(jnp.bfloat16)
    settle(
        3,
        jnp.einsum(
            "ihwc,ihwd->cd", hidden_two_full, d_expand_pre, preferred_element_type=jnp.float32
        ),
    )
    settle(1, jnp.einsum("ihwc,ihwd->cd", whole, d_short_pre, preferred_element_type=jnp.float32))
    d_two = scatter_channels(jnp.dot(d_expand_pre, w_expand.T, preferred_element_type=jnp.float32))
    back_four, sums_four, unused = norm_backward([(d_two * silu_slope(second[0][0]), second[0])])
    d_middle_pre = back_four[0].astype(jnp.bfloat16)
    settle(2, conv_kernel_back(hidden_full, d_middle_pre, 4))
    d_one = scatter_channels(conv_input_back(d_middle_pre, w_middle, 4))
    back_five, sums_five, unused = norm_backward(
        [(d_one * silu_slope(leading_part[0][0]), leading_part[0])]
    )
    settle(
        0,
        jnp.einsum(
            "ihwc,ihwd->cd",
            whole,
            back_five[0].astype(jnp.bfloat16),
            preferred_element_type=jnp.float32,
        ),
    )
    beta_grads = (
        [sums_five[0], sums_three[2], sums_four[0], sums_three[0]]
        + [sums_two[2 * g] for g in range(4)]
        + [sums_one[0], sums_one[2]]
    )
    gamma_grads = (
        [sums_five[1], sums_three[3], sums_four[1], sums_three[1]]
        + [sums_two[2 * g + 1] for g in range(4)]
        + [sums_one[1], sums_one[3]]
    )
    settle(9, jnp.stack([jnp.concatenate(gamma_grads), jnp.concatenate(beta_grads)]))
    ordered = [reduced[index] for index in range(10)]
    grad_share = lax.psum_scatter(
        jnp.concatenate([part.reshape(owners, -1) for part in ordered], axis=1),
        "batch",
        scatter_dimension=0,
        tiled=True,
    )
    square_all, loss_sum = lax.psum(
        (jnp.sum(grad_share * grad_share), loss_local), ("batch", "tensor")
    )
    grad_norm = jnp.sqrt(square_all)
    clipped = grad_share * jnp.minimum(1.0, 0.05 / (grad_norm + 1e-06))
    new_first = 0.5 * first_moment + 0.5 * clipped
    new_second = 0.5 * squared_mean + 0.5 * clipped * clipped
    keep = 1.0 - 0.5**STEP
    new_params = params - 0.01 * (
        new_first / keep / (jnp.sqrt(new_second / keep) + 1e-08) + 0.01 * params
    )
    new_average = 0.999 * average + 0.001 * new_params
    return (
        new_params,
        new_first,
        new_second,
        new_average,
        new_params.astype(jnp.bfloat16),
        grad_norm,
        loss_sum,
        loss_weight,
        unite_shift_grad,
    )


CELLS = MAP * MAP
EDGE = 104
BATCH = "batch"
TENSOR = "tensor"
GROUP_ROWS = ((0, 1), (1, 5), (5, 14), (14, 50))
BINS = 64
BF = jnp.bfloat16
F32 = jnp.float32
MESH = pl.DeviceIdType.MESH
HALF = 4
OWNERS = 8
SPLITS = 4
MERGED = 4
SLOTS = 5


def scratch_plan():
    plan = dict(
        w_r=((1024, 128), BF),
        w_s=((1024, 512), BF),
        w_m=((4608, 128), BF),
        w_e=((512, 512), BF),
        w_b=((2048, 512), BF),
        w_u=((18432, 128), BF),
        w_own=((4608, 128), BF),
        w_a=((4608, 128), BF),
        w_pair=((1024, 640), BF),
        w_c=((128, 256), BF),
        w_ac=((64, 256), F32),
        gain_in=((OWNERS, 32, 128), F32),
        whole=((SPLITS, CELLS, 256), BF),
        ins=((CELLS, 128), F32),
        col=((CELLS, 128), F32),
        lab=((CELLS, 128), F32),
        table=((BINS, CELLS), F32),
        pool=((BINS, CELLS), BF),
        pick=((BINS, CELLS), BF),
        cells_in=((BINS, 128), F32),
        pad=((9, CELLS + 2 * EDGE, 128), F32),
        grad_pad=((CELLS + 2 * EDGE, 128), F32),
        pre_r=((CELLS, 128), F32),
        pre_s=((CELLS, 512), F32),
        pre_a=((CELLS, 128), F32),
        pre_m=((CELLS, 128), F32),
        pre_e=((CELLS, 512), F32),
        pre_u=((CELLS, 128), F32),
        act_a=((CELLS, 128), BF),
        h1=((SPLITS, CELLS, 128), BF),
        h2=((SPLITS, CELLS, 128), BF),
        joined=((SPLITS, CELLS, 512), BF),
        joined_t=((SPLITS, 512, CELLS), BF),
        pooled=((BINS, 512), BF),
        part_b=((SPLITS, BINS, 128), BF),
        recv_b=((SPLITS, BINS, 128), BF),
        all_b=((OWNERS, BINS, 128), BF),
        act_b=((SPLITS, OWNERS * BINS, 128), BF),
        zsum=((2, OWNERS * BINS, 128), F32),
        z_send=((OWNERS, 2, BINS, 128), BF),
        z_recv=((OWNERS, 2, BINS, 128), BF),
        united=((CELLS, 128), BF),
        logit_send=((CELLS, 512), BF),
        logit_recv=((SPLITS, 144, 512), BF),
        slope_in=((SPLITS, 144, 512), BF),
        d_f=((CELLS, 128), F32),
        d_f2=((CELLS, 128), F32),
        cat_u=((CELLS, 1152), BF),
        cat_a=((CELLS, 640), BF),
        dz_send=((9, BINS, 128), BF),
        dz_recv=((OWNERS, 2, BINS, 128), BF),
        d_act_send=((SPLITS, OWNERS * BINS, 128), BF),
        d_act_recv=((SPLITS, OWNERS * BINS, 128), BF),
        d_img_send=((OWNERS, BINS, 128), BF),
        d_img_recv=((OWNERS, BINS, 128), BF),
        d_bp=((SPLITS, BINS, 128), BF),
        dm_near=((2, CELLS, 512), BF),
        dm_far=((CELLS, 512), BF),
        d_sum=((CELLS, 512), F32),
        d_e=((CELLS, 512), BF),
        d_s=((CELLS, 512), BF),
        dh_send=((SPLITS, CELLS, 128), BF),
        dh_recv=((2, SPLITS, CELLS, 128), BF),
        d_low=((CELLS, 128), BF),
        end_t=((SPLITS, 8, 128), F32),
    )
    for name, rows in SYNCS.items():
        plan["sync_" + name] = ((OWNERS, rows, 128), F32)
    for name, (rows, lanes, kind) in PARTS.items():
        plan["first_" + name] = ((HALF, rows, lanes), kind)
        plan["second_" + name] = ((HALF - 1, rows, lanes), kind)
    plan["first_u"] = ((HALF, SLOTS, 512, 128), BF)
    plan["second_u"] = ((HALF - 1, SLOTS, 512, 128), BF)
    return plan


SYNCS = dict(one=16, two=8, three=8, five=8, b1=8, b3=8, b4=16, b5=8, b6=8, end=8)
PARTS = dict(
    r=(128, 128, BF),
    s=(128, 512, BF),
    m=(576, 128, BF),
    e=(64, 512, BF),
    b=(256, 512, BF),
    a=(576, 128, BF),
    c=(16, 256, BF),
    ac=(8, 256, F32),
)
SEMAPHORES = 1100


class Refs:
    pass


def fold(value):
    return value.reshape(-1, 8, value.shape[-1]).sum(0)


def total(value):
    return jnp.sum(value, axis=0, keepdims=True)


def wide(value, times):
    return jnp.concatenate([value] * times, axis=1)


def dot(left, right):
    return jnp.dot(left, right, preferred_element_type=F32)


def dot_nt(left, right):
    return lax.dot_general(left, right, (((1,), (1,)), ((), ())), preferred_element_type=F32)


def dot_tn(left, right):
    return lax.dot_general(left, right, (((0,), (0,)), ((), ())), preferred_element_type=F32)


def loop(count, body):
    def step(k, carry):
        body(k)
        return carry

    lax.fori_loop(0, count, step, 0)


def rows_at(k, block):
    return pl.ds(pl.multiple_of(k * block, block), block)


def step_kernel(names, *refs):
    (
        sizes, lab_in, feat, gain_own, p_r, p_s, p_m, p_e, p_b, p_u, p_a, p_c, p_ac,
        o_r, o_s, o_m, o_e, o_b, o_u, o_a, o_c, o_ac, o_gain, o_misc,
    ) = refs[:24]
    v = Refs()
    for name, ref in zip(names, refs[24:]):
        setattr(v, name, ref)
    sems = refs[-1]
    me = lax.axis_index(BATCH)
    t = lax.axis_index(TENSOR)
    partner = me + 1 - 2 * lax.rem(me, 2)
    t_core = t + 1 - 2 * lax.rem(t, 2)
    t_x = lax.rem(t + 2, SPLITS)
    t_diag = lax.rem(t_core + 2, SPLITS)
    taken = [0]

    def take(count):
        start = taken[0]
        taken[0] = start + count
        assert taken[0] <= SEMAPHORES
        return start

    def far_peer(base, step):
        return lax.rem(base + 2 * step, OWNERS)

    def remote(src, dst, send, recv, device):
        return pltpu.make_async_remote_copy(
            src_ref=src,
            dst_ref=dst,
            send_sem=sems.at[send],
            recv_sem=sems.at[recv],
            device_id=device,
            device_id_type=MESH,
        )

    late = []

    barrier = pltpu.get_barrier_semaphore()
    for k in range(1, OWNERS):
        pl.semaphore_signal(
            barrier, inc=1, device_id={BATCH: lax.rem(me + k, OWNERS)}, device_id_type=MESH
        )
    for k in range(1, SPLITS):
        pl.semaphore_signal(
            barrier, inc=1, device_id={TENSOR: lax.rem(t + k, SPLITS)}, device_id_type=MESH
        )
    pl.semaphore_wait(barrier, OWNERS + SPLITS - 2)

    class Gather:
        def __init__(self, piece, full, rows):
            self.piece, self.full, self.rows = piece, full, rows
            self.near_s, self.far_s, self.pass_s = take(1), take(HALF), take(HALF)
            self.recv, self.keep = take(OWNERS), take(1)

        def at(self, owner):
            if self.rows is None:
                return self.full.at[owner]
            return self.full.at[rows_at(owner, self.rows), :]

        def local(self):
            return pltpu.make_async_copy(self.piece, self.at(me), sems.at[self.keep])

        def near(self):
            return remote(
                self.piece, self.at(me), self.near_s, self.recv + me, {BATCH: partner}
            )

        def far(self, step):
            return remote(
                self.piece,
                self.at(me),
                self.far_s + step,
                self.recv + me,
                {BATCH: far_peer(me, step)},
            )

        def passed(self, step, base):
            source = far_peer(base, step)
            return remote(
                self.at(source),
                self.at(source),
                self.pass_s + step,
                self.recv + source,
                {BATCH: partner},
            )

        def start(self):
            self.local().start()
            for step in range(1, HALF):
                self.far(step).start()
            self.near().start()

        def forward(self):
            for step in range(1, HALF):
                self.passed(step, me).wait_recv()
                self.passed(step, me).start()

        def finish(self):
            for step in range(HALF):
                self.passed(step, partner).wait_recv()
            self.local().wait()
            self.near().wait_send()
            for step in range(1, HALF):
                self.far(step).wait_send()

        def drain(self):
            for step in range(1, HALF):
                self.passed(step, me).wait_send()

    g_gain = Gather(gain_own, v.gain_in, None)
    g_r = Gather(p_r, v.w_r, 128)
    g_s = Gather(p_s, v.w_s, 128)
    g_a = Gather(p_a, v.w_a, 576)
    g_m = Gather(p_m, v.w_m, 576)
    g_e = Gather(p_e, v.w_e, 64)
    g_b = Gather(p_b, v.w_b, 256)
    g_c = Gather(p_c, v.w_c, 16)
    g_ac = Gather(p_ac, v.w_ac, 8)

    def chunk_of(owner, j):
        return lax.rem(owner + j, 8)

    def merged_rows(owner, j):
        tap = owner + lax.div(owner + j, 8)
        return pl.ds(pl.multiple_of((tap * MERGED + chunk_of(owner, j)) * 512, 512), 512)

    def each_merged(owner, body):
        def step(j):
            pl.when(chunk_of(owner, j) < MERGED)(lambda: body(j))

        loop(9, step)

    class GatherUnite:
        def __init__(self):
            self.near_s, self.far_s, self.pass_s = take(9), take(9 * HALF), take(9 * HALF)
            self.recv, self.keep, self.keep_all = take(9 * OWNERS), take(9), take(1)

        def source(self, j):
            return p_u.at[rows_at(j, 512), :]

        def full(self, owner, j):
            return v.w_u.at[merged_rows(owner, j), :]

        def local(self, j):
            return pltpu.make_async_copy(
                self.source(j), self.full(me, j), sems.at[self.keep + j]
            )

        def whole(self):
            return pltpu.make_async_copy(p_u, v.w_own, sems.at[self.keep_all])

        def near(self, j):
            return remote(
                self.source(j),
                self.full(me, j),
                self.near_s + j,
                self.recv + me * 9 + j,
                {BATCH: partner},
            )

        def far(self, step, j):
            return remote(
                self.source(j),
                self.full(me, j),
                self.far_s + step * 9 + j,
                self.recv + me * 9 + j,
                {BATCH: far_peer(me, step)},
            )

        def passed(self, step, j, base):
            source = far_peer(base, step)
            return remote(
                self.full(source, j),
                self.full(source, j),
                self.pass_s + step * 9 + j,
                self.recv + source * 9 + j,
                {BATCH: partner},
            )

        def start(self):
            self.whole().start()

            def begin(j):
                self.local(j).start()
                for step in range(1, HALF):
                    self.far(step, j).start()
                self.near(j).start()

            each_merged(me, begin)

        def forward(self, step):
            def go(j):
                self.passed(step, j, me).wait_recv()
                self.passed(step, j, me).start()

            each_merged(far_peer(me, step), go)

        def finish(self):
            for step in range(HALF):
                each_merged(
                    far_peer(partner, step),
                    lambda j, step=step: self.passed(step, j, partner).wait_recv(),
                )

            def end(j):
                self.local(j).wait()
                self.near(j).wait_send()
                for step in range(1, HALF):
                    self.far(step, j).wait_send()

            each_merged(me, end)

        def drain(self):
            for step in range(1, HALF):
                each_merged(
                    far_peer(me, step),
                    lambda j, step=step: self.passed(step, j, me).wait_send(),
                )

    g_u = GatherUnite()

    class Sync:
        def __init__(self, buf):
            self.buf = buf
            self.send, self.recv = take(OWNERS), take(OWNERS)

        def copy(self, k, slot):
            return remote(
                self.buf.at[slot],
                self.buf.at[slot],
                self.send + k,
                self.recv + slot,
                {BATCH: lax.rem(me + k, OWNERS)},
            )

        def start(self, rows):
            for index, row in enumerate(rows):
                self.buf[me, index : index + 1, :] = row
            for index in range(len(rows), self.buf.shape[1]):
                self.buf[me, index : index + 1, :] = jnp.zeros((1, 128), F32)
            for k in range(1, OWNERS):
                self.copy(k, me).start()

        def wait(self):
            for k in range(1, OWNERS):
                self.copy(k, lax.rem(me + k, OWNERS)).wait_recv()
            for k in range(1, OWNERS):
                self.copy(k, me).wait_send()
            value = self.buf[0]
            for slot in range(1, OWNERS):
                value = value + self.buf[slot]
            return value

    class Spread:

        def __init__(self, buf):
            self.buf = buf
            self.send, self.recv = take(SPLITS), take(SPLITS)

        def copy(self, k, slot):
            return remote(
                self.buf.at[slot],
                self.buf.at[slot],
                self.send + k,
                self.recv + slot,
                {TENSOR: lax.rem(t + k, SPLITS)},
            )

        def start(self):
            for k in range(1, SPLITS):
                self.copy(k, t).start()

        def wait(self):
            for k in range(1, SPLITS):
                self.copy(k, lax.rem(t + k, SPLITS)).wait_recv()
            for k in range(1, SPLITS):
                self.copy(k, t).wait_send()

    class Exchange:

        def __init__(self, axis, count, part, into):
            self.axis, self.count, self.part, self.into = axis, count, part, into
            self.mine = me if axis == BATCH else t
            self.send, self.recv = take(count), take(count)

        def copy(self, k, slot):
            other = lax.rem(self.mine + k, self.count)
            return remote(
                self.part(other),
                self.into(slot),
                self.send + k,
                self.recv + slot,
                {self.axis: other},
            )

        def start(self):
            for k in range(1, self.count):
                self.copy(k, self.mine).start()

        def wait(self):
            for k in range(1, self.count):
                self.copy(k, lax.rem(self.mine + k, self.count)).wait_recv()
            for k in range(1, self.count):
                self.copy(k, self.mine).wait_send()

    feat_keep = take(1)
    feat_local = pltpu.make_async_copy(feat, v.whole.at[t], sems.at[feat_keep])
    feat_spread = Exchange(TENSOR, SPLITS, lambda other: feat, lambda slot: v.whole.at[slot])
    for item in (g_gain, g_r, g_s, g_a):
        item.start()
    feat_local.start()
    feat_spread.start()

    high, across = sizes[0, 0], sizes[0, 1]
    place = lax.broadcasted_iota(jnp.int32, (CELLS, 128), 0).astype(F32)
    row_of = jnp.floor((place + 0.5) / MAP)
    col_of = place - MAP * row_of
    within = (row_of < high.astype(F32)) & (col_of < across.astype(F32))
    v.ins[...] = jnp.where(within, 1.0, 0.0)
    v.col[...] = col_of
    v.lab[...] = jnp.where(within, lab_in[...], -1.0)
    v.table[...] = jnp.zeros((BINS, CELLS), F32)
    lane_place = lax.broadcasted_iota(jnp.int32, (1, CELLS), 1).astype(F32)
    lane_row = jnp.floor((lane_place + 0.5) / MAP)
    lane_col = lane_place - MAP * lane_row

    def ranges(extent, bins, where):
        inside, chosen, counts = [], [], []
        for k in range(bins):
            low = lax.div(k * extent, bins)
            top = lax.div((k + 1) * extent + (bins - 1), bins)
            member = (where >= low.astype(F32)) & (where < top.astype(F32))
            inside.append(jnp.where(member, 1.0, 0.0))
            picked = where * bins >= (k * extent).astype(F32)
            if k < bins - 1:
                picked = picked & (where * bins < ((k + 1) * extent).astype(F32))
            chosen.append(jnp.where(picked, 1.0, 0.0))
            counts.append(top - low)
        return inside, chosen, counts

    picks = []
    v.cells_in[...] = jnp.ones((BINS, 128), F32)
    for group, bins in enumerate(BIN_COUNTS):
        r_in, r_pick, r_count = ranges(high, bins, lane_row)
        c_in, c_pick, c_count = ranges(across, bins, lane_col)
        for a in range(bins):
            for b in range(bins):
                spot = BIN_STARTS[group] + a * bins + b
                v.table[spot : spot + 1, :] = r_in[a] * c_in[b]
                v.cells_in[spot : spot + 1, :] = jnp.full(
                    (1, 128), (r_count[a] * c_count[b]).astype(F32)
                )
                picks.append((spot, r_pick[a] * c_pick[b]))
    v.pool[...] = v.table[...].astype(BF)
    for spot, value in picks:
        v.table[spot : spot + 1, :] = value
    v.pick[...] = v.table[...].astype(BF)
    zeros_edge = jnp.zeros((EDGE, 128), F32)
    for tap in range(9):
        v.pad[tap, 0:EDGE, :] = zeros_edge
        v.pad[tap, EDGE + CELLS :, :] = zeros_edge
    v.grad_pad[0:EDGE, :] = zeros_edge
    v.grad_pad[EDGE + CELLS :, :] = zeros_edge
    lanes = lax.broadcasted_iota(jnp.int32, (1, 256), 1).astype(F32)
    counts = jnp.zeros((8, 256), F32)
    for k in range(0, CELLS, 96):
        counts = counts + fold(
            jnp.where(wide(v.lab[k : k + 96, :], 2) == lanes, 1.0, 0.0)
        )
    class_local = total(counts)
    cells_local = jnp.full((1, 128), (high * across).astype(F32))
    left_half = lax.broadcasted_iota(jnp.int32, (64, 128), 1) < 64

    for item in (g_gain, g_r, g_s, g_a):
        item.forward()
    for item in (g_m, g_e, g_b, g_c, g_ac):
        item.start()
    g_u.start()
    for item in (g_gain, g_r, g_s, g_a):
        item.finish()
    feat_local.wait()
    feat_spread.wait()
    gains = v.gain_in[0]
    for slot in range(1, OWNERS):
        gains = gains + v.gain_in[slot]

    def gamma(row, width=1):
        return jnp.concatenate([gains[row + k : row + k + 1] for k in range(width)], axis=1)

    def beta(row, width=1):
        return gamma(16 + row, width)

    def unpack(chunk):
        for pair in range(5):
            even = v.w_a[rows_at(2 * pair * 8 + chunk, 64), :].astype(F32)
            if pair < 4:
                odd = v.w_a[rows_at((2 * pair + 1) * 8 + chunk, 64), :].astype(F32)
            else:
                odd = jnp.zeros((64, 128), F32)
            low = jnp.where(left_half, even, pltpu.roll(odd, 64, 1))
            top = jnp.where(left_half, pltpu.roll(even, 64, 1), odd)
            v.w_pair[rows_at(2 * chunk, 64), pair * 128 : pair * 128 + 128] = low.astype(BF)
            v.w_pair[rows_at(2 * chunk + 1, 64), pair * 128 : pair * 128 + 128] = top.astype(BF)

    loop(8, unpack)

    def whole_feat():
        return jnp.concatenate([v.whole[k] for k in range(SPLITS)], axis=1)

    v.pre_r[...] = dot(whole_feat(), v.w_r[...])
    for k in range(0, 512, 256):
        v.pre_s[:, k : k + 256] = dot(whole_feat(), v.w_s[:, k : k + 256])
    for pair in (0, 2):
        value = dot(whole_feat(), v.w_pair[:, pair * 128 : pair * 128 + 256])
        v.pad[pair, EDGE : EDGE + CELLS, :] = value[:, :128]
        v.pad[pair + 1, EDGE : EDGE + CELLS, :] = value[:, 128:]
    v.pad[4, EDGE : EDGE + CELLS, :] = dot(whole_feat(), v.w_pair[:, 512:640])

    def offset(tap, spacing):
        return ((tap // 3 - 1) * MAP + (tap % 3 - 1)) * spacing

    def col_mask(at, right):
        where = v.col[at, :] + float(right)
        return jnp.where((where >= 0.0) & (where < float(MAP)), 1.0, 0.0)

    BLOCK = 72

    def shift_sum(taps, spacing, at, slot_of):
        out = None
        for b in (-1, 0, 1):
            part = None
            for tap in taps:
                if tap % 3 - 1 != b:
                    continue
                start = EDGE + at + offset(tap, spacing)
                value = v.pad[slot_of(tap), start : start + BLOCK, :]
                part = value if part is None else part + value
            if part is None:
                continue
            if b:
                part = part * col_mask(slice(at, at + BLOCK), b * spacing)
            out = part if out is None else out + part
        return out

    left_wide = lax.broadcasted_iota(jnp.int32, (BLOCK, 128), 1) < 64
    for at in range(0, CELLS, BLOCK):
        even = shift_sum((0, 2, 4, 6, 8), 1, at, lambda tap: tap // 2)
        odd = shift_sum((1, 3, 5, 7), 1, at, lambda tap: tap // 2)
        v.pre_a[at : at + BLOCK, :] = jnp.where(left_wide, even + pltpu.roll(odd, 64, 1), 0.0)

    def masked_sums(ref):
        width = ref.shape[1]

        def step(k, carry):
            at = rows_at(k, 96)
            value = ref[at, :]
            kept = value * (v.ins[at, :] if width == 128 else wide(v.ins[at, :], width // 128))
            return (carry[0] + fold(kept), carry[1] + fold(kept * value))

        zero = jnp.zeros((8, width), F32)
        sums = lax.fori_loop(0, 6, step, (zero, zero))
        return total(sums[0]), total(sums[1])

    def split_rows(value):
        return [value[:, k : k + 128] for k in range(0, value.shape[1], 128)]

    def join_rows(value, row, count):
        return jnp.concatenate([value[row + k : row + k + 1] for k in range(count)], axis=1)

    def moments(first, second, count):
        mean = first / count
        return mean, lax.rsqrt(second / count - mean * mean + 1e-05)

    sync = Sync(v.sync_one)
    r1, r2 = masked_sums(v.pre_r)
    s1, s2 = masked_sums(v.pre_s)
    a1, a2 = masked_sums(v.pre_a)
    sync.start(
        [r1, r2] + split_rows(s1) + split_rows(s2) + [a1, a2, cells_local] + split_rows(class_local)
    )
    g_m.forward()
    sums = sync.wait()
    count = sums[12:13]
    count4 = wide(count, 4)
    norm_r = moments(sums[0:1], sums[1:2], count)
    norm_s = moments(join_rows(sums, 2, 4), join_rows(sums, 6, 4), count4)
    norm_a = moments(sums[10:11], sums[11:12], count)
    class_count = join_rows(sums, 13, 2)

    def normed(ref, at, norm):
        return (ref[at, :] - norm[0]) * norm[1]

    spread_1 = Spread(v.h1)

    def make_h1(k):
        at = rows_at(k, 96)
        v.h1[t, at, :] = jax.nn.silu(gamma(0) * normed(v.pre_r, at, norm_r) + beta(0)).astype(BF)

    loop(6, make_h1)
    spread_1.start()

    def make_a(k):
        at = rows_at(k, 96)
        v.act_a[at, :] = jax.nn.silu(gamma(15) * normed(v.pre_a, at, norm_a) + beta(15)).astype(BF)

    loop(6, make_a)
    g_e.forward()
    g_m.finish()
    spread_1.wait()

    def full_h(ref):
        return jnp.concatenate([ref[k] for k in range(SPLITS)], axis=1)

    def middle(tap):
        v.pad[tap, EDGE : EDGE + CELLS, :] = dot(full_h(v.h1), v.w_m[rows_at(tap, 512), :])

    loop(9, middle)
    for at in range(0, CELLS, BLOCK):
        v.pre_m[at : at + BLOCK, :] = shift_sum(range(9), 4, at, lambda tap: tap)
    sync = Sync(v.sync_two)
    sync.start(list(masked_sums(v.pre_m)))
    g_e.finish()
    sums = sync.wait()
    norm_m = moments(sums[0:1], sums[1:2], count)
    spread_2 = Spread(v.h2)

    def make_h2(k):
        at = rows_at(k, 96)
        v.h2[t, at, :] = jax.nn.silu(gamma(5) * normed(v.pre_m, at, norm_m) + beta(5)).astype(BF)

    loop(6, make_h2)
    spread_2.start()
    g_b.forward()
    spread_2.wait()
    for k in range(0, 512, 256):
        v.pre_e[:, k : k + 256] = dot(full_h(v.h2), v.w_e[:, k : k + 256])
    sync = Sync(v.sync_three)
    e1, e2 = masked_sums(v.pre_e)
    sync.start(split_rows(e1) + split_rows(e2))
    g_c.forward()
    g_ac.forward()
    sums = sync.wait()
    norm_e = moments(join_rows(sums, 0, 4), join_rows(sums, 4, 4), count4)

    def summed(at):
        return (
            gamma(6, 4) * normed(v.pre_e, at, norm_e)
            + beta(6, 4)
            + gamma(1, 4) * normed(v.pre_s, at, norm_s)
            + beta(1, 4)
        )

    def make_merged(k):
        at = rows_at(k, 48)
        v.joined[t, at, :] = jax.nn.silu(summed(at)).astype(BF)

    loop(12, make_merged)

    j_send, j_recv = take(3), take(SPLITS)

    def joined_copy(k, slot, device):
        return remote(
            v.joined.at[slot], v.joined.at[slot], j_send + k, j_recv + slot, {TENSOR: device}
        )

    joined_copy(0, t, t_x).start()
    joined_copy(1, t, t_core).start()

    bin_row = lax.broadcasted_iota(jnp.int32, (BINS, 1), 0)

    def group_mask(group, shape=None):
        low, top = GROUP_ROWS[group]
        kept = jnp.where((bin_row >= low) & (bin_row < top), 1.0, 0.0)
        return kept if shape is None else jnp.broadcast_to(kept, shape)

    cells_in = wide(v.cells_in[...], 4)
    pooled = dot(v.pool[...], v.joined[t]) / cells_in
    v.pooled[...] = pooled.astype(BF)
    g_b.finish()
    part = jnp.zeros((BINS, 512), F32)
    for group in range(4):
        rows = (v.pooled[...].astype(F32) * group_mask(group)).astype(BF)
        part = part + dot(rows, v.w_b[group * 512 : group * 512 + 512, :])
    for k in range(SPLITS):
        v.part_b[k] = part[:, k * 128 : k * 128 + 128].astype(BF)
    v.recv_b[t] = v.part_b[t]
    ex = Exchange(TENSOR, SPLITS, lambda o: v.part_b.at[o], lambda s: v.recv_b.at[s])
    ex.start()
    joined_copy(0, t_x, t_x).wait_recv()
    joined_copy(2, t_x, t_core).start()
    ex.wait()
    own_b = v.recv_b[0].astype(F32)
    for k in range(1, SPLITS):
        own_b = own_b + v.recv_b[k].astype(F32)
    v.all_b[me] = own_b.astype(BF)
    ex = Exchange(BATCH, OWNERS, lambda o: v.all_b.at[me], lambda s: v.all_b.at[s])
    ex.start()
    g_u.forward(1)
    ex.wait()
    all_b = [v.all_b[k].astype(F32) for k in range(OWNERS)]
    sum_b, square_b = all_b[0], all_b[0] * all_b[0]
    for k in range(1, OWNERS):
        sum_b = sum_b + all_b[k]
        square_b = square_b + all_b[k] * all_b[k]
    mean_b = jnp.zeros((BINS, 128), F32)
    scale_b = jnp.zeros((BINS, 128), F32)
    gamma_b = jnp.zeros((BINS, 128), F32)
    beta_b = jnp.zeros((BINS, 128), F32)
    count_b = jnp.zeros((BINS, 1), F32)
    for group, bins in enumerate(BIN_COUNTS):
        kept = group_mask(group)
        size = float(OWNERS * bins * bins)
        mean, scaling = moments(total(sum_b * kept), total(square_b * kept), size)
        mean_b = mean_b + kept * mean
        scale_b = scale_b + kept * scaling
        gamma_b = gamma_b + kept * gamma(10 + group)
        beta_b = beta_b + kept * beta(10 + group)
        count_b = count_b + kept / size
    spread_b = Spread(v.act_b)
    for k in range(OWNERS):
        out = gamma_b * ((all_b[k] - mean_b) * scale_b) + beta_b
        v.act_b[t, k * BINS : k * BINS + BINS, :] = jax.nn.silu(out).astype(BF)
    spread_b.start()
    g_u.forward(2)
    spread_b.wait()
    g_u.whole().wait()
    row_512 = lax.broadcasted_iota(jnp.int32, (OWNERS * BINS, 1), 0) & (BINS - 1)
    group_id = jnp.where(
        row_512 < 1, 0, jnp.where(row_512 < 5, 1, jnp.where(row_512 < 14, 2, jnp.where(row_512 < 50, 3, 9)))
    )

    def full_act():
        return jnp.concatenate([v.act_b[k] for k in range(SPLITS)], axis=1)

    v.zsum[...] = jnp.zeros((2, OWNERS * BINS, 128), F32)

    def own_branch(j, body):
        chunk = chunk_of(me, j)
        pl.when(chunk >= MERGED)(lambda: body(chunk - MERGED, lax.div(me + j, 8)))

    def make_z(j):
        def body(group, side):
            kept = jnp.where(group_id == group, 1.0, 0.0)
            rows = (full_act().astype(F32) * kept).astype(BF)
            v.zsum[side] = v.zsum[side] + dot(rows, v.w_own[rows_at(j, 512), :])

        own_branch(j, body)

    loop(9, make_z)
    for k in range(OWNERS):
        for side in range(2):
            v.z_send[k, side] = v.zsum[side, k * BINS : k * BINS + BINS, :].astype(BF)
    v.z_recv[me] = v.z_send[me]
    ex = Exchange(BATCH, OWNERS, lambda o: v.z_send.at[o], lambda s: v.z_recv.at[s])
    ex.start()
    g_u.forward(3)
    joined_copy(1, t_core, t_core).wait_recv()
    joined_copy(2, t_diag, t_core).wait_recv()
    for k in range(SPLITS):
        v.joined_t[k] = v.joined[k].T
    ex.wait()
    g_u.finish()

    pick2 = jnp.concatenate([v.pick[...], v.pick[...]], axis=0)

    def tap_z(tap):
        if tap == 0:
            return v.z_recv[0, 0].astype(F32)
        if tap == 8:
            return v.z_recv[7, 1].astype(F32)
        return v.z_recv[tap, 0].astype(F32) + v.z_recv[tap - 1, 1].astype(F32)

    def full_joined():
        return jnp.concatenate([v.joined[k] for k in range(SPLITS)], axis=1)

    def w_tap(tap):
        return v.w_u[rows_at(tap, 2048), :]

    def unite_pair(p):
        value = dot(full_joined(), jnp.concatenate([w_tap(2 * p), w_tap(2 * p + 1)], axis=1))
        v.pad[2 * p, EDGE : EDGE + CELLS, :] = value[:, :128]
        v.pad[2 * p + 1, EDGE : EDGE + CELLS, :] = value[:, 128:]

    loop(4, unite_pair)
    v.pad[8, EDGE : EDGE + CELLS, :] = dot(full_joined(), w_tap(8))
    for tap in range(9):
        z = tap_z(tap)
        high_z = z.astype(BF)
        low_z = (z - high_z.astype(F32)).astype(BF)
        v.pad[tap, EDGE : EDGE + CELLS, :] = v.pad[tap, EDGE : EDGE + CELLS, :] + dot_tn(
            pick2, jnp.concatenate([high_z, low_z], axis=0)
        )
    for at in range(0, CELLS, BLOCK):
        v.pre_u[at : at + BLOCK, :] = shift_sum(range(9), 1, at, lambda tap: tap)
    sync = Sync(v.sync_five)
    sync.start(list(masked_sums(v.pre_u)))
    for item in (g_c, g_ac):
        item.finish()
    for item in (g_gain, g_r, g_s, g_a, g_m, g_e, g_b, g_c, g_ac, g_u):
        item.drain()
    joined_copy(0, t, t_x).wait_send()
    joined_copy(1, t, t_core).wait_send()
    joined_copy(2, t_x, t_core).wait_send()
    w_ac = jnp.concatenate([v.w_ac[...], jnp.zeros((64, 256), F32)], axis=0).astype(BF)
    sums = sync.wait()
    norm_u = moments(sums[0:1], sums[1:2], count)

    def make_u(k):
        at = rows_at(k, 96)
        v.united[at, :] = jax.nn.silu(gamma(14) * normed(v.pre_u, at, norm_u) + beta(14)).astype(BF)

    loop(6, make_u)

    v.logit_send[:, :256] = dot(v.united[...], v.w_c[...]).astype(BF)
    v.logit_send[:, 256:] = dot(v.act_a[...], w_ac).astype(BF)
    ex = Exchange(
        TENSOR,
        SPLITS,
        lambda o: v.logit_send.at[rows_at(o, 144), :],
        lambda s: v.logit_recv.at[s],
    )
    ex.start()
    v.logit_recv[t] = v.logit_send[rows_at(t, 144), :]
    total_valid = jnp.sum(class_count, axis=1, keepdims=True)
    class_weight = total_valid / (NCLS * class_count + total_valid)
    loss_weight = jnp.sum(class_count * class_weight, axis=1, keepdims=True)
    class_weight = jnp.where(lanes < float(NCLS), class_weight, 0.0)
    hot = jnp.where(wide(v.lab[rows_at(t, 144), :], 2) == lanes, 1.0, 0.0)
    cell_weight = jnp.sum(hot * class_weight, axis=1, keepdims=True)
    ex.wait()
    logits = v.logit_recv[0].astype(F32)
    for k in range(1, SPLITS):
        logits = logits + v.logit_recv[k].astype(F32)

    def log_softmax(value):
        value = jnp.where(lanes < float(NCLS), value, -1e30)
        value = value - jnp.max(value, axis=1, keepdims=True)
        powers = jnp.exp(value)
        mass = jnp.sum(powers, axis=1, keepdims=True)
        return value - jnp.log(mass), powers / mass

    log_main, p_main = log_softmax(logits[:, :256])
    log_aux, p_aux = log_softmax(logits[:, 256:])
    loss_rows = total(fold(-cell_weight * hot * (log_main + 0.4 * log_aux)))
    loss_local = loss_rows[:, :128] + loss_rows[:, 128:]
    o_misc[1:2, :] = loss_local
    v.slope_in[t, :, :256] = (cell_weight * (p_main - hot) / loss_weight).astype(BF)
    v.slope_in[t, :, 256:] = (0.4 * cell_weight * (p_aux - hot) / loss_weight).astype(BF)
    spread_g = Spread(v.slope_in)
    spread_g.start()
    spread_g.wait()
    g_main = v.slope_in[:, :, :256].reshape(CELLS, 256)
    g_aux = v.slope_in[:, :, 256:].reshape(CELLS, 256)
    v.d_f[...] = dot_nt(g_main, v.w_c[...])
    v.d_f2[...] = dot_nt(g_aux, w_ac)

    def slope(value):
        gate = jax.nn.sigmoid(value)
        return gate * (1.0 + value * (1.0 - gate))

    def through_silu(ref, pre, norm, row):
        def step(k, carry):
            at = rows_at(k, 96)
            unit = normed(pre, at, norm)
            value = ref[at, :] * slope(gamma(row) * unit + beta(row))
            ref[at, :] = value
            return (carry[0] + fold(value), carry[1] + fold(value * unit))

        zero = jnp.zeros((8, 128), F32)
        sums = lax.fori_loop(0, 6, step, (zero, zero))
        return [total(sums[0]), total(sums[1])]

    def back_norm(value, unit, mask, norm, gain, first, second, size):
        inner = value - mask * (first + unit * second) / size
        return gain * norm[1] * inner

    gain_grads = {}
    sync = Sync(v.sync_b1)
    sync.start(
        through_silu(v.d_f, v.pre_u, norm_u, 14) + through_silu(v.d_f2, v.pre_a, norm_a, 15)
    )

    class Scatter:
        def __init__(self, first, second, full, rows, out):
            self.full, self.rows, self.out = full, rows, out
            self.first, self.second = first, second
            self.near_s, self.near_r = take(HALF), take(HALF)
            self.far_s, self.far_r = take(HALF), take(HALF)
            self.block = min(rows, 64)

        def near(self, step):
            dest = far_peer(partner, step)
            return remote(
                self.full.at[rows_at(dest, self.rows), :],
                self.first.at[step],
                self.near_s + step,
                self.near_r + step,
                {BATCH: partner},
            )

        def far(self, step):
            return remote(
                self.first.at[step],
                self.second.at[step - 1],
                self.far_s + step,
                self.far_r + step,
                {BATCH: far_peer(me, step)},
            )

        def start(self):
            for step in (1, 2, 3, 0):
                self.near(step).start()

        def middle(self):
            kind = self.first.dtype
            for step in (1, 2, 3, 0):
                self.near(step).wait_recv()
                base = far_peer(me, step) * (self.rows // self.block)

                def add(k, step=step, base=base):
                    at = rows_at(k, self.block)
                    value = self.full[rows_at(base + k, self.block), :].astype(F32)
                    value = value + self.first[step, at, :].astype(F32)
                    if step:
                        self.first[step, at, :] = value.astype(kind)
                    else:
                        self.out[at, :] = value

                loop(self.rows // self.block, add)
                if step:
                    self.far(step).start()

        def end(self):
            for step in range(1, HALF):
                self.far(step).wait_recv()

            def add(k, carry):
                at = rows_at(k, self.block)
                value = self.out[at, :]
                for step in range(1, HALF):
                    value = value + self.second[step - 1, at, :].astype(F32)
                self.out[at, :] = value
                return carry + fold(value * value)

            squares = lax.fori_loop(
                0, self.rows // self.block, add, jnp.zeros((8, self.out.shape[1]), F32)
            )
            for step in (1, 2, 3, 0):
                self.near(step).wait_send()
                if step:
                    self.far(step).wait_send()
            return sum(split_rows(total(squares)))

    s_c = Scatter(v.first_c, v.second_c, v.w_c, 16, o_c)
    s_ac = Scatter(v.first_ac, v.second_ac, v.w_ac, 8, o_ac)
    s_a = Scatter(v.first_a, v.second_a, v.w_a, 576, o_a)
    s_b = Scatter(v.first_b, v.second_b, v.w_b, 256, o_b)
    s_s = Scatter(v.first_s, v.second_s, v.w_s, 128, o_s)
    s_e = Scatter(v.first_e, v.second_e, v.w_e, 64, o_e)
    s_m = Scatter(v.first_m, v.second_m, v.w_m, 576, o_m)
    s_r = Scatter(v.first_r, v.second_r, v.w_r, 128, o_r)

    class ScatterUnite:
        def __init__(self):
            self.near_s, self.near_r = take(9 * HALF), take(9 * HALF)
            self.far_s, self.far_r = take(9 * HALF), take(9 * HALF)

        def slot(self, owner, j):
            return jnp.where(j == 8, SLOTS - 1, chunk_of(owner, j))

        def near(self, step, j, base):
            dest = far_peer(base, step)
            return remote(
                v.w_u.at[merged_rows(dest, j), :],
                v.first_u.at[step, self.slot(dest, j)],
                self.near_s + step * 9 + j,
                self.near_r + step * 9 + j,
                {BATCH: partner},
            )

        def far(self, step, j, owner):
            at = self.slot(owner, j)
            return remote(
                v.first_u.at[step, at],
                v.second_u.at[step - 1, at],
                self.far_s + step * 9 + j,
                self.far_r + step * 9 + j,
                {BATCH: far_peer(me, step)},
            )

        def start(self):
            for step in (1, 2, 3, 0):
                each_merged(
                    far_peer(partner, step),
                    lambda j, step=step: self.near(step, j, partner).start(),
                )

        def middle(self, step):
            owner = far_peer(me, step)

            def go(j):
                self.near(step, j, me).wait_recv()
                slot = self.slot(owner, j)
                tap = owner + lax.div(owner + j, 8)
                base = (tap * MERGED + chunk_of(owner, j)) * 8

                def add(k):
                    at = rows_at(k, 64)
                    value = v.w_u[rows_at(base + k, 64), :].astype(F32)
                    value = value + v.first_u[step, slot, at, :].astype(F32)
                    if step:
                        v.first_u[step, slot, at, :] = value.astype(BF)
                    else:
                        o_u[rows_at(j * 8 + k, 64), :] = value

                loop(8, add)
                if step:
                    self.far(step, j, owner).start()

            each_merged(owner, go)

        def end(self):
            def go(j):
                slot = self.slot(me, j)
                for step in range(1, HALF):
                    self.far(step, j, me).wait_recv()

                def add(k):
                    at = rows_at(k, 64)
                    value = o_u[rows_at(j * 8 + k, 64), :]
                    for step in range(1, HALF):
                        value = value + v.second_u[step - 1, slot, at, :].astype(F32)
                    o_u[rows_at(j * 8 + k, 64), :] = value

                loop(8, add)

            each_merged(me, go)
            for step in (1, 2, 3, 0):
                each_merged(
                    far_peer(partner, step),
                    lambda j, step=step: self.near(step, j, partner).wait_send(),
                )
                if step:
                    each_merged(
                        far_peer(me, step),
                        lambda j, step=step: self.far(step, j, far_peer(me, step)).wait_send(),
                    )

            def square(k, carry):
                value = o_u[rows_at(k, 64), :]
                return carry + fold(value * value)

            squares = lax.fori_loop(0, 72, square, jnp.zeros((8, 128), F32))
            return sum(split_rows(total(squares)))

    s_u = ScatterUnite()

    v.w_c[...] = dot_tn(v.united[...], g_main).astype(BF)
    v.w_ac[...] = dot_tn(v.act_a[...], g_aux)[:64]
    s_c.start()
    s_ac.start()
    sums = sync.wait()
    gain_grads[14] = (sums[1:2], sums[0:1])
    gain_grads[15] = (sums[3:4], sums[2:3])

    def spread_taps(ref, pre, norm, row, first, second):
        def step(k):
            at = rows_at(k, 96)
            value = back_norm(
                ref[at, :], normed(pre, at, norm), v.ins[at, :], norm, gamma(row), first, second, count
            )
            ref[at, :] = value.astype(BF).astype(F32)

        loop(6, step)
        v.grad_pad[EDGE : EDGE + CELLS, :] = ref[...]

    def back_tap(tap, spacing, at):
        start = EDGE + at - offset(tap, spacing)
        value = v.grad_pad[start : start + 96, :]
        right = tap % 3 - 1
        if right:
            value = value * col_mask(slice(at, at + 96), -right * spacing)
        return value

    def fill(cat, spacing):
        for tap in range(9):
            for at in range(0, CELLS, 96):
                cat[at : at + 96, tap * 128 : tap * 128 + 128] = back_tap(tap, spacing, at).astype(
                    BF
                )

    spread_taps(v.d_f, v.pre_u, norm_u, 14, sums[0:1], sums[1:2])
    fill(v.cat_u, 1)

    dz = dot(v.pick[...], v.cat_u[...])
    for tap in range(9):
        v.dz_send[tap] = dz[:, tap * 128 : tap * 128 + 128].astype(BF)
    v.dz_recv[me] = v.dz_send[pl.ds(me, 2)]
    ex_dz = Exchange(
        BATCH, OWNERS, lambda o: v.dz_send.at[pl.ds(o, 2)], lambda s: v.dz_recv.at[s]
    )
    ex_dz.start()

    def merged_back(c):
        weight = jnp.concatenate(
            [v.w_u[rows_at(tap * MERGED + c, 512), :] for tap in range(9)], axis=1
        )
        v.joined[c] = dot_nt(v.cat_u[...], weight).astype(BF)

    near_s, near_r, far_s, far_r = take(2), take(2), take(1), take(1)

    def dm_near(k, slot):
        return remote(
            v.joined.at[slot], v.dm_near.at[k], near_s + k, near_r + k, {TENSOR: t_core}
        )

    merged_back(t_diag)
    dm_near(1, t_diag).start()
    merged_back(t_core)
    dm_near(0, t_core).start()
    ex_dz.wait()

    d_act = v.d_sum.at[0 : OWNERS * BINS, :]
    d_act[...] = jnp.zeros((OWNERS * BINS, 512), F32)

    def branch_back(j):
        def body(group, side):
            kept = jnp.where(group_id == group, 1.0, 0.0)
            value = v.dz_recv[:, side].reshape(OWNERS * BINS, 128).astype(F32) * kept
            value = value.astype(BF)
            o_u[rows_at(j, 512), :] = dot_tn(full_act(), value)
            d_act[...] = d_act[...] + dot_nt(value, v.w_own[rows_at(j, 512), :])

        own_branch(j, body)

    loop(9, branch_back)
    for k in range(SPLITS):
        v.d_act_send[k] = d_act[:, k * 128 : k * 128 + 128].astype(BF)
    v.d_act_recv[t] = v.d_act_send[t]
    ex = Exchange(TENSOR, SPLITS, lambda o: v.d_act_send.at[o], lambda s: v.d_act_recv.at[s])
    ex.start()
    merged_back(t_x)
    merged_back(t)
    dm_near(1, t_x).wait_recv()

    def add_x(k):
        at = rows_at(k, 48)
        value = v.joined[t_x, at, :].astype(F32) + v.dm_near[1, at, :].astype(F32)
        v.joined[t_x, at, :] = value.astype(BF)

    loop(12, add_x)
    dm_far = remote(v.joined.at[t_x], v.dm_far, far_s, far_r, {TENSOR: t_x})
    dm_far.start()
    ex.wait()
    for k in range(OWNERS):
        at = slice(k * BINS, k * BINS + BINS)
        value = v.d_act_recv[0, at, :].astype(F32)
        for slot in range(1, SPLITS):
            value = value + v.d_act_recv[slot, at, :].astype(F32)
        v.d_img_send[k] = value.astype(BF)
    v.d_img_recv[me] = v.d_img_send[me]
    ex = Exchange(BATCH, OWNERS, lambda o: v.d_img_send.at[o], lambda s: v.d_img_recv.at[s])
    ex.start()

    def unite_grad(c):
        for p in range(5):
            width = 256 if p < 4 else 128
            value = dot(v.joined_t[c], v.cat_u[:, p * 256 : p * 256 + width])
            v.w_u[rows_at(2 * p * MERGED + c, 512), :] = value[:, :128].astype(BF)
            if p < 4:
                v.w_u[rows_at((2 * p + 1) * MERGED + c, 512), :] = value[:, 128:].astype(BF)

    loop(SPLITS, unite_grad)
    s_u.start()
    ex.wait()
    d_b = v.d_img_recv[0].astype(F32)
    for k in range(1, OWNERS):
        d_b = d_b + v.d_img_recv[k].astype(F32)
    unit_b = (v.all_b[me].astype(F32) - mean_b) * scale_b
    d_b = d_b * slope(gamma_b * unit_b + beta_b)
    sync = Sync(v.sync_b3)
    sync.start(
        [total(d_b * group_mask(g)) for g in range(4)]
        + [total(d_b * unit_b * group_mask(g)) for g in range(4)]
    )
    spread_taps(v.d_f2, v.pre_a, norm_a, 15, sums[2:3], sums[3:4])
    for p in range(5):
        for at in range(0, CELLS, 96):
            value = back_tap(2 * p, 1, at)
            if p < 4:
                value = value + pltpu.roll(back_tap(2 * p + 1, 1, at), 64, 1)
            v.cat_a[at : at + 96, p * 128 : p * 128 + 128] = value.astype(BF)
    sums = sync.wait()
    first_b = jnp.zeros((BINS, 128), F32)
    second_b = jnp.zeros((BINS, 128), F32)
    for group in range(4):
        kept = group_mask(group)
        gain_grads[10 + group] = (sums[4 + group : 5 + group], sums[group : group + 1])
        first_b = first_b + kept * sums[group : group + 1]
        second_b = second_b + kept * sums[4 + group : 5 + group]
    inner = d_b - (first_b + unit_b * second_b) * count_b
    v.d_bp[t] = (gamma_b * scale_b * inner).astype(BF)
    spread_d = Spread(v.d_bp)
    spread_d.start()

    def aux_grad(c2):
        value2 = dot_tn(v.whole[c2], v.cat_a[...])
        for half in range(2):
            value = value2[half * 128 : half * 128 + 128]
            c = 2 * c2 + half
            for p in range(5):
                low = value[:64, p * 128 : p * 128 + 128]
                top = value[64:, p * 128 : p * 128 + 128]
                even = jnp.where(left_half, low, pltpu.roll(top, 64, 1))
                v.w_a[rows_at(2 * p * 8 + c, 64), :] = even.astype(BF)
                if p < 4:
                    odd = jnp.where(left_half, pltpu.roll(low, 64, 1), top)
                    v.w_a[rows_at((2 * p + 1) * 8 + c, 64), :] = odd.astype(BF)

    spread_d.wait()
    d_bp = jnp.concatenate([v.d_bp[k] for k in range(SPLITS)], axis=1)
    d_pooled = jnp.zeros((BINS, 512), F32)
    d_groups = []
    for group in range(4):
        d_groups.append((d_bp.astype(F32) * group_mask(group)).astype(BF))
        d_pooled = d_pooled + dot_nt(d_groups[group], v.w_b[group * 512 : group * 512 + 512, :])
    for group in range(4):
        v.w_b[group * 512 : group * 512 + 512, :] = dot_tn(v.pooled[...], d_groups[group]).astype(BF)
    s_b.start()
    d_pooled = (d_pooled / cells_in).astype(BF)
    v.d_sum[...] = dot_tn(v.pool[...], d_pooled)
    dm_near(0, t).wait_recv()
    dm_far.wait_recv()

    def through_sum(k, carry):
        at = rows_at(k, 48)
        value = v.d_sum[at, :] + v.joined[t, at, :].astype(F32) + v.dm_near[0, at, :].astype(F32)
        value = (value + v.dm_far[at, :].astype(F32)) * slope(summed(at))
        v.d_sum[at, :] = value
        return (
            carry[0] + fold(value),
            carry[1] + fold(value * normed(v.pre_e, at, norm_e)),
            carry[2] + fold(value * normed(v.pre_s, at, norm_s)),
        )

    zero = jnp.zeros((8, 512), F32)
    three = [total(item) for item in lax.fori_loop(0, 12, through_sum, (zero, zero, zero))]
    sync = Sync(v.sync_b4)
    sync.start(split_rows(three[0]) + split_rows(three[1]) + split_rows(three[2]))
    loop(SPLITS, aux_grad)
    s_a.start()
    sums = sync.wait()
    first_s = join_rows(sums, 0, 4)
    second_e, second_s = join_rows(sums, 4, 4), join_rows(sums, 8, 4)
    for k in range(4):
        gain_grads[6 + k] = (sums[4 + k : 5 + k], sums[k : k + 1])
        gain_grads[1 + k] = (sums[8 + k : 9 + k], sums[k : k + 1])

    def back_both(k):
        at = rows_at(k, 48)
        value, mask = v.d_sum[at, :], wide(v.ins[at, :], 4)
        v.d_e[at, :] = back_norm(
            value, normed(v.pre_e, at, norm_e), mask, norm_e, gamma(6, 4), first_s, second_e, count4
        ).astype(BF)
        v.d_s[at, :] = back_norm(
            value, normed(v.pre_s, at, norm_s), mask, norm_s, gamma(1, 4), first_s, second_s, count4
        ).astype(BF)

    loop(12, back_both)

    def back_hidden(grad, weight, index):
        value = dot_nt(grad, weight)
        for k in range(SPLITS):
            v.dh_send[k] = value[:, k * 128 : k * 128 + 128].astype(BF)
        v.dh_recv[index, t] = v.dh_send[t]
        ex = Exchange(
            TENSOR, SPLITS, lambda o: v.dh_send.at[o], lambda s: v.dh_recv.at[index, s]
        )
        ex.start()
        return ex

    def hidden_sum(index):
        def step(k):
            at = rows_at(k, 96)
            value = v.dh_recv[index, 0, at, :].astype(F32)
            for slot in range(1, SPLITS):
                value = value + v.dh_recv[index, slot, at, :].astype(F32)
            v.d_f[at, :] = value

        loop(6, step)

    ex = back_hidden(v.d_e[...], v.w_e[...], 0)
    s_u.middle(1)
    for k in range(SPLITS):
        v.w_e[k * 128 : k * 128 + 128, :] = dot_tn(v.h2[k], v.d_e[...]).astype(BF)
    s_e.start()
    ex.wait()
    hidden_sum(0)
    sync = Sync(v.sync_b5)
    sync.start(through_silu(v.d_f, v.pre_m, norm_m, 5))
    s_u.middle(2)
    sums = sync.wait()
    gain_grads[5] = (sums[1:2], sums[0:1])
    spread_taps(v.d_f, v.pre_m, norm_m, 5, sums[0:1], sums[1:2])
    fill(v.cat_u, 4)
    weight = jnp.concatenate([v.w_m[tap * 512 : tap * 512 + 512, :] for tap in range(9)], axis=1)
    ex = back_hidden(v.cat_u[...], weight, 1)

    def short_grad(c):
        v.w_s[rows_at(c, 256), :] = dot_tn(v.whole[c], v.d_s[...]).astype(BF)

    loop(SPLITS, short_grad)
    s_s.start()
    s_u.middle(3)
    ex.wait()
    hidden_sum(1)
    sync = Sync(v.sync_b6)
    sync.start(through_silu(v.d_f, v.pre_r, norm_r, 0))

    def middle_grad(k):
        value = dot_tn(v.h1[k], v.cat_u[...])
        for tap in range(9):
            v.w_m[rows_at(tap * 4 + k, 128), :] = value[:, tap * 128 : tap * 128 + 128].astype(BF)

    loop(SPLITS, middle_grad)
    s_m.start()
    s_u.middle(0)
    sums = sync.wait()
    gain_grads[0] = (sums[1:2], sums[0:1])

    def back_reduce(k):
        at = rows_at(k, 96)
        v.d_low[at, :] = back_norm(
            v.d_f[at, :], normed(v.pre_r, at, norm_r), v.ins[at, :], norm_r, gamma(0), sums[0:1], sums[1:2], count
        ).astype(BF)

    loop(6, back_reduce)

    def reduce_grad(c):
        v.w_r[rows_at(c, 256), :] = dot_tn(v.whole[c], v.d_low[...]).astype(BF)

    loop(SPLITS, reduce_grad)
    s_r.start()
    rest = (s_c, s_ac, s_b, s_a, s_e, s_s, s_m, s_r)
    for item in rest:
        item.middle()
    squares = s_u.end()
    for item in rest:
        squares = squares + item.end()
    dm_near(1, t_diag).wait_send()
    dm_near(0, t_core).wait_send()
    dm_far.wait_send()

    for row in range(16):
        o_gain[row : row + 1, :] = gain_grads[row][0]
        o_gain[16 + row : 17 + row, :] = gain_grads[row][1]
    gain_square = o_gain[...] * o_gain[...]
    squares = squares + total(gain_square) / OWNERS

    sync = Sync(v.sync_end)
    sync.start([squares, o_misc[1:2, :]])
    v.end_t[t] = sync.wait()
    spread_e = Spread(v.end_t)
    spread_e.start()
    spread_e.wait()
    ends = v.end_t[0]
    for k in range(1, SPLITS):
        ends = ends + v.end_t[k]
    o_misc[...] = ends
    o_misc[2:3, :] = jnp.broadcast_to(loss_weight, (1, 128))


def whole_step(sizes, labels, feat, gains, pieces):
    plan = scratch_plan()
    vmem = pl.BlockSpec(memory_space=pltpu.VMEM)
    anywhere = pl.BlockSpec(memory_space=pl.ANY)
    outs = [(128, 128), (128, 512), (576, 128), (64, 512), (256, 512), (4608, 128), (576, 128)]
    outs = outs + [(16, 256), (8, 256), (32, 128), (8, 128)]
    return pl.pallas_call(
        functools.partial(step_kernel, tuple(plan)),
        out_shape=[jax.ShapeDtypeStruct(shape, F32) for shape in outs],
        in_specs=[pl.BlockSpec(memory_space=pltpu.SMEM), vmem, anywhere, anywhere]
        + [anywhere] * len(pieces),
        out_specs=[vmem] * len(outs),
        scratch_shapes=[pltpu.VMEM(shape, kind) for shape, kind in plan.values()]
        + [pltpu.SemaphoreType.DMA((SEMAPHORES,))],
        compiler_params=pltpu.CompilerParams(
            collective_id=0, has_side_effects=True, vmem_limit_bytes=63 * 1024 * 1024
        ),
        name="whole_step",
    )(sizes, labels, feat, gains, *pieces)


def update_kernel(scale, grad, param, first, second, average, o_param, o_first, o_second, o_average):
    clipped = grad[...] * scale[0]
    new_first = 0.5 * first[...] + 0.5 * clipped
    new_second = 0.5 * second[...] + 0.5 * clipped * clipped
    keep = 1.0 - 0.5**STEP
    old = param[...]
    new = old - 0.01 * (new_first / keep / (jnp.sqrt(new_second / keep) + 1e-08) + 0.01 * old)
    o_param[...] = new
    o_first[...] = new_first
    o_second[...] = new_second
    o_average[...] = 0.999 * average[...] + 0.001 * new


def update(scale, grad, param, first, second, average):
    rows = grad.shape[0]
    block = pl.BlockSpec((512, 128), lambda i: (i, 0))
    return pl.pallas_call(
        update_kernel,
        grid=(pl.cdiv(rows, 512),),
        out_shape=[jax.ShapeDtypeStruct((rows, 128), jnp.float32)] * 4,
        in_specs=[pl.BlockSpec(memory_space=pltpu.SMEM)] + [block] * 5,
        out_specs=[block] * 4,
        name="update",
    )(scale.reshape(1), grad, param, first, second, average)

def fits(splits, owners):
    return splits == SPLITS and owners == OWNERS


def local_fast(features, labels, valid, sizes, params, first_moment, squared_mean, average):
    me = lax.axis_index("batch")
    shapes = segment_shapes(SPLITS)
    counts = []
    for shape in shapes:
        count = 1
        for extent in shape:
            count = count * extent
        counts.append(count // OWNERS)
    starts = [0]
    for count in counts:
        starts.append(starts[-1] + count)
    flat = params.reshape(-1, 128)
    low = flat.astype(BF)
    tail = flat[starts[6] // 128 :].reshape(-1)
    cut = [tail[starts[k] - starts[6] : starts[k + 1] - starts[6]] for k in range(6, 10)]
    rows = [low[starts[k] // 128 : starts[k + 1] // 128] for k in range(6)]
    aux = cut[1].astype(BF).reshape(9, 2, 64, 64)
    pieces = [
        rows[0],
        rows[1].reshape(128, 512),
        rows[2],
        rows[3].reshape(64, 512),
        rows[4].reshape(256, 512),
        rows[5],
        jnp.concatenate([aux[:, 0], aux[:, 1]], axis=-1).reshape(576, 128),
        jnp.pad(cut[0].astype(BF).reshape(16, NCLS), ((0, 0), (0, 256 - NCLS))),
        jnp.pad(
            cut[2].astype(BF).astype(F32).reshape(8, NCLS), ((0, 0), (0, 256 - NCLS))
        ),
    ]
    width = shapes[9][1]
    share = counts[9]
    per_row = width // share
    spot = jnp.zeros((2, 2048), F32)
    spot = lax.dynamic_update_slice(
        spot,
        cut[3].astype(BF).astype(F32).reshape(1, share),
        (me // per_row, (me % per_row) * share),
    )
    marked = jnp.where(valid > 0, labels, -1).astype(F32).reshape(CELLS, 1)
    outs = whole_step(
        sizes,
        jnp.broadcast_to(marked, (CELLS, 128)),
        features.reshape(CELLS, -1),
        spot.reshape(32, 128),
        pieces,
    )
    gain_grad = lax.dynamic_slice(
        outs[9].reshape(2, 2048)[:, :width].reshape(-1), (me * share,), (share,)
    )
    aux_grad = outs[6].reshape(9, 64, 2, 64).transpose(0, 2, 1, 3)
    grad_share = jnp.concatenate(
        [outs[k].reshape(-1, 128) for k in range(6)]
        + [
            jnp.concatenate(
                [
                    outs[7][:, :NCLS].reshape(-1),
                    aux_grad.reshape(-1),
                    outs[8][:, :NCLS].reshape(-1),
                    gain_grad,
                ]
            ).reshape(-1, 128)
        ]
    )
    misc = outs[10]
    grad_norm = jnp.sqrt(jnp.sum(misc[0]))
    scale = jnp.minimum(1.0, 0.05 / (grad_norm + 1e-06))
    new_params, new_first, new_second, new_average = [
        item.reshape(params.shape)
        for item in update(
            scale,
            grad_share,
            flat,
            first_moment.reshape(-1, 128),
            squared_mean.reshape(-1, 128),
            average.reshape(-1, 128),
        )
    ]
    return (
        new_params,
        new_first,
        new_second,
        new_average,
        new_params.astype(BF),
        grad_norm,
        jnp.sum(misc[1]),
        misc[2, 0],
        outs[9][30],
    )


def solution(mesh):
    chosen = local_fast if fits(mesh.shape["tensor"], mesh.shape["batch"]) else local
    return jax.shard_map(
        chosen,
        mesh=mesh,
        in_specs=(
            P("batch", None, None, "tensor"),
            P("batch", None, None),
            P("batch", None, None),
            P("batch", None),
            P("tensor", "batch"),
            P("tensor", "batch"),
            P("tensor", "batch"),
            P("tensor", "batch"),
        ),
        out_specs=(
            P("tensor", "batch"),
            P("tensor", "batch"),
            P("tensor", "batch"),
            P("tensor", "batch"),
            P("tensor", "batch"),
            P(),
            P(),
            P(),
            P("tensor"),
        ),
        check_vma=False,
    )
```

```python
import functools

import jax
import jax.numpy as jnp
from jax import lax
from jax.experimental import pallas as pl
from jax.experimental.pallas import tpu as pltpu
from jax.sharding import PartitionSpec as P

C_IN = 1024
MID = 512
C_OUT = 2048
PPM = 512
AUXW = 256
NCLS = 150
MAP = 24
STEP = 3


BIN_COUNTS = (1, 2, 3, 6)
BIN_STARTS = (0, 1, 5, 14)


def segment_shapes(splits):
    return [
        (C_IN, MID // splits),
        (C_IN, C_OUT // splits),
        (9, MID, MID // splits),
        (MID, C_OUT // splits),
        (4, C_OUT // splits, PPM),
        (9, C_OUT + 4 * PPM, PPM // splits),
        (PPM // splits, NCLS),
        (9, C_IN, AUXW // splits),
        (AUXW // splits, NCLS),
        (2, (2 * MID + 2 * C_OUT + 5 * PPM + AUXW) // splits),
    ]


def unflatten(rows, splits):
    split_parts = []
    start = 0
    for shape in segment_shapes(splits):
        count = 1
        for extent in shape:
            count = count * extent
        count = count // rows.shape[0]
        split_parts.append(rows[:, start : start + count].reshape(shape))
        start = start + count
    return split_parts


def gain_pieces(gains, splits):
    widths = [MID, C_OUT, MID, C_OUT, PPM, PPM, PPM, PPM, PPM, AUXW]
    split_parts = []
    start = 0
    for width in widths:
        step_width = width // splits
        split_parts.append(gains[:, start : start + step_width])
        start = start + step_width
    return split_parts


def shifted(field, down, right):
    image_height, width = (field.shape[1], field.shape[2])
    rows_pad, cols_pad = (abs(down), abs(right))
    padded = jnp.pad(field, ((0, 0), (rows_pad, rows_pad), (cols_pad, cols_pad), (0, 0)))
    return padded[
        :,
        rows_pad + down : rows_pad + down + image_height,
        cols_pad + right : cols_pad + right + width,
        :,
    ]


def conv_forward(field, kernel, spacing):
    total = jnp.zeros(field.shape[:-1] + (kernel.shape[2],), jnp.float32)
    for tap in range(9):
        moved = shifted(field, (tap // 3 - 1) * spacing, (tap % 3 - 1) * spacing)
        total = total + jnp.dot(moved, kernel[tap], preferred_element_type=jnp.float32)
    return total


def conv_input_back(grad, kernel, spacing):
    total = jnp.zeros(grad.shape[:-1] + (kernel.shape[1],), jnp.float32)
    for tap in range(9):
        product = jnp.dot(grad, kernel[tap].T, preferred_element_type=jnp.float32)
        total = total + shifted(product, -(tap // 3 - 1) * spacing, -(tap % 3 - 1) * spacing)
    return total


def conv_kernel_back(field, grad, spacing):
    return jnp.stack(
        [
            jnp.einsum(
                "ihwc,ihwd->cd",
                shifted(field, (tap // 3 - 1) * spacing, (tap % 3 - 1) * spacing),
                grad,
                preferred_element_type=jnp.float32,
            )
            for tap in range(9)
        ]
    )


def silu_slope(value):
    gate = jax.nn.sigmoid(value)
    return gate * (1.0 + value * (1.0 - gate))


def channel_sums(values):
    return values.reshape(-1, values.shape[-1]).sum(0)


def masked_norm_apply(items, extra):
    sends = []
    for value, mask, norm in items:
        sends = sends + [
            channel_sums(value * mask),
            channel_sums(value * value * mask),
            jnp.sum(mask) * jnp.ones((1,), jnp.float32),
        ]
    totals = lax.psum(tuple(sends + extra), "batch")
    results = []
    for index, (value, mask, norm) in enumerate(items):
        count = totals[3 * index + 2]
        mean = totals[3 * index] / count
        spread = totals[3 * index + 1] / count - mean * mean
        scaling = lax.rsqrt(spread + 1e-05)
        normed = (value - mean) * scaling
        results.append((norm[0] * normed + norm[1], normed, scaling, count, mask, norm[0]))
    return (results, totals[3 * len(items) :])


def norm_backward(items):
    sends = []
    for grad, kept in items:
        sends = sends + [channel_sums(grad), channel_sums(grad * kept[1])]
    totals = lax.psum(tuple(sends), "batch")
    results = []
    for index, (grad, kept) in enumerate(items):
        outcome, normed, scaling, count, mask, gamma = kept
        first_sum, second_sum = (totals[2 * index], totals[2 * index + 1])
        inner = grad - mask * (first_sum + normed * second_sum) / count
        results.append(gamma * scaling * inner)
    return (results, sends, totals)


def bin_tables(extent, bins, length):
    which = jnp.arange(bins, dtype=jnp.int32)[None, :, None]
    place = jnp.arange(length, dtype=jnp.int32)[None, None, :]
    edge = extent[:, None, None]
    lower = which * edge // bins
    upper = ((which + 1) * edge + bins - 1) // bins
    member = ((place >= lower) & (place < upper)).astype(jnp.float32)
    target = jnp.minimum(place * bins // edge, bins - 1)
    chosen = (target == which).astype(jnp.float32)
    return (member, chosen)


def spread_bins(merged, branch, tables, images):
    joined = [merged]
    for group, bins in enumerate(BIN_COUNTS):
        rows_in, cols_in, rows_pick, cols_pick, cell_count = tables[group]
        piece = branch[:, BIN_STARTS[group] : BIN_STARTS[group] + bins * bins].reshape(
            images, bins, bins, -1
        )
        joined.append(
            jnp.einsum(
                "ikh,ilw,iklc->ihwc",
                rows_pick.astype(jnp.bfloat16),
                cols_pick.astype(jnp.bfloat16),
                piece,
                preferred_element_type=jnp.float32,
            ).astype(jnp.bfloat16)
        )
    return jnp.concatenate(joined, axis=-1)


def pick_bins(d_joined, width, tables, images):
    branch_width = (d_joined.shape[-1] - width) // 4
    d_up = []
    for group, bins in enumerate(BIN_COUNTS):
        rows_in, cols_in, rows_pick, cols_pick, cell_count = tables[group]
        piece = d_joined[..., width + group * branch_width : width + (group + 1) * branch_width]
        d_up.append(
            jnp.einsum("ikh,ilw,ihwc->iklc", rows_pick, cols_pick, piece).reshape(
                images, bins * bins, -1
            )
        )
    return (d_joined[..., :width], jnp.concatenate(d_up, axis=1))


def gather_channels(field):
    return lax.all_gather(field, "tensor", axis=3, tiled=True)


def scatter_channels(field):
    return lax.psum_scatter(
        field.astype(jnp.bfloat16), "tensor", scatter_dimension=3, tiled=True
    ).astype(jnp.float32)


def local(features, labels, valid, sizes, params, first_moment, squared_mean, average):
    splits = lax.axis_size("tensor")
    owners = lax.axis_size("batch")
    images = features.shape[0]
    gathered = lax.all_gather(params.astype(jnp.bfloat16), "batch", axis=0, tiled=True)
    (
        w_reduce,
        w_short,
        w_middle,
        w_expand,
        w_branch,
        w_unite,
        w_classes,
        w_aux,
        w_aux_classes,
        gains,
    ) = unflatten(gathered, splits)
    norms = [(piece[0], piece[1]) for piece in gain_pieces(gains.astype(jnp.float32), splits)]
    rows_at = jnp.arange(MAP, dtype=jnp.int32)
    inside = (rows_at[None, :, None] < sizes[:, 0][:, None, None]) & (
        rows_at[None, None, :] < sizes[:, 1][:, None, None]
    )
    inside = inside.astype(jnp.float32)[..., None]
    counted = inside * valid.astype(jnp.float32)[..., None]
    labels_hot = (labels[..., None] == jnp.arange(NCLS, dtype=jnp.int32)).astype(jnp.float32)
    class_local = channel_sums(labels_hot * counted)
    whole = lax.all_gather(features, "tensor", axis=3, tiled=True)
    pre_reduce = jnp.dot(whole, w_reduce, preferred_element_type=jnp.float32)
    pre_short = jnp.dot(whole, w_short, preferred_element_type=jnp.float32)
    pre_aux = conv_forward(whole, w_aux, 1)
    leading_part, label_tally = masked_norm_apply(
        [
            (pre_reduce, inside, norms[0]),
            (pre_short, inside, norms[1]),
            (pre_aux, inside, norms[9]),
        ],
        [class_local],
    )
    class_pixel_counts = label_tally[0]
    hidden_one = jax.nn.silu(leading_part[0][0]).astype(jnp.bfloat16)
    aux_act = jax.nn.silu(leading_part[2][0]).astype(jnp.bfloat16)
    hidden_full = gather_channels(hidden_one)
    pre_middle = conv_forward(hidden_full, w_middle, 4)
    second, unused = masked_norm_apply([(pre_middle, inside, norms[2])], [])
    hidden_two = jax.nn.silu(second[0][0]).astype(jnp.bfloat16)
    hidden_two_full = gather_channels(hidden_two)
    pre_expand = jnp.dot(hidden_two_full, w_expand, preferred_element_type=jnp.float32)
    third, unused = masked_norm_apply([(pre_expand, inside, norms[3])], [])
    summed = third[0][0] + leading_part[1][0]
    merged = jax.nn.silu(summed).astype(jnp.bfloat16)
    tables = []
    pooled_list = []
    partial_list = []
    for group, bins in enumerate(BIN_COUNTS):
        rows_in, rows_pick = bin_tables(sizes[:, 0], bins, MAP)
        cols_in, cols_pick = bin_tables(sizes[:, 1], bins, MAP)
        cell_count = (
            jnp.sum(rows_in, axis=2)[:, :, None, None] * jnp.sum(cols_in, axis=2)[:, None, :, None]
        )
        tables.append((rows_in, cols_in, rows_pick, cols_pick, cell_count))
        pooled = (
            jnp.einsum(
                "ikh,ilw,ihwc->iklc",
                rows_in.astype(jnp.bfloat16),
                cols_in.astype(jnp.bfloat16),
                merged,
                preferred_element_type=jnp.float32,
            )
            / cell_count
        )
        pooled = pooled.astype(jnp.bfloat16).reshape(images, bins * bins, -1)
        pooled_list.append(pooled)
        partial_list.append(
            jnp.einsum("ipc,cd->ipd", pooled, w_branch[group], preferred_element_type=jnp.float32)
        )
    branch_pre = lax.psum_scatter(
        jnp.concatenate(partial_list, axis=1).astype(jnp.bfloat16),
        "tensor",
        scatter_dimension=2,
        tiled=True,
    ).astype(jnp.float32)
    branch_items = []
    for group, bins in enumerate(BIN_COUNTS):
        piece = branch_pre[:, BIN_STARTS[group] : BIN_STARTS[group] + bins * bins]
        branch_items.append(
            (piece, jnp.ones(piece.shape[:-1] + (1,), jnp.float32), norms[4 + group])
        )
    fourth, unused = masked_norm_apply(branch_items, [])
    branch_act = jnp.concatenate([jax.nn.silu(kept[0]) for kept in fourth], axis=1).astype(
        jnp.bfloat16
    )
    merged_full, branch_full = (
        lax.all_gather(merged, "tensor", axis=3, tiled=True),
        lax.all_gather(branch_act, "tensor", axis=2, tiled=True),
    )
    joined = spread_bins(merged_full, branch_full, tables, images)
    pre_unite = conv_forward(joined, w_unite, 1)
    fifth, unused = masked_norm_apply([(pre_unite, inside, norms[8])], [])
    united = jax.nn.silu(fifth[0][0]).astype(jnp.bfloat16)
    logit_main, logit_aux = (
        lax.psum_scatter(
            jnp.dot(united, w_classes, preferred_element_type=jnp.float32).astype(jnp.bfloat16),
            "tensor",
            scatter_dimension=1,
            tiled=True,
        ).astype(jnp.float32),
        lax.psum_scatter(
            jnp.dot(aux_act, w_aux_classes, preferred_element_type=jnp.float32).astype(
                jnp.bfloat16
            ),
            "tensor",
            scatter_dimension=1,
            tiled=True,
        ).astype(jnp.float32),
    )
    total_valid = jnp.sum(class_pixel_counts)
    class_weight = total_valid / (NCLS * class_pixel_counts + total_valid)
    loss_weight = jnp.sum(class_pixel_counts * class_weight)
    cell_weight = jnp.sum(labels_hot * class_weight, axis=-1, keepdims=True) * counted
    band_rows = labels.shape[1] // splits
    band_start = lax.axis_index("tensor") * band_rows
    hot_band = lax.dynamic_slice_in_dim(labels_hot, band_start, band_rows, 1)
    weight_band = lax.dynamic_slice_in_dim(cell_weight, band_start, band_rows, 1)
    log_main = jax.nn.log_softmax(logit_main, axis=-1)
    log_aux = jax.nn.log_softmax(logit_aux, axis=-1)
    loss_cells = -jnp.sum(hot_band * (log_main + 0.4 * log_aux), axis=-1, keepdims=True)
    loss_local = jnp.sum(weight_band * loss_cells)
    band_main = (weight_band * (jnp.exp(log_main) - hot_band) / loss_weight).astype(jnp.bfloat16)
    band_aux = (0.4 * weight_band * (jnp.exp(log_aux) - hot_band) / loss_weight).astype(
        jnp.bfloat16
    )
    grad_main, grad_aux = (
        lax.all_gather(band_main, "tensor", axis=1, tiled=True),
        lax.all_gather(band_aux, "tensor", axis=1, tiled=True),
    )
    reduced = {}

    def settle(index, value):
        reduced[index] = value

    settle(6, jnp.einsum("ihwc,ihwk->ck", united, grad_main, preferred_element_type=jnp.float32))
    settle(8, jnp.einsum("ihwc,ihwk->ck", aux_act, grad_aux, preferred_element_type=jnp.float32))
    d_united = jnp.dot(grad_main, w_classes.T, preferred_element_type=jnp.float32) * silu_slope(
        fifth[0][0]
    )
    d_aux = jnp.dot(grad_aux, w_aux_classes.T, preferred_element_type=jnp.float32) * silu_slope(
        leading_part[2][0]
    )
    back_one, sums_one, totals_one = norm_backward([(d_united, fifth[0]), (d_aux, leading_part[2])])
    unite_shift_grad = totals_one[0]
    d_unite_pre = back_one[0].astype(jnp.bfloat16)
    d_aux_pre = back_one[1].astype(jnp.bfloat16)
    settle(5, conv_kernel_back(joined, d_unite_pre, 1))
    d_merged, d_branch = pick_bins(conv_input_back(d_unite_pre, w_unite, 1), C_OUT, tables, images)
    d_merged, d_branch = (
        lax.psum_scatter(
            d_merged.astype(jnp.bfloat16), "tensor", scatter_dimension=3, tiled=True
        ).astype(jnp.float32),
        lax.psum_scatter(
            d_branch.astype(jnp.bfloat16), "tensor", scatter_dimension=2, tiled=True
        ).astype(jnp.float32),
    )
    settle(7, conv_kernel_back(whole, d_aux_pre, 1))
    branch_back = []
    for group, bins in enumerate(BIN_COUNTS):
        piece = d_branch[:, BIN_STARTS[group] : BIN_STARTS[group] + bins * bins]
        branch_back.append((piece * silu_slope(fourth[group][0]), fourth[group]))
    back_two, sums_two, unused = norm_backward(branch_back)
    d_branch_pre = jnp.concatenate(back_two, axis=1).astype(jnp.bfloat16)
    d_branch_full = lax.all_gather(d_branch_pre, "tensor", axis=2, tiled=True)
    branch_grads = []
    for group, bins in enumerate(BIN_COUNTS):
        rows_in, cols_in, rows_pick, cols_pick, cell_count = tables[group]
        piece = d_branch_full[:, BIN_STARTS[group] : BIN_STARTS[group] + bins * bins]
        branch_grads.append(
            jnp.einsum("ipc,ipd->cd", pooled_list[group], piece, preferred_element_type=jnp.float32)
        )
        d_pooled = jnp.dot(piece, w_branch[group].T, preferred_element_type=jnp.float32).reshape(
            images, bins, bins, -1
        )
        d_merged = d_merged + jnp.einsum(
            "ikh,ilw,iklc->ihwc", rows_in, cols_in, d_pooled / cell_count
        )
    settle(4, jnp.stack(branch_grads))
    d_summed = d_merged * silu_slope(summed)
    back_three, sums_three, unused = norm_backward(
        [(d_summed, third[0]), (d_summed, leading_part[1])]
    )
    d_expand_pre = back_three[0].astype(jnp.bfloat16)
    d_short_pre = back_three[1].astype(jnp.bfloat16)
    settle(
        3,
        jnp.einsum(
            "ihwc,ihwd->cd", hidden_two_full, d_expand_pre, preferred_element_type=jnp.float32
        ),
    )
    settle(1, jnp.einsum("ihwc,ihwd->cd", whole, d_short_pre, preferred_element_type=jnp.float32))
    d_two = scatter_channels(jnp.dot(d_expand_pre, w_expand.T, preferred_element_type=jnp.float32))
    back_four, sums_four, unused = norm_backward([(d_two * silu_slope(second[0][0]), second[0])])
    d_middle_pre = back_four[0].astype(jnp.bfloat16)
    settle(2, conv_kernel_back(hidden_full, d_middle_pre, 4))
    d_one = scatter_channels(conv_input_back(d_middle_pre, w_middle, 4))
    back_five, sums_five, unused = norm_backward(
        [(d_one * silu_slope(leading_part[0][0]), leading_part[0])]
    )
    settle(
        0,
        jnp.einsum(
            "ihwc,ihwd->cd",
            whole,
            back_five[0].astype(jnp.bfloat16),
            preferred_element_type=jnp.float32,
        ),
    )
    beta_grads = (
        [sums_five[0], sums_three[2], sums_four[0], sums_three[0]]
        + [sums_two[2 * g] for g in range(4)]
        + [sums_one[0], sums_one[2]]
    )
    gamma_grads = (
        [sums_five[1], sums_three[3], sums_four[1], sums_three[1]]
        + [sums_two[2 * g + 1] for g in range(4)]
        + [sums_one[1], sums_one[3]]
    )
    settle(9, jnp.stack([jnp.concatenate(gamma_grads), jnp.concatenate(beta_grads)]))
    ordered = [reduced[index] for index in range(10)]
    grad_share = lax.psum_scatter(
        jnp.concatenate([part.reshape(owners, -1) for part in ordered], axis=1),
        "batch",
        scatter_dimension=0,
        tiled=True,
    )
    square_all, loss_sum = lax.psum(
        (jnp.sum(grad_share * grad_share), loss_local), ("batch", "tensor")
    )
    grad_norm = jnp.sqrt(square_all)
    clipped = grad_share * jnp.minimum(1.0, 0.05 / (grad_norm + 1e-06))
    new_first = 0.5 * first_moment + 0.5 * clipped
    new_second = 0.5 * squared_mean + 0.5 * clipped * clipped
    keep = 1.0 - 0.5**STEP
    new_params = params - 0.01 * (
        new_first / keep / (jnp.sqrt(new_second / keep) + 1e-08) + 0.01 * params
    )
    new_average = 0.999 * average + 0.001 * new_params
    return (
        new_params,
        new_first,
        new_second,
        new_average,
        new_params.astype(jnp.bfloat16),
        grad_norm,
        loss_sum,
        loss_weight,
        unite_shift_grad,
    )


CELLS = MAP * MAP
EDGE = 104
BATCH = "batch"
TENSOR = "tensor"
GROUP_ROWS = ((0, 1), (1, 5), (5, 14), (14, 50))
BINS = 64
BF = jnp.bfloat16
F32 = jnp.float32
MESH = pl.DeviceIdType.MESH
HALF = 4
OWNERS = 8
SPLITS = 4
MERGED = 4
SLOTS = 5


def scratch_plan():
    plan = dict(
        w_r=((1024, 128), BF),
        w_s=((1024, 512), BF),
        w_m=((4608, 128), BF),
        w_e=((512, 512), BF),
        w_b=((2048, 512), BF),
        w_u=((18432, 128), BF),
        w_own=((4608, 128), BF),
        w_a=((4608, 128), BF),
        w_pair=((1024, 640), BF),
        w_c=((128, 256), BF),
        w_ac=((64, 256), F32),
        gain_in=((OWNERS, 32, 128), F32),
        whole=((SPLITS, CELLS, 256), BF),
        ins=((CELLS, 128), F32),
        col=((CELLS, 128), F32),
        lab=((CELLS, 128), F32),
        table=((BINS, CELLS), F32),
        pool=((BINS, CELLS), BF),
        pick=((BINS, CELLS), BF),
        cells_in=((BINS, 128), F32),
        pad=((9, CELLS + 2 * EDGE, 128), F32),
        grad_pad=((CELLS + 2 * EDGE, 128), F32),
        pre_r=((CELLS, 128), F32),
        pre_s=((CELLS, 512), F32),
        pre_a=((CELLS, 128), F32),
        pre_m=((CELLS, 128), F32),
        pre_e=((CELLS, 512), F32),
        pre_u=((CELLS, 128), F32),
        act_a=((CELLS, 128), BF),
        h1=((SPLITS, CELLS, 128), BF),
        h2=((SPLITS, CELLS, 128), BF),
        joined=((SPLITS, CELLS, 512), BF),
        joined_t=((SPLITS, 512, CELLS), BF),
        pooled=((BINS, 512), BF),
        part_b=((SPLITS, BINS, 128), BF),
        recv_b=((SPLITS, BINS, 128), BF),
        all_b=((OWNERS, BINS, 128), BF),
        act_b=((SPLITS, OWNERS * BINS, 128), BF),
        zsum=((2, OWNERS * BINS, 128), F32),
        z_send=((OWNERS, 2, BINS, 128), BF),
        z_recv=((OWNERS, 2, BINS, 128), BF),
        united=((CELLS, 128), BF),
        logit_send=((CELLS, 512), BF),
        logit_recv=((SPLITS, 144, 512), BF),
        slope_in=((SPLITS, 144, 512), BF),
        d_f=((CELLS, 128), F32),
        d_f2=((CELLS, 128), F32),
        cat_u=((CELLS, 1152), BF),
        cat_a=((CELLS, 640), BF),
        dz_send=((9, BINS, 128), BF),
        dz_recv=((OWNERS, 2, BINS, 128), BF),
        d_act_send=((SPLITS, OWNERS * BINS, 128), BF),
        d_act_recv=((SPLITS, OWNERS * BINS, 128), BF),
        d_img_send=((OWNERS, BINS, 128), BF),
        d_img_recv=((OWNERS, BINS, 128), BF),
        d_bp=((SPLITS, BINS, 128), BF),
        dm_near=((2, CELLS, 512), BF),
        dm_far=((CELLS, 512), BF),
        d_sum=((CELLS, 512), F32),
        d_e=((CELLS, 512), BF),
        d_s=((CELLS, 512), BF),
        dh_send=((SPLITS, CELLS, 128), BF),
        dh_recv=((2, SPLITS, CELLS, 128), BF),
        d_low=((CELLS, 128), BF),
        end_t=((SPLITS, 8, 128), F32),
    )
    for name, rows in SYNCS.items():
        plan["sync_" + name] = ((OWNERS, rows, 128), F32)
    for name, (rows, lanes, kind) in PARTS.items():
        plan["first_" + name] = ((HALF, rows, lanes), kind)
        plan["second_" + name] = ((HALF - 1, rows, lanes), kind)
    plan["first_u"] = ((HALF, SLOTS, 512, 128), BF)
    plan["second_u"] = ((HALF - 1, SLOTS, 512, 128), BF)
    return plan


SYNCS = dict(one=16, two=8, three=8, five=8, b1=8, b3=8, b4=16, b5=8, b6=8, end=8)
PARTS = dict(
    r=(128, 128, BF),
    s=(128, 512, BF),
    m=(576, 128, BF),
    e=(64, 512, BF),
    b=(256, 512, BF),
    a=(576, 128, BF),
    c=(16, 256, BF),
    ac=(8, 256, F32),
)
SEMAPHORES = 1100


class Refs:
    pass


def fold(value):
    return value.reshape(-1, 8, value.shape[-1]).sum(0)


def total(value):
    return jnp.sum(value, axis=0, keepdims=True)


def wide(value, times):
    return jnp.concatenate([value] * times, axis=1)


def dot(left, right):
    return jnp.dot(left, right, preferred_element_type=F32)


def dot_nt(left, right):
    return lax.dot_general(left, right, (((1,), (1,)), ((), ())), preferred_element_type=F32)


def dot_tn(left, right):
    return lax.dot_general(left, right, (((0,), (0,)), ((), ())), preferred_element_type=F32)


def loop(count, body):
    def step(k, carry):
        body(k)
        return carry

    lax.fori_loop(0, count, step, 0)


def rows_at(k, block):
    return pl.ds(pl.multiple_of(k * block, block), block)


def step_kernel(names, *refs):
    (
        sizes, lab_in, feat, gain_own, p_r, p_s, p_m, p_e, p_b, p_u, p_a, p_c, p_ac,
        o_r, o_s, o_m, o_e, o_b, o_u, o_a, o_c, o_ac, o_gain, o_misc,
    ) = refs[:24]
    v = Refs()
    for name, ref in zip(names, refs[24:]):
        setattr(v, name, ref)
    sems = refs[-1]
    me = lax.axis_index(BATCH)
    t = lax.axis_index(TENSOR)
    partner = me + 1 - 2 * lax.rem(me, 2)
    t_core = t + 1 - 2 * lax.rem(t, 2)
    t_x = lax.rem(t + 2, SPLITS)
    t_diag = lax.rem(t_core + 2, SPLITS)
    taken = [0]

    def take(count):
        start = taken[0]
        taken[0] = start + count
        assert taken[0] <= SEMAPHORES
        return start

    def far_peer(base, step):
        return lax.rem(base + 2 * step, OWNERS)

    def remote(src, dst, send, recv, device):
        return pltpu.make_async_remote_copy(
            src_ref=src,
            dst_ref=dst,
            send_sem=sems.at[send],
            recv_sem=sems.at[recv],
            device_id=device,
            device_id_type=MESH,
        )

    late = []

    barrier = pltpu.get_barrier_semaphore()
    for k in range(1, OWNERS):
        pl.semaphore_signal(
            barrier, inc=1, device_id={BATCH: lax.rem(me + k, OWNERS)}, device_id_type=MESH
        )
    for k in range(1, SPLITS):
        pl.semaphore_signal(
            barrier, inc=1, device_id={TENSOR: lax.rem(t + k, SPLITS)}, device_id_type=MESH
        )
    pl.semaphore_wait(barrier, OWNERS + SPLITS - 2)

    class Gather:
        def __init__(self, piece, full, rows):
            self.piece, self.full, self.rows = piece, full, rows
            self.near_s, self.far_s, self.pass_s = take(1), take(HALF), take(HALF)
            self.recv, self.keep = take(OWNERS), take(1)

        def at(self, owner):
            if self.rows is None:
                return self.full.at[owner]
            return self.full.at[rows_at(owner, self.rows), :]

        def local(self):
            return pltpu.make_async_copy(self.piece, self.at(me), sems.at[self.keep])

        def near(self):
            return remote(
                self.piece, self.at(me), self.near_s, self.recv + me, {BATCH: partner}
            )

        def far(self, step):
            return remote(
                self.piece,
                self.at(me),
                self.far_s + step,
                self.recv + me,
                {BATCH: far_peer(me, step)},
            )

        def passed(self, step, base):
            source = far_peer(base, step)
            return remote(
                self.at(source),
                self.at(source),
                self.pass_s + step,
                self.recv + source,
                {BATCH: partner},
            )

        def start_far(self):
            self.local().start()
            for step in range(1, HALF):
                self.far(step).start()

        def start_near(self):
            self.near().start()

        def forward(self):
            for step in range(1, HALF):
                self.passed(step, me).wait_recv()
                self.passed(step, me).start()

        def finish(self):
            for step in range(HALF):
                self.passed(step, partner).wait_recv()
            self.local().wait()
            self.near().wait_send()
            for step in range(1, HALF):
                self.far(step).wait_send()

        def drain(self):
            for step in range(1, HALF):
                self.passed(step, me).wait_send()

    g_gain = Gather(gain_own, v.gain_in, None)
    g_r = Gather(p_r, v.w_r, 128)
    g_s = Gather(p_s, v.w_s, 128)
    g_a = Gather(p_a, v.w_a, 576)
    g_m = Gather(p_m, v.w_m, 576)
    g_e = Gather(p_e, v.w_e, 64)
    g_b = Gather(p_b, v.w_b, 256)
    g_c = Gather(p_c, v.w_c, 16)
    g_ac = Gather(p_ac, v.w_ac, 8)

    def chunk_of(owner, j):
        return lax.rem(owner + j, 8)

    def merged_rows(owner, j):
        tap = owner + lax.div(owner + j, 8)
        return pl.ds(pl.multiple_of((tap * MERGED + chunk_of(owner, j)) * 512, 512), 512)

    def each_merged(owner, body):
        def step(j):
            pl.when(chunk_of(owner, j) < MERGED)(lambda: body(j))

        loop(9, step)

    class GatherUnite:
        def __init__(self):
            self.near_s, self.far_s, self.pass_s = take(9), take(9 * HALF), take(9 * HALF)
            self.recv, self.keep, self.keep_all = take(9 * OWNERS), take(9), take(1)

        def source(self, j):
            return p_u.at[rows_at(j, 512), :]

        def full(self, owner, j):
            return v.w_u.at[merged_rows(owner, j), :]

        def local(self, j):
            return pltpu.make_async_copy(
                self.source(j), self.full(me, j), sems.at[self.keep + j]
            )

        def whole(self):
            return pltpu.make_async_copy(p_u, v.w_own, sems.at[self.keep_all])

        def near(self, j):
            return remote(
                self.source(j),
                self.full(me, j),
                self.near_s + j,
                self.recv + me * 9 + j,
                {BATCH: partner},
            )

        def far(self, step, j):
            return remote(
                self.source(j),
                self.full(me, j),
                self.far_s + step * 9 + j,
                self.recv + me * 9 + j,
                {BATCH: far_peer(me, step)},
            )

        def passed(self, step, j, base):
            source = far_peer(base, step)
            return remote(
                self.full(source, j),
                self.full(source, j),
                self.pass_s + step * 9 + j,
                self.recv + source * 9 + j,
                {BATCH: partner},
            )

        def start_far(self):
            self.whole().start()

            def begin(j):
                self.local(j).start()
                for step in range(1, HALF):
                    self.far(step, j).start()

            each_merged(me, begin)

        def start_near(self):
            each_merged(me, lambda j: self.near(j).start())

        def forward(self, low, top):
            def step_j(k):
                j = low + k
                for step in range(1, HALF):

                    def go(step=step):
                        self.passed(step, j, me).wait_recv()
                        self.passed(step, j, me).start()

                    pl.when(chunk_of(far_peer(me, step), j) < MERGED)(go)

            loop(top - low, step_j)

        def finish(self):
            for step in range(HALF):
                each_merged(
                    far_peer(partner, step),
                    lambda j, step=step: self.passed(step, j, partner).wait_recv(),
                )

            def end(j):
                self.local(j).wait()
                self.near(j).wait_send()
                for step in range(1, HALF):
                    self.far(step, j).wait_send()

            each_merged(me, end)

        def drain(self):
            for step in range(1, HALF):
                each_merged(
                    far_peer(me, step),
                    lambda j, step=step: self.passed(step, j, me).wait_send(),
                )

    g_u = GatherUnite()

    class Sync:
        def __init__(self, buf):
            self.buf = buf
            self.send, self.recv = take(OWNERS), take(OWNERS)

        def copy(self, k, slot):
            return remote(
                self.buf.at[slot],
                self.buf.at[slot],
                self.send + k,
                self.recv + slot,
                {BATCH: lax.rem(me + k, OWNERS)},
            )

        def start(self, rows):
            for index, row in enumerate(rows):
                self.buf[me, index : index + 1, :] = row
            for index in range(len(rows), self.buf.shape[1]):
                self.buf[me, index : index + 1, :] = jnp.zeros((1, 128), F32)
            for k in range(1, OWNERS):
                self.copy(k, me).start()

        def wait(self):
            for k in range(1, OWNERS):
                self.copy(k, lax.rem(me + k, OWNERS)).wait_recv()
            for k in range(1, OWNERS):
                self.copy(k, me).wait_send()
            value = self.buf[0]
            for slot in range(1, OWNERS):
                value = value + self.buf[slot]
            return value

    class Spread:

        def __init__(self, buf):
            self.buf = buf
            self.send, self.recv = take(SPLITS), take(SPLITS)

        def copy(self, k, slot):
            return remote(
                self.buf.at[slot],
                self.buf.at[slot],
                self.send + k,
                self.recv + slot,
                {TENSOR: lax.rem(t + k, SPLITS)},
            )

        def start(self):
            for k in range(1, SPLITS):
                self.copy(k, t).start()

        def wait(self):
            for k in range(1, SPLITS):
                self.copy(k, lax.rem(t + k, SPLITS)).wait_recv()
            for k in range(1, SPLITS):
                self.copy(k, t).wait_send()

    class Exchange:

        def __init__(self, axis, count, part, into):
            self.axis, self.count, self.part, self.into = axis, count, part, into
            self.mine = me if axis == BATCH else t
            self.send, self.recv = take(count), take(count)

        def copy(self, k, slot):
            other = lax.rem(self.mine + k, self.count)
            return remote(
                self.part(other),
                self.into(slot),
                self.send + k,
                self.recv + slot,
                {self.axis: other},
            )

        def start(self):
            for k in range(1, self.count):
                self.copy(k, self.mine).start()

        def wait(self):
            for k in range(1, self.count):
                self.copy(k, lax.rem(self.mine + k, self.count)).wait_recv()
            for k in range(1, self.count):
                self.copy(k, self.mine).wait_send()

    feat_keep = take(1)
    feat_local = pltpu.make_async_copy(feat, v.whole.at[t], sems.at[feat_keep])
    feat_spread = Exchange(TENSOR, SPLITS, lambda other: feat, lambda slot: v.whole.at[slot])
    for item in (g_gain, g_r, g_s, g_a):
        item.start_far()
        item.start_near()
    feat_local.start()
    feat_spread.start()

    high, across = sizes[0, 0], sizes[0, 1]
    place = lax.broadcasted_iota(jnp.int32, (CELLS, 128), 0).astype(F32)
    row_of = jnp.floor((place + 0.5) / MAP)
    col_of = place - MAP * row_of
    within = (row_of < high.astype(F32)) & (col_of < across.astype(F32))
    v.ins[...] = jnp.where(within, 1.0, 0.0)
    v.col[...] = col_of
    v.lab[...] = jnp.where(within, lab_in[...], -1.0)
    v.table[...] = jnp.zeros((BINS, CELLS), F32)
    lane_place = lax.broadcasted_iota(jnp.int32, (1, CELLS), 1).astype(F32)
    lane_row = jnp.floor((lane_place + 0.5) / MAP)
    lane_col = lane_place - MAP * lane_row

    def ranges(extent, bins, where):
        inside, chosen, counts = [], [], []
        for k in range(bins):
            low = lax.div(k * extent, bins)
            top = lax.div((k + 1) * extent + (bins - 1), bins)
            member = (where >= low.astype(F32)) & (where < top.astype(F32))
            inside.append(jnp.where(member, 1.0, 0.0))
            picked = where * bins >= (k * extent).astype(F32)
            if k < bins - 1:
                picked = picked & (where * bins < ((k + 1) * extent).astype(F32))
            chosen.append(jnp.where(picked, 1.0, 0.0))
            counts.append(top - low)
        return inside, chosen, counts

    picks = []
    v.cells_in[...] = jnp.ones((BINS, 128), F32)
    for group, bins in enumerate(BIN_COUNTS):
        r_in, r_pick, r_count = ranges(high, bins, lane_row)
        c_in, c_pick, c_count = ranges(across, bins, lane_col)
        for a in range(bins):
            for b in range(bins):
                spot = BIN_STARTS[group] + a * bins + b
                v.table[spot : spot + 1, :] = r_in[a] * c_in[b]
                v.cells_in[spot : spot + 1, :] = jnp.full(
                    (1, 128), (r_count[a] * c_count[b]).astype(F32)
                )
                picks.append((spot, r_pick[a] * c_pick[b]))
    v.pool[...] = v.table[...].astype(BF)
    for spot, value in picks:
        v.table[spot : spot + 1, :] = value
    v.pick[...] = v.table[...].astype(BF)
    zeros_edge = jnp.zeros((EDGE, 128), F32)
    for tap in range(9):
        v.pad[tap, 0:EDGE, :] = zeros_edge
        v.pad[tap, EDGE + CELLS :, :] = zeros_edge
    v.grad_pad[0:EDGE, :] = zeros_edge
    v.grad_pad[EDGE + CELLS :, :] = zeros_edge
    lanes = lax.broadcasted_iota(jnp.int32, (1, 256), 1).astype(F32)
    counts = jnp.zeros((8, 256), F32)
    for k in range(0, CELLS, 96):
        counts = counts + fold(
            jnp.where(wide(v.lab[k : k + 96, :], 2) == lanes, 1.0, 0.0)
        )
    class_local = total(counts)
    cells_local = jnp.full((1, 128), (high * across).astype(F32))
    left_half = lax.broadcasted_iota(jnp.int32, (64, 128), 1) < 64

    for item in (g_gain, g_r, g_s):
        item.forward()
    for item in (g_m, g_e):
        item.start_far()
    g_a.forward()
    for item in (g_b, g_c, g_ac, g_u):
        item.start_far()
    for item in (g_gain, g_r, g_s, g_a):
        item.finish()
    for item in (g_m, g_e, g_b, g_c, g_ac):
        item.start_near()
    feat_local.wait()
    feat_spread.wait()
    gains = v.gain_in[0]
    for slot in range(1, OWNERS):
        gains = gains + v.gain_in[slot]

    def gamma(row, width=1):
        return jnp.concatenate([gains[row + k : row + k + 1] for k in range(width)], axis=1)

    def beta(row, width=1):
        return gamma(16 + row, width)

    def unpack(chunk):
        for pair in range(5):
            even = v.w_a[rows_at(2 * pair * 8 + chunk, 64), :].astype(F32)
            if pair < 4:
                odd = v.w_a[rows_at((2 * pair + 1) * 8 + chunk, 64), :].astype(F32)
            else:
                odd = jnp.zeros((64, 128), F32)
            low = jnp.where(left_half, even, pltpu.roll(odd, 64, 1))
            top = jnp.where(left_half, pltpu.roll(even, 64, 1), odd)
            v.w_pair[rows_at(2 * chunk, 64), pair * 128 : pair * 128 + 128] = low.astype(BF)
            v.w_pair[rows_at(2 * chunk + 1, 64), pair * 128 : pair * 128 + 128] = top.astype(BF)

    loop(8, unpack)

    def whole_feat():
        return jnp.concatenate([v.whole[k] for k in range(SPLITS)], axis=1)

    v.pre_r[...] = dot(whole_feat(), v.w_r[...])
    for k in range(0, 512, 256):
        v.pre_s[:, k : k + 256] = dot(whole_feat(), v.w_s[:, k : k + 256])
    for pair in (0, 2):
        value = dot(whole_feat(), v.w_pair[:, pair * 128 : pair * 128 + 256])
        v.pad[pair, EDGE : EDGE + CELLS, :] = value[:, :128]
        v.pad[pair + 1, EDGE : EDGE + CELLS, :] = value[:, 128:]
    v.pad[4, EDGE : EDGE + CELLS, :] = dot(whole_feat(), v.w_pair[:, 512:640])
    g_m.forward()

    def offset(tap, spacing):
        return ((tap // 3 - 1) * MAP + (tap % 3 - 1)) * spacing

    def col_mask(at, right):
        where = v.col[at, :] + float(right)
        return jnp.where((where >= 0.0) & (where < float(MAP)), 1.0, 0.0)

    BLOCK = 72

    def shift_sum(taps, spacing, at, slot_of):
        out = None
        for b in (-1, 0, 1):
            part = None
            for tap in taps:
                if tap % 3 - 1 != b:
                    continue
                start = EDGE + at + offset(tap, spacing)
                value = v.pad[slot_of(tap), start : start + BLOCK, :]
                part = value if part is None else part + value
            if part is None:
                continue
            if b:
                part = part * col_mask(slice(at, at + BLOCK), b * spacing)
            out = part if out is None else out + part
        return out

    left_wide = lax.broadcasted_iota(jnp.int32, (BLOCK, 128), 1) < 64
    for at in range(0, CELLS, BLOCK):
        even = shift_sum((0, 2, 4, 6, 8), 1, at, lambda tap: tap // 2)
        odd = shift_sum((1, 3, 5, 7), 1, at, lambda tap: tap // 2)
        v.pre_a[at : at + BLOCK, :] = jnp.where(left_wide, even + pltpu.roll(odd, 64, 1), 0.0)

    def masked_sums(ref):
        width = ref.shape[1]

        def step(k, carry):
            at = rows_at(k, 96)
            value = ref[at, :]
            kept = value * (v.ins[at, :] if width == 128 else wide(v.ins[at, :], width // 128))
            return (carry[0] + fold(kept), carry[1] + fold(kept * value))

        zero = jnp.zeros((8, width), F32)
        sums = lax.fori_loop(0, 6, step, (zero, zero))
        return total(sums[0]), total(sums[1])

    def split_rows(value):
        return [value[:, k : k + 128] for k in range(0, value.shape[1], 128)]

    def join_rows(value, row, count):
        return jnp.concatenate([value[row + k : row + k + 1] for k in range(count)], axis=1)

    def moments(first, second, count):
        mean = first / count
        return mean, lax.rsqrt(second / count - mean * mean + 1e-05)

    sync = Sync(v.sync_one)
    r1, r2 = masked_sums(v.pre_r)
    s1, s2 = masked_sums(v.pre_s)
    a1, a2 = masked_sums(v.pre_a)
    sync.start(
        [r1, r2] + split_rows(s1) + split_rows(s2) + [a1, a2, cells_local] + split_rows(class_local)
    )
    sums = sync.wait()
    g_u.start_near()
    count = sums[12:13]
    count4 = wide(count, 4)
    norm_r = moments(sums[0:1], sums[1:2], count)
    norm_s = moments(join_rows(sums, 2, 4), join_rows(sums, 6, 4), count4)
    norm_a = moments(sums[10:11], sums[11:12], count)
    class_count = join_rows(sums, 13, 2)

    def normed(ref, at, norm):
        return (ref[at, :] - norm[0]) * norm[1]

    spread_1 = Spread(v.h1)

    def make_h1(k):
        at = rows_at(k, 96)
        v.h1[t, at, :] = jax.nn.silu(gamma(0) * normed(v.pre_r, at, norm_r) + beta(0)).astype(BF)

    loop(6, make_h1)
    spread_1.start()

    def make_a(k):
        at = rows_at(k, 96)
        v.act_a[at, :] = jax.nn.silu(gamma(15) * normed(v.pre_a, at, norm_a) + beta(15)).astype(BF)

    loop(6, make_a)
    g_e.forward()
    g_m.finish()
    spread_1.wait()

    def full_h(ref):
        return jnp.concatenate([ref[k] for k in range(SPLITS)], axis=1)

    def middle(tap):
        v.pad[tap, EDGE : EDGE + CELLS, :] = dot(full_h(v.h1), v.w_m[rows_at(tap, 512), :])

    loop(9, middle)
    for at in range(0, CELLS, BLOCK):
        v.pre_m[at : at + BLOCK, :] = shift_sum(range(9), 4, at, lambda tap: tap)
    sync = Sync(v.sync_two)
    sync.start(list(masked_sums(v.pre_m)))
    g_e.finish()
    sums = sync.wait()
    g_b.forward()
    norm_m = moments(sums[0:1], sums[1:2], count)
    spread_2 = Spread(v.h2)

    def make_h2(k):
        at = rows_at(k, 96)
        v.h2[t, at, :] = jax.nn.silu(gamma(5) * normed(v.pre_m, at, norm_m) + beta(5)).astype(BF)

    loop(6, make_h2)
    spread_2.start()
    spread_2.wait()
    for k in range(0, 512, 256):
        v.pre_e[:, k : k + 256] = dot(full_h(v.h2), v.w_e[:, k : k + 256])
    sync = Sync(v.sync_three)
    e1, e2 = masked_sums(v.pre_e)
    sync.start(split_rows(e1) + split_rows(e2))
    g_c.forward()
    g_ac.forward()
    sums = sync.wait()
    norm_e = moments(join_rows(sums, 0, 4), join_rows(sums, 4, 4), count4)

    def summed(at):
        return (
            gamma(6, 4) * normed(v.pre_e, at, norm_e)
            + beta(6, 4)
            + gamma(1, 4) * normed(v.pre_s, at, norm_s)
            + beta(1, 4)
        )

    def make_merged(k):
        at = rows_at(k, 48)
        v.joined[t, at, :] = jax.nn.silu(summed(at)).astype(BF)

    loop(12, make_merged)

    j_send, j_recv = take(3), take(SPLITS)

    def joined_copy(k, slot, device):
        return remote(
            v.joined.at[slot], v.joined.at[slot], j_send + k, j_recv + slot, {TENSOR: device}
        )

    joined_copy(0, t, t_x).start()
    joined_copy(1, t, t_core).start()

    bin_row = lax.broadcasted_iota(jnp.int32, (BINS, 1), 0)

    def group_mask(group, shape=None):
        low, top = GROUP_ROWS[group]
        kept = jnp.where((bin_row >= low) & (bin_row < top), 1.0, 0.0)
        return kept if shape is None else jnp.broadcast_to(kept, shape)

    cells_in = wide(v.cells_in[...], 4)
    pooled = dot(v.pool[...], v.joined[t]) / cells_in
    v.pooled[...] = pooled.astype(BF)
    g_b.finish()
    part = jnp.zeros((BINS, 512), F32)
    for group in range(4):
        rows = (v.pooled[...].astype(F32) * group_mask(group)).astype(BF)
        part = part + dot(rows, v.w_b[group * 512 : group * 512 + 512, :])
    for k in range(SPLITS):
        v.part_b[k] = part[:, k * 128 : k * 128 + 128].astype(BF)
    v.recv_b[t] = v.part_b[t]
    ex = Exchange(TENSOR, SPLITS, lambda o: v.part_b.at[o], lambda s: v.recv_b.at[s])
    ex.start()
    g_u.forward(0, 2)
    joined_copy(0, t_x, t_x).wait_recv()
    joined_copy(2, t_x, t_core).start()
    ex.wait()
    own_b = v.recv_b[0].astype(F32)
    for k in range(1, SPLITS):
        own_b = own_b + v.recv_b[k].astype(F32)
    v.all_b[me] = own_b.astype(BF)
    ex = Exchange(BATCH, OWNERS, lambda o: v.all_b.at[me], lambda s: v.all_b.at[s])
    ex.start()
    g_u.forward(2, 4)
    ex.wait()
    all_b = [v.all_b[k].astype(F32) for k in range(OWNERS)]
    sum_b, square_b = all_b[0], all_b[0] * all_b[0]
    for k in range(1, OWNERS):
        sum_b = sum_b + all_b[k]
        square_b = square_b + all_b[k] * all_b[k]
    mean_b = jnp.zeros((BINS, 128), F32)
    scale_b = jnp.zeros((BINS, 128), F32)
    gamma_b = jnp.zeros((BINS, 128), F32)
    beta_b = jnp.zeros((BINS, 128), F32)
    count_b = jnp.zeros((BINS, 1), F32)
    for group, bins in enumerate(BIN_COUNTS):
        kept = group_mask(group)
        size = float(OWNERS * bins * bins)
        mean, scaling = moments(total(sum_b * kept), total(square_b * kept), size)
        mean_b = mean_b + kept * mean
        scale_b = scale_b + kept * scaling
        gamma_b = gamma_b + kept * gamma(10 + group)
        beta_b = beta_b + kept * beta(10 + group)
        count_b = count_b + kept / size
    spread_b = Spread(v.act_b)
    for k in range(OWNERS):
        out = gamma_b * ((all_b[k] - mean_b) * scale_b) + beta_b
        v.act_b[t, k * BINS : k * BINS + BINS, :] = jax.nn.silu(out).astype(BF)
    spread_b.start()
    g_u.forward(4, 6)
    spread_b.wait()
    g_u.whole().wait()
    row_512 = lax.broadcasted_iota(jnp.int32, (OWNERS * BINS, 1), 0) & (BINS - 1)
    group_id = jnp.where(
        row_512 < 1, 0, jnp.where(row_512 < 5, 1, jnp.where(row_512 < 14, 2, jnp.where(row_512 < 50, 3, 9)))
    )

    def full_act():
        return jnp.concatenate([v.act_b[k] for k in range(SPLITS)], axis=1)

    v.zsum[...] = jnp.zeros((2, OWNERS * BINS, 128), F32)

    def own_branch(j, body):
        chunk = chunk_of(me, j)
        pl.when(chunk >= MERGED)(lambda: body(chunk - MERGED, lax.div(me + j, 8)))

    def make_z(j):
        def body(group, side):
            kept = jnp.where(group_id == group, 1.0, 0.0)
            rows = (full_act().astype(F32) * kept).astype(BF)
            v.zsum[side] = v.zsum[side] + dot(rows, v.w_own[rows_at(j, 512), :])

        own_branch(j, body)

    loop(9, make_z)
    for k in range(OWNERS):
        for side in range(2):
            v.z_send[k, side] = v.zsum[side, k * BINS : k * BINS + BINS, :].astype(BF)
    v.z_recv[me] = v.z_send[me]
    ex = Exchange(BATCH, OWNERS, lambda o: v.z_send.at[o], lambda s: v.z_recv.at[s])
    ex.start()
    g_u.forward(6, 9)
    joined_copy(1, t_core, t_core).wait_recv()
    joined_copy(2, t_diag, t_core).wait_recv()
    for k in range(SPLITS):
        v.joined_t[k] = v.joined[k].T
    ex.wait()
    g_u.finish()

    pick2 = jnp.concatenate([v.pick[...], v.pick[...]], axis=0)

    def tap_z(tap):
        if tap == 0:
            return v.z_recv[0, 0].astype(F32)
        if tap == 8:
            return v.z_recv[7, 1].astype(F32)
        return v.z_recv[tap, 0].astype(F32) + v.z_recv[tap - 1, 1].astype(F32)

    def full_joined():
        return jnp.concatenate([v.joined[k] for k in range(SPLITS)], axis=1)

    def w_tap(tap):
        return v.w_u[rows_at(tap, 2048), :]

    def unite_pair(p):
        value = dot(full_joined(), jnp.concatenate([w_tap(2 * p), w_tap(2 * p + 1)], axis=1))
        v.pad[2 * p, EDGE : EDGE + CELLS, :] = value[:, :128]
        v.pad[2 * p + 1, EDGE : EDGE + CELLS, :] = value[:, 128:]

    loop(4, unite_pair)
    v.pad[8, EDGE : EDGE + CELLS, :] = dot(full_joined(), w_tap(8))
    for tap in range(9):
        z = tap_z(tap)
        high_z = z.astype(BF)
        low_z = (z - high_z.astype(F32)).astype(BF)
        v.pad[tap, EDGE : EDGE + CELLS, :] = v.pad[tap, EDGE : EDGE + CELLS, :] + dot_tn(
            pick2, jnp.concatenate([high_z, low_z], axis=0)
        )
    for at in range(0, CELLS, BLOCK):
        v.pre_u[at : at + BLOCK, :] = shift_sum(range(9), 1, at, lambda tap: tap)
    sync = Sync(v.sync_five)
    sync.start(list(masked_sums(v.pre_u)))
    for item in (g_c, g_ac):
        item.finish()
    for item in (g_gain, g_r, g_s, g_a, g_m, g_e, g_b, g_c, g_ac, g_u):
        item.drain()
    joined_copy(0, t, t_x).wait_send()
    joined_copy(1, t, t_core).wait_send()
    joined_copy(2, t_x, t_core).wait_send()
    w_ac = jnp.concatenate([v.w_ac[...], jnp.zeros((64, 256), F32)], axis=0).astype(BF)
    sums = sync.wait()
    norm_u = moments(sums[0:1], sums[1:2], count)

    def make_u(k):
        at = rows_at(k, 96)
        v.united[at, :] = jax.nn.silu(gamma(14) * normed(v.pre_u, at, norm_u) + beta(14)).astype(BF)

    loop(6, make_u)

    v.logit_send[:, :256] = dot(v.united[...], v.w_c[...]).astype(BF)
    v.logit_send[:, 256:] = dot(v.act_a[...], w_ac).astype(BF)
    ex = Exchange(
        TENSOR,
        SPLITS,
        lambda o: v.logit_send.at[rows_at(o, 144), :],
        lambda s: v.logit_recv.at[s],
    )
    ex.start()
    v.logit_recv[t] = v.logit_send[rows_at(t, 144), :]
    total_valid = jnp.sum(class_count, axis=1, keepdims=True)
    class_weight = total_valid / (NCLS * class_count + total_valid)
    loss_weight = jnp.sum(class_count * class_weight, axis=1, keepdims=True)
    class_weight = jnp.where(lanes < float(NCLS), class_weight, 0.0)
    hot = jnp.where(wide(v.lab[rows_at(t, 144), :], 2) == lanes, 1.0, 0.0)
    cell_weight = jnp.sum(hot * class_weight, axis=1, keepdims=True)
    ex.wait()
    logits = v.logit_recv[0].astype(F32)
    for k in range(1, SPLITS):
        logits = logits + v.logit_recv[k].astype(F32)

    def log_softmax(value):
        value = jnp.where(lanes < float(NCLS), value, -1e30)
        value = value - jnp.max(value, axis=1, keepdims=True)
        powers = jnp.exp(value)
        mass = jnp.sum(powers, axis=1, keepdims=True)
        return value - jnp.log(mass), powers / mass

    log_main, p_main = log_softmax(logits[:, :256])
    log_aux, p_aux = log_softmax(logits[:, 256:])
    loss_rows = total(fold(-cell_weight * hot * (log_main + 0.4 * log_aux)))
    loss_local = loss_rows[:, :128] + loss_rows[:, 128:]
    o_misc[1:2, :] = loss_local
    v.slope_in[t, :, :256] = (cell_weight * (p_main - hot) / loss_weight).astype(BF)
    v.slope_in[t, :, 256:] = (0.4 * cell_weight * (p_aux - hot) / loss_weight).astype(BF)
    spread_g = Spread(v.slope_in)
    spread_g.start()
    spread_g.wait()
    g_main = v.slope_in[:, :, :256].reshape(CELLS, 256)
    g_aux = v.slope_in[:, :, 256:].reshape(CELLS, 256)
    v.d_f[...] = dot_nt(g_main, v.w_c[...])
    v.d_f2[...] = dot_nt(g_aux, w_ac)

    def slope(value):
        gate = jax.nn.sigmoid(value)
        return gate * (1.0 + value * (1.0 - gate))

    def through_silu(ref, pre, norm, row):
        def step(k, carry):
            at = rows_at(k, 96)
            unit = normed(pre, at, norm)
            value = ref[at, :] * slope(gamma(row) * unit + beta(row))
            ref[at, :] = value
            return (carry[0] + fold(value), carry[1] + fold(value * unit))

        zero = jnp.zeros((8, 128), F32)
        sums = lax.fori_loop(0, 6, step, (zero, zero))
        return [total(sums[0]), total(sums[1])]

    def back_norm(value, unit, mask, norm, gain, first, second, size):
        inner = value - mask * (first + unit * second) / size
        return gain * norm[1] * inner

    gain_grads = {}
    sync = Sync(v.sync_b1)
    sync.start(
        through_silu(v.d_f, v.pre_u, norm_u, 14) + through_silu(v.d_f2, v.pre_a, norm_a, 15)
    )

    class Scatter:
        def __init__(self, first, second, full, rows, out):
            self.full, self.rows, self.out = full, rows, out
            self.first, self.second = first, second
            self.near_s, self.near_r = take(HALF), take(HALF)
            self.far_s, self.far_r = take(HALF), take(HALF)
            self.block = min(rows, 64)

        def near(self, step):
            dest = far_peer(partner, step)
            return remote(
                self.full.at[rows_at(dest, self.rows), :],
                self.first.at[step],
                self.near_s + step,
                self.near_r + step,
                {BATCH: partner},
            )

        def far(self, step):
            return remote(
                self.first.at[step],
                self.second.at[step - 1],
                self.far_s + step,
                self.far_r + step,
                {BATCH: far_peer(me, step)},
            )

        def start(self):
            for step in (1, 2, 3, 0):
                self.near(step).start()

        def middle(self):
            kind = self.first.dtype
            for step in (1, 2, 3, 0):
                self.near(step).wait_recv()
                base = far_peer(me, step) * (self.rows // self.block)

                def add(k, step=step, base=base):
                    at = rows_at(k, self.block)
                    value = self.full[rows_at(base + k, self.block), :].astype(F32)
                    value = value + self.first[step, at, :].astype(F32)
                    if step:
                        self.first[step, at, :] = value.astype(kind)
                    else:
                        self.out[at, :] = value

                loop(self.rows // self.block, add)
                if step:
                    self.far(step).start()

        def end(self):
            for step in range(1, HALF):
                self.far(step).wait_recv()

            def add(k, carry):
                at = rows_at(k, self.block)
                value = self.out[at, :]
                for step in range(1, HALF):
                    value = value + self.second[step - 1, at, :].astype(F32)
                self.out[at, :] = value
                return carry + fold(value * value)

            squares = lax.fori_loop(
                0, self.rows // self.block, add, jnp.zeros((8, self.out.shape[1]), F32)
            )
            for step in (1, 2, 3, 0):
                self.near(step).wait_send()
                if step:
                    self.far(step).wait_send()
            return sum(split_rows(total(squares)))

    s_c = Scatter(v.first_c, v.second_c, v.w_c, 16, o_c)
    s_ac = Scatter(v.first_ac, v.second_ac, v.w_ac, 8, o_ac)
    s_a = Scatter(v.first_a, v.second_a, v.w_a, 576, o_a)
    s_b = Scatter(v.first_b, v.second_b, v.w_b, 256, o_b)
    s_s = Scatter(v.first_s, v.second_s, v.w_s, 128, o_s)
    s_e = Scatter(v.first_e, v.second_e, v.w_e, 64, o_e)
    s_m = Scatter(v.first_m, v.second_m, v.w_m, 576, o_m)
    s_r = Scatter(v.first_r, v.second_r, v.w_r, 128, o_r)

    class ScatterUnite:
        def __init__(self):
            self.near_s, self.near_r = take(9 * HALF), take(9 * HALF)
            self.far_s, self.far_r = take(9 * HALF), take(9 * HALF)

        def slot(self, owner, j):
            return jnp.where(j == 8, SLOTS - 1, chunk_of(owner, j))

        def near(self, step, j, base):
            dest = far_peer(base, step)
            return remote(
                v.w_u.at[merged_rows(dest, j), :],
                v.first_u.at[step, self.slot(dest, j)],
                self.near_s + step * 9 + j,
                self.near_r + step * 9 + j,
                {BATCH: partner},
            )

        def far(self, step, j, owner):
            at = self.slot(owner, j)
            return remote(
                v.first_u.at[step, at],
                v.second_u.at[step - 1, at],
                self.far_s + step * 9 + j,
                self.far_r + step * 9 + j,
                {BATCH: far_peer(me, step)},
            )

        def start(self):
            for step in (1, 2, 3, 0):
                each_merged(
                    far_peer(partner, step),
                    lambda j, step=step: self.near(step, j, partner).start(),
                )

        def middle(self, step):
            owner = far_peer(me, step)

            def go(j):
                self.near(step, j, me).wait_recv()
                slot = self.slot(owner, j)
                tap = owner + lax.div(owner + j, 8)
                base = (tap * MERGED + chunk_of(owner, j)) * 8

                def add(k):
                    at = rows_at(k, 64)
                    value = v.w_u[rows_at(base + k, 64), :].astype(F32)
                    value = value + v.first_u[step, slot, at, :].astype(F32)
                    if step:
                        v.first_u[step, slot, at, :] = value.astype(BF)
                    else:
                        o_u[rows_at(j * 8 + k, 64), :] = value

                loop(8, add)
                if step:
                    self.far(step, j, owner).start()

            each_merged(owner, go)

        def end(self):
            def go(j):
                slot = self.slot(me, j)
                for step in range(1, HALF):
                    self.far(step, j, me).wait_recv()

                def add(k):
                    at = rows_at(k, 64)
                    value = o_u[rows_at(j * 8 + k, 64), :]
                    for step in range(1, HALF):
                        value = value + v.second_u[step - 1, slot, at, :].astype(F32)
                    o_u[rows_at(j * 8 + k, 64), :] = value

                loop(8, add)

            each_merged(me, go)
            for step in (1, 2, 3, 0):
                each_merged(
                    far_peer(partner, step),
                    lambda j, step=step: self.near(step, j, partner).wait_send(),
                )
                if step:
                    each_merged(
                        far_peer(me, step),
                        lambda j, step=step: self.far(step, j, far_peer(me, step)).wait_send(),
                    )

            def square(k, carry):
                value = o_u[rows_at(k, 64), :]
                return carry + fold(value * value)

            squares = lax.fori_loop(0, 72, square, jnp.zeros((8, 128), F32))
            return sum(split_rows(total(squares)))

    s_u = ScatterUnite()

    v.w_c[...] = dot_tn(v.united[...], g_main).astype(BF)
    v.w_ac[...] = dot_tn(v.act_a[...], g_aux)[:64]
    s_c.start()
    s_ac.start()
    sums = sync.wait()
    gain_grads[14] = (sums[1:2], sums[0:1])
    gain_grads[15] = (sums[3:4], sums[2:3])

    def spread_taps(ref, pre, norm, row, first, second):
        def step(k):
            at = rows_at(k, 96)
            value = back_norm(
                ref[at, :], normed(pre, at, norm), v.ins[at, :], norm, gamma(row), first, second, count
            )
            ref[at, :] = value.astype(BF).astype(F32)

        loop(6, step)
        v.grad_pad[EDGE : EDGE + CELLS, :] = ref[...]

    def back_tap(tap, spacing, at):
        start = EDGE + at - offset(tap, spacing)
        value = v.grad_pad[start : start + 96, :]
        right = tap % 3 - 1
        if right:
            value = value * col_mask(slice(at, at + 96), -right * spacing)
        return value

    def fill(cat, spacing):
        for tap in range(9):
            for at in range(0, CELLS, 96):
                cat[at : at + 96, tap * 128 : tap * 128 + 128] = back_tap(tap, spacing, at).astype(
                    BF
                )

    spread_taps(v.d_f, v.pre_u, norm_u, 14, sums[0:1], sums[1:2])
    fill(v.cat_u, 1)

    dz = dot(v.pick[...], v.cat_u[...])
    for tap in range(9):
        v.dz_send[tap] = dz[:, tap * 128 : tap * 128 + 128].astype(BF)
    v.dz_recv[me] = v.dz_send[pl.ds(me, 2)]
    ex_dz = Exchange(
        BATCH, OWNERS, lambda o: v.dz_send.at[pl.ds(o, 2)], lambda s: v.dz_recv.at[s]
    )
    ex_dz.start()

    def merged_back(c):
        weight = jnp.concatenate(
            [v.w_u[rows_at(tap * MERGED + c, 512), :] for tap in range(9)], axis=1
        )
        v.joined[c] = dot_nt(v.cat_u[...], weight).astype(BF)

    near_s, near_r, far_s, far_r = take(2), take(2), take(1), take(1)

    def dm_near(k, slot):
        return remote(
            v.joined.at[slot], v.dm_near.at[k], near_s + k, near_r + k, {TENSOR: t_core}
        )

    merged_back(t_diag)
    dm_near(1, t_diag).start()
    merged_back(t_core)
    dm_near(0, t_core).start()
    ex_dz.wait()

    d_act = v.d_sum.at[0 : OWNERS * BINS, :]
    d_act[...] = jnp.zeros((OWNERS * BINS, 512), F32)

    def branch_back(j):
        def body(group, side):
            kept = jnp.where(group_id == group, 1.0, 0.0)
            value = v.dz_recv[:, side].reshape(OWNERS * BINS, 128).astype(F32) * kept
            value = value.astype(BF)
            o_u[rows_at(j, 512), :] = dot_tn(full_act(), value)
            d_act[...] = d_act[...] + dot_nt(value, v.w_own[rows_at(j, 512), :])

        own_branch(j, body)

    loop(9, branch_back)
    for k in range(SPLITS):
        v.d_act_send[k] = d_act[:, k * 128 : k * 128 + 128].astype(BF)
    v.d_act_recv[t] = v.d_act_send[t]
    ex = Exchange(TENSOR, SPLITS, lambda o: v.d_act_send.at[o], lambda s: v.d_act_recv.at[s])
    ex.start()
    merged_back(t_x)
    merged_back(t)
    dm_near(1, t_x).wait_recv()

    def add_x(k):
        at = rows_at(k, 48)
        value = v.joined[t_x, at, :].astype(F32) + v.dm_near[1, at, :].astype(F32)
        v.joined[t_x, at, :] = value.astype(BF)

    loop(12, add_x)
    dm_far = remote(v.joined.at[t_x], v.dm_far, far_s, far_r, {TENSOR: t_x})
    dm_far.start()
    ex.wait()
    for k in range(OWNERS):
        at = slice(k * BINS, k * BINS + BINS)
        value = v.d_act_recv[0, at, :].astype(F32)
        for slot in range(1, SPLITS):
            value = value + v.d_act_recv[slot, at, :].astype(F32)
        v.d_img_send[k] = value.astype(BF)
    v.d_img_recv[me] = v.d_img_send[me]
    ex = Exchange(BATCH, OWNERS, lambda o: v.d_img_send.at[o], lambda s: v.d_img_recv.at[s])
    ex.start()

    def unite_grad(c):
        for p in range(5):
            width = 256 if p < 4 else 128
            value = dot(v.joined_t[c], v.cat_u[:, p * 256 : p * 256 + width])
            v.w_u[rows_at(2 * p * MERGED + c, 512), :] = value[:, :128].astype(BF)
            if p < 4:
                v.w_u[rows_at((2 * p + 1) * MERGED + c, 512), :] = value[:, 128:].astype(BF)

    loop(SPLITS, unite_grad)
    s_u.start()
    ex.wait()
    d_b = v.d_img_recv[0].astype(F32)
    for k in range(1, OWNERS):
        d_b = d_b + v.d_img_recv[k].astype(F32)
    unit_b = (v.all_b[me].astype(F32) - mean_b) * scale_b
    d_b = d_b * slope(gamma_b * unit_b + beta_b)
    sync = Sync(v.sync_b3)
    sync.start(
        [total(d_b * group_mask(g)) for g in range(4)]
        + [total(d_b * unit_b * group_mask(g)) for g in range(4)]
    )
    spread_taps(v.d_f2, v.pre_a, norm_a, 15, sums[2:3], sums[3:4])
    for p in range(5):
        for at in range(0, CELLS, 96):
            value = back_tap(2 * p, 1, at)
            if p < 4:
                value = value + pltpu.roll(back_tap(2 * p + 1, 1, at), 64, 1)
            v.cat_a[at : at + 96, p * 128 : p * 128 + 128] = value.astype(BF)
    sums = sync.wait()
    first_b = jnp.zeros((BINS, 128), F32)
    second_b = jnp.zeros((BINS, 128), F32)
    for group in range(4):
        kept = group_mask(group)
        gain_grads[10 + group] = (sums[4 + group : 5 + group], sums[group : group + 1])
        first_b = first_b + kept * sums[group : group + 1]
        second_b = second_b + kept * sums[4 + group : 5 + group]
    inner = d_b - (first_b + unit_b * second_b) * count_b
    v.d_bp[t] = (gamma_b * scale_b * inner).astype(BF)
    spread_d = Spread(v.d_bp)
    spread_d.start()

    def aux_grad(c2):
        value2 = dot_tn(v.whole[c2], v.cat_a[...])
        for half in range(2):
            value = value2[half * 128 : half * 128 + 128]
            c = 2 * c2 + half
            for p in range(5):
                low = value[:64, p * 128 : p * 128 + 128]
                top = value[64:, p * 128 : p * 128 + 128]
                even = jnp.where(left_half, low, pltpu.roll(top, 64, 1))
                v.w_a[rows_at(2 * p * 8 + c, 64), :] = even.astype(BF)
                if p < 4:
                    odd = jnp.where(left_half, pltpu.roll(low, 64, 1), top)
                    v.w_a[rows_at((2 * p + 1) * 8 + c, 64), :] = odd.astype(BF)

    spread_d.wait()
    d_bp = jnp.concatenate([v.d_bp[k] for k in range(SPLITS)], axis=1)
    d_pooled = jnp.zeros((BINS, 512), F32)
    d_groups = []
    for group in range(4):
        d_groups.append((d_bp.astype(F32) * group_mask(group)).astype(BF))
        d_pooled = d_pooled + dot_nt(d_groups[group], v.w_b[group * 512 : group * 512 + 512, :])
    for group in range(4):
        v.w_b[group * 512 : group * 512 + 512, :] = dot_tn(v.pooled[...], d_groups[group]).astype(BF)
    s_b.start()
    d_pooled = (d_pooled / cells_in).astype(BF)
    v.d_sum[...] = dot_tn(v.pool[...], d_pooled)
    dm_near(0, t).wait_recv()
    dm_far.wait_recv()

    def through_sum(k, carry):
        at = rows_at(k, 48)
        value = v.d_sum[at, :] + v.joined[t, at, :].astype(F32) + v.dm_near[0, at, :].astype(F32)
        value = (value + v.dm_far[at, :].astype(F32)) * slope(summed(at))
        v.d_sum[at, :] = value
        return (
            carry[0] + fold(value),
            carry[1] + fold(value * normed(v.pre_e, at, norm_e)),
            carry[2] + fold(value * normed(v.pre_s, at, norm_s)),
        )

    zero = jnp.zeros((8, 512), F32)
    three = [total(item) for item in lax.fori_loop(0, 12, through_sum, (zero, zero, zero))]
    sync = Sync(v.sync_b4)
    sync.start(split_rows(three[0]) + split_rows(three[1]) + split_rows(three[2]))
    loop(SPLITS, aux_grad)
    s_a.start()
    s_u.middle(1)
    sums = sync.wait()
    first_s = join_rows(sums, 0, 4)
    second_e, second_s = join_rows(sums, 4, 4), join_rows(sums, 8, 4)
    for k in range(4):
        gain_grads[6 + k] = (sums[4 + k : 5 + k], sums[k : k + 1])
        gain_grads[1 + k] = (sums[8 + k : 9 + k], sums[k : k + 1])

    def back_both(k):
        at = rows_at(k, 48)
        value, mask = v.d_sum[at, :], wide(v.ins[at, :], 4)
        v.d_e[at, :] = back_norm(
            value, normed(v.pre_e, at, norm_e), mask, norm_e, gamma(6, 4), first_s, second_e, count4
        ).astype(BF)
        v.d_s[at, :] = back_norm(
            value, normed(v.pre_s, at, norm_s), mask, norm_s, gamma(1, 4), first_s, second_s, count4
        ).astype(BF)

    loop(12, back_both)

    def back_hidden(grad, weight, index):
        value = dot_nt(grad, weight)
        for k in range(SPLITS):
            v.dh_send[k] = value[:, k * 128 : k * 128 + 128].astype(BF)
        v.dh_recv[index, t] = v.dh_send[t]
        ex = Exchange(
            TENSOR, SPLITS, lambda o: v.dh_send.at[o], lambda s: v.dh_recv.at[index, s]
        )
        ex.start()
        return ex

    def hidden_sum(index):
        def step(k):
            at = rows_at(k, 96)
            value = v.dh_recv[index, 0, at, :].astype(F32)
            for slot in range(1, SPLITS):
                value = value + v.dh_recv[index, slot, at, :].astype(F32)
            v.d_f[at, :] = value

        loop(6, step)

    ex = back_hidden(v.d_e[...], v.w_e[...], 0)
    s_c.middle()
    s_ac.middle()
    s_u.middle(2)
    for k in range(SPLITS):
        v.w_e[k * 128 : k * 128 + 128, :] = dot_tn(v.h2[k], v.d_e[...]).astype(BF)
    s_e.start()
    ex.wait()
    hidden_sum(0)
    sync = Sync(v.sync_b5)
    sync.start(through_silu(v.d_f, v.pre_m, norm_m, 5))
    s_u.middle(3)
    sums = sync.wait()
    gain_grads[5] = (sums[1:2], sums[0:1])
    spread_taps(v.d_f, v.pre_m, norm_m, 5, sums[0:1], sums[1:2])
    fill(v.cat_u, 4)
    weight = jnp.concatenate([v.w_m[tap * 512 : tap * 512 + 512, :] for tap in range(9)], axis=1)
    ex = back_hidden(v.cat_u[...], weight, 1)

    def short_grad(c):
        v.w_s[rows_at(c, 256), :] = dot_tn(v.whole[c], v.d_s[...]).astype(BF)

    loop(SPLITS, short_grad)
    s_s.start()
    s_u.middle(0)
    s_b.middle()
    ex.wait()
    hidden_sum(1)
    sync = Sync(v.sync_b6)
    sync.start(through_silu(v.d_f, v.pre_r, norm_r, 0))

    def middle_grad(k):
        value = dot_tn(v.h1[k], v.cat_u[...])
        for tap in range(9):
            v.w_m[rows_at(tap * 4 + k, 128), :] = value[:, tap * 128 : tap * 128 + 128].astype(BF)

    loop(SPLITS, middle_grad)
    s_m.start()
    s_a.middle()
    s_e.middle()
    sums = sync.wait()
    gain_grads[0] = (sums[1:2], sums[0:1])

    def back_reduce(k):
        at = rows_at(k, 96)
        v.d_low[at, :] = back_norm(
            v.d_f[at, :], normed(v.pre_r, at, norm_r), v.ins[at, :], norm_r, gamma(0), sums[0:1], sums[1:2], count
        ).astype(BF)

    loop(6, back_reduce)

    def reduce_grad(c):
        v.w_r[rows_at(c, 256), :] = dot_tn(v.whole[c], v.d_low[...]).astype(BF)

    loop(SPLITS, reduce_grad)
    s_r.start()
    for item in (s_s, s_m, s_r):
        item.middle()
    rest = (s_c, s_ac, s_b, s_a, s_e, s_s, s_m, s_r)
    squares = s_u.end()
    for item in rest:
        squares = squares + item.end()
    dm_near(1, t_diag).wait_send()
    dm_near(0, t_core).wait_send()
    dm_far.wait_send()

    for row in range(16):
        o_gain[row : row + 1, :] = gain_grads[row][0]
        o_gain[16 + row : 17 + row, :] = gain_grads[row][1]
    gain_square = o_gain[...] * o_gain[...]
    squares = squares + total(gain_square) / OWNERS

    sync = Sync(v.sync_end)
    sync.start([squares, o_misc[1:2, :]])
    v.end_t[t] = sync.wait()
    spread_e = Spread(v.end_t)
    spread_e.start()
    spread_e.wait()
    ends = v.end_t[0]
    for k in range(1, SPLITS):
        ends = ends + v.end_t[k]
    o_misc[...] = ends
    o_misc[2:3, :] = jnp.broadcast_to(loss_weight, (1, 128))


def whole_step(sizes, labels, feat, gains, pieces):
    plan = scratch_plan()
    vmem = pl.BlockSpec(memory_space=pltpu.VMEM)
    anywhere = pl.BlockSpec(memory_space=pl.ANY)
    outs = [(128, 128), (128, 512), (576, 128), (64, 512), (256, 512), (4608, 128), (576, 128)]
    outs = outs + [(16, 256), (8, 256), (32, 128), (8, 128)]
    return pl.pallas_call(
        functools.partial(step_kernel, tuple(plan)),
        out_shape=[jax.ShapeDtypeStruct(shape, F32) for shape in outs],
        in_specs=[pl.BlockSpec(memory_space=pltpu.SMEM), vmem, anywhere, anywhere]
        + [anywhere] * len(pieces),
        out_specs=[vmem] * len(outs),
        scratch_shapes=[pltpu.VMEM(shape, kind) for shape, kind in plan.values()]
        + [pltpu.SemaphoreType.DMA((SEMAPHORES,))],
        compiler_params=pltpu.CompilerParams(
            collective_id=0, has_side_effects=True, vmem_limit_bytes=63 * 1024 * 1024
        ),
        name="whole_step",
    )(sizes, labels, feat, gains, *pieces)


def update_kernel(scale, grad, param, first, second, average, o_param, o_first, o_second, o_average):
    clipped = grad[...] * scale[0]
    new_first = 0.5 * first[...] + 0.5 * clipped
    new_second = 0.5 * second[...] + 0.5 * clipped * clipped
    keep = 1.0 - 0.5**STEP
    old = param[...]
    new = old - 0.01 * (new_first / keep / (jnp.sqrt(new_second / keep) + 1e-08) + 0.01 * old)
    o_param[...] = new
    o_first[...] = new_first
    o_second[...] = new_second
    o_average[...] = 0.999 * average[...] + 0.001 * new


def update(scale, grad, param, first, second, average):
    rows = grad.shape[0]
    block = pl.BlockSpec((512, 128), lambda i: (i, 0))
    return pl.pallas_call(
        update_kernel,
        grid=(pl.cdiv(rows, 512),),
        out_shape=[jax.ShapeDtypeStruct((rows, 128), jnp.float32)] * 4,
        in_specs=[pl.BlockSpec(memory_space=pltpu.SMEM)] + [block] * 5,
        out_specs=[block] * 4,
        name="update",
    )(scale.reshape(1), grad, param, first, second, average)

def fits(splits, owners):
    return splits == SPLITS and owners == OWNERS


def local_fast(features, labels, valid, sizes, params, first_moment, squared_mean, average):
    me = lax.axis_index("batch")
    shapes = segment_shapes(SPLITS)
    counts = []
    for shape in shapes:
        count = 1
        for extent in shape:
            count = count * extent
        counts.append(count // OWNERS)
    starts = [0]
    for count in counts:
        starts.append(starts[-1] + count)
    flat = params.reshape(-1, 128)
    low = flat.astype(BF)
    tail = flat[starts[6] // 128 :].reshape(-1)
    cut = [tail[starts[k] - starts[6] : starts[k + 1] - starts[6]] for k in range(6, 10)]
    rows = [low[starts[k] // 128 : starts[k + 1] // 128] for k in range(6)]
    aux = cut[1].astype(BF).reshape(9, 2, 64, 64)
    pieces = [
        rows[0],
        rows[1].reshape(128, 512),
        rows[2],
        rows[3].reshape(64, 512),
        rows[4].reshape(256, 512),
        rows[5],
        jnp.concatenate([aux[:, 0], aux[:, 1]], axis=-1).reshape(576, 128),
        jnp.pad(cut[0].astype(BF).reshape(16, NCLS), ((0, 0), (0, 256 - NCLS))),
        jnp.pad(
            cut[2].astype(BF).astype(F32).reshape(8, NCLS), ((0, 0), (0, 256 - NCLS))
        ),
    ]
    width = shapes[9][1]
    share = counts[9]
    per_row = width // share
    spot = jnp.zeros((2, 2048), F32)
    spot = lax.dynamic_update_slice(
        spot,
        cut[3].astype(BF).astype(F32).reshape(1, share),
        (me // per_row, (me % per_row) * share),
    )
    marked = jnp.where(valid > 0, labels, -1).astype(F32).reshape(CELLS, 1)
    outs = whole_step(
        sizes,
        jnp.broadcast_to(marked, (CELLS, 128)),
        features.reshape(CELLS, -1),
        spot.reshape(32, 128),
        pieces,
    )
    gain_grad = lax.dynamic_slice(
        outs[9].reshape(2, 2048)[:, :width].reshape(-1), (me * share,), (share,)
    )
    aux_grad = outs[6].reshape(9, 64, 2, 64).transpose(0, 2, 1, 3)
    grad_share = jnp.concatenate(
        [outs[k].reshape(-1, 128) for k in range(6)]
        + [
            jnp.concatenate(
                [
                    outs[7][:, :NCLS].reshape(-1),
                    aux_grad.reshape(-1),
                    outs[8][:, :NCLS].reshape(-1),
                    gain_grad,
                ]
            ).reshape(-1, 128)
        ]
    )
    misc = outs[10]
    grad_norm = jnp.sqrt(jnp.sum(misc[0]))
    scale = jnp.minimum(1.0, 0.05 / (grad_norm + 1e-06))
    new_params, new_first, new_second, new_average = [
        item.reshape(params.shape)
        for item in update(
            scale,
            grad_share,
            flat,
            first_moment.reshape(-1, 128),
            squared_mean.reshape(-1, 128),
            average.reshape(-1, 128),
        )
    ]
    return (
        new_params,
        new_first,
        new_second,
        new_average,
        new_params.astype(BF),
        grad_norm,
        jnp.sum(misc[1]),
        misc[2, 0],
        outs[9][30],
    )


def solution(mesh):
    chosen = local_fast if fits(mesh.shape["tensor"], mesh.shape["batch"]) else local
    return jax.shard_map(
        chosen,
        mesh=mesh,
        in_specs=(
            P("batch", None, None, "tensor"),
            P("batch", None, None),
            P("batch", None, None),
            P("batch", None),
            P("tensor", "batch"),
            P("tensor", "batch"),
            P("tensor", "batch"),
            P("tensor", "batch"),
        ),
        out_specs=(
            P("tensor", "batch"),
            P("tensor", "batch"),
            P("tensor", "batch"),
            P("tensor", "batch"),
            P("tensor", "batch"),
            P(),
            P(),
            P(),
            P("tensor"),
        ),
        check_vma=False,
    )
```

```python
import functools

import jax
import jax.numpy as jnp
from jax import lax
from jax.experimental import pallas as pl
from jax.experimental.pallas import tpu as pltpu
from jax.sharding import PartitionSpec as P

C_IN = 1024
MID = 512
C_OUT = 2048
PPM = 512
AUXW = 256
NCLS = 150
MAP = 24
STEP = 3


BIN_COUNTS = (1, 2, 3, 6)
BIN_STARTS = (0, 1, 5, 14)


def segment_shapes(splits):
    return [
        (C_IN, MID // splits),
        (C_IN, C_OUT // splits),
        (9, MID, MID // splits),
        (MID, C_OUT // splits),
        (4, C_OUT // splits, PPM),
        (9, C_OUT + 4 * PPM, PPM // splits),
        (PPM // splits, NCLS),
        (9, C_IN, AUXW // splits),
        (AUXW // splits, NCLS),
        (2, (2 * MID + 2 * C_OUT + 5 * PPM + AUXW) // splits),
    ]


def unflatten(rows, splits):
    split_parts = []
    start = 0
    for shape in segment_shapes(splits):
        count = 1
        for extent in shape:
            count = count * extent
        count = count // rows.shape[0]
        split_parts.append(rows[:, start : start + count].reshape(shape))
        start = start + count
    return split_parts


def gain_pieces(gains, splits):
    widths = [MID, C_OUT, MID, C_OUT, PPM, PPM, PPM, PPM, PPM, AUXW]
    split_parts = []
    start = 0
    for width in widths:
        step_width = width // splits
        split_parts.append(gains[:, start : start + step_width])
        start = start + step_width
    return split_parts


def shifted(field, down, right):
    image_height, width = (field.shape[1], field.shape[2])
    rows_pad, cols_pad = (abs(down), abs(right))
    padded = jnp.pad(field, ((0, 0), (rows_pad, rows_pad), (cols_pad, cols_pad), (0, 0)))
    return padded[
        :,
        rows_pad + down : rows_pad + down + image_height,
        cols_pad + right : cols_pad + right + width,
        :,
    ]


def conv_forward(field, kernel, spacing):
    total = jnp.zeros(field.shape[:-1] + (kernel.shape[2],), jnp.float32)
    for tap in range(9):
        moved = shifted(field, (tap // 3 - 1) * spacing, (tap % 3 - 1) * spacing)
        total = total + jnp.dot(moved, kernel[tap], preferred_element_type=jnp.float32)
    return total


def conv_input_back(grad, kernel, spacing):
    total = jnp.zeros(grad.shape[:-1] + (kernel.shape[1],), jnp.float32)
    for tap in range(9):
        product = jnp.dot(grad, kernel[tap].T, preferred_element_type=jnp.float32)
        total = total + shifted(product, -(tap // 3 - 1) * spacing, -(tap % 3 - 1) * spacing)
    return total


def conv_kernel_back(field, grad, spacing):
    return jnp.stack(
        [
            jnp.einsum(
                "ihwc,ihwd->cd",
                shifted(field, (tap // 3 - 1) * spacing, (tap % 3 - 1) * spacing),
                grad,
                preferred_element_type=jnp.float32,
            )
            for tap in range(9)
        ]
    )


def silu_slope(value):
    gate = jax.nn.sigmoid(value)
    return gate * (1.0 + value * (1.0 - gate))


def channel_sums(values):
    return values.reshape(-1, values.shape[-1]).sum(0)


def masked_norm_apply(items, extra):
    sends = []
    for value, mask, norm in items:
        sends = sends + [
            channel_sums(value * mask),
            channel_sums(value * value * mask),
            jnp.sum(mask) * jnp.ones((1,), jnp.float32),
        ]
    totals = lax.psum(tuple(sends + extra), "batch")
    results = []
    for index, (value, mask, norm) in enumerate(items):
        count = totals[3 * index + 2]
        mean = totals[3 * index] / count
        spread = totals[3 * index + 1] / count - mean * mean
        scaling = lax.rsqrt(spread + 1e-05)
        normed = (value - mean) * scaling
        results.append((norm[0] * normed + norm[1], normed, scaling, count, mask, norm[0]))
    return (results, totals[3 * len(items) :])


def norm_backward(items):
    sends = []
    for grad, kept in items:
        sends = sends + [channel_sums(grad), channel_sums(grad * kept[1])]
    totals = lax.psum(tuple(sends), "batch")
    results = []
    for index, (grad, kept) in enumerate(items):
        outcome, normed, scaling, count, mask, gamma = kept
        first_sum, second_sum = (totals[2 * index], totals[2 * index + 1])
        inner = grad - mask * (first_sum + normed * second_sum) / count
        results.append(gamma * scaling * inner)
    return (results, sends, totals)


def bin_tables(extent, bins, length):
    which = jnp.arange(bins, dtype=jnp.int32)[None, :, None]
    place = jnp.arange(length, dtype=jnp.int32)[None, None, :]
    edge = extent[:, None, None]
    lower = which * edge // bins
    upper = ((which + 1) * edge + bins - 1) // bins
    member = ((place >= lower) & (place < upper)).astype(jnp.float32)
    target = jnp.minimum(place * bins // edge, bins - 1)
    chosen = (target == which).astype(jnp.float32)
    return (member, chosen)


def spread_bins(merged, branch, tables, images):
    joined = [merged]
    for group, bins in enumerate(BIN_COUNTS):
        rows_in, cols_in, rows_pick, cols_pick, cell_count = tables[group]
        piece = branch[:, BIN_STARTS[group] : BIN_STARTS[group] + bins * bins].reshape(
            images, bins, bins, -1
        )
        joined.append(
            jnp.einsum(
                "ikh,ilw,iklc->ihwc",
                rows_pick.astype(jnp.bfloat16),
                cols_pick.astype(jnp.bfloat16),
                piece,
                preferred_element_type=jnp.float32,
            ).astype(jnp.bfloat16)
        )
    return jnp.concatenate(joined, axis=-1)


def pick_bins(d_joined, width, tables, images):
    branch_width = (d_joined.shape[-1] - width) // 4
    d_up = []
    for group, bins in enumerate(BIN_COUNTS):
        rows_in, cols_in, rows_pick, cols_pick, cell_count = tables[group]
        piece = d_joined[..., width + group * branch_width : width + (group + 1) * branch_width]
        d_up.append(
            jnp.einsum("ikh,ilw,ihwc->iklc", rows_pick, cols_pick, piece).reshape(
                images, bins * bins, -1
            )
        )
    return (d_joined[..., :width], jnp.concatenate(d_up, axis=1))


def gather_channels(field):
    return lax.all_gather(field, "tensor", axis=3, tiled=True)


def scatter_channels(field):
    return lax.psum_scatter(
        field.astype(jnp.bfloat16), "tensor", scatter_dimension=3, tiled=True
    ).astype(jnp.float32)


def local(features, labels, valid, sizes, params, first_moment, squared_mean, average):
    splits = lax.axis_size("tensor")
    owners = lax.axis_size("batch")
    images = features.shape[0]
    gathered = lax.all_gather(params.astype(jnp.bfloat16), "batch", axis=0, tiled=True)
    (
        w_reduce,
        w_short,
        w_middle,
        w_expand,
        w_branch,
        w_unite,
        w_classes,
        w_aux,
        w_aux_classes,
        gains,
    ) = unflatten(gathered, splits)
    norms = [(piece[0], piece[1]) for piece in gain_pieces(gains.astype(jnp.float32), splits)]
    rows_at = jnp.arange(MAP, dtype=jnp.int32)
    inside = (rows_at[None, :, None] < sizes[:, 0][:, None, None]) & (
        rows_at[None, None, :] < sizes[:, 1][:, None, None]
    )
    inside = inside.astype(jnp.float32)[..., None]
    counted = inside * valid.astype(jnp.float32)[..., None]
    labels_hot = (labels[..., None] == jnp.arange(NCLS, dtype=jnp.int32)).astype(jnp.float32)
    class_local = channel_sums(labels_hot * counted)
    whole = lax.all_gather(features, "tensor", axis=3, tiled=True)
    pre_reduce = jnp.dot(whole, w_reduce, preferred_element_type=jnp.float32)
    pre_short = jnp.dot(whole, w_short, preferred_element_type=jnp.float32)
    pre_aux = conv_forward(whole, w_aux, 1)
    leading_part, label_tally = masked_norm_apply(
        [
            (pre_reduce, inside, norms[0]),
            (pre_short, inside, norms[1]),
            (pre_aux, inside, norms[9]),
        ],
        [class_local],
    )
    class_pixel_counts = label_tally[0]
    hidden_one = jax.nn.silu(leading_part[0][0]).astype(jnp.bfloat16)
    aux_act = jax.nn.silu(leading_part[2][0]).astype(jnp.bfloat16)
    hidden_full = gather_channels(hidden_one)
    pre_middle = conv_forward(hidden_full, w_middle, 4)
    second, unused = masked_norm_apply([(pre_middle, inside, norms[2])], [])
    hidden_two = jax.nn.silu(second[0][0]).astype(jnp.bfloat16)
    hidden_two_full = gather_channels(hidden_two)
    pre_expand = jnp.dot(hidden_two_full, w_expand, preferred_element_type=jnp.float32)
    third, unused = masked_norm_apply([(pre_expand, inside, norms[3])], [])
    summed = third[0][0] + leading_part[1][0]
    merged = jax.nn.silu(summed).astype(jnp.bfloat16)
    tables = []
    pooled_list = []
    partial_list = []
    for group, bins in enumerate(BIN_COUNTS):
        rows_in, rows_pick = bin_tables(sizes[:, 0], bins, MAP)
        cols_in, cols_pick = bin_tables(sizes[:, 1], bins, MAP)
        cell_count = (
            jnp.sum(rows_in, axis=2)[:, :, None, None] * jnp.sum(cols_in, axis=2)[:, None, :, None]
        )
        tables.append((rows_in, cols_in, rows_pick, cols_pick, cell_count))
        pooled = (
            jnp.einsum(
                "ikh,ilw,ihwc->iklc",
                rows_in.astype(jnp.bfloat16),
                cols_in.astype(jnp.bfloat16),
                merged,
                preferred_element_type=jnp.float32,
            )
            / cell_count
        )
        pooled = pooled.astype(jnp.bfloat16).reshape(images, bins * bins, -1)
        pooled_list.append(pooled)
        partial_list.append(
            jnp.einsum("ipc,cd->ipd", pooled, w_branch[group], preferred_element_type=jnp.float32)
        )
    branch_pre = lax.psum_scatter(
        jnp.concatenate(partial_list, axis=1).astype(jnp.bfloat16),
        "tensor",
        scatter_dimension=2,
        tiled=True,
    ).astype(jnp.float32)
    branch_items = []
    for group, bins in enumerate(BIN_COUNTS):
        piece = branch_pre[:, BIN_STARTS[group] : BIN_STARTS[group] + bins * bins]
        branch_items.append(
            (piece, jnp.ones(piece.shape[:-1] + (1,), jnp.float32), norms[4 + group])
        )
    fourth, unused = masked_norm_apply(branch_items, [])
    branch_act = jnp.concatenate([jax.nn.silu(kept[0]) for kept in fourth], axis=1).astype(
        jnp.bfloat16
    )
    merged_full, branch_full = (
        lax.all_gather(merged, "tensor", axis=3, tiled=True),
        lax.all_gather(branch_act, "tensor", axis=2, tiled=True),
    )
    joined = spread_bins(merged_full, branch_full, tables, images)
    pre_unite = conv_forward(joined, w_unite, 1)
    fifth, unused = masked_norm_apply([(pre_unite, inside, norms[8])], [])
    united = jax.nn.silu(fifth[0][0]).astype(jnp.bfloat16)
    logit_main, logit_aux = (
        lax.psum_scatter(
            jnp.dot(united, w_classes, preferred_element_type=jnp.float32).astype(jnp.bfloat16),
            "tensor",
            scatter_dimension=1,
            tiled=True,
        ).astype(jnp.float32),
        lax.psum_scatter(
            jnp.dot(aux_act, w_aux_classes, preferred_element_type=jnp.float32).astype(
                jnp.bfloat16
            ),
            "tensor",
            scatter_dimension=1,
            tiled=True,
        ).astype(jnp.float32),
    )
    total_valid = jnp.sum(class_pixel_counts)
    class_weight = total_valid / (NCLS * class_pixel_counts + total_valid)
    loss_weight = jnp.sum(class_pixel_counts * class_weight)
    cell_weight = jnp.sum(labels_hot * class_weight, axis=-1, keepdims=True) * counted
    band_rows = labels.shape[1] // splits
    band_start = lax.axis_index("tensor") * band_rows
    hot_band = lax.dynamic_slice_in_dim(labels_hot, band_start, band_rows, 1)
    weight_band = lax.dynamic_slice_in_dim(cell_weight, band_start, band_rows, 1)
    log_main = jax.nn.log_softmax(logit_main, axis=-1)
    log_aux = jax.nn.log_softmax(logit_aux, axis=-1)
    loss_cells = -jnp.sum(hot_band * (log_main + 0.4 * log_aux), axis=-1, keepdims=True)
    loss_local = jnp.sum(weight_band * loss_cells)
    band_main = (weight_band * (jnp.exp(log_main) - hot_band) / loss_weight).astype(jnp.bfloat16)
    band_aux = (0.4 * weight_band * (jnp.exp(log_aux) - hot_band) / loss_weight).astype(
        jnp.bfloat16
    )
    grad_main, grad_aux = (
        lax.all_gather(band_main, "tensor", axis=1, tiled=True),
        lax.all_gather(band_aux, "tensor", axis=1, tiled=True),
    )
    reduced = {}

    def settle(index, value):
        reduced[index] = value

    settle(6, jnp.einsum("ihwc,ihwk->ck", united, grad_main, preferred_element_type=jnp.float32))
    settle(8, jnp.einsum("ihwc,ihwk->ck", aux_act, grad_aux, preferred_element_type=jnp.float32))
    d_united = jnp.dot(grad_main, w_classes.T, preferred_element_type=jnp.float32) * silu_slope(
        fifth[0][0]
    )
    d_aux = jnp.dot(grad_aux, w_aux_classes.T, preferred_element_type=jnp.float32) * silu_slope(
        leading_part[2][0]
    )
    back_one, sums_one, totals_one = norm_backward([(d_united, fifth[0]), (d_aux, leading_part[2])])
    unite_shift_grad = totals_one[0]
    d_unite_pre = back_one[0].astype(jnp.bfloat16)
    d_aux_pre = back_one[1].astype(jnp.bfloat16)
    settle(5, conv_kernel_back(joined, d_unite_pre, 1))
    d_merged, d_branch = pick_bins(conv_input_back(d_unite_pre, w_unite, 1), C_OUT, tables, images)
    d_merged, d_branch = (
        lax.psum_scatter(
            d_merged.astype(jnp.bfloat16), "tensor", scatter_dimension=3, tiled=True
        ).astype(jnp.float32),
        lax.psum_scatter(
            d_branch.astype(jnp.bfloat16), "tensor", scatter_dimension=2, tiled=True
        ).astype(jnp.float32),
    )
    settle(7, conv_kernel_back(whole, d_aux_pre, 1))
    branch_back = []
    for group, bins in enumerate(BIN_COUNTS):
        piece = d_branch[:, BIN_STARTS[group] : BIN_STARTS[group] + bins * bins]
        branch_back.append((piece * silu_slope(fourth[group][0]), fourth[group]))
    back_two, sums_two, unused = norm_backward(branch_back)
    d_branch_pre = jnp.concatenate(back_two, axis=1).astype(jnp.bfloat16)
    d_branch_full = lax.all_gather(d_branch_pre, "tensor", axis=2, tiled=True)
    branch_grads = []
    for group, bins in enumerate(BIN_COUNTS):
        rows_in, cols_in, rows_pick, cols_pick, cell_count = tables[group]
        piece = d_branch_full[:, BIN_STARTS[group] : BIN_STARTS[group] + bins * bins]
        branch_grads.append(
            jnp.einsum("ipc,ipd->cd", pooled_list[group], piece, preferred_element_type=jnp.float32)
        )
        d_pooled = jnp.dot(piece, w_branch[group].T, preferred_element_type=jnp.float32).reshape(
            images, bins, bins, -1
        )
        d_merged = d_merged + jnp.einsum(
            "ikh,ilw,iklc->ihwc", rows_in, cols_in, d_pooled / cell_count
        )
    settle(4, jnp.stack(branch_grads))
    d_summed = d_merged * silu_slope(summed)
    back_three, sums_three, unused = norm_backward(
        [(d_summed, third[0]), (d_summed, leading_part[1])]
    )
    d_expand_pre = back_three[0].astype(jnp.bfloat16)
    d_short_pre = back_three[1].astype(jnp.bfloat16)
    settle(
        3,
        jnp.einsum(
            "ihwc,ihwd->cd", hidden_two_full, d_expand_pre, preferred_element_type=jnp.float32
        ),
    )
    settle(1, jnp.einsum("ihwc,ihwd->cd", whole, d_short_pre, preferred_element_type=jnp.float32))
    d_two = scatter_channels(jnp.dot(d_expand_pre, w_expand.T, preferred_element_type=jnp.float32))
    back_four, sums_four, unused = norm_backward([(d_two * silu_slope(second[0][0]), second[0])])
    d_middle_pre = back_four[0].astype(jnp.bfloat16)
    settle(2, conv_kernel_back(hidden_full, d_middle_pre, 4))
    d_one = scatter_channels(conv_input_back(d_middle_pre, w_middle, 4))
    back_five, sums_five, unused = norm_backward(
        [(d_one * silu_slope(leading_part[0][0]), leading_part[0])]
    )
    settle(
        0,
        jnp.einsum(
            "ihwc,ihwd->cd",
            whole,
            back_five[0].astype(jnp.bfloat16),
            preferred_element_type=jnp.float32,
        ),
    )
    beta_grads = (
        [sums_five[0], sums_three[2], sums_four[0], sums_three[0]]
        + [sums_two[2 * g] for g in range(4)]
        + [sums_one[0], sums_one[2]]
    )
    gamma_grads = (
        [sums_five[1], sums_three[3], sums_four[1], sums_three[1]]
        + [sums_two[2 * g + 1] for g in range(4)]
        + [sums_one[1], sums_one[3]]
    )
    settle(9, jnp.stack([jnp.concatenate(gamma_grads), jnp.concatenate(beta_grads)]))
    ordered = [reduced[index] for index in range(10)]
    grad_share = lax.psum_scatter(
        jnp.concatenate([part.reshape(owners, -1) for part in ordered], axis=1),
        "batch",
        scatter_dimension=0,
        tiled=True,
    )
    square_all, loss_sum = lax.psum(
        (jnp.sum(grad_share * grad_share), loss_local), ("batch", "tensor")
    )
    grad_norm = jnp.sqrt(square_all)
    clipped = grad_share * jnp.minimum(1.0, 0.05 / (grad_norm + 1e-06))
    new_first = 0.5 * first_moment + 0.5 * clipped
    new_second = 0.5 * squared_mean + 0.5 * clipped * clipped
    keep = 1.0 - 0.5**STEP
    new_params = params - 0.01 * (
        new_first / keep / (jnp.sqrt(new_second / keep) + 1e-08) + 0.01 * params
    )
    new_average = 0.999 * average + 0.001 * new_params
    return (
        new_params,
        new_first,
        new_second,
        new_average,
        new_params.astype(jnp.bfloat16),
        grad_norm,
        loss_sum,
        loss_weight,
        unite_shift_grad,
    )


CELLS = MAP * MAP
EDGE = 104
BATCH = "batch"
TENSOR = "tensor"
GROUP_ROWS = ((0, 1), (1, 5), (5, 14), (14, 50))
BINS = 64
BF = jnp.bfloat16
F32 = jnp.float32
MESH = pl.DeviceIdType.MESH
HALF = 4
OWNERS = 8
SPLITS = 4
MERGED = 4
SLOTS = 5


def scratch_plan():
    plan = dict(
        w_r=((1024, 128), BF),
        w_s=((1024, 512), BF),
        w_m=((4608, 128), BF),
        w_e=((512, 512), BF),
        w_b=((2048, 512), BF),
        w_u=((18432, 128), BF),
        w_own=((4608, 128), BF),
        w_a=((4608, 128), BF),
        w_pair=((1024, 640), BF),
        w_c=((128, 256), BF),
        w_ac=((64, 256), F32),
        gain_in=((OWNERS, 32, 128), F32),
        whole=((SPLITS, CELLS, 256), BF),
        ins=((CELLS, 128), F32),
        col=((CELLS, 128), F32),
        lab=((CELLS, 128), F32),
        table=((BINS, CELLS), F32),
        pool=((BINS, CELLS), BF),
        pick=((BINS, CELLS), BF),
        cells_in=((BINS, 128), F32),
        pad=((9, CELLS + 2 * EDGE, 128), F32),
        grad_pad=((CELLS + 2 * EDGE, 128), F32),
        pre_r=((CELLS, 128), F32),
        pre_s=((CELLS, 512), F32),
        pre_a=((CELLS, 128), F32),
        pre_m=((CELLS, 128), F32),
        pre_e=((CELLS, 512), F32),
        pre_u=((CELLS, 128), F32),
        act_a=((CELLS, 128), BF),
        h1=((SPLITS, CELLS, 128), BF),
        h2=((SPLITS, CELLS, 128), BF),
        joined=((SPLITS, CELLS, 512), BF),
        joined_t=((SPLITS, 512, CELLS), BF),
        pooled=((BINS, 512), BF),
        part_b=((SPLITS, BINS, 128), BF),
        recv_b=((SPLITS, BINS, 128), BF),
        all_b=((OWNERS, BINS, 128), BF),
        act_b=((SPLITS, OWNERS * BINS, 128), BF),
        zsum=((2, OWNERS * BINS, 128), F32),
        z_send=((OWNERS, 2, BINS, 128), BF),
        z_recv=((OWNERS, 2, BINS, 128), BF),
        united=((CELLS, 128), BF),
        logit_send=((CELLS, 512), BF),
        logit_recv=((SPLITS, 144, 512), BF),
        slope_in=((SPLITS, 144, 512), BF),
        d_f=((CELLS, 128), F32),
        d_f2=((CELLS, 128), F32),
        cat_u=((CELLS, 1152), BF),
        cat_a=((CELLS, 640), BF),
        dz_send=((9, BINS, 128), BF),
        dz_recv=((OWNERS, 2, BINS, 128), BF),
        d_act_send=((SPLITS, OWNERS * BINS, 128), BF),
        d_act_recv=((SPLITS, OWNERS * BINS, 128), BF),
        d_img_send=((OWNERS, BINS, 128), BF),
        d_img_recv=((OWNERS, BINS, 128), BF),
        d_bp=((SPLITS, BINS, 128), BF),
        dm_near=((2, CELLS, 512), BF),
        dm_far=((CELLS, 512), BF),
        d_sum=((CELLS, 512), F32),
        d_e=((CELLS, 512), BF),
        d_s=((CELLS, 512), BF),
        dh_send=((SPLITS, CELLS, 128), BF),
        dh_recv=((2, SPLITS, CELLS, 128), BF),
        d_low=((CELLS, 128), BF),
        end_t=((SPLITS, 8, 128), F32),
    )
    for name, rows in SYNCS.items():
        plan["sync_" + name] = ((OWNERS, rows, 128), F32)
    for name, (rows, lanes, kind) in PARTS.items():
        plan["first_" + name] = ((HALF, rows, lanes), kind)
        plan["second_" + name] = ((HALF - 1, rows, lanes), kind)
    plan["first_u"] = ((HALF, SLOTS, 512, 128), BF)
    plan["second_u"] = ((HALF - 1, SLOTS, 512, 128), BF)
    return plan


SYNCS = dict(one=16, two=8, three=8, five=8, b1=8, b3=8, b4=16, b5=8, b6=8, end=8)
PARTS = dict(
    r=(128, 128, BF),
    s=(128, 512, BF),
    m=(576, 128, BF),
    e=(64, 512, BF),
    b=(256, 512, BF),
    a=(576, 128, BF),
    c=(16, 256, BF),
    ac=(8, 256, F32),
)
SEMAPHORES = 1100


class Refs:
    pass


def fold(value):
    return value.reshape(-1, 8, value.shape[-1]).sum(0)


def total(value):
    return jnp.sum(value, axis=0, keepdims=True)


def wide(value, times):
    return jnp.concatenate([value] * times, axis=1)


def dot(left, right):
    return jnp.dot(left, right, preferred_element_type=F32)


def dot_nt(left, right):
    return lax.dot_general(left, right, (((1,), (1,)), ((), ())), preferred_element_type=F32)


def dot_tn(left, right):
    return lax.dot_general(left, right, (((0,), (0,)), ((), ())), preferred_element_type=F32)


def loop(count, body):
    def step(k, carry):
        body(k)
        return carry

    lax.fori_loop(0, count, step, 0)


def rows_at(k, block):
    return pl.ds(pl.multiple_of(k * block, block), block)


def step_kernel(names, *refs):
    (
        sizes, lab_in, feat, gain_own, p_r, p_s, p_m, p_e, p_b, p_u, p_a, p_c, p_ac,
        o_r, o_s, o_m, o_e, o_b, o_u, o_a, o_c, o_ac, o_gain, o_misc,
    ) = refs[:24]
    v = Refs()
    for name, ref in zip(names, refs[24:]):
        setattr(v, name, ref)
    sems = refs[-1]
    me = lax.axis_index(BATCH)
    t = lax.axis_index(TENSOR)
    partner = me + 1 - 2 * lax.rem(me, 2)
    t_core = t + 1 - 2 * lax.rem(t, 2)
    t_x = lax.rem(t + 2, SPLITS)
    t_diag = lax.rem(t_core + 2, SPLITS)
    taken = [0]

    def take(count):
        start = taken[0]
        taken[0] = start + count
        assert taken[0] <= SEMAPHORES
        return start

    def far_peer(base, step):
        return lax.rem(base + 2 * step, OWNERS)

    def remote(src, dst, send, recv, device):
        return pltpu.make_async_remote_copy(
            src_ref=src,
            dst_ref=dst,
            send_sem=sems.at[send],
            recv_sem=sems.at[recv],
            device_id=device,
            device_id_type=MESH,
        )

    late = []

    barrier = pltpu.get_barrier_semaphore()
    for k in range(1, OWNERS):
        pl.semaphore_signal(
            barrier, inc=1, device_id={BATCH: lax.rem(me + k, OWNERS)}, device_id_type=MESH
        )
    for k in range(1, SPLITS):
        pl.semaphore_signal(
            barrier, inc=1, device_id={TENSOR: lax.rem(t + k, SPLITS)}, device_id_type=MESH
        )
    pl.semaphore_wait(barrier, OWNERS + SPLITS - 2)

    class Gather:
        def __init__(self, piece, full, rows):
            self.piece, self.full, self.rows = piece, full, rows
            self.near_s, self.far_s, self.pass_s = take(1), take(HALF), take(HALF)
            self.recv, self.keep = take(OWNERS), take(1)

        def at(self, owner):
            if self.rows is None:
                return self.full.at[owner]
            return self.full.at[rows_at(owner, self.rows), :]

        def local(self):
            return pltpu.make_async_copy(self.piece, self.at(me), sems.at[self.keep])

        def near(self):
            return remote(
                self.piece, self.at(me), self.near_s, self.recv + me, {BATCH: partner}
            )

        def far(self, step):
            return remote(
                self.piece,
                self.at(me),
                self.far_s + step,
                self.recv + me,
                {BATCH: far_peer(me, step)},
            )

        def passed(self, step, base):
            source = far_peer(base, step)
            return remote(
                self.at(source),
                self.at(source),
                self.pass_s + step,
                self.recv + source,
                {BATCH: partner},
            )

        def start_far(self):
            self.local().start()
            for step in range(1, HALF):
                self.far(step).start()

        def start_near(self):
            self.near().start()

        def forward(self):
            for step in range(1, HALF):
                self.passed(step, me).wait_recv()
                self.passed(step, me).start()

        def finish(self):
            for step in range(HALF):
                self.passed(step, partner).wait_recv()
            self.local().wait()
            self.near().wait_send()
            for step in range(1, HALF):
                self.far(step).wait_send()

        def drain(self):
            for step in range(1, HALF):
                self.passed(step, me).wait_send()

    g_gain = Gather(gain_own, v.gain_in, None)
    g_r = Gather(p_r, v.w_r, 128)
    g_s = Gather(p_s, v.w_s, 128)
    g_a = Gather(p_a, v.w_a, 576)
    g_m = Gather(p_m, v.w_m, 576)
    g_e = Gather(p_e, v.w_e, 64)
    g_b = Gather(p_b, v.w_b, 256)
    g_c = Gather(p_c, v.w_c, 16)
    g_ac = Gather(p_ac, v.w_ac, 8)

    def chunk_of(owner, j):
        return lax.rem(owner + j, 8)

    def merged_rows(owner, j):
        tap = owner + lax.div(owner + j, 8)
        return pl.ds(pl.multiple_of((tap * MERGED + chunk_of(owner, j)) * 512, 512), 512)

    def each_merged(owner, body):
        def step(j):
            pl.when(chunk_of(owner, j) < MERGED)(lambda: body(j))

        loop(9, step)

    class GatherUnite:
        def __init__(self):
            self.near_s, self.far_s, self.pass_s = take(9), take(9 * HALF), take(9 * HALF)
            self.recv, self.keep, self.keep_all = take(9 * OWNERS), take(9), take(1)

        def source(self, j):
            return p_u.at[rows_at(j, 512), :]

        def full(self, owner, j):
            return v.w_u.at[merged_rows(owner, j), :]

        def local(self, j):
            return pltpu.make_async_copy(
                self.source(j), self.full(me, j), sems.at[self.keep + j]
            )

        def whole(self):
            return pltpu.make_async_copy(p_u, v.w_own, sems.at[self.keep_all])

        def near(self, j):
            return remote(
                self.source(j),
                self.full(me, j),
                self.near_s + j,
                self.recv + me * 9 + j,
                {BATCH: partner},
            )

        def far(self, step, j):
            return remote(
                self.source(j),
                self.full(me, j),
                self.far_s + step * 9 + j,
                self.recv + me * 9 + j,
                {BATCH: far_peer(me, step)},
            )

        def passed(self, step, j, base):
            source = far_peer(base, step)
            return remote(
                self.full(source, j),
                self.full(source, j),
                self.pass_s + step * 9 + j,
                self.recv + source * 9 + j,
                {BATCH: partner},
            )

        def start_far(self):
            self.whole().start()

            def begin(j):
                self.local(j).start()
                for step in range(1, HALF):
                    self.far(step, j).start()

            each_merged(me, begin)

        def start_near(self):
            each_merged(me, lambda j: self.near(j).start())

        def forward(self, low, top):
            def step_j(k):
                j = low + k
                for step in range(1, HALF):

                    def go(step=step):
                        self.passed(step, j, me).wait_recv()
                        self.passed(step, j, me).start()

                    pl.when(chunk_of(far_peer(me, step), j) < MERGED)(go)

            loop(top - low, step_j)

        def finish(self):
            for step in range(HALF):
                each_merged(
                    far_peer(partner, step),
                    lambda j, step=step: self.passed(step, j, partner).wait_recv(),
                )

            def end(j):
                self.local(j).wait()
                self.near(j).wait_send()
                for step in range(1, HALF):
                    self.far(step, j).wait_send()

            each_merged(me, end)

        def drain(self):
            for step in range(1, HALF):
                each_merged(
                    far_peer(me, step),
                    lambda j, step=step: self.passed(step, j, me).wait_send(),
                )

    g_u = GatherUnite()

    class Sync:
        def __init__(self, buf):
            self.buf = buf
            self.send, self.recv = take(OWNERS), take(OWNERS)

        def copy(self, k, slot):
            return remote(
                self.buf.at[slot],
                self.buf.at[slot],
                self.send + k,
                self.recv + slot,
                {BATCH: lax.rem(me + k, OWNERS)},
            )

        def start(self, rows):
            for index, row in enumerate(rows):
                self.buf[me, index : index + 1, :] = row
            for index in range(len(rows), self.buf.shape[1]):
                self.buf[me, index : index + 1, :] = jnp.zeros((1, 128), F32)
            for k in range(1, OWNERS):
                self.copy(k, me).start()

        def wait(self):
            for k in range(1, OWNERS):
                self.copy(k, lax.rem(me + k, OWNERS)).wait_recv()
            for k in range(1, OWNERS):
                self.copy(k, me).wait_send()
            value = self.buf[0]
            for slot in range(1, OWNERS):
                value = value + self.buf[slot]
            return value

    class Spread:

        def __init__(self, buf):
            self.buf = buf
            self.send, self.recv = take(SPLITS), take(SPLITS)

        def copy(self, k, slot):
            return remote(
                self.buf.at[slot],
                self.buf.at[slot],
                self.send + k,
                self.recv + slot,
                {TENSOR: lax.rem(t + k, SPLITS)},
            )

        def start(self):
            for k in range(1, SPLITS):
                self.copy(k, t).start()

        def wait(self):
            for k in range(1, SPLITS):
                self.copy(k, lax.rem(t + k, SPLITS)).wait_recv()
            for k in range(1, SPLITS):
                self.copy(k, t).wait_send()

    class Exchange:

        def __init__(self, axis, count, part, into):
            self.axis, self.count, self.part, self.into = axis, count, part, into
            self.mine = me if axis == BATCH else t
            self.send, self.recv = take(count), take(count)

        def copy(self, k, slot):
            other = lax.rem(self.mine + k, self.count)
            return remote(
                self.part(other),
                self.into(slot),
                self.send + k,
                self.recv + slot,
                {self.axis: other},
            )

        def start(self):
            for k in range(1, self.count):
                self.copy(k, self.mine).start()

        def wait(self):
            for k in range(1, self.count):
                self.copy(k, lax.rem(self.mine + k, self.count)).wait_recv()
            for k in range(1, self.count):
                self.copy(k, self.mine).wait_send()

    feat_keep = take(1)
    feat_local = pltpu.make_async_copy(feat, v.whole.at[t], sems.at[feat_keep])
    feat_spread = Exchange(TENSOR, SPLITS, lambda other: feat, lambda slot: v.whole.at[slot])
    for item in (g_gain, g_r, g_s, g_a):
        item.start_far()
        item.start_near()
    feat_local.start()
    feat_spread.start()

    high, across = sizes[0, 0], sizes[0, 1]
    place = lax.broadcasted_iota(jnp.int32, (CELLS, 128), 0).astype(F32)
    row_of = jnp.floor((place + 0.5) / MAP)
    col_of = place - MAP * row_of
    within = (row_of < high.astype(F32)) & (col_of < across.astype(F32))
    v.ins[...] = jnp.where(within, 1.0, 0.0)
    v.col[...] = col_of
    v.lab[...] = jnp.where(within, lab_in[...], -1.0)
    v.table[...] = jnp.zeros((BINS, CELLS), F32)
    lane_place = lax.broadcasted_iota(jnp.int32, (1, CELLS), 1).astype(F32)
    lane_row = jnp.floor((lane_place + 0.5) / MAP)
    lane_col = lane_place - MAP * lane_row

    def ranges(extent, bins, where):
        inside, chosen, counts = [], [], []
        for k in range(bins):
            low = lax.div(k * extent, bins)
            top = lax.div((k + 1) * extent + (bins - 1), bins)
            member = (where >= low.astype(F32)) & (where < top.astype(F32))
            inside.append(jnp.where(member, 1.0, 0.0))
            picked = where * bins >= (k * extent).astype(F32)
            if k < bins - 1:
                picked = picked & (where * bins < ((k + 1) * extent).astype(F32))
            chosen.append(jnp.where(picked, 1.0, 0.0))
            counts.append(top - low)
        return inside, chosen, counts

    picks = []
    v.cells_in[...] = jnp.ones((BINS, 128), F32)
    for group, bins in enumerate(BIN_COUNTS):
        r_in, r_pick, r_count = ranges(high, bins, lane_row)
        c_in, c_pick, c_count = ranges(across, bins, lane_col)
        for a in range(bins):
            for b in range(bins):
                spot = BIN_STARTS[group] + a * bins + b
                v.table[spot : spot + 1, :] = r_in[a] * c_in[b]
                v.cells_in[spot : spot + 1, :] = jnp.full(
                    (1, 128), (r_count[a] * c_count[b]).astype(F32)
                )
                picks.append((spot, r_pick[a] * c_pick[b]))
    v.pool[...] = v.table[...].astype(BF)
    for spot, value in picks:
        v.table[spot : spot + 1, :] = value
    v.pick[...] = v.table[...].astype(BF)
    zeros_edge = jnp.zeros((EDGE, 128), F32)
    for tap in range(9):
        v.pad[tap, 0:EDGE, :] = zeros_edge
        v.pad[tap, EDGE + CELLS :, :] = zeros_edge
    v.grad_pad[0:EDGE, :] = zeros_edge
    v.grad_pad[EDGE + CELLS :, :] = zeros_edge
    lanes = lax.broadcasted_iota(jnp.int32, (1, 256), 1).astype(F32)
    counts = jnp.zeros((8, 256), F32)
    for k in range(0, CELLS, 96):
        counts = counts + fold(
            jnp.where(wide(v.lab[k : k + 96, :], 2) == lanes, 1.0, 0.0)
        )
    class_local = total(counts)
    cells_local = jnp.full((1, 128), (high * across).astype(F32))
    left_half = lax.broadcasted_iota(jnp.int32, (64, 128), 1) < 64

    for item in (g_gain, g_r, g_s):
        item.forward()
    for item in (g_m, g_e):
        item.start_far()
    g_a.forward()
    for item in (g_b, g_c, g_ac, g_u):
        item.start_far()
    for item in (g_gain, g_r, g_s, g_a):
        item.finish()
    for item in (g_m, g_e, g_b, g_c, g_ac):
        item.start_near()
    feat_local.wait()
    feat_spread.wait()
    gains = v.gain_in[0]
    for slot in range(1, OWNERS):
        gains = gains + v.gain_in[slot]

    def gamma(row, width=1):
        return jnp.concatenate([gains[row + k : row + k + 1] for k in range(width)], axis=1)

    def beta(row, width=1):
        return gamma(16 + row, width)

    def unpack(chunk):
        for pair in range(5):
            even = v.w_a[rows_at(2 * pair * 8 + chunk, 64), :].astype(F32)
            if pair < 4:
                odd = v.w_a[rows_at((2 * pair + 1) * 8 + chunk, 64), :].astype(F32)
            else:
                odd = jnp.zeros((64, 128), F32)
            low = jnp.where(left_half, even, pltpu.roll(odd, 64, 1))
            top = jnp.where(left_half, pltpu.roll(even, 64, 1), odd)
            v.w_pair[rows_at(2 * chunk, 64), pair * 128 : pair * 128 + 128] = low.astype(BF)
            v.w_pair[rows_at(2 * chunk + 1, 64), pair * 128 : pair * 128 + 128] = top.astype(BF)

    loop(8, unpack)

    def whole_feat():
        return jnp.concatenate([v.whole[k] for k in range(SPLITS)], axis=1)

    v.pre_r[...] = dot(whole_feat(), v.w_r[...])
    for k in range(0, 512, 256):
        v.pre_s[:, k : k + 256] = dot(whole_feat(), v.w_s[:, k : k + 256])
    for pair in (0, 2):
        value = dot(whole_feat(), v.w_pair[:, pair * 128 : pair * 128 + 256])
        v.pad[pair, EDGE : EDGE + CELLS, :] = value[:, :128]
        v.pad[pair + 1, EDGE : EDGE + CELLS, :] = value[:, 128:]
    v.pad[4, EDGE : EDGE + CELLS, :] = dot(whole_feat(), v.w_pair[:, 512:640])
    g_m.forward()

    def offset(tap, spacing):
        return ((tap // 3 - 1) * MAP + (tap % 3 - 1)) * spacing

    def col_mask(at, right):
        where = v.col[at, :] + float(right)
        return jnp.where((where >= 0.0) & (where < float(MAP)), 1.0, 0.0)

    BLOCK = 72

    def shift_sum(taps, spacing, at, slot_of):
        out = None
        for b in (-1, 0, 1):
            part = None
            for tap in taps:
                if tap % 3 - 1 != b:
                    continue
                start = EDGE + at + offset(tap, spacing)
                value = v.pad[slot_of(tap), start : start + BLOCK, :]
                part = value if part is None else part + value
            if part is None:
                continue
            if b:
                part = part * col_mask(slice(at, at + BLOCK), b * spacing)
            out = part if out is None else out + part
        return out

    left_wide = lax.broadcasted_iota(jnp.int32, (BLOCK, 128), 1) < 64
    for at in range(0, CELLS, BLOCK):
        even = shift_sum((0, 2, 4, 6, 8), 1, at, lambda tap: tap // 2)
        odd = shift_sum((1, 3, 5, 7), 1, at, lambda tap: tap // 2)
        v.pre_a[at : at + BLOCK, :] = jnp.where(left_wide, even + pltpu.roll(odd, 64, 1), 0.0)

    def masked_sums(ref):
        width = ref.shape[1]

        def step(k, carry):
            at = rows_at(k, 96)
            value = ref[at, :]
            kept = value * (v.ins[at, :] if width == 128 else wide(v.ins[at, :], width // 128))
            return (carry[0] + fold(kept), carry[1] + fold(kept * value))

        zero = jnp.zeros((8, width), F32)
        sums = lax.fori_loop(0, 6, step, (zero, zero))
        return total(sums[0]), total(sums[1])

    def split_rows(value):
        return [value[:, k : k + 128] for k in range(0, value.shape[1], 128)]

    def join_rows(value, row, count):
        return jnp.concatenate([value[row + k : row + k + 1] for k in range(count)], axis=1)

    def moments(first, second, count):
        mean = first / count
        return mean, lax.rsqrt(second / count - mean * mean + 1e-05)

    sync = Sync(v.sync_one)
    r1, r2 = masked_sums(v.pre_r)
    s1, s2 = masked_sums(v.pre_s)
    a1, a2 = masked_sums(v.pre_a)
    sync.start(
        [r1, r2] + split_rows(s1) + split_rows(s2) + [a1, a2, cells_local] + split_rows(class_local)
    )
    sums = sync.wait()
    g_u.start_near()
    count = sums[12:13]
    count4 = wide(count, 4)
    norm_r = moments(sums[0:1], sums[1:2], count)
    norm_s = moments(join_rows(sums, 2, 4), join_rows(sums, 6, 4), count4)
    norm_a = moments(sums[10:11], sums[11:12], count)
    class_count = join_rows(sums, 13, 2)

    def normed(ref, at, norm):
        return (ref[at, :] - norm[0]) * norm[1]

    spread_1 = Spread(v.h1)

    def make_h1(k):
        at = rows_at(k, 96)
        v.h1[t, at, :] = jax.nn.silu(gamma(0) * normed(v.pre_r, at, norm_r) + beta(0)).astype(BF)

    loop(6, make_h1)
    spread_1.start()

    def make_a(k):
        at = rows_at(k, 96)
        v.act_a[at, :] = jax.nn.silu(gamma(15) * normed(v.pre_a, at, norm_a) + beta(15)).astype(BF)

    loop(6, make_a)
    g_e.forward()
    g_m.finish()
    spread_1.wait()

    def full_h(ref):
        return jnp.concatenate([ref[k] for k in range(SPLITS)], axis=1)

    def middle(tap):
        v.pad[tap, EDGE : EDGE + CELLS, :] = dot(full_h(v.h1), v.w_m[rows_at(tap, 512), :])

    loop(9, middle)
    for at in range(0, CELLS, BLOCK):
        v.pre_m[at : at + BLOCK, :] = shift_sum(range(9), 4, at, lambda tap: tap)
    sync = Sync(v.sync_two)
    sync.start(list(masked_sums(v.pre_m)))
    g_e.finish()
    sums = sync.wait()
    g_b.forward()
    norm_m = moments(sums[0:1], sums[1:2], count)
    spread_2 = Spread(v.h2)

    def make_h2(k):
        at = rows_at(k, 96)
        v.h2[t, at, :] = jax.nn.silu(gamma(5) * normed(v.pre_m, at, norm_m) + beta(5)).astype(BF)

    loop(6, make_h2)
    spread_2.start()
    spread_2.wait()
    for k in range(0, 512, 256):
        v.pre_e[:, k : k + 256] = dot(full_h(v.h2), v.w_e[:, k : k + 256])
    sync = Sync(v.sync_three)
    e1, e2 = masked_sums(v.pre_e)
    sync.start(split_rows(e1) + split_rows(e2))
    g_c.forward()
    g_ac.forward()
    sums = sync.wait()
    g_u.forward(0, 1)
    norm_e = moments(join_rows(sums, 0, 4), join_rows(sums, 4, 4), count4)

    def summed(at):
        return (
            gamma(6, 4) * normed(v.pre_e, at, norm_e)
            + beta(6, 4)
            + gamma(1, 4) * normed(v.pre_s, at, norm_s)
            + beta(1, 4)
        )

    def make_merged(k):
        at = rows_at(k, 48)
        v.joined[t, at, :] = jax.nn.silu(summed(at)).astype(BF)

    loop(12, make_merged)

    j_send, j_recv = take(3), take(SPLITS)

    def joined_copy(k, slot, device):
        return remote(
            v.joined.at[slot], v.joined.at[slot], j_send + k, j_recv + slot, {TENSOR: device}
        )

    joined_copy(0, t, t_x).start()
    joined_copy(1, t, t_core).start()

    bin_row = lax.broadcasted_iota(jnp.int32, (BINS, 1), 0)

    def group_mask(group, shape=None):
        low, top = GROUP_ROWS[group]
        kept = jnp.where((bin_row >= low) & (bin_row < top), 1.0, 0.0)
        return kept if shape is None else jnp.broadcast_to(kept, shape)

    cells_in = wide(v.cells_in[...], 4)
    pooled = dot(v.pool[...], v.joined[t]) / cells_in
    v.pooled[...] = pooled.astype(BF)
    g_b.finish()
    part = jnp.zeros((BINS, 512), F32)
    for group in range(4):
        rows = (v.pooled[...].astype(F32) * group_mask(group)).astype(BF)
        part = part + dot(rows, v.w_b[group * 512 : group * 512 + 512, :])
    for k in range(SPLITS):
        v.part_b[k] = part[:, k * 128 : k * 128 + 128].astype(BF)
    v.recv_b[t] = v.part_b[t]
    ex = Exchange(TENSOR, SPLITS, lambda o: v.part_b.at[o], lambda s: v.recv_b.at[s])
    ex.start()
    g_u.forward(1, 3)
    joined_copy(0, t_x, t_x).wait_recv()
    joined_copy(2, t_x, t_core).start()
    ex.wait()
    own_b = v.recv_b[0].astype(F32)
    for k in range(1, SPLITS):
        own_b = own_b + v.recv_b[k].astype(F32)
    v.all_b[me] = own_b.astype(BF)
    ex = Exchange(BATCH, OWNERS, lambda o: v.all_b.at[me], lambda s: v.all_b.at[s])
    ex.start()
    g_u.forward(3, 5)
    ex.wait()
    all_b = [v.all_b[k].astype(F32) for k in range(OWNERS)]
    sum_b, square_b = all_b[0], all_b[0] * all_b[0]
    for k in range(1, OWNERS):
        sum_b = sum_b + all_b[k]
        square_b = square_b + all_b[k] * all_b[k]
    mean_b = jnp.zeros((BINS, 128), F32)
    scale_b = jnp.zeros((BINS, 128), F32)
    gamma_b = jnp.zeros((BINS, 128), F32)
    beta_b = jnp.zeros((BINS, 128), F32)
    count_b = jnp.zeros((BINS, 1), F32)
    for group, bins in enumerate(BIN_COUNTS):
        kept = group_mask(group)
        size = float(OWNERS * bins * bins)
        mean, scaling = moments(total(sum_b * kept), total(square_b * kept), size)
        mean_b = mean_b + kept * mean
        scale_b = scale_b + kept * scaling
        gamma_b = gamma_b + kept * gamma(10 + group)
        beta_b = beta_b + kept * beta(10 + group)
        count_b = count_b + kept / size
    spread_b = Spread(v.act_b)
    for k in range(OWNERS):
        out = gamma_b * ((all_b[k] - mean_b) * scale_b) + beta_b
        v.act_b[t, k * BINS : k * BINS + BINS, :] = jax.nn.silu(out).astype(BF)
    spread_b.start()
    g_u.forward(5, 7)
    spread_b.wait()
    g_u.whole().wait()
    row_512 = lax.broadcasted_iota(jnp.int32, (OWNERS * BINS, 1), 0) & (BINS - 1)
    group_id = jnp.where(
        row_512 < 1, 0, jnp.where(row_512 < 5, 1, jnp.where(row_512 < 14, 2, jnp.where(row_512 < 50, 3, 9)))
    )

    def full_act():
        return jnp.concatenate([v.act_b[k] for k in range(SPLITS)], axis=1)

    v.zsum[...] = jnp.zeros((2, OWNERS * BINS, 128), F32)

    def own_branch(j, body):
        chunk = chunk_of(me, j)
        pl.when(chunk >= MERGED)(lambda: body(chunk - MERGED, lax.div(me + j, 8)))

    def make_z(j):
        def body(group, side):
            kept = jnp.where(group_id == group, 1.0, 0.0)
            rows = (full_act().astype(F32) * kept).astype(BF)
            v.zsum[side] = v.zsum[side] + dot(rows, v.w_own[rows_at(j, 512), :])

        own_branch(j, body)

    loop(9, make_z)
    for k in range(OWNERS):
        for side in range(2):
            v.z_send[k, side] = v.zsum[side, k * BINS : k * BINS + BINS, :].astype(BF)
    v.z_recv[me] = v.z_send[me]
    ex = Exchange(BATCH, OWNERS, lambda o: v.z_send.at[o], lambda s: v.z_recv.at[s])
    ex.start()
    g_u.forward(7, 9)
    joined_copy(1, t_core, t_core).wait_recv()
    joined_copy(2, t_diag, t_core).wait_recv()
    for k in range(SPLITS):
        v.joined_t[k] = v.joined[k].T
    ex.wait()
    g_u.finish()

    pick2 = jnp.concatenate([v.pick[...], v.pick[...]], axis=0)

    def tap_z(tap):
        if tap == 0:
            return v.z_recv[0, 0].astype(F32)
        if tap == 8:
            return v.z_recv[7, 1].astype(F32)
        return v.z_recv[tap, 0].astype(F32) + v.z_recv[tap - 1, 1].astype(F32)

    def full_joined():
        return jnp.concatenate([v.joined[k] for k in range(SPLITS)], axis=1)

    def w_tap(tap):
        return v.w_u[rows_at(tap, 2048), :]

    def unite_pair(p):
        value = dot(full_joined(), jnp.concatenate([w_tap(2 * p), w_tap(2 * p + 1)], axis=1))
        v.pad[2 * p, EDGE : EDGE + CELLS, :] = value[:, :128]
        v.pad[2 * p + 1, EDGE : EDGE + CELLS, :] = value[:, 128:]

    loop(4, unite_pair)
    v.pad[8, EDGE : EDGE + CELLS, :] = dot(full_joined(), w_tap(8))
    for tap in range(9):
        z = tap_z(tap)
        high_z = z.astype(BF)
        low_z = (z - high_z.astype(F32)).astype(BF)
        v.pad[tap, EDGE : EDGE + CELLS, :] = v.pad[tap, EDGE : EDGE + CELLS, :] + dot_tn(
            pick2, jnp.concatenate([high_z, low_z], axis=0)
        )
    for at in range(0, CELLS, BLOCK):
        v.pre_u[at : at + BLOCK, :] = shift_sum(range(9), 1, at, lambda tap: tap)
    sync = Sync(v.sync_five)
    sync.start(list(masked_sums(v.pre_u)))
    for item in (g_c, g_ac):
        item.finish()
    for item in (g_gain, g_r, g_s, g_a, g_m, g_e, g_b, g_c, g_ac, g_u):
        item.drain()
    joined_copy(0, t, t_x).wait_send()
    joined_copy(1, t, t_core).wait_send()
    joined_copy(2, t_x, t_core).wait_send()
    w_ac = jnp.concatenate([v.w_ac[...], jnp.zeros((64, 256), F32)], axis=0).astype(BF)
    sums = sync.wait()
    norm_u = moments(sums[0:1], sums[1:2], count)

    def make_u(k):
        at = rows_at(k, 96)
        v.united[at, :] = jax.nn.silu(gamma(14) * normed(v.pre_u, at, norm_u) + beta(14)).astype(BF)

    loop(6, make_u)

    v.logit_send[:, :256] = dot(v.united[...], v.w_c[...]).astype(BF)
    v.logit_send[:, 256:] = dot(v.act_a[...], w_ac).astype(BF)
    ex = Exchange(
        TENSOR,
        SPLITS,
        lambda o: v.logit_send.at[rows_at(o, 144), :],
        lambda s: v.logit_recv.at[s],
    )
    ex.start()
    v.logit_recv[t] = v.logit_send[rows_at(t, 144), :]
    total_valid = jnp.sum(class_count, axis=1, keepdims=True)
    class_weight = total_valid / (NCLS * class_count + total_valid)
    loss_weight = jnp.sum(class_count * class_weight, axis=1, keepdims=True)
    class_weight = jnp.where(lanes < float(NCLS), class_weight, 0.0)
    hot = jnp.where(wide(v.lab[rows_at(t, 144), :], 2) == lanes, 1.0, 0.0)
    cell_weight = jnp.sum(hot * class_weight, axis=1, keepdims=True)
    ex.wait()
    logits = v.logit_recv[0].astype(F32)
    for k in range(1, SPLITS):
        logits = logits + v.logit_recv[k].astype(F32)

    def log_softmax(value):
        value = jnp.where(lanes < float(NCLS), value, -1e30)
        value = value - jnp.max(value, axis=1, keepdims=True)
        powers = jnp.exp(value)
        mass = jnp.sum(powers, axis=1, keepdims=True)
        return value - jnp.log(mass), powers / mass

    log_main, p_main = log_softmax(logits[:, :256])
    log_aux, p_aux = log_softmax(logits[:, 256:])
    loss_rows = total(fold(-cell_weight * hot * (log_main + 0.4 * log_aux)))
    loss_local = loss_rows[:, :128] + loss_rows[:, 128:]
    o_misc[1:2, :] = loss_local
    v.slope_in[t, :, :256] = (cell_weight * (p_main - hot) / loss_weight).astype(BF)
    v.slope_in[t, :, 256:] = (0.4 * cell_weight * (p_aux - hot) / loss_weight).astype(BF)
    spread_g = Spread(v.slope_in)
    spread_g.start()
    spread_g.wait()
    g_main = v.slope_in[:, :, :256].reshape(CELLS, 256)
    g_aux = v.slope_in[:, :, 256:].reshape(CELLS, 256)
    v.d_f[...] = dot_nt(g_main, v.w_c[...])
    v.d_f2[...] = dot_nt(g_aux, w_ac)

    def slope(value):
        gate = jax.nn.sigmoid(value)
        return gate * (1.0 + value * (1.0 - gate))

    def through_silu(ref, pre, norm, row):
        def step(k, carry):
            at = rows_at(k, 96)
            unit = normed(pre, at, norm)
            value = ref[at, :] * slope(gamma(row) * unit + beta(row))
            ref[at, :] = value
            return (carry[0] + fold(value), carry[1] + fold(value * unit))

        zero = jnp.zeros((8, 128), F32)
        sums = lax.fori_loop(0, 6, step, (zero, zero))
        return [total(sums[0]), total(sums[1])]

    def back_norm(value, unit, mask, norm, gain, first, second, size):
        inner = value - mask * (first + unit * second) / size
        return gain * norm[1] * inner

    gain_grads = {}
    sync = Sync(v.sync_b1)
    sync.start(
        through_silu(v.d_f, v.pre_u, norm_u, 14) + through_silu(v.d_f2, v.pre_a, norm_a, 15)
    )

    class Scatter:
        def __init__(self, first, second, full, rows, out):
            self.full, self.rows, self.out = full, rows, out
            self.first, self.second = first, second
            self.near_s, self.near_r = take(HALF), take(HALF)
            self.far_s, self.far_r = take(HALF), take(HALF)
            self.block = min(rows, 64)

        def near(self, step):
            dest = far_peer(partner, step)
            return remote(
                self.full.at[rows_at(dest, self.rows), :],
                self.first.at[step],
                self.near_s + step,
                self.near_r + step,
                {BATCH: partner},
            )

        def far(self, step):
            return remote(
                self.first.at[step],
                self.second.at[step - 1],
                self.far_s + step,
                self.far_r + step,
                {BATCH: far_peer(me, step)},
            )

        def start(self):
            for step in (1, 2, 3, 0):
                self.near(step).start()

        def middle(self):
            kind = self.first.dtype
            for step in range(1, HALF):
                self.near(step).wait_recv()
                base = far_peer(me, step) * (self.rows // self.block)

                def add(k, step=step, base=base):
                    at = rows_at(k, self.block)
                    value = self.full[rows_at(base + k, self.block), :].astype(F32)
                    value = value + self.first[step, at, :].astype(F32)
                    self.first[step, at, :] = value.astype(kind)

                loop(self.rows // self.block, add)
                self.far(step).start()

        def end(self):
            self.near(0).wait_recv()
            for step in range(1, HALF):
                self.far(step).wait_recv()
            base = me * (self.rows // self.block)

            def add(k, carry):
                at = rows_at(k, self.block)
                value = self.full[rows_at(base + k, self.block), :].astype(F32)
                value = value + self.first[0, at, :].astype(F32)
                for step in range(1, HALF):
                    value = value + self.second[step - 1, at, :].astype(F32)
                self.out[at, :] = value
                return carry + fold(value * value)

            squares = lax.fori_loop(
                0, self.rows // self.block, add, jnp.zeros((8, self.out.shape[1]), F32)
            )
            for step in (1, 2, 3, 0):
                self.near(step).wait_send()
                if step:
                    self.far(step).wait_send()
            return sum(split_rows(total(squares)))

    s_c = Scatter(v.first_c, v.second_c, v.w_c, 16, o_c)
    s_ac = Scatter(v.first_ac, v.second_ac, v.w_ac, 8, o_ac)
    s_a = Scatter(v.first_a, v.second_a, v.w_a, 576, o_a)
    s_b = Scatter(v.first_b, v.second_b, v.w_b, 256, o_b)
    s_s = Scatter(v.first_s, v.second_s, v.w_s, 128, o_s)
    s_e = Scatter(v.first_e, v.second_e, v.w_e, 64, o_e)
    s_m = Scatter(v.first_m, v.second_m, v.w_m, 576, o_m)
    s_r = Scatter(v.first_r, v.second_r, v.w_r, 128, o_r)

    class ScatterUnite:
        def __init__(self):
            self.near_s, self.near_r = take(9 * HALF), take(9 * HALF)
            self.far_s, self.far_r = take(9 * HALF), take(9 * HALF)

        def slot(self, owner, j):
            return jnp.where(j == 8, SLOTS - 1, chunk_of(owner, j))

        def near(self, step, j, base):
            dest = far_peer(base, step)
            return remote(
                v.w_u.at[merged_rows(dest, j), :],
                v.first_u.at[step, self.slot(dest, j)],
                self.near_s + step * 9 + j,
                self.near_r + step * 9 + j,
                {BATCH: partner},
            )

        def far(self, step, j, owner):
            at = self.slot(owner, j)
            return remote(
                v.first_u.at[step, at],
                v.second_u.at[step - 1, at],
                self.far_s + step * 9 + j,
                self.far_r + step * 9 + j,
                {BATCH: far_peer(me, step)},
            )

        def start(self):
            for step in (1, 2, 3, 0):
                each_merged(
                    far_peer(partner, step),
                    lambda j, step=step: self.near(step, j, partner).start(),
                )

        def middle(self, step):
            owner = far_peer(me, step)

            def go(j):
                self.near(step, j, me).wait_recv()
                slot = self.slot(owner, j)
                tap = owner + lax.div(owner + j, 8)
                base = (tap * MERGED + chunk_of(owner, j)) * 8

                def add(k):
                    at = rows_at(k, 64)
                    value = v.w_u[rows_at(base + k, 64), :].astype(F32)
                    value = value + v.first_u[step, slot, at, :].astype(F32)
                    v.first_u[step, slot, at, :] = value.astype(BF)

                loop(8, add)
                self.far(step, j, owner).start()

            each_merged(owner, go)

        def end(self):
            def go(j):
                slot = self.slot(me, j)
                self.near(0, j, me).wait_recv()
                for step in range(1, HALF):
                    self.far(step, j, me).wait_recv()
                tap = me + lax.div(me + j, 8)
                base = (tap * MERGED + chunk_of(me, j)) * 8

                def add(k):
                    at = rows_at(k, 64)
                    value = v.w_u[rows_at(base + k, 64), :].astype(F32)
                    value = value + v.first_u[0, slot, at, :].astype(F32)
                    for step in range(1, HALF):
                        value = value + v.second_u[step - 1, slot, at, :].astype(F32)
                    o_u[rows_at(j * 8 + k, 64), :] = value

                loop(8, add)

            each_merged(me, go)
            for step in (1, 2, 3, 0):
                each_merged(
                    far_peer(partner, step),
                    lambda j, step=step: self.near(step, j, partner).wait_send(),
                )
                if step:
                    each_merged(
                        far_peer(me, step),
                        lambda j, step=step: self.far(step, j, far_peer(me, step)).wait_send(),
                    )

            def square(k, carry):
                value = o_u[rows_at(k, 64), :]
                return carry + fold(value * value)

            squares = lax.fori_loop(0, 72, square, jnp.zeros((8, 128), F32))
            return sum(split_rows(total(squares)))

    s_u = ScatterUnite()

    v.w_c[...] = dot_tn(v.united[...], g_main).astype(BF)
    v.w_ac[...] = dot_tn(v.act_a[...], g_aux)[:64]
    s_c.start()
    s_ac.start()
    sums = sync.wait()
    gain_grads[14] = (sums[1:2], sums[0:1])
    gain_grads[15] = (sums[3:4], sums[2:3])

    def spread_taps(ref, pre, norm, row, first, second):
        def step(k):
            at = rows_at(k, 96)
            value = back_norm(
                ref[at, :], normed(pre, at, norm), v.ins[at, :], norm, gamma(row), first, second, count
            )
            ref[at, :] = value.astype(BF).astype(F32)

        loop(6, step)
        v.grad_pad[EDGE : EDGE + CELLS, :] = ref[...]

    def back_tap(tap, spacing, at):
        start = EDGE + at - offset(tap, spacing)
        value = v.grad_pad[start : start + 96, :]
        right = tap % 3 - 1
        if right:
            value = value * col_mask(slice(at, at + 96), -right * spacing)
        return value

    def fill(cat, spacing):
        for tap in range(9):
            for at in range(0, CELLS, 96):
                cat[at : at + 96, tap * 128 : tap * 128 + 128] = back_tap(tap, spacing, at).astype(
                    BF
                )

    spread_taps(v.d_f, v.pre_u, norm_u, 14, sums[0:1], sums[1:2])
    fill(v.cat_u, 1)

    dz = dot(v.pick[...], v.cat_u[...])
    for tap in range(9):
        v.dz_send[tap] = dz[:, tap * 128 : tap * 128 + 128].astype(BF)
    v.dz_recv[me] = v.dz_send[pl.ds(me, 2)]
    ex_dz = Exchange(
        BATCH, OWNERS, lambda o: v.dz_send.at[pl.ds(o, 2)], lambda s: v.dz_recv.at[s]
    )
    ex_dz.start()

    def merged_back(c):
        weight = jnp.concatenate(
            [v.w_u[rows_at(tap * MERGED + c, 512), :] for tap in range(9)], axis=1
        )
        v.joined[c] = dot_nt(v.cat_u[...], weight).astype(BF)

    near_s, near_r, far_s, far_r = take(2), take(2), take(1), take(1)

    def dm_near(k, slot):
        return remote(
            v.joined.at[slot], v.dm_near.at[k], near_s + k, near_r + k, {TENSOR: t_core}
        )

    merged_back(t_diag)
    dm_near(1, t_diag).start()
    merged_back(t_core)
    dm_near(0, t_core).start()
    merged_back(t_x)
    merged_back(t)

    def unite_grad(c):
        for p in range(5):
            width = 256 if p < 4 else 128
            value = dot(v.joined_t[c], v.cat_u[:, p * 256 : p * 256 + width])
            v.w_u[rows_at(2 * p * MERGED + c, 512), :] = value[:, :128].astype(BF)
            if p < 4:
                v.w_u[rows_at((2 * p + 1) * MERGED + c, 512), :] = value[:, 128:].astype(BF)

    loop(SPLITS, unite_grad)
    s_u.start()
    dm_near(1, t_x).wait_recv()

    def add_x(k):
        at = rows_at(k, 48)
        value = v.joined[t_x, at, :].astype(F32) + v.dm_near[1, at, :].astype(F32)
        v.joined[t_x, at, :] = value.astype(BF)

    loop(12, add_x)
    dm_far = remote(v.joined.at[t_x], v.dm_far, far_s, far_r, {TENSOR: t_x})
    dm_far.start()
    ex_dz.wait()

    d_act = v.d_sum.at[0 : OWNERS * BINS, :]
    d_act[...] = jnp.zeros((OWNERS * BINS, 512), F32)

    def branch_back(j):
        def body(group, side):
            kept = jnp.where(group_id == group, 1.0, 0.0)
            value = v.dz_recv[:, side].reshape(OWNERS * BINS, 128).astype(F32) * kept
            value = value.astype(BF)
            o_u[rows_at(j, 512), :] = dot_tn(full_act(), value)
            d_act[...] = d_act[...] + dot_nt(value, v.w_own[rows_at(j, 512), :])

        own_branch(j, body)

    loop(9, branch_back)
    for k in range(SPLITS):
        v.d_act_send[k] = d_act[:, k * 128 : k * 128 + 128].astype(BF)
    v.d_act_recv[t] = v.d_act_send[t]
    ex = Exchange(TENSOR, SPLITS, lambda o: v.d_act_send.at[o], lambda s: v.d_act_recv.at[s])
    ex.start()
    spread_taps(v.d_f2, v.pre_a, norm_a, 15, sums[2:3], sums[3:4])
    for p in range(5):
        for at in range(0, CELLS, 96):
            value = back_tap(2 * p, 1, at)
            if p < 4:
                value = value + pltpu.roll(back_tap(2 * p + 1, 1, at), 64, 1)
            v.cat_a[at : at + 96, p * 128 : p * 128 + 128] = value.astype(BF)

    def aux_grad(c2):
        value2 = dot_tn(v.whole[c2], v.cat_a[...])
        for half in range(2):
            value = value2[half * 128 : half * 128 + 128]
            c = 2 * c2 + half
            for p in range(5):
                low = value[:64, p * 128 : p * 128 + 128]
                top = value[64:, p * 128 : p * 128 + 128]
                even = jnp.where(left_half, low, pltpu.roll(top, 64, 1))
                v.w_a[rows_at(2 * p * 8 + c, 64), :] = even.astype(BF)
                if p < 4:
                    odd = jnp.where(left_half, pltpu.roll(low, 64, 1), top)
                    v.w_a[rows_at((2 * p + 1) * 8 + c, 64), :] = odd.astype(BF)

    loop(SPLITS, aux_grad)
    s_a.start()
    ex.wait()
    for k in range(OWNERS):
        at = slice(k * BINS, k * BINS + BINS)
        value = v.d_act_recv[0, at, :].astype(F32)
        for slot in range(1, SPLITS):
            value = value + v.d_act_recv[slot, at, :].astype(F32)
        v.d_img_send[k] = value.astype(BF)
    v.d_img_recv[me] = v.d_img_send[me]
    ex = Exchange(BATCH, OWNERS, lambda o: v.d_img_send.at[o], lambda s: v.d_img_recv.at[s])
    ex.start()

    s_u.middle(1)
    ex.wait()
    d_b = v.d_img_recv[0].astype(F32)
    for k in range(1, OWNERS):
        d_b = d_b + v.d_img_recv[k].astype(F32)
    unit_b = (v.all_b[me].astype(F32) - mean_b) * scale_b
    d_b = d_b * slope(gamma_b * unit_b + beta_b)
    sync = Sync(v.sync_b3)
    sync.start(
        [total(d_b * group_mask(g)) for g in range(4)]
        + [total(d_b * unit_b * group_mask(g)) for g in range(4)]
    )
    s_u.middle(2)
    sums = sync.wait()
    first_b = jnp.zeros((BINS, 128), F32)
    second_b = jnp.zeros((BINS, 128), F32)
    for group in range(4):
        kept = group_mask(group)
        gain_grads[10 + group] = (sums[4 + group : 5 + group], sums[group : group + 1])
        first_b = first_b + kept * sums[group : group + 1]
        second_b = second_b + kept * sums[4 + group : 5 + group]
    inner = d_b - (first_b + unit_b * second_b) * count_b
    v.d_bp[t] = (gamma_b * scale_b * inner).astype(BF)
    spread_d = Spread(v.d_bp)
    spread_d.start()

    spread_d.wait()
    d_bp = jnp.concatenate([v.d_bp[k] for k in range(SPLITS)], axis=1)
    d_pooled = jnp.zeros((BINS, 512), F32)
    d_groups = []
    for group in range(4):
        d_groups.append((d_bp.astype(F32) * group_mask(group)).astype(BF))
        d_pooled = d_pooled + dot_nt(d_groups[group], v.w_b[group * 512 : group * 512 + 512, :])
    for group in range(4):
        v.w_b[group * 512 : group * 512 + 512, :] = dot_tn(v.pooled[...], d_groups[group]).astype(BF)
    s_b.start()
    d_pooled = (d_pooled / cells_in).astype(BF)
    v.d_sum[...] = dot_tn(v.pool[...], d_pooled)
    dm_near(0, t).wait_recv()
    dm_far.wait_recv()

    def through_sum(k, carry):
        at = rows_at(k, 48)
        value = v.d_sum[at, :] + v.joined[t, at, :].astype(F32) + v.dm_near[0, at, :].astype(F32)
        value = (value + v.dm_far[at, :].astype(F32)) * slope(summed(at))
        v.d_sum[at, :] = value
        return (
            carry[0] + fold(value),
            carry[1] + fold(value * normed(v.pre_e, at, norm_e)),
            carry[2] + fold(value * normed(v.pre_s, at, norm_s)),
        )

    zero = jnp.zeros((8, 512), F32)
    three = [total(item) for item in lax.fori_loop(0, 12, through_sum, (zero, zero, zero))]
    sync = Sync(v.sync_b4)
    sync.start(split_rows(three[0]) + split_rows(three[1]) + split_rows(three[2]))
    s_u.middle(3)
    sums = sync.wait()
    first_s = join_rows(sums, 0, 4)
    second_e, second_s = join_rows(sums, 4, 4), join_rows(sums, 8, 4)
    for k in range(4):
        gain_grads[6 + k] = (sums[4 + k : 5 + k], sums[k : k + 1])
        gain_grads[1 + k] = (sums[8 + k : 9 + k], sums[k : k + 1])

    def back_both(k):
        at = rows_at(k, 48)
        value, mask = v.d_sum[at, :], wide(v.ins[at, :], 4)
        v.d_e[at, :] = back_norm(
            value, normed(v.pre_e, at, norm_e), mask, norm_e, gamma(6, 4), first_s, second_e, count4
        ).astype(BF)
        v.d_s[at, :] = back_norm(
            value, normed(v.pre_s, at, norm_s), mask, norm_s, gamma(1, 4), first_s, second_s, count4
        ).astype(BF)

    loop(12, back_both)

    def back_hidden(grad, weight, index):
        value = dot_nt(grad, weight)
        for k in range(SPLITS):
            v.dh_send[k] = value[:, k * 128 : k * 128 + 128].astype(BF)
        v.dh_recv[index, t] = v.dh_send[t]
        ex = Exchange(
            TENSOR, SPLITS, lambda o: v.dh_send.at[o], lambda s: v.dh_recv.at[index, s]
        )
        ex.start()
        return ex

    def hidden_sum(index):
        def step(k):
            at = rows_at(k, 96)
            value = v.dh_recv[index, 0, at, :].astype(F32)
            for slot in range(1, SPLITS):
                value = value + v.dh_recv[index, slot, at, :].astype(F32)
            v.d_f[at, :] = value

        loop(6, step)

    ex = back_hidden(v.d_e[...], v.w_e[...], 0)
    s_c.middle()
    s_ac.middle()
    s_a.middle()
    for k in range(SPLITS):
        v.w_e[k * 128 : k * 128 + 128, :] = dot_tn(v.h2[k], v.d_e[...]).astype(BF)
    s_e.start()
    ex.wait()
    hidden_sum(0)
    sync = Sync(v.sync_b5)
    sync.start(through_silu(v.d_f, v.pre_m, norm_m, 5))
    s_b.middle()
    sums = sync.wait()
    gain_grads[5] = (sums[1:2], sums[0:1])
    spread_taps(v.d_f, v.pre_m, norm_m, 5, sums[0:1], sums[1:2])
    fill(v.cat_u, 4)
    weight = jnp.concatenate([v.w_m[tap * 512 : tap * 512 + 512, :] for tap in range(9)], axis=1)
    ex = back_hidden(v.cat_u[...], weight, 1)

    def short_grad(c):
        v.w_s[rows_at(c, 256), :] = dot_tn(v.whole[c], v.d_s[...]).astype(BF)

    loop(SPLITS, short_grad)
    s_s.start()
    s_e.middle()
    ex.wait()
    hidden_sum(1)
    sync = Sync(v.sync_b6)
    sync.start(through_silu(v.d_f, v.pre_r, norm_r, 0))

    def middle_grad(k):
        value = dot_tn(v.h1[k], v.cat_u[...])
        for tap in range(9):
            v.w_m[rows_at(tap * 4 + k, 128), :] = value[:, tap * 128 : tap * 128 + 128].astype(BF)

    loop(SPLITS, middle_grad)
    s_m.start()
    s_s.middle()
    sums = sync.wait()
    gain_grads[0] = (sums[1:2], sums[0:1])

    def back_reduce(k):
        at = rows_at(k, 96)
        v.d_low[at, :] = back_norm(
            v.d_f[at, :], normed(v.pre_r, at, norm_r), v.ins[at, :], norm_r, gamma(0), sums[0:1], sums[1:2], count
        ).astype(BF)

    loop(6, back_reduce)

    def reduce_grad(c):
        v.w_r[rows_at(c, 256), :] = dot_tn(v.whole[c], v.d_low[...]).astype(BF)

    loop(SPLITS, reduce_grad)
    s_r.start()
    for item in (s_m, s_r):
        item.middle()
    rest = (s_c, s_ac, s_b, s_a, s_e, s_s, s_m, s_r)
    squares = s_u.end()
    for item in rest:
        squares = squares + item.end()
    dm_near(1, t_diag).wait_send()
    dm_near(0, t_core).wait_send()
    dm_far.wait_send()

    for row in range(16):
        o_gain[row : row + 1, :] = gain_grads[row][0]
        o_gain[16 + row : 17 + row, :] = gain_grads[row][1]
    gain_square = o_gain[...] * o_gain[...]
    squares = squares + total(gain_square) / OWNERS

    sync = Sync(v.sync_end)
    sync.start([squares, o_misc[1:2, :]])
    v.end_t[t] = sync.wait()
    spread_e = Spread(v.end_t)
    spread_e.start()
    spread_e.wait()
    ends = v.end_t[0]
    for k in range(1, SPLITS):
        ends = ends + v.end_t[k]
    o_misc[...] = ends
    o_misc[2:3, :] = jnp.broadcast_to(loss_weight, (1, 128))


def whole_step(sizes, labels, feat, gains, pieces):
    plan = scratch_plan()
    vmem = pl.BlockSpec(memory_space=pltpu.VMEM)
    anywhere = pl.BlockSpec(memory_space=pl.ANY)
    outs = [(128, 128), (128, 512), (576, 128), (64, 512), (256, 512), (4608, 128), (576, 128)]
    outs = outs + [(16, 256), (8, 256), (32, 128), (8, 128)]
    return pl.pallas_call(
        functools.partial(step_kernel, tuple(plan)),
        out_shape=[jax.ShapeDtypeStruct(shape, F32) for shape in outs],
        in_specs=[pl.BlockSpec(memory_space=pltpu.SMEM), vmem, anywhere, anywhere]
        + [anywhere] * len(pieces),
        out_specs=[vmem] * len(outs),
        scratch_shapes=[pltpu.VMEM(shape, kind) for shape, kind in plan.values()]
        + [pltpu.SemaphoreType.DMA((SEMAPHORES,))],
        compiler_params=pltpu.CompilerParams(
            collective_id=0, has_side_effects=True, vmem_limit_bytes=63 * 1024 * 1024
        ),
        name="whole_step",
    )(sizes, labels, feat, gains, *pieces)


def update_kernel(scale, grad, param, first, second, average, o_param, o_first, o_second, o_average):
    clipped = grad[...] * scale[0]
    new_first = 0.5 * first[...] + 0.5 * clipped
    new_second = 0.5 * second[...] + 0.5 * clipped * clipped
    keep = 1.0 - 0.5**STEP
    old = param[...]
    new = old - 0.01 * (new_first / keep / (jnp.sqrt(new_second / keep) + 1e-08) + 0.01 * old)
    o_param[...] = new
    o_first[...] = new_first
    o_second[...] = new_second
    o_average[...] = 0.999 * average[...] + 0.001 * new


def update(scale, grad, param, first, second, average):
    rows = grad.shape[0]
    block = pl.BlockSpec((512, 128), lambda i: (i, 0))
    return pl.pallas_call(
        update_kernel,
        grid=(pl.cdiv(rows, 512),),
        out_shape=[jax.ShapeDtypeStruct((rows, 128), jnp.float32)] * 4,
        in_specs=[pl.BlockSpec(memory_space=pltpu.SMEM)] + [block] * 5,
        out_specs=[block] * 4,
        name="update",
    )(scale.reshape(1), grad, param, first, second, average)

def fits(splits, owners):
    return splits == SPLITS and owners == OWNERS


def local_fast(features, labels, valid, sizes, params, first_moment, squared_mean, average):
    me = lax.axis_index("batch")
    shapes = segment_shapes(SPLITS)
    counts = []
    for shape in shapes:
        count = 1
        for extent in shape:
            count = count * extent
        counts.append(count // OWNERS)
    starts = [0]
    for count in counts:
        starts.append(starts[-1] + count)
    flat = params.reshape(-1, 128)
    low = flat.astype(BF)
    tail = lax.optimization_barrier(flat[starts[6] // 128 :]).reshape(-1)
    cut = [tail[starts[k] - starts[6] : starts[k + 1] - starts[6]] for k in range(6, 10)]
    rows = [low[starts[k] // 128 : starts[k + 1] // 128] for k in range(6)]
    aux = cut[1].astype(BF).reshape(9, 2, 64, 64)
    pieces = [
        rows[0],
        rows[1].reshape(128, 512),
        rows[2],
        rows[3].reshape(64, 512),
        rows[4].reshape(256, 512),
        rows[5],
        jnp.concatenate([aux[:, 0], aux[:, 1]], axis=-1).reshape(576, 128),
        jnp.pad(cut[0].astype(BF).reshape(16, NCLS), ((0, 0), (0, 256 - NCLS))),
        jnp.pad(
            cut[2].astype(BF).astype(F32).reshape(8, NCLS), ((0, 0), (0, 256 - NCLS))
        ),
    ]
    width = shapes[9][1]
    share = counts[9]
    per_row = width // share
    spot = jnp.zeros((2, 2048), F32)
    spot = lax.dynamic_update_slice(
        spot,
        cut[3].astype(BF).astype(F32).reshape(1, share),
        (me // per_row, (me % per_row) * share),
    )
    marked = jnp.where(valid > 0, labels, -1).astype(F32).reshape(CELLS, 1)
    outs = whole_step(
        sizes,
        jnp.broadcast_to(marked, (CELLS, 128)),
        features.reshape(CELLS, -1),
        spot.reshape(32, 128),
        pieces,
    )
    gain_grad = lax.dynamic_slice(
        outs[9].reshape(2, 2048)[:, :width].reshape(-1), (me * share,), (share,)
    )
    aux_grad = outs[6].reshape(9, 64, 2, 64).transpose(0, 2, 1, 3)
    grad_share = jnp.concatenate(
        [outs[k].reshape(-1, 128) for k in range(6)]
        + [
            jnp.concatenate(
                [
                    outs[7][:, :NCLS].reshape(-1),
                    aux_grad.reshape(-1),
                    outs[8][:, :NCLS].reshape(-1),
                    gain_grad,
                ]
            ).reshape(-1, 128)
        ]
    )
    misc = outs[10]
    grad_norm = jnp.sqrt(jnp.sum(misc[0]))
    scale = jnp.minimum(1.0, 0.05 / (grad_norm + 1e-06))
    new_params, new_first, new_second, new_average = [
        item.reshape(params.shape)
        for item in update(
            scale,
            grad_share,
            flat,
            first_moment.reshape(-1, 128),
            squared_mean.reshape(-1, 128),
            average.reshape(-1, 128),
        )
    ]
    return (
        new_params,
        new_first,
        new_second,
        new_average,
        new_params.astype(BF),
        grad_norm,
        jnp.sum(misc[1]),
        misc[2, 0],
        outs[9][30],
    )


def solution(mesh):
    chosen = local_fast if fits(mesh.shape["tensor"], mesh.shape["batch"]) else local
    return jax.shard_map(
        chosen,
        mesh=mesh,
        in_specs=(
            P("batch", None, None, "tensor"),
            P("batch", None, None),
            P("batch", None, None),
            P("batch", None),
            P("tensor", "batch"),
            P("tensor", "batch"),
            P("tensor", "batch"),
            P("tensor", "batch"),
        ),
        out_specs=(
            P("tensor", "batch"),
            P("tensor", "batch"),
            P("tensor", "batch"),
            P("tensor", "batch"),
            P("tensor", "batch"),
            P(),
            P(),
            P(),
            P("tensor"),
        ),
        check_vma=False,
    )
```

```python
import functools

import jax
import jax.numpy as jnp
from jax import lax
from jax.experimental import pallas as pl
from jax.experimental.pallas import tpu as pltpu
from jax.sharding import PartitionSpec as P

C_IN = 1024
MID = 512
C_OUT = 2048
PPM = 512
AUXW = 256
NCLS = 150
MAP = 24
STEP = 3


BIN_COUNTS = (1, 2, 3, 6)
BIN_STARTS = (0, 1, 5, 14)


def segment_shapes(splits):
    return [
        (C_IN, MID // splits),
        (C_IN, C_OUT // splits),
        (9, MID, MID // splits),
        (MID, C_OUT // splits),
        (4, C_OUT // splits, PPM),
        (9, C_OUT + 4 * PPM, PPM // splits),
        (PPM // splits, NCLS),
        (9, C_IN, AUXW // splits),
        (AUXW // splits, NCLS),
        (2, (2 * MID + 2 * C_OUT + 5 * PPM + AUXW) // splits),
    ]


def unflatten(rows, splits):
    split_parts = []
    start = 0
    for shape in segment_shapes(splits):
        count = 1
        for extent in shape:
            count = count * extent
        count = count // rows.shape[0]
        split_parts.append(rows[:, start : start + count].reshape(shape))
        start = start + count
    return split_parts


def gain_pieces(gains, splits):
    widths = [MID, C_OUT, MID, C_OUT, PPM, PPM, PPM, PPM, PPM, AUXW]
    split_parts = []
    start = 0
    for width in widths:
        step_width = width // splits
        split_parts.append(gains[:, start : start + step_width])
        start = start + step_width
    return split_parts


def shifted(field, down, right):
    image_height, width = (field.shape[1], field.shape[2])
    rows_pad, cols_pad = (abs(down), abs(right))
    padded = jnp.pad(field, ((0, 0), (rows_pad, rows_pad), (cols_pad, cols_pad), (0, 0)))
    return padded[
        :,
        rows_pad + down : rows_pad + down + image_height,
        cols_pad + right : cols_pad + right + width,
        :,
    ]


def conv_forward(field, kernel, spacing):
    total = jnp.zeros(field.shape[:-1] + (kernel.shape[2],), jnp.float32)
    for tap in range(9):
        moved = shifted(field, (tap // 3 - 1) * spacing, (tap % 3 - 1) * spacing)
        total = total + jnp.dot(moved, kernel[tap], preferred_element_type=jnp.float32)
    return total


def conv_input_back(grad, kernel, spacing):
    total = jnp.zeros(grad.shape[:-1] + (kernel.shape[1],), jnp.float32)
    for tap in range(9):
        product = jnp.dot(grad, kernel[tap].T, preferred_element_type=jnp.float32)
        total = total + shifted(product, -(tap // 3 - 1) * spacing, -(tap % 3 - 1) * spacing)
    return total


def conv_kernel_back(field, grad, spacing):
    return jnp.stack(
        [
            jnp.einsum(
                "ihwc,ihwd->cd",
                shifted(field, (tap // 3 - 1) * spacing, (tap % 3 - 1) * spacing),
                grad,
                preferred_element_type=jnp.float32,
            )
            for tap in range(9)
        ]
    )


def silu_slope(value):
    gate = jax.nn.sigmoid(value)
    return gate * (1.0 + value * (1.0 - gate))


def channel_sums(values):
    return values.reshape(-1, values.shape[-1]).sum(0)


def masked_norm_apply(items, extra):
    sends = []
    for value, mask, norm in items:
        sends = sends + [
            channel_sums(value * mask),
            channel_sums(value * value * mask),
            jnp.sum(mask) * jnp.ones((1,), jnp.float32),
        ]
    totals = lax.psum(tuple(sends + extra), "batch")
    results = []
    for index, (value, mask, norm) in enumerate(items):
        count = totals[3 * index + 2]
        mean = totals[3 * index] / count
        spread = totals[3 * index + 1] / count - mean * mean
        scaling = lax.rsqrt(spread + 1e-05)
        normed = (value - mean) * scaling
        results.append((norm[0] * normed + norm[1], normed, scaling, count, mask, norm[0]))
    return (results, totals[3 * len(items) :])


def norm_backward(items):
    sends = []
    for grad, kept in items:
        sends = sends + [channel_sums(grad), channel_sums(grad * kept[1])]
    totals = lax.psum(tuple(sends), "batch")
    results = []
    for index, (grad, kept) in enumerate(items):
        outcome, normed, scaling, count, mask, gamma = kept
        first_sum, second_sum = (totals[2 * index], totals[2 * index + 1])
        inner = grad - mask * (first_sum + normed * second_sum) / count
        results.append(gamma * scaling * inner)
    return (results, sends, totals)


def bin_tables(extent, bins, length):
    which = jnp.arange(bins, dtype=jnp.int32)[None, :, None]
    place = jnp.arange(length, dtype=jnp.int32)[None, None, :]
    edge = extent[:, None, None]
    lower = which * edge // bins
    upper = ((which + 1) * edge + bins - 1) // bins
    member = ((place >= lower) & (place < upper)).astype(jnp.float32)
    target = jnp.minimum(place * bins // edge, bins - 1)
    chosen = (target == which).astype(jnp.float32)
    return (member, chosen)


def spread_bins(merged, branch, tables, images):
    joined = [merged]
    for group, bins in enumerate(BIN_COUNTS):
        rows_in, cols_in, rows_pick, cols_pick, cell_count = tables[group]
        piece = branch[:, BIN_STARTS[group] : BIN_STARTS[group] + bins * bins].reshape(
            images, bins, bins, -1
        )
        joined.append(
            jnp.einsum(
                "ikh,ilw,iklc->ihwc",
                rows_pick.astype(jnp.bfloat16),
                cols_pick.astype(jnp.bfloat16),
                piece,
                preferred_element_type=jnp.float32,
            ).astype(jnp.bfloat16)
        )
    return jnp.concatenate(joined, axis=-1)


def pick_bins(d_joined, width, tables, images):
    branch_width = (d_joined.shape[-1] - width) // 4
    d_up = []
    for group, bins in enumerate(BIN_COUNTS):
        rows_in, cols_in, rows_pick, cols_pick, cell_count = tables[group]
        piece = d_joined[..., width + group * branch_width : width + (group + 1) * branch_width]
        d_up.append(
            jnp.einsum("ikh,ilw,ihwc->iklc", rows_pick, cols_pick, piece).reshape(
                images, bins * bins, -1
            )
        )
    return (d_joined[..., :width], jnp.concatenate(d_up, axis=1))


def gather_channels(field):
    return lax.all_gather(field, "tensor", axis=3, tiled=True)


def scatter_channels(field):
    return lax.psum_scatter(
        field.astype(jnp.bfloat16), "tensor", scatter_dimension=3, tiled=True
    ).astype(jnp.float32)


def local(features, labels, valid, sizes, params, first_moment, squared_mean, average):
    splits = lax.axis_size("tensor")
    owners = lax.axis_size("batch")
    images = features.shape[0]
    gathered = lax.all_gather(params.astype(jnp.bfloat16), "batch", axis=0, tiled=True)
    (
        w_reduce,
        w_short,
        w_middle,
        w_expand,
        w_branch,
        w_unite,
        w_classes,
        w_aux,
        w_aux_classes,
        gains,
    ) = unflatten(gathered, splits)
    norms = [(piece[0], piece[1]) for piece in gain_pieces(gains.astype(jnp.float32), splits)]
    rows_at = jnp.arange(MAP, dtype=jnp.int32)
    inside = (rows_at[None, :, None] < sizes[:, 0][:, None, None]) & (
        rows_at[None, None, :] < sizes[:, 1][:, None, None]
    )
    inside = inside.astype(jnp.float32)[..., None]
    counted = inside * valid.astype(jnp.float32)[..., None]
    labels_hot = (labels[..., None] == jnp.arange(NCLS, dtype=jnp.int32)).astype(jnp.float32)
    class_local = channel_sums(labels_hot * counted)
    whole = lax.all_gather(features, "tensor", axis=3, tiled=True)
    pre_reduce = jnp.dot(whole, w_reduce, preferred_element_type=jnp.float32)
    pre_short = jnp.dot(whole, w_short, preferred_element_type=jnp.float32)
    pre_aux = conv_forward(whole, w_aux, 1)
    leading_part, label_tally = masked_norm_apply(
        [
            (pre_reduce, inside, norms[0]),
            (pre_short, inside, norms[1]),
            (pre_aux, inside, norms[9]),
        ],
        [class_local],
    )
    class_pixel_counts = label_tally[0]
    hidden_one = jax.nn.silu(leading_part[0][0]).astype(jnp.bfloat16)
    aux_act = jax.nn.silu(leading_part[2][0]).astype(jnp.bfloat16)
    hidden_full = gather_channels(hidden_one)
    pre_middle = conv_forward(hidden_full, w_middle, 4)
    second, unused = masked_norm_apply([(pre_middle, inside, norms[2])], [])
    hidden_two = jax.nn.silu(second[0][0]).astype(jnp.bfloat16)
    hidden_two_full = gather_channels(hidden_two)
    pre_expand = jnp.dot(hidden_two_full, w_expand, preferred_element_type=jnp.float32)
    third, unused = masked_norm_apply([(pre_expand, inside, norms[3])], [])
    summed = third[0][0] + leading_part[1][0]
    merged = jax.nn.silu(summed).astype(jnp.bfloat16)
    tables = []
    pooled_list = []
    partial_list = []
    for group, bins in enumerate(BIN_COUNTS):
        rows_in, rows_pick = bin_tables(sizes[:, 0], bins, MAP)
        cols_in, cols_pick = bin_tables(sizes[:, 1], bins, MAP)
        cell_count = (
            jnp.sum(rows_in, axis=2)[:, :, None, None] * jnp.sum(cols_in, axis=2)[:, None, :, None]
        )
        tables.append((rows_in, cols_in, rows_pick, cols_pick, cell_count))
        pooled = (
            jnp.einsum(
                "ikh,ilw,ihwc->iklc",
                rows_in.astype(jnp.bfloat16),
                cols_in.astype(jnp.bfloat16),
                merged,
                preferred_element_type=jnp.float32,
            )
            / cell_count
        )
        pooled = pooled.astype(jnp.bfloat16).reshape(images, bins * bins, -1)
        pooled_list.append(pooled)
        partial_list.append(
            jnp.einsum("ipc,cd->ipd", pooled, w_branch[group], preferred_element_type=jnp.float32)
        )
    branch_pre = lax.psum_scatter(
        jnp.concatenate(partial_list, axis=1).astype(jnp.bfloat16),
        "tensor",
        scatter_dimension=2,
        tiled=True,
    ).astype(jnp.float32)
    branch_items = []
    for group, bins in enumerate(BIN_COUNTS):
        piece = branch_pre[:, BIN_STARTS[group] : BIN_STARTS[group] + bins * bins]
        branch_items.append(
            (piece, jnp.ones(piece.shape[:-1] + (1,), jnp.float32), norms[4 + group])
        )
    fourth, unused = masked_norm_apply(branch_items, [])
    branch_act = jnp.concatenate([jax.nn.silu(kept[0]) for kept in fourth], axis=1).astype(
        jnp.bfloat16
    )
    merged_full, branch_full = (
        lax.all_gather(merged, "tensor", axis=3, tiled=True),
        lax.all_gather(branch_act, "tensor", axis=2, tiled=True),
    )
    joined = spread_bins(merged_full, branch_full, tables, images)
    pre_unite = conv_forward(joined, w_unite, 1)
    fifth, unused = masked_norm_apply([(pre_unite, inside, norms[8])], [])
    united = jax.nn.silu(fifth[0][0]).astype(jnp.bfloat16)
    logit_main, logit_aux = (
        lax.psum_scatter(
            jnp.dot(united, w_classes, preferred_element_type=jnp.float32).astype(jnp.bfloat16),
            "tensor",
            scatter_dimension=1,
            tiled=True,
        ).astype(jnp.float32),
        lax.psum_scatter(
            jnp.dot(aux_act, w_aux_classes, preferred_element_type=jnp.float32).astype(
                jnp.bfloat16
            ),
            "tensor",
            scatter_dimension=1,
            tiled=True,
        ).astype(jnp.float32),
    )
    total_valid = jnp.sum(class_pixel_counts)
    class_weight = total_valid / (NCLS * class_pixel_counts + total_valid)
    loss_weight = jnp.sum(class_pixel_counts * class_weight)
    cell_weight = jnp.sum(labels_hot * class_weight, axis=-1, keepdims=True) * counted
    band_rows = labels.shape[1] // splits
    band_start = lax.axis_index("tensor") * band_rows
    hot_band = lax.dynamic_slice_in_dim(labels_hot, band_start, band_rows, 1)
    weight_band = lax.dynamic_slice_in_dim(cell_weight, band_start, band_rows, 1)
    log_main = jax.nn.log_softmax(logit_main, axis=-1)
    log_aux = jax.nn.log_softmax(logit_aux, axis=-1)
    loss_cells = -jnp.sum(hot_band * (log_main + 0.4 * log_aux), axis=-1, keepdims=True)
    loss_local = jnp.sum(weight_band * loss_cells)
    band_main = (weight_band * (jnp.exp(log_main) - hot_band) / loss_weight).astype(jnp.bfloat16)
    band_aux = (0.4 * weight_band * (jnp.exp(log_aux) - hot_band) / loss_weight).astype(
        jnp.bfloat16
    )
    grad_main, grad_aux = (
        lax.all_gather(band_main, "tensor", axis=1, tiled=True),
        lax.all_gather(band_aux, "tensor", axis=1, tiled=True),
    )
    reduced = {}

    def settle(index, value):
        reduced[index] = value

    settle(6, jnp.einsum("ihwc,ihwk->ck", united, grad_main, preferred_element_type=jnp.float32))
    settle(8, jnp.einsum("ihwc,ihwk->ck", aux_act, grad_aux, preferred_element_type=jnp.float32))
    d_united = jnp.dot(grad_main, w_classes.T, preferred_element_type=jnp.float32) * silu_slope(
        fifth[0][0]
    )
    d_aux = jnp.dot(grad_aux, w_aux_classes.T, preferred_element_type=jnp.float32) * silu_slope(
        leading_part[2][0]
    )
    back_one, sums_one, totals_one = norm_backward([(d_united, fifth[0]), (d_aux, leading_part[2])])
    unite_shift_grad = totals_one[0]
    d_unite_pre = back_one[0].astype(jnp.bfloat16)
    d_aux_pre = back_one[1].astype(jnp.bfloat16)
    settle(5, conv_kernel_back(joined, d_unite_pre, 1))
    d_merged, d_branch = pick_bins(conv_input_back(d_unite_pre, w_unite, 1), C_OUT, tables, images)
    d_merged, d_branch = (
        lax.psum_scatter(
            d_merged.astype(jnp.bfloat16), "tensor", scatter_dimension=3, tiled=True
        ).astype(jnp.float32),
        lax.psum_scatter(
            d_branch.astype(jnp.bfloat16), "tensor", scatter_dimension=2, tiled=True
        ).astype(jnp.float32),
    )
    settle(7, conv_kernel_back(whole, d_aux_pre, 1))
    branch_back = []
    for group, bins in enumerate(BIN_COUNTS):
        piece = d_branch[:, BIN_STARTS[group] : BIN_STARTS[group] + bins * bins]
        branch_back.append((piece * silu_slope(fourth[group][0]), fourth[group]))
    back_two, sums_two, unused = norm_backward(branch_back)
    d_branch_pre = jnp.concatenate(back_two, axis=1).astype(jnp.bfloat16)
    d_branch_full = lax.all_gather(d_branch_pre, "tensor", axis=2, tiled=True)
    branch_grads = []
    for group, bins in enumerate(BIN_COUNTS):
        rows_in, cols_in, rows_pick, cols_pick, cell_count = tables[group]
        piece = d_branch_full[:, BIN_STARTS[group] : BIN_STARTS[group] + bins * bins]
        branch_grads.append(
            jnp.einsum("ipc,ipd->cd", pooled_list[group], piece, preferred_element_type=jnp.float32)
        )
        d_pooled = jnp.dot(piece, w_branch[group].T, preferred_element_type=jnp.float32).reshape(
            images, bins, bins, -1
        )
        d_merged = d_merged + jnp.einsum(
            "ikh,ilw,iklc->ihwc", rows_in, cols_in, d_pooled / cell_count
        )
    settle(4, jnp.stack(branch_grads))
    d_summed = d_merged * silu_slope(summed)
    back_three, sums_three, unused = norm_backward(
        [(d_summed, third[0]), (d_summed, leading_part[1])]
    )
    d_expand_pre = back_three[0].astype(jnp.bfloat16)
    d_short_pre = back_three[1].astype(jnp.bfloat16)
    settle(
        3,
        jnp.einsum(
            "ihwc,ihwd->cd", hidden_two_full, d_expand_pre, preferred_element_type=jnp.float32
        ),
    )
    settle(1, jnp.einsum("ihwc,ihwd->cd", whole, d_short_pre, preferred_element_type=jnp.float32))
    d_two = scatter_channels(jnp.dot(d_expand_pre, w_expand.T, preferred_element_type=jnp.float32))
    back_four, sums_four, unused = norm_backward([(d_two * silu_slope(second[0][0]), second[0])])
    d_middle_pre = back_four[0].astype(jnp.bfloat16)
    settle(2, conv_kernel_back(hidden_full, d_middle_pre, 4))
    d_one = scatter_channels(conv_input_back(d_middle_pre, w_middle, 4))
    back_five, sums_five, unused = norm_backward(
        [(d_one * silu_slope(leading_part[0][0]), leading_part[0])]
    )
    settle(
        0,
        jnp.einsum(
            "ihwc,ihwd->cd",
            whole,
            back_five[0].astype(jnp.bfloat16),
            preferred_element_type=jnp.float32,
        ),
    )
    beta_grads = (
        [sums_five[0], sums_three[2], sums_four[0], sums_three[0]]
        + [sums_two[2 * g] for g in range(4)]
        + [sums_one[0], sums_one[2]]
    )
    gamma_grads = (
        [sums_five[1], sums_three[3], sums_four[1], sums_three[1]]
        + [sums_two[2 * g + 1] for g in range(4)]
        + [sums_one[1], sums_one[3]]
    )
    settle(9, jnp.stack([jnp.concatenate(gamma_grads), jnp.concatenate(beta_grads)]))
    ordered = [reduced[index] for index in range(10)]
    grad_share = lax.psum_scatter(
        jnp.concatenate([part.reshape(owners, -1) for part in ordered], axis=1),
        "batch",
        scatter_dimension=0,
        tiled=True,
    )
    square_all, loss_sum = lax.psum(
        (jnp.sum(grad_share * grad_share), loss_local), ("batch", "tensor")
    )
    grad_norm = jnp.sqrt(square_all)
    clipped = grad_share * jnp.minimum(1.0, 0.05 / (grad_norm + 1e-06))
    new_first = 0.5 * first_moment + 0.5 * clipped
    new_second = 0.5 * squared_mean + 0.5 * clipped * clipped
    keep = 1.0 - 0.5**STEP
    new_params = params - 0.01 * (
        new_first / keep / (jnp.sqrt(new_second / keep) + 1e-08) + 0.01 * params
    )
    new_average = 0.999 * average + 0.001 * new_params
    return (
        new_params,
        new_first,
        new_second,
        new_average,
        new_params.astype(jnp.bfloat16),
        grad_norm,
        loss_sum,
        loss_weight,
        unite_shift_grad,
    )


CELLS = MAP * MAP
EDGE = 104
BATCH = "batch"
TENSOR = "tensor"
GROUP_ROWS = ((0, 1), (1, 5), (5, 14), (14, 50))
BINS = 64
BF = jnp.bfloat16
F32 = jnp.float32
MESH = pl.DeviceIdType.MESH
HALF = 4
OWNERS = 8
SPLITS = 4
MERGED = 4
SLOTS = 5


def scratch_plan():
    plan = dict(
        w_r=((1024, 128), BF),
        w_s=((1024, 512), BF),
        w_m=((4608, 128), BF),
        w_e=((512, 512), BF),
        w_b=((2048, 512), BF),
        w_u=((18432, 128), BF),
        w_own=((4608, 128), BF),
        w_a=((4608, 128), BF),
        w_pair=((1024, 640), BF),
        w_c=((128, 256), BF),
        w_ac=((64, 256), F32),
        gain_in=((OWNERS, 32, 128), F32),
        whole=((SPLITS, CELLS, 256), BF),
        ins=((CELLS, 128), F32),
        col=((CELLS, 128), F32),
        lab=((CELLS, 128), F32),
        table=((BINS, CELLS), F32),
        pool=((BINS, CELLS), BF),
        pick=((BINS, CELLS), BF),
        cells_in=((BINS, 128), F32),
        pad=((9, CELLS + 2 * EDGE, 128), F32),
        grad_pad=((CELLS + 2 * EDGE, 128), F32),
        pre_r=((CELLS, 128), F32),
        pre_s=((CELLS, 512), F32),
        pre_a=((CELLS, 128), F32),
        pre_m=((CELLS, 128), F32),
        pre_e=((CELLS, 512), F32),
        pre_u=((CELLS, 128), F32),
        act_a=((CELLS, 128), BF),
        h1=((SPLITS, CELLS, 128), BF),
        h2=((SPLITS, CELLS, 128), BF),
        joined=((SPLITS, CELLS, 512), BF),
        joined_t=((SPLITS, 512, CELLS), BF),
        pooled=((BINS, 512), BF),
        part_b=((SPLITS, BINS, 128), BF),
        recv_b=((SPLITS, BINS, 128), BF),
        all_b=((OWNERS, BINS, 128), BF),
        act_b=((SPLITS, OWNERS * BINS, 128), BF),
        zsum=((2, OWNERS * BINS, 128), F32),
        z_send=((OWNERS, 2, BINS, 128), BF),
        z_recv=((OWNERS, 2, BINS, 128), BF),
        united=((CELLS, 128), BF),
        logit_send=((CELLS, 512), BF),
        logit_recv=((SPLITS, 144, 512), BF),
        slope_in=((SPLITS, 144, 512), BF),
        d_f=((CELLS, 128), F32),
        d_f2=((CELLS, 128), F32),
        cat_u=((CELLS, 1152), BF),
        cat_a=((CELLS, 640), BF),
        dz_send=((9, BINS, 128), BF),
        dz_recv=((OWNERS, 2, BINS, 128), BF),
        d_act_send=((SPLITS, OWNERS * BINS, 128), BF),
        d_act_recv=((SPLITS, OWNERS * BINS, 128), BF),
        d_img_send=((OWNERS, BINS, 128), BF),
        d_img_recv=((OWNERS, BINS, 128), BF),
        d_bp=((SPLITS, BINS, 128), BF),
        dm_near=((2, CELLS, 512), BF),
        dm_far=((CELLS, 512), BF),
        d_sum=((CELLS, 512), F32),
        d_e=((CELLS, 512), BF),
        d_s=((CELLS, 512), BF),
        dh_send=((SPLITS, CELLS, 128), BF),
        dh_recv=((2, SPLITS, CELLS, 128), BF),
        d_low=((CELLS, 128), BF),
        end_t=((SPLITS, 8, 128), F32),
    )
    for name, rows in SYNCS.items():
        plan["sync_" + name] = ((OWNERS, rows, 128), F32)
    for name, (rows, lanes, kind) in PARTS.items():
        plan["first_" + name] = ((HALF, rows, lanes), kind)
        plan["second_" + name] = ((HALF - 1, rows, lanes), kind)
    plan["first_u"] = ((HALF, SLOTS, 512, 128), BF)
    plan["second_u"] = ((HALF - 1, SLOTS, 512, 128), BF)
    return plan


SYNCS = dict(one=16, two=8, three=8, five=8, b1=8, b3=8, b4=16, b5=8, b6=8, end=8)
PARTS = dict(
    r=(128, 128, BF),
    s=(128, 512, BF),
    m=(576, 128, BF),
    e=(64, 512, BF),
    b=(256, 512, BF),
    a=(576, 128, BF),
    c=(16, 256, BF),
    ac=(8, 256, F32),
)
SEMAPHORES = 1100


class Refs:
    pass


def fold(value):
    return value.reshape(-1, 8, value.shape[-1]).sum(0)


def total(value):
    return jnp.sum(value, axis=0, keepdims=True)


def wide(value, times):
    return jnp.concatenate([value] * times, axis=1)


def dot(left, right):
    return jnp.dot(left, right, preferred_element_type=F32)


def dot_nt(left, right):
    return lax.dot_general(left, right, (((1,), (1,)), ((), ())), preferred_element_type=F32)


def dot_tn(left, right):
    return lax.dot_general(left, right, (((0,), (0,)), ((), ())), preferred_element_type=F32)


def loop(count, body):
    def step(k, carry):
        body(k)
        return carry

    lax.fori_loop(0, count, step, 0)


def rows_at(k, block):
    return pl.ds(pl.multiple_of(k * block, block), block)


def step_kernel(names, *refs):
    (
        sizes, lab_in, feat, gain_own, p_r, p_s, p_m, p_e, p_b, p_u, p_a, p_c, p_ac,
        o_flat, o_a, o_c, o_ac, o_gain, o_misc,
    ) = refs[:19]
    v = Refs()
    for name, ref in zip(names, refs[19:]):
        setattr(v, name, ref)
    sems = refs[-1]
    o_u = o_flat.at[2496:7104, :]
    me = lax.axis_index(BATCH)
    t = lax.axis_index(TENSOR)
    partner = me + 1 - 2 * lax.rem(me, 2)
    t_core = t + 1 - 2 * lax.rem(t, 2)
    t_x = lax.rem(t + 2, SPLITS)
    t_diag = lax.rem(t_core + 2, SPLITS)
    taken = [0]

    def take(count):
        start = taken[0]
        taken[0] = start + count
        assert taken[0] <= SEMAPHORES
        return start

    def far_peer(base, step):
        return lax.rem(base + 2 * step, OWNERS)

    def remote(src, dst, send, recv, device):
        return pltpu.make_async_remote_copy(
            src_ref=src,
            dst_ref=dst,
            send_sem=sems.at[send],
            recv_sem=sems.at[recv],
            device_id=device,
            device_id_type=MESH,
        )

    late = []

    barrier = pltpu.get_barrier_semaphore()
    for k in range(1, OWNERS):
        pl.semaphore_signal(
            barrier, inc=1, device_id={BATCH: lax.rem(me + k, OWNERS)}, device_id_type=MESH
        )
    for k in range(1, SPLITS):
        pl.semaphore_signal(
            barrier, inc=1, device_id={TENSOR: lax.rem(t + k, SPLITS)}, device_id_type=MESH
        )
    pl.semaphore_wait(barrier, OWNERS + SPLITS - 2)

    class Gather:
        def __init__(self, piece, full, rows, skip=0, step=None):
            self.piece, self.full, self.rows = piece, full, rows
            self.skip, self.part = skip, step or rows
            if step:
                self.piece = piece.at[skip : skip + step, :]
            self.near_s, self.far_s, self.pass_s = take(1), take(HALF), take(HALF)
            self.recv, self.keep = take(OWNERS), take(1)

        def at(self, owner):
            if self.rows is None:
                return self.full.at[owner]
            start = pl.multiple_of(owner * self.rows + self.skip, self.part)
            return self.full.at[pl.ds(start, self.part), :]

        def local(self):
            return pltpu.make_async_copy(self.piece, self.at(me), sems.at[self.keep])

        def near(self):
            return remote(
                self.piece, self.at(me), self.near_s, self.recv + me, {BATCH: partner}
            )

        def far(self, step):
            return remote(
                self.piece,
                self.at(me),
                self.far_s + step,
                self.recv + me,
                {BATCH: far_peer(me, step)},
            )

        def passed(self, step, base):
            source = far_peer(base, step)
            return remote(
                self.at(source),
                self.at(source),
                self.pass_s + step,
                self.recv + source,
                {BATCH: partner},
            )

        def start_far(self):
            self.local().start()
            for step in range(1, HALF):
                self.far(step).start()

        def start_near(self):
            self.near().start()

        def forward(self):
            for step in range(1, HALF):
                self.passed(step, me).wait_recv()
                self.passed(step, me).start()

        def finish(self):
            for step in range(HALF):
                self.passed(step, partner).wait_recv()
            self.local().wait()
            self.near().wait_send()
            for step in range(1, HALF):
                self.far(step).wait_send()

        def drain(self):
            for step in range(1, HALF):
                self.passed(step, me).wait_send()

    g_gain = Gather(gain_own, v.gain_in, None)
    g_r = Gather(p_r, v.w_r, 128)
    g_s = Gather(p_s, v.w_s, 128)
    g_a = Gather(p_a, v.w_a, 576)
    g_m = Gather(p_m, v.w_m, 576)
    g_e = Gather(p_e, v.w_e, 64)
    g_b0 = Gather(p_b, v.w_b, 256, 0, 128)
    g_b1 = Gather(p_b, v.w_b, 256, 128, 128)
    g_c = Gather(p_c, v.w_c, 16)
    g_ac = Gather(p_ac, v.w_ac, 8)

    def block_of(owner, slot):
        return 8 if slot == SLOTS - 1 else lax.rem(slot - owner + 8, 8)

    def merged_rows(owner, slot):
        block = owner * 9 + block_of(owner, slot)
        index = lax.div(block, 8) * MERGED + lax.rem(block, 8)
        return pl.ds(pl.multiple_of(index * 512, 512), 512)

    def has(owner, slot, body):
        if slot == SLOTS - 1:
            pl.when(owner < MERGED)(body)
        else:
            body()

    class GatherUnite:
        def __init__(self):
            self.near_s, self.far_s, self.pass_s = (
                take(SLOTS),
                take(SLOTS * HALF),
                take(SLOTS * HALF),
            )
            self.recv, self.keep, self.keep_all = take(SLOTS * OWNERS), take(SLOTS), take(1)

        def source(self, slot):
            return p_u.at[rows_at(block_of(me, slot), 512), :]

        def full(self, owner, slot):
            return v.w_u.at[merged_rows(owner, slot), :]

        def local(self, slot):
            return pltpu.make_async_copy(
                self.source(slot), self.full(me, slot), sems.at[self.keep + slot]
            )

        def whole(self):
            return pltpu.make_async_copy(p_u, v.w_own, sems.at[self.keep_all])

        def near(self, slot):
            return remote(
                self.source(slot),
                self.full(me, slot),
                self.near_s + slot,
                self.recv + me * SLOTS + slot,
                {BATCH: partner},
            )

        def far(self, step, slot):
            return remote(
                self.source(slot),
                self.full(me, slot),
                self.far_s + step * SLOTS + slot,
                self.recv + me * SLOTS + slot,
                {BATCH: far_peer(me, step)},
            )

        def passed(self, step, slot, base):
            source = far_peer(base, step)
            return remote(
                self.full(source, slot),
                self.full(source, slot),
                self.pass_s + step * SLOTS + slot,
                self.recv + source * SLOTS + slot,
                {BATCH: partner},
            )

        def start_far(self, slot):
            def go():
                self.local(slot).start()
                for step in range(1, HALF):
                    self.far(step, slot).start()

            has(me, slot, go)

        def start_near(self, slot):
            has(me, slot, lambda: self.near(slot).start())

        def forward(self, slot):
            for step in range(1, HALF):

                def go(step=step):
                    self.passed(step, slot, me).wait_recv()
                    self.passed(step, slot, me).start()

                has(far_peer(me, step), slot, go)

        def finish(self):
            for slot in range(SLOTS):
                for step in range(HALF):
                    has(
                        far_peer(partner, step),
                        slot,
                        lambda step=step, slot=slot: self.passed(step, slot, partner).wait_recv(),
                    )

                def end(slot=slot):
                    self.local(slot).wait()
                    self.near(slot).wait_send()
                    for step in range(1, HALF):
                        self.far(step, slot).wait_send()

                has(me, slot, end)

        def drain(self):
            for slot in range(SLOTS):
                for step in range(1, HALF):
                    has(
                        far_peer(me, step),
                        slot,
                        lambda step=step, slot=slot: self.passed(step, slot, me).wait_send(),
                    )

    g_u = GatherUnite()

    class Sync:
        def __init__(self, buf):
            self.buf = buf
            self.send, self.recv = take(OWNERS), take(OWNERS)

        def copy(self, k, slot):
            return remote(
                self.buf.at[slot],
                self.buf.at[slot],
                self.send + k,
                self.recv + slot,
                {BATCH: lax.rem(me + k, OWNERS)},
            )

        def start(self, rows):
            for index, row in enumerate(rows):
                self.buf[me, index : index + 1, :] = row
            for index in range(len(rows), self.buf.shape[1]):
                self.buf[me, index : index + 1, :] = jnp.zeros((1, 128), F32)
            for k in range(1, OWNERS):
                self.copy(k, me).start()

        def wait(self):
            for k in range(1, OWNERS):
                self.copy(k, lax.rem(me + k, OWNERS)).wait_recv()
            for k in range(1, OWNERS):
                self.copy(k, me).wait_send()
            value = self.buf[0]
            for slot in range(1, OWNERS):
                value = value + self.buf[slot]
            return value

    class Spread:

        def __init__(self, buf):
            self.buf = buf
            self.send, self.recv = take(SPLITS), take(SPLITS)

        def copy(self, k, slot):
            return remote(
                self.buf.at[slot],
                self.buf.at[slot],
                self.send + k,
                self.recv + slot,
                {TENSOR: lax.rem(t + k, SPLITS)},
            )

        def start(self):
            for k in range(1, SPLITS):
                self.copy(k, t).start()

        def wait(self):
            for k in range(1, SPLITS):
                self.copy(k, lax.rem(t + k, SPLITS)).wait_recv()
            for k in range(1, SPLITS):
                self.copy(k, t).wait_send()

    class Exchange:

        def __init__(self, axis, count, part, into):
            self.axis, self.count, self.part, self.into = axis, count, part, into
            self.mine = me if axis == BATCH else t
            self.send, self.recv = take(count), take(count)

        def copy(self, k, slot):
            other = lax.rem(self.mine + k, self.count)
            return remote(
                self.part(other),
                self.into(slot),
                self.send + k,
                self.recv + slot,
                {self.axis: other},
            )

        def start(self):
            for k in range(1, self.count):
                self.copy(k, self.mine).start()

        def wait(self):
            for k in range(1, self.count):
                self.copy(k, lax.rem(self.mine + k, self.count)).wait_recv()
            for k in range(1, self.count):
                self.copy(k, self.mine).wait_send()

    feat_keep = take(1)
    feat_local = pltpu.make_async_copy(feat, v.whole.at[t], sems.at[feat_keep])
    feat_spread = Exchange(TENSOR, SPLITS, lambda other: feat, lambda slot: v.whole.at[slot])
    for item in (g_gain, g_r, g_s, g_a):
        item.start_far()
        item.start_near()
    feat_local.start()
    feat_spread.start()

    high, across = sizes[0, 0], sizes[0, 1]
    place = lax.broadcasted_iota(jnp.int32, (CELLS, 128), 0).astype(F32)
    row_of = jnp.floor((place + 0.5) / MAP)
    col_of = place - MAP * row_of
    within = (row_of < high.astype(F32)) & (col_of < across.astype(F32))
    v.ins[...] = jnp.where(within, 1.0, 0.0)
    v.col[...] = col_of
    v.lab[...] = jnp.where(within, lab_in[...], -1.0)
    v.table[...] = jnp.zeros((BINS, CELLS), F32)
    lane_place = lax.broadcasted_iota(jnp.int32, (1, CELLS), 1).astype(F32)
    lane_row = jnp.floor((lane_place + 0.5) / MAP)
    lane_col = lane_place - MAP * lane_row

    def ranges(extent, bins, where):
        inside, chosen, counts = [], [], []
        for k in range(bins):
            low = lax.div(k * extent, bins)
            top = lax.div((k + 1) * extent + (bins - 1), bins)
            member = (where >= low.astype(F32)) & (where < top.astype(F32))
            inside.append(jnp.where(member, 1.0, 0.0))
            picked = where * bins >= (k * extent).astype(F32)
            if k < bins - 1:
                picked = picked & (where * bins < ((k + 1) * extent).astype(F32))
            chosen.append(jnp.where(picked, 1.0, 0.0))
            counts.append(top - low)
        return inside, chosen, counts

    picks = []
    v.cells_in[...] = jnp.ones((BINS, 128), F32)
    for group, bins in enumerate(BIN_COUNTS):
        r_in, r_pick, r_count = ranges(high, bins, lane_row)
        c_in, c_pick, c_count = ranges(across, bins, lane_col)
        for a in range(bins):
            for b in range(bins):
                spot = BIN_STARTS[group] + a * bins + b
                v.table[spot : spot + 1, :] = r_in[a] * c_in[b]
                v.cells_in[spot : spot + 1, :] = jnp.full(
                    (1, 128), (r_count[a] * c_count[b]).astype(F32)
                )
                picks.append((spot, r_pick[a] * c_pick[b]))
    v.pool[...] = v.table[...].astype(BF)
    for spot, value in picks:
        v.table[spot : spot + 1, :] = value
    v.pick[...] = v.table[...].astype(BF)
    zeros_edge = jnp.zeros((EDGE, 128), F32)
    for tap in range(9):
        v.pad[tap, 0:EDGE, :] = zeros_edge
        v.pad[tap, EDGE + CELLS :, :] = zeros_edge
    v.grad_pad[0:EDGE, :] = zeros_edge
    v.grad_pad[EDGE + CELLS :, :] = zeros_edge
    lanes = lax.broadcasted_iota(jnp.int32, (1, 256), 1).astype(F32)
    counts = jnp.zeros((8, 256), F32)
    for k in range(0, CELLS, 96):
        counts = counts + fold(
            jnp.where(wide(v.lab[k : k + 96, :], 2) == lanes, 1.0, 0.0)
        )
    class_local = total(counts)
    cells_local = jnp.full((1, 128), (high * across).astype(F32))
    left_half = lax.broadcasted_iota(jnp.int32, (64, 128), 1) < 64

    for item in (g_gain, g_r, g_s):
        item.forward()
    g_a.forward()
    for item in (g_m, g_e):
        item.start_far()
    g_u.whole().start()
    for item in (g_gain, g_r, g_s, g_a):
        item.finish()
    feat_local.wait()
    feat_spread.wait()
    gains = v.gain_in[0]
    for slot in range(1, OWNERS):
        gains = gains + v.gain_in[slot]

    def gamma(row, width=1):
        return jnp.concatenate([gains[row + k : row + k + 1] for k in range(width)], axis=1)

    def beta(row, width=1):
        return gamma(16 + row, width)

    def unpack(chunk):
        for pair in range(5):
            even = v.w_a[rows_at(2 * pair * 8 + chunk, 64), :].astype(F32)
            if pair < 4:
                odd = v.w_a[rows_at((2 * pair + 1) * 8 + chunk, 64), :].astype(F32)
            else:
                odd = jnp.zeros((64, 128), F32)
            low = jnp.where(left_half, even, pltpu.roll(odd, 64, 1))
            top = jnp.where(left_half, pltpu.roll(even, 64, 1), odd)
            v.w_pair[rows_at(2 * chunk, 64), pair * 128 : pair * 128 + 128] = low.astype(BF)
            v.w_pair[rows_at(2 * chunk + 1, 64), pair * 128 : pair * 128 + 128] = top.astype(BF)

    loop(8, unpack)

    def whole_feat():
        return jnp.concatenate([v.whole[k] for k in range(SPLITS)], axis=1)

    v.pre_r[...] = dot(whole_feat(), v.w_r[...])
    for k in range(0, 512, 256):
        v.pre_s[:, k : k + 256] = dot(whole_feat(), v.w_s[:, k : k + 256])
    for pair in (0, 2):
        value = dot(whole_feat(), v.w_pair[:, pair * 128 : pair * 128 + 256])
        v.pad[pair, EDGE : EDGE + CELLS, :] = value[:, :128]
        v.pad[pair + 1, EDGE : EDGE + CELLS, :] = value[:, 128:]
    v.pad[4, EDGE : EDGE + CELLS, :] = dot(whole_feat(), v.w_pair[:, 512:640])

    def offset(tap, spacing):
        return ((tap // 3 - 1) * MAP + (tap % 3 - 1)) * spacing

    def col_mask(at, right):
        where = v.col[at, :] + float(right)
        return jnp.where((where >= 0.0) & (where < float(MAP)), 1.0, 0.0)

    BLOCK = 72

    def shift_sum(taps, spacing, at, slot_of):
        out = None
        for b in (-1, 0, 1):
            part = None
            for tap in taps:
                if tap % 3 - 1 != b:
                    continue
                start = EDGE + at + offset(tap, spacing)
                value = v.pad[slot_of(tap), start : start + BLOCK, :]
                part = value if part is None else part + value
            if part is None:
                continue
            if b:
                part = part * col_mask(slice(at, at + BLOCK), b * spacing)
            out = part if out is None else out + part
        return out

    left_wide = lax.broadcasted_iota(jnp.int32, (BLOCK, 128), 1) < 64
    for at in range(0, CELLS, BLOCK):
        even = shift_sum((0, 2, 4, 6, 8), 1, at, lambda tap: tap // 2)
        odd = shift_sum((1, 3, 5, 7), 1, at, lambda tap: tap // 2)
        v.pre_a[at : at + BLOCK, :] = jnp.where(left_wide, even + pltpu.roll(odd, 64, 1), 0.0)

    def masked_sums(ref):
        width = ref.shape[1]

        def step(k, carry):
            at = rows_at(k, 96)
            value = ref[at, :]
            kept = value * (v.ins[at, :] if width == 128 else wide(v.ins[at, :], width // 128))
            return (carry[0] + fold(kept), carry[1] + fold(kept * value))

        zero = jnp.zeros((8, width), F32)
        sums = lax.fori_loop(0, 6, step, (zero, zero))
        return total(sums[0]), total(sums[1])

    def split_rows(value):
        return [value[:, k : k + 128] for k in range(0, value.shape[1], 128)]

    def join_rows(value, row, count):
        return jnp.concatenate([value[row + k : row + k + 1] for k in range(count)], axis=1)

    def moments(first, second, count):
        mean = first / count
        return mean, lax.rsqrt(second / count - mean * mean + 1e-05)

    sync = Sync(v.sync_one)
    r1, r2 = masked_sums(v.pre_r)
    s1, s2 = masked_sums(v.pre_s)
    a1, a2 = masked_sums(v.pre_a)
    sync.start(
        [r1, r2] + split_rows(s1) + split_rows(s2) + [a1, a2, cells_local] + split_rows(class_local)
    )
    for item in (g_m, g_e):
        item.start_near()
    g_b0.start_far()
    sums = sync.wait()
    count = sums[12:13]
    count4 = wide(count, 4)
    norm_r = moments(sums[0:1], sums[1:2], count)
    norm_s = moments(join_rows(sums, 2, 4), join_rows(sums, 6, 4), count4)
    norm_a = moments(sums[10:11], sums[11:12], count)
    class_count = join_rows(sums, 13, 2)

    def normed(ref, at, norm):
        return (ref[at, :] - norm[0]) * norm[1]

    spread_1 = Spread(v.h1)

    def make_h1(k):
        at = rows_at(k, 96)
        v.h1[t, at, :] = jax.nn.silu(gamma(0) * normed(v.pre_r, at, norm_r) + beta(0)).astype(BF)

    loop(6, make_h1)
    spread_1.start()
    g_m.forward()

    def make_a(k):
        at = rows_at(k, 96)
        v.act_a[at, :] = jax.nn.silu(gamma(15) * normed(v.pre_a, at, norm_a) + beta(15)).astype(BF)

    loop(6, make_a)
    g_e.forward()
    g_m.finish()
    spread_1.wait()

    def full_h(ref):
        return jnp.concatenate([ref[k] for k in range(SPLITS)], axis=1)

    def middle(tap):
        v.pad[tap, EDGE : EDGE + CELLS, :] = dot(full_h(v.h1), v.w_m[rows_at(tap, 512), :])

    loop(9, middle)
    for at in range(0, CELLS, BLOCK):
        v.pre_m[at : at + BLOCK, :] = shift_sum(range(9), 4, at, lambda tap: tap)
    sync = Sync(v.sync_two)
    sync.start(list(masked_sums(v.pre_m)))
    g_b1.start_far()
    g_b0.start_near()
    g_e.finish()
    sums = sync.wait()
    norm_m = moments(sums[0:1], sums[1:2], count)
    spread_2 = Spread(v.h2)

    def make_h2(k):
        at = rows_at(k, 96)
        v.h2[t, at, :] = jax.nn.silu(gamma(5) * normed(v.pre_m, at, norm_m) + beta(5)).astype(BF)

    loop(6, make_h2)
    spread_2.start()
    g_u.start_far(0)
    g_b0.forward()
    g_b1.start_near()
    spread_2.wait()
    for k in range(0, 512, 256):
        v.pre_e[:, k : k + 256] = dot(full_h(v.h2), v.w_e[:, k : k + 256])
    sync = Sync(v.sync_three)
    e1, e2 = masked_sums(v.pre_e)
    sync.start(split_rows(e1) + split_rows(e2))
    g_u.start_far(1)
    g_b1.forward()
    g_u.start_near(0)
    sums = sync.wait()
    norm_e = moments(join_rows(sums, 0, 4), join_rows(sums, 4, 4), count4)

    def summed(at):
        return (
            gamma(6, 4) * normed(v.pre_e, at, norm_e)
            + beta(6, 4)
            + gamma(1, 4) * normed(v.pre_s, at, norm_s)
            + beta(1, 4)
        )

    def make_merged(k):
        at = rows_at(k, 48)
        v.joined[t, at, :] = jax.nn.silu(summed(at)).astype(BF)

    loop(12, make_merged)

    j_send, j_recv = take(3), take(SPLITS)

    def joined_copy(k, slot, device):
        return remote(
            v.joined.at[slot], v.joined.at[slot], j_send + k, j_recv + slot, {TENSOR: device}
        )

    joined_copy(0, t, t_x).start()
    joined_copy(1, t, t_core).start()

    bin_row = lax.broadcasted_iota(jnp.int32, (BINS, 1), 0)

    def group_mask(group, shape=None):
        low, top = GROUP_ROWS[group]
        kept = jnp.where((bin_row >= low) & (bin_row < top), 1.0, 0.0)
        return kept if shape is None else jnp.broadcast_to(kept, shape)

    cells_in = wide(v.cells_in[...], 4)
    pooled = dot(v.pool[...], v.joined[t]) / cells_in
    v.pooled[...] = pooled.astype(BF)
    g_b0.finish()
    g_b1.finish()
    part = jnp.zeros((BINS, 512), F32)
    for group in range(4):
        rows = (v.pooled[...].astype(F32) * group_mask(group)).astype(BF)
        part = part + dot(rows, v.w_b[group * 512 : group * 512 + 512, :])
    for k in range(SPLITS):
        v.part_b[k] = part[:, k * 128 : k * 128 + 128].astype(BF)
    v.recv_b[t] = v.part_b[t]
    ex = Exchange(TENSOR, SPLITS, lambda o: v.part_b.at[o], lambda s: v.recv_b.at[s])
    ex.start()
    g_u.start_far(2)
    g_u.forward(0)
    g_u.start_near(1)
    joined_copy(0, t_x, t_x).wait_recv()
    joined_copy(2, t_x, t_core).start()
    ex.wait()
    own_b = v.recv_b[0].astype(F32)
    for k in range(1, SPLITS):
        own_b = own_b + v.recv_b[k].astype(F32)
    v.all_b[me] = own_b.astype(BF)
    ex = Exchange(BATCH, OWNERS, lambda o: v.all_b.at[me], lambda s: v.all_b.at[s])
    ex.start()
    g_u.start_far(3)
    g_u.forward(1)
    g_u.start_near(2)
    ex.wait()
    all_b = [v.all_b[k].astype(F32) for k in range(OWNERS)]
    sum_b, square_b = all_b[0], all_b[0] * all_b[0]
    for k in range(1, OWNERS):
        sum_b = sum_b + all_b[k]
        square_b = square_b + all_b[k] * all_b[k]
    mean_b = jnp.zeros((BINS, 128), F32)
    scale_b = jnp.zeros((BINS, 128), F32)
    gamma_b = jnp.zeros((BINS, 128), F32)
    beta_b = jnp.zeros((BINS, 128), F32)
    count_b = jnp.zeros((BINS, 1), F32)
    for group, bins in enumerate(BIN_COUNTS):
        kept = group_mask(group)
        size = float(OWNERS * bins * bins)
        mean, scaling = moments(total(sum_b * kept), total(square_b * kept), size)
        mean_b = mean_b + kept * mean
        scale_b = scale_b + kept * scaling
        gamma_b = gamma_b + kept * gamma(10 + group)
        beta_b = beta_b + kept * beta(10 + group)
        count_b = count_b + kept / size
    spread_b = Spread(v.act_b)
    for k in range(OWNERS):
        out = gamma_b * ((all_b[k] - mean_b) * scale_b) + beta_b
        v.act_b[t, k * BINS : k * BINS + BINS, :] = jax.nn.silu(out).astype(BF)
    spread_b.start()
    g_u.start_far(4)
    for item in (g_c, g_ac):
        item.start_far()
        item.start_near()
    g_u.forward(2)
    g_u.start_near(3)
    spread_b.wait()
    g_u.whole().wait()
    row_512 = lax.broadcasted_iota(jnp.int32, (OWNERS * BINS, 1), 0) & (BINS - 1)
    group_id = jnp.where(
        row_512 < 1, 0, jnp.where(row_512 < 5, 1, jnp.where(row_512 < 14, 2, jnp.where(row_512 < 50, 3, 9)))
    )

    def full_act():
        return jnp.concatenate([v.act_b[k] for k in range(SPLITS)], axis=1)

    v.zsum[...] = jnp.zeros((2, OWNERS * BINS, 128), F32)

    def own_branch(j, body):
        chunk = lax.rem(me + j, 8)
        pl.when(chunk >= MERGED)(lambda: body(chunk - MERGED, lax.div(me + j, 8)))

    def make_z(j):
        def body(group, side):
            kept = jnp.where(group_id == group, 1.0, 0.0)
            rows = (full_act().astype(F32) * kept).astype(BF)
            v.zsum[side] = v.zsum[side] + dot(rows, v.w_own[rows_at(j, 512), :])

        own_branch(j, body)

    loop(9, make_z)
    for k in range(OWNERS):
        for side in range(2):
            v.z_send[k, side] = v.zsum[side, k * BINS : k * BINS + BINS, :].astype(BF)
    v.z_recv[me] = v.z_send[me]
    ex = Exchange(BATCH, OWNERS, lambda o: v.z_send.at[o], lambda s: v.z_recv.at[s])
    ex.start()
    g_u.start_near(4)
    g_u.forward(3)
    g_u.forward(4)
    g_c.forward()
    g_ac.forward()
    joined_copy(1, t_core, t_core).wait_recv()
    joined_copy(2, t_diag, t_core).wait_recv()
    for k in range(SPLITS):
        v.joined_t[k] = v.joined[k].T
    ex.wait()
    g_u.finish()

    pick2 = jnp.concatenate([v.pick[...], v.pick[...]], axis=0)

    def tap_z(tap):
        if tap == 0:
            return v.z_recv[0, 0].astype(F32)
        if tap == 8:
            return v.z_recv[7, 1].astype(F32)
        return v.z_recv[tap, 0].astype(F32) + v.z_recv[tap - 1, 1].astype(F32)

    def full_joined():
        return jnp.concatenate([v.joined[k] for k in range(SPLITS)], axis=1)

    def w_tap(tap):
        return v.w_u[rows_at(tap, 2048), :]

    def unite_pair(p):
        value = dot(full_joined(), jnp.concatenate([w_tap(2 * p), w_tap(2 * p + 1)], axis=1))
        v.pad[2 * p, EDGE : EDGE + CELLS, :] = value[:, :128]
        v.pad[2 * p + 1, EDGE : EDGE + CELLS, :] = value[:, 128:]

    loop(4, unite_pair)
    v.pad[8, EDGE : EDGE + CELLS, :] = dot(full_joined(), w_tap(8))
    for tap in range(9):
        z = tap_z(tap)
        high_z = z.astype(BF)
        low_z = (z - high_z.astype(F32)).astype(BF)
        v.pad[tap, EDGE : EDGE + CELLS, :] = v.pad[tap, EDGE : EDGE + CELLS, :] + dot_tn(
            pick2, jnp.concatenate([high_z, low_z], axis=0)
        )
    for at in range(0, CELLS, BLOCK):
        v.pre_u[at : at + BLOCK, :] = shift_sum(range(9), 1, at, lambda tap: tap)
    sync = Sync(v.sync_five)
    sync.start(list(masked_sums(v.pre_u)))
    for item in (g_c, g_ac):
        item.finish()
    for item in (g_gain, g_r, g_s, g_a, g_m, g_e, g_b0, g_b1, g_c, g_ac, g_u):
        item.drain()
    joined_copy(0, t, t_x).wait_send()
    joined_copy(1, t, t_core).wait_send()
    joined_copy(2, t_x, t_core).wait_send()
    w_ac = jnp.concatenate([v.w_ac[...], jnp.zeros((64, 256), F32)], axis=0).astype(BF)
    sums = sync.wait()
    norm_u = moments(sums[0:1], sums[1:2], count)

    def make_u(k):
        at = rows_at(k, 96)
        v.united[at, :] = jax.nn.silu(gamma(14) * normed(v.pre_u, at, norm_u) + beta(14)).astype(BF)

    loop(6, make_u)

    v.logit_send[:, :256] = dot(v.united[...], v.w_c[...]).astype(BF)
    v.logit_send[:, 256:] = dot(v.act_a[...], w_ac).astype(BF)
    ex = Exchange(
        TENSOR,
        SPLITS,
        lambda o: v.logit_send.at[rows_at(o, 144), :],
        lambda s: v.logit_recv.at[s],
    )
    ex.start()
    v.logit_recv[t] = v.logit_send[rows_at(t, 144), :]
    total_valid = jnp.sum(class_count, axis=1, keepdims=True)
    class_weight = total_valid / (NCLS * class_count + total_valid)
    loss_weight = jnp.sum(class_count * class_weight, axis=1, keepdims=True)
    class_weight = jnp.where(lanes < float(NCLS), class_weight, 0.0)
    hot = jnp.where(wide(v.lab[rows_at(t, 144), :], 2) == lanes, 1.0, 0.0)
    cell_weight = jnp.sum(hot * class_weight, axis=1, keepdims=True)
    ex.wait()
    logits = v.logit_recv[0].astype(F32)
    for k in range(1, SPLITS):
        logits = logits + v.logit_recv[k].astype(F32)

    def log_softmax(value):
        value = jnp.where(lanes < float(NCLS), value, -1e30)
        value = value - jnp.max(value, axis=1, keepdims=True)
        powers = jnp.exp(value)
        mass = jnp.sum(powers, axis=1, keepdims=True)
        return value - jnp.log(mass), powers / mass

    log_main, p_main = log_softmax(logits[:, :256])
    log_aux, p_aux = log_softmax(logits[:, 256:])
    loss_rows = total(fold(-cell_weight * hot * (log_main + 0.4 * log_aux)))
    loss_local = loss_rows[:, :128] + loss_rows[:, 128:]
    o_misc[1:2, :] = loss_local
    v.slope_in[t, :, :256] = (cell_weight * (p_main - hot) / loss_weight).astype(BF)
    v.slope_in[t, :, 256:] = (0.4 * cell_weight * (p_aux - hot) / loss_weight).astype(BF)
    spread_g = Spread(v.slope_in)
    spread_g.start()
    spread_g.wait()
    g_main = v.slope_in[:, :, :256].reshape(CELLS, 256)
    g_aux = v.slope_in[:, :, 256:].reshape(CELLS, 256)
    v.d_f[...] = dot_nt(g_main, v.w_c[...])
    v.d_f2[...] = dot_nt(g_aux, w_ac)

    def slope(value):
        gate = jax.nn.sigmoid(value)
        return gate * (1.0 + value * (1.0 - gate))

    def through_silu(ref, pre, norm, row):
        def step(k, carry):
            at = rows_at(k, 96)
            unit = normed(pre, at, norm)
            value = ref[at, :] * slope(gamma(row) * unit + beta(row))
            ref[at, :] = value
            return (carry[0] + fold(value), carry[1] + fold(value * unit))

        zero = jnp.zeros((8, 128), F32)
        sums = lax.fori_loop(0, 6, step, (zero, zero))
        return [total(sums[0]), total(sums[1])]

    def back_norm(value, unit, mask, norm, gain, first, second, size):
        inner = value - mask * (first + unit * second) / size
        return gain * norm[1] * inner

    gain_grads = {}
    sync = Sync(v.sync_b1)
    sync.start(
        through_silu(v.d_f, v.pre_u, norm_u, 14) + through_silu(v.d_f2, v.pre_a, norm_a, 15)
    )

    class Scatter:
        def __init__(self, first, second, full, rows, out, base=0):
            self.full, self.rows, self.out, self.base = full, rows, out, base
            self.first, self.second = first, second
            self.near_s, self.near_r = take(HALF), take(HALF)
            self.far_s, self.far_r = take(HALF), take(HALF)
            self.block = min(rows, 64)

        def near(self, step):
            dest = far_peer(partner, step)
            return remote(
                self.full.at[rows_at(dest, self.rows), :],
                self.first.at[step],
                self.near_s + step,
                self.near_r + step,
                {BATCH: partner},
            )

        def far(self, step):
            return remote(
                self.first.at[step],
                self.second.at[step - 1],
                self.far_s + step,
                self.far_r + step,
                {BATCH: far_peer(me, step)},
            )

        def start(self):
            for step in (1, 2, 3, 0):
                self.near(step).start()

        def middle(self):
            kind = self.first.dtype
            for step in range(1, HALF):
                self.near(step).wait_recv()
                base = far_peer(me, step) * (self.rows // self.block)

                def add(k, step=step, base=base):
                    at = rows_at(k, self.block)
                    value = self.full[rows_at(base + k, self.block), :].astype(F32)
                    value = value + self.first[step, at, :].astype(F32)
                    self.first[step, at, :] = value.astype(kind)

                loop(self.rows // self.block, add)
                self.far(step).start()

        def end(self):
            self.near(0).wait_recv()
            for step in range(1, HALF):
                self.far(step).wait_recv()
            base = me * (self.rows // self.block)

            def add(k, carry):
                at = rows_at(k, self.block)
                value = self.full[rows_at(base + k, self.block), :].astype(F32)
                value = value + self.first[0, at, :].astype(F32)
                for step in range(1, HALF):
                    value = value + self.second[step - 1, at, :].astype(F32)
                if self.out is o_flat:
                    times = value.shape[1] // 128
                    start = self.base + k * self.block * times
                    for q in range(times):
                        where = pl.ds(start + q, self.block, stride=times if times > 1 else None)
                        self.out[where, :] = value[:, q * 128 : q * 128 + 128]
                else:
                    self.out[at, :] = value
                return carry + fold(value * value)

            squares = lax.fori_loop(
                0, self.rows // self.block, add, jnp.zeros((8, self.full.shape[1]), F32)
            )
            for step in (1, 2, 3, 0):
                self.near(step).wait_send()
                if step:
                    self.far(step).wait_send()
            return sum(split_rows(total(squares)))

    s_c = Scatter(v.first_c, v.second_c, v.w_c, 16, o_c)
    s_ac = Scatter(v.first_ac, v.second_ac, v.w_ac, 8, o_ac)
    s_a = Scatter(v.first_a, v.second_a, v.w_a, 576, o_a)
    s_b = Scatter(v.first_b, v.second_b, v.w_b, 256, o_flat, 1472)
    s_s = Scatter(v.first_s, v.second_s, v.w_s, 128, o_flat, 128)
    s_e = Scatter(v.first_e, v.second_e, v.w_e, 64, o_flat, 1216)
    s_m = Scatter(v.first_m, v.second_m, v.w_m, 576, o_flat, 640)
    s_r = Scatter(v.first_r, v.second_r, v.w_r, 128, o_flat, 0)

    class ScatterUnite:
        def __init__(self):
            self.near_s, self.near_r = take(SLOTS * HALF), take(SLOTS * HALF)
            self.far_s, self.far_r = take(SLOTS * HALF), take(SLOTS * HALF)

        def near(self, step, slot, base):
            dest = far_peer(base, step)
            return remote(
                v.w_u.at[merged_rows(dest, slot), :],
                v.first_u.at[step, slot],
                self.near_s + step * SLOTS + slot,
                self.near_r + step * SLOTS + slot,
                {BATCH: partner},
            )

        def far(self, step, slot):
            return remote(
                v.first_u.at[step, slot],
                v.second_u.at[step - 1, slot],
                self.far_s + step * SLOTS + slot,
                self.far_r + step * SLOTS + slot,
                {BATCH: far_peer(me, step)},
            )

        def own_rows(self, owner, slot, k):
            block = owner * 9 + block_of(owner, slot)
            index = lax.div(block, 8) * MERGED + lax.rem(block, 8)
            return rows_at(index * 8 + k, 64)

        def start(self, slot):
            for step in (1, 2, 3, 0):
                has(
                    far_peer(partner, step),
                    slot,
                    lambda step=step: self.near(step, slot, partner).start(),
                )

        def middle(self, slot):
            for step in range(1, HALF):
                owner = far_peer(me, step)

                def go(step=step, owner=owner):
                    self.near(step, slot, me).wait_recv()

                    def add(k):
                        at = rows_at(k, 64)
                        value = v.w_u[self.own_rows(owner, slot, k), :].astype(F32)
                        value = value + v.first_u[step, slot, at, :].astype(F32)
                        v.first_u[step, slot, at, :] = value.astype(BF)

                    loop(8, add)
                    self.far(step, slot).start()

                has(owner, slot, go)

        def end(self):
            for slot in range(SLOTS):

                def go(slot=slot):
                    self.near(0, slot, me).wait_recv()
                    for step in range(1, HALF):
                        self.far(step, slot).wait_recv()
                    j = block_of(me, slot)

                    def add(k):
                        at = rows_at(k, 64)
                        value = v.w_u[self.own_rows(me, slot, k), :].astype(F32)
                        value = value + v.first_u[0, slot, at, :].astype(F32)
                        for step in range(1, HALF):
                            value = value + v.second_u[step - 1, slot, at, :].astype(F32)
                        o_u[rows_at(j * 8 + k, 64), :] = value

                    loop(8, add)

                has(me, slot, go)
                for step in (1, 2, 3, 0):
                    has(
                        far_peer(partner, step),
                        slot,
                        lambda step=step, slot=slot: self.near(step, slot, partner).wait_send(),
                    )
                    if step:
                        has(
                            far_peer(me, step),
                            slot,
                            lambda step=step, slot=slot: self.far(step, slot).wait_send(),
                        )

            def square(k, carry):
                value = o_u[rows_at(k, 64), :]
                return carry + fold(value * value)

            squares = lax.fori_loop(0, 72, square, jnp.zeros((8, 128), F32))
            return sum(split_rows(total(squares)))

    s_u = ScatterUnite()

    v.w_c[...] = dot_tn(v.united[...], g_main).astype(BF)
    v.w_ac[...] = dot_tn(v.act_a[...], g_aux)[:64]
    s_c.start()
    s_ac.start()
    sums = sync.wait()
    gain_grads[14] = (sums[1:2], sums[0:1])
    gain_grads[15] = (sums[3:4], sums[2:3])

    def spread_taps(ref, pre, norm, row, first, second):
        def step(k):
            at = rows_at(k, 96)
            value = back_norm(
                ref[at, :], normed(pre, at, norm), v.ins[at, :], norm, gamma(row), first, second, count
            )
            ref[at, :] = value.astype(BF).astype(F32)

        loop(6, step)
        v.grad_pad[EDGE : EDGE + CELLS, :] = ref[...]

    def back_tap(tap, spacing, at):
        start = EDGE + at - offset(tap, spacing)
        value = v.grad_pad[start : start + 96, :]
        right = tap % 3 - 1
        if right:
            value = value * col_mask(slice(at, at + 96), -right * spacing)
        return value

    def fill(cat, spacing):
        for tap in range(9):
            for at in range(0, CELLS, 96):
                cat[at : at + 96, tap * 128 : tap * 128 + 128] = back_tap(tap, spacing, at).astype(
                    BF
                )

    spread_taps(v.d_f, v.pre_u, norm_u, 14, sums[0:1], sums[1:2])
    fill(v.cat_u, 1)

    dz = dot(v.pick[...], v.cat_u[...])
    for tap in range(9):
        v.dz_send[tap] = dz[:, tap * 128 : tap * 128 + 128].astype(BF)
    v.dz_recv[me] = v.dz_send[pl.ds(me, 2)]
    ex_dz = Exchange(
        BATCH, OWNERS, lambda o: v.dz_send.at[pl.ds(o, 2)], lambda s: v.dz_recv.at[s]
    )
    ex_dz.start()

    def merged_back(c):
        weight = jnp.concatenate(
            [v.w_u[rows_at(tap * MERGED + c, 512), :] for tap in range(9)], axis=1
        )
        v.joined[c] = dot_nt(v.cat_u[...], weight).astype(BF)

    near_s, near_r, far_s, far_r = take(2), take(2), take(1), take(1)

    def dm_near(k, slot):
        return remote(
            v.joined.at[slot], v.dm_near.at[k], near_s + k, near_r + k, {TENSOR: t_core}
        )

    merged_back(t_diag)
    dm_near(1, t_diag).start()
    merged_back(t_core)
    dm_near(0, t_core).start()
    ex_dz.wait()

    d_act = v.d_sum.at[0 : OWNERS * BINS, :]
    d_act[...] = jnp.zeros((OWNERS * BINS, 512), F32)

    def branch_back(j):
        def body(group, side):
            kept = jnp.where(group_id == group, 1.0, 0.0)
            value = v.dz_recv[:, side].reshape(OWNERS * BINS, 128).astype(F32) * kept
            value = value.astype(BF)
            o_u[rows_at(j, 512), :] = dot_tn(full_act(), value)
            d_act[...] = d_act[...] + dot_nt(value, v.w_own[rows_at(j, 512), :])

        own_branch(j, body)

    loop(9, branch_back)
    for k in range(SPLITS):
        v.d_act_send[k] = d_act[:, k * 128 : k * 128 + 128].astype(BF)
    v.d_act_recv[t] = v.d_act_send[t]
    ex = Exchange(TENSOR, SPLITS, lambda o: v.d_act_send.at[o], lambda s: v.d_act_recv.at[s])
    ex.start()
    merged_back(t_x)
    merged_back(t)

    def unite_grad(c):
        for p in range(5):
            width = 256 if p < 4 else 128
            value = dot(v.joined_t[c], v.cat_u[:, p * 256 : p * 256 + width])
            v.w_u[rows_at(2 * p * MERGED + c, 512), :] = value[:, :128].astype(BF)
            if p < 4:
                v.w_u[rows_at((2 * p + 1) * MERGED + c, 512), :] = value[:, 128:].astype(BF)

    loop(SPLITS, unite_grad)
    s_u.start(0)
    dm_near(1, t_x).wait_recv()

    def add_x(k):
        at = rows_at(k, 48)
        value = v.joined[t_x, at, :].astype(F32) + v.dm_near[1, at, :].astype(F32)
        v.joined[t_x, at, :] = value.astype(BF)

    loop(12, add_x)
    dm_far = remote(v.joined.at[t_x], v.dm_far, far_s, far_r, {TENSOR: t_x})
    ex.wait()
    for k in range(OWNERS):
        at = slice(k * BINS, k * BINS + BINS)
        value = v.d_act_recv[0, at, :].astype(F32)
        for slot in range(1, SPLITS):
            value = value + v.d_act_recv[slot, at, :].astype(F32)
        v.d_img_send[k] = value.astype(BF)
    v.d_img_recv[me] = v.d_img_send[me]
    ex = Exchange(BATCH, OWNERS, lambda o: v.d_img_send.at[o], lambda s: v.d_img_recv.at[s])
    ex.start()
    dm_far.start()
    s_u.start(1)

    spread_taps(v.d_f2, v.pre_a, norm_a, 15, sums[2:3], sums[3:4])
    for p in range(5):
        for at in range(0, CELLS, 96):
            value = back_tap(2 * p, 1, at)
            if p < 4:
                value = value + pltpu.roll(back_tap(2 * p + 1, 1, at), 64, 1)
            v.cat_a[at : at + 96, p * 128 : p * 128 + 128] = value.astype(BF)

    def aux_grad(c2):
        value2 = dot_tn(v.whole[c2], v.cat_a[...])
        for half in range(2):
            value = value2[half * 128 : half * 128 + 128]
            c = 2 * c2 + half
            for p in range(5):
                low = value[:64, p * 128 : p * 128 + 128]
                top = value[64:, p * 128 : p * 128 + 128]
                even = jnp.where(left_half, low, pltpu.roll(top, 64, 1))
                v.w_a[rows_at(2 * p * 8 + c, 64), :] = even.astype(BF)
                if p < 4:
                    odd = jnp.where(left_half, pltpu.roll(low, 64, 1), top)
                    v.w_a[rows_at((2 * p + 1) * 8 + c, 64), :] = odd.astype(BF)

    loop(SPLITS, aux_grad)
    s_u.middle(0)
    ex.wait()
    d_b = v.d_img_recv[0].astype(F32)
    for k in range(1, OWNERS):
        d_b = d_b + v.d_img_recv[k].astype(F32)
    unit_b = (v.all_b[me].astype(F32) - mean_b) * scale_b
    d_b = d_b * slope(gamma_b * unit_b + beta_b)
    sync = Sync(v.sync_b3)
    sync.start(
        [total(d_b * group_mask(g)) for g in range(4)]
        + [total(d_b * unit_b * group_mask(g)) for g in range(4)]
    )
    s_u.start(2)
    s_a.start()
    sums = sync.wait()
    first_b = jnp.zeros((BINS, 128), F32)
    second_b = jnp.zeros((BINS, 128), F32)
    for group in range(4):
        kept = group_mask(group)
        gain_grads[10 + group] = (sums[4 + group : 5 + group], sums[group : group + 1])
        first_b = first_b + kept * sums[group : group + 1]
        second_b = second_b + kept * sums[4 + group : 5 + group]
    inner = d_b - (first_b + unit_b * second_b) * count_b
    v.d_bp[t] = (gamma_b * scale_b * inner).astype(BF)
    spread_d = Spread(v.d_bp)
    spread_d.start()
    s_u.start(3)
    s_u.middle(1)
    spread_d.wait()
    d_bp = jnp.concatenate([v.d_bp[k] for k in range(SPLITS)], axis=1)
    d_pooled = jnp.zeros((BINS, 512), F32)
    d_groups = []
    for group in range(4):
        d_groups.append((d_bp.astype(F32) * group_mask(group)).astype(BF))
        d_pooled = d_pooled + dot_nt(d_groups[group], v.w_b[group * 512 : group * 512 + 512, :])
    for group in range(4):
        v.w_b[group * 512 : group * 512 + 512, :] = dot_tn(v.pooled[...], d_groups[group]).astype(BF)
    d_pooled = (d_pooled / cells_in).astype(BF)
    v.d_sum[...] = dot_tn(v.pool[...], d_pooled)
    dm_near(0, t).wait_recv()
    dm_far.wait_recv()

    def through_sum(k, carry):
        at = rows_at(k, 48)
        value = v.d_sum[at, :] + v.joined[t, at, :].astype(F32) + v.dm_near[0, at, :].astype(F32)
        value = (value + v.dm_far[at, :].astype(F32)) * slope(summed(at))
        v.d_sum[at, :] = value
        return (
            carry[0] + fold(value),
            carry[1] + fold(value * normed(v.pre_e, at, norm_e)),
            carry[2] + fold(value * normed(v.pre_s, at, norm_s)),
        )

    zero = jnp.zeros((8, 512), F32)
    three = [total(item) for item in lax.fori_loop(0, 12, through_sum, (zero, zero, zero))]
    sync = Sync(v.sync_b4)
    sync.start(split_rows(three[0]) + split_rows(three[1]) + split_rows(three[2]))
    s_u.start(4)
    s_u.middle(2)
    sums = sync.wait()
    first_s = join_rows(sums, 0, 4)
    second_e, second_s = join_rows(sums, 4, 4), join_rows(sums, 8, 4)
    for k in range(4):
        gain_grads[6 + k] = (sums[4 + k : 5 + k], sums[k : k + 1])
        gain_grads[1 + k] = (sums[8 + k : 9 + k], sums[k : k + 1])

    def back_both(k):
        at = rows_at(k, 48)
        value, mask = v.d_sum[at, :], wide(v.ins[at, :], 4)
        v.d_e[at, :] = back_norm(
            value, normed(v.pre_e, at, norm_e), mask, norm_e, gamma(6, 4), first_s, second_e, count4
        ).astype(BF)
        v.d_s[at, :] = back_norm(
            value, normed(v.pre_s, at, norm_s), mask, norm_s, gamma(1, 4), first_s, second_s, count4
        ).astype(BF)

    loop(12, back_both)

    def back_hidden(grad, weight, index):
        value = dot_nt(grad, weight)
        for k in range(SPLITS):
            v.dh_send[k] = value[:, k * 128 : k * 128 + 128].astype(BF)
        v.dh_recv[index, t] = v.dh_send[t]
        ex = Exchange(
            TENSOR, SPLITS, lambda o: v.dh_send.at[o], lambda s: v.dh_recv.at[index, s]
        )
        ex.start()
        return ex

    def hidden_sum(index):
        def step(k):
            at = rows_at(k, 96)
            value = v.dh_recv[index, 0, at, :].astype(F32)
            for slot in range(1, SPLITS):
                value = value + v.dh_recv[index, slot, at, :].astype(F32)
            v.d_f[at, :] = value

        loop(6, step)

    ex = back_hidden(v.d_e[...], v.w_e[...], 0)
    s_b.start()
    s_u.middle(3)
    for k in range(SPLITS):
        v.w_e[k * 128 : k * 128 + 128, :] = dot_tn(v.h2[k], v.d_e[...]).astype(BF)
    ex.wait()
    hidden_sum(0)
    sync = Sync(v.sync_b5)
    sync.start(through_silu(v.d_f, v.pre_m, norm_m, 5))
    s_e.start()
    s_c.middle()
    s_ac.middle()
    s_a.middle()
    s_u.middle(4)
    sums = sync.wait()
    gain_grads[5] = (sums[1:2], sums[0:1])
    spread_taps(v.d_f, v.pre_m, norm_m, 5, sums[0:1], sums[1:2])
    fill(v.cat_u, 4)
    weight = jnp.concatenate([v.w_m[tap * 512 : tap * 512 + 512, :] for tap in range(9)], axis=1)
    ex = back_hidden(v.cat_u[...], weight, 1)

    def short_grad(c):
        v.w_s[rows_at(c, 256), :] = dot_tn(v.whole[c], v.d_s[...]).astype(BF)

    loop(SPLITS, short_grad)
    s_s.start()
    s_b.middle()
    ex.wait()
    hidden_sum(1)
    sync = Sync(v.sync_b6)
    sync.start(through_silu(v.d_f, v.pre_r, norm_r, 0))

    def middle_grad(k):
        value = dot_tn(v.h1[k], v.cat_u[...])
        for tap in range(9):
            v.w_m[rows_at(tap * 4 + k, 128), :] = value[:, tap * 128 : tap * 128 + 128].astype(BF)

    loop(SPLITS, middle_grad)
    s_m.start()
    s_e.middle()
    s_s.middle()
    sums = sync.wait()
    gain_grads[0] = (sums[1:2], sums[0:1])

    def back_reduce(k):
        at = rows_at(k, 96)
        v.d_low[at, :] = back_norm(
            v.d_f[at, :], normed(v.pre_r, at, norm_r), v.ins[at, :], norm_r, gamma(0), sums[0:1], sums[1:2], count
        ).astype(BF)

    loop(6, back_reduce)

    def reduce_grad(c):
        v.w_r[rows_at(c, 256), :] = dot_tn(v.whole[c], v.d_low[...]).astype(BF)

    loop(SPLITS, reduce_grad)
    s_r.start()
    for item in (s_m, s_r):
        item.middle()
    rest = (s_c, s_ac, s_b, s_a, s_e, s_s, s_m, s_r)
    squares = s_u.end()
    for item in rest:
        squares = squares + item.end()
    dm_near(1, t_diag).wait_send()
    dm_near(0, t_core).wait_send()
    dm_far.wait_send()

    for row in range(16):
        o_gain[row : row + 1, :] = gain_grads[row][0]
        o_gain[16 + row : 17 + row, :] = gain_grads[row][1]
    gain_square = o_gain[...] * o_gain[...]
    squares = squares + total(gain_square) / OWNERS

    sync = Sync(v.sync_end)
    sync.start([squares, o_misc[1:2, :]])
    v.end_t[t] = sync.wait()
    spread_e = Spread(v.end_t)
    spread_e.start()
    spread_e.wait()
    ends = v.end_t[0]
    for k in range(1, SPLITS):
        ends = ends + v.end_t[k]
    o_misc[...] = ends
    o_misc[2:3, :] = jnp.broadcast_to(loss_weight, (1, 128))


def whole_step(sizes, labels, feat, gains, pieces):
    plan = scratch_plan()
    vmem = pl.BlockSpec(memory_space=pltpu.VMEM)
    anywhere = pl.BlockSpec(memory_space=pl.ANY)
    outs = [(7712, 128), (576, 128), (16, 256), (8, 256), (32, 128), (8, 128)]
    return pl.pallas_call(
        functools.partial(step_kernel, tuple(plan)),
        out_shape=[jax.ShapeDtypeStruct(shape, F32) for shape in outs],
        in_specs=[pl.BlockSpec(memory_space=pltpu.SMEM), vmem, anywhere, anywhere]
        + [anywhere] * len(pieces),
        out_specs=[vmem] * len(outs),
        scratch_shapes=[pltpu.VMEM(shape, kind) for shape, kind in plan.values()]
        + [pltpu.SemaphoreType.DMA((SEMAPHORES,))],
        compiler_params=pltpu.CompilerParams(
            collective_id=0, has_side_effects=True, vmem_limit_bytes=63 * 1024 * 1024
        ),
        name="whole_step",
    )(sizes, labels, feat, gains, *pieces)


def update_kernel(scale, grad, param, first, second, average, o_param, o_first, o_second, o_average):
    clipped = grad[...] * scale[0]
    new_first = 0.5 * first[...] + 0.5 * clipped
    new_second = 0.5 * second[...] + 0.5 * clipped * clipped
    keep = 1.0 - 0.5**STEP
    old = param[...]
    new = old - 0.01 * (new_first / keep / (jnp.sqrt(new_second / keep) + 1e-08) + 0.01 * old)
    o_param[...] = new
    o_first[...] = new_first
    o_second[...] = new_second
    o_average[...] = 0.999 * average[...] + 0.001 * new


def update(scale, grad, param, first, second, average):
    rows = grad.shape[0]
    block = pl.BlockSpec((512, 128), lambda i: (i, 0))
    return pl.pallas_call(
        update_kernel,
        grid=(pl.cdiv(rows, 512),),
        out_shape=[jax.ShapeDtypeStruct((rows, 128), jnp.float32)] * 4,
        in_specs=[pl.BlockSpec(memory_space=pltpu.SMEM)] + [block] * 5,
        out_specs=[block] * 4,
        name="update",
    )(scale.reshape(1), grad, param, first, second, average)

def fits(splits, owners):
    return splits == SPLITS and owners == OWNERS


def local_fast(features, labels, valid, sizes, params, first_moment, squared_mean, average):
    me = lax.axis_index("batch")
    shapes = segment_shapes(SPLITS)
    counts = []
    for shape in shapes:
        count = 1
        for extent in shape:
            count = count * extent
        counts.append(count // OWNERS)
    starts = [0]
    for count in counts:
        starts.append(starts[-1] + count)
    flat = params.reshape(-1, 128)
    low = flat.astype(BF)
    tail = lax.optimization_barrier(flat[starts[6] // 128 :]).reshape(-1)
    cut = [tail[starts[k] - starts[6] : starts[k + 1] - starts[6]] for k in range(6, 10)]
    rows = [low[starts[k] // 128 : starts[k + 1] // 128] for k in range(6)]
    aux = cut[1].astype(BF).reshape(9, 2, 64, 64)
    pieces = [
        rows[0],
        rows[1].reshape(128, 512),
        rows[2],
        rows[3].reshape(64, 512),
        rows[4].reshape(256, 512),
        rows[5],
        jnp.concatenate([aux[:, 0], aux[:, 1]], axis=-1).reshape(576, 128),
        jnp.pad(cut[0].astype(BF).reshape(16, NCLS), ((0, 0), (0, 256 - NCLS))),
        jnp.pad(
            cut[2].astype(BF).astype(F32).reshape(8, NCLS), ((0, 0), (0, 256 - NCLS))
        ),
    ]
    width = shapes[9][1]
    share = counts[9]
    per_row = width // share
    spot = jnp.zeros((2, 2048), F32)
    spot = lax.dynamic_update_slice(
        spot,
        cut[3].astype(BF).astype(F32).reshape(1, share),
        (me // per_row, (me % per_row) * share),
    )
    marked = jnp.where(valid > 0, labels, -1).astype(F32).reshape(CELLS, 1)
    outs = whole_step(
        sizes,
        jnp.broadcast_to(marked, (CELLS, 128)),
        features.reshape(CELLS, -1),
        spot.reshape(32, 128),
        pieces,
    )
    gain_grad = lax.dynamic_slice(
        outs[4].reshape(2, 2048)[:, :width].reshape(-1), (me * share,), (share,)
    )
    aux_grad = outs[1].reshape(9, 64, 2, 64).transpose(0, 2, 1, 3)
    tail_grad = jnp.concatenate(
        [
            outs[2][:, :NCLS].reshape(-1),
            aux_grad.reshape(-1),
            outs[3][:, :NCLS].reshape(-1),
            gain_grad,
        ]
    ).reshape(-1, 128)
    grad_share = lax.dynamic_update_slice(outs[0], tail_grad, (starts[6] // 128, 0))
    misc = outs[5]
    grad_norm = jnp.sqrt(jnp.sum(misc[0]))
    scale = jnp.minimum(1.0, 0.05 / (grad_norm + 1e-06))
    new_params, new_first, new_second, new_average = [
        item.reshape(params.shape)
        for item in update(
            scale,
            grad_share,
            flat,
            first_moment.reshape(-1, 128),
            squared_mean.reshape(-1, 128),
            average.reshape(-1, 128),
        )
    ]
    return (
        new_params,
        new_first,
        new_second,
        new_average,
        new_params.astype(BF),
        grad_norm,
        jnp.sum(misc[1]),
        misc[2, 0],
        outs[4][30],
    )


def solution(mesh):
    chosen = local_fast if fits(mesh.shape["tensor"], mesh.shape["batch"]) else local
    return jax.shard_map(
        chosen,
        mesh=mesh,
        in_specs=(
            P("batch", None, None, "tensor"),
            P("batch", None, None),
            P("batch", None, None),
            P("batch", None),
            P("tensor", "batch"),
            P("tensor", "batch"),
            P("tensor", "batch"),
            P("tensor", "batch"),
        ),
        out_specs=(
            P("tensor", "batch"),
            P("tensor", "batch"),
            P("tensor", "batch"),
            P("tensor", "batch"),
            P("tensor", "batch"),
            P(),
            P(),
            P(),
            P("tensor"),
        ),
        check_vma=False,
    )
```

```python
import functools

import jax
import jax.numpy as jnp
from jax import lax
from jax.experimental import pallas as pl
from jax.experimental.pallas import tpu as pltpu
from jax.sharding import PartitionSpec as P

C_IN = 1024
MID = 512
C_OUT = 2048
PPM = 512
AUXW = 256
NCLS = 150
MAP = 24
STEP = 3


BIN_COUNTS = (1, 2, 3, 6)
BIN_STARTS = (0, 1, 5, 14)


def segment_shapes(splits):
    return [
        (C_IN, MID // splits),
        (C_IN, C_OUT // splits),
        (9, MID, MID // splits),
        (MID, C_OUT // splits),
        (4, C_OUT // splits, PPM),
        (9, C_OUT + 4 * PPM, PPM // splits),
        (PPM // splits, NCLS),
        (9, C_IN, AUXW // splits),
        (AUXW // splits, NCLS),
        (2, (2 * MID + 2 * C_OUT + 5 * PPM + AUXW) // splits),
    ]


def unflatten(rows, splits):
    split_parts = []
    start = 0
    for shape in segment_shapes(splits):
        count = 1
        for extent in shape:
            count = count * extent
        count = count // rows.shape[0]
        split_parts.append(rows[:, start : start + count].reshape(shape))
        start = start + count
    return split_parts


def gain_pieces(gains, splits):
    widths = [MID, C_OUT, MID, C_OUT, PPM, PPM, PPM, PPM, PPM, AUXW]
    split_parts = []
    start = 0
    for width in widths:
        step_width = width // splits
        split_parts.append(gains[:, start : start + step_width])
        start = start + step_width
    return split_parts


def shifted(field, down, right):
    image_height, width = (field.shape[1], field.shape[2])
    rows_pad, cols_pad = (abs(down), abs(right))
    padded = jnp.pad(field, ((0, 0), (rows_pad, rows_pad), (cols_pad, cols_pad), (0, 0)))
    return padded[
        :,
        rows_pad + down : rows_pad + down + image_height,
        cols_pad + right : cols_pad + right + width,
        :,
    ]


def conv_forward(field, kernel, spacing):
    total = jnp.zeros(field.shape[:-1] + (kernel.shape[2],), jnp.float32)
    for tap in range(9):
        moved = shifted(field, (tap // 3 - 1) * spacing, (tap % 3 - 1) * spacing)
        total = total + jnp.dot(moved, kernel[tap], preferred_element_type=jnp.float32)
    return total


def conv_input_back(grad, kernel, spacing):
    total = jnp.zeros(grad.shape[:-1] + (kernel.shape[1],), jnp.float32)
    for tap in range(9):
        product = jnp.dot(grad, kernel[tap].T, preferred_element_type=jnp.float32)
        total = total + shifted(product, -(tap // 3 - 1) * spacing, -(tap % 3 - 1) * spacing)
    return total


def conv_kernel_back(field, grad, spacing):
    return jnp.stack(
        [
            jnp.einsum(
                "ihwc,ihwd->cd",
                shifted(field, (tap // 3 - 1) * spacing, (tap % 3 - 1) * spacing),
                grad,
                preferred_element_type=jnp.float32,
            )
            for tap in range(9)
        ]
    )


def silu_slope(value):
    gate = jax.nn.sigmoid(value)
    return gate * (1.0 + value * (1.0 - gate))


def channel_sums(values):
    return values.reshape(-1, values.shape[-1]).sum(0)


def masked_norm_apply(items, extra):
    sends = []
    for value, mask, norm in items:
        sends = sends + [
            channel_sums(value * mask),
            channel_sums(value * value * mask),
            jnp.sum(mask) * jnp.ones((1,), jnp.float32),
        ]
    totals = lax.psum(tuple(sends + extra), "batch")
    results = []
    for index, (value, mask, norm) in enumerate(items):
        count = totals[3 * index + 2]
        mean = totals[3 * index] / count
        spread = totals[3 * index + 1] / count - mean * mean
        scaling = lax.rsqrt(spread + 1e-05)
        normed = (value - mean) * scaling
        results.append((norm[0] * normed + norm[1], normed, scaling, count, mask, norm[0]))
    return (results, totals[3 * len(items) :])


def norm_backward(items):
    sends = []
    for grad, kept in items:
        sends = sends + [channel_sums(grad), channel_sums(grad * kept[1])]
    totals = lax.psum(tuple(sends), "batch")
    results = []
    for index, (grad, kept) in enumerate(items):
        outcome, normed, scaling, count, mask, gamma = kept
        first_sum, second_sum = (totals[2 * index], totals[2 * index + 1])
        inner = grad - mask * (first_sum + normed * second_sum) / count
        results.append(gamma * scaling * inner)
    return (results, sends, totals)


def bin_tables(extent, bins, length):
    which = jnp.arange(bins, dtype=jnp.int32)[None, :, None]
    place = jnp.arange(length, dtype=jnp.int32)[None, None, :]
    edge = extent[:, None, None]
    lower = which * edge // bins
    upper = ((which + 1) * edge + bins - 1) // bins
    member = ((place >= lower) & (place < upper)).astype(jnp.float32)
    target = jnp.minimum(place * bins // edge, bins - 1)
    chosen = (target == which).astype(jnp.float32)
    return (member, chosen)


def spread_bins(merged, branch, tables, images):
    joined = [merged]
    for group, bins in enumerate(BIN_COUNTS):
        rows_in, cols_in, rows_pick, cols_pick, cell_count = tables[group]
        piece = branch[:, BIN_STARTS[group] : BIN_STARTS[group] + bins * bins].reshape(
            images, bins, bins, -1
        )
        joined.append(
            jnp.einsum(
                "ikh,ilw,iklc->ihwc",
                rows_pick.astype(jnp.bfloat16),
                cols_pick.astype(jnp.bfloat16),
                piece,
                preferred_element_type=jnp.float32,
            ).astype(jnp.bfloat16)
        )
    return jnp.concatenate(joined, axis=-1)


def pick_bins(d_joined, width, tables, images):
    branch_width = (d_joined.shape[-1] - width) // 4
    d_up = []
    for group, bins in enumerate(BIN_COUNTS):
        rows_in, cols_in, rows_pick, cols_pick, cell_count = tables[group]
        piece = d_joined[..., width + group * branch_width : width + (group + 1) * branch_width]
        d_up.append(
            jnp.einsum("ikh,ilw,ihwc->iklc", rows_pick, cols_pick, piece).reshape(
                images, bins * bins, -1
            )
        )
    return (d_joined[..., :width], jnp.concatenate(d_up, axis=1))


def gather_channels(field):
    return lax.all_gather(field, "tensor", axis=3, tiled=True)


def scatter_channels(field):
    return lax.psum_scatter(
        field.astype(jnp.bfloat16), "tensor", scatter_dimension=3, tiled=True
    ).astype(jnp.float32)


def local(features, labels, valid, sizes, params, first_moment, squared_mean, average):
    splits = lax.axis_size("tensor")
    owners = lax.axis_size("batch")
    images = features.shape[0]
    gathered = lax.all_gather(params.astype(jnp.bfloat16), "batch", axis=0, tiled=True)
    (
        w_reduce,
        w_short,
        w_middle,
        w_expand,
        w_branch,
        w_unite,
        w_classes,
        w_aux,
        w_aux_classes,
        gains,
    ) = unflatten(gathered, splits)
    norms = [(piece[0], piece[1]) for piece in gain_pieces(gains.astype(jnp.float32), splits)]
    rows_at = jnp.arange(MAP, dtype=jnp.int32)
    inside = (rows_at[None, :, None] < sizes[:, 0][:, None, None]) & (
        rows_at[None, None, :] < sizes[:, 1][:, None, None]
    )
    inside = inside.astype(jnp.float32)[..., None]
    counted = inside * valid.astype(jnp.float32)[..., None]
    labels_hot = (labels[..., None] == jnp.arange(NCLS, dtype=jnp.int32)).astype(jnp.float32)
    class_local = channel_sums(labels_hot * counted)
    whole = lax.all_gather(features, "tensor", axis=3, tiled=True)
    pre_reduce = jnp.dot(whole, w_reduce, preferred_element_type=jnp.float32)
    pre_short = jnp.dot(whole, w_short, preferred_element_type=jnp.float32)
    pre_aux = conv_forward(whole, w_aux, 1)
    leading_part, label_tally = masked_norm_apply(
        [
            (pre_reduce, inside, norms[0]),
            (pre_short, inside, norms[1]),
            (pre_aux, inside, norms[9]),
        ],
        [class_local],
    )
    class_pixel_counts = label_tally[0]
    hidden_one = jax.nn.silu(leading_part[0][0]).astype(jnp.bfloat16)
    aux_act = jax.nn.silu(leading_part[2][0]).astype(jnp.bfloat16)
    hidden_full = gather_channels(hidden_one)
    pre_middle = conv_forward(hidden_full, w_middle, 4)
    second, unused = masked_norm_apply([(pre_middle, inside, norms[2])], [])
    hidden_two = jax.nn.silu(second[0][0]).astype(jnp.bfloat16)
    hidden_two_full = gather_channels(hidden_two)
    pre_expand = jnp.dot(hidden_two_full, w_expand, preferred_element_type=jnp.float32)
    third, unused = masked_norm_apply([(pre_expand, inside, norms[3])], [])
    summed = third[0][0] + leading_part[1][0]
    merged = jax.nn.silu(summed).astype(jnp.bfloat16)
    tables = []
    pooled_list = []
    partial_list = []
    for group, bins in enumerate(BIN_COUNTS):
        rows_in, rows_pick = bin_tables(sizes[:, 0], bins, MAP)
        cols_in, cols_pick = bin_tables(sizes[:, 1], bins, MAP)
        cell_count = (
            jnp.sum(rows_in, axis=2)[:, :, None, None] * jnp.sum(cols_in, axis=2)[:, None, :, None]
        )
        tables.append((rows_in, cols_in, rows_pick, cols_pick, cell_count))
        pooled = (
            jnp.einsum(
                "ikh,ilw,ihwc->iklc",
                rows_in.astype(jnp.bfloat16),
                cols_in.astype(jnp.bfloat16),
                merged,
                preferred_element_type=jnp.float32,
            )
            / cell_count
        )
        pooled = pooled.astype(jnp.bfloat16).reshape(images, bins * bins, -1)
        pooled_list.append(pooled)
        partial_list.append(
            jnp.einsum("ipc,cd->ipd", pooled, w_branch[group], preferred_element_type=jnp.float32)
        )
    branch_pre = lax.psum_scatter(
        jnp.concatenate(partial_list, axis=1).astype(jnp.bfloat16),
        "tensor",
        scatter_dimension=2,
        tiled=True,
    ).astype(jnp.float32)
    branch_items = []
    for group, bins in enumerate(BIN_COUNTS):
        piece = branch_pre[:, BIN_STARTS[group] : BIN_STARTS[group] + bins * bins]
        branch_items.append(
            (piece, jnp.ones(piece.shape[:-1] + (1,), jnp.float32), norms[4 + group])
        )
    fourth, unused = masked_norm_apply(branch_items, [])
    branch_act = jnp.concatenate([jax.nn.silu(kept[0]) for kept in fourth], axis=1).astype(
        jnp.bfloat16
    )
    merged_full, branch_full = (
        lax.all_gather(merged, "tensor", axis=3, tiled=True),
        lax.all_gather(branch_act, "tensor", axis=2, tiled=True),
    )
    joined = spread_bins(merged_full, branch_full, tables, images)
    pre_unite = conv_forward(joined, w_unite, 1)
    fifth, unused = masked_norm_apply([(pre_unite, inside, norms[8])], [])
    united = jax.nn.silu(fifth[0][0]).astype(jnp.bfloat16)
    logit_main, logit_aux = (
        lax.psum_scatter(
            jnp.dot(united, w_classes, preferred_element_type=jnp.float32).astype(jnp.bfloat16),
            "tensor",
            scatter_dimension=1,
            tiled=True,
        ).astype(jnp.float32),
        lax.psum_scatter(
            jnp.dot(aux_act, w_aux_classes, preferred_element_type=jnp.float32).astype(
                jnp.bfloat16
            ),
            "tensor",
            scatter_dimension=1,
            tiled=True,
        ).astype(jnp.float32),
    )
    total_valid = jnp.sum(class_pixel_counts)
    class_weight = total_valid / (NCLS * class_pixel_counts + total_valid)
    loss_weight = jnp.sum(class_pixel_counts * class_weight)
    cell_weight = jnp.sum(labels_hot * class_weight, axis=-1, keepdims=True) * counted
    band_rows = labels.shape[1] // splits
    band_start = lax.axis_index("tensor") * band_rows
    hot_band = lax.dynamic_slice_in_dim(labels_hot, band_start, band_rows, 1)
    weight_band = lax.dynamic_slice_in_dim(cell_weight, band_start, band_rows, 1)
    log_main = jax.nn.log_softmax(logit_main, axis=-1)
    log_aux = jax.nn.log_softmax(logit_aux, axis=-1)
    loss_cells = -jnp.sum(hot_band * (log_main + 0.4 * log_aux), axis=-1, keepdims=True)
    loss_local = jnp.sum(weight_band * loss_cells)
    band_main = (weight_band * (jnp.exp(log_main) - hot_band) / loss_weight).astype(jnp.bfloat16)
    band_aux = (0.4 * weight_band * (jnp.exp(log_aux) - hot_band) / loss_weight).astype(
        jnp.bfloat16
    )
    grad_main, grad_aux = (
        lax.all_gather(band_main, "tensor", axis=1, tiled=True),
        lax.all_gather(band_aux, "tensor", axis=1, tiled=True),
    )
    reduced = {}

    def settle(index, value):
        reduced[index] = value

    settle(6, jnp.einsum("ihwc,ihwk->ck", united, grad_main, preferred_element_type=jnp.float32))
    settle(8, jnp.einsum("ihwc,ihwk->ck", aux_act, grad_aux, preferred_element_type=jnp.float32))
    d_united = jnp.dot(grad_main, w_classes.T, preferred_element_type=jnp.float32) * silu_slope(
        fifth[0][0]
    )
    d_aux = jnp.dot(grad_aux, w_aux_classes.T, preferred_element_type=jnp.float32) * silu_slope(
        leading_part[2][0]
    )
    back_one, sums_one, totals_one = norm_backward([(d_united, fifth[0]), (d_aux, leading_part[2])])
    unite_shift_grad = totals_one[0]
    d_unite_pre = back_one[0].astype(jnp.bfloat16)
    d_aux_pre = back_one[1].astype(jnp.bfloat16)
    settle(5, conv_kernel_back(joined, d_unite_pre, 1))
    d_merged, d_branch = pick_bins(conv_input_back(d_unite_pre, w_unite, 1), C_OUT, tables, images)
    d_merged, d_branch = (
        lax.psum_scatter(
            d_merged.astype(jnp.bfloat16), "tensor", scatter_dimension=3, tiled=True
        ).astype(jnp.float32),
        lax.psum_scatter(
            d_branch.astype(jnp.bfloat16), "tensor", scatter_dimension=2, tiled=True
        ).astype(jnp.float32),
    )
    settle(7, conv_kernel_back(whole, d_aux_pre, 1))
    branch_back = []
    for group, bins in enumerate(BIN_COUNTS):
        piece = d_branch[:, BIN_STARTS[group] : BIN_STARTS[group] + bins * bins]
        branch_back.append((piece * silu_slope(fourth[group][0]), fourth[group]))
    back_two, sums_two, unused = norm_backward(branch_back)
    d_branch_pre = jnp.concatenate(back_two, axis=1).astype(jnp.bfloat16)
    d_branch_full = lax.all_gather(d_branch_pre, "tensor", axis=2, tiled=True)
    branch_grads = []
    for group, bins in enumerate(BIN_COUNTS):
        rows_in, cols_in, rows_pick, cols_pick, cell_count = tables[group]
        piece = d_branch_full[:, BIN_STARTS[group] : BIN_STARTS[group] + bins * bins]
        branch_grads.append(
            jnp.einsum("ipc,ipd->cd", pooled_list[group], piece, preferred_element_type=jnp.float32)
        )
        d_pooled = jnp.dot(piece, w_branch[group].T, preferred_element_type=jnp.float32).reshape(
            images, bins, bins, -1
        )
        d_merged = d_merged + jnp.einsum(
            "ikh,ilw,iklc->ihwc", rows_in, cols_in, d_pooled / cell_count
        )
    settle(4, jnp.stack(branch_grads))
    d_summed = d_merged * silu_slope(summed)
    back_three, sums_three, unused = norm_backward(
        [(d_summed, third[0]), (d_summed, leading_part[1])]
    )
    d_expand_pre = back_three[0].astype(jnp.bfloat16)
    d_short_pre = back_three[1].astype(jnp.bfloat16)
    settle(
        3,
        jnp.einsum(
            "ihwc,ihwd->cd", hidden_two_full, d_expand_pre, preferred_element_type=jnp.float32
        ),
    )
    settle(1, jnp.einsum("ihwc,ihwd->cd", whole, d_short_pre, preferred_element_type=jnp.float32))
    d_two = scatter_channels(jnp.dot(d_expand_pre, w_expand.T, preferred_element_type=jnp.float32))
    back_four, sums_four, unused = norm_backward([(d_two * silu_slope(second[0][0]), second[0])])
    d_middle_pre = back_four[0].astype(jnp.bfloat16)
    settle(2, conv_kernel_back(hidden_full, d_middle_pre, 4))
    d_one = scatter_channels(conv_input_back(d_middle_pre, w_middle, 4))
    back_five, sums_five, unused = norm_backward(
        [(d_one * silu_slope(leading_part[0][0]), leading_part[0])]
    )
    settle(
        0,
        jnp.einsum(
            "ihwc,ihwd->cd",
            whole,
            back_five[0].astype(jnp.bfloat16),
            preferred_element_type=jnp.float32,
        ),
    )
    beta_grads = (
        [sums_five[0], sums_three[2], sums_four[0], sums_three[0]]
        + [sums_two[2 * g] for g in range(4)]
        + [sums_one[0], sums_one[2]]
    )
    gamma_grads = (
        [sums_five[1], sums_three[3], sums_four[1], sums_three[1]]
        + [sums_two[2 * g + 1] for g in range(4)]
        + [sums_one[1], sums_one[3]]
    )
    settle(9, jnp.stack([jnp.concatenate(gamma_grads), jnp.concatenate(beta_grads)]))
    ordered = [reduced[index] for index in range(10)]
    grad_share = lax.psum_scatter(
        jnp.concatenate([part.reshape(owners, -1) for part in ordered], axis=1),
        "batch",
        scatter_dimension=0,
        tiled=True,
    )
    square_all, loss_sum = lax.psum(
        (jnp.sum(grad_share * grad_share), loss_local), ("batch", "tensor")
    )
    grad_norm = jnp.sqrt(square_all)
    clipped = grad_share * jnp.minimum(1.0, 0.05 / (grad_norm + 1e-06))
    new_first = 0.5 * first_moment + 0.5 * clipped
    new_second = 0.5 * squared_mean + 0.5 * clipped * clipped
    keep = 1.0 - 0.5**STEP
    new_params = params - 0.01 * (
        new_first / keep / (jnp.sqrt(new_second / keep) + 1e-08) + 0.01 * params
    )
    new_average = 0.999 * average + 0.001 * new_params
    return (
        new_params,
        new_first,
        new_second,
        new_average,
        new_params.astype(jnp.bfloat16),
        grad_norm,
        loss_sum,
        loss_weight,
        unite_shift_grad,
    )


CELLS = MAP * MAP
EDGE = 104
BATCH = "batch"
TENSOR = "tensor"
GROUP_ROWS = ((0, 1), (1, 5), (5, 14), (14, 50))
BINS = 64
BF = jnp.bfloat16
F32 = jnp.float32
MESH = pl.DeviceIdType.MESH
HALF = 4
OWNERS = 8
SPLITS = 4
MERGED = 4
SLOTS = 5


def scratch_plan():
    plan = dict(
        w_r=((1024, 128), BF),
        w_s=((1024, 512), BF),
        w_m=((4608, 128), BF),
        w_e=((512, 512), BF),
        w_b=((2048, 512), BF),
        w_u=((18432, 128), BF),
        w_own=((4608, 128), BF),
        w_a=((4608, 128), BF),
        w_pair=((1024, 640), BF),
        w_c=((128, 256), BF),
        w_ac=((64, 256), F32),
        gain_in=((OWNERS, 32, 128), F32),
        whole=((SPLITS, CELLS, 256), BF),
        ins=((CELLS, 128), F32),
        col=((CELLS, 128), F32),
        lab=((CELLS, 128), F32),
        table=((BINS, CELLS), F32),
        pool=((BINS, CELLS), BF),
        pick=((BINS, CELLS), BF),
        cells_in=((BINS, 128), F32),
        pad=((9, CELLS + 2 * EDGE, 128), F32),
        grad_pad=((CELLS + 2 * EDGE, 128), F32),
        pre_r=((CELLS, 128), F32),
        pre_s=((CELLS, 512), F32),
        pre_a=((CELLS, 128), F32),
        pre_m=((CELLS, 128), F32),
        pre_e=((CELLS, 512), F32),
        pre_u=((CELLS, 128), F32),
        act_a=((CELLS, 128), BF),
        h1=((SPLITS, CELLS, 128), BF),
        h2=((SPLITS, CELLS, 128), BF),
        joined=((SPLITS, CELLS, 512), BF),
        joined_t=((SPLITS, 512, CELLS), BF),
        pooled=((BINS, 512), BF),
        pool_half=((2, BINS, 256), BF),
        pool_all=((OWNERS, BINS, 256), BF),
        d_bp_all=((OWNERS, SPLITS, BINS, 128), BF),
        part_b=((SPLITS, BINS, 128), BF),
        recv_b=((SPLITS, BINS, 128), BF),
        all_b=((OWNERS, BINS, 128), BF),
        act_b=((SPLITS, OWNERS * BINS, 128), BF),
        zsum=((2, OWNERS * BINS, 128), F32),
        z_send=((OWNERS, 2, BINS, 128), BF),
        z_recv=((OWNERS, 2, BINS, 128), BF),
        united=((CELLS, 128), BF),
        logit_send=((CELLS, 512), BF),
        logit_recv=((SPLITS, 144, 512), BF),
        slope_in=((SPLITS, 144, 512), BF),
        d_f=((CELLS, 128), F32),
        d_f2=((CELLS, 128), F32),
        cat_u=((CELLS, 1152), BF),
        cat_a=((CELLS, 640), BF),
        dz_send=((9, BINS, 128), BF),
        dz_recv=((OWNERS, 2, BINS, 128), BF),
        d_act_send=((SPLITS, OWNERS * BINS, 128), BF),
        d_act_recv=((SPLITS, OWNERS * BINS, 128), BF),
        d_img_send=((OWNERS, BINS, 128), BF),
        d_img_recv=((OWNERS, BINS, 128), BF),
        d_bp=((SPLITS, BINS, 128), BF),
        dm_near=((2, CELLS, 512), BF),
        dm_far=((CELLS, 512), BF),
        d_sum=((CELLS, 512), F32),
        d_e=((CELLS, 512), BF),
        d_s=((CELLS, 512), BF),
        dh_send=((SPLITS, CELLS, 128), BF),
        dh_recv=((2, SPLITS, CELLS, 128), BF),
        d_low=((CELLS, 128), BF),
        end_t=((SPLITS, 8, 128), F32),
    )
    for name, rows in SYNCS.items():
        plan["sync_" + name] = ((OWNERS, rows, 128), F32)
    for name, (rows, lanes, kind) in PARTS.items():
        plan["first_" + name] = ((HALF, rows, lanes), kind)
        plan["second_" + name] = ((HALF - 1, rows, lanes), kind)
    plan["first_u"] = ((HALF, SLOTS, 512, 128), BF)
    plan["second_u"] = ((HALF - 1, SLOTS, 512, 128), BF)
    return plan


SYNCS = dict(one=8, two=8, three=16, five=8, aux=8, b1=8, b3=8, b4=16, b5=8, b6=8, end=8)
PARTS = dict(
    r=(128, 128, BF),
    s=(128, 512, BF),
    m=(576, 128, BF),
    e=(64, 512, BF),
    a=(576, 128, BF),
    c=(16, 256, BF),
    ac=(8, 256, F32),
)
SEMAPHORES = 1100


class Refs:
    pass


def fold(value):
    return value.reshape(-1, 8, value.shape[-1]).sum(0)


def total(value):
    return jnp.sum(value, axis=0, keepdims=True)


def wide(value, times):
    return jnp.concatenate([value] * times, axis=1)


def dot(left, right):
    return jnp.dot(left, right, preferred_element_type=F32)


def dot_nt(left, right):
    return lax.dot_general(left, right, (((1,), (1,)), ((), ())), preferred_element_type=F32)


def dot_tn(left, right):
    return lax.dot_general(left, right, (((0,), (0,)), ((), ())), preferred_element_type=F32)


def loop(count, body):
    def step(k, carry):
        body(k)
        return carry

    lax.fori_loop(0, count, step, 0)


def rows_at(k, block):
    return pl.ds(pl.multiple_of(k * block, block), block)


def step_kernel(names, *refs):
    (
        sizes, lab_in, feat, gain_own, p_r, p_s, p_m, p_e, p_b, p_u, p_a, p_c, p_ac,
        o_flat, o_a, o_c, o_ac, o_gain, o_misc,
    ) = refs[:19]
    v = Refs()
    for name, ref in zip(names, refs[19:]):
        setattr(v, name, ref)
    sems = refs[-1]
    o_u = o_flat.at[2496:7104, :]
    me = lax.axis_index(BATCH)
    t = lax.axis_index(TENSOR)
    partner = me + 1 - 2 * lax.rem(me, 2)
    t_core = t + 1 - 2 * lax.rem(t, 2)
    t_x = lax.rem(t + 2, SPLITS)
    t_diag = lax.rem(t_core + 2, SPLITS)
    taken = [0]

    def take(count):
        start = taken[0]
        taken[0] = start + count
        assert taken[0] <= SEMAPHORES
        return start

    def far_peer(base, step):
        return lax.rem(base + 2 * step, OWNERS)

    def remote(src, dst, send, recv, device):
        return pltpu.make_async_remote_copy(
            src_ref=src,
            dst_ref=dst,
            send_sem=sems.at[send],
            recv_sem=sems.at[recv],
            device_id=device,
            device_id_type=MESH,
        )

    late = []

    v.pool_all[...] = jnp.zeros((OWNERS, BINS, 256), BF)
    v.d_bp_all[...] = jnp.zeros((OWNERS, SPLITS, BINS, 128), BF)
    barrier = pltpu.get_barrier_semaphore()
    for k in range(1, OWNERS):
        pl.semaphore_signal(
            barrier, inc=1, device_id={BATCH: lax.rem(me + k, OWNERS)}, device_id_type=MESH
        )
    for k in range(1, SPLITS):
        pl.semaphore_signal(
            barrier, inc=1, device_id={TENSOR: lax.rem(t + k, SPLITS)}, device_id_type=MESH
        )
    pl.semaphore_wait(barrier, OWNERS + SPLITS - 2)

    class Gather:
        def __init__(self, piece, full, rows, skip=0, step=None):
            self.piece, self.full, self.rows = piece, full, rows
            self.skip, self.part = skip, step or rows
            if step:
                self.piece = piece.at[skip : skip + step, :]
            self.near_s, self.far_s, self.pass_s = take(1), take(HALF), take(HALF)
            self.recv, self.keep = take(OWNERS), take(1)

        def at(self, owner):
            if self.rows is None:
                return self.full.at[owner]
            start = pl.multiple_of(owner * self.rows + self.skip, self.part)
            return self.full.at[pl.ds(start, self.part), :]

        def local(self):
            return pltpu.make_async_copy(self.piece, self.at(me), sems.at[self.keep])

        def near(self):
            return remote(
                self.piece, self.at(me), self.near_s, self.recv + me, {BATCH: partner}
            )

        def far(self, step):
            return remote(
                self.piece,
                self.at(me),
                self.far_s + step,
                self.recv + me,
                {BATCH: far_peer(me, step)},
            )

        def passed(self, step, base):
            source = far_peer(base, step)
            return remote(
                self.at(source),
                self.at(source),
                self.pass_s + step,
                self.recv + source,
                {BATCH: partner},
            )

        def start_far(self):
            self.local().start()
            for step in range(1, HALF):
                self.far(step).start()

        def start_near(self):
            self.near().start()

        def forward(self):
            for step in range(1, HALF):
                self.passed(step, me).wait_recv()
                self.passed(step, me).start()

        def finish(self):
            for step in range(HALF):
                self.passed(step, partner).wait_recv()
            self.local().wait()
            self.near().wait_send()
            for step in range(1, HALF):
                self.far(step).wait_send()

        def drain(self):
            for step in range(1, HALF):
                self.passed(step, me).wait_send()

    g_gain = Gather(gain_own, v.gain_in, None)
    g_r = Gather(p_r, v.w_r, 128)
    g_s = Gather(p_s, v.w_s, 128)
    g_a = Gather(p_a, v.w_a, 576)
    g_m = Gather(p_m, v.w_m, 576)
    g_e = Gather(p_e, v.w_e, 64)
    g_b0 = Gather(p_b, v.w_b, 256, 0, 128)
    g_b1 = Gather(p_b, v.w_b, 256, 128, 128)
    g_c = Gather(p_c, v.w_c, 16)
    g_ac = Gather(p_ac, v.w_ac, 8)

    def block_of(owner, slot):
        return 8 if slot == SLOTS - 1 else lax.rem(slot - owner + 8, 8)

    def merged_rows(owner, slot):
        block = owner * 9 + block_of(owner, slot)
        index = lax.div(block, 8) * MERGED + lax.rem(block, 8)
        return pl.ds(pl.multiple_of(index * 512, 512), 512)

    def has(owner, slot, body):
        if slot == SLOTS - 1:
            pl.when(owner < MERGED)(body)
        else:
            body()

    class GatherUnite:
        def __init__(self):
            self.near_s, self.far_s, self.pass_s = (
                take(SLOTS),
                take(SLOTS * HALF),
                take(SLOTS * HALF),
            )
            self.recv, self.keep, self.keep_all = take(SLOTS * OWNERS), take(SLOTS), take(1)

        def source(self, slot):
            return p_u.at[rows_at(block_of(me, slot), 512), :]

        def full(self, owner, slot):
            return v.w_u.at[merged_rows(owner, slot), :]

        def local(self, slot):
            return pltpu.make_async_copy(
                self.source(slot), self.full(me, slot), sems.at[self.keep + slot]
            )

        def whole(self):
            return pltpu.make_async_copy(p_u, v.w_own, sems.at[self.keep_all])

        def near(self, slot):
            return remote(
                self.source(slot),
                self.full(me, slot),
                self.near_s + slot,
                self.recv + me * SLOTS + slot,
                {BATCH: partner},
            )

        def far(self, step, slot):
            return remote(
                self.source(slot),
                self.full(me, slot),
                self.far_s + step * SLOTS + slot,
                self.recv + me * SLOTS + slot,
                {BATCH: far_peer(me, step)},
            )

        def passed(self, step, slot, base):
            source = far_peer(base, step)
            return remote(
                self.full(source, slot),
                self.full(source, slot),
                self.pass_s + step * SLOTS + slot,
                self.recv + source * SLOTS + slot,
                {BATCH: partner},
            )

        def start_far(self, slot):
            def go():
                self.local(slot).start()
                for step in range(1, HALF):
                    self.far(step, slot).start()

            has(me, slot, go)

        def start_near(self, slot):
            has(me, slot, lambda: self.near(slot).start())

        def forward(self, slot):
            for step in range(1, HALF):

                def go(step=step):
                    self.passed(step, slot, me).wait_recv()
                    self.passed(step, slot, me).start()

                has(far_peer(me, step), slot, go)

        def finish(self):
            for slot in range(SLOTS):
                for step in range(HALF):
                    has(
                        far_peer(partner, step),
                        slot,
                        lambda step=step, slot=slot: self.passed(step, slot, partner).wait_recv(),
                    )

                def end(slot=slot):
                    self.local(slot).wait()
                    self.near(slot).wait_send()
                    for step in range(1, HALF):
                        self.far(step, slot).wait_send()

                has(me, slot, end)

        def drain(self):
            for slot in range(SLOTS):
                for step in range(1, HALF):
                    has(
                        far_peer(me, step),
                        slot,
                        lambda step=step, slot=slot: self.passed(step, slot, me).wait_send(),
                    )

    g_u = GatherUnite()

    class Sync:
        def __init__(self, buf):
            self.buf = buf
            self.send, self.recv = take(OWNERS), take(OWNERS)

        def copy(self, k, slot):
            return remote(
                self.buf.at[slot],
                self.buf.at[slot],
                self.send + k,
                self.recv + slot,
                {BATCH: lax.rem(me + k, OWNERS)},
            )

        def start(self, rows):
            for index, row in enumerate(rows):
                self.buf[me, index : index + 1, :] = row
            for index in range(len(rows), self.buf.shape[1]):
                self.buf[me, index : index + 1, :] = jnp.zeros((1, 128), F32)
            for k in range(1, OWNERS):
                self.copy(k, me).start()

        def wait(self):
            for k in range(1, OWNERS):
                self.copy(k, lax.rem(me + k, OWNERS)).wait_recv()
            for k in range(1, OWNERS):
                self.copy(k, me).wait_send()
            value = self.buf[0]
            for slot in range(1, OWNERS):
                value = value + self.buf[slot]
            return value

    class ToGroup:
        def __init__(self, part, into):
            self.part, self.into = part, into
            self.send, self.recv = take(OWNERS), take(OWNERS)

        def each(self, k, owner, slot, act):
            for rows, fits_ in ((16, owner < 6), (BINS, owner >= 6)):

                def go(rows=rows):
                    act(
                        remote(
                            self.part(owner, rows),
                            self.into(slot, rows),
                            self.send + k,
                            self.recv + slot,
                            {BATCH: lax.rem(me + k, OWNERS)},
                        )
                    )

                pl.when(fits_)(go)

        def start(self):
            for k in range(1, OWNERS):
                self.each(k, lax.rem(me + k, OWNERS), me, lambda c: c.start())

        def wait(self):
            for k in range(1, OWNERS):
                self.each(k, me, lax.rem(me + k, OWNERS), lambda c: c.wait_recv())
            for k in range(1, OWNERS):
                self.each(k, lax.rem(me + k, OWNERS), me, lambda c: c.wait_send())

    class Spread:

        def __init__(self, buf):
            self.buf = buf
            self.send, self.recv = take(SPLITS), take(SPLITS)

        def copy(self, k, slot):
            return remote(
                self.buf.at[slot],
                self.buf.at[slot],
                self.send + k,
                self.recv + slot,
                {TENSOR: lax.rem(t + k, SPLITS)},
            )

        def start(self):
            for k in range(1, SPLITS):
                self.copy(k, t).start()

        def wait(self):
            for k in range(1, SPLITS):
                self.copy(k, lax.rem(t + k, SPLITS)).wait_recv()
            for k in range(1, SPLITS):
                self.copy(k, t).wait_send()

    class Exchange:

        def __init__(self, axis, count, part, into):
            self.axis, self.count, self.part, self.into = axis, count, part, into
            self.mine = me if axis == BATCH else t
            self.send, self.recv = take(count), take(count)

        def copy(self, k, slot):
            other = lax.rem(self.mine + k, self.count)
            return remote(
                self.part(other),
                self.into(slot),
                self.send + k,
                self.recv + slot,
                {self.axis: other},
            )

        def start(self):
            for k in range(1, self.count):
                self.copy(k, self.mine).start()

        def wait(self):
            for k in range(1, self.count):
                self.copy(k, lax.rem(self.mine + k, self.count)).wait_recv()
            for k in range(1, self.count):
                self.copy(k, self.mine).wait_send()

    feat_keep = take(1)
    feat_local = pltpu.make_async_copy(feat, v.whole.at[t], sems.at[feat_keep])
    feat_spread = Exchange(TENSOR, SPLITS, lambda other: feat, lambda slot: v.whole.at[slot])
    for item in (g_gain, g_r):
        item.start_far()
        item.start_near()
    feat_local.start()
    feat_spread.start()
    for item in (g_m, g_e):
        item.start_far()
        item.start_near()

    high, across = sizes[0, 0], sizes[0, 1]
    place = lax.broadcasted_iota(jnp.int32, (CELLS, 128), 0).astype(F32)
    row_of = jnp.floor((place + 0.5) / MAP)
    col_of = place - MAP * row_of
    within = (row_of < high.astype(F32)) & (col_of < across.astype(F32))
    v.ins[...] = jnp.where(within, 1.0, 0.0)
    v.col[...] = col_of
    v.lab[...] = jnp.where(within, lab_in[...], -1.0)
    v.table[...] = jnp.zeros((BINS, CELLS), F32)
    lane_place = lax.broadcasted_iota(jnp.int32, (1, CELLS), 1).astype(F32)
    lane_row = jnp.floor((lane_place + 0.5) / MAP)
    lane_col = lane_place - MAP * lane_row

    def ranges(extent, bins, where):
        inside, chosen, counts = [], [], []
        for k in range(bins):
            low = lax.div(k * extent, bins)
            top = lax.div((k + 1) * extent + (bins - 1), bins)
            member = (where >= low.astype(F32)) & (where < top.astype(F32))
            inside.append(jnp.where(member, 1.0, 0.0))
            picked = where * bins >= (k * extent).astype(F32)
            if k < bins - 1:
                picked = picked & (where * bins < ((k + 1) * extent).astype(F32))
            chosen.append(jnp.where(picked, 1.0, 0.0))
            counts.append(top - low)
        return inside, chosen, counts

    picks = []
    v.cells_in[...] = jnp.ones((BINS, 128), F32)
    for group, bins in enumerate(BIN_COUNTS):
        r_in, r_pick, r_count = ranges(high, bins, lane_row)
        c_in, c_pick, c_count = ranges(across, bins, lane_col)
        for a in range(bins):
            for b in range(bins):
                spot = BIN_STARTS[group] + a * bins + b
                v.table[spot : spot + 1, :] = r_in[a] * c_in[b]
                v.cells_in[spot : spot + 1, :] = jnp.full(
                    (1, 128), (r_count[a] * c_count[b]).astype(F32)
                )
                picks.append((spot, r_pick[a] * c_pick[b]))
    v.pool[...] = v.table[...].astype(BF)
    for spot, value in picks:
        v.table[spot : spot + 1, :] = value
    v.pick[...] = v.table[...].astype(BF)
    zeros_edge = jnp.zeros((EDGE, 128), F32)
    for tap in range(9):
        v.pad[tap, 0:EDGE, :] = zeros_edge
        v.pad[tap, EDGE + CELLS :, :] = zeros_edge
    v.grad_pad[0:EDGE, :] = zeros_edge
    v.grad_pad[EDGE + CELLS :, :] = zeros_edge
    lanes = lax.broadcasted_iota(jnp.int32, (1, 256), 1).astype(F32)
    counts = jnp.zeros((8, 256), F32)
    for k in range(0, CELLS, 96):
        counts = counts + fold(
            jnp.where(wide(v.lab[k : k + 96, :], 2) == lanes, 1.0, 0.0)
        )
    class_local = total(counts)
    cells_local = jnp.full((1, 128), (high * across).astype(F32))
    left_half = lax.broadcasted_iota(jnp.int32, (64, 128), 1) < 64

    for item in (g_gain, g_r):
        item.forward()
    for item in (g_gain, g_r):
        item.finish()
    feat_local.wait()
    feat_spread.wait()
    gains = v.gain_in[0]
    for slot in range(1, OWNERS):
        gains = gains + v.gain_in[slot]

    def gamma(row, width=1):
        return jnp.concatenate([gains[row + k : row + k + 1] for k in range(width)], axis=1)

    def beta(row, width=1):
        return gamma(16 + row, width)

    def whole_feat():
        return jnp.concatenate([v.whole[k] for k in range(SPLITS)], axis=1)

    v.pre_r[...] = dot(whole_feat(), v.w_r[...])
    def offset(tap, spacing):
        return ((tap // 3 - 1) * MAP + (tap % 3 - 1)) * spacing

    def col_mask(at, right):
        where = v.col[at, :] + float(right)
        return jnp.where((where >= 0.0) & (where < float(MAP)), 1.0, 0.0)

    BLOCK = 72

    def shift_sum(taps, spacing, at, slot_of):
        out = None
        for b in (-1, 0, 1):
            part = None
            for tap in taps:
                if tap % 3 - 1 != b:
                    continue
                start = EDGE + at + offset(tap, spacing)
                value = v.pad[slot_of(tap), start : start + BLOCK, :]
                part = value if part is None else part + value
            if part is None:
                continue
            if b:
                part = part * col_mask(slice(at, at + BLOCK), b * spacing)
            out = part if out is None else out + part
        return out

    def masked_sums(ref):
        width = ref.shape[1]

        def step(k, carry):
            at = rows_at(k, 96)
            value = ref[at, :]
            kept = value * (v.ins[at, :] if width == 128 else wide(v.ins[at, :], width // 128))
            return (carry[0] + fold(kept), carry[1] + fold(kept * value))

        zero = jnp.zeros((8, width), F32)
        sums = lax.fori_loop(0, 6, step, (zero, zero))
        return total(sums[0]), total(sums[1])

    def split_rows(value):
        return [value[:, k : k + 128] for k in range(0, value.shape[1], 128)]

    def join_rows(value, row, count):
        return jnp.concatenate([value[row + k : row + k + 1] for k in range(count)], axis=1)

    def moments(first, second, count):
        mean = first / count
        return mean, lax.rsqrt(second / count - mean * mean + 1e-05)

    sync = Sync(v.sync_one)
    r1, r2 = masked_sums(v.pre_r)
    sync.start([r1, r2, cells_local] + split_rows(class_local))
    g_m.forward()
    g_e.forward()
    g_s.start_far()
    g_u.whole().start()
    sums = sync.wait()
    count = sums[2:3]
    count4 = wide(count, 4)
    norm_r = moments(sums[0:1], sums[1:2], count)
    class_count = join_rows(sums, 3, 2)

    def normed(ref, at, norm):
        return (ref[at, :] - norm[0]) * norm[1]

    spread_1 = Spread(v.h1)

    def make_h1(k):
        at = rows_at(k, 96)
        v.h1[t, at, :] = jax.nn.silu(gamma(0) * normed(v.pre_r, at, norm_r) + beta(0)).astype(BF)

    loop(6, make_h1)
    spread_1.start()
    g_s.start_near()
    g_b0.start_far()
    g_m.finish()
    spread_1.wait()

    def full_h(ref):
        return jnp.concatenate([ref[k] for k in range(SPLITS)], axis=1)

    def middle(tap):
        v.pad[tap, EDGE : EDGE + CELLS, :] = dot(full_h(v.h1), v.w_m[rows_at(tap, 512), :])

    loop(9, middle)
    for at in range(0, CELLS, BLOCK):
        v.pre_m[at : at + BLOCK, :] = shift_sum(range(9), 4, at, lambda tap: tap)
    sync = Sync(v.sync_two)
    sync.start(list(masked_sums(v.pre_m)))
    g_s.forward()
    g_b0.start_near()
    g_b1.start_far()
    sums = sync.wait()
    norm_m = moments(sums[0:1], sums[1:2], count)
    spread_2 = Spread(v.h2)

    def make_h2(k):
        at = rows_at(k, 96)
        v.h2[t, at, :] = jax.nn.silu(gamma(5) * normed(v.pre_m, at, norm_m) + beta(5)).astype(BF)

    loop(6, make_h2)
    spread_2.start()
    g_b0.forward()
    g_b1.start_near()
    g_u.start_far(0)
    g_e.finish()
    g_s.finish()
    for k in range(0, 512, 256):
        v.pre_s[:, k : k + 256] = dot(whole_feat(), v.w_s[:, k : k + 256])
    s1, s2 = masked_sums(v.pre_s)
    spread_2.wait()
    for k in range(0, 512, 256):
        v.pre_e[:, k : k + 256] = dot(full_h(v.h2), v.w_e[:, k : k + 256])
    sync = Sync(v.sync_three)
    e1, e2 = masked_sums(v.pre_e)
    sync.start(split_rows(e1) + split_rows(e2) + split_rows(s1) + split_rows(s2))
    g_b1.forward()
    g_u.start_near(0)
    g_u.start_far(1)
    for item in (g_c, g_ac):
        item.start_far()
        item.start_near()
    sums = sync.wait()
    norm_e = moments(join_rows(sums, 0, 4), join_rows(sums, 4, 4), count4)
    norm_s = moments(join_rows(sums, 8, 4), join_rows(sums, 12, 4), count4)

    def summed(at):
        return (
            gamma(6, 4) * normed(v.pre_e, at, norm_e)
            + beta(6, 4)
            + gamma(1, 4) * normed(v.pre_s, at, norm_s)
            + beta(1, 4)
        )

    def make_merged(k):
        at = rows_at(k, 48)
        v.joined[t, at, :] = jax.nn.silu(summed(at)).astype(BF)

    loop(12, make_merged)

    j_send, j_recv = take(3), take(SPLITS)

    def joined_copy(k, slot, device):
        return remote(
            v.joined.at[slot], v.joined.at[slot], j_send + k, j_recv + slot, {TENSOR: device}
        )

    joined_copy(0, t, t_x).start()
    joined_copy(1, t, t_core).start()

    pool_move = ToGroup(
        lambda owner, rows: v.pool_half.at[lax.rem(owner, 2), 0:rows, :],
        lambda slot, rows: v.pool_all.at[slot, 0:rows, :],
    )
    bin_row = lax.broadcasted_iota(jnp.int32, (BINS, 1), 0)

    def group_mask(group, shape=None):
        low, top = GROUP_ROWS[group]
        kept = jnp.where((bin_row >= low) & (bin_row < top), 1.0, 0.0)
        return kept if shape is None else jnp.broadcast_to(kept, shape)

    cells_in = wide(v.cells_in[...], 4)
    pooled = dot(v.pool[...], v.joined[t]) / cells_in
    v.pooled[...] = pooled.astype(BF)
    for k in range(2):
        v.pool_half[k] = v.pooled[:, k * 256 : k * 256 + 256]
    v.pool_all[me] = v.pool_half[lax.rem(me, 2)]
    g_b0.finish()
    g_b1.finish()
    part = jnp.zeros((BINS, 512), F32)
    for group in range(4):
        rows = (v.pooled[...].astype(F32) * group_mask(group)).astype(BF)
        part = part + dot(rows, v.w_b[group * 512 : group * 512 + 512, :])
    for k in range(SPLITS):
        v.part_b[k] = part[:, k * 128 : k * 128 + 128].astype(BF)
    v.recv_b[t] = v.part_b[t]
    ex = Exchange(TENSOR, SPLITS, lambda o: v.part_b.at[o], lambda s: v.recv_b.at[s])
    ex.start()
    g_u.forward(0)
    g_u.start_near(1)
    g_u.start_far(2)
    joined_copy(0, t_x, t_x).wait_recv()
    joined_copy(2, t_x, t_core).start()
    ex.wait()
    own_b = v.recv_b[0].astype(F32)
    for k in range(1, SPLITS):
        own_b = own_b + v.recv_b[k].astype(F32)
    v.all_b[me] = own_b.astype(BF)
    ex = Exchange(BATCH, OWNERS, lambda o: v.all_b.at[me], lambda s: v.all_b.at[s])
    ex.start()
    g_u.forward(1)
    g_u.start_near(2)
    g_u.start_far(3)
    ex.wait()
    all_b = [v.all_b[k].astype(F32) for k in range(OWNERS)]
    sum_b, square_b = all_b[0], all_b[0] * all_b[0]
    for k in range(1, OWNERS):
        sum_b = sum_b + all_b[k]
        square_b = square_b + all_b[k] * all_b[k]
    mean_b = jnp.zeros((BINS, 128), F32)
    scale_b = jnp.zeros((BINS, 128), F32)
    gamma_b = jnp.zeros((BINS, 128), F32)
    beta_b = jnp.zeros((BINS, 128), F32)
    count_b = jnp.zeros((BINS, 1), F32)
    for group, bins in enumerate(BIN_COUNTS):
        kept = group_mask(group)
        size = float(OWNERS * bins * bins)
        mean, scaling = moments(total(sum_b * kept), total(square_b * kept), size)
        mean_b = mean_b + kept * mean
        scale_b = scale_b + kept * scaling
        gamma_b = gamma_b + kept * gamma(10 + group)
        beta_b = beta_b + kept * beta(10 + group)
        count_b = count_b + kept / size
    spread_b = Spread(v.act_b)
    for k in range(OWNERS):
        out = gamma_b * ((all_b[k] - mean_b) * scale_b) + beta_b
        v.act_b[t, k * BINS : k * BINS + BINS, :] = jax.nn.silu(out).astype(BF)
    spread_b.start()
    g_u.forward(2)
    g_u.start_near(3)
    g_u.start_far(4)
    spread_b.wait()
    g_u.whole().wait()
    row_512 = lax.broadcasted_iota(jnp.int32, (OWNERS * BINS, 1), 0) & (BINS - 1)
    group_id = jnp.where(
        row_512 < 1, 0, jnp.where(row_512 < 5, 1, jnp.where(row_512 < 14, 2, jnp.where(row_512 < 50, 3, 9)))
    )

    def full_act():
        return jnp.concatenate([v.act_b[k] for k in range(SPLITS)], axis=1)

    v.zsum[...] = jnp.zeros((2, OWNERS * BINS, 128), F32)

    def own_branch(j, body):
        chunk = lax.rem(me + j, 8)
        pl.when(chunk >= MERGED)(lambda: body(chunk - MERGED, lax.div(me + j, 8)))

    def make_z(j):
        def body(group, side):
            kept = jnp.where(group_id == group, 1.0, 0.0)
            rows = (full_act().astype(F32) * kept).astype(BF)
            v.zsum[side] = v.zsum[side] + dot(rows, v.w_own[rows_at(j, 512), :])

        own_branch(j, body)

    loop(9, make_z)
    for k in range(OWNERS):
        for side in range(2):
            v.z_send[k, side] = v.zsum[side, k * BINS : k * BINS + BINS, :].astype(BF)
    v.z_recv[me] = v.z_send[me]
    ex = Exchange(BATCH, OWNERS, lambda o: v.z_send.at[o], lambda s: v.z_recv.at[s])
    ex.start()
    g_u.forward(3)
    g_u.start_near(4)
    g_a.start_far()
    joined_copy(1, t_core, t_core).wait_recv()
    joined_copy(2, t_diag, t_core).wait_recv()
    for k in range(SPLITS):
        v.joined_t[k] = v.joined[k].T
    g_u.forward(4)
    g_a.start_near()
    g_c.forward()
    g_ac.forward()
    ex.wait()
    g_u.finish()
    g_a.forward()

    pick2 = jnp.concatenate([v.pick[...], v.pick[...]], axis=0)

    def tap_z(tap):
        if tap == 0:
            return v.z_recv[0, 0].astype(F32)
        if tap == 8:
            return v.z_recv[7, 1].astype(F32)
        return v.z_recv[tap, 0].astype(F32) + v.z_recv[tap - 1, 1].astype(F32)

    def full_joined():
        return jnp.concatenate([v.joined[k] for k in range(SPLITS)], axis=1)

    def w_tap(tap):
        return v.w_u[rows_at(tap, 2048), :]

    def unite_pair(p):
        value = dot(full_joined(), jnp.concatenate([w_tap(2 * p), w_tap(2 * p + 1)], axis=1))
        v.pad[2 * p, EDGE : EDGE + CELLS, :] = value[:, :128]
        v.pad[2 * p + 1, EDGE : EDGE + CELLS, :] = value[:, 128:]

    loop(4, unite_pair)
    v.pad[8, EDGE : EDGE + CELLS, :] = dot(full_joined(), w_tap(8))
    for tap in range(9):
        z = tap_z(tap)
        high_z = z.astype(BF)
        low_z = (z - high_z.astype(F32)).astype(BF)
        v.pad[tap, EDGE : EDGE + CELLS, :] = v.pad[tap, EDGE : EDGE + CELLS, :] + dot_tn(
            pick2, jnp.concatenate([high_z, low_z], axis=0)
        )
    for at in range(0, CELLS, BLOCK):
        v.pre_u[at : at + BLOCK, :] = shift_sum(range(9), 1, at, lambda tap: tap)
    sync = Sync(v.sync_five)
    sync.start(list(masked_sums(v.pre_u)))
    pool_move.start()
    for item in (g_a, g_c, g_ac):
        item.finish()

    def unpack(chunk):
        for pair in range(5):
            even = v.w_a[rows_at(2 * pair * 8 + chunk, 64), :].astype(F32)
            if pair < 4:
                odd = v.w_a[rows_at((2 * pair + 1) * 8 + chunk, 64), :].astype(F32)
            else:
                odd = jnp.zeros((64, 128), F32)
            low = jnp.where(left_half, even, pltpu.roll(odd, 64, 1))
            top = jnp.where(left_half, pltpu.roll(even, 64, 1), odd)
            v.w_pair[rows_at(2 * chunk, 64), pair * 128 : pair * 128 + 128] = low.astype(BF)
            v.w_pair[rows_at(2 * chunk + 1, 64), pair * 128 : pair * 128 + 128] = top.astype(BF)

    loop(8, unpack)

    for pair in (0, 2):
        value = dot(whole_feat(), v.w_pair[:, pair * 128 : pair * 128 + 256])
        v.pad[pair, EDGE : EDGE + CELLS, :] = value[:, :128]
        v.pad[pair + 1, EDGE : EDGE + CELLS, :] = value[:, 128:]
    v.pad[4, EDGE : EDGE + CELLS, :] = dot(whole_feat(), v.w_pair[:, 512:640])

    left_wide = lax.broadcasted_iota(jnp.int32, (BLOCK, 128), 1) < 64
    for at in range(0, CELLS, BLOCK):
        even = shift_sum((0, 2, 4, 6, 8), 1, at, lambda tap: tap // 2)
        odd = shift_sum((1, 3, 5, 7), 1, at, lambda tap: tap // 2)
        v.pre_a[at : at + BLOCK, :] = jnp.where(left_wide, even + pltpu.roll(odd, 64, 1), 0.0)

    sync_a = Sync(v.sync_aux)
    sync_a.start(list(masked_sums(v.pre_a)))
    for item in (g_gain, g_r, g_s, g_a, g_m, g_e, g_b0, g_b1, g_c, g_ac, g_u):
        item.drain()
    joined_copy(0, t, t_x).wait_send()
    joined_copy(1, t, t_core).wait_send()
    joined_copy(2, t_x, t_core).wait_send()
    w_ac = jnp.concatenate([v.w_ac[...], jnp.zeros((64, 256), F32)], axis=0).astype(BF)
    sums = sync.wait()
    norm_u = moments(sums[0:1], sums[1:2], count)

    def make_u(k):
        at = rows_at(k, 96)
        v.united[at, :] = jax.nn.silu(gamma(14) * normed(v.pre_u, at, norm_u) + beta(14)).astype(BF)

    loop(6, make_u)
    v.logit_send[:, :256] = dot(v.united[...], v.w_c[...]).astype(BF)
    sums = sync_a.wait()
    norm_a = moments(sums[0:1], sums[1:2], count)

    def make_a(k):
        at = rows_at(k, 96)
        v.act_a[at, :] = jax.nn.silu(gamma(15) * normed(v.pre_a, at, norm_a) + beta(15)).astype(BF)

    loop(6, make_a)

    v.logit_send[:, 256:] = dot(v.act_a[...], w_ac).astype(BF)
    ex = Exchange(
        TENSOR,
        SPLITS,
        lambda o: v.logit_send.at[rows_at(o, 144), :],
        lambda s: v.logit_recv.at[s],
    )
    ex.start()
    v.logit_recv[t] = v.logit_send[rows_at(t, 144), :]
    total_valid = jnp.sum(class_count, axis=1, keepdims=True)
    class_weight = total_valid / (NCLS * class_count + total_valid)
    loss_weight = jnp.sum(class_count * class_weight, axis=1, keepdims=True)
    class_weight = jnp.where(lanes < float(NCLS), class_weight, 0.0)
    hot = jnp.where(wide(v.lab[rows_at(t, 144), :], 2) == lanes, 1.0, 0.0)
    cell_weight = jnp.sum(hot * class_weight, axis=1, keepdims=True)
    ex.wait()
    logits = v.logit_recv[0].astype(F32)
    for k in range(1, SPLITS):
        logits = logits + v.logit_recv[k].astype(F32)

    def log_softmax(value):
        value = jnp.where(lanes < float(NCLS), value, -1e30)
        value = value - jnp.max(value, axis=1, keepdims=True)
        powers = jnp.exp(value)
        mass = jnp.sum(powers, axis=1, keepdims=True)
        return value - jnp.log(mass), powers / mass

    log_main, p_main = log_softmax(logits[:, :256])
    log_aux, p_aux = log_softmax(logits[:, 256:])
    loss_rows = total(fold(-cell_weight * hot * (log_main + 0.4 * log_aux)))
    loss_local = loss_rows[:, :128] + loss_rows[:, 128:]
    o_misc[1:2, :] = loss_local
    v.slope_in[t, :, :256] = (cell_weight * (p_main - hot) / loss_weight).astype(BF)
    v.slope_in[t, :, 256:] = (0.4 * cell_weight * (p_aux - hot) / loss_weight).astype(BF)
    spread_g = Spread(v.slope_in)
    spread_g.start()
    spread_g.wait()
    g_main = v.slope_in[:, :, :256].reshape(CELLS, 256)
    g_aux = v.slope_in[:, :, 256:].reshape(CELLS, 256)
    v.d_f[...] = dot_nt(g_main, v.w_c[...])
    v.d_f2[...] = dot_nt(g_aux, w_ac)

    def slope(value):
        gate = jax.nn.sigmoid(value)
        return gate * (1.0 + value * (1.0 - gate))

    def through_silu(ref, pre, norm, row):
        def step(k, carry):
            at = rows_at(k, 96)
            unit = normed(pre, at, norm)
            value = ref[at, :] * slope(gamma(row) * unit + beta(row))
            ref[at, :] = value
            return (carry[0] + fold(value), carry[1] + fold(value * unit))

        zero = jnp.zeros((8, 128), F32)
        sums = lax.fori_loop(0, 6, step, (zero, zero))
        return [total(sums[0]), total(sums[1])]

    def back_norm(value, unit, mask, norm, gain, first, second, size):
        inner = value - mask * (first + unit * second) / size
        return gain * norm[1] * inner

    gain_grads = {}
    sync = Sync(v.sync_b1)
    sync.start(
        through_silu(v.d_f, v.pre_u, norm_u, 14) + through_silu(v.d_f2, v.pre_a, norm_a, 15)
    )

    class Scatter:
        def __init__(self, first, second, full, rows, out, base=0):
            self.full, self.rows, self.out, self.base = full, rows, out, base
            self.first, self.second = first, second
            self.near_s, self.near_r = take(HALF), take(HALF)
            self.far_s, self.far_r = take(HALF), take(HALF)
            self.block = min(rows, 64)

        def near(self, step):
            dest = far_peer(partner, step)
            return remote(
                self.full.at[rows_at(dest, self.rows), :],
                self.first.at[step],
                self.near_s + step,
                self.near_r + step,
                {BATCH: partner},
            )

        def far(self, step):
            return remote(
                self.first.at[step],
                self.second.at[step - 1],
                self.far_s + step,
                self.far_r + step,
                {BATCH: far_peer(me, step)},
            )

        def start(self):
            for step in (1, 2, 3, 0):
                self.near(step).start()

        def middle(self):
            kind = self.first.dtype
            for step in range(1, HALF):
                self.near(step).wait_recv()
                base = far_peer(me, step) * (self.rows // self.block)

                def add(k, step=step, base=base):
                    at = rows_at(k, self.block)
                    value = self.full[rows_at(base + k, self.block), :].astype(F32)
                    value = value + self.first[step, at, :].astype(F32)
                    self.first[step, at, :] = value.astype(kind)

                loop(self.rows // self.block, add)
                self.far(step).start()

        def end(self):
            self.near(0).wait_recv()
            for step in range(1, HALF):
                self.far(step).wait_recv()
            base = me * (self.rows // self.block)

            def add(k, carry):
                at = rows_at(k, self.block)
                value = self.full[rows_at(base + k, self.block), :].astype(F32)
                value = value + self.first[0, at, :].astype(F32)
                for step in range(1, HALF):
                    value = value + self.second[step - 1, at, :].astype(F32)
                if self.out is o_flat:
                    times = value.shape[1] // 128
                    start = self.base + k * self.block * times
                    for q in range(times):
                        where = pl.ds(start + q, self.block, stride=times if times > 1 else None)
                        self.out[where, :] = value[:, q * 128 : q * 128 + 128]
                else:
                    self.out[at, :] = value
                return carry + fold(value * value)

            squares = lax.fori_loop(
                0, self.rows // self.block, add, jnp.zeros((8, self.full.shape[1]), F32)
            )
            for step in (1, 2, 3, 0):
                self.near(step).wait_send()
                if step:
                    self.far(step).wait_send()
            return sum(split_rows(total(squares)))

    s_c = Scatter(v.first_c, v.second_c, v.w_c, 16, o_c)
    s_ac = Scatter(v.first_ac, v.second_ac, v.w_ac, 8, o_ac)
    s_a = Scatter(v.first_a, v.second_a, v.w_a, 576, o_a)
    s_s = Scatter(v.first_s, v.second_s, v.w_s, 128, o_flat, 128)
    s_e = Scatter(v.first_e, v.second_e, v.w_e, 64, o_flat, 1216)
    s_m = Scatter(v.first_m, v.second_m, v.w_m, 576, o_flat, 640)
    s_r = Scatter(v.first_r, v.second_r, v.w_r, 128, o_flat, 0)

    class ScatterUnite:
        def __init__(self):
            self.near_s, self.near_r = take(SLOTS * HALF), take(SLOTS * HALF)
            self.far_s, self.far_r = take(SLOTS * HALF), take(SLOTS * HALF)

        def near(self, step, slot, base):
            dest = far_peer(base, step)
            return remote(
                v.w_u.at[merged_rows(dest, slot), :],
                v.first_u.at[step, slot],
                self.near_s + step * SLOTS + slot,
                self.near_r + step * SLOTS + slot,
                {BATCH: partner},
            )

        def far(self, step, slot):
            return remote(
                v.first_u.at[step, slot],
                v.second_u.at[step - 1, slot],
                self.far_s + step * SLOTS + slot,
                self.far_r + step * SLOTS + slot,
                {BATCH: far_peer(me, step)},
            )

        def own_rows(self, owner, slot, k):
            block = owner * 9 + block_of(owner, slot)
            index = lax.div(block, 8) * MERGED + lax.rem(block, 8)
            return rows_at(index * 8 + k, 64)

        def start(self, slot):
            for step in (1, 2, 3, 0):
                has(
                    far_peer(partner, step),
                    slot,
                    lambda step=step: self.near(step, slot, partner).start(),
                )

        def middle(self, slot):
            for step in range(1, HALF):
                owner = far_peer(me, step)

                def go(step=step, owner=owner):
                    self.near(step, slot, me).wait_recv()

                    def add(k):
                        at = rows_at(k, 64)
                        value = v.w_u[self.own_rows(owner, slot, k), :].astype(F32)
                        value = value + v.first_u[step, slot, at, :].astype(F32)
                        v.first_u[step, slot, at, :] = value.astype(BF)

                    loop(8, add)
                    self.far(step, slot).start()

                has(owner, slot, go)

        def end(self):
            for slot in range(SLOTS):

                def go(slot=slot):
                    self.near(0, slot, me).wait_recv()
                    for step in range(1, HALF):
                        self.far(step, slot).wait_recv()
                    j = block_of(me, slot)

                    def add(k):
                        at = rows_at(k, 64)
                        value = v.w_u[self.own_rows(me, slot, k), :].astype(F32)
                        value = value + v.first_u[0, slot, at, :].astype(F32)
                        for step in range(1, HALF):
                            value = value + v.second_u[step - 1, slot, at, :].astype(F32)
                        o_u[rows_at(j * 8 + k, 64), :] = value

                    loop(8, add)

                has(me, slot, go)
                for step in (1, 2, 3, 0):
                    has(
                        far_peer(partner, step),
                        slot,
                        lambda step=step, slot=slot: self.near(step, slot, partner).wait_send(),
                    )
                    if step:
                        has(
                            far_peer(me, step),
                            slot,
                            lambda step=step, slot=slot: self.far(step, slot).wait_send(),
                        )

            def square(k, carry):
                value = o_u[rows_at(k, 64), :]
                return carry + fold(value * value)

            squares = lax.fori_loop(0, 72, square, jnp.zeros((8, 128), F32))
            return sum(split_rows(total(squares)))

    s_u = ScatterUnite()

    v.w_c[...] = dot_tn(v.united[...], g_main).astype(BF)
    v.w_ac[...] = dot_tn(v.act_a[...], g_aux)[:64]
    s_c.start()
    s_ac.start()
    sums = sync.wait()
    gain_grads[14] = (sums[1:2], sums[0:1])
    gain_grads[15] = (sums[3:4], sums[2:3])

    def spread_taps(ref, pre, norm, row, first, second):
        def step(k):
            at = rows_at(k, 96)
            value = back_norm(
                ref[at, :], normed(pre, at, norm), v.ins[at, :], norm, gamma(row), first, second, count
            )
            ref[at, :] = value.astype(BF).astype(F32)

        loop(6, step)
        v.grad_pad[EDGE : EDGE + CELLS, :] = ref[...]

    def back_tap(tap, spacing, at):
        start = EDGE + at - offset(tap, spacing)
        value = v.grad_pad[start : start + 96, :]
        right = tap % 3 - 1
        if right:
            value = value * col_mask(slice(at, at + 96), -right * spacing)
        return value

    def fill(cat, spacing):
        for tap in range(9):
            for at in range(0, CELLS, 96):
                cat[at : at + 96, tap * 128 : tap * 128 + 128] = back_tap(tap, spacing, at).astype(
                    BF
                )

    spread_taps(v.d_f, v.pre_u, norm_u, 14, sums[0:1], sums[1:2])
    fill(v.cat_u, 1)

    dz = dot(v.pick[...], v.cat_u[...])
    for tap in range(9):
        v.dz_send[tap] = dz[:, tap * 128 : tap * 128 + 128].astype(BF)
    v.dz_recv[me] = v.dz_send[pl.ds(me, 2)]
    ex_dz = Exchange(
        BATCH, OWNERS, lambda o: v.dz_send.at[pl.ds(o, 2)], lambda s: v.dz_recv.at[s]
    )
    ex_dz.start()

    def merged_back(c):
        weight = jnp.concatenate(
            [v.w_u[rows_at(tap * MERGED + c, 512), :] for tap in range(9)], axis=1
        )
        v.joined[c] = dot_nt(v.cat_u[...], weight).astype(BF)

    near_s, near_r, far_s, far_r = take(2), take(2), take(1), take(1)

    def dm_near(k, slot):
        return remote(
            v.joined.at[slot], v.dm_near.at[k], near_s + k, near_r + k, {TENSOR: t_core}
        )

    merged_back(t_diag)
    dm_near(1, t_diag).start()
    merged_back(t_core)
    dm_near(0, t_core).start()
    ex_dz.wait()

    d_act = v.d_sum.at[0 : OWNERS * BINS, :]
    d_act[...] = jnp.zeros((OWNERS * BINS, 512), F32)

    def branch_back(j):
        def body(group, side):
            kept = jnp.where(group_id == group, 1.0, 0.0)
            value = v.dz_recv[:, side].reshape(OWNERS * BINS, 128).astype(F32) * kept
            value = value.astype(BF)
            o_u[rows_at(j, 512), :] = dot_tn(full_act(), value)
            d_act[...] = d_act[...] + dot_nt(value, v.w_own[rows_at(j, 512), :])

        own_branch(j, body)

    loop(9, branch_back)
    for k in range(SPLITS):
        v.d_act_send[k] = d_act[:, k * 128 : k * 128 + 128].astype(BF)
    v.d_act_recv[t] = v.d_act_send[t]
    ex = Exchange(TENSOR, SPLITS, lambda o: v.d_act_send.at[o], lambda s: v.d_act_recv.at[s])
    ex.start()
    merged_back(t_x)
    merged_back(t)

    def unite_grad(c):
        for p in range(5):
            width = 256 if p < 4 else 128
            value = dot(v.joined_t[c], v.cat_u[:, p * 256 : p * 256 + width])
            v.w_u[rows_at(2 * p * MERGED + c, 512), :] = value[:, :128].astype(BF)
            if p < 4:
                v.w_u[rows_at((2 * p + 1) * MERGED + c, 512), :] = value[:, 128:].astype(BF)

    loop(SPLITS, unite_grad)
    s_u.start(0)
    dm_near(1, t_x).wait_recv()

    def add_x(k):
        at = rows_at(k, 48)
        value = v.joined[t_x, at, :].astype(F32) + v.dm_near[1, at, :].astype(F32)
        v.joined[t_x, at, :] = value.astype(BF)

    loop(12, add_x)
    dm_far = remote(v.joined.at[t_x], v.dm_far, far_s, far_r, {TENSOR: t_x})
    ex.wait()
    for k in range(OWNERS):
        at = slice(k * BINS, k * BINS + BINS)
        value = v.d_act_recv[0, at, :].astype(F32)
        for slot in range(1, SPLITS):
            value = value + v.d_act_recv[slot, at, :].astype(F32)
        v.d_img_send[k] = value.astype(BF)
    v.d_img_recv[me] = v.d_img_send[me]
    ex = Exchange(BATCH, OWNERS, lambda o: v.d_img_send.at[o], lambda s: v.d_img_recv.at[s])
    ex.start()
    dm_far.start()
    s_u.start(1)

    spread_taps(v.d_f2, v.pre_a, norm_a, 15, sums[2:3], sums[3:4])
    for p in range(5):
        for at in range(0, CELLS, 96):
            value = back_tap(2 * p, 1, at)
            if p < 4:
                value = value + pltpu.roll(back_tap(2 * p + 1, 1, at), 64, 1)
            v.cat_a[at : at + 96, p * 128 : p * 128 + 128] = value.astype(BF)

    def aux_grad(c2):
        value2 = dot_tn(v.whole[c2], v.cat_a[...])
        for half in range(2):
            value = value2[half * 128 : half * 128 + 128]
            c = 2 * c2 + half
            for p in range(5):
                low = value[:64, p * 128 : p * 128 + 128]
                top = value[64:, p * 128 : p * 128 + 128]
                even = jnp.where(left_half, low, pltpu.roll(top, 64, 1))
                v.w_a[rows_at(2 * p * 8 + c, 64), :] = even.astype(BF)
                if p < 4:
                    odd = jnp.where(left_half, pltpu.roll(low, 64, 1), top)
                    v.w_a[rows_at((2 * p + 1) * 8 + c, 64), :] = odd.astype(BF)

    loop(SPLITS, aux_grad)
    s_u.middle(0)
    ex.wait()
    d_b = v.d_img_recv[0].astype(F32)
    for k in range(1, OWNERS):
        d_b = d_b + v.d_img_recv[k].astype(F32)
    unit_b = (v.all_b[me].astype(F32) - mean_b) * scale_b
    d_b = d_b * slope(gamma_b * unit_b + beta_b)
    sync = Sync(v.sync_b3)
    sync.start(
        [total(d_b * group_mask(g)) for g in range(4)]
        + [total(d_b * unit_b * group_mask(g)) for g in range(4)]
    )
    s_u.start(2)
    sums = sync.wait()
    first_b = jnp.zeros((BINS, 128), F32)
    second_b = jnp.zeros((BINS, 128), F32)
    for group in range(4):
        kept = group_mask(group)
        gain_grads[10 + group] = (sums[4 + group : 5 + group], sums[group : group + 1])
        first_b = first_b + kept * sums[group : group + 1]
        second_b = second_b + kept * sums[4 + group : 5 + group]
    inner = d_b - (first_b + unit_b * second_b) * count_b
    v.d_bp[t] = (gamma_b * scale_b * inner).astype(BF)
    spread_d = Spread(v.d_bp)
    spread_d.start()
    s_u.start(3)
    s_u.middle(1)
    spread_d.wait()
    d_bp_move = ToGroup(
        lambda owner, rows: v.d_bp.at[:, 0:rows, :],
        lambda slot, rows: v.d_bp_all.at[slot, :, 0:rows, :],
    )
    d_bp_move.start()
    v.d_bp_all[me] = v.d_bp[...]
    d_bp = jnp.concatenate([v.d_bp[k] for k in range(SPLITS)], axis=1)
    d_pooled = jnp.zeros((BINS, 512), F32)
    for group in range(4):
        rows = (d_bp.astype(F32) * group_mask(group)).astype(BF)
        d_pooled = d_pooled + dot_nt(rows, v.w_b[group * 512 : group * 512 + 512, :])
    d_pooled = (d_pooled / cells_in).astype(BF)
    v.d_sum[...] = dot_tn(v.pool[...], d_pooled)
    dm_near(0, t).wait_recv()
    dm_far.wait_recv()

    def through_sum(k, carry):
        at = rows_at(k, 48)
        value = v.d_sum[at, :] + v.joined[t, at, :].astype(F32) + v.dm_near[0, at, :].astype(F32)
        value = (value + v.dm_far[at, :].astype(F32)) * slope(summed(at))
        v.d_sum[at, :] = value
        return (
            carry[0] + fold(value),
            carry[1] + fold(value * normed(v.pre_e, at, norm_e)),
            carry[2] + fold(value * normed(v.pre_s, at, norm_s)),
        )

    zero = jnp.zeros((8, 512), F32)
    three = [total(item) for item in lax.fori_loop(0, 12, through_sum, (zero, zero, zero))]
    sync = Sync(v.sync_b4)
    sync.start(split_rows(three[0]) + split_rows(three[1]) + split_rows(three[2]))
    s_u.start(4)
    s_u.middle(2)
    sums = sync.wait()
    first_s = join_rows(sums, 0, 4)
    second_e, second_s = join_rows(sums, 4, 4), join_rows(sums, 8, 4)
    for k in range(4):
        gain_grads[6 + k] = (sums[4 + k : 5 + k], sums[k : k + 1])
        gain_grads[1 + k] = (sums[8 + k : 9 + k], sums[k : k + 1])

    def back_both(k):
        at = rows_at(k, 48)
        value, mask = v.d_sum[at, :], wide(v.ins[at, :], 4)
        v.d_e[at, :] = back_norm(
            value, normed(v.pre_e, at, norm_e), mask, norm_e, gamma(6, 4), first_s, second_e, count4
        ).astype(BF)
        v.d_s[at, :] = back_norm(
            value, normed(v.pre_s, at, norm_s), mask, norm_s, gamma(1, 4), first_s, second_s, count4
        ).astype(BF)

    loop(12, back_both)

    def back_hidden(grad, weight, index):
        value = dot_nt(grad, weight)
        for k in range(SPLITS):
            v.dh_send[k] = value[:, k * 128 : k * 128 + 128].astype(BF)
        v.dh_recv[index, t] = v.dh_send[t]
        ex = Exchange(
            TENSOR, SPLITS, lambda o: v.dh_send.at[o], lambda s: v.dh_recv.at[index, s]
        )
        ex.start()
        return ex

    def hidden_sum(index):
        def step(k):
            at = rows_at(k, 96)
            value = v.dh_recv[index, 0, at, :].astype(F32)
            for slot in range(1, SPLITS):
                value = value + v.dh_recv[index, slot, at, :].astype(F32)
            v.d_f[at, :] = value

        loop(6, step)

    ex = back_hidden(v.d_e[...], v.w_e[...], 0)
    s_a.start()
    s_u.middle(3)
    for k in range(SPLITS):
        v.w_e[k * 128 : k * 128 + 128, :] = dot_tn(v.h2[k], v.d_e[...]).astype(BF)
    ex.wait()
    hidden_sum(0)
    sync = Sync(v.sync_b5)
    sync.start(through_silu(v.d_f, v.pre_m, norm_m, 5))
    s_e.start()
    s_c.middle()
    s_ac.middle()
    s_u.middle(4)
    sums = sync.wait()
    gain_grads[5] = (sums[1:2], sums[0:1])
    spread_taps(v.d_f, v.pre_m, norm_m, 5, sums[0:1], sums[1:2])
    fill(v.cat_u, 4)
    weight = jnp.concatenate([v.w_m[tap * 512 : tap * 512 + 512, :] for tap in range(9)], axis=1)
    ex = back_hidden(v.cat_u[...], weight, 1)

    def short_grad(c):
        v.w_s[rows_at(c, 256), :] = dot_tn(v.whole[c], v.d_s[...]).astype(BF)

    loop(SPLITS, short_grad)
    s_s.start()
    s_a.middle()
    ex.wait()
    hidden_sum(1)
    sync = Sync(v.sync_b6)
    sync.start(through_silu(v.d_f, v.pre_r, norm_r, 0))

    def middle_grad(k):
        value = dot_tn(v.h1[k], v.cat_u[...])
        for tap in range(9):
            v.w_m[rows_at(tap * 4 + k, 128), :] = value[:, tap * 128 : tap * 128 + 128].astype(BF)

    loop(SPLITS, middle_grad)
    s_m.start()
    s_e.middle()
    s_s.middle()
    sums = sync.wait()
    gain_grads[0] = (sums[1:2], sums[0:1])

    def back_reduce(k):
        at = rows_at(k, 96)
        v.d_low[at, :] = back_norm(
            v.d_f[at, :], normed(v.pre_r, at, norm_r), v.ins[at, :], norm_r, gamma(0), sums[0:1], sums[1:2], count
        ).astype(BF)

    loop(6, back_reduce)

    def reduce_grad(c):
        v.w_r[rows_at(c, 256), :] = dot_tn(v.whole[c], v.d_low[...]).astype(BF)

    loop(SPLITS, reduce_grad)
    s_r.start()
    for item in (s_m, s_r):
        item.middle()
    pool_move.wait()
    d_bp_move.wait()
    own_group = jnp.where(group_id == lax.div(me, 2), 1.0, 0.0)
    d_rows = jnp.concatenate(
        [v.d_bp_all[:, k].reshape(OWNERS * BINS, 128) for k in range(SPLITS)], axis=1
    )
    d_rows = (d_rows.astype(F32) * own_group).astype(BF)
    branch_grad = dot_tn(v.pool_all[...].reshape(OWNERS * BINS, 256), d_rows)
    for k in range(4):
        o_flat[pl.ds(1472 + k, 256, stride=4), :] = branch_grad[:, k * 128 : k * 128 + 128]
    rest = (s_c, s_ac, s_a, s_e, s_s, s_m, s_r)
    squares = s_u.end() + sum(split_rows(total(branch_grad * branch_grad)))
    for item in rest:
        squares = squares + item.end()
    dm_near(1, t_diag).wait_send()
    dm_near(0, t_core).wait_send()
    dm_far.wait_send()

    for row in range(16):
        o_gain[row : row + 1, :] = gain_grads[row][0]
        o_gain[16 + row : 17 + row, :] = gain_grads[row][1]
    gain_square = o_gain[...] * o_gain[...]
    squares = squares + total(gain_square) / OWNERS

    sync = Sync(v.sync_end)
    sync.start([squares, o_misc[1:2, :]])
    v.end_t[t] = sync.wait()
    spread_e = Spread(v.end_t)
    spread_e.start()
    spread_e.wait()
    ends = v.end_t[0]
    for k in range(1, SPLITS):
        ends = ends + v.end_t[k]
    o_misc[...] = ends
    o_misc[2:3, :] = jnp.broadcast_to(loss_weight, (1, 128))


def whole_step(sizes, labels, feat, gains, pieces):
    plan = scratch_plan()
    vmem = pl.BlockSpec(memory_space=pltpu.VMEM)
    anywhere = pl.BlockSpec(memory_space=pl.ANY)
    outs = [(7712, 128), (576, 128), (16, 256), (8, 256), (32, 128), (8, 128)]
    return pl.pallas_call(
        functools.partial(step_kernel, tuple(plan)),
        out_shape=[jax.ShapeDtypeStruct(shape, F32) for shape in outs],
        in_specs=[pl.BlockSpec(memory_space=pltpu.SMEM), vmem, anywhere, anywhere]
        + [anywhere] * len(pieces),
        out_specs=[vmem] * len(outs),
        scratch_shapes=[pltpu.VMEM(shape, kind) for shape, kind in plan.values()]
        + [pltpu.SemaphoreType.DMA((SEMAPHORES,))],
        compiler_params=pltpu.CompilerParams(
            collective_id=0, has_side_effects=True, vmem_limit_bytes=63 * 1024 * 1024
        ),
        name="whole_step",
    )(sizes, labels, feat, gains, *pieces)


def update_kernel(scale, grad, param, first, second, average, o_param, o_first, o_second, o_average):
    clipped = grad[...] * scale[0]
    new_first = 0.5 * first[...] + 0.5 * clipped
    new_second = 0.5 * second[...] + 0.5 * clipped * clipped
    keep = 1.0 - 0.5**STEP
    old = param[...]
    new = old - 0.01 * (new_first / keep / (jnp.sqrt(new_second / keep) + 1e-08) + 0.01 * old)
    o_param[...] = new
    o_first[...] = new_first
    o_second[...] = new_second
    o_average[...] = 0.999 * average[...] + 0.001 * new


def update(scale, grad, param, first, second, average):
    rows = grad.shape[0]
    block = pl.BlockSpec((512, 128), lambda i: (i, 0))
    return pl.pallas_call(
        update_kernel,
        grid=(pl.cdiv(rows, 512),),
        out_shape=[jax.ShapeDtypeStruct((rows, 128), jnp.float32)] * 4,
        in_specs=[pl.BlockSpec(memory_space=pltpu.SMEM)] + [block] * 5,
        out_specs=[block] * 4,
        name="update",
    )(scale.reshape(1), grad, param, first, second, average)

def fits(splits, owners):
    return splits == SPLITS and owners == OWNERS


def local_fast(features, labels, valid, sizes, params, first_moment, squared_mean, average):
    me = lax.axis_index("batch")
    shapes = segment_shapes(SPLITS)
    counts = []
    for shape in shapes:
        count = 1
        for extent in shape:
            count = count * extent
        counts.append(count // OWNERS)
    starts = [0]
    for count in counts:
        starts.append(starts[-1] + count)
    flat = params.reshape(-1, 128)
    low = flat.astype(BF)
    tail = lax.optimization_barrier(flat[starts[6] // 128 :]).reshape(-1)
    cut = [tail[starts[k] - starts[6] : starts[k + 1] - starts[6]] for k in range(6, 10)]
    rows = [low[starts[k] // 128 : starts[k + 1] // 128] for k in range(6)]
    aux = cut[1].astype(BF).reshape(9, 2, 64, 64)
    pieces = [
        rows[0],
        rows[1].reshape(128, 512),
        rows[2],
        rows[3].reshape(64, 512),
        rows[4].reshape(256, 512),
        rows[5],
        jnp.concatenate([aux[:, 0], aux[:, 1]], axis=-1).reshape(576, 128),
        jnp.pad(cut[0].astype(BF).reshape(16, NCLS), ((0, 0), (0, 256 - NCLS))),
        jnp.pad(
            cut[2].astype(BF).astype(F32).reshape(8, NCLS), ((0, 0), (0, 256 - NCLS))
        ),
    ]
    width = shapes[9][1]
    share = counts[9]
    per_row = width // share
    spot = jnp.zeros((2, 2048), F32)
    spot = lax.dynamic_update_slice(
        spot,
        cut[3].astype(BF).astype(F32).reshape(1, share),
        (me // per_row, (me % per_row) * share),
    )
    marked = jnp.where(valid > 0, labels, -1).astype(F32).reshape(CELLS, 1)
    outs = whole_step(
        sizes,
        jnp.broadcast_to(marked, (CELLS, 128)),
        features.reshape(CELLS, -1),
        spot.reshape(32, 128),
        pieces,
    )
    gain_grad = lax.dynamic_slice(
        outs[4].reshape(2, 2048)[:, :width].reshape(-1), (me * share,), (share,)
    )
    aux_grad = outs[1].reshape(9, 64, 2, 64).transpose(0, 2, 1, 3)
    tail_grad = jnp.concatenate(
        [
            outs[2][:, :NCLS].reshape(-1),
            aux_grad.reshape(-1),
            outs[3][:, :NCLS].reshape(-1),
            gain_grad,
        ]
    ).reshape(-1, 128)
    grad_share = lax.dynamic_update_slice(outs[0], tail_grad, (starts[6] // 128, 0))
    misc = outs[5]
    grad_norm = jnp.sqrt(jnp.sum(misc[0]))
    scale = jnp.minimum(1.0, 0.05 / (grad_norm + 1e-06))
    new_params, new_first, new_second, new_average = [
        item.reshape(params.shape)
        for item in update(
            scale,
            grad_share,
            flat,
            first_moment.reshape(-1, 128),
            squared_mean.reshape(-1, 128),
            average.reshape(-1, 128),
        )
    ]
    return (
        new_params,
        new_first,
        new_second,
        new_average,
        new_params.astype(BF),
        grad_norm,
        jnp.sum(misc[1]),
        misc[2, 0],
        outs[4][30],
    )


def solution(mesh):
    chosen = local_fast if fits(mesh.shape["tensor"], mesh.shape["batch"]) else local
    return jax.shard_map(
        chosen,
        mesh=mesh,
        in_specs=(
            P("batch", None, None, "tensor"),
            P("batch", None, None),
            P("batch", None, None),
            P("batch", None),
            P("tensor", "batch"),
            P("tensor", "batch"),
            P("tensor", "batch"),
            P("tensor", "batch"),
        ),
        out_specs=(
            P("tensor", "batch"),
            P("tensor", "batch"),
            P("tensor", "batch"),
            P("tensor", "batch"),
            P("tensor", "batch"),
            P(),
            P(),
            P(),
            P("tensor"),
        ),
        check_vma=False,
    )
```

```python
import functools

import jax
import jax.numpy as jnp
from jax import lax
from jax.experimental import pallas as pl
from jax.experimental.pallas import tpu as pltpu
from jax.sharding import PartitionSpec as P

C_IN = 1024
MID = 512
C_OUT = 2048
PPM = 512
AUXW = 256
NCLS = 150
MAP = 24
STEP = 3


BIN_COUNTS = (1, 2, 3, 6)
BIN_STARTS = (0, 1, 5, 14)


def segment_shapes(splits):
    return [
        (C_IN, MID // splits),
        (C_IN, C_OUT // splits),
        (9, MID, MID // splits),
        (MID, C_OUT // splits),
        (4, C_OUT // splits, PPM),
        (9, C_OUT + 4 * PPM, PPM // splits),
        (PPM // splits, NCLS),
        (9, C_IN, AUXW // splits),
        (AUXW // splits, NCLS),
        (2, (2 * MID + 2 * C_OUT + 5 * PPM + AUXW) // splits),
    ]


def unflatten(rows, splits):
    split_parts = []
    start = 0
    for shape in segment_shapes(splits):
        count = 1
        for extent in shape:
            count = count * extent
        count = count // rows.shape[0]
        split_parts.append(rows[:, start : start + count].reshape(shape))
        start = start + count
    return split_parts


def gain_pieces(gains, splits):
    widths = [MID, C_OUT, MID, C_OUT, PPM, PPM, PPM, PPM, PPM, AUXW]
    split_parts = []
    start = 0
    for width in widths:
        step_width = width // splits
        split_parts.append(gains[:, start : start + step_width])
        start = start + step_width
    return split_parts


def shifted(field, down, right):
    image_height, width = (field.shape[1], field.shape[2])
    rows_pad, cols_pad = (abs(down), abs(right))
    padded = jnp.pad(field, ((0, 0), (rows_pad, rows_pad), (cols_pad, cols_pad), (0, 0)))
    return padded[
        :,
        rows_pad + down : rows_pad + down + image_height,
        cols_pad + right : cols_pad + right + width,
        :,
    ]


def conv_forward(field, kernel, spacing):
    total = jnp.zeros(field.shape[:-1] + (kernel.shape[2],), jnp.float32)
    for tap in range(9):
        moved = shifted(field, (tap // 3 - 1) * spacing, (tap % 3 - 1) * spacing)
        total = total + jnp.dot(moved, kernel[tap], preferred_element_type=jnp.float32)
    return total


def conv_input_back(grad, kernel, spacing):
    total = jnp.zeros(grad.shape[:-1] + (kernel.shape[1],), jnp.float32)
    for tap in range(9):
        product = jnp.dot(grad, kernel[tap].T, preferred_element_type=jnp.float32)
        total = total + shifted(product, -(tap // 3 - 1) * spacing, -(tap % 3 - 1) * spacing)
    return total


def conv_kernel_back(field, grad, spacing):
    return jnp.stack(
        [
            jnp.einsum(
                "ihwc,ihwd->cd",
                shifted(field, (tap // 3 - 1) * spacing, (tap % 3 - 1) * spacing),
                grad,
                preferred_element_type=jnp.float32,
            )
            for tap in range(9)
        ]
    )


def silu_slope(value):
    gate = jax.nn.sigmoid(value)
    return gate * (1.0 + value * (1.0 - gate))


def channel_sums(values):
    return values.reshape(-1, values.shape[-1]).sum(0)


def masked_norm_apply(items, extra):
    sends = []
    for value, mask, norm in items:
        sends = sends + [
            channel_sums(value * mask),
            channel_sums(value * value * mask),
            jnp.sum(mask) * jnp.ones((1,), jnp.float32),
        ]
    totals = lax.psum(tuple(sends + extra), "batch")
    results = []
    for index, (value, mask, norm) in enumerate(items):
        count = totals[3 * index + 2]
        mean = totals[3 * index] / count
        spread = totals[3 * index + 1] / count - mean * mean
        scaling = lax.rsqrt(spread + 1e-05)
        normed = (value - mean) * scaling
        results.append((norm[0] * normed + norm[1], normed, scaling, count, mask, norm[0]))
    return (results, totals[3 * len(items) :])


def norm_backward(items):
    sends = []
    for grad, kept in items:
        sends = sends + [channel_sums(grad), channel_sums(grad * kept[1])]
    totals = lax.psum(tuple(sends), "batch")
    results = []
    for index, (grad, kept) in enumerate(items):
        outcome, normed, scaling, count, mask, gamma = kept
        first_sum, second_sum = (totals[2 * index], totals[2 * index + 1])
        inner = grad - mask * (first_sum + normed * second_sum) / count
        results.append(gamma * scaling * inner)
    return (results, sends, totals)


def bin_tables(extent, bins, length):
    which = jnp.arange(bins, dtype=jnp.int32)[None, :, None]
    place = jnp.arange(length, dtype=jnp.int32)[None, None, :]
    edge = extent[:, None, None]
    lower = which * edge // bins
    upper = ((which + 1) * edge + bins - 1) // bins
    member = ((place >= lower) & (place < upper)).astype(jnp.float32)
    target = jnp.minimum(place * bins // edge, bins - 1)
    chosen = (target == which).astype(jnp.float32)
    return (member, chosen)


def spread_bins(merged, branch, tables, images):
    joined = [merged]
    for group, bins in enumerate(BIN_COUNTS):
        rows_in, cols_in, rows_pick, cols_pick, cell_count = tables[group]
        piece = branch[:, BIN_STARTS[group] : BIN_STARTS[group] + bins * bins].reshape(
            images, bins, bins, -1
        )
        joined.append(
            jnp.einsum(
                "ikh,ilw,iklc->ihwc",
                rows_pick.astype(jnp.bfloat16),
                cols_pick.astype(jnp.bfloat16),
                piece,
                preferred_element_type=jnp.float32,
            ).astype(jnp.bfloat16)
        )
    return jnp.concatenate(joined, axis=-1)


def pick_bins(d_joined, width, tables, images):
    branch_width = (d_joined.shape[-1] - width) // 4
    d_up = []
    for group, bins in enumerate(BIN_COUNTS):
        rows_in, cols_in, rows_pick, cols_pick, cell_count = tables[group]
        piece = d_joined[..., width + group * branch_width : width + (group + 1) * branch_width]
        d_up.append(
            jnp.einsum("ikh,ilw,ihwc->iklc", rows_pick, cols_pick, piece).reshape(
                images, bins * bins, -1
            )
        )
    return (d_joined[..., :width], jnp.concatenate(d_up, axis=1))


def gather_channels(field):
    return lax.all_gather(field, "tensor", axis=3, tiled=True)


def scatter_channels(field):
    return lax.psum_scatter(
        field.astype(jnp.bfloat16), "tensor", scatter_dimension=3, tiled=True
    ).astype(jnp.float32)


def local(features, labels, valid, sizes, params, first_moment, squared_mean, average):
    splits = lax.axis_size("tensor")
    owners = lax.axis_size("batch")
    images = features.shape[0]
    gathered = lax.all_gather(params.astype(jnp.bfloat16), "batch", axis=0, tiled=True)
    (
        w_reduce,
        w_short,
        w_middle,
        w_expand,
        w_branch,
        w_unite,
        w_classes,
        w_aux,
        w_aux_classes,
        gains,
    ) = unflatten(gathered, splits)
    norms = [(piece[0], piece[1]) for piece in gain_pieces(gains.astype(jnp.float32), splits)]
    rows_at = jnp.arange(MAP, dtype=jnp.int32)
    inside = (rows_at[None, :, None] < sizes[:, 0][:, None, None]) & (
        rows_at[None, None, :] < sizes[:, 1][:, None, None]
    )
    inside = inside.astype(jnp.float32)[..., None]
    counted = inside * valid.astype(jnp.float32)[..., None]
    labels_hot = (labels[..., None] == jnp.arange(NCLS, dtype=jnp.int32)).astype(jnp.float32)
    class_local = channel_sums(labels_hot * counted)
    whole = lax.all_gather(features, "tensor", axis=3, tiled=True)
    pre_reduce = jnp.dot(whole, w_reduce, preferred_element_type=jnp.float32)
    pre_short = jnp.dot(whole, w_short, preferred_element_type=jnp.float32)
    pre_aux = conv_forward(whole, w_aux, 1)
    leading_part, label_tally = masked_norm_apply(
        [
            (pre_reduce, inside, norms[0]),
            (pre_short, inside, norms[1]),
            (pre_aux, inside, norms[9]),
        ],
        [class_local],
    )
    class_pixel_counts = label_tally[0]
    hidden_one = jax.nn.silu(leading_part[0][0]).astype(jnp.bfloat16)
    aux_act = jax.nn.silu(leading_part[2][0]).astype(jnp.bfloat16)
    hidden_full = gather_channels(hidden_one)
    pre_middle = conv_forward(hidden_full, w_middle, 4)
    second, unused = masked_norm_apply([(pre_middle, inside, norms[2])], [])
    hidden_two = jax.nn.silu(second[0][0]).astype(jnp.bfloat16)
    hidden_two_full = gather_channels(hidden_two)
    pre_expand = jnp.dot(hidden_two_full, w_expand, preferred_element_type=jnp.float32)
    third, unused = masked_norm_apply([(pre_expand, inside, norms[3])], [])
    summed = third[0][0] + leading_part[1][0]
    merged = jax.nn.silu(summed).astype(jnp.bfloat16)
    tables = []
    pooled_list = []
    partial_list = []
    for group, bins in enumerate(BIN_COUNTS):
        rows_in, rows_pick = bin_tables(sizes[:, 0], bins, MAP)
        cols_in, cols_pick = bin_tables(sizes[:, 1], bins, MAP)
        cell_count = (
            jnp.sum(rows_in, axis=2)[:, :, None, None] * jnp.sum(cols_in, axis=2)[:, None, :, None]
        )
        tables.append((rows_in, cols_in, rows_pick, cols_pick, cell_count))
        pooled = (
            jnp.einsum(
                "ikh,ilw,ihwc->iklc",
                rows_in.astype(jnp.bfloat16),
                cols_in.astype(jnp.bfloat16),
                merged,
                preferred_element_type=jnp.float32,
            )
            / cell_count
        )
        pooled = pooled.astype(jnp.bfloat16).reshape(images, bins * bins, -1)
        pooled_list.append(pooled)
        partial_list.append(
            jnp.einsum("ipc,cd->ipd", pooled, w_branch[group], preferred_element_type=jnp.float32)
        )
    branch_pre = lax.psum_scatter(
        jnp.concatenate(partial_list, axis=1).astype(jnp.bfloat16),
        "tensor",
        scatter_dimension=2,
        tiled=True,
    ).astype(jnp.float32)
    branch_items = []
    for group, bins in enumerate(BIN_COUNTS):
        piece = branch_pre[:, BIN_STARTS[group] : BIN_STARTS[group] + bins * bins]
        branch_items.append(
            (piece, jnp.ones(piece.shape[:-1] + (1,), jnp.float32), norms[4 + group])
        )
    fourth, unused = masked_norm_apply(branch_items, [])
    branch_act = jnp.concatenate([jax.nn.silu(kept[0]) for kept in fourth], axis=1).astype(
        jnp.bfloat16
    )
    merged_full, branch_full = (
        lax.all_gather(merged, "tensor", axis=3, tiled=True),
        lax.all_gather(branch_act, "tensor", axis=2, tiled=True),
    )
    joined = spread_bins(merged_full, branch_full, tables, images)
    pre_unite = conv_forward(joined, w_unite, 1)
    fifth, unused = masked_norm_apply([(pre_unite, inside, norms[8])], [])
    united = jax.nn.silu(fifth[0][0]).astype(jnp.bfloat16)
    logit_main, logit_aux = (
        lax.psum_scatter(
            jnp.dot(united, w_classes, preferred_element_type=jnp.float32).astype(jnp.bfloat16),
            "tensor",
            scatter_dimension=1,
            tiled=True,
        ).astype(jnp.float32),
        lax.psum_scatter(
            jnp.dot(aux_act, w_aux_classes, preferred_element_type=jnp.float32).astype(
                jnp.bfloat16
            ),
            "tensor",
            scatter_dimension=1,
            tiled=True,
        ).astype(jnp.float32),
    )
    total_valid = jnp.sum(class_pixel_counts)
    class_weight = total_valid / (NCLS * class_pixel_counts + total_valid)
    loss_weight = jnp.sum(class_pixel_counts * class_weight)
    cell_weight = jnp.sum(labels_hot * class_weight, axis=-1, keepdims=True) * counted
    band_rows = labels.shape[1] // splits
    band_start = lax.axis_index("tensor") * band_rows
    hot_band = lax.dynamic_slice_in_dim(labels_hot, band_start, band_rows, 1)
    weight_band = lax.dynamic_slice_in_dim(cell_weight, band_start, band_rows, 1)
    log_main = jax.nn.log_softmax(logit_main, axis=-1)
    log_aux = jax.nn.log_softmax(logit_aux, axis=-1)
    loss_cells = -jnp.sum(hot_band * (log_main + 0.4 * log_aux), axis=-1, keepdims=True)
    loss_local = jnp.sum(weight_band * loss_cells)
    band_main = (weight_band * (jnp.exp(log_main) - hot_band) / loss_weight).astype(jnp.bfloat16)
    band_aux = (0.4 * weight_band * (jnp.exp(log_aux) - hot_band) / loss_weight).astype(
        jnp.bfloat16
    )
    grad_main, grad_aux = (
        lax.all_gather(band_main, "tensor", axis=1, tiled=True),
        lax.all_gather(band_aux, "tensor", axis=1, tiled=True),
    )
    reduced = {}

    def settle(index, value):
        reduced[index] = value

    settle(6, jnp.einsum("ihwc,ihwk->ck", united, grad_main, preferred_element_type=jnp.float32))
    settle(8, jnp.einsum("ihwc,ihwk->ck", aux_act, grad_aux, preferred_element_type=jnp.float32))
    d_united = jnp.dot(grad_main, w_classes.T, preferred_element_type=jnp.float32) * silu_slope(
        fifth[0][0]
    )
    d_aux = jnp.dot(grad_aux, w_aux_classes.T, preferred_element_type=jnp.float32) * silu_slope(
        leading_part[2][0]
    )
    back_one, sums_one, totals_one = norm_backward([(d_united, fifth[0]), (d_aux, leading_part[2])])
    unite_shift_grad = totals_one[0]
    d_unite_pre = back_one[0].astype(jnp.bfloat16)
    d_aux_pre = back_one[1].astype(jnp.bfloat16)
    settle(5, conv_kernel_back(joined, d_unite_pre, 1))
    d_merged, d_branch = pick_bins(conv_input_back(d_unite_pre, w_unite, 1), C_OUT, tables, images)
    d_merged, d_branch = (
        lax.psum_scatter(
            d_merged.astype(jnp.bfloat16), "tensor", scatter_dimension=3, tiled=True
        ).astype(jnp.float32),
        lax.psum_scatter(
            d_branch.astype(jnp.bfloat16), "tensor", scatter_dimension=2, tiled=True
        ).astype(jnp.float32),
    )
    settle(7, conv_kernel_back(whole, d_aux_pre, 1))
    branch_back = []
    for group, bins in enumerate(BIN_COUNTS):
        piece = d_branch[:, BIN_STARTS[group] : BIN_STARTS[group] + bins * bins]
        branch_back.append((piece * silu_slope(fourth[group][0]), fourth[group]))
    back_two, sums_two, unused = norm_backward(branch_back)
    d_branch_pre = jnp.concatenate(back_two, axis=1).astype(jnp.bfloat16)
    d_branch_full = lax.all_gather(d_branch_pre, "tensor", axis=2, tiled=True)
    branch_grads = []
    for group, bins in enumerate(BIN_COUNTS):
        rows_in, cols_in, rows_pick, cols_pick, cell_count = tables[group]
        piece = d_branch_full[:, BIN_STARTS[group] : BIN_STARTS[group] + bins * bins]
        branch_grads.append(
            jnp.einsum("ipc,ipd->cd", pooled_list[group], piece, preferred_element_type=jnp.float32)
        )
        d_pooled = jnp.dot(piece, w_branch[group].T, preferred_element_type=jnp.float32).reshape(
            images, bins, bins, -1
        )
        d_merged = d_merged + jnp.einsum(
            "ikh,ilw,iklc->ihwc", rows_in, cols_in, d_pooled / cell_count
        )
    settle(4, jnp.stack(branch_grads))
    d_summed = d_merged * silu_slope(summed)
    back_three, sums_three, unused = norm_backward(
        [(d_summed, third[0]), (d_summed, leading_part[1])]
    )
    d_expand_pre = back_three[0].astype(jnp.bfloat16)
    d_short_pre = back_three[1].astype(jnp.bfloat16)
    settle(
        3,
        jnp.einsum(
            "ihwc,ihwd->cd", hidden_two_full, d_expand_pre, preferred_element_type=jnp.float32
        ),
    )
    settle(1, jnp.einsum("ihwc,ihwd->cd", whole, d_short_pre, preferred_element_type=jnp.float32))
    d_two = scatter_channels(jnp.dot(d_expand_pre, w_expand.T, preferred_element_type=jnp.float32))
    back_four, sums_four, unused = norm_backward([(d_two * silu_slope(second[0][0]), second[0])])
    d_middle_pre = back_four[0].astype(jnp.bfloat16)
    settle(2, conv_kernel_back(hidden_full, d_middle_pre, 4))
    d_one = scatter_channels(conv_input_back(d_middle_pre, w_middle, 4))
    back_five, sums_five, unused = norm_backward(
        [(d_one * silu_slope(leading_part[0][0]), leading_part[0])]
    )
    settle(
        0,
        jnp.einsum(
            "ihwc,ihwd->cd",
            whole,
            back_five[0].astype(jnp.bfloat16),
            preferred_element_type=jnp.float32,
        ),
    )
    beta_grads = (
        [sums_five[0], sums_three[2], sums_four[0], sums_three[0]]
        + [sums_two[2 * g] for g in range(4)]
        + [sums_one[0], sums_one[2]]
    )
    gamma_grads = (
        [sums_five[1], sums_three[3], sums_four[1], sums_three[1]]
        + [sums_two[2 * g + 1] for g in range(4)]
        + [sums_one[1], sums_one[3]]
    )
    settle(9, jnp.stack([jnp.concatenate(gamma_grads), jnp.concatenate(beta_grads)]))
    ordered = [reduced[index] for index in range(10)]
    grad_share = lax.psum_scatter(
        jnp.concatenate([part.reshape(owners, -1) for part in ordered], axis=1),
        "batch",
        scatter_dimension=0,
        tiled=True,
    )
    square_all, loss_sum = lax.psum(
        (jnp.sum(grad_share * grad_share), loss_local), ("batch", "tensor")
    )
    grad_norm = jnp.sqrt(square_all)
    clipped = grad_share * jnp.minimum(1.0, 0.05 / (grad_norm + 1e-06))
    new_first = 0.5 * first_moment + 0.5 * clipped
    new_second = 0.5 * squared_mean + 0.5 * clipped * clipped
    keep = 1.0 - 0.5**STEP
    new_params = params - 0.01 * (
        new_first / keep / (jnp.sqrt(new_second / keep) + 1e-08) + 0.01 * params
    )
    new_average = 0.999 * average + 0.001 * new_params
    return (
        new_params,
        new_first,
        new_second,
        new_average,
        new_params.astype(jnp.bfloat16),
        grad_norm,
        loss_sum,
        loss_weight,
        unite_shift_grad,
    )


CELLS = MAP * MAP
EDGE = 104
BATCH = "batch"
TENSOR = "tensor"
GROUP_ROWS = ((0, 1), (1, 5), (5, 14), (14, 50))
BINS = 64
BF = jnp.bfloat16
F32 = jnp.float32
MESH = pl.DeviceIdType.MESH
HALF = 4
OWNERS = 8
SPLITS = 4
MERGED = 4
SLOTS = 5


def scratch_plan():
    plan = dict(
        w_r=((1024, 128), BF),
        w_s=((1024, 512), BF),
        w_m=((4608, 128), BF),
        w_e=((512, 512), BF),
        w_b=((2048, 512), BF),
        w_u=((18432, 128), BF),
        w_own=((4608, 128), BF),
        w_a=((4608, 128), BF),
        w_pair=((1024, 640), BF),
        w_c=((128, 256), BF),
        w_ac=((64, 256), F32),
        gain_in=((OWNERS, 8, 128), F32),
        gain_rows=((40, 128), F32),
        out_a=((576, 128), F32),
        out_c=((16, 256), F32),
        out_ac=((8, 256), F32),
        whole=((SPLITS, CELLS, 256), BF),
        ins=((CELLS, 128), F32),
        col=((CELLS, 128), F32),
        lab=((CELLS, 128), F32),
        table=((BINS, CELLS), F32),
        pool=((BINS, CELLS), BF),
        pick=((BINS, CELLS), BF),
        cells_in=((BINS, 128), F32),
        pad=((9, CELLS + 2 * EDGE, 128), F32),
        grad_pad=((CELLS + 2 * EDGE, 128), F32),
        pre_r=((CELLS, 128), F32),
        pre_s=((CELLS, 512), F32),
        pre_a=((CELLS, 128), F32),
        pre_m=((CELLS, 128), F32),
        pre_e=((CELLS, 512), F32),
        pre_u=((CELLS, 128), F32),
        act_a=((CELLS, 128), BF),
        h1=((SPLITS, CELLS, 128), BF),
        h2=((SPLITS, CELLS, 128), BF),
        joined=((SPLITS, CELLS, 512), BF),
        joined_t=((SPLITS, 512, CELLS), BF),
        pooled=((BINS, 512), BF),
        pool_half=((2, BINS, 256), BF),
        pool_all=((OWNERS, BINS, 256), BF),
        d_bp_all=((OWNERS, SPLITS, BINS, 128), BF),
        part_b=((SPLITS, BINS, 128), BF),
        recv_b=((SPLITS, BINS, 128), BF),
        all_b=((OWNERS, BINS, 128), BF),
        act_b=((SPLITS, OWNERS * BINS, 128), BF),
        zsum=((2, OWNERS * BINS, 128), F32),
        z_send=((OWNERS, 2, BINS, 128), BF),
        z_recv=((OWNERS, 2, BINS, 128), BF),
        united=((CELLS, 128), BF),
        logit_send=((CELLS, 512), BF),
        logit_recv=((SPLITS, 144, 512), BF),
        slope_in=((SPLITS, 144, 512), BF),
        d_f=((CELLS, 128), F32),
        d_f2=((CELLS, 128), F32),
        cat_u=((CELLS, 1152), BF),
        cat_a=((CELLS, 640), BF),
        dz_send=((9, BINS, 128), BF),
        dz_recv=((OWNERS, 2, BINS, 128), BF),
        d_act_send=((SPLITS, OWNERS * BINS, 128), BF),
        d_act_recv=((SPLITS, OWNERS * BINS, 128), BF),
        d_img_send=((OWNERS, BINS, 128), BF),
        d_img_recv=((OWNERS, BINS, 128), BF),
        d_bp=((SPLITS, BINS, 128), BF),
        dm_near=((2, CELLS, 512), BF),
        dm_far=((CELLS, 512), BF),
        d_sum=((CELLS, 512), F32),
        d_e=((CELLS, 512), BF),
        d_s=((CELLS, 512), BF),
        dh_send=((SPLITS, CELLS, 128), BF),
        dh_recv=((2, SPLITS, CELLS, 128), BF),
        d_low=((CELLS, 128), BF),
        end_t=((SPLITS, 8, 128), F32),
    )
    for name, rows in SYNCS.items():
        plan["sync_" + name] = ((OWNERS, rows, 128), F32)
    for name, (rows, lanes, kind) in PARTS.items():
        plan["first_" + name] = ((HALF, rows, lanes), kind)
        plan["second_" + name] = ((HALF - 1, rows, lanes), kind)
    plan["first_u"] = ((HALF, SLOTS, 512, 128), BF)
    plan["second_u"] = ((HALF - 1, SLOTS, 512, 128), BF)
    return plan


SYNCS = dict(one=8, two=8, three=16, five=8, aux=8, b1=8, b3=8, b4=16, b5=8, b6=8, end=8)
PARTS = dict(
    r=(128, 128, BF),
    s=(128, 512, BF),
    m=(576, 128, BF),
    e=(64, 512, BF),
    a=(576, 128, BF),
    c=(16, 256, BF),
    ac=(8, 256, F32),
)
SEMAPHORES = 1100
LOADS = (0, 128, 640, 1216, 1472, 2496, 7104, 7712)
LOAD_ORDER = (0, 2, 3, 1, 4, 6, 5)


class Refs:
    pass


def fold(value):
    return value.reshape(-1, 8, value.shape[-1]).sum(0)


def total(value):
    return jnp.sum(value, axis=0, keepdims=True)


def wide(value, times):
    return jnp.concatenate([value] * times, axis=1)


def dot(left, right):
    return jnp.dot(left, right, preferred_element_type=F32)


def dot_nt(left, right):
    return lax.dot_general(left, right, (((1,), (1,)), ((), ())), preferred_element_type=F32)


def dot_tn(left, right):
    return lax.dot_general(left, right, (((0,), (0,)), ((), ())), preferred_element_type=F32)


def loop(count, body):
    def step(k, carry):
        body(k)
        return carry

    lax.fori_loop(0, count, step, 0)


def rows_at(k, block):
    return pl.ds(pl.multiple_of(k * block, block), block)


def step_kernel(names, *refs):
    (
        sizes, lab_in, feat, flat, o_flat, o_shift, o_misc,
    ) = refs[:7]
    v = Refs()
    for name, ref in zip(names, refs[7:]):
        setattr(v, name, ref)
    sems = refs[-1]
    o_u = o_flat.at[2496:7104, :]
    me = lax.axis_index(BATCH)
    t = lax.axis_index(TENSOR)
    partner = me + 1 - 2 * lax.rem(me, 2)
    t_core = t + 1 - 2 * lax.rem(t, 2)
    t_x = lax.rem(t + 2, SPLITS)
    t_diag = lax.rem(t_core + 2, SPLITS)
    taken = [0]

    def take(count):
        start = taken[0]
        taken[0] = start + count
        assert taken[0] <= SEMAPHORES
        return start

    def far_peer(base, step):
        return lax.rem(base + 2 * step, OWNERS)

    def remote(src, dst, send, recv, device):
        return pltpu.make_async_remote_copy(
            src_ref=src,
            dst_ref=dst,
            send_sem=sems.at[send],
            recv_sem=sems.at[recv],
            device_id=device,
            device_id_type=MESH,
        )

    late = []

    load_at = take(len(LOADS))

    def load(index):
        at = pl.ds(LOADS[index], LOADS[index + 1] - LOADS[index])
        return pltpu.make_async_copy(flat.at[at, :], o_flat.at[at, :], sems.at[load_at + index])

    for index in LOAD_ORDER:
        load(index).start()
    v.pool_all[...] = jnp.zeros((OWNERS, BINS, 256), BF)
    v.d_bp_all[...] = jnp.zeros((OWNERS, SPLITS, BINS, 128), BF)
    barrier = pltpu.get_barrier_semaphore()
    for k in range(1, OWNERS):
        pl.semaphore_signal(
            barrier, inc=1, device_id={BATCH: lax.rem(me + k, OWNERS)}, device_id_type=MESH
        )
    for k in range(1, SPLITS):
        pl.semaphore_signal(
            barrier, inc=1, device_id={TENSOR: lax.rem(t + k, SPLITS)}, device_id_type=MESH
        )
    pl.semaphore_wait(barrier, OWNERS + SPLITS - 2)

    class Gather:
        def __init__(self, full, rows, skip=0, step=None, piece=None):
            self.full, self.rows, self.piece = full, rows, piece
            self.skip, self.part = skip, step or rows
            self.near_s, self.far_s, self.pass_s = take(1), take(HALF), take(HALF)
            self.recv, self.keep = take(OWNERS), take(1)

        def at(self, owner):
            if self.rows is None:
                return self.full.at[owner]
            start = pl.multiple_of(owner * self.rows + self.skip, self.part)
            return self.full.at[pl.ds(start, self.part), :]

        def source(self):
            return self.at(me) if self.piece is None else self.piece

        def local(self):
            return pltpu.make_async_copy(self.piece, self.at(me), sems.at[self.keep])

        def near(self):
            return remote(
                self.source(), self.at(me), self.near_s, self.recv + me, {BATCH: partner}
            )

        def far(self, step):
            return remote(
                self.source(),
                self.at(me),
                self.far_s + step,
                self.recv + me,
                {BATCH: far_peer(me, step)},
            )

        def passed(self, step, base):
            source = far_peer(base, step)
            return remote(
                self.at(source),
                self.at(source),
                self.pass_s + step,
                self.recv + source,
                {BATCH: partner},
            )

        def start_far(self):
            if self.piece is not None:
                self.local().start()
            for step in range(1, HALF):
                self.far(step).start()

        def start_near(self):
            self.near().start()

        def forward(self):
            for step in range(1, HALF):
                self.passed(step, me).wait_recv()
                self.passed(step, me).start()

        def finish(self):
            for step in range(HALF):
                self.passed(step, partner).wait_recv()
            if self.piece is not None:
                self.local().wait()
            self.near().wait_send()
            for step in range(1, HALF):
                self.far(step).wait_send()

        def drain(self):
            for step in range(1, HALF):
                self.passed(step, me).wait_send()

    g_gain = Gather(v.gain_in, None, piece=flat.at[7704:7712, :])
    g_r = Gather(v.w_r, 128)
    g_s = Gather(v.w_s, 128)
    g_a = Gather(v.w_a, 576)
    g_m = Gather(v.w_m, 576)
    g_e = Gather(v.w_e, 64)
    g_b0 = Gather(v.w_b, 256, 0, 128)
    g_b1 = Gather(v.w_b, 256, 128, 128)
    g_c = Gather(v.w_c, 16)
    g_ac = Gather(v.w_ac, 8)

    def block_of(owner, slot):
        return 8 if slot == SLOTS - 1 else lax.rem(slot - owner + 8, 8)

    def merged_rows(owner, slot):
        block = owner * 9 + block_of(owner, slot)
        index = lax.div(block, 8) * MERGED + lax.rem(block, 8)
        return pl.ds(pl.multiple_of(index * 512, 512), 512)

    def has(owner, slot, body):
        if slot == SLOTS - 1:
            pl.when(owner < MERGED)(body)
        else:
            body()

    class GatherUnite:
        def __init__(self):
            self.near_s, self.far_s, self.pass_s = (
                take(SLOTS),
                take(SLOTS * HALF),
                take(SLOTS * HALF),
            )
            self.recv, self.keep = take(SLOTS * OWNERS), take(SLOTS)

        def source(self, slot):
            return v.w_own.at[rows_at(block_of(me, slot), 512), :]

        def full(self, owner, slot):
            return v.w_u.at[merged_rows(owner, slot), :]

        def local(self, slot):
            return pltpu.make_async_copy(
                self.source(slot), self.full(me, slot), sems.at[self.keep + slot]
            )

        def near(self, slot):
            return remote(
                self.source(slot),
                self.full(me, slot),
                self.near_s + slot,
                self.recv + me * SLOTS + slot,
                {BATCH: partner},
            )

        def far(self, step, slot):
            return remote(
                self.source(slot),
                self.full(me, slot),
                self.far_s + step * SLOTS + slot,
                self.recv + me * SLOTS + slot,
                {BATCH: far_peer(me, step)},
            )

        def passed(self, step, slot, base):
            source = far_peer(base, step)
            return remote(
                self.full(source, slot),
                self.full(source, slot),
                self.pass_s + step * SLOTS + slot,
                self.recv + source * SLOTS + slot,
                {BATCH: partner},
            )

        def start_far(self, slot):
            def go():
                self.local(slot).start()
                for step in range(1, HALF):
                    self.far(step, slot).start()

            has(me, slot, go)

        def start_near(self, slot):
            has(me, slot, lambda: self.near(slot).start())

        def forward(self, slot):
            for step in range(1, HALF):

                def go(step=step):
                    self.passed(step, slot, me).wait_recv()
                    self.passed(step, slot, me).start()

                has(far_peer(me, step), slot, go)

        def finish(self):
            for slot in range(SLOTS):
                for step in range(HALF):
                    has(
                        far_peer(partner, step),
                        slot,
                        lambda step=step, slot=slot: self.passed(step, slot, partner).wait_recv(),
                    )

                def end(slot=slot):
                    self.local(slot).wait()
                    self.near(slot).wait_send()
                    for step in range(1, HALF):
                        self.far(step, slot).wait_send()

                has(me, slot, end)

        def drain(self):
            for slot in range(SLOTS):
                for step in range(1, HALF):
                    has(
                        far_peer(me, step),
                        slot,
                        lambda step=step, slot=slot: self.passed(step, slot, me).wait_send(),
                    )

    g_u = GatherUnite()

    class Sync:
        def __init__(self, buf):
            self.buf = buf
            self.send, self.recv = take(OWNERS), take(OWNERS)

        def copy(self, k, slot):
            return remote(
                self.buf.at[slot],
                self.buf.at[slot],
                self.send + k,
                self.recv + slot,
                {BATCH: lax.rem(me + k, OWNERS)},
            )

        def start(self, rows):
            for index, row in enumerate(rows):
                self.buf[me, index : index + 1, :] = row
            for index in range(len(rows), self.buf.shape[1]):
                self.buf[me, index : index + 1, :] = jnp.zeros((1, 128), F32)
            for k in range(1, OWNERS):
                self.copy(k, me).start()

        def wait(self):
            for k in range(1, OWNERS):
                self.copy(k, lax.rem(me + k, OWNERS)).wait_recv()
            for k in range(1, OWNERS):
                self.copy(k, me).wait_send()
            value = self.buf[0]
            for slot in range(1, OWNERS):
                value = value + self.buf[slot]
            return value

    class ToGroup:
        def __init__(self, part, into):
            self.part, self.into = part, into
            self.send, self.recv = take(OWNERS), take(OWNERS)

        def each(self, k, owner, slot, act):
            for rows, fits_ in ((16, owner < 6), (BINS, owner >= 6)):

                def go(rows=rows):
                    act(
                        remote(
                            self.part(owner, rows),
                            self.into(slot, rows),
                            self.send + k,
                            self.recv + slot,
                            {BATCH: lax.rem(me + k, OWNERS)},
                        )
                    )

                pl.when(fits_)(go)

        def start(self):
            for k in range(1, OWNERS):
                self.each(k, lax.rem(me + k, OWNERS), me, lambda c: c.start())

        def wait(self):
            for k in range(1, OWNERS):
                self.each(k, me, lax.rem(me + k, OWNERS), lambda c: c.wait_recv())
            for k in range(1, OWNERS):
                self.each(k, lax.rem(me + k, OWNERS), me, lambda c: c.wait_send())

    class Spread:

        def __init__(self, buf):
            self.buf = buf
            self.send, self.recv = take(SPLITS), take(SPLITS)

        def copy(self, k, slot):
            return remote(
                self.buf.at[slot],
                self.buf.at[slot],
                self.send + k,
                self.recv + slot,
                {TENSOR: lax.rem(t + k, SPLITS)},
            )

        def start(self):
            for k in range(1, SPLITS):
                self.copy(k, t).start()

        def wait(self):
            for k in range(1, SPLITS):
                self.copy(k, lax.rem(t + k, SPLITS)).wait_recv()
            for k in range(1, SPLITS):
                self.copy(k, t).wait_send()

    class Exchange:

        def __init__(self, axis, count, part, into):
            self.axis, self.count, self.part, self.into = axis, count, part, into
            self.mine = me if axis == BATCH else t
            self.send, self.recv = take(count), take(count)

        def copy(self, k, slot):
            other = lax.rem(self.mine + k, self.count)
            return remote(
                self.part(other),
                self.into(slot),
                self.send + k,
                self.recv + slot,
                {self.axis: other},
            )

        def start(self):
            for k in range(1, self.count):
                self.copy(k, self.mine).start()

        def wait(self):
            for k in range(1, self.count):
                self.copy(k, lax.rem(self.mine + k, self.count)).wait_recv()
            for k in range(1, self.count):
                self.copy(k, self.mine).wait_send()

    feat_keep = take(1)
    feat_local = pltpu.make_async_copy(feat, v.whole.at[t], sems.at[feat_keep])
    feat_spread = Exchange(TENSOR, SPLITS, lambda other: feat, lambda slot: v.whole.at[slot])
    def wide_rows(into, rows, low):
        for k in range(4):
            value = o_flat[pl.ds(low + k, rows, stride=4), :]
            into[rows_at(me, rows), k * 128 : k * 128 + 128] = value.astype(BF)

    load(0).wait()
    v.w_r[rows_at(me, 128), :] = o_flat[0:128, :].astype(BF)
    for item in (g_gain, g_r):
        item.start_far()
        item.start_near()
    feat_local.start()
    feat_spread.start()
    load(2).wait()
    v.w_m[rows_at(me, 576), :] = o_flat[640:1216, :].astype(BF)
    load(3).wait()
    wide_rows(v.w_e, 64, 1216)
    for item in (g_m, g_e):
        item.start_far()
        item.start_near()
    lane = lax.broadcasted_iota(jnp.int32, (1, 128), 1)

    def roll(value, shift):
        return pltpu.roll(value, shift % 128, 1) if shift % 128 else value

    high, across = sizes[0, 0], sizes[0, 1]
    place = lax.broadcasted_iota(jnp.int32, (CELLS, 128), 0).astype(F32)
    row_of = jnp.floor((place + 0.5) / MAP)
    col_of = place - MAP * row_of
    within = (row_of < high.astype(F32)) & (col_of < across.astype(F32))
    v.ins[...] = jnp.where(within, 1.0, 0.0)
    v.col[...] = col_of
    v.lab[...] = jnp.where(within, lab_in[...], -1.0)
    v.table[...] = jnp.zeros((BINS, CELLS), F32)
    lane_place = lax.broadcasted_iota(jnp.int32, (1, CELLS), 1).astype(F32)
    lane_row = jnp.floor((lane_place + 0.5) / MAP)
    lane_col = lane_place - MAP * lane_row

    def ranges(extent, bins, where):
        inside, chosen, counts = [], [], []
        for k in range(bins):
            low = lax.div(k * extent, bins)
            top = lax.div((k + 1) * extent + (bins - 1), bins)
            member = (where >= low.astype(F32)) & (where < top.astype(F32))
            inside.append(jnp.where(member, 1.0, 0.0))
            picked = where * bins >= (k * extent).astype(F32)
            if k < bins - 1:
                picked = picked & (where * bins < ((k + 1) * extent).astype(F32))
            chosen.append(jnp.where(picked, 1.0, 0.0))
            counts.append(top - low)
        return inside, chosen, counts

    picks = []
    v.cells_in[...] = jnp.ones((BINS, 128), F32)
    for group, bins in enumerate(BIN_COUNTS):
        r_in, r_pick, r_count = ranges(high, bins, lane_row)
        c_in, c_pick, c_count = ranges(across, bins, lane_col)
        for a in range(bins):
            for b in range(bins):
                spot = BIN_STARTS[group] + a * bins + b
                v.table[spot : spot + 1, :] = r_in[a] * c_in[b]
                v.cells_in[spot : spot + 1, :] = jnp.full(
                    (1, 128), (r_count[a] * c_count[b]).astype(F32)
                )
                picks.append((spot, r_pick[a] * c_pick[b]))
    v.pool[...] = v.table[...].astype(BF)
    for spot, value in picks:
        v.table[spot : spot + 1, :] = value
    v.pick[...] = v.table[...].astype(BF)
    zeros_edge = jnp.zeros((EDGE, 128), F32)
    for tap in range(9):
        v.pad[tap, 0:EDGE, :] = zeros_edge
        v.pad[tap, EDGE + CELLS :, :] = zeros_edge
    v.grad_pad[0:EDGE, :] = zeros_edge
    v.grad_pad[EDGE + CELLS :, :] = zeros_edge
    lanes = lax.broadcasted_iota(jnp.int32, (1, 256), 1).astype(F32)
    counts = jnp.zeros((8, 256), F32)
    for k in range(0, CELLS, 96):
        counts = counts + fold(
            jnp.where(wide(v.lab[k : k + 96, :], 2) == lanes, 1.0, 0.0)
        )
    class_local = total(counts)
    cells_local = jnp.full((1, 128), (high * across).astype(F32))
    left_half = lax.broadcasted_iota(jnp.int32, (64, 128), 1) < 64

    for item in (g_gain, g_r):
        item.forward()
    load(1).wait()
    wide_rows(v.w_s, 128, 128)
    load(4).wait()
    wide_rows(v.w_b, 256, 1472)
    load(6).wait()
    before = pltpu.roll(o_flat[7122:7698, :], 32, 1)
    after = pltpu.roll(o_flat[7123:7699, :], 32, 1)
    v.w_a[rows_at(me, 576), :] = jnp.where(lane < 32, before, after).astype(BF)

    def class_rows(count, base, into):
        for row in range(count):
            first, shift = divmod(base + NCLS * row, 128)
            three = [
                roll(o_flat[7104 + first + k : 7105 + first + k, :], 128 - shift) for k in range(3)
            ]
            into[row : row + 1, :128] = jnp.where(lane < 128 - shift, three[0], three[1])
            high_half = jnp.where(lane < 128 - shift, three[1], three[2])
            into[row : row + 1, 128:] = jnp.where(lane < NCLS - 128, high_half, 0.0)

    class_rows(16, 0, v.out_c)
    class_rows(8, 76128, v.out_ac)
    v.w_c[rows_at(me, 16), :] = v.out_c[...].astype(BF)
    v.w_ac[rows_at(me, 8), :] = v.out_ac[...].astype(BF).astype(F32)
    load(5).wait()

    def own_rows(j):
        at = pl.ds(pl.multiple_of(2496 + 512 * j, 64), 512)
        v.w_own[rows_at(j, 512), :] = o_flat[at, :].astype(BF)

    loop(9, own_rows)
    for item in (g_gain, g_r):
        item.finish()
    feat_local.wait()
    feat_spread.wait()
    gain_of = [None] * 33
    for owner in range(OWNERS):
        start = 496 * (owner % 4) - 16
        first, shift = start // 128, start % 128
        for k in range(4):
            value = v.gain_in[owner, 4 + k : 5 + k, :].astype(BF).astype(F32)
            if k == 0:
                value = jnp.where(lane < 16, 0.0, value)
            value = roll(value, shift)
            spot = 16 * (owner // 4) + first + k
            for where, part in (
                (spot, jnp.where(lane >= shift, value, 0.0)),
                (spot + 1, jnp.where(lane < shift, value, 0.0)),
            ):
                gain_of[where] = part if gain_of[where] is None else gain_of[where] + part

    def gamma(row, width=1):
        return jnp.concatenate([gain_of[row + k] for k in range(width)], axis=1)

    def beta(row, width=1):
        return gamma(16 + row, width)

    def whole_feat():
        return jnp.concatenate([v.whole[k] for k in range(SPLITS)], axis=1)

    v.pre_r[...] = dot(whole_feat(), v.w_r[...])
    def offset(tap, spacing):
        return ((tap // 3 - 1) * MAP + (tap % 3 - 1)) * spacing

    def col_mask(at, right):
        where = v.col[at, :] + float(right)
        return jnp.where((where >= 0.0) & (where < float(MAP)), 1.0, 0.0)

    BLOCK = 72

    def shift_sum(taps, spacing, at, slot_of):
        out = None
        for b in (-1, 0, 1):
            part = None
            for tap in taps:
                if tap % 3 - 1 != b:
                    continue
                start = EDGE + at + offset(tap, spacing)
                value = v.pad[slot_of(tap), start : start + BLOCK, :]
                part = value if part is None else part + value
            if part is None:
                continue
            if b:
                part = part * col_mask(slice(at, at + BLOCK), b * spacing)
            out = part if out is None else out + part
        return out

    def masked_sums(ref):
        width = ref.shape[1]

        def step(k, carry):
            at = rows_at(k, 96)
            value = ref[at, :]
            kept = value * (v.ins[at, :] if width == 128 else wide(v.ins[at, :], width // 128))
            return (carry[0] + fold(kept), carry[1] + fold(kept * value))

        zero = jnp.zeros((8, width), F32)
        sums = lax.fori_loop(0, 6, step, (zero, zero))
        return total(sums[0]), total(sums[1])

    def split_rows(value):
        return [value[:, k : k + 128] for k in range(0, value.shape[1], 128)]

    def join_rows(value, row, count):
        return jnp.concatenate([value[row + k : row + k + 1] for k in range(count)], axis=1)

    def moments(first, second, count):
        mean = first / count
        return mean, lax.rsqrt(second / count - mean * mean + 1e-05)

    sync = Sync(v.sync_one)
    r1, r2 = masked_sums(v.pre_r)
    sync.start([r1, r2, cells_local] + split_rows(class_local))
    g_m.forward()
    g_e.forward()
    g_s.start_far()
    sums = sync.wait()
    count = sums[2:3]
    count4 = wide(count, 4)
    norm_r = moments(sums[0:1], sums[1:2], count)
    class_count = join_rows(sums, 3, 2)

    def normed(ref, at, norm):
        return (ref[at, :] - norm[0]) * norm[1]

    spread_1 = Spread(v.h1)

    def make_h1(k):
        at = rows_at(k, 96)
        v.h1[t, at, :] = jax.nn.silu(gamma(0) * normed(v.pre_r, at, norm_r) + beta(0)).astype(BF)

    loop(6, make_h1)
    spread_1.start()
    g_s.start_near()
    g_b0.start_far()
    g_m.finish()
    spread_1.wait()

    def full_h(ref):
        return jnp.concatenate([ref[k] for k in range(SPLITS)], axis=1)

    def middle(tap):
        v.pad[tap, EDGE : EDGE + CELLS, :] = dot(full_h(v.h1), v.w_m[rows_at(tap, 512), :])

    loop(9, middle)
    for at in range(0, CELLS, BLOCK):
        v.pre_m[at : at + BLOCK, :] = shift_sum(range(9), 4, at, lambda tap: tap)
    sync = Sync(v.sync_two)
    sync.start(list(masked_sums(v.pre_m)))
    g_s.forward()
    g_b0.start_near()
    g_b1.start_far()
    sums = sync.wait()
    norm_m = moments(sums[0:1], sums[1:2], count)
    spread_2 = Spread(v.h2)

    def make_h2(k):
        at = rows_at(k, 96)
        v.h2[t, at, :] = jax.nn.silu(gamma(5) * normed(v.pre_m, at, norm_m) + beta(5)).astype(BF)

    loop(6, make_h2)
    spread_2.start()
    g_b0.forward()
    g_b1.start_near()
    g_u.start_far(0)
    g_e.finish()
    g_s.finish()
    for k in range(0, 512, 256):
        v.pre_s[:, k : k + 256] = dot(whole_feat(), v.w_s[:, k : k + 256])
    s1, s2 = masked_sums(v.pre_s)
    spread_2.wait()
    for k in range(0, 512, 256):
        v.pre_e[:, k : k + 256] = dot(full_h(v.h2), v.w_e[:, k : k + 256])
    sync = Sync(v.sync_three)
    e1, e2 = masked_sums(v.pre_e)
    sync.start(split_rows(e1) + split_rows(e2) + split_rows(s1) + split_rows(s2))
    g_b1.forward()
    g_u.start_near(0)
    g_u.start_far(1)
    for item in (g_c, g_ac):
        item.start_far()
        item.start_near()
    sums = sync.wait()
    norm_e = moments(join_rows(sums, 0, 4), join_rows(sums, 4, 4), count4)
    norm_s = moments(join_rows(sums, 8, 4), join_rows(sums, 12, 4), count4)

    def summed(at):
        return (
            gamma(6, 4) * normed(v.pre_e, at, norm_e)
            + beta(6, 4)
            + gamma(1, 4) * normed(v.pre_s, at, norm_s)
            + beta(1, 4)
        )

    def make_merged(k):
        at = rows_at(k, 48)
        v.joined[t, at, :] = jax.nn.silu(summed(at)).astype(BF)

    loop(12, make_merged)

    j_send, j_recv = take(3), take(SPLITS)

    def joined_copy(k, slot, device):
        return remote(
            v.joined.at[slot], v.joined.at[slot], j_send + k, j_recv + slot, {TENSOR: device}
        )

    joined_copy(0, t, t_x).start()
    joined_copy(1, t, t_core).start()

    pool_move = ToGroup(
        lambda owner, rows: v.pool_half.at[lax.rem(owner, 2), 0:rows, :],
        lambda slot, rows: v.pool_all.at[slot, 0:rows, :],
    )
    bin_row = lax.broadcasted_iota(jnp.int32, (BINS, 1), 0)

    def group_mask(group, shape=None):
        low, top = GROUP_ROWS[group]
        kept = jnp.where((bin_row >= low) & (bin_row < top), 1.0, 0.0)
        return kept if shape is None else jnp.broadcast_to(kept, shape)

    cells_in = wide(v.cells_in[...], 4)
    pooled = dot(v.pool[...], v.joined[t]) / cells_in
    v.pooled[...] = pooled.astype(BF)
    for k in range(2):
        v.pool_half[k] = v.pooled[:, k * 256 : k * 256 + 256]
    v.pool_all[me] = v.pool_half[lax.rem(me, 2)]
    g_b0.finish()
    g_b1.finish()
    part = jnp.zeros((BINS, 512), F32)
    for group in range(4):
        rows = (v.pooled[...].astype(F32) * group_mask(group)).astype(BF)
        part = part + dot(rows, v.w_b[group * 512 : group * 512 + 512, :])
    for k in range(SPLITS):
        v.part_b[k] = part[:, k * 128 : k * 128 + 128].astype(BF)
    v.recv_b[t] = v.part_b[t]
    ex = Exchange(TENSOR, SPLITS, lambda o: v.part_b.at[o], lambda s: v.recv_b.at[s])
    ex.start()
    g_u.forward(0)
    g_u.start_near(1)
    g_u.start_far(2)
    joined_copy(0, t_x, t_x).wait_recv()
    joined_copy(2, t_x, t_core).start()
    ex.wait()
    own_b = v.recv_b[0].astype(F32)
    for k in range(1, SPLITS):
        own_b = own_b + v.recv_b[k].astype(F32)
    v.all_b[me] = own_b.astype(BF)
    ex = Exchange(BATCH, OWNERS, lambda o: v.all_b.at[me], lambda s: v.all_b.at[s])
    ex.start()
    g_u.forward(1)
    g_u.start_near(2)
    g_u.start_far(3)
    ex.wait()
    all_b = [v.all_b[k].astype(F32) for k in range(OWNERS)]
    sum_b, square_b = all_b[0], all_b[0] * all_b[0]
    for k in range(1, OWNERS):
        sum_b = sum_b + all_b[k]
        square_b = square_b + all_b[k] * all_b[k]
    mean_b = jnp.zeros((BINS, 128), F32)
    scale_b = jnp.zeros((BINS, 128), F32)
    gamma_b = jnp.zeros((BINS, 128), F32)
    beta_b = jnp.zeros((BINS, 128), F32)
    count_b = jnp.zeros((BINS, 1), F32)
    for group, bins in enumerate(BIN_COUNTS):
        kept = group_mask(group)
        size = float(OWNERS * bins * bins)
        mean, scaling = moments(total(sum_b * kept), total(square_b * kept), size)
        mean_b = mean_b + kept * mean
        scale_b = scale_b + kept * scaling
        gamma_b = gamma_b + kept * gamma(10 + group)
        beta_b = beta_b + kept * beta(10 + group)
        count_b = count_b + kept / size
    spread_b = Spread(v.act_b)
    for k in range(OWNERS):
        out = gamma_b * ((all_b[k] - mean_b) * scale_b) + beta_b
        v.act_b[t, k * BINS : k * BINS + BINS, :] = jax.nn.silu(out).astype(BF)
    spread_b.start()
    g_u.forward(2)
    g_u.start_near(3)
    g_u.start_far(4)
    spread_b.wait()
    row_512 = lax.broadcasted_iota(jnp.int32, (OWNERS * BINS, 1), 0) & (BINS - 1)
    group_id = jnp.where(
        row_512 < 1, 0, jnp.where(row_512 < 5, 1, jnp.where(row_512 < 14, 2, jnp.where(row_512 < 50, 3, 9)))
    )

    def full_act():
        return jnp.concatenate([v.act_b[k] for k in range(SPLITS)], axis=1)

    v.zsum[...] = jnp.zeros((2, OWNERS * BINS, 128), F32)

    def own_branch(j, body):
        chunk = lax.rem(me + j, 8)
        pl.when(chunk >= MERGED)(lambda: body(chunk - MERGED, lax.div(me + j, 8)))

    def make_z(j):
        def body(group, side):
            kept = jnp.where(group_id == group, 1.0, 0.0)
            rows = (full_act().astype(F32) * kept).astype(BF)
            v.zsum[side] = v.zsum[side] + dot(rows, v.w_own[rows_at(j, 512), :])

        own_branch(j, body)

    loop(9, make_z)
    for k in range(OWNERS):
        for side in range(2):
            v.z_send[k, side] = v.zsum[side, k * BINS : k * BINS + BINS, :].astype(BF)
    v.z_recv[me] = v.z_send[me]
    ex = Exchange(BATCH, OWNERS, lambda o: v.z_send.at[o], lambda s: v.z_recv.at[s])
    ex.start()
    g_u.forward(3)
    g_u.start_near(4)
    g_a.start_far()
    joined_copy(1, t_core, t_core).wait_recv()
    joined_copy(2, t_diag, t_core).wait_recv()
    for k in range(SPLITS):
        v.joined_t[k] = v.joined[k].T
    g_u.forward(4)
    g_a.start_near()
    g_c.forward()
    g_ac.forward()
    ex.wait()
    g_u.finish()
    g_a.forward()

    pick2 = jnp.concatenate([v.pick[...], v.pick[...]], axis=0)

    def tap_z(tap):
        if tap == 0:
            return v.z_recv[0, 0].astype(F32)
        if tap == 8:
            return v.z_recv[7, 1].astype(F32)
        return v.z_recv[tap, 0].astype(F32) + v.z_recv[tap - 1, 1].astype(F32)

    def full_joined():
        return jnp.concatenate([v.joined[k] for k in range(SPLITS)], axis=1)

    def w_tap(tap):
        return v.w_u[rows_at(tap, 2048), :]

    def unite_pair(p):
        value = dot(full_joined(), jnp.concatenate([w_tap(2 * p), w_tap(2 * p + 1)], axis=1))
        v.pad[2 * p, EDGE : EDGE + CELLS, :] = value[:, :128]
        v.pad[2 * p + 1, EDGE : EDGE + CELLS, :] = value[:, 128:]

    loop(4, unite_pair)
    v.pad[8, EDGE : EDGE + CELLS, :] = dot(full_joined(), w_tap(8))
    for tap in range(9):
        z = tap_z(tap)
        high_z = z.astype(BF)
        low_z = (z - high_z.astype(F32)).astype(BF)
        v.pad[tap, EDGE : EDGE + CELLS, :] = v.pad[tap, EDGE : EDGE + CELLS, :] + dot_tn(
            pick2, jnp.concatenate([high_z, low_z], axis=0)
        )
    for at in range(0, CELLS, BLOCK):
        v.pre_u[at : at + BLOCK, :] = shift_sum(range(9), 1, at, lambda tap: tap)
    sync = Sync(v.sync_five)
    sync.start(list(masked_sums(v.pre_u)))
    pool_move.start()
    for item in (g_a, g_c, g_ac):
        item.finish()

    def unpack(chunk):
        for pair in range(5):
            even = v.w_a[rows_at(2 * pair * 8 + chunk, 64), :].astype(F32)
            if pair < 4:
                odd = v.w_a[rows_at((2 * pair + 1) * 8 + chunk, 64), :].astype(F32)
            else:
                odd = jnp.zeros((64, 128), F32)
            low = jnp.where(left_half, even, pltpu.roll(odd, 64, 1))
            top = jnp.where(left_half, pltpu.roll(even, 64, 1), odd)
            v.pad[pair, pl.ds(EDGE, 64, stride=2), :] = low
            v.pad[pair, pl.ds(EDGE + 1, 64, stride=2), :] = top
            both = v.pad[pair, EDGE : EDGE + 128, :]
            v.w_pair[rows_at(chunk, 128), pair * 128 : pair * 128 + 128] = both.astype(BF)

    loop(8, unpack)

    for pair in (0, 2):
        value = dot(whole_feat(), v.w_pair[:, pair * 128 : pair * 128 + 256])
        v.pad[pair, EDGE : EDGE + CELLS, :] = value[:, :128]
        v.pad[pair + 1, EDGE : EDGE + CELLS, :] = value[:, 128:]
    v.pad[4, EDGE : EDGE + CELLS, :] = dot(whole_feat(), v.w_pair[:, 512:640])

    left_wide = lax.broadcasted_iota(jnp.int32, (BLOCK, 128), 1) < 64
    for at in range(0, CELLS, BLOCK):
        even = shift_sum((0, 2, 4, 6, 8), 1, at, lambda tap: tap // 2)
        odd = shift_sum((1, 3, 5, 7), 1, at, lambda tap: tap // 2)
        v.pre_a[at : at + BLOCK, :] = jnp.where(left_wide, even + pltpu.roll(odd, 64, 1), 0.0)

    sync_a = Sync(v.sync_aux)
    sync_a.start(list(masked_sums(v.pre_a)))
    for item in (g_gain, g_r, g_s, g_a, g_m, g_e, g_b0, g_b1, g_c, g_ac, g_u):
        item.drain()
    joined_copy(0, t, t_x).wait_send()
    joined_copy(1, t, t_core).wait_send()
    joined_copy(2, t_x, t_core).wait_send()
    w_ac = jnp.concatenate([v.w_ac[...], jnp.zeros((64, 256), F32)], axis=0).astype(BF)
    sums = sync.wait()
    norm_u = moments(sums[0:1], sums[1:2], count)

    def make_u(k):
        at = rows_at(k, 96)
        v.united[at, :] = jax.nn.silu(gamma(14) * normed(v.pre_u, at, norm_u) + beta(14)).astype(BF)

    loop(6, make_u)
    v.logit_send[:, :256] = dot(v.united[...], v.w_c[...]).astype(BF)
    sums = sync_a.wait()
    norm_a = moments(sums[0:1], sums[1:2], count)

    def make_a(k):
        at = rows_at(k, 96)
        v.act_a[at, :] = jax.nn.silu(gamma(15) * normed(v.pre_a, at, norm_a) + beta(15)).astype(BF)

    loop(6, make_a)

    v.logit_send[:, 256:] = dot(v.act_a[...], w_ac).astype(BF)
    ex = Exchange(
        TENSOR,
        SPLITS,
        lambda o: v.logit_send.at[rows_at(o, 144), :],
        lambda s: v.logit_recv.at[s],
    )
    ex.start()
    v.logit_recv[t] = v.logit_send[rows_at(t, 144), :]
    total_valid = jnp.sum(class_count, axis=1, keepdims=True)
    class_weight = total_valid / (NCLS * class_count + total_valid)
    loss_weight = jnp.sum(class_count * class_weight, axis=1, keepdims=True)
    class_weight = jnp.where(lanes < float(NCLS), class_weight, 0.0)
    hot = jnp.where(wide(v.lab[rows_at(t, 144), :], 2) == lanes, 1.0, 0.0)
    cell_weight = jnp.sum(hot * class_weight, axis=1, keepdims=True)
    ex.wait()
    logits = v.logit_recv[0].astype(F32)
    for k in range(1, SPLITS):
        logits = logits + v.logit_recv[k].astype(F32)

    def log_softmax(value):
        value = jnp.where(lanes < float(NCLS), value, -1e30)
        value = value - jnp.max(value, axis=1, keepdims=True)
        powers = jnp.exp(value)
        mass = jnp.sum(powers, axis=1, keepdims=True)
        return value - jnp.log(mass), powers / mass

    log_main, p_main = log_softmax(logits[:, :256])
    log_aux, p_aux = log_softmax(logits[:, 256:])
    loss_rows = total(fold(-cell_weight * hot * (log_main + 0.4 * log_aux)))
    loss_local = loss_rows[:, :128] + loss_rows[:, 128:]
    o_misc[1:2, :] = loss_local
    v.slope_in[t, :, :256] = (cell_weight * (p_main - hot) / loss_weight).astype(BF)
    v.slope_in[t, :, 256:] = (0.4 * cell_weight * (p_aux - hot) / loss_weight).astype(BF)
    spread_g = Spread(v.slope_in)
    spread_g.start()
    spread_g.wait()
    g_main = v.slope_in[:, :, :256].reshape(CELLS, 256)
    g_aux = v.slope_in[:, :, 256:].reshape(CELLS, 256)
    v.d_f[...] = dot_nt(g_main, v.w_c[...])
    v.d_f2[...] = dot_nt(g_aux, w_ac)

    def slope(value):
        gate = jax.nn.sigmoid(value)
        return gate * (1.0 + value * (1.0 - gate))

    def through_silu(ref, pre, norm, row):
        def step(k, carry):
            at = rows_at(k, 96)
            unit = normed(pre, at, norm)
            value = ref[at, :] * slope(gamma(row) * unit + beta(row))
            ref[at, :] = value
            return (carry[0] + fold(value), carry[1] + fold(value * unit))

        zero = jnp.zeros((8, 128), F32)
        sums = lax.fori_loop(0, 6, step, (zero, zero))
        return [total(sums[0]), total(sums[1])]

    def back_norm(value, unit, mask, norm, gain, first, second, size):
        inner = value - mask * (first + unit * second) / size
        return gain * norm[1] * inner

    gain_grads = {}
    sync = Sync(v.sync_b1)
    sync.start(
        through_silu(v.d_f, v.pre_u, norm_u, 14) + through_silu(v.d_f2, v.pre_a, norm_a, 15)
    )

    class Scatter:
        def __init__(self, first, second, full, rows, out, base=0):
            self.full, self.rows, self.out, self.base = full, rows, out, base
            self.first, self.second = first, second
            self.near_s, self.near_r = take(HALF), take(HALF)
            self.far_s, self.far_r = take(HALF), take(HALF)
            self.block = min(rows, 64)

        def near(self, step):
            dest = far_peer(partner, step)
            return remote(
                self.full.at[rows_at(dest, self.rows), :],
                self.first.at[step],
                self.near_s + step,
                self.near_r + step,
                {BATCH: partner},
            )

        def far(self, step):
            return remote(
                self.first.at[step],
                self.second.at[step - 1],
                self.far_s + step,
                self.far_r + step,
                {BATCH: far_peer(me, step)},
            )

        def start(self):
            for step in (1, 2, 3, 0):
                self.near(step).start()

        def middle(self):
            kind = self.first.dtype
            for step in range(1, HALF):
                self.near(step).wait_recv()
                base = far_peer(me, step) * (self.rows // self.block)

                def add(k, step=step, base=base):
                    at = rows_at(k, self.block)
                    value = self.full[rows_at(base + k, self.block), :].astype(F32)
                    value = value + self.first[step, at, :].astype(F32)
                    self.first[step, at, :] = value.astype(kind)

                loop(self.rows // self.block, add)
                self.far(step).start()

        def end(self):
            self.near(0).wait_recv()
            for step in range(1, HALF):
                self.far(step).wait_recv()
            base = me * (self.rows // self.block)

            def add(k, carry):
                at = rows_at(k, self.block)
                value = self.full[rows_at(base + k, self.block), :].astype(F32)
                value = value + self.first[0, at, :].astype(F32)
                for step in range(1, HALF):
                    value = value + self.second[step - 1, at, :].astype(F32)
                if self.out is o_flat:
                    times = value.shape[1] // 128
                    start = self.base + k * self.block * times
                    for q in range(times):
                        where = pl.ds(start + q, self.block, stride=times if times > 1 else None)
                        self.out[where, :] = value[:, q * 128 : q * 128 + 128]
                else:
                    self.out[at, :] = value
                return carry + fold(value * value)

            squares = lax.fori_loop(
                0, self.rows // self.block, add, jnp.zeros((8, self.full.shape[1]), F32)
            )
            for step in (1, 2, 3, 0):
                self.near(step).wait_send()
                if step:
                    self.far(step).wait_send()
            return sum(split_rows(total(squares)))

    s_c = Scatter(v.first_c, v.second_c, v.w_c, 16, v.out_c)
    s_ac = Scatter(v.first_ac, v.second_ac, v.w_ac, 8, v.out_ac)
    s_a = Scatter(v.first_a, v.second_a, v.w_a, 576, v.out_a)
    s_s = Scatter(v.first_s, v.second_s, v.w_s, 128, o_flat, 128)
    s_e = Scatter(v.first_e, v.second_e, v.w_e, 64, o_flat, 1216)
    s_m = Scatter(v.first_m, v.second_m, v.w_m, 576, o_flat, 640)
    s_r = Scatter(v.first_r, v.second_r, v.w_r, 128, o_flat, 0)

    class ScatterUnite:
        def __init__(self):
            self.near_s, self.near_r = take(SLOTS * HALF), take(SLOTS * HALF)
            self.far_s, self.far_r = take(SLOTS * HALF), take(SLOTS * HALF)

        def near(self, step, slot, base):
            dest = far_peer(base, step)
            return remote(
                v.w_u.at[merged_rows(dest, slot), :],
                v.first_u.at[step, slot],
                self.near_s + step * SLOTS + slot,
                self.near_r + step * SLOTS + slot,
                {BATCH: partner},
            )

        def far(self, step, slot):
            return remote(
                v.first_u.at[step, slot],
                v.second_u.at[step - 1, slot],
                self.far_s + step * SLOTS + slot,
                self.far_r + step * SLOTS + slot,
                {BATCH: far_peer(me, step)},
            )

        def own_rows(self, owner, slot, k):
            block = owner * 9 + block_of(owner, slot)
            index = lax.div(block, 8) * MERGED + lax.rem(block, 8)
            return rows_at(index * 8 + k, 64)

        def start(self, slot):
            for step in (1, 2, 3, 0):
                has(
                    far_peer(partner, step),
                    slot,
                    lambda step=step: self.near(step, slot, partner).start(),
                )

        def middle(self, slot):
            for step in range(1, HALF):
                owner = far_peer(me, step)

                def go(step=step, owner=owner):
                    self.near(step, slot, me).wait_recv()

                    def add(k):
                        at = rows_at(k, 64)
                        value = v.w_u[self.own_rows(owner, slot, k), :].astype(F32)
                        value = value + v.first_u[step, slot, at, :].astype(F32)
                        v.first_u[step, slot, at, :] = value.astype(BF)

                    loop(8, add)
                    self.far(step, slot).start()

                has(owner, slot, go)

        def end(self):
            for slot in range(SLOTS):

                def go(slot=slot):
                    self.near(0, slot, me).wait_recv()
                    for step in range(1, HALF):
                        self.far(step, slot).wait_recv()
                    j = block_of(me, slot)

                    def add(k):
                        at = rows_at(k, 64)
                        value = v.w_u[self.own_rows(me, slot, k), :].astype(F32)
                        value = value + v.first_u[0, slot, at, :].astype(F32)
                        for step in range(1, HALF):
                            value = value + v.second_u[step - 1, slot, at, :].astype(F32)
                        o_u[rows_at(j * 8 + k, 64), :] = value

                    loop(8, add)

                has(me, slot, go)
                for step in (1, 2, 3, 0):
                    has(
                        far_peer(partner, step),
                        slot,
                        lambda step=step, slot=slot: self.near(step, slot, partner).wait_send(),
                    )
                    if step:
                        has(
                            far_peer(me, step),
                            slot,
                            lambda step=step, slot=slot: self.far(step, slot).wait_send(),
                        )

            def square(k, carry):
                value = o_u[rows_at(k, 64), :]
                return carry + fold(value * value)

            squares = lax.fori_loop(0, 72, square, jnp.zeros((8, 128), F32))
            return sum(split_rows(total(squares)))

    s_u = ScatterUnite()

    v.w_c[...] = dot_tn(v.united[...], g_main).astype(BF)
    v.w_ac[...] = dot_tn(v.act_a[...], g_aux)[:64]
    s_c.start()
    s_ac.start()
    sums = sync.wait()
    gain_grads[14] = (sums[1:2], sums[0:1])
    gain_grads[15] = (sums[3:4], sums[2:3])

    def spread_taps(ref, pre, norm, row, first, second):
        def step(k):
            at = rows_at(k, 96)
            value = back_norm(
                ref[at, :], normed(pre, at, norm), v.ins[at, :], norm, gamma(row), first, second, count
            )
            ref[at, :] = value.astype(BF).astype(F32)

        loop(6, step)
        v.grad_pad[EDGE : EDGE + CELLS, :] = ref[...]

    def back_tap(tap, spacing, at):
        start = EDGE + at - offset(tap, spacing)
        value = v.grad_pad[start : start + 96, :]
        right = tap % 3 - 1
        if right:
            value = value * col_mask(slice(at, at + 96), -right * spacing)
        return value

    def fill(cat, spacing):
        for tap in range(9):
            for at in range(0, CELLS, 96):
                cat[at : at + 96, tap * 128 : tap * 128 + 128] = back_tap(tap, spacing, at).astype(
                    BF
                )

    spread_taps(v.d_f, v.pre_u, norm_u, 14, sums[0:1], sums[1:2])
    fill(v.cat_u, 1)

    dz = dot(v.pick[...], v.cat_u[...])
    for tap in range(9):
        v.dz_send[tap] = dz[:, tap * 128 : tap * 128 + 128].astype(BF)
    v.dz_recv[me] = v.dz_send[pl.ds(me, 2)]
    ex_dz = Exchange(
        BATCH, OWNERS, lambda o: v.dz_send.at[pl.ds(o, 2)], lambda s: v.dz_recv.at[s]
    )
    ex_dz.start()

    def merged_back(c):
        weight = jnp.concatenate(
            [v.w_u[rows_at(tap * MERGED + c, 512), :] for tap in range(9)], axis=1
        )
        v.joined[c] = dot_nt(v.cat_u[...], weight).astype(BF)

    near_s, near_r, far_s, far_r = take(2), take(2), take(1), take(1)

    def dm_near(k, slot):
        return remote(
            v.joined.at[slot], v.dm_near.at[k], near_s + k, near_r + k, {TENSOR: t_core}
        )

    merged_back(t_diag)
    dm_near(1, t_diag).start()
    merged_back(t_core)
    dm_near(0, t_core).start()
    ex_dz.wait()

    d_act = v.d_sum.at[0 : OWNERS * BINS, :]
    d_act[...] = jnp.zeros((OWNERS * BINS, 512), F32)

    def branch_back(j):
        def body(group, side):
            kept = jnp.where(group_id == group, 1.0, 0.0)
            value = v.dz_recv[:, side].reshape(OWNERS * BINS, 128).astype(F32) * kept
            value = value.astype(BF)
            o_u[rows_at(j, 512), :] = dot_tn(full_act(), value)
            d_act[...] = d_act[...] + dot_nt(value, v.w_own[rows_at(j, 512), :])

        own_branch(j, body)

    loop(9, branch_back)
    for k in range(SPLITS):
        v.d_act_send[k] = d_act[:, k * 128 : k * 128 + 128].astype(BF)
    v.d_act_recv[t] = v.d_act_send[t]
    ex = Exchange(TENSOR, SPLITS, lambda o: v.d_act_send.at[o], lambda s: v.d_act_recv.at[s])
    ex.start()
    merged_back(t_x)
    merged_back(t)

    def unite_grad(c):
        for p in range(5):
            width = 256 if p < 4 else 128
            value = dot(v.joined_t[c], v.cat_u[:, p * 256 : p * 256 + width])
            v.w_u[rows_at(2 * p * MERGED + c, 512), :] = value[:, :128].astype(BF)
            if p < 4:
                v.w_u[rows_at((2 * p + 1) * MERGED + c, 512), :] = value[:, 128:].astype(BF)

    loop(SPLITS, unite_grad)
    s_u.start(0)
    dm_near(1, t_x).wait_recv()

    def add_x(k):
        at = rows_at(k, 48)
        value = v.joined[t_x, at, :].astype(F32) + v.dm_near[1, at, :].astype(F32)
        v.joined[t_x, at, :] = value.astype(BF)

    loop(12, add_x)
    dm_far = remote(v.joined.at[t_x], v.dm_far, far_s, far_r, {TENSOR: t_x})
    ex.wait()
    for k in range(OWNERS):
        at = slice(k * BINS, k * BINS + BINS)
        value = v.d_act_recv[0, at, :].astype(F32)
        for slot in range(1, SPLITS):
            value = value + v.d_act_recv[slot, at, :].astype(F32)
        v.d_img_send[k] = value.astype(BF)
    v.d_img_recv[me] = v.d_img_send[me]
    ex = Exchange(BATCH, OWNERS, lambda o: v.d_img_send.at[o], lambda s: v.d_img_recv.at[s])
    ex.start()
    dm_far.start()
    s_u.start(1)

    spread_taps(v.d_f2, v.pre_a, norm_a, 15, sums[2:3], sums[3:4])
    for p in range(5):
        for at in range(0, CELLS, 96):
            value = back_tap(2 * p, 1, at)
            if p < 4:
                value = value + pltpu.roll(back_tap(2 * p + 1, 1, at), 64, 1)
            v.cat_a[at : at + 96, p * 128 : p * 128 + 128] = value.astype(BF)

    def aux_grad(c2):
        value2 = dot_tn(v.whole[c2], v.cat_a[...])
        for half in range(2):
            value = value2[half * 128 : half * 128 + 128]
            c = 2 * c2 + half
            for p in range(5):
                v.pad[p, EDGE : EDGE + 128, :] = value[:, p * 128 : p * 128 + 128]
                low = v.pad[p, pl.ds(EDGE, 64, stride=2), :]
                top = v.pad[p, pl.ds(EDGE + 1, 64, stride=2), :]
                even = jnp.where(left_half, low, pltpu.roll(top, 64, 1))
                v.w_a[rows_at(2 * p * 8 + c, 64), :] = even.astype(BF)
                if p < 4:
                    odd = jnp.where(left_half, pltpu.roll(low, 64, 1), top)
                    v.w_a[rows_at((2 * p + 1) * 8 + c, 64), :] = odd.astype(BF)

    loop(SPLITS, aux_grad)
    s_u.middle(0)
    ex.wait()
    d_b = v.d_img_recv[0].astype(F32)
    for k in range(1, OWNERS):
        d_b = d_b + v.d_img_recv[k].astype(F32)
    unit_b = (v.all_b[me].astype(F32) - mean_b) * scale_b
    d_b = d_b * slope(gamma_b * unit_b + beta_b)
    sync = Sync(v.sync_b3)
    sync.start(
        [total(d_b * group_mask(g)) for g in range(4)]
        + [total(d_b * unit_b * group_mask(g)) for g in range(4)]
    )
    s_u.start(2)
    sums = sync.wait()
    first_b = jnp.zeros((BINS, 128), F32)
    second_b = jnp.zeros((BINS, 128), F32)
    for group in range(4):
        kept = group_mask(group)
        gain_grads[10 + group] = (sums[4 + group : 5 + group], sums[group : group + 1])
        first_b = first_b + kept * sums[group : group + 1]
        second_b = second_b + kept * sums[4 + group : 5 + group]
    inner = d_b - (first_b + unit_b * second_b) * count_b
    v.d_bp[t] = (gamma_b * scale_b * inner).astype(BF)
    spread_d = Spread(v.d_bp)
    spread_d.start()
    s_u.start(3)
    s_u.middle(1)
    spread_d.wait()
    d_bp_move = ToGroup(
        lambda owner, rows: v.d_bp.at[:, 0:rows, :],
        lambda slot, rows: v.d_bp_all.at[slot, :, 0:rows, :],
    )
    d_bp_move.start()
    v.d_bp_all[me] = v.d_bp[...]
    d_bp = jnp.concatenate([v.d_bp[k] for k in range(SPLITS)], axis=1)
    d_pooled = jnp.zeros((BINS, 512), F32)
    for group in range(4):
        rows = (d_bp.astype(F32) * group_mask(group)).astype(BF)
        d_pooled = d_pooled + dot_nt(rows, v.w_b[group * 512 : group * 512 + 512, :])
    d_pooled = (d_pooled / cells_in).astype(BF)
    v.d_sum[...] = dot_tn(v.pool[...], d_pooled)
    dm_near(0, t).wait_recv()
    dm_far.wait_recv()

    def through_sum(k, carry):
        at = rows_at(k, 48)
        value = v.d_sum[at, :] + v.joined[t, at, :].astype(F32) + v.dm_near[0, at, :].astype(F32)
        value = (value + v.dm_far[at, :].astype(F32)) * slope(summed(at))
        v.d_sum[at, :] = value
        return (
            carry[0] + fold(value),
            carry[1] + fold(value * normed(v.pre_e, at, norm_e)),
            carry[2] + fold(value * normed(v.pre_s, at, norm_s)),
        )

    zero = jnp.zeros((8, 512), F32)
    three = [total(item) for item in lax.fori_loop(0, 12, through_sum, (zero, zero, zero))]
    sync = Sync(v.sync_b4)
    sync.start(split_rows(three[0]) + split_rows(three[1]) + split_rows(three[2]))
    s_u.start(4)
    s_u.middle(2)
    sums = sync.wait()
    first_s = join_rows(sums, 0, 4)
    second_e, second_s = join_rows(sums, 4, 4), join_rows(sums, 8, 4)
    for k in range(4):
        gain_grads[6 + k] = (sums[4 + k : 5 + k], sums[k : k + 1])
        gain_grads[1 + k] = (sums[8 + k : 9 + k], sums[k : k + 1])

    def back_both(k):
        at = rows_at(k, 48)
        value, mask = v.d_sum[at, :], wide(v.ins[at, :], 4)
        v.d_e[at, :] = back_norm(
            value, normed(v.pre_e, at, norm_e), mask, norm_e, gamma(6, 4), first_s, second_e, count4
        ).astype(BF)
        v.d_s[at, :] = back_norm(
            value, normed(v.pre_s, at, norm_s), mask, norm_s, gamma(1, 4), first_s, second_s, count4
        ).astype(BF)

    loop(12, back_both)

    def back_hidden(grad, weight, index):
        value = dot_nt(grad, weight)
        for k in range(SPLITS):
            v.dh_send[k] = value[:, k * 128 : k * 128 + 128].astype(BF)
        v.dh_recv[index, t] = v.dh_send[t]
        ex = Exchange(
            TENSOR, SPLITS, lambda o: v.dh_send.at[o], lambda s: v.dh_recv.at[index, s]
        )
        ex.start()
        return ex

    def hidden_sum(index):
        def step(k):
            at = rows_at(k, 96)
            value = v.dh_recv[index, 0, at, :].astype(F32)
            for slot in range(1, SPLITS):
                value = value + v.dh_recv[index, slot, at, :].astype(F32)
            v.d_f[at, :] = value

        loop(6, step)

    ex = back_hidden(v.d_e[...], v.w_e[...], 0)
    s_a.start()
    s_u.middle(3)
    for k in range(SPLITS):
        v.w_e[k * 128 : k * 128 + 128, :] = dot_tn(v.h2[k], v.d_e[...]).astype(BF)
    ex.wait()
    hidden_sum(0)
    sync = Sync(v.sync_b5)
    sync.start(through_silu(v.d_f, v.pre_m, norm_m, 5))
    s_e.start()
    s_c.middle()
    s_ac.middle()
    s_u.middle(4)
    sums = sync.wait()
    gain_grads[5] = (sums[1:2], sums[0:1])
    spread_taps(v.d_f, v.pre_m, norm_m, 5, sums[0:1], sums[1:2])
    fill(v.cat_u, 4)
    weight = jnp.concatenate([v.w_m[tap * 512 : tap * 512 + 512, :] for tap in range(9)], axis=1)
    ex = back_hidden(v.cat_u[...], weight, 1)

    def short_grad(c):
        v.w_s[rows_at(c, 256), :] = dot_tn(v.whole[c], v.d_s[...]).astype(BF)

    loop(SPLITS, short_grad)
    s_s.start()
    s_a.middle()
    ex.wait()
    hidden_sum(1)
    sync = Sync(v.sync_b6)
    sync.start(through_silu(v.d_f, v.pre_r, norm_r, 0))

    def middle_grad(k):
        value = dot_tn(v.h1[k], v.cat_u[...])
        for tap in range(9):
            v.w_m[rows_at(tap * 4 + k, 128), :] = value[:, tap * 128 : tap * 128 + 128].astype(BF)

    loop(SPLITS, middle_grad)
    s_m.start()
    s_e.middle()
    s_s.middle()
    sums = sync.wait()
    gain_grads[0] = (sums[1:2], sums[0:1])

    def back_reduce(k):
        at = rows_at(k, 96)
        v.d_low[at, :] = back_norm(
            v.d_f[at, :], normed(v.pre_r, at, norm_r), v.ins[at, :], norm_r, gamma(0), sums[0:1], sums[1:2], count
        ).astype(BF)

    loop(6, back_reduce)

    def reduce_grad(c):
        v.w_r[rows_at(c, 256), :] = dot_tn(v.whole[c], v.d_low[...]).astype(BF)

    loop(SPLITS, reduce_grad)
    s_r.start()
    for item in (s_m, s_r):
        item.middle()
    pool_move.wait()
    d_bp_move.wait()
    own_group = jnp.where(group_id == lax.div(me, 2), 1.0, 0.0)
    d_rows = jnp.concatenate(
        [v.d_bp_all[:, k].reshape(OWNERS * BINS, 128) for k in range(SPLITS)], axis=1
    )
    d_rows = (d_rows.astype(F32) * own_group).astype(BF)
    branch_grad = dot_tn(v.pool_all[...].reshape(OWNERS * BINS, 256), d_rows)
    for k in range(4):
        o_flat[pl.ds(1472 + k, 256, stride=4), :] = branch_grad[:, k * 128 : k * 128 + 128]
    rest = (s_c, s_ac, s_a, s_e, s_s, s_m, s_r)
    squares = s_u.end() + sum(split_rows(total(branch_grad * branch_grad)))
    for item in rest:
        squares = squares + item.end()
    dm_near(1, t_diag).wait_send()
    dm_near(0, t_core).wait_send()
    dm_far.wait_send()

    v.gain_rows[...] = jnp.zeros((40, 128), F32)
    gammas = [gain_grads[row][0] for row in range(16)]
    betas = [pltpu.roll(gain_grads[row][1], 64, 1) for row in range(16)]
    o_shift[...] = gain_grads[14][1]
    for row in range(31):
        if row < 15:
            value = gammas[row]
        else:
            left = gammas[15] if row == 15 else betas[row - 16]
            value = jnp.where(lane < 64, left, betas[row - 15])
        v.gain_rows[row + 1 : row + 2, :] = value
    squares = squares + total(fold(v.gain_rows[...] * v.gain_rows[...])) / OWNERS

    sync = Sync(v.sync_end)
    sync.start([squares, o_misc[1:2, :]])

    tail = {}

    def put(where, value):
        tail[where] = value if where not in tail else tail[where] + value

    def class_tail(ref, count, base):
        for row in range(count):
            first, shift = divmod(base + NCLS * row, 128)
            for k in range(2):
                value = roll(ref[row : row + 1, k * 128 : k * 128 + 128], shift)
                put(first + k, jnp.where(lane >= shift, value, 0.0))
                if shift:
                    put(first + k + 1, jnp.where(lane < shift, value, 0.0))

    class_tail(v.out_c, 16, 0)
    class_tail(v.out_ac, 8, 76128)
    start = lax.rem(496 * me, 128)
    first = lax.div(496 * me, 128)
    own = [
        pltpu.roll(v.gain_rows[pl.ds(first + k, 1), :], lax.rem(16 - start + 128, 128), 1)
        for k in range(6)
    ]
    spot = lane - 16 + start
    for k in range(4):
        value = jnp.where(spot < 0, own[k], jnp.where(spot >= 128, own[k + 2], own[k + 1]))
        put(604 + k, jnp.where(lane >= 16, value, 0.0) if k == 0 else value)
    v.grad_pad[EDGE : EDGE + 576, :] = pltpu.roll(v.out_a[...], 96, 1)
    o_flat[7122:7706, :] = jnp.where(
        lane >= 96, v.grad_pad[EDGE : EDGE + 584, :], v.grad_pad[EDGE - 1 : EDGE + 583, :]
    )
    for row in range(608):
        if row in (18, 594):
            o_flat[7104 + row : 7105 + row, :] = o_flat[7104 + row : 7105 + row, :] + tail[row]
        elif row < 18 or row > 594:
            o_flat[7104 + row : 7105 + row, :] = tail[row]
    v.end_t[t] = sync.wait()
    spread_e = Spread(v.end_t)
    spread_e.start()
    spread_e.wait()
    ends = v.end_t[0]
    for k in range(1, SPLITS):
        ends = ends + v.end_t[k]
    o_misc[...] = ends
    o_misc[2:3, :] = jnp.broadcast_to(loss_weight, (1, 128))


def whole_step(sizes, labels, feat, flat):
    plan = scratch_plan()
    vmem = pl.BlockSpec(memory_space=pltpu.VMEM)
    anywhere = pl.BlockSpec(memory_space=pl.ANY)
    outs = [flat.shape, (1, 128), (8, 128)]
    return pl.pallas_call(
        functools.partial(step_kernel, tuple(plan)),
        out_shape=[jax.ShapeDtypeStruct(shape, F32) for shape in outs],
        in_specs=[pl.BlockSpec(memory_space=pltpu.SMEM), vmem, anywhere, anywhere],
        out_specs=[vmem] * len(outs),
        scratch_shapes=[pltpu.VMEM(shape, kind) for shape, kind in plan.values()]
        + [pltpu.SemaphoreType.DMA((SEMAPHORES,))],
        compiler_params=pltpu.CompilerParams(
            collective_id=0, has_side_effects=True, vmem_limit_bytes=63 * 1024 * 1024
        ),
        name="whole_step",
    )(sizes, labels, feat, flat)


def update_kernel(
    misc, grad, param, first, second, average,
    o_param, o_first, o_second, o_average, o_norm, o_loss, o_weight,
):
    norm = jnp.sqrt(jnp.sum(misc[0:1, :], axis=1, keepdims=True))
    o_norm[...] = norm
    o_loss[...] = jnp.sum(misc[1:2, :], axis=1, keepdims=True)
    o_weight[...] = misc[2:3, 0:1]
    clipped = grad[...] * jnp.minimum(1.0, 0.05 / (norm + 1e-06))
    new_first = 0.5 * first[...] + 0.5 * clipped
    new_second = 0.5 * second[...] + 0.5 * clipped * clipped
    lift = 1.0 / (1.0 - 0.5**STEP)
    old = param[...]
    ratio = (new_first * lift) / (jnp.sqrt(new_second * lift) + 1e-08)
    new = old - 0.01 * (ratio + 0.01 * old)
    o_param[...] = new
    o_first[...] = new_first
    o_second[...] = new_second
    o_average[...] = 0.999 * average[...] + 0.001 * new


def update(misc, grad, param, first, second, average):
    rows = grad.shape[0]
    block = pl.BlockSpec((1024, 128), lambda i: (i, 0))
    whole = pl.BlockSpec((8, 128), lambda i: (0, 0))
    one = pl.BlockSpec((1, 1), lambda i: (0, 0))
    big = jax.ShapeDtypeStruct((rows, 128), F32)
    return pl.pallas_call(
        update_kernel,
        grid=(pl.cdiv(rows, 1024),),
        out_shape=[big] * 4 + [jax.ShapeDtypeStruct((1, 1), F32)] * 3,
        in_specs=[whole] + [block] * 5,
        out_specs=[block] * 4 + [one] * 3,
        compiler_params=pltpu.CompilerParams(vmem_limit_bytes=32 * 1024 * 1024),
        name="update",
    )(misc, grad, param, first, second, average)


def fits(splits, owners):
    return splits == SPLITS and owners == OWNERS


def local_fast(features, labels, valid, sizes, params, first_moment, squared_mean, average):
    flat = params.reshape(-1, 128)
    marked = jnp.where(valid > 0, labels, -1).astype(F32).reshape(CELLS, 1)
    grad, shift_grad, misc = whole_step(
        sizes, jnp.broadcast_to(marked, (CELLS, 128)), features.reshape(CELLS, -1), flat
    )
    news = update(
        misc,
        grad,
        flat,
        first_moment.reshape(-1, 128),
        squared_mean.reshape(-1, 128),
        average.reshape(-1, 128),
    )
    new_params, new_first, new_second, new_average = [
        item.reshape(params.shape) for item in news[:4]
    ]
    return (
        new_params,
        new_first,
        new_second,
        new_average,
        new_params.astype(BF),
        news[4].reshape(()),
        news[5].reshape(()),
        news[6].reshape(()),
        shift_grad.reshape(128),
    )


def solution(mesh):
    chosen = local_fast if fits(mesh.shape["tensor"], mesh.shape["batch"]) else local
    return jax.shard_map(
        chosen,
        mesh=mesh,
        in_specs=(
            P("batch", None, None, "tensor"),
            P("batch", None, None),
            P("batch", None, None),
            P("batch", None),
            P("tensor", "batch"),
            P("tensor", "batch"),
            P("tensor", "batch"),
            P("tensor", "batch"),
        ),
        out_specs=(
            P("tensor", "batch"),
            P("tensor", "batch"),
            P("tensor", "batch"),
            P("tensor", "batch"),
            P("tensor", "batch"),
            P(),
            P(),
            P(),
            P("tensor"),
        ),
        check_vma=False,
    )
```

```python
import functools

import jax
import jax.numpy as jnp
from jax import lax
from jax.experimental import pallas as pl
from jax.experimental.pallas import tpu as pltpu
from jax.sharding import PartitionSpec as P

C_IN = 1024
MID = 512
C_OUT = 2048
PPM = 512
AUXW = 256
NCLS = 150
MAP = 24
STEP = 3


BIN_COUNTS = (1, 2, 3, 6)
BIN_STARTS = (0, 1, 5, 14)


def segment_shapes(splits):
    return [
        (C_IN, MID // splits),
        (C_IN, C_OUT // splits),
        (9, MID, MID // splits),
        (MID, C_OUT // splits),
        (4, C_OUT // splits, PPM),
        (9, C_OUT + 4 * PPM, PPM // splits),
        (PPM // splits, NCLS),
        (9, C_IN, AUXW // splits),
        (AUXW // splits, NCLS),
        (2, (2 * MID + 2 * C_OUT + 5 * PPM + AUXW) // splits),
    ]


def unflatten(rows, splits):
    split_parts = []
    start = 0
    for shape in segment_shapes(splits):
        count = 1
        for extent in shape:
            count = count * extent
        count = count // rows.shape[0]
        split_parts.append(rows[:, start : start + count].reshape(shape))
        start = start + count
    return split_parts


def gain_pieces(gains, splits):
    widths = [MID, C_OUT, MID, C_OUT, PPM, PPM, PPM, PPM, PPM, AUXW]
    split_parts = []
    start = 0
    for width in widths:
        step_width = width // splits
        split_parts.append(gains[:, start : start + step_width])
        start = start + step_width
    return split_parts


def shifted(field, down, right):
    image_height, width = (field.shape[1], field.shape[2])
    rows_pad, cols_pad = (abs(down), abs(right))
    padded = jnp.pad(field, ((0, 0), (rows_pad, rows_pad), (cols_pad, cols_pad), (0, 0)))
    return padded[
        :,
        rows_pad + down : rows_pad + down + image_height,
        cols_pad + right : cols_pad + right + width,
        :,
    ]


def conv_forward(field, kernel, spacing):
    total = jnp.zeros(field.shape[:-1] + (kernel.shape[2],), jnp.float32)
    for tap in range(9):
        moved = shifted(field, (tap // 3 - 1) * spacing, (tap % 3 - 1) * spacing)
        total = total + jnp.dot(moved, kernel[tap], preferred_element_type=jnp.float32)
    return total


def conv_input_back(grad, kernel, spacing):
    total = jnp.zeros(grad.shape[:-1] + (kernel.shape[1],), jnp.float32)
    for tap in range(9):
        product = jnp.dot(grad, kernel[tap].T, preferred_element_type=jnp.float32)
        total = total + shifted(product, -(tap // 3 - 1) * spacing, -(tap % 3 - 1) * spacing)
    return total


def conv_kernel_back(field, grad, spacing):
    return jnp.stack(
        [
            jnp.einsum(
                "ihwc,ihwd->cd",
                shifted(field, (tap // 3 - 1) * spacing, (tap % 3 - 1) * spacing),
                grad,
                preferred_element_type=jnp.float32,
            )
            for tap in range(9)
        ]
    )


def silu_slope(value):
    gate = jax.nn.sigmoid(value)
    return gate * (1.0 + value * (1.0 - gate))


def channel_sums(values):
    return values.reshape(-1, values.shape[-1]).sum(0)


def masked_norm_apply(items, extra):
    sends = []
    for value, mask, norm in items:
        sends = sends + [
            channel_sums(value * mask),
            channel_sums(value * value * mask),
            jnp.sum(mask) * jnp.ones((1,), jnp.float32),
        ]
    totals = lax.psum(tuple(sends + extra), "batch")
    results = []
    for index, (value, mask, norm) in enumerate(items):
        count = totals[3 * index + 2]
        mean = totals[3 * index] / count
        spread = totals[3 * index + 1] / count - mean * mean
        scaling = lax.rsqrt(spread + 1e-05)
        normed = (value - mean) * scaling
        results.append((norm[0] * normed + norm[1], normed, scaling, count, mask, norm[0]))
    return (results, totals[3 * len(items) :])


def norm_backward(items):
    sends = []
    for grad, kept in items:
        sends = sends + [channel_sums(grad), channel_sums(grad * kept[1])]
    totals = lax.psum(tuple(sends), "batch")
    results = []
    for index, (grad, kept) in enumerate(items):
        outcome, normed, scaling, count, mask, gamma = kept
        first_sum, second_sum = (totals[2 * index], totals[2 * index + 1])
        inner = grad - mask * (first_sum + normed * second_sum) / count
        results.append(gamma * scaling * inner)
    return (results, sends, totals)


def bin_tables(extent, bins, length):
    which = jnp.arange(bins, dtype=jnp.int32)[None, :, None]
    place = jnp.arange(length, dtype=jnp.int32)[None, None, :]
    edge = extent[:, None, None]
    lower = which * edge // bins
    upper = ((which + 1) * edge + bins - 1) // bins
    member = ((place >= lower) & (place < upper)).astype(jnp.float32)
    target = jnp.minimum(place * bins // edge, bins - 1)
    chosen = (target == which).astype(jnp.float32)
    return (member, chosen)


def spread_bins(merged, branch, tables, images):
    joined = [merged]
    for group, bins in enumerate(BIN_COUNTS):
        rows_in, cols_in, rows_pick, cols_pick, cell_count = tables[group]
        piece = branch[:, BIN_STARTS[group] : BIN_STARTS[group] + bins * bins].reshape(
            images, bins, bins, -1
        )
        joined.append(
            jnp.einsum(
                "ikh,ilw,iklc->ihwc",
                rows_pick.astype(jnp.bfloat16),
                cols_pick.astype(jnp.bfloat16),
                piece,
                preferred_element_type=jnp.float32,
            ).astype(jnp.bfloat16)
        )
    return jnp.concatenate(joined, axis=-1)


def pick_bins(d_joined, width, tables, images):
    branch_width = (d_joined.shape[-1] - width) // 4
    d_up = []
    for group, bins in enumerate(BIN_COUNTS):
        rows_in, cols_in, rows_pick, cols_pick, cell_count = tables[group]
        piece = d_joined[..., width + group * branch_width : width + (group + 1) * branch_width]
        d_up.append(
            jnp.einsum("ikh,ilw,ihwc->iklc", rows_pick, cols_pick, piece).reshape(
                images, bins * bins, -1
            )
        )
    return (d_joined[..., :width], jnp.concatenate(d_up, axis=1))


def gather_channels(field):
    return lax.all_gather(field, "tensor", axis=3, tiled=True)


def scatter_channels(field):
    return lax.psum_scatter(
        field.astype(jnp.bfloat16), "tensor", scatter_dimension=3, tiled=True
    ).astype(jnp.float32)


def local(features, labels, valid, sizes, params, first_moment, squared_mean, average):
    splits = lax.axis_size("tensor")
    owners = lax.axis_size("batch")
    images = features.shape[0]
    gathered = lax.all_gather(params.astype(jnp.bfloat16), "batch", axis=0, tiled=True)
    (
        w_reduce,
        w_short,
        w_middle,
        w_expand,
        w_branch,
        w_unite,
        w_classes,
        w_aux,
        w_aux_classes,
        gains,
    ) = unflatten(gathered, splits)
    norms = [(piece[0], piece[1]) for piece in gain_pieces(gains.astype(jnp.float32), splits)]
    rows_at = jnp.arange(MAP, dtype=jnp.int32)
    inside = (rows_at[None, :, None] < sizes[:, 0][:, None, None]) & (
        rows_at[None, None, :] < sizes[:, 1][:, None, None]
    )
    inside = inside.astype(jnp.float32)[..., None]
    counted = inside * valid.astype(jnp.float32)[..., None]
    labels_hot = (labels[..., None] == jnp.arange(NCLS, dtype=jnp.int32)).astype(jnp.float32)
    class_local = channel_sums(labels_hot * counted)
    whole = lax.all_gather(features, "tensor", axis=3, tiled=True)
    pre_reduce = jnp.dot(whole, w_reduce, preferred_element_type=jnp.float32)
    pre_short = jnp.dot(whole, w_short, preferred_element_type=jnp.float32)
    pre_aux = conv_forward(whole, w_aux, 1)
    leading_part, label_tally = masked_norm_apply(
        [
            (pre_reduce, inside, norms[0]),
            (pre_short, inside, norms[1]),
            (pre_aux, inside, norms[9]),
        ],
        [class_local],
    )
    class_pixel_counts = label_tally[0]
    hidden_one = jax.nn.silu(leading_part[0][0]).astype(jnp.bfloat16)
    aux_act = jax.nn.silu(leading_part[2][0]).astype(jnp.bfloat16)
    hidden_full = gather_channels(hidden_one)
    pre_middle = conv_forward(hidden_full, w_middle, 4)
    second, unused = masked_norm_apply([(pre_middle, inside, norms[2])], [])
    hidden_two = jax.nn.silu(second[0][0]).astype(jnp.bfloat16)
    hidden_two_full = gather_channels(hidden_two)
    pre_expand = jnp.dot(hidden_two_full, w_expand, preferred_element_type=jnp.float32)
    third, unused = masked_norm_apply([(pre_expand, inside, norms[3])], [])
    summed = third[0][0] + leading_part[1][0]
    merged = jax.nn.silu(summed).astype(jnp.bfloat16)
    tables = []
    pooled_list = []
    partial_list = []
    for group, bins in enumerate(BIN_COUNTS):
        rows_in, rows_pick = bin_tables(sizes[:, 0], bins, MAP)
        cols_in, cols_pick = bin_tables(sizes[:, 1], bins, MAP)
        cell_count = (
            jnp.sum(rows_in, axis=2)[:, :, None, None] * jnp.sum(cols_in, axis=2)[:, None, :, None]
        )
        tables.append((rows_in, cols_in, rows_pick, cols_pick, cell_count))
        pooled = (
            jnp.einsum(
                "ikh,ilw,ihwc->iklc",
                rows_in.astype(jnp.bfloat16),
                cols_in.astype(jnp.bfloat16),
                merged,
                preferred_element_type=jnp.float32,
            )
            / cell_count
        )
        pooled = pooled.astype(jnp.bfloat16).reshape(images, bins * bins, -1)
        pooled_list.append(pooled)
        partial_list.append(
            jnp.einsum("ipc,cd->ipd", pooled, w_branch[group], preferred_element_type=jnp.float32)
        )
    branch_pre = lax.psum_scatter(
        jnp.concatenate(partial_list, axis=1).astype(jnp.bfloat16),
        "tensor",
        scatter_dimension=2,
        tiled=True,
    ).astype(jnp.float32)
    branch_items = []
    for group, bins in enumerate(BIN_COUNTS):
        piece = branch_pre[:, BIN_STARTS[group] : BIN_STARTS[group] + bins * bins]
        branch_items.append(
            (piece, jnp.ones(piece.shape[:-1] + (1,), jnp.float32), norms[4 + group])
        )
    fourth, unused = masked_norm_apply(branch_items, [])
    branch_act = jnp.concatenate([jax.nn.silu(kept[0]) for kept in fourth], axis=1).astype(
        jnp.bfloat16
    )
    merged_full, branch_full = (
        lax.all_gather(merged, "tensor", axis=3, tiled=True),
        lax.all_gather(branch_act, "tensor", axis=2, tiled=True),
    )
    joined = spread_bins(merged_full, branch_full, tables, images)
    pre_unite = conv_forward(joined, w_unite, 1)
    fifth, unused = masked_norm_apply([(pre_unite, inside, norms[8])], [])
    united = jax.nn.silu(fifth[0][0]).astype(jnp.bfloat16)
    logit_main, logit_aux = (
        lax.psum_scatter(
            jnp.dot(united, w_classes, preferred_element_type=jnp.float32).astype(jnp.bfloat16),
            "tensor",
            scatter_dimension=1,
            tiled=True,
        ).astype(jnp.float32),
        lax.psum_scatter(
            jnp.dot(aux_act, w_aux_classes, preferred_element_type=jnp.float32).astype(
                jnp.bfloat16
            ),
            "tensor",
            scatter_dimension=1,
            tiled=True,
        ).astype(jnp.float32),
    )
    total_valid = jnp.sum(class_pixel_counts)
    class_weight = total_valid / (NCLS * class_pixel_counts + total_valid)
    loss_weight = jnp.sum(class_pixel_counts * class_weight)
    cell_weight = jnp.sum(labels_hot * class_weight, axis=-1, keepdims=True) * counted
    band_rows = labels.shape[1] // splits
    band_start = lax.axis_index("tensor") * band_rows
    hot_band = lax.dynamic_slice_in_dim(labels_hot, band_start, band_rows, 1)
    weight_band = lax.dynamic_slice_in_dim(cell_weight, band_start, band_rows, 1)
    log_main = jax.nn.log_softmax(logit_main, axis=-1)
    log_aux = jax.nn.log_softmax(logit_aux, axis=-1)
    loss_cells = -jnp.sum(hot_band * (log_main + 0.4 * log_aux), axis=-1, keepdims=True)
    loss_local = jnp.sum(weight_band * loss_cells)
    band_main = (weight_band * (jnp.exp(log_main) - hot_band) / loss_weight).astype(jnp.bfloat16)
    band_aux = (0.4 * weight_band * (jnp.exp(log_aux) - hot_band) / loss_weight).astype(
        jnp.bfloat16
    )
    grad_main, grad_aux = (
        lax.all_gather(band_main, "tensor", axis=1, tiled=True),
        lax.all_gather(band_aux, "tensor", axis=1, tiled=True),
    )
    reduced = {}

    def settle(index, value):
        reduced[index] = value

    settle(6, jnp.einsum("ihwc,ihwk->ck", united, grad_main, preferred_element_type=jnp.float32))
    settle(8, jnp.einsum("ihwc,ihwk->ck", aux_act, grad_aux, preferred_element_type=jnp.float32))
    d_united = jnp.dot(grad_main, w_classes.T, preferred_element_type=jnp.float32) * silu_slope(
        fifth[0][0]
    )
    d_aux = jnp.dot(grad_aux, w_aux_classes.T, preferred_element_type=jnp.float32) * silu_slope(
        leading_part[2][0]
    )
    back_one, sums_one, totals_one = norm_backward([(d_united, fifth[0]), (d_aux, leading_part[2])])
    unite_shift_grad = totals_one[0]
    d_unite_pre = back_one[0].astype(jnp.bfloat16)
    d_aux_pre = back_one[1].astype(jnp.bfloat16)
    settle(5, conv_kernel_back(joined, d_unite_pre, 1))
    d_merged, d_branch = pick_bins(conv_input_back(d_unite_pre, w_unite, 1), C_OUT, tables, images)
    d_merged, d_branch = (
        lax.psum_scatter(
            d_merged.astype(jnp.bfloat16), "tensor", scatter_dimension=3, tiled=True
        ).astype(jnp.float32),
        lax.psum_scatter(
            d_branch.astype(jnp.bfloat16), "tensor", scatter_dimension=2, tiled=True
        ).astype(jnp.float32),
    )
    settle(7, conv_kernel_back(whole, d_aux_pre, 1))
    branch_back = []
    for group, bins in enumerate(BIN_COUNTS):
        piece = d_branch[:, BIN_STARTS[group] : BIN_STARTS[group] + bins * bins]
        branch_back.append((piece * silu_slope(fourth[group][0]), fourth[group]))
    back_two, sums_two, unused = norm_backward(branch_back)
    d_branch_pre = jnp.concatenate(back_two, axis=1).astype(jnp.bfloat16)
    d_branch_full = lax.all_gather(d_branch_pre, "tensor", axis=2, tiled=True)
    branch_grads = []
    for group, bins in enumerate(BIN_COUNTS):
        rows_in, cols_in, rows_pick, cols_pick, cell_count = tables[group]
        piece = d_branch_full[:, BIN_STARTS[group] : BIN_STARTS[group] + bins * bins]
        branch_grads.append(
            jnp.einsum("ipc,ipd->cd", pooled_list[group], piece, preferred_element_type=jnp.float32)
        )
        d_pooled = jnp.dot(piece, w_branch[group].T, preferred_element_type=jnp.float32).reshape(
            images, bins, bins, -1
        )
        d_merged = d_merged + jnp.einsum(
            "ikh,ilw,iklc->ihwc", rows_in, cols_in, d_pooled / cell_count
        )
    settle(4, jnp.stack(branch_grads))
    d_summed = d_merged * silu_slope(summed)
    back_three, sums_three, unused = norm_backward(
        [(d_summed, third[0]), (d_summed, leading_part[1])]
    )
    d_expand_pre = back_three[0].astype(jnp.bfloat16)
    d_short_pre = back_three[1].astype(jnp.bfloat16)
    settle(
        3,
        jnp.einsum(
            "ihwc,ihwd->cd", hidden_two_full, d_expand_pre, preferred_element_type=jnp.float32
        ),
    )
    settle(1, jnp.einsum("ihwc,ihwd->cd", whole, d_short_pre, preferred_element_type=jnp.float32))
    d_two = scatter_channels(jnp.dot(d_expand_pre, w_expand.T, preferred_element_type=jnp.float32))
    back_four, sums_four, unused = norm_backward([(d_two * silu_slope(second[0][0]), second[0])])
    d_middle_pre = back_four[0].astype(jnp.bfloat16)
    settle(2, conv_kernel_back(hidden_full, d_middle_pre, 4))
    d_one = scatter_channels(conv_input_back(d_middle_pre, w_middle, 4))
    back_five, sums_five, unused = norm_backward(
        [(d_one * silu_slope(leading_part[0][0]), leading_part[0])]
    )
    settle(
        0,
        jnp.einsum(
            "ihwc,ihwd->cd",
            whole,
            back_five[0].astype(jnp.bfloat16),
            preferred_element_type=jnp.float32,
        ),
    )
    beta_grads = (
        [sums_five[0], sums_three[2], sums_four[0], sums_three[0]]
        + [sums_two[2 * g] for g in range(4)]
        + [sums_one[0], sums_one[2]]
    )
    gamma_grads = (
        [sums_five[1], sums_three[3], sums_four[1], sums_three[1]]
        + [sums_two[2 * g + 1] for g in range(4)]
        + [sums_one[1], sums_one[3]]
    )
    settle(9, jnp.stack([jnp.concatenate(gamma_grads), jnp.concatenate(beta_grads)]))
    ordered = [reduced[index] for index in range(10)]
    grad_share = lax.psum_scatter(
        jnp.concatenate([part.reshape(owners, -1) for part in ordered], axis=1),
        "batch",
        scatter_dimension=0,
        tiled=True,
    )
    square_all, loss_sum = lax.psum(
        (jnp.sum(grad_share * grad_share), loss_local), ("batch", "tensor")
    )
    grad_norm = jnp.sqrt(square_all)
    clipped = grad_share * jnp.minimum(1.0, 0.05 / (grad_norm + 1e-06))
    new_first = 0.5 * first_moment + 0.5 * clipped
    new_second = 0.5 * squared_mean + 0.5 * clipped * clipped
    keep = 1.0 - 0.5**STEP
    new_params = params - 0.01 * (
        new_first / keep / (jnp.sqrt(new_second / keep) + 1e-08) + 0.01 * params
    )
    new_average = 0.999 * average + 0.001 * new_params
    return (
        new_params,
        new_first,
        new_second,
        new_average,
        new_params.astype(jnp.bfloat16),
        grad_norm,
        loss_sum,
        loss_weight,
        unite_shift_grad,
    )


CELLS = MAP * MAP
EDGE = 104
BATCH = "batch"
TENSOR = "tensor"
GROUP_ROWS = ((0, 1), (1, 5), (5, 14), (14, 50))
BINS = 64
BF = jnp.bfloat16
F32 = jnp.float32
MESH = pl.DeviceIdType.MESH
HALF = 4
OWNERS = 8
SPLITS = 4
MERGED = 4
SLOTS = 5


def scratch_plan():
    plan = dict(
        w_r=((1024, 128), BF),
        w_s=((1024, 512), BF),
        w_m=((4608, 128), BF),
        w_e=((512, 512), BF),
        w_b=((2048, 512), BF),
        w_u=((18432, 128), BF),
        w_own=((4608, 128), BF),
        w_a=((4608, 128), BF),
        w_pair=((1024, 640), BF),
        w_c=((128, 256), BF),
        w_ac=((64, 256), F32),
        gain_in=((OWNERS, 8, 128), F32),
        gain_rows=((40, 128), F32),
        out_a=((576, 128), F32),
        out_c=((16, 256), F32),
        out_ac=((8, 256), F32),
        whole=((SPLITS, CELLS, 256), BF),
        ins=((CELLS, 128), F32),
        col=((CELLS, 128), F32),
        lab=((CELLS, 128), F32),
        table=((BINS, CELLS), F32),
        pool=((BINS, CELLS), BF),
        pick=((BINS, CELLS), BF),
        cells_in=((BINS, 128), F32),
        pad=((9, CELLS + 2 * EDGE, 128), F32),
        grad_pad=((CELLS + 2 * EDGE, 128), F32),
        pre_r=((CELLS, 128), F32),
        pre_s=((CELLS, 512), F32),
        pre_a=((CELLS, 128), F32),
        pre_m=((CELLS, 128), F32),
        pre_e=((CELLS, 512), F32),
        pre_u=((CELLS, 128), F32),
        act_a=((CELLS, 128), BF),
        h1=((SPLITS, CELLS, 128), BF),
        h2=((SPLITS, CELLS, 128), BF),
        joined=((SPLITS, CELLS, 512), BF),
        joined_t=((SPLITS, 512, CELLS), BF),
        pooled=((BINS, 512), BF),
        pool_half=((2, BINS, 256), BF),
        pool_all=((OWNERS, BINS, 256), BF),
        d_bp_all=((OWNERS, SPLITS, BINS, 128), BF),
        part_b=((SPLITS, BINS, 128), BF),
        recv_b=((SPLITS, BINS, 128), BF),
        all_b=((OWNERS, BINS, 128), BF),
        act_b=((SPLITS, OWNERS * BINS, 128), BF),
        pick_t=((CELLS, 128), BF),
        z_cat=((9, 128, 128), BF),
        zsum=((2, OWNERS * BINS, 128), F32),
        z_send=((OWNERS, 2, BINS, 128), BF),
        z_recv=((OWNERS, 2, BINS, 128), BF),
        united=((CELLS, 128), BF),
        logit_send=((CELLS, 512), BF),
        logit_recv=((SPLITS, 144, 512), BF),
        slope_in=((SPLITS, 144, 512), BF),
        d_f=((CELLS, 128), F32),
        d_f2=((CELLS, 128), F32),
        cat_u=((CELLS, 1152), BF),
        cat_a=((CELLS, 640), BF),
        dz_send=((9, BINS, 128), BF),
        dz_recv=((OWNERS, 2, BINS, 128), BF),
        d_act_send=((SPLITS, OWNERS * BINS, 128), BF),
        d_act_recv=((SPLITS, OWNERS * BINS, 128), BF),
        d_img_send=((OWNERS, BINS, 128), BF),
        d_img_recv=((OWNERS, BINS, 128), BF),
        d_bp=((SPLITS, BINS, 128), BF),
        dm_near=((2, CELLS, 512), BF),
        dm_far=((CELLS, 512), BF),
        d_sum=((CELLS, 512), F32),
        d_e=((CELLS, 512), BF),
        d_s=((CELLS, 512), BF),
        dh_send=((SPLITS, CELLS, 128), BF),
        dh_recv=((2, SPLITS, CELLS, 128), BF),
        d_low=((CELLS, 128), BF),
        end_t=((SPLITS, 8, 128), F32),
    )
    for name, rows in SYNCS.items():
        plan["sync_" + name] = ((OWNERS, rows, 128), F32)
    for name, (rows, lanes, kind) in PARTS.items():
        plan["first_" + name] = ((HALF, rows, lanes), kind)
        plan["second_" + name] = ((HALF - 1, rows, lanes), kind)
    plan["first_u"] = ((HALF, SLOTS, 512, 128), BF)
    plan["second_u"] = ((HALF - 1, SLOTS, 512, 128), BF)
    return plan


SYNCS = dict(one=8, two=8, three=16, five=8, aux=8, b1=8, b2=8, b3=8, b4=16, b5=8, b6=8, end=8)
PARTS = dict(
    r=(128, 128, BF),
    s=(128, 512, BF),
    m=(576, 128, BF),
    e=(64, 512, BF),
    a=(576, 128, BF),
    c=(16, 256, BF),
    ac=(8, 256, F32),
)
SEMAPHORES = 1100
LOADS = (0, 128, 640, 1216, 1472, 2496, 7104, 7712)
LOAD_ORDER = (0, 2, 3, 1, 4, 6, 5)


class Refs:
    pass


def fold(value):
    return value.reshape(-1, 8, value.shape[-1]).sum(0)


def total(value):
    return jnp.sum(value, axis=0, keepdims=True)


def wide(value, times):
    return jnp.concatenate([value] * times, axis=1)


def dot(left, right):
    return jnp.dot(left, right, preferred_element_type=F32)


def dot_nt(left, right):
    return lax.dot_general(left, right, (((1,), (1,)), ((), ())), preferred_element_type=F32)


def dot_tn(left, right):
    return lax.dot_general(left, right, (((0,), (0,)), ((), ())), preferred_element_type=F32)


def loop(count, body):
    def step(k, carry):
        body(k)
        return carry

    lax.fori_loop(0, count, step, 0)


def rows_at(k, block):
    return pl.ds(pl.multiple_of(k * block, block), block)


def step_kernel(names, *refs):
    (
        sizes, lab_in, feat, flat, o_flat, o_shift, o_misc,
    ) = refs[:7]
    v = Refs()
    for name, ref in zip(names, refs[7:]):
        setattr(v, name, ref)
    sems = refs[-1]
    o_u = o_flat.at[2496:7104, :]
    me = lax.axis_index(BATCH)
    t = lax.axis_index(TENSOR)
    partner = me + 1 - 2 * lax.rem(me, 2)
    t_core = t + 1 - 2 * lax.rem(t, 2)
    t_x = lax.rem(t + 2, SPLITS)
    t_diag = lax.rem(t_core + 2, SPLITS)
    taken = [0]

    def take(count):
        start = taken[0]
        taken[0] = start + count
        assert taken[0] <= SEMAPHORES
        return start

    def far_peer(base, step):
        return lax.rem(base + 2 * step, OWNERS)

    def remote(src, dst, send, recv, device):
        return pltpu.make_async_remote_copy(
            src_ref=src,
            dst_ref=dst,
            send_sem=sems.at[send],
            recv_sem=sems.at[recv],
            device_id=device,
            device_id_type=MESH,
        )

    late = []

    load_at = take(len(LOADS))

    def load(index):
        at = pl.ds(LOADS[index], LOADS[index + 1] - LOADS[index])
        return pltpu.make_async_copy(flat.at[at, :], o_flat.at[at, :], sems.at[load_at + index])

    for index in LOAD_ORDER:
        load(index).start()
    v.pool_all[...] = jnp.zeros((OWNERS, BINS, 256), BF)
    v.d_bp_all[...] = jnp.zeros((OWNERS, SPLITS, BINS, 128), BF)
    barrier = pltpu.get_barrier_semaphore()
    for k in range(1, OWNERS):
        pl.semaphore_signal(
            barrier, inc=1, device_id={BATCH: lax.rem(me + k, OWNERS)}, device_id_type=MESH
        )
    for k in range(1, SPLITS):
        pl.semaphore_signal(
            barrier, inc=1, device_id={TENSOR: lax.rem(t + k, SPLITS)}, device_id_type=MESH
        )
    pl.semaphore_wait(barrier, OWNERS + SPLITS - 2)

    class Gather:
        def __init__(self, full, rows, skip=0, step=None, piece=None):
            self.full, self.rows, self.piece = full, rows, piece
            self.skip, self.part = skip, step or rows
            self.near_s, self.far_s, self.pass_s = take(1), take(HALF), take(HALF)
            self.recv, self.keep = take(OWNERS), take(1)

        def at(self, owner):
            if self.rows is None:
                return self.full.at[owner]
            start = pl.multiple_of(owner * self.rows + self.skip, self.part)
            return self.full.at[pl.ds(start, self.part), :]

        def source(self):
            return self.at(me) if self.piece is None else self.piece

        def local(self):
            return pltpu.make_async_copy(self.piece, self.at(me), sems.at[self.keep])

        def near(self):
            return remote(
                self.source(), self.at(me), self.near_s, self.recv + me, {BATCH: partner}
            )

        def far(self, step):
            return remote(
                self.source(),
                self.at(me),
                self.far_s + step,
                self.recv + me,
                {BATCH: far_peer(me, step)},
            )

        def passed(self, step, base):
            source = far_peer(base, step)
            return remote(
                self.at(source),
                self.at(source),
                self.pass_s + step,
                self.recv + source,
                {BATCH: partner},
            )

        def start_far(self):
            if self.piece is not None:
                self.local().start()
            for step in range(1, HALF):
                self.far(step).start()

        def start_near(self):
            self.near().start()

        def forward(self):
            for step in range(1, HALF):
                self.passed(step, me).wait_recv()
                self.passed(step, me).start()

        def finish(self):
            for step in range(HALF):
                self.passed(step, partner).wait_recv()
            if self.piece is not None:
                self.local().wait()
            self.near().wait_send()
            for step in range(1, HALF):
                self.far(step).wait_send()

        def drain(self):
            for step in range(1, HALF):
                self.passed(step, me).wait_send()

    g_gain = Gather(v.gain_in, None, piece=flat.at[7704:7712, :])
    g_r = Gather(v.w_r, 128)
    g_s = Gather(v.w_s, 128)
    g_a = Gather(v.w_a, 576)
    g_m = Gather(v.w_m, 576)
    g_e = Gather(v.w_e, 64)
    g_b0 = Gather(v.w_b, 256, 0, 128)
    g_b1 = Gather(v.w_b, 256, 128, 128)
    g_c = Gather(v.w_c, 16)
    g_ac = Gather(v.w_ac, 8)

    def block_of(owner, slot):
        return 8 if slot == SLOTS - 1 else lax.rem(slot - owner + 8, 8)

    def merged_rows(owner, slot):
        block = owner * 9 + block_of(owner, slot)
        index = lax.div(block, 8) * MERGED + lax.rem(block, 8)
        return pl.ds(pl.multiple_of(index * 512, 512), 512)

    def has(owner, slot, body):
        if slot == SLOTS - 1:
            pl.when(owner < MERGED)(body)
        else:
            body()

    class GatherUnite:
        def __init__(self):
            self.near_s, self.far_s, self.pass_s = (
                take(SLOTS),
                take(SLOTS * HALF),
                take(SLOTS * HALF),
            )
            self.recv, self.keep = take(SLOTS * OWNERS), take(SLOTS)

        def source(self, slot):
            return v.w_own.at[rows_at(block_of(me, slot), 512), :]

        def full(self, owner, slot):
            return v.w_u.at[merged_rows(owner, slot), :]

        def local(self, slot):
            return pltpu.make_async_copy(
                self.source(slot), self.full(me, slot), sems.at[self.keep + slot]
            )

        def near(self, slot):
            return remote(
                self.source(slot),
                self.full(me, slot),
                self.near_s + slot,
                self.recv + me * SLOTS + slot,
                {BATCH: partner},
            )

        def far(self, step, slot):
            return remote(
                self.source(slot),
                self.full(me, slot),
                self.far_s + step * SLOTS + slot,
                self.recv + me * SLOTS + slot,
                {BATCH: far_peer(me, step)},
            )

        def passed(self, step, slot, base):
            source = far_peer(base, step)
            return remote(
                self.full(source, slot),
                self.full(source, slot),
                self.pass_s + step * SLOTS + slot,
                self.recv + source * SLOTS + slot,
                {BATCH: partner},
            )

        def start_far(self, slot):
            def go():
                self.local(slot).start()
                for step in range(1, HALF):
                    self.far(step, slot).start()

            has(me, slot, go)

        def start_near(self, slot):
            has(me, slot, lambda: self.near(slot).start())

        def forward(self, slot):
            for step in range(1, HALF):

                def go(step=step):
                    self.passed(step, slot, me).wait_recv()
                    self.passed(step, slot, me).start()

                has(far_peer(me, step), slot, go)

        def finish(self):
            for slot in range(SLOTS):
                for step in range(HALF):
                    has(
                        far_peer(partner, step),
                        slot,
                        lambda step=step, slot=slot: self.passed(step, slot, partner).wait_recv(),
                    )

                def end(slot=slot):
                    self.local(slot).wait()
                    self.near(slot).wait_send()
                    for step in range(1, HALF):
                        self.far(step, slot).wait_send()

                has(me, slot, end)

        def drain(self):
            for slot in range(SLOTS):
                for step in range(1, HALF):
                    has(
                        far_peer(me, step),
                        slot,
                        lambda step=step, slot=slot: self.passed(step, slot, me).wait_send(),
                    )

    g_u = GatherUnite()

    class Sync:
        def __init__(self, buf):
            self.buf = buf
            self.send, self.recv = take(OWNERS), take(OWNERS)

        def copy(self, k, slot):
            return remote(
                self.buf.at[slot],
                self.buf.at[slot],
                self.send + k,
                self.recv + slot,
                {BATCH: lax.rem(me + k, OWNERS)},
            )

        def start(self, rows):
            for index, row in enumerate(rows):
                self.buf[me, index : index + 1, :] = row
            for index in range(len(rows), self.buf.shape[1]):
                self.buf[me, index : index + 1, :] = jnp.zeros((1, 128), F32)
            for k in range(1, OWNERS):
                self.copy(k, me).start()

        def wait(self):
            for k in range(1, OWNERS):
                self.copy(k, lax.rem(me + k, OWNERS)).wait_recv()
            for k in range(1, OWNERS):
                self.copy(k, me).wait_send()
            value = self.buf[0]
            for slot in range(1, OWNERS):
                value = value + self.buf[slot]
            return value

    class ToGroup:
        def __init__(self, part, into):
            self.part, self.into = part, into
            self.send, self.recv = take(OWNERS), take(OWNERS)

        def each(self, k, owner, slot, act):
            for rows, fits_ in ((16, owner < 6), (BINS, owner >= 6)):

                def go(rows=rows):
                    act(
                        remote(
                            self.part(owner, rows),
                            self.into(slot, rows),
                            self.send + k,
                            self.recv + slot,
                            {BATCH: lax.rem(me + k, OWNERS)},
                        )
                    )

                pl.when(fits_)(go)

        def start(self):
            for k in range(1, OWNERS):
                self.each(k, lax.rem(me + k, OWNERS), me, lambda c: c.start())

        def wait(self):
            for k in range(1, OWNERS):
                self.each(k, me, lax.rem(me + k, OWNERS), lambda c: c.wait_recv())
            for k in range(1, OWNERS):
                self.each(k, lax.rem(me + k, OWNERS), me, lambda c: c.wait_send())

    class Spread:

        def __init__(self, buf, lanes_=None):
            self.buf, self.lanes = buf, lanes_
            self.send, self.recv = take(SPLITS), take(SPLITS)

        def view(self, slot):
            return self.buf.at[slot] if self.lanes is None else self.buf.at[slot, :, self.lanes]

        def copy(self, k, slot):
            return remote(
                self.view(slot),
                self.view(slot),
                self.send + k,
                self.recv + slot,
                {TENSOR: lax.rem(t + k, SPLITS)},
            )

        def start(self):
            for k in range(1, SPLITS):
                self.copy(k, t).start()

        def wait(self):
            for k in range(1, SPLITS):
                self.copy(k, lax.rem(t + k, SPLITS)).wait_recv()
            for k in range(1, SPLITS):
                self.copy(k, t).wait_send()

    class Exchange:

        def __init__(self, axis, count, part, into):
            self.axis, self.count, self.part, self.into = axis, count, part, into
            self.mine = me if axis == BATCH else t
            self.send, self.recv = take(count), take(count)

        def copy(self, k, slot):
            other = lax.rem(self.mine + k, self.count)
            return remote(
                self.part(other),
                self.into(slot),
                self.send + k,
                self.recv + slot,
                {self.axis: other},
            )

        def start(self):
            for k in range(1, self.count):
                self.copy(k, self.mine).start()

        def wait(self):
            for k in range(1, self.count):
                self.copy(k, lax.rem(self.mine + k, self.count)).wait_recv()
            for k in range(1, self.count):
                self.copy(k, self.mine).wait_send()

    feat_keep = take(1)
    feat_local = pltpu.make_async_copy(feat, v.whole.at[t], sems.at[feat_keep])
    feat_spread = Exchange(TENSOR, SPLITS, lambda other: feat, lambda slot: v.whole.at[slot])
    def wide_rows(into, rows, low):
        for k in range(4):
            value = o_flat[pl.ds(low + k, rows, stride=4), :]
            into[rows_at(me, rows), k * 128 : k * 128 + 128] = value.astype(BF)

    load(0).wait()
    v.w_r[rows_at(me, 128), :] = o_flat[0:128, :].astype(BF)
    for item in (g_gain, g_r):
        item.start_far()
        item.start_near()
    feat_local.start()
    feat_spread.start()
    load(2).wait()
    v.w_m[rows_at(me, 576), :] = o_flat[640:1216, :].astype(BF)
    load(3).wait()
    wide_rows(v.w_e, 64, 1216)
    for item in (g_m, g_e):
        item.start_far()
        item.start_near()
    lane = lax.broadcasted_iota(jnp.int32, (1, 128), 1)

    def roll(value, shift):
        return pltpu.roll(value, shift % 128, 1) if shift % 128 else value

    high, across = sizes[0, 0], sizes[0, 1]
    place = lax.broadcasted_iota(jnp.int32, (CELLS, 128), 0).astype(F32)
    row_of = jnp.floor((place + 0.5) / MAP)
    col_of = place - MAP * row_of
    within = (row_of < high.astype(F32)) & (col_of < across.astype(F32))
    v.ins[...] = jnp.where(within, 1.0, 0.0)
    v.col[...] = col_of
    v.lab[...] = jnp.where(within, lab_in[...], -1.0)
    v.table[...] = jnp.zeros((BINS, CELLS), F32)
    lane_place = lax.broadcasted_iota(jnp.int32, (1, CELLS), 1).astype(F32)
    lane_row = jnp.floor((lane_place + 0.5) / MAP)
    lane_col = lane_place - MAP * lane_row

    def ranges(extent, bins, where):
        inside, chosen, counts = [], [], []
        for k in range(bins):
            low = lax.div(k * extent, bins)
            top = lax.div((k + 1) * extent + (bins - 1), bins)
            member = (where >= low.astype(F32)) & (where < top.astype(F32))
            inside.append(jnp.where(member, 1.0, 0.0))
            picked = where * bins >= (k * extent).astype(F32)
            if k < bins - 1:
                picked = picked & (where * bins < ((k + 1) * extent).astype(F32))
            chosen.append(jnp.where(picked, 1.0, 0.0))
            counts.append(top - low)
        return inside, chosen, counts

    picks = []
    v.cells_in[...] = jnp.ones((BINS, 128), F32)
    for group, bins in enumerate(BIN_COUNTS):
        r_in, r_pick, r_count = ranges(high, bins, lane_row)
        c_in, c_pick, c_count = ranges(across, bins, lane_col)
        for a in range(bins):
            for b in range(bins):
                spot = BIN_STARTS[group] + a * bins + b
                v.table[spot : spot + 1, :] = r_in[a] * c_in[b]
                v.cells_in[spot : spot + 1, :] = jnp.full(
                    (1, 128), (r_count[a] * c_count[b]).astype(F32)
                )
                picks.append((spot, r_pick[a] * c_pick[b]))
    v.pool[...] = v.table[...].astype(BF)
    for spot, value in picks:
        v.table[spot : spot + 1, :] = value
    v.pick[...] = v.table[...].astype(BF)
    v.pick_t[...] = jnp.concatenate([v.pick[...], v.pick[...]], axis=0).T
    zeros_edge = jnp.zeros((EDGE, 128), F32)
    for tap in range(9):
        v.pad[tap, 0:EDGE, :] = zeros_edge
        v.pad[tap, EDGE + CELLS :, :] = zeros_edge
    v.grad_pad[0:EDGE, :] = zeros_edge
    v.grad_pad[EDGE + CELLS :, :] = zeros_edge
    lanes = lax.broadcasted_iota(jnp.int32, (1, 256), 1).astype(F32)
    counts = jnp.zeros((8, 256), F32)
    for k in range(0, CELLS, 96):
        counts = counts + fold(
            jnp.where(wide(v.lab[k : k + 96, :], 2) == lanes, 1.0, 0.0)
        )
    class_local = total(counts)
    cells_local = jnp.full((1, 128), (high * across).astype(F32))
    left_half = lax.broadcasted_iota(jnp.int32, (64, 128), 1) < 64

    for item in (g_gain, g_r):
        item.forward()
    load(1).wait()
    wide_rows(v.w_s, 128, 128)
    load(4).wait()
    wide_rows(v.w_b, 256, 1472)
    load(6).wait()
    before = pltpu.roll(o_flat[7122:7698, :], 32, 1)
    after = pltpu.roll(o_flat[7123:7699, :], 32, 1)
    v.w_a[rows_at(me, 576), :] = jnp.where(lane < 32, before, after).astype(BF)

    def class_rows(count, base, into):
        for row in range(count):
            first, shift = divmod(base + NCLS * row, 128)
            three = [
                roll(o_flat[7104 + first + k : 7105 + first + k, :], 128 - shift) for k in range(3)
            ]
            into[row : row + 1, :128] = jnp.where(lane < 128 - shift, three[0], three[1])
            high_half = jnp.where(lane < 128 - shift, three[1], three[2])
            into[row : row + 1, 128:] = jnp.where(lane < NCLS - 128, high_half, 0.0)

    class_rows(16, 0, v.out_c)
    class_rows(8, 76128, v.out_ac)
    v.w_c[rows_at(me, 16), :] = v.out_c[...].astype(BF)
    v.w_ac[rows_at(me, 8), :] = v.out_ac[...].astype(BF).astype(F32)
    load(5).wait()

    def own_rows(j):
        at = pl.ds(pl.multiple_of(2496 + 512 * j, 64), 512)
        v.w_own[rows_at(j, 512), :] = o_flat[at, :].astype(BF)

    loop(9, own_rows)
    for item in (g_gain, g_r):
        item.finish()
    feat_local.wait()
    feat_spread.wait()
    gain_of = [None] * 33
    for owner in range(OWNERS):
        start = 496 * (owner % 4) - 16
        first, shift = start // 128, start % 128
        for k in range(4):
            value = v.gain_in[owner, 4 + k : 5 + k, :].astype(BF).astype(F32)
            if k == 0:
                value = jnp.where(lane < 16, 0.0, value)
            value = roll(value, shift)
            spot = 16 * (owner // 4) + first + k
            for where, part in (
                (spot, jnp.where(lane >= shift, value, 0.0)),
                (spot + 1, jnp.where(lane < shift, value, 0.0)),
            ):
                gain_of[where] = part if gain_of[where] is None else gain_of[where] + part

    def gamma(row, width=1):
        return jnp.concatenate([gain_of[row + k] for k in range(width)], axis=1)

    def beta(row, width=1):
        return gamma(16 + row, width)

    def whole_feat():
        return jnp.concatenate([v.whole[k] for k in range(SPLITS)], axis=1)

    v.pre_r[...] = dot(whole_feat(), v.w_r[...])
    def offset(tap, spacing):
        return ((tap // 3 - 1) * MAP + (tap % 3 - 1)) * spacing

    def col_mask(at, right):
        where = v.col[at, :] + float(right)
        return jnp.where((where >= 0.0) & (where < float(MAP)), 1.0, 0.0)

    BLOCK = 72

    def shift_sum(taps, spacing, at, slot_of):
        out = None
        for b in (-1, 0, 1):
            part = None
            for tap in taps:
                if tap % 3 - 1 != b:
                    continue
                start = EDGE + at + offset(tap, spacing)
                value = v.pad[slot_of(tap), start : start + BLOCK, :]
                part = value if part is None else part + value
            if part is None:
                continue
            if b:
                part = part * col_mask(slice(at, at + BLOCK), b * spacing)
            out = part if out is None else out + part
        return out

    def masked_sums(ref):
        width = ref.shape[1]

        def step(k, carry):
            at = rows_at(k, 96)
            value = ref[at, :]
            kept = value * (v.ins[at, :] if width == 128 else wide(v.ins[at, :], width // 128))
            return (carry[0] + fold(kept), carry[1] + fold(kept * value))

        zero = jnp.zeros((8, width), F32)
        sums = lax.fori_loop(0, 6, step, (zero, zero))
        return total(sums[0]), total(sums[1])

    def split_rows(value):
        return [value[:, k : k + 128] for k in range(0, value.shape[1], 128)]

    def join_rows(value, row, count):
        return jnp.concatenate([value[row + k : row + k + 1] for k in range(count)], axis=1)

    def moments(first, second, count):
        mean = first / count
        return mean, lax.rsqrt(second / count - mean * mean + 1e-05)

    sync = Sync(v.sync_one)
    r1, r2 = masked_sums(v.pre_r)
    sync.start([r1, r2, cells_local] + split_rows(class_local))
    g_m.forward()
    g_e.forward()
    g_s.start_far()
    sums = sync.wait()
    count = sums[2:3]
    count4 = wide(count, 4)
    norm_r = moments(sums[0:1], sums[1:2], count)
    class_count = join_rows(sums, 3, 2)

    def normed(ref, at, norm):
        return (ref[at, :] - norm[0]) * norm[1]

    spread_1 = Spread(v.h1)

    def make_h1(k):
        at = rows_at(k, 96)
        v.h1[t, at, :] = jax.nn.silu(gamma(0) * normed(v.pre_r, at, norm_r) + beta(0)).astype(BF)

    loop(6, make_h1)
    spread_1.start()
    g_s.start_near()
    g_b0.start_far()
    g_m.finish()
    spread_1.wait()

    def full_h(ref):
        return jnp.concatenate([ref[k] for k in range(SPLITS)], axis=1)

    def middle(tap):
        v.pad[tap, EDGE : EDGE + CELLS, :] = dot(full_h(v.h1), v.w_m[rows_at(tap, 512), :])

    loop(9, middle)
    for at in range(0, CELLS, BLOCK):
        v.pre_m[at : at + BLOCK, :] = shift_sum(range(9), 4, at, lambda tap: tap)
    sync = Sync(v.sync_two)
    sync.start(list(masked_sums(v.pre_m)))
    g_s.forward()
    g_b0.start_near()
    g_b1.start_far()
    sums = sync.wait()
    norm_m = moments(sums[0:1], sums[1:2], count)
    spread_2 = Spread(v.h2)

    def make_h2(k):
        at = rows_at(k, 96)
        v.h2[t, at, :] = jax.nn.silu(gamma(5) * normed(v.pre_m, at, norm_m) + beta(5)).astype(BF)

    loop(6, make_h2)
    spread_2.start()
    g_b0.forward()
    g_b1.start_near()
    g_u.start_far(0)
    g_e.finish()
    g_s.finish()
    for k in range(0, 512, 256):
        v.pre_s[:, k : k + 256] = dot(whole_feat(), v.w_s[:, k : k + 256])
    s1, s2 = masked_sums(v.pre_s)
    spread_2.wait()
    for k in range(0, 512, 256):
        v.pre_e[:, k : k + 256] = dot(full_h(v.h2), v.w_e[:, k : k + 256])
    sync = Sync(v.sync_three)
    e1, e2 = masked_sums(v.pre_e)
    sync.start(split_rows(e1) + split_rows(e2) + split_rows(s1) + split_rows(s2))
    g_b1.forward()
    g_u.start_near(0)
    g_u.start_far(1)
    for item in (g_c, g_ac):
        item.start_far()
        item.start_near()
    sums = sync.wait()
    norm_e = moments(join_rows(sums, 0, 4), join_rows(sums, 4, 4), count4)
    norm_s = moments(join_rows(sums, 8, 4), join_rows(sums, 12, 4), count4)

    def summed(at):
        return (
            gamma(6, 4) * normed(v.pre_e, at, norm_e)
            + beta(6, 4)
            + gamma(1, 4) * normed(v.pre_s, at, norm_s)
            + beta(1, 4)
        )

    def make_merged(k):
        at = rows_at(k, 48)
        v.joined[t, at, :] = jax.nn.silu(summed(at)).astype(BF)

    loop(12, make_merged)

    j_send, j_recv = take(3), take(SPLITS)

    def joined_copy(k, slot, device):
        return remote(
            v.joined.at[slot], v.joined.at[slot], j_send + k, j_recv + slot, {TENSOR: device}
        )

    joined_copy(0, t, t_x).start()
    joined_copy(1, t, t_core).start()

    pool_move = ToGroup(
        lambda owner, rows: v.pool_half.at[lax.rem(owner, 2), 0:rows, :],
        lambda slot, rows: v.pool_all.at[slot, 0:rows, :],
    )
    bin_row = lax.broadcasted_iota(jnp.int32, (BINS, 1), 0)

    def group_mask(group, shape=None):
        low, top = GROUP_ROWS[group]
        kept = jnp.where((bin_row >= low) & (bin_row < top), 1.0, 0.0)
        return kept if shape is None else jnp.broadcast_to(kept, shape)

    cells_in = wide(v.cells_in[...], 4)
    pooled = dot(v.pool[...], v.joined[t]) / cells_in
    v.pooled[...] = pooled.astype(BF)
    for k in range(2):
        v.pool_half[k] = v.pooled[:, k * 256 : k * 256 + 256]
    v.pool_all[me] = v.pool_half[lax.rem(me, 2)]
    g_b0.finish()
    g_b1.finish()
    part = jnp.zeros((BINS, 512), F32)
    for group in range(4):
        rows = (v.pooled[...].astype(F32) * group_mask(group)).astype(BF)
        part = part + dot(rows, v.w_b[group * 512 : group * 512 + 512, :])
    for k in range(SPLITS):
        v.part_b[k] = part[:, k * 128 : k * 128 + 128].astype(BF)
    v.recv_b[t] = v.part_b[t]
    ex = Exchange(TENSOR, SPLITS, lambda o: v.part_b.at[o], lambda s: v.recv_b.at[s])
    ex.start()
    g_u.forward(0)
    g_u.start_near(1)
    g_u.start_far(2)
    joined_copy(0, t_x, t_x).wait_recv()
    joined_copy(2, t_x, t_core).start()
    ex.wait()
    own_b = v.recv_b[0].astype(F32)
    for k in range(1, SPLITS):
        own_b = own_b + v.recv_b[k].astype(F32)
    v.all_b[me] = own_b.astype(BF)
    ex = Exchange(BATCH, OWNERS, lambda o: v.all_b.at[me], lambda s: v.all_b.at[s])
    ex.start()
    g_u.forward(1)
    g_u.start_near(2)
    g_u.start_far(3)
    ex.wait()
    all_b = [v.all_b[k].astype(F32) for k in range(OWNERS)]
    sum_b, square_b = all_b[0], all_b[0] * all_b[0]
    for k in range(1, OWNERS):
        sum_b = sum_b + all_b[k]
        square_b = square_b + all_b[k] * all_b[k]
    mean_b = jnp.zeros((BINS, 128), F32)
    scale_b = jnp.zeros((BINS, 128), F32)
    gamma_b = jnp.zeros((BINS, 128), F32)
    beta_b = jnp.zeros((BINS, 128), F32)
    count_b = jnp.zeros((BINS, 1), F32)
    for group, bins in enumerate(BIN_COUNTS):
        kept = group_mask(group)
        size = float(OWNERS * bins * bins)
        mean, scaling = moments(total(sum_b * kept), total(square_b * kept), size)
        mean_b = mean_b + kept * mean
        scale_b = scale_b + kept * scaling
        gamma_b = gamma_b + kept * gamma(10 + group)
        beta_b = beta_b + kept * beta(10 + group)
        count_b = count_b + kept / size
    spread_b = Spread(v.act_b)
    for k in range(OWNERS):
        out = gamma_b * ((all_b[k] - mean_b) * scale_b) + beta_b
        v.act_b[t, k * BINS : k * BINS + BINS, :] = jax.nn.silu(out).astype(BF)
    spread_b.start()
    g_u.forward(2)
    g_u.start_near(3)
    g_u.start_far(4)
    spread_b.wait()
    row_512 = lax.broadcasted_iota(jnp.int32, (OWNERS * BINS, 1), 0) & (BINS - 1)
    group_id = jnp.where(
        row_512 < 1, 0, jnp.where(row_512 < 5, 1, jnp.where(row_512 < 14, 2, jnp.where(row_512 < 50, 3, 9)))
    )

    def full_act():
        return jnp.concatenate([v.act_b[k] for k in range(SPLITS)], axis=1)

    v.zsum[...] = jnp.zeros((2, OWNERS * BINS, 128), F32)

    def own_branch(j, body):
        chunk = lax.rem(me + j, 8)
        pl.when(chunk >= MERGED)(lambda: body(chunk - MERGED, lax.div(me + j, 8)))

    def make_z(j):
        def body(group, side):
            kept = jnp.where(group_id == group, 1.0, 0.0)
            rows = (full_act().astype(F32) * kept).astype(BF)
            v.zsum[side] = v.zsum[side] + dot(rows, v.w_own[rows_at(j, 512), :])

        own_branch(j, body)

    loop(9, make_z)
    for k in range(OWNERS):
        for side in range(2):
            v.z_send[k, side] = v.zsum[side, k * BINS : k * BINS + BINS, :].astype(BF)
    v.z_recv[me] = v.z_send[me]
    ex = Exchange(BATCH, OWNERS, lambda o: v.z_send.at[o], lambda s: v.z_recv.at[s])
    ex.start()
    g_u.forward(3)
    g_u.start_near(4)
    joined_copy(1, t_core, t_core).wait_recv()
    joined_copy(2, t_diag, t_core).wait_recv()
    for k in range(SPLITS):
        v.joined_t[k] = v.joined[k].T
    g_u.forward(4)
    g_c.forward()
    g_ac.forward()
    ex.wait()
    g_u.finish()

    def tap_z(tap):
        if tap == 0:
            return v.z_recv[0, 0].astype(F32)
        if tap == 8:
            return v.z_recv[7, 1].astype(F32)
        return v.z_recv[tap, 0].astype(F32) + v.z_recv[tap - 1, 1].astype(F32)

    for tap in range(9):
        z = tap_z(tap)
        high_z = z.astype(BF)
        v.z_cat[tap, :BINS, :] = high_z
        v.z_cat[tap, BINS:, :] = (z - high_z.astype(F32)).astype(BF)

    def full_joined():
        return jnp.concatenate([v.joined[k] for k in range(SPLITS)] + [v.pick_t[...]], axis=1)

    def w_tap(tap):
        return jnp.concatenate([v.w_u[rows_at(tap, 2048), :], v.z_cat[tap]], axis=0)

    def unite_pair(p):
        value = dot(full_joined(), jnp.concatenate([w_tap(2 * p), w_tap(2 * p + 1)], axis=1))
        v.pad[2 * p, EDGE : EDGE + CELLS, :] = value[:, :128]
        v.pad[2 * p + 1, EDGE : EDGE + CELLS, :] = value[:, 128:]

    loop(4, unite_pair)
    v.pad[8, EDGE : EDGE + CELLS, :] = dot(full_joined(), w_tap(8))
    for at in range(0, CELLS, BLOCK):
        v.pre_u[at : at + BLOCK, :] = shift_sum(range(9), 1, at, lambda tap: tap)
    sync = Sync(v.sync_five)
    sync.start(list(masked_sums(v.pre_u)))
    pool_move.start()
    g_a.start_far()
    g_a.start_near()
    for item in (g_c, g_ac):
        item.finish()
    for item in (g_gain, g_r, g_s, g_m, g_e, g_b0, g_b1, g_c, g_ac, g_u):
        item.drain()
    joined_copy(0, t, t_x).wait_send()
    joined_copy(1, t, t_core).wait_send()
    joined_copy(2, t_x, t_core).wait_send()
    w_ac = jnp.concatenate([v.w_ac[...], jnp.zeros((64, 256), F32)], axis=0).astype(BF)
    sums = sync.wait()
    norm_u = moments(sums[0:1], sums[1:2], count)

    def make_u(k):
        at = rows_at(k, 96)
        v.united[at, :] = jax.nn.silu(gamma(14) * normed(v.pre_u, at, norm_u) + beta(14)).astype(BF)

    loop(6, make_u)
    class Band:
        def __init__(self, at):
            self.at = at
            self.ex = Exchange(
                TENSOR,
                SPLITS,
                lambda o: v.logit_send.at[rows_at(o, 144), at],
                lambda s: v.logit_recv.at[s, :, at],
            )
            self.back = Spread(v.slope_in, at)

        def start(self, value):
            v.logit_send[:, self.at] = value.astype(BF)
            self.ex.start()
            v.logit_recv[t, :, self.at] = v.logit_send[rows_at(t, 144), self.at]

        def finish(self, factor):
            self.ex.wait()
            logits = v.logit_recv[0, :, self.at].astype(F32)
            for k in range(1, SPLITS):
                logits = logits + v.logit_recv[k, :, self.at].astype(F32)
            class_weight, loss_weight = class_weights()
            hot = jnp.where(wide(v.lab[rows_at(t, 144), :], 2) == lanes, 1.0, 0.0)
            cell_weight = factor * jnp.sum(hot * class_weight, axis=1, keepdims=True)
            value = jnp.where(lanes < float(NCLS), logits, -1e30)
            value = value - jnp.max(value, axis=1, keepdims=True)
            powers = jnp.exp(value)
            mass = jnp.sum(powers, axis=1, keepdims=True)
            loss_rows = total(fold(-cell_weight * hot * (value - jnp.log(mass))))
            grad = cell_weight * (powers / mass - hot) / loss_weight
            v.slope_in[t, :, self.at] = grad.astype(BF)
            self.back.start()
            return loss_rows[:, :128] + loss_rows[:, 128:]

        def grad(self):
            self.back.wait()
            return v.slope_in[:, :, self.at].reshape(CELLS, 256)

    def class_weights():
        total_valid = jnp.sum(class_count, axis=1, keepdims=True)
        weight = total_valid / (NCLS * class_count + total_valid)
        whole = jnp.sum(class_count * weight, axis=1, keepdims=True)
        return jnp.where(lanes < float(NCLS), weight, 0.0), whole

    main_head, aux_head = Band(slice(0, 256)), Band(slice(256, 512))
    main_head.start(dot(v.united[...], v.w_c[...]))
    g_a.forward()
    o_misc[1:2, :] = main_head.finish(1.0)

    g_a.finish()
    g_a.drain()

    def unpack(chunk):
        for pair in range(5):
            even = v.w_a[rows_at(2 * pair * 8 + chunk, 64), :].astype(F32)
            if pair < 4:
                odd = v.w_a[rows_at((2 * pair + 1) * 8 + chunk, 64), :].astype(F32)
            else:
                odd = jnp.zeros((64, 128), F32)
            low = jnp.where(left_half, even, pltpu.roll(odd, 64, 1))
            top = jnp.where(left_half, pltpu.roll(even, 64, 1), odd)
            v.pad[pair, pl.ds(EDGE, 64, stride=2), :] = low
            v.pad[pair, pl.ds(EDGE + 1, 64, stride=2), :] = top
            both = v.pad[pair, EDGE : EDGE + 128, :]
            v.w_pair[rows_at(chunk, 128), pair * 128 : pair * 128 + 128] = both.astype(BF)

    loop(8, unpack)

    for pair in (0, 2):
        value = dot(whole_feat(), v.w_pair[:, pair * 128 : pair * 128 + 256])
        v.pad[pair, EDGE : EDGE + CELLS, :] = value[:, :128]
        v.pad[pair + 1, EDGE : EDGE + CELLS, :] = value[:, 128:]
    v.pad[4, EDGE : EDGE + CELLS, :] = dot(whole_feat(), v.w_pair[:, 512:640])

    left_wide = lax.broadcasted_iota(jnp.int32, (BLOCK, 128), 1) < 64
    for at in range(0, CELLS, BLOCK):
        even = shift_sum((0, 2, 4, 6, 8), 1, at, lambda tap: tap // 2)
        odd = shift_sum((1, 3, 5, 7), 1, at, lambda tap: tap // 2)
        v.pre_a[at : at + BLOCK, :] = jnp.where(left_wide, even + pltpu.roll(odd, 64, 1), 0.0)

    sync_a = Sync(v.sync_aux)
    sync_a.start(list(masked_sums(v.pre_a)))
    g_main = main_head.grad()
    v.d_f[...] = dot_nt(g_main, v.w_c[...])

    def slope(value):
        gate = jax.nn.sigmoid(value)
        return gate * (1.0 + value * (1.0 - gate))

    def through_silu(ref, pre, norm, row):
        def step(k, carry):
            at = rows_at(k, 96)
            unit = normed(pre, at, norm)
            value = ref[at, :] * slope(gamma(row) * unit + beta(row))
            ref[at, :] = value
            return (carry[0] + fold(value), carry[1] + fold(value * unit))

        zero = jnp.zeros((8, 128), F32)
        sums = lax.fori_loop(0, 6, step, (zero, zero))
        return [total(sums[0]), total(sums[1])]

    def back_norm(value, unit, mask, norm, gain, first, second, size):
        inner = value - mask * (first + unit * second) / size
        return gain * norm[1] * inner

    gain_grads = {}
    sync = Sync(v.sync_b1)
    sync.start(through_silu(v.d_f, v.pre_u, norm_u, 14))
    sums = sync_a.wait()
    norm_a = moments(sums[0:1], sums[1:2], count)

    def make_a(k):
        at = rows_at(k, 96)
        v.act_a[at, :] = jax.nn.silu(gamma(15) * normed(v.pre_a, at, norm_a) + beta(15)).astype(BF)

    loop(6, make_a)
    aux_head.start(dot(v.act_a[...], w_ac))

    class Scatter:
        def __init__(self, first, second, full, rows, out, base=0):
            self.full, self.rows, self.out, self.base = full, rows, out, base
            self.first, self.second = first, second
            self.near_s, self.near_r = take(HALF), take(HALF)
            self.far_s, self.far_r = take(HALF), take(HALF)
            self.block = min(rows, 64)

        def near(self, step):
            dest = far_peer(partner, step)
            return remote(
                self.full.at[rows_at(dest, self.rows), :],
                self.first.at[step],
                self.near_s + step,
                self.near_r + step,
                {BATCH: partner},
            )

        def far(self, step):
            return remote(
                self.first.at[step],
                self.second.at[step - 1],
                self.far_s + step,
                self.far_r + step,
                {BATCH: far_peer(me, step)},
            )

        def start(self):
            for step in (1, 2, 3, 0):
                self.near(step).start()

        def middle(self):
            kind = self.first.dtype
            for step in range(1, HALF):
                self.near(step).wait_recv()
                base = far_peer(me, step) * (self.rows // self.block)

                def add(k, step=step, base=base):
                    at = rows_at(k, self.block)
                    value = self.full[rows_at(base + k, self.block), :].astype(F32)
                    value = value + self.first[step, at, :].astype(F32)
                    self.first[step, at, :] = value.astype(kind)

                loop(self.rows // self.block, add)
                self.far(step).start()

        def end(self):
            self.near(0).wait_recv()
            for step in range(1, HALF):
                self.far(step).wait_recv()
            base = me * (self.rows // self.block)

            def add(k, carry):
                at = rows_at(k, self.block)
                value = self.full[rows_at(base + k, self.block), :].astype(F32)
                value = value + self.first[0, at, :].astype(F32)
                for step in range(1, HALF):
                    value = value + self.second[step - 1, at, :].astype(F32)
                if self.out is o_flat:
                    times = value.shape[1] // 128
                    start = self.base + k * self.block * times
                    for q in range(times):
                        where = pl.ds(start + q, self.block, stride=times if times > 1 else None)
                        self.out[where, :] = value[:, q * 128 : q * 128 + 128]
                else:
                    self.out[at, :] = value
                return carry + fold(value * value)

            squares = lax.fori_loop(
                0, self.rows // self.block, add, jnp.zeros((8, self.full.shape[1]), F32)
            )
            for step in (1, 2, 3, 0):
                self.near(step).wait_send()
                if step:
                    self.far(step).wait_send()
            return sum(split_rows(total(squares)))

    s_c = Scatter(v.first_c, v.second_c, v.w_c, 16, v.out_c)
    s_ac = Scatter(v.first_ac, v.second_ac, v.w_ac, 8, v.out_ac)
    s_a = Scatter(v.first_a, v.second_a, v.w_a, 576, v.out_a)
    s_s = Scatter(v.first_s, v.second_s, v.w_s, 128, o_flat, 128)
    s_e = Scatter(v.first_e, v.second_e, v.w_e, 64, o_flat, 1216)
    s_m = Scatter(v.first_m, v.second_m, v.w_m, 576, o_flat, 640)
    s_r = Scatter(v.first_r, v.second_r, v.w_r, 128, o_flat, 0)

    class ScatterUnite:
        def __init__(self):
            self.near_s, self.near_r = take(SLOTS * HALF), take(SLOTS * HALF)
            self.far_s, self.far_r = take(SLOTS * HALF), take(SLOTS * HALF)

        def near(self, step, slot, base):
            dest = far_peer(base, step)
            return remote(
                v.w_u.at[merged_rows(dest, slot), :],
                v.first_u.at[step, slot],
                self.near_s + step * SLOTS + slot,
                self.near_r + step * SLOTS + slot,
                {BATCH: partner},
            )

        def far(self, step, slot):
            return remote(
                v.first_u.at[step, slot],
                v.second_u.at[step - 1, slot],
                self.far_s + step * SLOTS + slot,
                self.far_r + step * SLOTS + slot,
                {BATCH: far_peer(me, step)},
            )

        def own_rows(self, owner, slot, k):
            block = owner * 9 + block_of(owner, slot)
            index = lax.div(block, 8) * MERGED + lax.rem(block, 8)
            return rows_at(index * 8 + k, 64)

        def start(self, slot):
            for step in (1, 2, 3, 0):
                has(
                    far_peer(partner, step),
                    slot,
                    lambda step=step: self.near(step, slot, partner).start(),
                )

        def middle(self, slot):
            for step in range(1, HALF):
                owner = far_peer(me, step)

                def go(step=step, owner=owner):
                    self.near(step, slot, me).wait_recv()

                    def add(k):
                        at = rows_at(k, 64)
                        value = v.w_u[self.own_rows(owner, slot, k), :].astype(F32)
                        value = value + v.first_u[step, slot, at, :].astype(F32)
                        v.first_u[step, slot, at, :] = value.astype(BF)

                    loop(8, add)
                    self.far(step, slot).start()

                has(owner, slot, go)

        def end(self):
            for slot in range(SLOTS):

                def go(slot=slot):
                    self.near(0, slot, me).wait_recv()
                    for step in range(1, HALF):
                        self.far(step, slot).wait_recv()
                    j = block_of(me, slot)

                    def add(k):
                        at = rows_at(k, 64)
                        value = v.w_u[self.own_rows(me, slot, k), :].astype(F32)
                        value = value + v.first_u[0, slot, at, :].astype(F32)
                        for step in range(1, HALF):
                            value = value + v.second_u[step - 1, slot, at, :].astype(F32)
                        o_u[rows_at(j * 8 + k, 64), :] = value

                    loop(8, add)

                has(me, slot, go)
                for step in (1, 2, 3, 0):
                    has(
                        far_peer(partner, step),
                        slot,
                        lambda step=step, slot=slot: self.near(step, slot, partner).wait_send(),
                    )
                    if step:
                        has(
                            far_peer(me, step),
                            slot,
                            lambda step=step, slot=slot: self.far(step, slot).wait_send(),
                        )

            def square(k, carry):
                value = o_u[rows_at(k, 64), :]
                return carry + fold(value * value)

            squares = lax.fori_loop(0, 72, square, jnp.zeros((8, 128), F32))
            return sum(split_rows(total(squares)))

    s_u = ScatterUnite()

    v.w_c[...] = dot_tn(v.united[...], g_main).astype(BF)
    s_c.start()
    sums = sync.wait()
    gain_grads[14] = (sums[1:2], sums[0:1])

    def spread_taps(ref, pre, norm, row, first, second):
        def step(k):
            at = rows_at(k, 96)
            value = back_norm(
                ref[at, :], normed(pre, at, norm), v.ins[at, :], norm, gamma(row), first, second, count
            )
            ref[at, :] = value.astype(BF).astype(F32)

        loop(6, step)
        v.grad_pad[EDGE : EDGE + CELLS, :] = ref[...]

    def back_tap(tap, spacing, at):
        start = EDGE + at - offset(tap, spacing)
        value = v.grad_pad[start : start + 96, :]
        right = tap % 3 - 1
        if right:
            value = value * col_mask(slice(at, at + 96), -right * spacing)
        return value

    def fill(cat, spacing):
        for tap in range(9):
            for at in range(0, CELLS, 96):
                cat[at : at + 96, tap * 128 : tap * 128 + 128] = back_tap(tap, spacing, at).astype(
                    BF
                )

    spread_taps(v.d_f, v.pre_u, norm_u, 14, sums[0:1], sums[1:2])
    fill(v.cat_u, 1)

    dz = dot(v.pick[...], v.cat_u[...])
    for tap in range(9):
        v.dz_send[tap] = dz[:, tap * 128 : tap * 128 + 128].astype(BF)
    v.dz_recv[me] = v.dz_send[pl.ds(me, 2)]
    ex_dz = Exchange(
        BATCH, OWNERS, lambda o: v.dz_send.at[pl.ds(o, 2)], lambda s: v.dz_recv.at[s]
    )
    ex_dz.start()

    def merged_back(c):
        weight = jnp.concatenate(
            [v.w_u[rows_at(tap * MERGED + c, 512), :] for tap in range(9)], axis=1
        )
        v.joined[c] = dot_nt(v.cat_u[...], weight).astype(BF)

    near_s, near_r, far_s, far_r = take(2), take(2), take(1), take(1)

    def dm_near(k, slot):
        return remote(
            v.joined.at[slot], v.dm_near.at[k], near_s + k, near_r + k, {TENSOR: t_core}
        )

    merged_back(t_diag)
    dm_near(1, t_diag).start()
    merged_back(t_core)
    dm_near(0, t_core).start()
    o_misc[1:2, :] = o_misc[1:2, :] + aux_head.finish(0.4)
    ex_dz.wait()

    d_act = v.d_sum.at[0 : OWNERS * BINS, :]
    d_act[...] = jnp.zeros((OWNERS * BINS, 512), F32)

    def branch_back(j):
        def body(group, side):
            kept = jnp.where(group_id == group, 1.0, 0.0)
            value = v.dz_recv[:, side].reshape(OWNERS * BINS, 128).astype(F32) * kept
            value = value.astype(BF)
            o_u[rows_at(j, 512), :] = dot_tn(full_act(), value)
            d_act[...] = d_act[...] + dot_nt(value, v.w_own[rows_at(j, 512), :])

        own_branch(j, body)

    loop(9, branch_back)
    for k in range(SPLITS):
        v.d_act_send[k] = d_act[:, k * 128 : k * 128 + 128].astype(BF)
    v.d_act_recv[t] = v.d_act_send[t]
    ex = Exchange(TENSOR, SPLITS, lambda o: v.d_act_send.at[o], lambda s: v.d_act_recv.at[s])
    ex.start()
    merged_back(t_x)
    merged_back(t)
    g_aux = aux_head.grad()
    v.d_f2[...] = dot_nt(g_aux, w_ac)
    sync_a = Sync(v.sync_b2)
    sync_a.start(through_silu(v.d_f2, v.pre_a, norm_a, 15))
    v.w_ac[...] = dot_tn(v.act_a[...], g_aux)[:64]
    s_ac.start()

    def unite_grad(c):
        for p in range(5):
            width = 256 if p < 4 else 128
            value = dot(v.joined_t[c], v.cat_u[:, p * 256 : p * 256 + width])
            v.w_u[rows_at(2 * p * MERGED + c, 512), :] = value[:, :128].astype(BF)
            if p < 4:
                v.w_u[rows_at((2 * p + 1) * MERGED + c, 512), :] = value[:, 128:].astype(BF)

    loop(SPLITS, unite_grad)
    s_u.start(0)
    dm_near(1, t_x).wait_recv()

    def add_x(k):
        at = rows_at(k, 48)
        value = v.joined[t_x, at, :].astype(F32) + v.dm_near[1, at, :].astype(F32)
        v.joined[t_x, at, :] = value.astype(BF)

    loop(12, add_x)
    dm_far = remote(v.joined.at[t_x], v.dm_far, far_s, far_r, {TENSOR: t_x})
    ex.wait()
    for k in range(OWNERS):
        at = slice(k * BINS, k * BINS + BINS)
        value = v.d_act_recv[0, at, :].astype(F32)
        for slot in range(1, SPLITS):
            value = value + v.d_act_recv[slot, at, :].astype(F32)
        v.d_img_send[k] = value.astype(BF)
    v.d_img_recv[me] = v.d_img_send[me]
    ex = Exchange(BATCH, OWNERS, lambda o: v.d_img_send.at[o], lambda s: v.d_img_recv.at[s])
    ex.start()
    dm_far.start()
    s_u.start(1)

    sums = sync_a.wait()
    gain_grads[15] = (sums[1:2], sums[0:1])
    spread_taps(v.d_f2, v.pre_a, norm_a, 15, sums[0:1], sums[1:2])
    for p in range(5):
        for at in range(0, CELLS, 96):
            value = back_tap(2 * p, 1, at)
            if p < 4:
                value = value + pltpu.roll(back_tap(2 * p + 1, 1, at), 64, 1)
            v.cat_a[at : at + 96, p * 128 : p * 128 + 128] = value.astype(BF)

    def aux_grad(c2):
        value2 = dot_tn(v.whole[c2], v.cat_a[...])
        for half in range(2):
            value = value2[half * 128 : half * 128 + 128]
            c = 2 * c2 + half
            for p in range(5):
                v.pad[p, EDGE : EDGE + 128, :] = value[:, p * 128 : p * 128 + 128]
                low = v.pad[p, pl.ds(EDGE, 64, stride=2), :]
                top = v.pad[p, pl.ds(EDGE + 1, 64, stride=2), :]
                even = jnp.where(left_half, low, pltpu.roll(top, 64, 1))
                v.w_a[rows_at(2 * p * 8 + c, 64), :] = even.astype(BF)
                if p < 4:
                    odd = jnp.where(left_half, pltpu.roll(low, 64, 1), top)
                    v.w_a[rows_at((2 * p + 1) * 8 + c, 64), :] = odd.astype(BF)

    loop(SPLITS, aux_grad)
    s_u.middle(0)
    ex.wait()
    d_b = v.d_img_recv[0].astype(F32)
    for k in range(1, OWNERS):
        d_b = d_b + v.d_img_recv[k].astype(F32)
    unit_b = (v.all_b[me].astype(F32) - mean_b) * scale_b
    d_b = d_b * slope(gamma_b * unit_b + beta_b)
    sync = Sync(v.sync_b3)
    sync.start(
        [total(d_b * group_mask(g)) for g in range(4)]
        + [total(d_b * unit_b * group_mask(g)) for g in range(4)]
    )
    s_u.start(2)
    sums = sync.wait()
    first_b = jnp.zeros((BINS, 128), F32)
    second_b = jnp.zeros((BINS, 128), F32)
    for group in range(4):
        kept = group_mask(group)
        gain_grads[10 + group] = (sums[4 + group : 5 + group], sums[group : group + 1])
        first_b = first_b + kept * sums[group : group + 1]
        second_b = second_b + kept * sums[4 + group : 5 + group]
    inner = d_b - (first_b + unit_b * second_b) * count_b
    v.d_bp[t] = (gamma_b * scale_b * inner).astype(BF)
    spread_d = Spread(v.d_bp)
    spread_d.start()
    s_u.start(3)
    s_u.middle(1)
    spread_d.wait()
    d_bp_move = ToGroup(
        lambda owner, rows: v.d_bp.at[:, 0:rows, :],
        lambda slot, rows: v.d_bp_all.at[slot, :, 0:rows, :],
    )
    d_bp_move.start()
    v.d_bp_all[me] = v.d_bp[...]
    d_bp = jnp.concatenate([v.d_bp[k] for k in range(SPLITS)], axis=1)
    d_pooled = jnp.zeros((BINS, 512), F32)
    for group in range(4):
        rows = (d_bp.astype(F32) * group_mask(group)).astype(BF)
        d_pooled = d_pooled + dot_nt(rows, v.w_b[group * 512 : group * 512 + 512, :])
    d_pooled = (d_pooled / cells_in).astype(BF)
    v.d_sum[...] = dot_tn(v.pool[...], d_pooled)
    dm_near(0, t).wait_recv()
    dm_far.wait_recv()

    def through_sum(k, carry):
        at = rows_at(k, 48)
        value = v.d_sum[at, :] + v.joined[t, at, :].astype(F32) + v.dm_near[0, at, :].astype(F32)
        value = (value + v.dm_far[at, :].astype(F32)) * slope(summed(at))
        v.d_sum[at, :] = value
        return (
            carry[0] + fold(value),
            carry[1] + fold(value * normed(v.pre_e, at, norm_e)),
            carry[2] + fold(value * normed(v.pre_s, at, norm_s)),
        )

    zero = jnp.zeros((8, 512), F32)
    three = [total(item) for item in lax.fori_loop(0, 12, through_sum, (zero, zero, zero))]
    sync = Sync(v.sync_b4)
    sync.start(split_rows(three[0]) + split_rows(three[1]) + split_rows(three[2]))
    s_u.start(4)
    s_u.middle(2)
    sums = sync.wait()
    first_s = join_rows(sums, 0, 4)
    second_e, second_s = join_rows(sums, 4, 4), join_rows(sums, 8, 4)
    for k in range(4):
        gain_grads[6 + k] = (sums[4 + k : 5 + k], sums[k : k + 1])
        gain_grads[1 + k] = (sums[8 + k : 9 + k], sums[k : k + 1])

    def back_both(k):
        at = rows_at(k, 48)
        value, mask = v.d_sum[at, :], wide(v.ins[at, :], 4)
        v.d_e[at, :] = back_norm(
            value, normed(v.pre_e, at, norm_e), mask, norm_e, gamma(6, 4), first_s, second_e, count4
        ).astype(BF)
        v.d_s[at, :] = back_norm(
            value, normed(v.pre_s, at, norm_s), mask, norm_s, gamma(1, 4), first_s, second_s, count4
        ).astype(BF)

    loop(12, back_both)

    def back_hidden(grad, weight, index):
        value = dot_nt(grad, weight)
        for k in range(SPLITS):
            v.dh_send[k] = value[:, k * 128 : k * 128 + 128].astype(BF)
        v.dh_recv[index, t] = v.dh_send[t]
        ex = Exchange(
            TENSOR, SPLITS, lambda o: v.dh_send.at[o], lambda s: v.dh_recv.at[index, s]
        )
        ex.start()
        return ex

    def hidden_sum(index):
        def step(k):
            at = rows_at(k, 96)
            value = v.dh_recv[index, 0, at, :].astype(F32)
            for slot in range(1, SPLITS):
                value = value + v.dh_recv[index, slot, at, :].astype(F32)
            v.d_f[at, :] = value

        loop(6, step)

    ex = back_hidden(v.d_e[...], v.w_e[...], 0)
    s_a.start()
    s_u.middle(3)
    for k in range(SPLITS):
        v.w_e[k * 128 : k * 128 + 128, :] = dot_tn(v.h2[k], v.d_e[...]).astype(BF)
    ex.wait()
    hidden_sum(0)
    sync = Sync(v.sync_b5)
    sync.start(through_silu(v.d_f, v.pre_m, norm_m, 5))
    s_e.start()
    s_c.middle()
    s_ac.middle()
    s_u.middle(4)
    sums = sync.wait()
    gain_grads[5] = (sums[1:2], sums[0:1])
    spread_taps(v.d_f, v.pre_m, norm_m, 5, sums[0:1], sums[1:2])
    fill(v.cat_u, 4)
    weight = jnp.concatenate([v.w_m[tap * 512 : tap * 512 + 512, :] for tap in range(9)], axis=1)
    ex = back_hidden(v.cat_u[...], weight, 1)

    def short_grad(c):
        v.w_s[rows_at(c, 256), :] = dot_tn(v.whole[c], v.d_s[...]).astype(BF)

    loop(SPLITS, short_grad)
    s_s.start()
    s_a.middle()
    ex.wait()
    hidden_sum(1)
    sync = Sync(v.sync_b6)
    sync.start(through_silu(v.d_f, v.pre_r, norm_r, 0))

    def middle_grad(k):
        value = dot_tn(v.h1[k], v.cat_u[...])
        for tap in range(9):
            v.w_m[rows_at(tap * 4 + k, 128), :] = value[:, tap * 128 : tap * 128 + 128].astype(BF)

    loop(SPLITS, middle_grad)
    s_m.start()
    s_e.middle()
    s_s.middle()
    sums = sync.wait()
    gain_grads[0] = (sums[1:2], sums[0:1])

    def back_reduce(k):
        at = rows_at(k, 96)
        v.d_low[at, :] = back_norm(
            v.d_f[at, :], normed(v.pre_r, at, norm_r), v.ins[at, :], norm_r, gamma(0), sums[0:1], sums[1:2], count
        ).astype(BF)

    loop(6, back_reduce)

    def reduce_grad(c):
        v.w_r[rows_at(c, 256), :] = dot_tn(v.whole[c], v.d_low[...]).astype(BF)

    loop(SPLITS, reduce_grad)
    s_r.start()
    for item in (s_m, s_r):
        item.middle()
    pool_move.wait()
    d_bp_move.wait()
    own_group = jnp.where(group_id == lax.div(me, 2), 1.0, 0.0)
    d_rows = jnp.concatenate(
        [v.d_bp_all[:, k].reshape(OWNERS * BINS, 128) for k in range(SPLITS)], axis=1
    )
    d_rows = (d_rows.astype(F32) * own_group).astype(BF)
    branch_grad = dot_tn(v.pool_all[...].reshape(OWNERS * BINS, 256), d_rows)
    for k in range(4):
        o_flat[pl.ds(1472 + k, 256, stride=4), :] = branch_grad[:, k * 128 : k * 128 + 128]
    rest = (s_c, s_ac, s_a, s_e, s_s, s_m, s_r)
    squares = s_u.end() + sum(split_rows(total(branch_grad * branch_grad)))
    for item in rest:
        squares = squares + item.end()
    dm_near(1, t_diag).wait_send()
    dm_near(0, t_core).wait_send()
    dm_far.wait_send()

    v.gain_rows[...] = jnp.zeros((40, 128), F32)
    gammas = [gain_grads[row][0] for row in range(16)]
    betas = [pltpu.roll(gain_grads[row][1], 64, 1) for row in range(16)]
    o_shift[...] = gain_grads[14][1]
    for row in range(31):
        if row < 15:
            value = gammas[row]
        else:
            left = gammas[15] if row == 15 else betas[row - 16]
            value = jnp.where(lane < 64, left, betas[row - 15])
        v.gain_rows[row + 1 : row + 2, :] = value
    squares = squares + total(fold(v.gain_rows[...] * v.gain_rows[...])) / OWNERS

    sync = Sync(v.sync_end)
    sync.start([squares, o_misc[1:2, :]])

    tail = {}

    def put(where, value):
        tail[where] = value if where not in tail else tail[where] + value

    def class_tail(ref, count, base):
        for row in range(count):
            first, shift = divmod(base + NCLS * row, 128)
            for k in range(2):
                value = roll(ref[row : row + 1, k * 128 : k * 128 + 128], shift)
                put(first + k, jnp.where(lane >= shift, value, 0.0))
                if shift:
                    put(first + k + 1, jnp.where(lane < shift, value, 0.0))

    class_tail(v.out_c, 16, 0)
    class_tail(v.out_ac, 8, 76128)
    start = lax.rem(496 * me, 128)
    first = lax.div(496 * me, 128)
    own = [
        pltpu.roll(v.gain_rows[pl.ds(first + k, 1), :], lax.rem(16 - start + 128, 128), 1)
        for k in range(6)
    ]
    spot = lane - 16 + start
    for k in range(4):
        value = jnp.where(spot < 0, own[k], jnp.where(spot >= 128, own[k + 2], own[k + 1]))
        put(604 + k, jnp.where(lane >= 16, value, 0.0) if k == 0 else value)
    v.grad_pad[EDGE : EDGE + 576, :] = pltpu.roll(v.out_a[...], 96, 1)
    o_flat[7122:7706, :] = jnp.where(
        lane >= 96, v.grad_pad[EDGE : EDGE + 584, :], v.grad_pad[EDGE - 1 : EDGE + 583, :]
    )
    for row in range(608):
        if row in (18, 594):
            o_flat[7104 + row : 7105 + row, :] = o_flat[7104 + row : 7105 + row, :] + tail[row]
        elif row < 18 or row > 594:
            o_flat[7104 + row : 7105 + row, :] = tail[row]
    v.end_t[t] = sync.wait()
    spread_e = Spread(v.end_t)
    spread_e.start()
    spread_e.wait()
    ends = v.end_t[0]
    for k in range(1, SPLITS):
        ends = ends + v.end_t[k]
    o_misc[...] = ends
    o_misc[2:3, :] = jnp.broadcast_to(class_weights()[1], (1, 128))


def whole_step(sizes, labels, feat, flat):
    plan = scratch_plan()
    vmem = pl.BlockSpec(memory_space=pltpu.VMEM)
    anywhere = pl.BlockSpec(memory_space=pl.ANY)
    outs = [flat.shape, (1, 128), (8, 128)]
    return pl.pallas_call(
        functools.partial(step_kernel, tuple(plan)),
        out_shape=[jax.ShapeDtypeStruct(shape, F32) for shape in outs],
        in_specs=[pl.BlockSpec(memory_space=pltpu.SMEM), vmem, anywhere, anywhere],
        out_specs=[vmem] * len(outs),
        scratch_shapes=[pltpu.VMEM(shape, kind) for shape, kind in plan.values()]
        + [pltpu.SemaphoreType.DMA((SEMAPHORES,))],
        compiler_params=pltpu.CompilerParams(
            collective_id=0, has_side_effects=True, vmem_limit_bytes=63 * 1024 * 1024
        ),
        name="whole_step",
    )(sizes, labels, feat, flat)


def update_kernel(
    misc, grad, param, first, second, average,
    o_param, o_first, o_second, o_average, o_norm, o_loss, o_weight,
):
    norm = jnp.sqrt(jnp.sum(misc[0:1, :], axis=1, keepdims=True))
    o_norm[...] = norm
    o_loss[...] = jnp.sum(misc[1:2, :], axis=1, keepdims=True)
    o_weight[...] = misc[2:3, 0:1]
    clipped = grad[...] * jnp.minimum(1.0, 0.05 / (norm + 1e-06))
    new_first = 0.5 * first[...] + 0.5 * clipped
    new_second = 0.5 * second[...] + 0.5 * clipped * clipped
    lift = 1.0 / (1.0 - 0.5**STEP)
    old = param[...]
    ratio = (new_first * lift) / (jnp.sqrt(new_second * lift) + 1e-08)
    new = old - 0.01 * (ratio + 0.01 * old)
    o_param[...] = new
    o_first[...] = new_first
    o_second[...] = new_second
    o_average[...] = 0.999 * average[...] + 0.001 * new


def update(misc, grad, param, first, second, average):
    rows = grad.shape[0]
    block = pl.BlockSpec((1024, 128), lambda i: (i, 0))
    whole = pl.BlockSpec((8, 128), lambda i: (0, 0))
    one = pl.BlockSpec((1, 1), lambda i: (0, 0))
    big = jax.ShapeDtypeStruct((rows, 128), F32)
    return pl.pallas_call(
        update_kernel,
        grid=(pl.cdiv(rows, 1024),),
        out_shape=[big] * 4 + [jax.ShapeDtypeStruct((1, 1), F32)] * 3,
        in_specs=[whole] + [block] * 5,
        out_specs=[block] * 4 + [one] * 3,
        compiler_params=pltpu.CompilerParams(vmem_limit_bytes=60 * 1024 * 1024),
        name="update",
    )(misc, grad, param, first, second, average)


def fits(splits, owners):
    return splits == SPLITS and owners == OWNERS


def local_fast(features, labels, valid, sizes, params, first_moment, squared_mean, average):
    flat = params.reshape(-1, 128)
    marked = jnp.where(valid > 0, labels, -1).astype(F32).reshape(CELLS, 1)
    grad, shift_grad, misc = whole_step(
        sizes, jnp.broadcast_to(marked, (CELLS, 128)), features.reshape(CELLS, -1), flat
    )
    news = update(
        misc,
        grad,
        flat,
        first_moment.reshape(-1, 128),
        squared_mean.reshape(-1, 128),
        average.reshape(-1, 128),
    )
    new_params, new_first, new_second, new_average = [
        item.reshape(params.shape) for item in news[:4]
    ]
    return (
        new_params,
        new_first,
        new_second,
        new_average,
        new_params.astype(BF),
        news[4].reshape(()),
        news[5].reshape(()),
        news[6].reshape(()),
        shift_grad.reshape(128),
    )


def solution(mesh):
    chosen = local_fast if fits(mesh.shape["tensor"], mesh.shape["batch"]) else local
    return jax.shard_map(
        chosen,
        mesh=mesh,
        in_specs=(
            P("batch", None, None, "tensor"),
            P("batch", None, None),
            P("batch", None, None),
            P("batch", None),
            P("tensor", "batch"),
            P("tensor", "batch"),
            P("tensor", "batch"),
            P("tensor", "batch"),
        ),
        out_specs=(
            P("tensor", "batch"),
            P("tensor", "batch"),
            P("tensor", "batch"),
            P("tensor", "batch"),
            P("tensor", "batch"),
            P(),
            P(),
            P(),
            P("tensor"),
        ),
        check_vma=False,
    )
```

```python
import functools

import jax
import jax.numpy as jnp
from jax import lax
from jax.experimental import pallas as pl
from jax.experimental.pallas import tpu as pltpu
from jax.sharding import PartitionSpec as P

C_IN = 1024
MID = 512
C_OUT = 2048
PPM = 512
AUXW = 256
NCLS = 150
MAP = 24
STEP = 3


BIN_COUNTS = (1, 2, 3, 6)
BIN_STARTS = (0, 1, 5, 14)


def segment_shapes(splits):
    return [
        (C_IN, MID // splits),
        (C_IN, C_OUT // splits),
        (9, MID, MID // splits),
        (MID, C_OUT // splits),
        (4, C_OUT // splits, PPM),
        (9, C_OUT + 4 * PPM, PPM // splits),
        (PPM // splits, NCLS),
        (9, C_IN, AUXW // splits),
        (AUXW // splits, NCLS),
        (2, (2 * MID + 2 * C_OUT + 5 * PPM + AUXW) // splits),
    ]


def unflatten(rows, splits):
    split_parts = []
    start = 0
    for shape in segment_shapes(splits):
        count = 1
        for extent in shape:
            count = count * extent
        count = count // rows.shape[0]
        split_parts.append(rows[:, start : start + count].reshape(shape))
        start = start + count
    return split_parts


def gain_pieces(gains, splits):
    widths = [MID, C_OUT, MID, C_OUT, PPM, PPM, PPM, PPM, PPM, AUXW]
    split_parts = []
    start = 0
    for width in widths:
        step_width = width // splits
        split_parts.append(gains[:, start : start + step_width])
        start = start + step_width
    return split_parts


def shifted(field, down, right):
    image_height, width = (field.shape[1], field.shape[2])
    rows_pad, cols_pad = (abs(down), abs(right))
    padded = jnp.pad(field, ((0, 0), (rows_pad, rows_pad), (cols_pad, cols_pad), (0, 0)))
    return padded[
        :,
        rows_pad + down : rows_pad + down + image_height,
        cols_pad + right : cols_pad + right + width,
        :,
    ]


def conv_forward(field, kernel, spacing):
    total = jnp.zeros(field.shape[:-1] + (kernel.shape[2],), jnp.float32)
    for tap in range(9):
        moved = shifted(field, (tap // 3 - 1) * spacing, (tap % 3 - 1) * spacing)
        total = total + jnp.dot(moved, kernel[tap], preferred_element_type=jnp.float32)
    return total


def conv_input_back(grad, kernel, spacing):
    total = jnp.zeros(grad.shape[:-1] + (kernel.shape[1],), jnp.float32)
    for tap in range(9):
        product = jnp.dot(grad, kernel[tap].T, preferred_element_type=jnp.float32)
        total = total + shifted(product, -(tap // 3 - 1) * spacing, -(tap % 3 - 1) * spacing)
    return total


def conv_kernel_back(field, grad, spacing):
    return jnp.stack(
        [
            jnp.einsum(
                "ihwc,ihwd->cd",
                shifted(field, (tap // 3 - 1) * spacing, (tap % 3 - 1) * spacing),
                grad,
                preferred_element_type=jnp.float32,
            )
            for tap in range(9)
        ]
    )


def silu_slope(value):
    gate = jax.nn.sigmoid(value)
    return gate * (1.0 + value * (1.0 - gate))


def channel_sums(values):
    return values.reshape(-1, values.shape[-1]).sum(0)


def masked_norm_apply(items, extra):
    sends = []
    for value, mask, norm in items:
        sends = sends + [
            channel_sums(value * mask),
            channel_sums(value * value * mask),
            jnp.sum(mask) * jnp.ones((1,), jnp.float32),
        ]
    totals = lax.psum(tuple(sends + extra), "batch")
    results = []
    for index, (value, mask, norm) in enumerate(items):
        count = totals[3 * index + 2]
        mean = totals[3 * index] / count
        spread = totals[3 * index + 1] / count - mean * mean
        scaling = lax.rsqrt(spread + 1e-05)
        normed = (value - mean) * scaling
        results.append((norm[0] * normed + norm[1], normed, scaling, count, mask, norm[0]))
    return (results, totals[3 * len(items) :])


def norm_backward(items):
    sends = []
    for grad, kept in items:
        sends = sends + [channel_sums(grad), channel_sums(grad * kept[1])]
    totals = lax.psum(tuple(sends), "batch")
    results = []
    for index, (grad, kept) in enumerate(items):
        outcome, normed, scaling, count, mask, gamma = kept
        first_sum, second_sum = (totals[2 * index], totals[2 * index + 1])
        inner = grad - mask * (first_sum + normed * second_sum) / count
        results.append(gamma * scaling * inner)
    return (results, sends, totals)


def bin_tables(extent, bins, length):
    which = jnp.arange(bins, dtype=jnp.int32)[None, :, None]
    place = jnp.arange(length, dtype=jnp.int32)[None, None, :]
    edge = extent[:, None, None]
    lower = which * edge // bins
    upper = ((which + 1) * edge + bins - 1) // bins
    member = ((place >= lower) & (place < upper)).astype(jnp.float32)
    target = jnp.minimum(place * bins // edge, bins - 1)
    chosen = (target == which).astype(jnp.float32)
    return (member, chosen)


def spread_bins(merged, branch, tables, images):
    joined = [merged]
    for group, bins in enumerate(BIN_COUNTS):
        rows_in, cols_in, rows_pick, cols_pick, cell_count = tables[group]
        piece = branch[:, BIN_STARTS[group] : BIN_STARTS[group] + bins * bins].reshape(
            images, bins, bins, -1
        )
        joined.append(
            jnp.einsum(
                "ikh,ilw,iklc->ihwc",
                rows_pick.astype(jnp.bfloat16),
                cols_pick.astype(jnp.bfloat16),
                piece,
                preferred_element_type=jnp.float32,
            ).astype(jnp.bfloat16)
        )
    return jnp.concatenate(joined, axis=-1)


def pick_bins(d_joined, width, tables, images):
    branch_width = (d_joined.shape[-1] - width) // 4
    d_up = []
    for group, bins in enumerate(BIN_COUNTS):
        rows_in, cols_in, rows_pick, cols_pick, cell_count = tables[group]
        piece = d_joined[..., width + group * branch_width : width + (group + 1) * branch_width]
        d_up.append(
            jnp.einsum("ikh,ilw,ihwc->iklc", rows_pick, cols_pick, piece).reshape(
                images, bins * bins, -1
            )
        )
    return (d_joined[..., :width], jnp.concatenate(d_up, axis=1))


def gather_channels(field):
    return lax.all_gather(field, "tensor", axis=3, tiled=True)


def scatter_channels(field):
    return lax.psum_scatter(
        field.astype(jnp.bfloat16), "tensor", scatter_dimension=3, tiled=True
    ).astype(jnp.float32)


def local(features, labels, valid, sizes, params, first_moment, squared_mean, average):
    splits = lax.axis_size("tensor")
    owners = lax.axis_size("batch")
    images = features.shape[0]
    gathered = lax.all_gather(params.astype(jnp.bfloat16), "batch", axis=0, tiled=True)
    (
        w_reduce,
        w_short,
        w_middle,
        w_expand,
        w_branch,
        w_unite,
        w_classes,
        w_aux,
        w_aux_classes,
        gains,
    ) = unflatten(gathered, splits)
    norms = [(piece[0], piece[1]) for piece in gain_pieces(gains.astype(jnp.float32), splits)]
    rows_at = jnp.arange(MAP, dtype=jnp.int32)
    inside = (rows_at[None, :, None] < sizes[:, 0][:, None, None]) & (
        rows_at[None, None, :] < sizes[:, 1][:, None, None]
    )
    inside = inside.astype(jnp.float32)[..., None]
    counted = inside * valid.astype(jnp.float32)[..., None]
    labels_hot = (labels[..., None] == jnp.arange(NCLS, dtype=jnp.int32)).astype(jnp.float32)
    class_local = channel_sums(labels_hot * counted)
    whole = lax.all_gather(features, "tensor", axis=3, tiled=True)
    pre_reduce = jnp.dot(whole, w_reduce, preferred_element_type=jnp.float32)
    pre_short = jnp.dot(whole, w_short, preferred_element_type=jnp.float32)
    pre_aux = conv_forward(whole, w_aux, 1)
    leading_part, label_tally = masked_norm_apply(
        [
            (pre_reduce, inside, norms[0]),
            (pre_short, inside, norms[1]),
            (pre_aux, inside, norms[9]),
        ],
        [class_local],
    )
    class_pixel_counts = label_tally[0]
    hidden_one = jax.nn.silu(leading_part[0][0]).astype(jnp.bfloat16)
    aux_act = jax.nn.silu(leading_part[2][0]).astype(jnp.bfloat16)
    hidden_full = gather_channels(hidden_one)
    pre_middle = conv_forward(hidden_full, w_middle, 4)
    second, unused = masked_norm_apply([(pre_middle, inside, norms[2])], [])
    hidden_two = jax.nn.silu(second[0][0]).astype(jnp.bfloat16)
    hidden_two_full = gather_channels(hidden_two)
    pre_expand = jnp.dot(hidden_two_full, w_expand, preferred_element_type=jnp.float32)
    third, unused = masked_norm_apply([(pre_expand, inside, norms[3])], [])
    summed = third[0][0] + leading_part[1][0]
    merged = jax.nn.silu(summed).astype(jnp.bfloat16)
    tables = []
    pooled_list = []
    partial_list = []
    for group, bins in enumerate(BIN_COUNTS):
        rows_in, rows_pick = bin_tables(sizes[:, 0], bins, MAP)
        cols_in, cols_pick = bin_tables(sizes[:, 1], bins, MAP)
        cell_count = (
            jnp.sum(rows_in, axis=2)[:, :, None, None] * jnp.sum(cols_in, axis=2)[:, None, :, None]
        )
        tables.append((rows_in, cols_in, rows_pick, cols_pick, cell_count))
        pooled = (
            jnp.einsum(
                "ikh,ilw,ihwc->iklc",
                rows_in.astype(jnp.bfloat16),
                cols_in.astype(jnp.bfloat16),
                merged,
                preferred_element_type=jnp.float32,
            )
            / cell_count
        )
        pooled = pooled.astype(jnp.bfloat16).reshape(images, bins * bins, -1)
        pooled_list.append(pooled)
        partial_list.append(
            jnp.einsum("ipc,cd->ipd", pooled, w_branch[group], preferred_element_type=jnp.float32)
        )
    branch_pre = lax.psum_scatter(
        jnp.concatenate(partial_list, axis=1).astype(jnp.bfloat16),
        "tensor",
        scatter_dimension=2,
        tiled=True,
    ).astype(jnp.float32)
    branch_items = []
    for group, bins in enumerate(BIN_COUNTS):
        piece = branch_pre[:, BIN_STARTS[group] : BIN_STARTS[group] + bins * bins]
        branch_items.append(
            (piece, jnp.ones(piece.shape[:-1] + (1,), jnp.float32), norms[4 + group])
        )
    fourth, unused = masked_norm_apply(branch_items, [])
    branch_act = jnp.concatenate([jax.nn.silu(kept[0]) for kept in fourth], axis=1).astype(
        jnp.bfloat16
    )
    merged_full, branch_full = (
        lax.all_gather(merged, "tensor", axis=3, tiled=True),
        lax.all_gather(branch_act, "tensor", axis=2, tiled=True),
    )
    joined = spread_bins(merged_full, branch_full, tables, images)
    pre_unite = conv_forward(joined, w_unite, 1)
    fifth, unused = masked_norm_apply([(pre_unite, inside, norms[8])], [])
    united = jax.nn.silu(fifth[0][0]).astype(jnp.bfloat16)
    logit_main, logit_aux = (
        lax.psum_scatter(
            jnp.dot(united, w_classes, preferred_element_type=jnp.float32).astype(jnp.bfloat16),
            "tensor",
            scatter_dimension=1,
            tiled=True,
        ).astype(jnp.float32),
        lax.psum_scatter(
            jnp.dot(aux_act, w_aux_classes, preferred_element_type=jnp.float32).astype(
                jnp.bfloat16
            ),
            "tensor",
            scatter_dimension=1,
            tiled=True,
        ).astype(jnp.float32),
    )
    total_valid = jnp.sum(class_pixel_counts)
    class_weight = total_valid / (NCLS * class_pixel_counts + total_valid)
    loss_weight = jnp.sum(class_pixel_counts * class_weight)
    cell_weight = jnp.sum(labels_hot * class_weight, axis=-1, keepdims=True) * counted
    band_rows = labels.shape[1] // splits
    band_start = lax.axis_index("tensor") * band_rows
    hot_band = lax.dynamic_slice_in_dim(labels_hot, band_start, band_rows, 1)
    weight_band = lax.dynamic_slice_in_dim(cell_weight, band_start, band_rows, 1)
    log_main = jax.nn.log_softmax(logit_main, axis=-1)
    log_aux = jax.nn.log_softmax(logit_aux, axis=-1)
    loss_cells = -jnp.sum(hot_band * (log_main + 0.4 * log_aux), axis=-1, keepdims=True)
    loss_local = jnp.sum(weight_band * loss_cells)
    band_main = (weight_band * (jnp.exp(log_main) - hot_band) / loss_weight).astype(jnp.bfloat16)
    band_aux = (0.4 * weight_band * (jnp.exp(log_aux) - hot_band) / loss_weight).astype(
        jnp.bfloat16
    )
    grad_main, grad_aux = (
        lax.all_gather(band_main, "tensor", axis=1, tiled=True),
        lax.all_gather(band_aux, "tensor", axis=1, tiled=True),
    )
    reduced = {}

    def settle(index, value):
        reduced[index] = value

    settle(6, jnp.einsum("ihwc,ihwk->ck", united, grad_main, preferred_element_type=jnp.float32))
    settle(8, jnp.einsum("ihwc,ihwk->ck", aux_act, grad_aux, preferred_element_type=jnp.float32))
    d_united = jnp.dot(grad_main, w_classes.T, preferred_element_type=jnp.float32) * silu_slope(
        fifth[0][0]
    )
    d_aux = jnp.dot(grad_aux, w_aux_classes.T, preferred_element_type=jnp.float32) * silu_slope(
        leading_part[2][0]
    )
    back_one, sums_one, totals_one = norm_backward([(d_united, fifth[0]), (d_aux, leading_part[2])])
    unite_shift_grad = totals_one[0]
    d_unite_pre = back_one[0].astype(jnp.bfloat16)
    d_aux_pre = back_one[1].astype(jnp.bfloat16)
    settle(5, conv_kernel_back(joined, d_unite_pre, 1))
    d_merged, d_branch = pick_bins(conv_input_back(d_unite_pre, w_unite, 1), C_OUT, tables, images)
    d_merged, d_branch = (
        lax.psum_scatter(
            d_merged.astype(jnp.bfloat16), "tensor", scatter_dimension=3, tiled=True
        ).astype(jnp.float32),
        lax.psum_scatter(
            d_branch.astype(jnp.bfloat16), "tensor", scatter_dimension=2, tiled=True
        ).astype(jnp.float32),
    )
    settle(7, conv_kernel_back(whole, d_aux_pre, 1))
    branch_back = []
    for group, bins in enumerate(BIN_COUNTS):
        piece = d_branch[:, BIN_STARTS[group] : BIN_STARTS[group] + bins * bins]
        branch_back.append((piece * silu_slope(fourth[group][0]), fourth[group]))
    back_two, sums_two, unused = norm_backward(branch_back)
    d_branch_pre = jnp.concatenate(back_two, axis=1).astype(jnp.bfloat16)
    d_branch_full = lax.all_gather(d_branch_pre, "tensor", axis=2, tiled=True)
    branch_grads = []
    for group, bins in enumerate(BIN_COUNTS):
        rows_in, cols_in, rows_pick, cols_pick, cell_count = tables[group]
        piece = d_branch_full[:, BIN_STARTS[group] : BIN_STARTS[group] + bins * bins]
        branch_grads.append(
            jnp.einsum("ipc,ipd->cd", pooled_list[group], piece, preferred_element_type=jnp.float32)
        )
        d_pooled = jnp.dot(piece, w_branch[group].T, preferred_element_type=jnp.float32).reshape(
            images, bins, bins, -1
        )
        d_merged = d_merged + jnp.einsum(
            "ikh,ilw,iklc->ihwc", rows_in, cols_in, d_pooled / cell_count
        )
    settle(4, jnp.stack(branch_grads))
    d_summed = d_merged * silu_slope(summed)
    back_three, sums_three, unused = norm_backward(
        [(d_summed, third[0]), (d_summed, leading_part[1])]
    )
    d_expand_pre = back_three[0].astype(jnp.bfloat16)
    d_short_pre = back_three[1].astype(jnp.bfloat16)
    settle(
        3,
        jnp.einsum(
            "ihwc,ihwd->cd", hidden_two_full, d_expand_pre, preferred_element_type=jnp.float32
        ),
    )
    settle(1, jnp.einsum("ihwc,ihwd->cd", whole, d_short_pre, preferred_element_type=jnp.float32))
    d_two = scatter_channels(jnp.dot(d_expand_pre, w_expand.T, preferred_element_type=jnp.float32))
    back_four, sums_four, unused = norm_backward([(d_two * silu_slope(second[0][0]), second[0])])
    d_middle_pre = back_four[0].astype(jnp.bfloat16)
    settle(2, conv_kernel_back(hidden_full, d_middle_pre, 4))
    d_one = scatter_channels(conv_input_back(d_middle_pre, w_middle, 4))
    back_five, sums_five, unused = norm_backward(
        [(d_one * silu_slope(leading_part[0][0]), leading_part[0])]
    )
    settle(
        0,
        jnp.einsum(
            "ihwc,ihwd->cd",
            whole,
            back_five[0].astype(jnp.bfloat16),
            preferred_element_type=jnp.float32,
        ),
    )
    beta_grads = (
        [sums_five[0], sums_three[2], sums_four[0], sums_three[0]]
        + [sums_two[2 * g] for g in range(4)]
        + [sums_one[0], sums_one[2]]
    )
    gamma_grads = (
        [sums_five[1], sums_three[3], sums_four[1], sums_three[1]]
        + [sums_two[2 * g + 1] for g in range(4)]
        + [sums_one[1], sums_one[3]]
    )
    settle(9, jnp.stack([jnp.concatenate(gamma_grads), jnp.concatenate(beta_grads)]))
    ordered = [reduced[index] for index in range(10)]
    grad_share = lax.psum_scatter(
        jnp.concatenate([part.reshape(owners, -1) for part in ordered], axis=1),
        "batch",
        scatter_dimension=0,
        tiled=True,
    )
    square_all, loss_sum = lax.psum(
        (jnp.sum(grad_share * grad_share), loss_local), ("batch", "tensor")
    )
    grad_norm = jnp.sqrt(square_all)
    clipped = grad_share * jnp.minimum(1.0, 0.05 / (grad_norm + 1e-06))
    new_first = 0.5 * first_moment + 0.5 * clipped
    new_second = 0.5 * squared_mean + 0.5 * clipped * clipped
    keep = 1.0 - 0.5**STEP
    new_params = params - 0.01 * (
        new_first / keep / (jnp.sqrt(new_second / keep) + 1e-08) + 0.01 * params
    )
    new_average = 0.999 * average + 0.001 * new_params
    return (
        new_params,
        new_first,
        new_second,
        new_average,
        new_params.astype(jnp.bfloat16),
        grad_norm,
        loss_sum,
        loss_weight,
        unite_shift_grad,
    )


CELLS = MAP * MAP
EDGE = 104
BATCH = "batch"
TENSOR = "tensor"
GROUP_ROWS = ((0, 1), (1, 5), (5, 14), (14, 50))
BINS = 64
BF = jnp.bfloat16
F32 = jnp.float32
MESH = pl.DeviceIdType.MESH
HALF = 4
OWNERS = 8
SPLITS = 4
MERGED = 4
SLOTS = 5


def scratch_plan():
    plan = dict(
        w_r=((1024, 128), BF),
        w_s=((1024, 512), BF),
        w_m=((4608, 128), BF),
        w_e=((512, 512), BF),
        w_b=((2048, 512), BF),
        w_u=((18432, 128), BF),
        w_own=((4608, 128), BF),
        w_a=((4608, 128), BF),
        w_pair=((1024, 640), BF),
        w_c=((128, 256), BF),
        w_ac=((64, 256), F32),
        gain_in=((OWNERS, 8, 128), F32),
        gain_rows=((40, 128), F32),
        out_a=((576, 128), F32),
        out_c=((16, 256), F32),
        out_ac=((8, 256), F32),
        whole=((SPLITS, CELLS, 256), BF),
        ins=((CELLS, 128), F32),
        col=((CELLS, 128), F32),
        lab=((CELLS, 128), F32),
        table=((BINS, CELLS), F32),
        pool=((BINS, CELLS), BF),
        pick=((BINS, CELLS), BF),
        cells_in=((BINS, 128), F32),
        pad=((9, CELLS + 2 * EDGE, 128), F32),
        grad_pad=((CELLS + 2 * EDGE, 128), F32),
        pre_r=((CELLS, 128), F32),
        pre_s=((CELLS, 512), F32),
        pre_a=((CELLS, 128), F32),
        pre_m=((CELLS, 128), F32),
        pre_e=((CELLS, 512), F32),
        pre_u=((CELLS, 128), F32),
        act_a=((CELLS, 128), BF),
        h1=((SPLITS, CELLS, 128), BF),
        h2=((SPLITS, CELLS, 128), BF),
        joined=((SPLITS, CELLS, 512), BF),
        joined_t=((SPLITS, 512, CELLS), BF),
        pooled=((BINS, 512), BF),
        pool_half=((2, BINS, 256), BF),
        pool_all=((OWNERS, BINS, 256), BF),
        d_bp_all=((OWNERS, SPLITS, BINS, 128), BF),
        part_b=((SPLITS, BINS, 128), BF),
        recv_b=((SPLITS, BINS, 128), BF),
        all_b=((OWNERS, BINS, 128), BF),
        act_b=((SPLITS, OWNERS * BINS, 128), BF),
        pick_t=((CELLS, 128), BF),
        z_cat=((9, 128, 128), BF),
        act_t=((512, OWNERS * BINS), BF),
        zsum=((2, OWNERS * BINS, 128), F32),
        z_send=((OWNERS, 2, BINS, 128), BF),
        z_recv=((OWNERS, 2, BINS, 128), BF),
        united=((CELLS, 128), BF),
        logit_send=((CELLS, 512), BF),
        logit_recv=((SPLITS, 144, 512), BF),
        slope_in=((SPLITS, 144, 512), BF),
        d_f=((CELLS, 128), F32),
        d_f2=((CELLS, 128), F32),
        cat_u=((CELLS, 1152), BF),
        cat_a=((CELLS, 640), BF),
        dz_send=((9, BINS, 128), BF),
        dz_recv=((OWNERS, 2, BINS, 128), BF),
        d_act_send=((SPLITS, OWNERS * BINS, 128), BF),
        d_act_recv=((SPLITS, OWNERS * BINS, 128), BF),
        d_img_send=((OWNERS, BINS, 128), BF),
        d_img_recv=((OWNERS, BINS, 128), BF),
        d_bp=((SPLITS, BINS, 128), BF),
        dm_near=((2, CELLS, 512), BF),
        dm_far=((CELLS, 512), BF),
        d_sum=((CELLS, 512), F32),
        d_e=((CELLS, 512), BF),
        d_s=((CELLS, 512), BF),
        dh_send=((SPLITS, CELLS, 128), BF),
        dh_recv=((2, SPLITS, CELLS, 128), BF),
        d_low=((CELLS, 128), BF),
        end_t=((SPLITS, 8, 128), F32),
    )
    for name, rows in SYNCS.items():
        plan["sync_" + name] = ((OWNERS, rows, 128), F32)
    for name, (rows, lanes, kind) in PARTS.items():
        plan["first_" + name] = ((HALF, rows, lanes), kind)
        plan["second_" + name] = ((HALF - 1, rows, lanes), kind)
    plan["first_u"] = ((HALF, SLOTS, 512, 128), BF)
    plan["second_u"] = ((HALF - 1, SLOTS, 512, 128), BF)
    return plan


SYNCS = dict(one=8, two=8, three=16, five=8, aux=8, b1=8, b2=8, b3=8, b4=16, b5=8, b6=8, end=8)
PARTS = dict(
    r=(128, 128, BF),
    s=(128, 512, BF),
    m=(576, 128, BF),
    e=(64, 512, BF),
    a=(576, 128, BF),
    c=(16, 256, BF),
    ac=(8, 256, F32),
)
SEMAPHORES = 1100
LOADS = (0, 128, 640, 1216, 1472, 2496, 7104, 7712)
LOAD_ORDER = (0, 2, 3, 1, 4, 6, 5)


class Refs:
    pass


def fold(value):
    return value.reshape(-1, 8, value.shape[-1]).sum(0)


def total(value):
    return jnp.sum(value, axis=0, keepdims=True)


def wide(value, times):
    return jnp.concatenate([value] * times, axis=1)


def dot(left, right):
    return jnp.dot(left, right, preferred_element_type=F32)


def dot_nt(left, right):
    return lax.dot_general(left, right, (((1,), (1,)), ((), ())), preferred_element_type=F32)


def dot_tn(left, right):
    return lax.dot_general(left, right, (((0,), (0,)), ((), ())), preferred_element_type=F32)


def loop(count, body):
    def step(k, carry):
        body(k)
        return carry

    lax.fori_loop(0, count, step, 0)


def rows_at(k, block):
    return pl.ds(pl.multiple_of(k * block, block), block)


def step_kernel(names, *refs):
    (
        sizes, lab_in, feat, flat, o_flat, o_shift, o_misc,
    ) = refs[:7]
    v = Refs()
    for name, ref in zip(names, refs[7:]):
        setattr(v, name, ref)
    sems = refs[-1]
    o_u = o_flat.at[2496:7104, :]
    me = lax.axis_index(BATCH)
    t = lax.axis_index(TENSOR)
    partner = me + 1 - 2 * lax.rem(me, 2)
    t_core = t + 1 - 2 * lax.rem(t, 2)
    t_x = lax.rem(t + 2, SPLITS)
    t_diag = lax.rem(t_core + 2, SPLITS)
    taken = [0]

    def take(count):
        start = taken[0]
        taken[0] = start + count
        assert taken[0] <= SEMAPHORES
        return start

    def far_peer(base, step):
        return lax.rem(base + 2 * step, OWNERS)

    def remote(src, dst, send, recv, device):
        return pltpu.make_async_remote_copy(
            src_ref=src,
            dst_ref=dst,
            send_sem=sems.at[send],
            recv_sem=sems.at[recv],
            device_id=device,
            device_id_type=MESH,
        )

    late = []

    load_at = take(len(LOADS))

    def load(index):
        at = pl.ds(LOADS[index], LOADS[index + 1] - LOADS[index])
        return pltpu.make_async_copy(flat.at[at, :], o_flat.at[at, :], sems.at[load_at + index])

    for index in LOAD_ORDER:
        load(index).start()
    v.pool_all[...] = jnp.zeros((OWNERS, BINS, 256), BF)
    v.d_bp_all[...] = jnp.zeros((OWNERS, SPLITS, BINS, 128), BF)
    barrier = pltpu.get_barrier_semaphore()
    for k in range(1, OWNERS):
        pl.semaphore_signal(
            barrier, inc=1, device_id={BATCH: lax.rem(me + k, OWNERS)}, device_id_type=MESH
        )
    for k in range(1, SPLITS):
        pl.semaphore_signal(
            barrier, inc=1, device_id={TENSOR: lax.rem(t + k, SPLITS)}, device_id_type=MESH
        )
    pl.semaphore_wait(barrier, OWNERS + SPLITS - 2)

    class Gather:
        def __init__(self, full, rows, skip=0, step=None, piece=None):
            self.full, self.rows, self.piece = full, rows, piece
            self.skip, self.part = skip, step or rows
            self.near_s, self.far_s, self.pass_s = take(1), take(HALF), take(HALF)
            self.recv, self.keep = take(OWNERS), take(1)

        def at(self, owner):
            if self.rows is None:
                return self.full.at[owner]
            start = pl.multiple_of(owner * self.rows + self.skip, self.part)
            return self.full.at[pl.ds(start, self.part), :]

        def source(self):
            return self.at(me) if self.piece is None else self.piece

        def local(self):
            return pltpu.make_async_copy(self.piece, self.at(me), sems.at[self.keep])

        def near(self):
            return remote(
                self.source(), self.at(me), self.near_s, self.recv + me, {BATCH: partner}
            )

        def far(self, step):
            return remote(
                self.source(),
                self.at(me),
                self.far_s + step,
                self.recv + me,
                {BATCH: far_peer(me, step)},
            )

        def passed(self, step, base):
            source = far_peer(base, step)
            return remote(
                self.at(source),
                self.at(source),
                self.pass_s + step,
                self.recv + source,
                {BATCH: partner},
            )

        def start_far(self):
            if self.piece is not None:
                self.local().start()
            for step in range(1, HALF):
                self.far(step).start()

        def start_near(self):
            self.near().start()

        def forward(self):
            for step in range(1, HALF):
                self.passed(step, me).wait_recv()
                self.passed(step, me).start()

        def finish(self):
            for step in range(HALF):
                self.passed(step, partner).wait_recv()
            if self.piece is not None:
                self.local().wait()
            self.near().wait_send()
            for step in range(1, HALF):
                self.far(step).wait_send()

        def drain(self):
            for step in range(1, HALF):
                self.passed(step, me).wait_send()

    g_gain = Gather(v.gain_in, None, piece=flat.at[7704:7712, :])
    g_r = Gather(v.w_r, 128)
    g_s = Gather(v.w_s, 128)
    g_a = Gather(v.w_a, 576)
    g_m = Gather(v.w_m, 576)
    g_e = Gather(v.w_e, 64)
    g_b0 = Gather(v.w_b, 256, 0, 128)
    g_b1 = Gather(v.w_b, 256, 128, 128)
    g_c = Gather(v.w_c, 16)
    g_ac = Gather(v.w_ac, 8)

    def block_of(owner, slot):
        return 8 if slot == SLOTS - 1 else lax.rem(slot - owner + 8, 8)

    def merged_rows(owner, slot):
        block = owner * 9 + block_of(owner, slot)
        index = lax.div(block, 8) * MERGED + lax.rem(block, 8)
        return pl.ds(pl.multiple_of(index * 512, 512), 512)

    def has(owner, slot, body):
        if slot == SLOTS - 1:
            pl.when(owner < MERGED)(body)
        else:
            body()

    class GatherUnite:
        def __init__(self):
            self.near_s, self.far_s, self.pass_s = (
                take(SLOTS),
                take(SLOTS * HALF),
                take(SLOTS * HALF),
            )
            self.recv, self.keep = take(SLOTS * OWNERS), take(SLOTS)

        def source(self, slot):
            return v.w_own.at[rows_at(block_of(me, slot), 512), :]

        def full(self, owner, slot):
            return v.w_u.at[merged_rows(owner, slot), :]

        def local(self, slot):
            return pltpu.make_async_copy(
                self.source(slot), self.full(me, slot), sems.at[self.keep + slot]
            )

        def near(self, slot):
            return remote(
                self.source(slot),
                self.full(me, slot),
                self.near_s + slot,
                self.recv + me * SLOTS + slot,
                {BATCH: partner},
            )

        def far(self, step, slot):
            return remote(
                self.source(slot),
                self.full(me, slot),
                self.far_s + step * SLOTS + slot,
                self.recv + me * SLOTS + slot,
                {BATCH: far_peer(me, step)},
            )

        def passed(self, step, slot, base):
            source = far_peer(base, step)
            return remote(
                self.full(source, slot),
                self.full(source, slot),
                self.pass_s + step * SLOTS + slot,
                self.recv + source * SLOTS + slot,
                {BATCH: partner},
            )

        def start_far(self, slot):
            def go():
                self.local(slot).start()
                for step in range(1, HALF):
                    self.far(step, slot).start()

            has(me, slot, go)

        def start_near(self, slot):
            has(me, slot, lambda: self.near(slot).start())

        def forward(self, slot):
            for step in range(1, HALF):

                def go(step=step):
                    self.passed(step, slot, me).wait_recv()
                    self.passed(step, slot, me).start()

                has(far_peer(me, step), slot, go)

        def finish(self):
            for slot in range(SLOTS):
                for step in range(HALF):
                    has(
                        far_peer(partner, step),
                        slot,
                        lambda step=step, slot=slot: self.passed(step, slot, partner).wait_recv(),
                    )

                def end(slot=slot):
                    self.local(slot).wait()
                    self.near(slot).wait_send()
                    for step in range(1, HALF):
                        self.far(step, slot).wait_send()

                has(me, slot, end)

        def drain(self):
            for slot in range(SLOTS):
                for step in range(1, HALF):
                    has(
                        far_peer(me, step),
                        slot,
                        lambda step=step, slot=slot: self.passed(step, slot, me).wait_send(),
                    )

    g_u = GatherUnite()

    class Sync:
        def __init__(self, buf):
            self.buf = buf
            self.send, self.recv = take(OWNERS), take(OWNERS)

        def copy(self, k, slot):
            return remote(
                self.buf.at[slot],
                self.buf.at[slot],
                self.send + k,
                self.recv + slot,
                {BATCH: lax.rem(me + k, OWNERS)},
            )

        def start(self, rows):
            for index, row in enumerate(rows):
                self.buf[me, index : index + 1, :] = row
            for index in range(len(rows), self.buf.shape[1]):
                self.buf[me, index : index + 1, :] = jnp.zeros((1, 128), F32)
            for k in range(1, OWNERS):
                self.copy(k, me).start()

        def wait(self):
            for k in range(1, OWNERS):
                self.copy(k, lax.rem(me + k, OWNERS)).wait_recv()
            for k in range(1, OWNERS):
                self.copy(k, me).wait_send()
            value = self.buf[0]
            for slot in range(1, OWNERS):
                value = value + self.buf[slot]
            return value

    class ToGroup:
        def __init__(self, part, into):
            self.part, self.into = part, into
            self.send, self.recv = take(OWNERS), take(OWNERS)

        def each(self, k, owner, slot, act):
            for rows, fits_ in ((16, owner < 6), (BINS, owner >= 6)):

                def go(rows=rows):
                    act(
                        remote(
                            self.part(owner, rows),
                            self.into(slot, rows),
                            self.send + k,
                            self.recv + slot,
                            {BATCH: lax.rem(me + k, OWNERS)},
                        )
                    )

                pl.when(fits_)(go)

        def start(self):
            for k in range(1, OWNERS):
                self.each(k, lax.rem(me + k, OWNERS), me, lambda c: c.start())

        def wait(self):
            for k in range(1, OWNERS):
                self.each(k, me, lax.rem(me + k, OWNERS), lambda c: c.wait_recv())
            for k in range(1, OWNERS):
                self.each(k, lax.rem(me + k, OWNERS), me, lambda c: c.wait_send())

    class Spread:

        def __init__(self, buf, lanes_=None):
            self.buf, self.lanes = buf, lanes_
            self.send, self.recv = take(SPLITS), take(SPLITS)

        def view(self, slot):
            return self.buf.at[slot] if self.lanes is None else self.buf.at[slot, :, self.lanes]

        def copy(self, k, slot):
            return remote(
                self.view(slot),
                self.view(slot),
                self.send + k,
                self.recv + slot,
                {TENSOR: lax.rem(t + k, SPLITS)},
            )

        def start(self):
            for k in range(1, SPLITS):
                self.copy(k, t).start()

        def wait(self):
            for k in range(1, SPLITS):
                self.copy(k, lax.rem(t + k, SPLITS)).wait_recv()
            for k in range(1, SPLITS):
                self.copy(k, t).wait_send()

    class Exchange:

        def __init__(self, axis, count, part, into):
            self.axis, self.count, self.part, self.into = axis, count, part, into
            self.mine = me if axis == BATCH else t
            self.send, self.recv = take(count), take(count)

        def copy(self, k, slot):
            other = lax.rem(self.mine + k, self.count)
            return remote(
                self.part(other),
                self.into(slot),
                self.send + k,
                self.recv + slot,
                {self.axis: other},
            )

        def start(self):
            for k in range(1, self.count):
                self.copy(k, self.mine).start()

        def wait(self):
            for k in range(1, self.count):
                self.copy(k, lax.rem(self.mine + k, self.count)).wait_recv()
            for k in range(1, self.count):
                self.copy(k, self.mine).wait_send()

    feat_keep = take(1)
    feat_local = pltpu.make_async_copy(feat, v.whole.at[t], sems.at[feat_keep])
    feat_s, feat_r = take(3), take(SPLITS)

    def feat_copy(k, slot, device):
        source = feat if k < 2 else v.whole.at[slot]
        return remote(source, v.whole.at[slot], feat_s + k, feat_r + slot, {TENSOR: device})

    def wide_rows(into, rows, low):
        for k in range(4):
            value = o_flat[pl.ds(low + k, rows, stride=4), :]
            into[rows_at(me, rows), k * 128 : k * 128 + 128] = value.astype(BF)

    load(0).wait()
    v.w_r[rows_at(me, 128), :] = o_flat[0:128, :].astype(BF)
    for item in (g_gain, g_r):
        item.start_far()
        item.start_near()
    feat_local.start()
    feat_copy(0, t, t_x).start()
    feat_copy(1, t, t_core).start()
    load(2).wait()
    v.w_m[rows_at(me, 576), :] = o_flat[640:1216, :].astype(BF)
    load(3).wait()
    wide_rows(v.w_e, 64, 1216)
    for item in (g_m, g_e):
        item.start_far()
        item.start_near()
    lane = lax.broadcasted_iota(jnp.int32, (1, 128), 1)

    def roll(value, shift):
        return pltpu.roll(value, shift % 128, 1) if shift % 128 else value

    high, across = sizes[0, 0], sizes[0, 1]
    place = lax.broadcasted_iota(jnp.int32, (CELLS, 128), 0).astype(F32)
    row_of = jnp.floor((place + 0.5) / MAP)
    col_of = place - MAP * row_of
    within = (row_of < high.astype(F32)) & (col_of < across.astype(F32))
    v.ins[...] = jnp.where(within, 1.0, 0.0)
    v.col[...] = col_of
    v.lab[...] = jnp.where(within, lab_in[...], -1.0)
    v.table[...] = jnp.zeros((BINS, CELLS), F32)
    lane_place = lax.broadcasted_iota(jnp.int32, (1, CELLS), 1).astype(F32)
    lane_row = jnp.floor((lane_place + 0.5) / MAP)
    lane_col = lane_place - MAP * lane_row

    def ranges(extent, bins, where):
        inside, chosen, counts = [], [], []
        for k in range(bins):
            low = lax.div(k * extent, bins)
            top = lax.div((k + 1) * extent + (bins - 1), bins)
            member = (where >= low.astype(F32)) & (where < top.astype(F32))
            inside.append(jnp.where(member, 1.0, 0.0))
            picked = where * bins >= (k * extent).astype(F32)
            if k < bins - 1:
                picked = picked & (where * bins < ((k + 1) * extent).astype(F32))
            chosen.append(jnp.where(picked, 1.0, 0.0))
            counts.append(top - low)
        return inside, chosen, counts

    picks = []
    v.cells_in[...] = jnp.ones((BINS, 128), F32)
    for group, bins in enumerate(BIN_COUNTS):
        r_in, r_pick, r_count = ranges(high, bins, lane_row)
        c_in, c_pick, c_count = ranges(across, bins, lane_col)
        for a in range(bins):
            for b in range(bins):
                spot = BIN_STARTS[group] + a * bins + b
                v.table[spot : spot + 1, :] = r_in[a] * c_in[b]
                v.cells_in[spot : spot + 1, :] = jnp.full(
                    (1, 128), (r_count[a] * c_count[b]).astype(F32)
                )
                picks.append((spot, r_pick[a] * c_pick[b]))
    v.pool[...] = v.table[...].astype(BF)
    for spot, value in picks:
        v.table[spot : spot + 1, :] = value
    v.pick[...] = v.table[...].astype(BF)
    v.pick_t[...] = jnp.concatenate([v.pick[...], v.pick[...]], axis=0).T
    zeros_edge = jnp.zeros((EDGE, 128), F32)
    for tap in range(9):
        v.pad[tap, 0:EDGE, :] = zeros_edge
        v.pad[tap, EDGE + CELLS :, :] = zeros_edge
    v.grad_pad[0:EDGE, :] = zeros_edge
    v.grad_pad[EDGE + CELLS :, :] = zeros_edge
    lanes = lax.broadcasted_iota(jnp.int32, (1, 256), 1).astype(F32)
    counts = jnp.zeros((8, 256), F32)
    for k in range(0, CELLS, 96):
        counts = counts + fold(
            jnp.where(wide(v.lab[k : k + 96, :], 2) == lanes, 1.0, 0.0)
        )
    class_local = total(counts)
    cells_local = jnp.full((1, 128), (high * across).astype(F32))
    left_half = lax.broadcasted_iota(jnp.int32, (64, 128), 1) < 64

    for item in (g_gain, g_r):
        item.forward()
    feat_copy(0, t_x, t_x).wait_recv()
    feat_copy(2, t_x, t_core).start()
    load(1).wait()
    wide_rows(v.w_s, 128, 128)
    load(4).wait()
    wide_rows(v.w_b, 256, 1472)
    load(6).wait()
    before = pltpu.roll(o_flat[7122:7698, :], 32, 1)
    after = pltpu.roll(o_flat[7123:7699, :], 32, 1)
    v.w_a[rows_at(me, 576), :] = jnp.where(lane < 32, before, after).astype(BF)

    def class_rows(count, base, into):
        for row in range(count):
            first, shift = divmod(base + NCLS * row, 128)
            three = [
                roll(o_flat[7104 + first + k : 7105 + first + k, :], 128 - shift) for k in range(3)
            ]
            into[row : row + 1, :128] = jnp.where(lane < 128 - shift, three[0], three[1])
            high_half = jnp.where(lane < 128 - shift, three[1], three[2])
            into[row : row + 1, 128:] = jnp.where(lane < NCLS - 128, high_half, 0.0)

    class_rows(16, 0, v.out_c)
    class_rows(8, 76128, v.out_ac)
    v.w_c[rows_at(me, 16), :] = v.out_c[...].astype(BF)
    v.w_ac[rows_at(me, 8), :] = v.out_ac[...].astype(BF).astype(F32)
    load(5).wait()

    def own_rows(j):
        at = pl.ds(pl.multiple_of(2496 + 512 * j, 64), 512)
        v.w_own[rows_at(j, 512), :] = o_flat[at, :].astype(BF)

    loop(9, own_rows)
    for item in (g_gain, g_r):
        item.finish()
    feat_local.wait()
    feat_copy(1, t_core, t_core).wait_recv()
    feat_copy(2, t_diag, t_core).wait_recv()
    feat_copy(0, t, t_x).wait_send()
    feat_copy(1, t, t_core).wait_send()
    feat_copy(2, t_x, t_core).wait_send()
    gain_of = [None] * 33
    for owner in range(OWNERS):
        start = 496 * (owner % 4) - 16
        first, shift = start // 128, start % 128
        for k in range(4):
            value = v.gain_in[owner, 4 + k : 5 + k, :].astype(BF).astype(F32)
            if k == 0:
                value = jnp.where(lane < 16, 0.0, value)
            value = roll(value, shift)
            spot = 16 * (owner // 4) + first + k
            for where, part in (
                (spot, jnp.where(lane >= shift, value, 0.0)),
                (spot + 1, jnp.where(lane < shift, value, 0.0)),
            ):
                gain_of[where] = part if gain_of[where] is None else gain_of[where] + part

    def gamma(row, width=1):
        return jnp.concatenate([gain_of[row + k] for k in range(width)], axis=1)

    def beta(row, width=1):
        return gamma(16 + row, width)

    def whole_feat():
        return jnp.concatenate([v.whole[k] for k in range(SPLITS)], axis=1)

    v.pre_r[...] = dot(whole_feat(), v.w_r[...])
    def offset(tap, spacing):
        return ((tap // 3 - 1) * MAP + (tap % 3 - 1)) * spacing

    def col_mask(at, right):
        where = v.col[at, :] + float(right)
        return jnp.where((where >= 0.0) & (where < float(MAP)), 1.0, 0.0)

    BLOCK = 72

    def shift_sum(taps, spacing, at, slot_of):
        out = None
        for b in (-1, 0, 1):
            part = None
            for tap in taps:
                if tap % 3 - 1 != b:
                    continue
                start = EDGE + at + offset(tap, spacing)
                value = v.pad[slot_of(tap), start : start + BLOCK, :]
                part = value if part is None else part + value
            if part is None:
                continue
            if b:
                part = part * col_mask(slice(at, at + BLOCK), b * spacing)
            out = part if out is None else out + part
        return out

    def masked_sums(ref):
        width = ref.shape[1]

        def step(k, carry):
            at = rows_at(k, 96)
            value = ref[at, :]
            kept = value * (v.ins[at, :] if width == 128 else wide(v.ins[at, :], width // 128))
            return (carry[0] + fold(kept), carry[1] + fold(kept * value))

        zero = jnp.zeros((8, width), F32)
        sums = lax.fori_loop(0, 6, step, (zero, zero))
        return total(sums[0]), total(sums[1])

    def split_rows(value):
        return [value[:, k : k + 128] for k in range(0, value.shape[1], 128)]

    def join_rows(value, row, count):
        return jnp.concatenate([value[row + k : row + k + 1] for k in range(count)], axis=1)

    def moments(first, second, count):
        mean = first / count
        return mean, lax.rsqrt(second / count - mean * mean + 1e-05)

    sync = Sync(v.sync_one)
    r1, r2 = masked_sums(v.pre_r)
    sync.start([r1, r2, cells_local] + split_rows(class_local))
    g_m.forward()
    g_e.forward()
    g_s.start_far()
    sums = sync.wait()
    count = sums[2:3]
    count4 = wide(count, 4)
    norm_r = moments(sums[0:1], sums[1:2], count)
    class_count = join_rows(sums, 3, 2)

    def normed(ref, at, norm):
        return (ref[at, :] - norm[0]) * norm[1]

    spread_1 = Spread(v.h1)

    def make_h1(k):
        at = rows_at(k, 96)
        v.h1[t, at, :] = jax.nn.silu(gamma(0) * normed(v.pre_r, at, norm_r) + beta(0)).astype(BF)

    loop(6, make_h1)
    spread_1.start()
    g_s.start_near()
    g_b0.start_far()
    g_m.finish()
    spread_1.wait()

    def full_h(ref):
        return jnp.concatenate([ref[k] for k in range(SPLITS)], axis=1)

    def middle(tap):
        v.pad[tap, EDGE : EDGE + CELLS, :] = dot(full_h(v.h1), v.w_m[rows_at(tap, 512), :])

    loop(9, middle)
    for at in range(0, CELLS, BLOCK):
        v.pre_m[at : at + BLOCK, :] = shift_sum(range(9), 4, at, lambda tap: tap)
    sync = Sync(v.sync_two)
    sync.start(list(masked_sums(v.pre_m)))
    g_s.forward()
    g_b0.start_near()
    g_b1.start_far()
    sums = sync.wait()
    norm_m = moments(sums[0:1], sums[1:2], count)
    spread_2 = Spread(v.h2)

    def make_h2(k):
        at = rows_at(k, 96)
        v.h2[t, at, :] = jax.nn.silu(gamma(5) * normed(v.pre_m, at, norm_m) + beta(5)).astype(BF)

    loop(6, make_h2)
    spread_2.start()
    g_b0.forward()
    g_b1.start_near()
    g_u.start_far(0)
    g_e.finish()
    g_s.finish()
    for k in range(0, 512, 256):
        v.pre_s[:, k : k + 256] = dot(whole_feat(), v.w_s[:, k : k + 256])
    s1, s2 = masked_sums(v.pre_s)
    spread_2.wait()
    for k in range(0, 512, 256):
        v.pre_e[:, k : k + 256] = dot(full_h(v.h2), v.w_e[:, k : k + 256])
    sync = Sync(v.sync_three)
    e1, e2 = masked_sums(v.pre_e)
    sync.start(split_rows(e1) + split_rows(e2) + split_rows(s1) + split_rows(s2))
    g_b1.forward()
    g_u.start_near(0)
    g_u.start_far(1)
    for item in (g_c, g_ac):
        item.start_far()
        item.start_near()
    sums = sync.wait()
    norm_e = moments(join_rows(sums, 0, 4), join_rows(sums, 4, 4), count4)
    norm_s = moments(join_rows(sums, 8, 4), join_rows(sums, 12, 4), count4)

    def summed(at):
        return (
            gamma(6, 4) * normed(v.pre_e, at, norm_e)
            + beta(6, 4)
            + gamma(1, 4) * normed(v.pre_s, at, norm_s)
            + beta(1, 4)
        )

    def make_merged(k):
        at = rows_at(k, 48)
        v.joined[t, at, :] = jax.nn.silu(summed(at)).astype(BF)

    loop(12, make_merged)

    j_send, j_recv = take(3), take(SPLITS)

    def joined_copy(k, slot, device):
        return remote(
            v.joined.at[slot], v.joined.at[slot], j_send + k, j_recv + slot, {TENSOR: device}
        )

    joined_copy(0, t, t_x).start()
    joined_copy(1, t, t_core).start()

    pool_move = ToGroup(
        lambda owner, rows: v.pool_half.at[lax.rem(owner, 2), 0:rows, :],
        lambda slot, rows: v.pool_all.at[slot, 0:rows, :],
    )
    bin_row = lax.broadcasted_iota(jnp.int32, (BINS, 1), 0)

    def group_mask(group, shape=None):
        low, top = GROUP_ROWS[group]
        kept = jnp.where((bin_row >= low) & (bin_row < top), 1.0, 0.0)
        return kept if shape is None else jnp.broadcast_to(kept, shape)

    cells_in = wide(v.cells_in[...], 4)
    pooled = dot(v.pool[...], v.joined[t]) / cells_in
    v.pooled[...] = pooled.astype(BF)
    for k in range(2):
        v.pool_half[k] = v.pooled[:, k * 256 : k * 256 + 256]
    v.pool_all[me] = v.pool_half[lax.rem(me, 2)]
    g_b0.finish()
    g_b1.finish()
    part = jnp.zeros((BINS, 512), F32)
    for group in range(4):
        rows = (v.pooled[...].astype(F32) * group_mask(group)).astype(BF)
        part = part + dot(rows, v.w_b[group * 512 : group * 512 + 512, :])
    for k in range(SPLITS):
        v.part_b[k] = part[:, k * 128 : k * 128 + 128].astype(BF)
    v.recv_b[t] = v.part_b[t]
    ex = Exchange(TENSOR, SPLITS, lambda o: v.part_b.at[o], lambda s: v.recv_b.at[s])
    ex.start()
    g_u.forward(0)
    g_u.start_near(1)
    g_u.start_far(2)
    joined_copy(0, t_x, t_x).wait_recv()
    joined_copy(2, t_x, t_core).start()
    ex.wait()
    own_b = v.recv_b[0].astype(F32)
    for k in range(1, SPLITS):
        own_b = own_b + v.recv_b[k].astype(F32)
    v.all_b[me] = own_b.astype(BF)
    ex = Exchange(BATCH, OWNERS, lambda o: v.all_b.at[me], lambda s: v.all_b.at[s])
    ex.start()
    g_u.forward(1)
    g_u.start_near(2)
    g_u.start_far(3)
    ex.wait()
    all_b = [v.all_b[k].astype(F32) for k in range(OWNERS)]
    sum_b, square_b = all_b[0], all_b[0] * all_b[0]
    for k in range(1, OWNERS):
        sum_b = sum_b + all_b[k]
        square_b = square_b + all_b[k] * all_b[k]
    mean_b = jnp.zeros((BINS, 128), F32)
    scale_b = jnp.zeros((BINS, 128), F32)
    gamma_b = jnp.zeros((BINS, 128), F32)
    beta_b = jnp.zeros((BINS, 128), F32)
    count_b = jnp.zeros((BINS, 1), F32)
    for group, bins in enumerate(BIN_COUNTS):
        kept = group_mask(group)
        size = float(OWNERS * bins * bins)
        mean, scaling = moments(total(sum_b * kept), total(square_b * kept), size)
        mean_b = mean_b + kept * mean
        scale_b = scale_b + kept * scaling
        gamma_b = gamma_b + kept * gamma(10 + group)
        beta_b = beta_b + kept * beta(10 + group)
        count_b = count_b + kept / size
    spread_b = Spread(v.act_b)
    for k in range(OWNERS):
        out = gamma_b * ((all_b[k] - mean_b) * scale_b) + beta_b
        v.act_b[t, k * BINS : k * BINS + BINS, :] = jax.nn.silu(out).astype(BF)
    spread_b.start()
    g_u.forward(2)
    g_u.start_near(3)
    g_u.start_far(4)
    spread_b.wait()
    row_512 = lax.broadcasted_iota(jnp.int32, (OWNERS * BINS, 1), 0) & (BINS - 1)
    group_id = jnp.where(
        row_512 < 1, 0, jnp.where(row_512 < 5, 1, jnp.where(row_512 < 14, 2, jnp.where(row_512 < 50, 3, 9)))
    )

    def full_act():
        return jnp.concatenate([v.act_b[k] for k in range(SPLITS)], axis=1)

    v.zsum[...] = jnp.zeros((2, OWNERS * BINS, 128), F32)

    def own_branch(j, body):
        chunk = lax.rem(me + j, 8)
        pl.when(chunk >= MERGED)(lambda: body(chunk - MERGED, lax.div(me + j, 8)))

    def make_z(j):
        def body(group, side):
            kept = jnp.where(group_id == group, 1.0, 0.0)
            v.zsum[side] = v.zsum[side] + kept * dot(full_act(), v.w_own[rows_at(j, 512), :])

        own_branch(j, body)

    loop(9, make_z)
    for k in range(OWNERS):
        for side in range(2):
            v.z_send[k, side] = v.zsum[side, k * BINS : k * BINS + BINS, :].astype(BF)
    v.z_recv[me] = v.z_send[me]
    ex = Exchange(BATCH, OWNERS, lambda o: v.z_send.at[o], lambda s: v.z_recv.at[s])
    ex.start()
    g_u.forward(3)
    g_u.start_near(4)
    v.act_t[...] = full_act().T
    joined_copy(1, t_core, t_core).wait_recv()
    joined_copy(2, t_diag, t_core).wait_recv()
    for k in range(SPLITS):
        v.joined_t[k] = v.joined[k].T
    g_u.forward(4)
    g_c.forward()
    g_ac.forward()
    ex.wait()
    g_u.finish()

    def tap_z(tap):
        if tap == 0:
            return v.z_recv[0, 0].astype(F32)
        if tap == 8:
            return v.z_recv[7, 1].astype(F32)
        return v.z_recv[tap, 0].astype(F32) + v.z_recv[tap - 1, 1].astype(F32)

    for tap in range(9):
        z = tap_z(tap)
        high_z = z.astype(BF)
        v.z_cat[tap, :BINS, :] = high_z
        v.z_cat[tap, BINS:, :] = (z - high_z.astype(F32)).astype(BF)

    def full_joined():
        return jnp.concatenate([v.joined[k] for k in range(SPLITS)] + [v.pick_t[...]], axis=1)

    def w_tap(tap):
        return jnp.concatenate([v.w_u[rows_at(tap, 2048), :], v.z_cat[tap]], axis=0)

    def unite_pair(p):
        value = dot(full_joined(), jnp.concatenate([w_tap(2 * p), w_tap(2 * p + 1)], axis=1))
        v.pad[2 * p, EDGE : EDGE + CELLS, :] = value[:, :128]
        v.pad[2 * p + 1, EDGE : EDGE + CELLS, :] = value[:, 128:]

    loop(4, unite_pair)
    v.pad[8, EDGE : EDGE + CELLS, :] = dot(full_joined(), w_tap(8))
    for at in range(0, CELLS, BLOCK):
        v.pre_u[at : at + BLOCK, :] = shift_sum(range(9), 1, at, lambda tap: tap)
    sync = Sync(v.sync_five)
    sync.start(list(masked_sums(v.pre_u)))
    pool_move.start()
    g_a.start_far()
    g_a.start_near()
    for item in (g_c, g_ac):
        item.finish()
    for item in (g_gain, g_r, g_s, g_m, g_e, g_b0, g_b1, g_c, g_ac, g_u):
        item.drain()
    joined_copy(0, t, t_x).wait_send()
    joined_copy(1, t, t_core).wait_send()
    joined_copy(2, t_x, t_core).wait_send()
    w_ac = jnp.concatenate([v.w_ac[...], jnp.zeros((64, 256), F32)], axis=0).astype(BF)
    sums = sync.wait()
    norm_u = moments(sums[0:1], sums[1:2], count)

    def make_u(k):
        at = rows_at(k, 96)
        v.united[at, :] = jax.nn.silu(gamma(14) * normed(v.pre_u, at, norm_u) + beta(14)).astype(BF)

    loop(6, make_u)
    class Band:
        def __init__(self, at):
            self.at = at
            self.ex = Exchange(
                TENSOR,
                SPLITS,
                lambda o: v.logit_send.at[rows_at(o, 144), at],
                lambda s: v.logit_recv.at[s, :, at],
            )
            self.back = Spread(v.slope_in, at)

        def start(self, value):
            v.logit_send[:, self.at] = value.astype(BF)
            self.ex.start()
            v.logit_recv[t, :, self.at] = v.logit_send[rows_at(t, 144), self.at]

        def finish(self, factor):
            self.ex.wait()
            logits = v.logit_recv[0, :, self.at].astype(F32)
            for k in range(1, SPLITS):
                logits = logits + v.logit_recv[k, :, self.at].astype(F32)
            class_weight, loss_weight = class_weights()
            hot = jnp.where(wide(v.lab[rows_at(t, 144), :], 2) == lanes, 1.0, 0.0)
            cell_weight = factor * jnp.sum(hot * class_weight, axis=1, keepdims=True)
            value = jnp.where(lanes < float(NCLS), logits, -1e30)
            value = value - jnp.max(value, axis=1, keepdims=True)
            powers = jnp.exp(value)
            mass = jnp.sum(powers, axis=1, keepdims=True)
            loss_rows = total(fold(-cell_weight * hot * (value - jnp.log(mass))))
            grad = cell_weight * (powers / mass - hot) / loss_weight
            v.slope_in[t, :, self.at] = grad.astype(BF)
            self.back.start()
            return loss_rows[:, :128] + loss_rows[:, 128:]

        def grad(self):
            self.back.wait()
            return v.slope_in[:, :, self.at].reshape(CELLS, 256)

    def class_weights():
        total_valid = jnp.sum(class_count, axis=1, keepdims=True)
        weight = total_valid / (NCLS * class_count + total_valid)
        whole = jnp.sum(class_count * weight, axis=1, keepdims=True)
        return jnp.where(lanes < float(NCLS), weight, 0.0), whole

    main_head, aux_head = Band(slice(0, 256)), Band(slice(256, 512))
    main_head.start(dot(v.united[...], v.w_c[...]))
    g_a.forward()
    o_misc[1:2, :] = main_head.finish(1.0)

    g_a.finish()
    g_a.drain()

    def unpack(chunk):
        for pair in range(5):
            even = v.w_a[rows_at(2 * pair * 8 + chunk, 64), :].astype(F32)
            if pair < 4:
                odd = v.w_a[rows_at((2 * pair + 1) * 8 + chunk, 64), :].astype(F32)
            else:
                odd = jnp.zeros((64, 128), F32)
            low = jnp.where(left_half, even, pltpu.roll(odd, 64, 1))
            top = jnp.where(left_half, pltpu.roll(even, 64, 1), odd)
            v.pad[pair, pl.ds(EDGE, 64, stride=2), :] = low
            v.pad[pair, pl.ds(EDGE + 1, 64, stride=2), :] = top
            both = v.pad[pair, EDGE : EDGE + 128, :]
            v.w_pair[rows_at(chunk, 128), pair * 128 : pair * 128 + 128] = both.astype(BF)

    loop(8, unpack)

    for pair in (0, 2):
        value = dot(whole_feat(), v.w_pair[:, pair * 128 : pair * 128 + 256])
        v.pad[pair, EDGE : EDGE + CELLS, :] = value[:, :128]
        v.pad[pair + 1, EDGE : EDGE + CELLS, :] = value[:, 128:]
    v.pad[4, EDGE : EDGE + CELLS, :] = dot(whole_feat(), v.w_pair[:, 512:640])

    left_wide = lax.broadcasted_iota(jnp.int32, (BLOCK, 128), 1) < 64
    for at in range(0, CELLS, BLOCK):
        even = shift_sum((0, 2, 4, 6, 8), 1, at, lambda tap: tap // 2)
        odd = shift_sum((1, 3, 5, 7), 1, at, lambda tap: tap // 2)
        v.pre_a[at : at + BLOCK, :] = jnp.where(left_wide, even + pltpu.roll(odd, 64, 1), 0.0)

    sync_a = Sync(v.sync_aux)
    sync_a.start(list(masked_sums(v.pre_a)))
    g_main = main_head.grad()
    v.d_f[...] = dot_nt(g_main, v.w_c[...])

    def slope(value):
        gate = jax.nn.sigmoid(value)
        return gate * (1.0 + value * (1.0 - gate))

    def through_silu(ref, pre, norm, row):
        def step(k, carry):
            at = rows_at(k, 96)
            unit = normed(pre, at, norm)
            value = ref[at, :] * slope(gamma(row) * unit + beta(row))
            ref[at, :] = value
            return (carry[0] + fold(value), carry[1] + fold(value * unit))

        zero = jnp.zeros((8, 128), F32)
        sums = lax.fori_loop(0, 6, step, (zero, zero))
        return [total(sums[0]), total(sums[1])]

    def back_norm(value, unit, mask, norm, gain, first, second, size):
        inner = value - mask * (first + unit * second) / size
        return gain * norm[1] * inner

    gain_grads = {}
    sync = Sync(v.sync_b1)
    sync.start(through_silu(v.d_f, v.pre_u, norm_u, 14))
    sums = sync_a.wait()
    norm_a = moments(sums[0:1], sums[1:2], count)

    def make_a(k):
        at = rows_at(k, 96)
        v.act_a[at, :] = jax.nn.silu(gamma(15) * normed(v.pre_a, at, norm_a) + beta(15)).astype(BF)

    loop(6, make_a)
    aux_head.start(dot(v.act_a[...], w_ac))

    class Scatter:
        def __init__(self, first, second, full, rows, out, base=0):
            self.full, self.rows, self.out, self.base = full, rows, out, base
            self.first, self.second = first, second
            self.near_s, self.near_r = take(HALF), take(HALF)
            self.far_s, self.far_r = take(HALF), take(HALF)
            self.block = min(rows, 64)

        def near(self, step):
            dest = far_peer(partner, step)
            return remote(
                self.full.at[rows_at(dest, self.rows), :],
                self.first.at[step],
                self.near_s + step,
                self.near_r + step,
                {BATCH: partner},
            )

        def far(self, step):
            return remote(
                self.first.at[step],
                self.second.at[step - 1],
                self.far_s + step,
                self.far_r + step,
                {BATCH: far_peer(me, step)},
            )

        def start(self):
            for step in (1, 2, 3, 0):
                self.near(step).start()

        def middle(self):
            kind = self.first.dtype
            for step in range(1, HALF):
                self.near(step).wait_recv()
                base = far_peer(me, step) * (self.rows // self.block)

                def add(k, step=step, base=base):
                    at = rows_at(k, self.block)
                    value = self.full[rows_at(base + k, self.block), :].astype(F32)
                    value = value + self.first[step, at, :].astype(F32)
                    self.first[step, at, :] = value.astype(kind)

                loop(self.rows // self.block, add)
                self.far(step).start()

        def end(self):
            self.near(0).wait_recv()
            for step in range(1, HALF):
                self.far(step).wait_recv()
            base = me * (self.rows // self.block)

            def add(k, carry):
                at = rows_at(k, self.block)
                value = self.full[rows_at(base + k, self.block), :].astype(F32)
                value = value + self.first[0, at, :].astype(F32)
                for step in range(1, HALF):
                    value = value + self.second[step - 1, at, :].astype(F32)
                if self.out is o_flat:
                    times = value.shape[1] // 128
                    start = self.base + k * self.block * times
                    for q in range(times):
                        where = pl.ds(start + q, self.block, stride=times if times > 1 else None)
                        self.out[where, :] = value[:, q * 128 : q * 128 + 128]
                else:
                    self.out[at, :] = value
                return carry + fold(value * value)

            squares = lax.fori_loop(
                0, self.rows // self.block, add, jnp.zeros((8, self.full.shape[1]), F32)
            )
            for step in (1, 2, 3, 0):
                self.near(step).wait_send()
                if step:
                    self.far(step).wait_send()
            return sum(split_rows(total(squares)))

    s_c = Scatter(v.first_c, v.second_c, v.w_c, 16, v.out_c)
    s_ac = Scatter(v.first_ac, v.second_ac, v.w_ac, 8, v.out_ac)
    s_a = Scatter(v.first_a, v.second_a, v.w_a, 576, v.out_a)
    s_s = Scatter(v.first_s, v.second_s, v.w_s, 128, o_flat, 128)
    s_e = Scatter(v.first_e, v.second_e, v.w_e, 64, o_flat, 1216)
    s_m = Scatter(v.first_m, v.second_m, v.w_m, 576, o_flat, 640)
    s_r = Scatter(v.first_r, v.second_r, v.w_r, 128, o_flat, 0)

    class ScatterUnite:
        def __init__(self):
            self.near_s, self.near_r = take(SLOTS * HALF), take(SLOTS * HALF)
            self.far_s, self.far_r = take(SLOTS * HALF), take(SLOTS * HALF)

        def near(self, step, slot, base):
            dest = far_peer(base, step)
            return remote(
                v.w_u.at[merged_rows(dest, slot), :],
                v.first_u.at[step, slot],
                self.near_s + step * SLOTS + slot,
                self.near_r + step * SLOTS + slot,
                {BATCH: partner},
            )

        def far(self, step, slot):
            return remote(
                v.first_u.at[step, slot],
                v.second_u.at[step - 1, slot],
                self.far_s + step * SLOTS + slot,
                self.far_r + step * SLOTS + slot,
                {BATCH: far_peer(me, step)},
            )

        def own_rows(self, owner, slot, k):
            block = owner * 9 + block_of(owner, slot)
            index = lax.div(block, 8) * MERGED + lax.rem(block, 8)
            return rows_at(index * 8 + k, 64)

        def start(self, slot):
            for step in (1, 2, 3, 0):
                has(
                    far_peer(partner, step),
                    slot,
                    lambda step=step: self.near(step, slot, partner).start(),
                )

        def middle(self, slot):
            for step in range(1, HALF):
                owner = far_peer(me, step)

                def go(step=step, owner=owner):
                    self.near(step, slot, me).wait_recv()

                    def add(k):
                        at = rows_at(k, 64)
                        value = v.w_u[self.own_rows(owner, slot, k), :].astype(F32)
                        value = value + v.first_u[step, slot, at, :].astype(F32)
                        v.first_u[step, slot, at, :] = value.astype(BF)

                    loop(8, add)
                    self.far(step, slot).start()

                has(owner, slot, go)

        def end(self):
            for slot in range(SLOTS):

                def go(slot=slot):
                    self.near(0, slot, me).wait_recv()
                    for step in range(1, HALF):
                        self.far(step, slot).wait_recv()
                    j = block_of(me, slot)

                    def add(k):
                        at = rows_at(k, 64)
                        value = v.w_u[self.own_rows(me, slot, k), :].astype(F32)
                        value = value + v.first_u[0, slot, at, :].astype(F32)
                        for step in range(1, HALF):
                            value = value + v.second_u[step - 1, slot, at, :].astype(F32)
                        o_u[rows_at(j * 8 + k, 64), :] = value

                    loop(8, add)

                has(me, slot, go)
                for step in (1, 2, 3, 0):
                    has(
                        far_peer(partner, step),
                        slot,
                        lambda step=step, slot=slot: self.near(step, slot, partner).wait_send(),
                    )
                    if step:
                        has(
                            far_peer(me, step),
                            slot,
                            lambda step=step, slot=slot: self.far(step, slot).wait_send(),
                        )

            def square(k, carry):
                value = o_u[rows_at(k, 64), :]
                return carry + fold(value * value)

            squares = lax.fori_loop(0, 72, square, jnp.zeros((8, 128), F32))
            return sum(split_rows(total(squares)))

    s_u = ScatterUnite()

    v.w_c[...] = dot_tn(v.united[...], g_main).astype(BF)
    s_c.start()
    sums = sync.wait()
    gain_grads[14] = (sums[1:2], sums[0:1])

    def spread_taps(ref, pre, norm, row, first, second):
        def step(k):
            at = rows_at(k, 96)
            value = back_norm(
                ref[at, :], normed(pre, at, norm), v.ins[at, :], norm, gamma(row), first, second, count
            )
            ref[at, :] = value.astype(BF).astype(F32)

        loop(6, step)
        v.grad_pad[EDGE : EDGE + CELLS, :] = ref[...]

    def back_tap(tap, spacing, at):
        start = EDGE + at - offset(tap, spacing)
        value = v.grad_pad[start : start + 96, :]
        right = tap % 3 - 1
        if right:
            value = value * col_mask(slice(at, at + 96), -right * spacing)
        return value

    def fill(cat, spacing):
        for tap in range(9):
            for at in range(0, CELLS, 96):
                cat[at : at + 96, tap * 128 : tap * 128 + 128] = back_tap(tap, spacing, at).astype(
                    BF
                )

    spread_taps(v.d_f, v.pre_u, norm_u, 14, sums[0:1], sums[1:2])
    fill(v.cat_u, 1)

    dz = dot(v.pick[...], v.cat_u[...])
    for tap in range(9):
        v.dz_send[tap] = dz[:, tap * 128 : tap * 128 + 128].astype(BF)
    v.dz_recv[me] = v.dz_send[pl.ds(me, 2)]
    ex_dz = Exchange(
        BATCH, OWNERS, lambda o: v.dz_send.at[pl.ds(o, 2)], lambda s: v.dz_recv.at[s]
    )
    ex_dz.start()

    def merged_back(c):
        weight = jnp.concatenate(
            [v.w_u[rows_at(tap * MERGED + c, 512), :] for tap in range(9)], axis=1
        )
        v.joined[c] = dot_nt(v.cat_u[...], weight).astype(BF)

    near_s, near_r, far_s, far_r = take(2), take(2), take(1), take(1)

    def dm_near(k, slot):
        return remote(
            v.joined.at[slot], v.dm_near.at[k], near_s + k, near_r + k, {TENSOR: t_core}
        )

    merged_back(t_diag)
    dm_near(1, t_diag).start()
    merged_back(t_core)
    dm_near(0, t_core).start()
    merged_back(t_x)
    merged_back(t)

    def unite_grad(c):
        for p in range(5):
            width = 256 if p < 4 else 128
            value = dot(v.joined_t[c], v.cat_u[:, p * 256 : p * 256 + width])
            v.w_u[rows_at(2 * p * MERGED + c, 512), :] = value[:, :128].astype(BF)
            if p < 4:
                v.w_u[rows_at((2 * p + 1) * MERGED + c, 512), :] = value[:, 128:].astype(BF)

    unite_grad(0)
    s_u.start(0)
    o_misc[1:2, :] = o_misc[1:2, :] + aux_head.finish(0.4)
    ex_dz.wait()

    d_act = v.d_sum.at[0 : OWNERS * BINS, :]
    d_act[...] = jnp.zeros((OWNERS * BINS, 512), F32)

    def branch_back(j):
        def body(group, side):
            kept = jnp.where(group_id == group, 1.0, 0.0)
            value = v.dz_recv[:, side].reshape(OWNERS * BINS, 128).astype(F32) * kept
            value = value.astype(BF)
            o_u[rows_at(j, 512), :] = dot(v.act_t[...], value)
            d_act[...] = d_act[...] + dot_nt(value, v.w_own[rows_at(j, 512), :])

        own_branch(j, body)

    loop(9, branch_back)
    for k in range(SPLITS):
        v.d_act_send[k] = d_act[:, k * 128 : k * 128 + 128].astype(BF)
    v.d_act_recv[t] = v.d_act_send[t]
    ex = Exchange(TENSOR, SPLITS, lambda o: v.d_act_send.at[o], lambda s: v.d_act_recv.at[s])
    ex.start()
    unite_grad(1)
    s_u.start(1)
    dm_near(1, t_x).wait_recv()

    def add_x(k):
        at = rows_at(k, 48)
        value = v.joined[t_x, at, :].astype(F32) + v.dm_near[1, at, :].astype(F32)
        v.joined[t_x, at, :] = value.astype(BF)

    loop(12, add_x)
    dm_far = remote(v.joined.at[t_x], v.dm_far, far_s, far_r, {TENSOR: t_x})
    dm_far.start()
    g_aux = aux_head.grad()
    v.d_f2[...] = dot_nt(g_aux, w_ac)
    sync_a = Sync(v.sync_b2)
    sync_a.start(through_silu(v.d_f2, v.pre_a, norm_a, 15))
    v.w_ac[...] = dot_tn(v.act_a[...], g_aux)[:64]
    s_ac.start()

    unite_grad(2)
    unite_grad(3)
    ex.wait()
    for k in range(OWNERS):
        at = slice(k * BINS, k * BINS + BINS)
        value = v.d_act_recv[0, at, :].astype(F32)
        for slot in range(1, SPLITS):
            value = value + v.d_act_recv[slot, at, :].astype(F32)
        v.d_img_send[k] = value.astype(BF)
    v.d_img_recv[me] = v.d_img_send[me]
    ex = Exchange(BATCH, OWNERS, lambda o: v.d_img_send.at[o], lambda s: v.d_img_recv.at[s])
    ex.start()
    s_u.start(2)
    s_u.middle(0)

    sums = sync_a.wait()
    gain_grads[15] = (sums[1:2], sums[0:1])
    spread_taps(v.d_f2, v.pre_a, norm_a, 15, sums[0:1], sums[1:2])
    for p in range(5):
        for at in range(0, CELLS, 96):
            value = back_tap(2 * p, 1, at)
            if p < 4:
                value = value + pltpu.roll(back_tap(2 * p + 1, 1, at), 64, 1)
            v.cat_a[at : at + 96, p * 128 : p * 128 + 128] = value.astype(BF)

    def aux_grad(c2):
        value2 = dot_tn(v.whole[c2], v.cat_a[...])
        for half in range(2):
            value = value2[half * 128 : half * 128 + 128]
            c = 2 * c2 + half
            for p in range(5):
                v.pad[p, EDGE : EDGE + 128, :] = value[:, p * 128 : p * 128 + 128]
                low = v.pad[p, pl.ds(EDGE, 64, stride=2), :]
                top = v.pad[p, pl.ds(EDGE + 1, 64, stride=2), :]
                even = jnp.where(left_half, low, pltpu.roll(top, 64, 1))
                v.w_a[rows_at(2 * p * 8 + c, 64), :] = even.astype(BF)
                if p < 4:
                    odd = jnp.where(left_half, pltpu.roll(low, 64, 1), top)
                    v.w_a[rows_at((2 * p + 1) * 8 + c, 64), :] = odd.astype(BF)

    loop(SPLITS, aux_grad)
    ex.wait()
    d_b = v.d_img_recv[0].astype(F32)
    for k in range(1, OWNERS):
        d_b = d_b + v.d_img_recv[k].astype(F32)
    unit_b = (v.all_b[me].astype(F32) - mean_b) * scale_b
    d_b = d_b * slope(gamma_b * unit_b + beta_b)
    sync = Sync(v.sync_b3)
    sync.start(
        [total(d_b * group_mask(g)) for g in range(4)]
        + [total(d_b * unit_b * group_mask(g)) for g in range(4)]
    )
    s_u.start(3)
    s_u.middle(1)
    sums = sync.wait()
    first_b = jnp.zeros((BINS, 128), F32)
    second_b = jnp.zeros((BINS, 128), F32)
    for group in range(4):
        kept = group_mask(group)
        gain_grads[10 + group] = (sums[4 + group : 5 + group], sums[group : group + 1])
        first_b = first_b + kept * sums[group : group + 1]
        second_b = second_b + kept * sums[4 + group : 5 + group]
    inner = d_b - (first_b + unit_b * second_b) * count_b
    v.d_bp[t] = (gamma_b * scale_b * inner).astype(BF)
    spread_d = Spread(v.d_bp)
    spread_d.start()
    s_u.start(4)
    s_u.middle(2)
    spread_d.wait()
    d_bp_move = ToGroup(
        lambda owner, rows: v.d_bp.at[:, 0:rows, :],
        lambda slot, rows: v.d_bp_all.at[slot, :, 0:rows, :],
    )
    d_bp_move.start()
    v.d_bp_all[me] = v.d_bp[...]
    d_bp = jnp.concatenate([v.d_bp[k] for k in range(SPLITS)], axis=1)
    d_pooled = jnp.zeros((BINS, 512), F32)
    for group in range(4):
        rows = (d_bp.astype(F32) * group_mask(group)).astype(BF)
        d_pooled = d_pooled + dot_nt(rows, v.w_b[group * 512 : group * 512 + 512, :])
    d_pooled = (d_pooled / cells_in).astype(BF)
    v.d_sum[...] = dot_tn(v.pool[...], d_pooled)
    dm_near(0, t).wait_recv()
    dm_far.wait_recv()

    def through_sum(k, carry):
        at = rows_at(k, 48)
        value = v.d_sum[at, :] + v.joined[t, at, :].astype(F32) + v.dm_near[0, at, :].astype(F32)
        value = (value + v.dm_far[at, :].astype(F32)) * slope(summed(at))
        v.d_sum[at, :] = value
        return (
            carry[0] + fold(value),
            carry[1] + fold(value * normed(v.pre_e, at, norm_e)),
            carry[2] + fold(value * normed(v.pre_s, at, norm_s)),
        )

    zero = jnp.zeros((8, 512), F32)
    three = [total(item) for item in lax.fori_loop(0, 12, through_sum, (zero, zero, zero))]
    sync = Sync(v.sync_b4)
    sync.start(split_rows(three[0]) + split_rows(three[1]) + split_rows(three[2]))
    s_a.start()
    s_u.middle(3)
    sums = sync.wait()
    first_s = join_rows(sums, 0, 4)
    second_e, second_s = join_rows(sums, 4, 4), join_rows(sums, 8, 4)
    for k in range(4):
        gain_grads[6 + k] = (sums[4 + k : 5 + k], sums[k : k + 1])
        gain_grads[1 + k] = (sums[8 + k : 9 + k], sums[k : k + 1])

    def back_both(k):
        at = rows_at(k, 48)
        value, mask = v.d_sum[at, :], wide(v.ins[at, :], 4)
        v.d_e[at, :] = back_norm(
            value, normed(v.pre_e, at, norm_e), mask, norm_e, gamma(6, 4), first_s, second_e, count4
        ).astype(BF)
        v.d_s[at, :] = back_norm(
            value, normed(v.pre_s, at, norm_s), mask, norm_s, gamma(1, 4), first_s, second_s, count4
        ).astype(BF)

    loop(12, back_both)

    def back_hidden(grad, weight, index):
        value = dot_nt(grad, weight)
        for k in range(SPLITS):
            v.dh_send[k] = value[:, k * 128 : k * 128 + 128].astype(BF)
        v.dh_recv[index, t] = v.dh_send[t]
        ex = Exchange(
            TENSOR, SPLITS, lambda o: v.dh_send.at[o], lambda s: v.dh_recv.at[index, s]
        )
        ex.start()
        return ex

    def hidden_sum(index):
        def step(k):
            at = rows_at(k, 96)
            value = v.dh_recv[index, 0, at, :].astype(F32)
            for slot in range(1, SPLITS):
                value = value + v.dh_recv[index, slot, at, :].astype(F32)
            v.d_f[at, :] = value

        loop(6, step)

    ex = back_hidden(v.d_e[...], v.w_e[...], 0)
    def short_grad(c):
        v.w_s[rows_at(c, 256), :] = dot_tn(v.whole[c], v.d_s[...]).astype(BF)

    loop(SPLITS, short_grad)
    s_s.start()
    s_u.middle(4)
    for k in range(SPLITS):
        v.w_e[k * 128 : k * 128 + 128, :] = dot_tn(v.h2[k], v.d_e[...]).astype(BF)
    ex.wait()
    hidden_sum(0)
    sync = Sync(v.sync_b5)
    sync.start(through_silu(v.d_f, v.pre_m, norm_m, 5))
    s_e.start()
    s_c.middle()
    s_ac.middle()
    s_a.middle()
    sums = sync.wait()
    gain_grads[5] = (sums[1:2], sums[0:1])
    spread_taps(v.d_f, v.pre_m, norm_m, 5, sums[0:1], sums[1:2])
    fill(v.cat_u, 4)
    weight = jnp.concatenate([v.w_m[tap * 512 : tap * 512 + 512, :] for tap in range(9)], axis=1)
    ex = back_hidden(v.cat_u[...], weight, 1)

    def middle_grad(k):
        value = dot_tn(v.h1[k], v.cat_u[...])
        for tap in range(9):
            v.w_m[rows_at(tap * 4 + k, 128), :] = value[:, tap * 128 : tap * 128 + 128].astype(BF)

    loop(SPLITS, middle_grad)
    s_m.start()
    s_s.middle()
    ex.wait()
    hidden_sum(1)
    sync = Sync(v.sync_b6)
    sync.start(through_silu(v.d_f, v.pre_r, norm_r, 0))

    s_e.middle()
    sums = sync.wait()
    gain_grads[0] = (sums[1:2], sums[0:1])

    def back_reduce(k):
        at = rows_at(k, 96)
        v.d_low[at, :] = back_norm(
            v.d_f[at, :], normed(v.pre_r, at, norm_r), v.ins[at, :], norm_r, gamma(0), sums[0:1], sums[1:2], count
        ).astype(BF)

    loop(6, back_reduce)

    def reduce_grad(c):
        v.w_r[rows_at(c, 256), :] = dot_tn(v.whole[c], v.d_low[...]).astype(BF)

    loop(SPLITS, reduce_grad)
    s_r.start()
    for item in (s_m, s_r):
        item.middle()
    pool_move.wait()
    d_bp_move.wait()
    own_group = jnp.where(group_id == lax.div(me, 2), 1.0, 0.0)
    d_rows = jnp.concatenate(
        [v.d_bp_all[:, k].reshape(OWNERS * BINS, 128) for k in range(SPLITS)], axis=1
    )
    d_rows = (d_rows.astype(F32) * own_group).astype(BF)
    branch_grad = dot_tn(v.pool_all[...].reshape(OWNERS * BINS, 256), d_rows)
    for k in range(4):
        o_flat[pl.ds(1472 + k, 256, stride=4), :] = branch_grad[:, k * 128 : k * 128 + 128]
    rest = (s_c, s_ac, s_a, s_e, s_s, s_m, s_r)
    squares = s_u.end() + sum(split_rows(total(branch_grad * branch_grad)))
    for item in rest:
        squares = squares + item.end()
    dm_near(1, t_diag).wait_send()
    dm_near(0, t_core).wait_send()
    dm_far.wait_send()

    v.gain_rows[...] = jnp.zeros((40, 128), F32)
    gammas = [gain_grads[row][0] for row in range(16)]
    betas = [pltpu.roll(gain_grads[row][1], 64, 1) for row in range(16)]
    o_shift[...] = gain_grads[14][1]
    for row in range(31):
        if row < 15:
            value = gammas[row]
        else:
            left = gammas[15] if row == 15 else betas[row - 16]
            value = jnp.where(lane < 64, left, betas[row - 15])
        v.gain_rows[row + 1 : row + 2, :] = value
    squares = squares + total(fold(v.gain_rows[...] * v.gain_rows[...])) / OWNERS

    sync = Sync(v.sync_end)
    sync.start([squares, o_misc[1:2, :]])

    tail = {}

    def put(where, value):
        tail[where] = value if where not in tail else tail[where] + value

    def class_tail(ref, count, base):
        for row in range(count):
            first, shift = divmod(base + NCLS * row, 128)
            for k in range(2):
                value = roll(ref[row : row + 1, k * 128 : k * 128 + 128], shift)
                put(first + k, jnp.where(lane >= shift, value, 0.0))
                if shift:
                    put(first + k + 1, jnp.where(lane < shift, value, 0.0))

    class_tail(v.out_c, 16, 0)
    class_tail(v.out_ac, 8, 76128)
    start = lax.rem(496 * me, 128)
    first = lax.div(496 * me, 128)
    own = [
        pltpu.roll(v.gain_rows[pl.ds(first + k, 1), :], lax.rem(16 - start + 128, 128), 1)
        for k in range(6)
    ]
    spot = lane - 16 + start
    for k in range(4):
        value = jnp.where(spot < 0, own[k], jnp.where(spot >= 128, own[k + 2], own[k + 1]))
        put(604 + k, jnp.where(lane >= 16, value, 0.0) if k == 0 else value)
    v.grad_pad[EDGE : EDGE + 576, :] = pltpu.roll(v.out_a[...], 96, 1)
    o_flat[7122:7706, :] = jnp.where(
        lane >= 96, v.grad_pad[EDGE : EDGE + 584, :], v.grad_pad[EDGE - 1 : EDGE + 583, :]
    )
    for row in range(608):
        if row in (18, 594):
            o_flat[7104 + row : 7105 + row, :] = o_flat[7104 + row : 7105 + row, :] + tail[row]
        elif row < 18 or row > 594:
            o_flat[7104 + row : 7105 + row, :] = tail[row]
    v.end_t[t] = sync.wait()
    spread_e = Spread(v.end_t)
    spread_e.start()
    spread_e.wait()
    ends = v.end_t[0]
    for k in range(1, SPLITS):
        ends = ends + v.end_t[k]
    o_misc[...] = ends
    o_misc[2:3, :] = jnp.broadcast_to(class_weights()[1], (1, 128))


def whole_step(sizes, labels, feat, flat):
    plan = scratch_plan()
    vmem = pl.BlockSpec(memory_space=pltpu.VMEM)
    anywhere = pl.BlockSpec(memory_space=pl.ANY)
    outs = [flat.shape, (1, 128), (8, 128)]
    return pl.pallas_call(
        functools.partial(step_kernel, tuple(plan)),
        out_shape=[jax.ShapeDtypeStruct(shape, F32) for shape in outs],
        in_specs=[pl.BlockSpec(memory_space=pltpu.SMEM), vmem, anywhere, anywhere],
        out_specs=[vmem] * len(outs),
        scratch_shapes=[pltpu.VMEM(shape, kind) for shape, kind in plan.values()]
        + [pltpu.SemaphoreType.DMA((SEMAPHORES,))],
        compiler_params=pltpu.CompilerParams(
            collective_id=0, has_side_effects=True, vmem_limit_bytes=63 * 1024 * 1024
        ),
        name="whole_step",
    )(sizes, labels, feat, flat)


def update_kernel(
    misc, grad, param, first, second, average,
    o_param, o_first, o_second, o_average, o_norm, o_loss, o_weight,
):
    norm = jnp.sqrt(jnp.sum(misc[0:1, :], axis=1, keepdims=True))
    o_norm[...] = norm
    o_loss[...] = jnp.sum(misc[1:2, :], axis=1, keepdims=True)
    o_weight[...] = misc[2:3, 0:1]
    clipped = grad[...] * jnp.minimum(1.0, 0.05 / (norm + 1e-06))
    new_first = 0.5 * first[...] + 0.5 * clipped
    new_second = 0.5 * second[...] + 0.5 * clipped * clipped
    lift = 1.0 / (1.0 - 0.5**STEP)
    old = param[...]
    ratio = (new_first * lift) / (jnp.sqrt(new_second * lift) + 1e-08)
    new = old - 0.01 * (ratio + 0.01 * old)
    o_param[...] = new
    o_first[...] = new_first
    o_second[...] = new_second
    o_average[...] = 0.999 * average[...] + 0.001 * new


def update(misc, grad, param, first, second, average):
    rows = grad.shape[0]
    block = pl.BlockSpec((1024, 128), lambda i: (i, 0))
    whole = pl.BlockSpec((8, 128), lambda i: (0, 0))
    one = pl.BlockSpec((1, 1), lambda i: (0, 0))
    big = jax.ShapeDtypeStruct((rows, 128), F32)
    return pl.pallas_call(
        update_kernel,
        grid=(pl.cdiv(rows, 1024),),
        out_shape=[big] * 4 + [jax.ShapeDtypeStruct((1, 1), F32)] * 3,
        in_specs=[whole] + [block] * 5,
        out_specs=[block] * 4 + [one] * 3,
        compiler_params=pltpu.CompilerParams(vmem_limit_bytes=60 * 1024 * 1024),
        name="update",
    )(misc, grad, param, first, second, average)


def fits(splits, owners):
    return splits == SPLITS and owners == OWNERS


def local_fast(features, labels, valid, sizes, params, first_moment, squared_mean, average):
    flat = params.reshape(-1, 128)
    marked = jnp.where(valid > 0, labels, -1).astype(F32).reshape(CELLS, 1)
    grad, shift_grad, misc = whole_step(
        sizes, jnp.broadcast_to(marked, (CELLS, 128)), features.reshape(CELLS, -1), flat
    )
    news = update(
        misc,
        grad,
        flat,
        first_moment.reshape(-1, 128),
        squared_mean.reshape(-1, 128),
        average.reshape(-1, 128),
    )
    new_params, new_first, new_second, new_average = [
        item.reshape(params.shape) for item in news[:4]
    ]
    return (
        new_params,
        new_first,
        new_second,
        new_average,
        new_params.astype(BF),
        news[4].reshape(()),
        news[5].reshape(()),
        news[6].reshape(()),
        shift_grad.reshape(128),
    )


def solution(mesh):
    chosen = local_fast if fits(mesh.shape["tensor"], mesh.shape["batch"]) else local
    return jax.shard_map(
        chosen,
        mesh=mesh,
        in_specs=(
            P("batch", None, None, "tensor"),
            P("batch", None, None),
            P("batch", None, None),
            P("batch", None),
            P("tensor", "batch"),
            P("tensor", "batch"),
            P("tensor", "batch"),
            P("tensor", "batch"),
        ),
        out_specs=(
            P("tensor", "batch"),
            P("tensor", "batch"),
            P("tensor", "batch"),
            P("tensor", "batch"),
            P("tensor", "batch"),
            P(),
            P(),
            P(),
            P("tensor"),
        ),
        check_vma=False,
    )
```

```python
import functools

import jax
import jax.numpy as jnp
from jax import lax
from jax.experimental import pallas as pl
from jax.experimental.pallas import tpu as pltpu
from jax.sharding import PartitionSpec as P

C_IN = 1024
MID = 512
C_OUT = 2048
PPM = 512
AUXW = 256
NCLS = 150
MAP = 24
STEP = 3


BIN_COUNTS = (1, 2, 3, 6)
BIN_STARTS = (0, 1, 5, 14)


def segment_shapes(splits):
    return [
        (C_IN, MID // splits),
        (C_IN, C_OUT // splits),
        (9, MID, MID // splits),
        (MID, C_OUT // splits),
        (4, C_OUT // splits, PPM),
        (9, C_OUT + 4 * PPM, PPM // splits),
        (PPM // splits, NCLS),
        (9, C_IN, AUXW // splits),
        (AUXW // splits, NCLS),
        (2, (2 * MID + 2 * C_OUT + 5 * PPM + AUXW) // splits),
    ]


def unflatten(rows, splits):
    split_parts = []
    start = 0
    for shape in segment_shapes(splits):
        count = 1
        for extent in shape:
            count = count * extent
        count = count // rows.shape[0]
        split_parts.append(rows[:, start : start + count].reshape(shape))
        start = start + count
    return split_parts


def gain_pieces(gains, splits):
    widths = [MID, C_OUT, MID, C_OUT, PPM, PPM, PPM, PPM, PPM, AUXW]
    split_parts = []
    start = 0
    for width in widths:
        step_width = width // splits
        split_parts.append(gains[:, start : start + step_width])
        start = start + step_width
    return split_parts


def shifted(field, down, right):
    image_height, width = (field.shape[1], field.shape[2])
    rows_pad, cols_pad = (abs(down), abs(right))
    padded = jnp.pad(field, ((0, 0), (rows_pad, rows_pad), (cols_pad, cols_pad), (0, 0)))
    return padded[
        :,
        rows_pad + down : rows_pad + down + image_height,
        cols_pad + right : cols_pad + right + width,
        :,
    ]


def conv_forward(field, kernel, spacing):
    total = jnp.zeros(field.shape[:-1] + (kernel.shape[2],), jnp.float32)
    for tap in range(9):
        moved = shifted(field, (tap // 3 - 1) * spacing, (tap % 3 - 1) * spacing)
        total = total + jnp.dot(moved, kernel[tap], preferred_element_type=jnp.float32)
    return total


def conv_input_back(grad, kernel, spacing):
    total = jnp.zeros(grad.shape[:-1] + (kernel.shape[1],), jnp.float32)
    for tap in range(9):
        product = jnp.dot(grad, kernel[tap].T, preferred_element_type=jnp.float32)
        total = total + shifted(product, -(tap // 3 - 1) * spacing, -(tap % 3 - 1) * spacing)
    return total


def conv_kernel_back(field, grad, spacing):
    return jnp.stack(
        [
            jnp.einsum(
                "ihwc,ihwd->cd",
                shifted(field, (tap // 3 - 1) * spacing, (tap % 3 - 1) * spacing),
                grad,
                preferred_element_type=jnp.float32,
            )
            for tap in range(9)
        ]
    )


def silu_slope(value):
    gate = jax.nn.sigmoid(value)
    return gate * (1.0 + value * (1.0 - gate))


def channel_sums(values):
    return values.reshape(-1, values.shape[-1]).sum(0)


def masked_norm_apply(items, extra):
    sends = []
    for value, mask, norm in items:
        sends = sends + [
            channel_sums(value * mask),
            channel_sums(value * value * mask),
            jnp.sum(mask) * jnp.ones((1,), jnp.float32),
        ]
    totals = lax.psum(tuple(sends + extra), "batch")
    results = []
    for index, (value, mask, norm) in enumerate(items):
        count = totals[3 * index + 2]
        mean = totals[3 * index] / count
        spread = totals[3 * index + 1] / count - mean * mean
        scaling = lax.rsqrt(spread + 1e-05)
        normed = (value - mean) * scaling
        results.append((norm[0] * normed + norm[1], normed, scaling, count, mask, norm[0]))
    return (results, totals[3 * len(items) :])


def norm_backward(items):
    sends = []
    for grad, kept in items:
        sends = sends + [channel_sums(grad), channel_sums(grad * kept[1])]
    totals = lax.psum(tuple(sends), "batch")
    results = []
    for index, (grad, kept) in enumerate(items):
        outcome, normed, scaling, count, mask, gamma = kept
        first_sum, second_sum = (totals[2 * index], totals[2 * index + 1])
        inner = grad - mask * (first_sum + normed * second_sum) / count
        results.append(gamma * scaling * inner)
    return (results, sends, totals)


def bin_tables(extent, bins, length):
    which = jnp.arange(bins, dtype=jnp.int32)[None, :, None]
    place = jnp.arange(length, dtype=jnp.int32)[None, None, :]
    edge = extent[:, None, None]
    lower = which * edge // bins
    upper = ((which + 1) * edge + bins - 1) // bins
    member = ((place >= lower) & (place < upper)).astype(jnp.float32)
    target = jnp.minimum(place * bins // edge, bins - 1)
    chosen = (target == which).astype(jnp.float32)
    return (member, chosen)


def spread_bins(merged, branch, tables, images):
    joined = [merged]
    for group, bins in enumerate(BIN_COUNTS):
        rows_in, cols_in, rows_pick, cols_pick, cell_count = tables[group]
        piece = branch[:, BIN_STARTS[group] : BIN_STARTS[group] + bins * bins].reshape(
            images, bins, bins, -1
        )
        joined.append(
            jnp.einsum(
                "ikh,ilw,iklc->ihwc",
                rows_pick.astype(jnp.bfloat16),
                cols_pick.astype(jnp.bfloat16),
                piece,
                preferred_element_type=jnp.float32,
            ).astype(jnp.bfloat16)
        )
    return jnp.concatenate(joined, axis=-1)


def pick_bins(d_joined, width, tables, images):
    branch_width = (d_joined.shape[-1] - width) // 4
    d_up = []
    for group, bins in enumerate(BIN_COUNTS):
        rows_in, cols_in, rows_pick, cols_pick, cell_count = tables[group]
        piece = d_joined[..., width + group * branch_width : width + (group + 1) * branch_width]
        d_up.append(
            jnp.einsum("ikh,ilw,ihwc->iklc", rows_pick, cols_pick, piece).reshape(
                images, bins * bins, -1
            )
        )
    return (d_joined[..., :width], jnp.concatenate(d_up, axis=1))


def gather_channels(field):
    return lax.all_gather(field, "tensor", axis=3, tiled=True)


def scatter_channels(field):
    return lax.psum_scatter(
        field.astype(jnp.bfloat16), "tensor", scatter_dimension=3, tiled=True
    ).astype(jnp.float32)


def local(features, labels, valid, sizes, params, first_moment, squared_mean, average):
    splits = lax.axis_size("tensor")
    owners = lax.axis_size("batch")
    images = features.shape[0]
    gathered = lax.all_gather(params.astype(jnp.bfloat16), "batch", axis=0, tiled=True)
    (
        w_reduce,
        w_short,
        w_middle,
        w_expand,
        w_branch,
        w_unite,
        w_classes,
        w_aux,
        w_aux_classes,
        gains,
    ) = unflatten(gathered, splits)
    norms = [(piece[0], piece[1]) for piece in gain_pieces(gains.astype(jnp.float32), splits)]
    rows_at = jnp.arange(MAP, dtype=jnp.int32)
    inside = (rows_at[None, :, None] < sizes[:, 0][:, None, None]) & (
        rows_at[None, None, :] < sizes[:, 1][:, None, None]
    )
    inside = inside.astype(jnp.float32)[..., None]
    counted = inside * valid.astype(jnp.float32)[..., None]
    labels_hot = (labels[..., None] == jnp.arange(NCLS, dtype=jnp.int32)).astype(jnp.float32)
    class_local = channel_sums(labels_hot * counted)
    whole = lax.all_gather(features, "tensor", axis=3, tiled=True)
    pre_reduce = jnp.dot(whole, w_reduce, preferred_element_type=jnp.float32)
    pre_short = jnp.dot(whole, w_short, preferred_element_type=jnp.float32)
    pre_aux = conv_forward(whole, w_aux, 1)
    leading_part, label_tally = masked_norm_apply(
        [
            (pre_reduce, inside, norms[0]),
            (pre_short, inside, norms[1]),
            (pre_aux, inside, norms[9]),
        ],
        [class_local],
    )
    class_pixel_counts = label_tally[0]
    hidden_one = jax.nn.silu(leading_part[0][0]).astype(jnp.bfloat16)
    aux_act = jax.nn.silu(leading_part[2][0]).astype(jnp.bfloat16)
    hidden_full = gather_channels(hidden_one)
    pre_middle = conv_forward(hidden_full, w_middle, 4)
    second, unused = masked_norm_apply([(pre_middle, inside, norms[2])], [])
    hidden_two = jax.nn.silu(second[0][0]).astype(jnp.bfloat16)
    hidden_two_full = gather_channels(hidden_two)
    pre_expand = jnp.dot(hidden_two_full, w_expand, preferred_element_type=jnp.float32)
    third, unused = masked_norm_apply([(pre_expand, inside, norms[3])], [])
    summed = third[0][0] + leading_part[1][0]
    merged = jax.nn.silu(summed).astype(jnp.bfloat16)
    tables = []
    pooled_list = []
    partial_list = []
    for group, bins in enumerate(BIN_COUNTS):
        rows_in, rows_pick = bin_tables(sizes[:, 0], bins, MAP)
        cols_in, cols_pick = bin_tables(sizes[:, 1], bins, MAP)
        cell_count = (
            jnp.sum(rows_in, axis=2)[:, :, None, None] * jnp.sum(cols_in, axis=2)[:, None, :, None]
        )
        tables.append((rows_in, cols_in, rows_pick, cols_pick, cell_count))
        pooled = (
            jnp.einsum(
                "ikh,ilw,ihwc->iklc",
                rows_in.astype(jnp.bfloat16),
                cols_in.astype(jnp.bfloat16),
                merged,
                preferred_element_type=jnp.float32,
            )
            / cell_count
        )
        pooled = pooled.astype(jnp.bfloat16).reshape(images, bins * bins, -1)
        pooled_list.append(pooled)
        partial_list.append(
            jnp.einsum("ipc,cd->ipd", pooled, w_branch[group], preferred_element_type=jnp.float32)
        )
    branch_pre = lax.psum_scatter(
        jnp.concatenate(partial_list, axis=1).astype(jnp.bfloat16),
        "tensor",
        scatter_dimension=2,
        tiled=True,
    ).astype(jnp.float32)
    branch_items = []
    for group, bins in enumerate(BIN_COUNTS):
        piece = branch_pre[:, BIN_STARTS[group] : BIN_STARTS[group] + bins * bins]
        branch_items.append(
            (piece, jnp.ones(piece.shape[:-1] + (1,), jnp.float32), norms[4 + group])
        )
    fourth, unused = masked_norm_apply(branch_items, [])
    branch_act = jnp.concatenate([jax.nn.silu(kept[0]) for kept in fourth], axis=1).astype(
        jnp.bfloat16
    )
    merged_full, branch_full = (
        lax.all_gather(merged, "tensor", axis=3, tiled=True),
        lax.all_gather(branch_act, "tensor", axis=2, tiled=True),
    )
    joined = spread_bins(merged_full, branch_full, tables, images)
    pre_unite = conv_forward(joined, w_unite, 1)
    fifth, unused = masked_norm_apply([(pre_unite, inside, norms[8])], [])
    united = jax.nn.silu(fifth[0][0]).astype(jnp.bfloat16)
    logit_main, logit_aux = (
        lax.psum_scatter(
            jnp.dot(united, w_classes, preferred_element_type=jnp.float32).astype(jnp.bfloat16),
            "tensor",
            scatter_dimension=1,
            tiled=True,
        ).astype(jnp.float32),
        lax.psum_scatter(
            jnp.dot(aux_act, w_aux_classes, preferred_element_type=jnp.float32).astype(
                jnp.bfloat16
            ),
            "tensor",
            scatter_dimension=1,
            tiled=True,
        ).astype(jnp.float32),
    )
    total_valid = jnp.sum(class_pixel_counts)
    class_weight = total_valid / (NCLS * class_pixel_counts + total_valid)
    loss_weight = jnp.sum(class_pixel_counts * class_weight)
    cell_weight = jnp.sum(labels_hot * class_weight, axis=-1, keepdims=True) * counted
    band_rows = labels.shape[1] // splits
    band_start = lax.axis_index("tensor") * band_rows
    hot_band = lax.dynamic_slice_in_dim(labels_hot, band_start, band_rows, 1)
    weight_band = lax.dynamic_slice_in_dim(cell_weight, band_start, band_rows, 1)
    log_main = jax.nn.log_softmax(logit_main, axis=-1)
    log_aux = jax.nn.log_softmax(logit_aux, axis=-1)
    loss_cells = -jnp.sum(hot_band * (log_main + 0.4 * log_aux), axis=-1, keepdims=True)
    loss_local = jnp.sum(weight_band * loss_cells)
    band_main = (weight_band * (jnp.exp(log_main) - hot_band) / loss_weight).astype(jnp.bfloat16)
    band_aux = (0.4 * weight_band * (jnp.exp(log_aux) - hot_band) / loss_weight).astype(
        jnp.bfloat16
    )
    grad_main, grad_aux = (
        lax.all_gather(band_main, "tensor", axis=1, tiled=True),
        lax.all_gather(band_aux, "tensor", axis=1, tiled=True),
    )
    reduced = {}

    def settle(index, value):
        reduced[index] = value

    settle(6, jnp.einsum("ihwc,ihwk->ck", united, grad_main, preferred_element_type=jnp.float32))
    settle(8, jnp.einsum("ihwc,ihwk->ck", aux_act, grad_aux, preferred_element_type=jnp.float32))
    d_united = jnp.dot(grad_main, w_classes.T, preferred_element_type=jnp.float32) * silu_slope(
        fifth[0][0]
    )
    d_aux = jnp.dot(grad_aux, w_aux_classes.T, preferred_element_type=jnp.float32) * silu_slope(
        leading_part[2][0]
    )
    back_one, sums_one, totals_one = norm_backward([(d_united, fifth[0]), (d_aux, leading_part[2])])
    unite_shift_grad = totals_one[0]
    d_unite_pre = back_one[0].astype(jnp.bfloat16)
    d_aux_pre = back_one[1].astype(jnp.bfloat16)
    settle(5, conv_kernel_back(joined, d_unite_pre, 1))
    d_merged, d_branch = pick_bins(conv_input_back(d_unite_pre, w_unite, 1), C_OUT, tables, images)
    d_merged, d_branch = (
        lax.psum_scatter(
            d_merged.astype(jnp.bfloat16), "tensor", scatter_dimension=3, tiled=True
        ).astype(jnp.float32),
        lax.psum_scatter(
            d_branch.astype(jnp.bfloat16), "tensor", scatter_dimension=2, tiled=True
        ).astype(jnp.float32),
    )
    settle(7, conv_kernel_back(whole, d_aux_pre, 1))
    branch_back = []
    for group, bins in enumerate(BIN_COUNTS):
        piece = d_branch[:, BIN_STARTS[group] : BIN_STARTS[group] + bins * bins]
        branch_back.append((piece * silu_slope(fourth[group][0]), fourth[group]))
    back_two, sums_two, unused = norm_backward(branch_back)
    d_branch_pre = jnp.concatenate(back_two, axis=1).astype(jnp.bfloat16)
    d_branch_full = lax.all_gather(d_branch_pre, "tensor", axis=2, tiled=True)
    branch_grads = []
    for group, bins in enumerate(BIN_COUNTS):
        rows_in, cols_in, rows_pick, cols_pick, cell_count = tables[group]
        piece = d_branch_full[:, BIN_STARTS[group] : BIN_STARTS[group] + bins * bins]
        branch_grads.append(
            jnp.einsum("ipc,ipd->cd", pooled_list[group], piece, preferred_element_type=jnp.float32)
        )
        d_pooled = jnp.dot(piece, w_branch[group].T, preferred_element_type=jnp.float32).reshape(
            images, bins, bins, -1
        )
        d_merged = d_merged + jnp.einsum(
            "ikh,ilw,iklc->ihwc", rows_in, cols_in, d_pooled / cell_count
        )
    settle(4, jnp.stack(branch_grads))
    d_summed = d_merged * silu_slope(summed)
    back_three, sums_three, unused = norm_backward(
        [(d_summed, third[0]), (d_summed, leading_part[1])]
    )
    d_expand_pre = back_three[0].astype(jnp.bfloat16)
    d_short_pre = back_three[1].astype(jnp.bfloat16)
    settle(
        3,
        jnp.einsum(
            "ihwc,ihwd->cd", hidden_two_full, d_expand_pre, preferred_element_type=jnp.float32
        ),
    )
    settle(1, jnp.einsum("ihwc,ihwd->cd", whole, d_short_pre, preferred_element_type=jnp.float32))
    d_two = scatter_channels(jnp.dot(d_expand_pre, w_expand.T, preferred_element_type=jnp.float32))
    back_four, sums_four, unused = norm_backward([(d_two * silu_slope(second[0][0]), second[0])])
    d_middle_pre = back_four[0].astype(jnp.bfloat16)
    settle(2, conv_kernel_back(hidden_full, d_middle_pre, 4))
    d_one = scatter_channels(conv_input_back(d_middle_pre, w_middle, 4))
    back_five, sums_five, unused = norm_backward(
        [(d_one * silu_slope(leading_part[0][0]), leading_part[0])]
    )
    settle(
        0,
        jnp.einsum(
            "ihwc,ihwd->cd",
            whole,
            back_five[0].astype(jnp.bfloat16),
            preferred_element_type=jnp.float32,
        ),
    )
    beta_grads = (
        [sums_five[0], sums_three[2], sums_four[0], sums_three[0]]
        + [sums_two[2 * g] for g in range(4)]
        + [sums_one[0], sums_one[2]]
    )
    gamma_grads = (
        [sums_five[1], sums_three[3], sums_four[1], sums_three[1]]
        + [sums_two[2 * g + 1] for g in range(4)]
        + [sums_one[1], sums_one[3]]
    )
    settle(9, jnp.stack([jnp.concatenate(gamma_grads), jnp.concatenate(beta_grads)]))
    ordered = [reduced[index] for index in range(10)]
    grad_share = lax.psum_scatter(
        jnp.concatenate([part.reshape(owners, -1) for part in ordered], axis=1),
        "batch",
        scatter_dimension=0,
        tiled=True,
    )
    square_all, loss_sum = lax.psum(
        (jnp.sum(grad_share * grad_share), loss_local), ("batch", "tensor")
    )
    grad_norm = jnp.sqrt(square_all)
    clipped = grad_share * jnp.minimum(1.0, 0.05 / (grad_norm + 1e-06))
    new_first = 0.5 * first_moment + 0.5 * clipped
    new_second = 0.5 * squared_mean + 0.5 * clipped * clipped
    keep = 1.0 - 0.5**STEP
    new_params = params - 0.01 * (
        new_first / keep / (jnp.sqrt(new_second / keep) + 1e-08) + 0.01 * params
    )
    new_average = 0.999 * average + 0.001 * new_params
    return (
        new_params,
        new_first,
        new_second,
        new_average,
        new_params.astype(jnp.bfloat16),
        grad_norm,
        loss_sum,
        loss_weight,
        unite_shift_grad,
    )


CELLS = MAP * MAP
EDGE = 104
BATCH = "batch"
TENSOR = "tensor"
GROUP_ROWS = ((0, 1), (1, 5), (5, 14), (14, 50))
BINS = 64
BF = jnp.bfloat16
F32 = jnp.float32
MESH = pl.DeviceIdType.MESH
HALF = 4
OWNERS = 8
SPLITS = 4
MERGED = 4
SLOTS = 5


def scratch_plan():
    plan = dict(
        w_r=((1024, 128), BF),
        w_s=((1024, 512), BF),
        w_m=((4608, 128), BF),
        w_e=((512, 512), BF),
        w_b=((2048, 512), BF),
        w_u=((18432, 128), BF),
        w_own=((4608, 128), BF),
        w_a=((4608, 128), BF),
        w_pair=((1024, 640), BF),
        w_c=((128, 256), BF),
        w_ac=((64, 256), F32),
        gain_in=((OWNERS, 8, 128), F32),
        gain_rows=((40, 128), F32),
        out_a=((576, 128), F32),
        out_c=((16, 256), F32),
        out_ac=((8, 256), F32),
        whole=((SPLITS, CELLS, 256), BF),
        ins=((CELLS, 128), F32),
        col=((CELLS, 128), F32),
        lab=((CELLS, 128), F32),
        table=((BINS, CELLS), F32),
        pool=((BINS, CELLS), BF),
        pick=((BINS, CELLS), BF),
        cells_in=((BINS, 128), F32),
        pad=((9, CELLS + 2 * EDGE, 128), F32),
        grad_pad=((CELLS + 2 * EDGE, 128), F32),
        pre_r=((CELLS, 128), F32),
        pre_s=((CELLS, 512), F32),
        pre_a=((CELLS, 128), F32),
        pre_m=((CELLS, 128), F32),
        pre_e=((CELLS, 512), F32),
        pre_u=((CELLS, 128), F32),
        act_a=((CELLS, 128), BF),
        h1=((SPLITS, CELLS, 128), BF),
        h2=((SPLITS, CELLS, 128), BF),
        joined=((SPLITS, CELLS, 512), BF),
        joined_t=((SPLITS, 512, CELLS), BF),
        pooled=((BINS, 512), BF),
        pool_half=((2, BINS, 256), BF),
        pool_all=((OWNERS, BINS, 256), BF),
        d_bp_all=((OWNERS, SPLITS, BINS, 128), BF),
        part_b=((SPLITS, BINS, 128), BF),
        recv_b=((SPLITS, BINS, 128), BF),
        all_b=((OWNERS, BINS, 128), BF),
        act_b=((SPLITS, OWNERS * BINS, 128), BF),
        pick_t=((CELLS, 128), BF),
        z_cat=((9, 128, 128), BF),
        act_t=((512, OWNERS * BINS), BF),
        zsum=((2, OWNERS * BINS, 128), F32),
        z_send=((OWNERS, 2, BINS, 128), BF),
        z_recv=((OWNERS, 2, BINS, 128), BF),
        united=((CELLS, 128), BF),
        logit_send=((CELLS, 512), BF),
        logit_recv=((SPLITS, 144, 512), BF),
        slope_in=((SPLITS, 144, 512), BF),
        d_f=((CELLS, 128), F32),
        d_f2=((CELLS, 128), F32),
        cat_u=((CELLS, 1152), BF),
        cat_a=((CELLS, 640), BF),
        dz_send=((9, BINS, 128), BF),
        dz_recv=((OWNERS, 2, BINS, 128), BF),
        d_act_send=((SPLITS, OWNERS * BINS, 128), BF),
        d_act_recv=((SPLITS, OWNERS * BINS, 128), BF),
        d_img_send=((OWNERS, BINS, 128), BF),
        d_img_recv=((OWNERS, BINS, 128), BF),
        d_bp=((SPLITS, BINS, 128), BF),
        dm_near=((2, CELLS, 512), BF),
        dm_far=((CELLS, 512), BF),
        d_sum=((CELLS, 512), F32),
        d_e=((CELLS, 512), BF),
        d_s=((CELLS, 512), BF),
        dh_send=((SPLITS, CELLS, 128), BF),
        dh_recv=((2, SPLITS, CELLS, 128), BF),
        d_low=((CELLS, 128), BF),
        end_t=((SPLITS, 8, 128), F32),
    )
    for name, rows in SYNCS.items():
        plan["sync_" + name] = ((OWNERS, rows, 128), F32)
    for name, (rows, lanes, kind) in PARTS.items():
        plan["first_" + name] = ((HALF, rows, lanes), kind)
        plan["second_" + name] = ((HALF - 1, rows, lanes), kind)
    plan["first_u"] = ((HALF, SLOTS, 512, 128), BF)
    plan["second_u"] = ((HALF - 1, SLOTS, 512, 128), BF)
    return plan


SYNCS = dict(one=8, two=8, three=16, five=8, aux=8, b1=8, b2=8, b3=8, b4=16, b5=8, b6=8, end=8)
PARTS = dict(
    r=(128, 128, BF),
    s=(128, 512, BF),
    m=(576, 128, BF),
    e=(64, 512, BF),
    a=(576, 128, BF),
    c=(16, 256, BF),
    ac=(8, 256, F32),
)
SEMAPHORES = 1100
LOADS = (0, 128, 640, 1216, 1472, 2496, 7104, 7712)
LOAD_ORDER = (0, 2, 3, 1, 4, 6, 5)


class Refs:
    pass


def fold(value):
    return value.reshape(-1, 8, value.shape[-1]).sum(0)


def total(value):
    return jnp.sum(value, axis=0, keepdims=True)


def wide(value, times):
    return jnp.concatenate([value] * times, axis=1)


def dot(left, right):
    return jnp.dot(left, right, preferred_element_type=F32)


def dot_nt(left, right):
    return lax.dot_general(left, right, (((1,), (1,)), ((), ())), preferred_element_type=F32)


def dot_tn(left, right):
    return lax.dot_general(left, right, (((0,), (0,)), ((), ())), preferred_element_type=F32)


def loop(count, body):
    def step(k, carry):
        body(k)
        return carry

    lax.fori_loop(0, count, step, 0)


def rows_at(k, block):
    return pl.ds(pl.multiple_of(k * block, block), block)


def step_kernel(names, *refs):
    (
        sizes, lab_in, feat, flat, o_flat, o_shift, o_misc,
    ) = refs[:7]
    v = Refs()
    for name, ref in zip(names, refs[7:]):
        setattr(v, name, ref)
    sems = refs[-1]
    o_u = o_flat.at[2496:7104, :]
    me = lax.axis_index(BATCH)
    t = lax.axis_index(TENSOR)
    partner = me + 1 - 2 * lax.rem(me, 2)
    t_core = t + 1 - 2 * lax.rem(t, 2)
    t_x = lax.rem(t + 2, SPLITS)
    t_diag = lax.rem(t_core + 2, SPLITS)
    taken = [0]

    def take(count):
        start = taken[0]
        taken[0] = start + count
        assert taken[0] <= SEMAPHORES
        return start

    def far_peer(base, step):
        return lax.rem(base + 2 * step, OWNERS)

    def remote(src, dst, send, recv, device):
        return pltpu.make_async_remote_copy(
            src_ref=src,
            dst_ref=dst,
            send_sem=sems.at[send],
            recv_sem=sems.at[recv],
            device_id=device,
            device_id_type=MESH,
        )

    def mix(*lists):
        for turn in range(max(len(items) for items in lists)):
            for items in lists:
                if turn < len(items):
                    items[turn]()

    load_at = take(len(LOADS))

    def load(index):
        at = pl.ds(LOADS[index], LOADS[index + 1] - LOADS[index])
        return pltpu.make_async_copy(flat.at[at, :], o_flat.at[at, :], sems.at[load_at + index])

    for index in LOAD_ORDER:
        load(index).start()
    v.pool_all[...] = jnp.zeros((OWNERS, BINS, 256), BF)
    v.d_bp_all[...] = jnp.zeros((OWNERS, SPLITS, BINS, 128), BF)
    barrier = pltpu.get_barrier_semaphore()
    for k in range(1, OWNERS):
        pl.semaphore_signal(
            barrier, inc=1, device_id={BATCH: lax.rem(me + k, OWNERS)}, device_id_type=MESH
        )
    for k in range(1, SPLITS):
        pl.semaphore_signal(
            barrier, inc=1, device_id={TENSOR: lax.rem(t + k, SPLITS)}, device_id_type=MESH
        )
    pl.semaphore_wait(barrier, OWNERS + SPLITS - 2)

    class Gather:
        def __init__(self, full, rows, skip=0, step=None, piece=None):
            self.full, self.rows, self.piece = full, rows, piece
            self.skip, self.part = skip, step or rows
            self.near_s, self.far_s, self.pass_s = take(1), take(HALF), take(HALF)
            self.recv, self.keep = take(OWNERS), take(1)

        def at(self, owner):
            if self.rows is None:
                return self.full.at[owner]
            start = pl.multiple_of(owner * self.rows + self.skip, self.part)
            return self.full.at[pl.ds(start, self.part), :]

        def source(self):
            return self.at(me) if self.piece is None else self.piece

        def local(self):
            return pltpu.make_async_copy(self.piece, self.at(me), sems.at[self.keep])

        def near(self):
            return remote(
                self.source(), self.at(me), self.near_s, self.recv + me, {BATCH: partner}
            )

        def far(self, step):
            return remote(
                self.source(),
                self.at(me),
                self.far_s + step,
                self.recv + me,
                {BATCH: far_peer(me, step)},
            )

        def passed(self, step, base):
            source = far_peer(base, step)
            return remote(
                self.at(source),
                self.at(source),
                self.pass_s + step,
                self.recv + source,
                {BATCH: partner},
            )

        def fars(self):
            def go(step):
                if step == 1 and self.piece is not None:
                    self.local().start()
                self.far(step).start()

            return [functools.partial(go, step) for step in range(1, HALF)]

        def nears(self):
            return [lambda: self.near().start()]

        def passes(self):
            def go(step):
                self.passed(step, me).wait_recv()
                self.passed(step, me).start()

            return [functools.partial(go, step) for step in range(1, HALF)]

        def finish(self):
            for step in range(HALF):
                self.passed(step, partner).wait_recv()
            if self.piece is not None:
                self.local().wait()
            self.near().wait_send()
            for step in range(1, HALF):
                self.far(step).wait_send()

        def drain(self):
            for step in range(1, HALF):
                self.passed(step, me).wait_send()

    g_gain = Gather(v.gain_in, None, piece=flat.at[7704:7712, :])
    g_r = Gather(v.w_r, 128)
    g_s = Gather(v.w_s, 128)
    g_a = Gather(v.w_a, 576)
    g_m = Gather(v.w_m, 576)
    g_e = Gather(v.w_e, 64)
    g_b0 = Gather(v.w_b, 256, 0, 128)
    g_b1 = Gather(v.w_b, 256, 128, 128)
    g_c = Gather(v.w_c, 16)
    g_ac = Gather(v.w_ac, 8)

    def block_of(owner, slot):
        return 8 if slot == SLOTS - 1 else lax.rem(slot - owner + 8, 8)

    def merged_rows(owner, slot):
        block = owner * 9 + block_of(owner, slot)
        index = lax.div(block, 8) * MERGED + lax.rem(block, 8)
        return pl.ds(pl.multiple_of(index * 512, 512), 512)

    def has(owner, slot, body):
        if slot == SLOTS - 1:
            pl.when(owner < MERGED)(body)
        else:
            body()

    class GatherUnite:
        def __init__(self):
            self.near_s, self.far_s, self.pass_s = (
                take(SLOTS),
                take(SLOTS * HALF),
                take(SLOTS * HALF),
            )
            self.recv, self.keep = take(SLOTS * OWNERS), take(SLOTS)

        def source(self, slot):
            return v.w_own.at[rows_at(block_of(me, slot), 512), :]

        def full(self, owner, slot):
            return v.w_u.at[merged_rows(owner, slot), :]

        def local(self, slot):
            return pltpu.make_async_copy(
                self.source(slot), self.full(me, slot), sems.at[self.keep + slot]
            )

        def near(self, slot):
            return remote(
                self.source(slot),
                self.full(me, slot),
                self.near_s + slot,
                self.recv + me * SLOTS + slot,
                {BATCH: partner},
            )

        def far(self, step, slot):
            return remote(
                self.source(slot),
                self.full(me, slot),
                self.far_s + step * SLOTS + slot,
                self.recv + me * SLOTS + slot,
                {BATCH: far_peer(me, step)},
            )

        def passed(self, step, slot, base):
            source = far_peer(base, step)
            return remote(
                self.full(source, slot),
                self.full(source, slot),
                self.pass_s + step * SLOTS + slot,
                self.recv + source * SLOTS + slot,
                {BATCH: partner},
            )

        def fars(self, slot):
            def go(step):
                if step == 1:
                    self.local(slot).start()
                self.far(step, slot).start()

            return [
                functools.partial(has, me, slot, functools.partial(go, step))
                for step in range(1, HALF)
            ]

        def nears(self, slot):
            return [lambda: has(me, slot, lambda: self.near(slot).start())]

        def passes(self, slot):
            def go(step):
                self.passed(step, slot, me).wait_recv()
                self.passed(step, slot, me).start()

            return [
                functools.partial(has, far_peer(me, step), slot, functools.partial(go, step))
                for step in range(1, HALF)
            ]

        def finish(self):
            for slot in range(SLOTS):
                for step in range(HALF):
                    has(
                        far_peer(partner, step),
                        slot,
                        lambda step=step, slot=slot: self.passed(step, slot, partner).wait_recv(),
                    )

                def end(slot=slot):
                    self.local(slot).wait()
                    self.near(slot).wait_send()
                    for step in range(1, HALF):
                        self.far(step, slot).wait_send()

                has(me, slot, end)

        def drain(self):
            for slot in range(SLOTS):
                for step in range(1, HALF):
                    has(
                        far_peer(me, step),
                        slot,
                        lambda step=step, slot=slot: self.passed(step, slot, me).wait_send(),
                    )

    g_u = GatherUnite()

    class Sync:
        def __init__(self, buf):
            self.buf = buf
            self.send, self.recv = take(OWNERS), take(OWNERS)

        def copy(self, k, slot):
            return remote(
                self.buf.at[slot],
                self.buf.at[slot],
                self.send + k,
                self.recv + slot,
                {BATCH: lax.rem(me + k, OWNERS)},
            )

        def start(self, rows):
            for index, row in enumerate(rows):
                self.buf[me, index : index + 1, :] = row
            for index in range(len(rows), self.buf.shape[1]):
                self.buf[me, index : index + 1, :] = jnp.zeros((1, 128), F32)
            for k in range(1, OWNERS):
                self.copy(k, me).start()

        def wait(self):
            for k in range(1, OWNERS):
                self.copy(k, lax.rem(me + k, OWNERS)).wait_recv()
            for k in range(1, OWNERS):
                self.copy(k, me).wait_send()
            value = self.buf[0]
            for slot in range(1, OWNERS):
                value = value + self.buf[slot]
            return value

    class ToGroup:
        def __init__(self, part, into):
            self.part, self.into = part, into
            self.send, self.recv = take(OWNERS), take(OWNERS)

        def each(self, k, owner, slot, act):
            for rows, fits_ in ((16, owner < 6), (BINS, owner >= 6)):

                def go(rows=rows):
                    act(
                        remote(
                            self.part(owner, rows),
                            self.into(slot, rows),
                            self.send + k,
                            self.recv + slot,
                            {BATCH: lax.rem(me + k, OWNERS)},
                        )
                    )

                pl.when(fits_)(go)

        def start(self):
            for k in range(1, OWNERS):
                self.each(k, lax.rem(me + k, OWNERS), me, lambda c: c.start())

        def wait(self):
            for k in range(1, OWNERS):
                self.each(k, me, lax.rem(me + k, OWNERS), lambda c: c.wait_recv())
            for k in range(1, OWNERS):
                self.each(k, lax.rem(me + k, OWNERS), me, lambda c: c.wait_send())

    class Spread:

        def __init__(self, buf, lanes_=None):
            self.buf, self.lanes = buf, lanes_
            self.send, self.recv = take(SPLITS), take(SPLITS)

        def view(self, slot):
            return self.buf.at[slot] if self.lanes is None else self.buf.at[slot, :, self.lanes]

        def copy(self, k, slot):
            return remote(
                self.view(slot),
                self.view(slot),
                self.send + k,
                self.recv + slot,
                {TENSOR: lax.rem(t + k, SPLITS)},
            )

        def start(self):
            for k in range(1, SPLITS):
                self.copy(k, t).start()

        def wait(self):
            for k in range(1, SPLITS):
                self.copy(k, lax.rem(t + k, SPLITS)).wait_recv()
            for k in range(1, SPLITS):
                self.copy(k, t).wait_send()

    class Exchange:

        def __init__(self, axis, count, part, into):
            self.axis, self.count, self.part, self.into = axis, count, part, into
            self.mine = me if axis == BATCH else t
            self.send, self.recv = take(count), take(count)

        def copy(self, k, slot):
            other = lax.rem(self.mine + k, self.count)
            return remote(
                self.part(other),
                self.into(slot),
                self.send + k,
                self.recv + slot,
                {self.axis: other},
            )

        def start(self):
            for k in range(1, self.count):
                self.copy(k, self.mine).start()

        def wait(self):
            for k in range(1, self.count):
                self.copy(k, lax.rem(self.mine + k, self.count)).wait_recv()
            for k in range(1, self.count):
                self.copy(k, self.mine).wait_send()

    feat_keep = take(1)
    feat_local = pltpu.make_async_copy(feat, v.whole.at[t], sems.at[feat_keep])
    feat_s, feat_r = take(3), take(SPLITS)

    def feat_copy(k, slot, device):
        source = feat if k < 2 else v.whole.at[slot]
        return remote(source, v.whole.at[slot], feat_s + k, feat_r + slot, {TENSOR: device})

    def wide_rows(into, rows, low):
        for k in range(4):
            value = o_flat[pl.ds(low + k, rows, stride=4), :]
            into[rows_at(me, rows), k * 128 : k * 128 + 128] = value.astype(BF)

    load(0).wait()
    v.w_r[rows_at(me, 128), :] = o_flat[0:128, :].astype(BF)
    mix(g_r.nears() + g_gain.nears(), g_r.fars() + g_gain.fars())
    feat_local.start()
    feat_copy(0, t, t_x).start()
    feat_copy(1, t, t_core).start()
    load(2).wait()
    v.w_m[rows_at(me, 576), :] = o_flat[640:1216, :].astype(BF)
    load(3).wait()
    wide_rows(v.w_e, 64, 1216)
    mix(g_m.nears() + g_e.nears(), g_m.fars() + g_e.fars())
    lane = lax.broadcasted_iota(jnp.int32, (1, 128), 1)

    def roll(value, shift):
        return pltpu.roll(value, shift % 128, 1) if shift % 128 else value

    high, across = sizes[0, 0], sizes[0, 1]
    place = lax.broadcasted_iota(jnp.int32, (CELLS, 128), 0).astype(F32)
    row_of = jnp.floor((place + 0.5) / MAP)
    col_of = place - MAP * row_of
    within = (row_of < high.astype(F32)) & (col_of < across.astype(F32))
    v.ins[...] = jnp.where(within, 1.0, 0.0)
    v.col[...] = col_of
    v.lab[...] = jnp.where(within, lab_in[...], -1.0)
    v.table[...] = jnp.zeros((BINS, CELLS), F32)
    lane_place = lax.broadcasted_iota(jnp.int32, (1, CELLS), 1).astype(F32)
    lane_row = jnp.floor((lane_place + 0.5) / MAP)
    lane_col = lane_place - MAP * lane_row

    def ranges(extent, bins, where):
        inside, chosen, counts = [], [], []
        for k in range(bins):
            low = lax.div(k * extent, bins)
            top = lax.div((k + 1) * extent + (bins - 1), bins)
            member = (where >= low.astype(F32)) & (where < top.astype(F32))
            inside.append(jnp.where(member, 1.0, 0.0))
            picked = where * bins >= (k * extent).astype(F32)
            if k < bins - 1:
                picked = picked & (where * bins < ((k + 1) * extent).astype(F32))
            chosen.append(jnp.where(picked, 1.0, 0.0))
            counts.append(top - low)
        return inside, chosen, counts

    picks = []
    v.cells_in[...] = jnp.ones((BINS, 128), F32)
    for group, bins in enumerate(BIN_COUNTS):
        r_in, r_pick, r_count = ranges(high, bins, lane_row)
        c_in, c_pick, c_count = ranges(across, bins, lane_col)
        for a in range(bins):
            for b in range(bins):
                spot = BIN_STARTS[group] + a * bins + b
                v.table[spot : spot + 1, :] = r_in[a] * c_in[b]
                v.cells_in[spot : spot + 1, :] = jnp.full(
                    (1, 128), (r_count[a] * c_count[b]).astype(F32)
                )
                picks.append((spot, r_pick[a] * c_pick[b]))
    v.pool[...] = v.table[...].astype(BF)
    for spot, value in picks:
        v.table[spot : spot + 1, :] = value
    v.pick[...] = v.table[...].astype(BF)
    v.pick_t[...] = jnp.concatenate([v.pick[...], v.pick[...]], axis=0).T
    zeros_edge = jnp.zeros((EDGE, 128), F32)
    for tap in range(9):
        v.pad[tap, 0:EDGE, :] = zeros_edge
        v.pad[tap, EDGE + CELLS :, :] = zeros_edge
    v.grad_pad[0:EDGE, :] = zeros_edge
    v.grad_pad[EDGE + CELLS :, :] = zeros_edge
    lanes = lax.broadcasted_iota(jnp.int32, (1, 256), 1).astype(F32)
    counts = jnp.zeros((8, 256), F32)
    for k in range(0, CELLS, 96):
        counts = counts + fold(
            jnp.where(wide(v.lab[k : k + 96, :], 2) == lanes, 1.0, 0.0)
        )
    class_local = total(counts)
    cells_local = jnp.full((1, 128), (high * across).astype(F32))
    left_half = lax.broadcasted_iota(jnp.int32, (64, 128), 1) < 64

    mix(g_r.passes() + g_gain.passes())
    feat_copy(0, t_x, t_x).wait_recv()
    feat_copy(2, t_x, t_core).start()
    load(1).wait()
    wide_rows(v.w_s, 128, 128)
    load(4).wait()
    wide_rows(v.w_b, 256, 1472)
    load(6).wait()
    before = pltpu.roll(o_flat[7122:7698, :], 32, 1)
    after = pltpu.roll(o_flat[7123:7699, :], 32, 1)
    v.w_a[rows_at(me, 576), :] = jnp.where(lane < 32, before, after).astype(BF)

    def class_rows(count, base, into):
        for row in range(count):
            first, shift = divmod(base + NCLS * row, 128)
            three = [
                roll(o_flat[7104 + first + k : 7105 + first + k, :], 128 - shift) for k in range(3)
            ]
            into[row : row + 1, :128] = jnp.where(lane < 128 - shift, three[0], three[1])
            high_half = jnp.where(lane < 128 - shift, three[1], three[2])
            into[row : row + 1, 128:] = jnp.where(lane < NCLS - 128, high_half, 0.0)

    class_rows(16, 0, v.out_c)
    class_rows(8, 76128, v.out_ac)
    v.w_c[rows_at(me, 16), :] = v.out_c[...].astype(BF)
    v.w_ac[rows_at(me, 8), :] = v.out_ac[...].astype(BF).astype(F32)
    load(5).wait()

    def own_rows(j):
        at = pl.ds(pl.multiple_of(2496 + 512 * j, 64), 512)
        v.w_own[rows_at(j, 512), :] = o_flat[at, :].astype(BF)

    loop(9, own_rows)
    for item in (g_gain, g_r):
        item.finish()
    feat_local.wait()
    feat_copy(1, t_core, t_core).wait_recv()
    feat_copy(2, t_diag, t_core).wait_recv()
    feat_copy(0, t, t_x).wait_send()
    feat_copy(1, t, t_core).wait_send()
    feat_copy(2, t_x, t_core).wait_send()
    gain_of = [None] * 33
    for owner in range(OWNERS):
        start = 496 * (owner % 4) - 16
        first, shift = start // 128, start % 128
        for k in range(4):
            value = v.gain_in[owner, 4 + k : 5 + k, :].astype(BF).astype(F32)
            if k == 0:
                value = jnp.where(lane < 16, 0.0, value)
            value = roll(value, shift)
            spot = 16 * (owner // 4) + first + k
            for where, part in (
                (spot, jnp.where(lane >= shift, value, 0.0)),
                (spot + 1, jnp.where(lane < shift, value, 0.0)),
            ):
                gain_of[where] = part if gain_of[where] is None else gain_of[where] + part

    def gamma(row, width=1):
        return jnp.concatenate([gain_of[row + k] for k in range(width)], axis=1)

    def beta(row, width=1):
        return gamma(16 + row, width)

    def whole_feat():
        return jnp.concatenate([v.whole[k] for k in range(SPLITS)], axis=1)

    v.pre_r[...] = dot(whole_feat(), v.w_r[...])
    def offset(tap, spacing):
        return ((tap // 3 - 1) * MAP + (tap % 3 - 1)) * spacing

    def col_mask(at, right):
        where = v.col[at, :] + float(right)
        return jnp.where((where >= 0.0) & (where < float(MAP)), 1.0, 0.0)

    BLOCK = 72

    def shift_sum(taps, spacing, at, slot_of):
        out = None
        for b in (-1, 0, 1):
            part = None
            for tap in taps:
                if tap % 3 - 1 != b:
                    continue
                start = EDGE + at + offset(tap, spacing)
                value = v.pad[slot_of(tap), start : start + BLOCK, :]
                part = value if part is None else part + value
            if part is None:
                continue
            if b:
                part = part * col_mask(slice(at, at + BLOCK), b * spacing)
            out = part if out is None else out + part
        return out

    def masked_sums(ref):
        width = ref.shape[1]

        def step(k, carry):
            at = rows_at(k, 96)
            value = ref[at, :]
            kept = value * (v.ins[at, :] if width == 128 else wide(v.ins[at, :], width // 128))
            return (carry[0] + fold(kept), carry[1] + fold(kept * value))

        zero = jnp.zeros((8, width), F32)
        sums = lax.fori_loop(0, 6, step, (zero, zero))
        return total(sums[0]), total(sums[1])

    def split_rows(value):
        return [value[:, k : k + 128] for k in range(0, value.shape[1], 128)]

    def join_rows(value, row, count):
        return jnp.concatenate([value[row + k : row + k + 1] for k in range(count)], axis=1)

    def moments(first, second, count):
        mean = first / count
        return mean, lax.rsqrt(second / count - mean * mean + 1e-05)

    sync = Sync(v.sync_one)
    r1, r2 = masked_sums(v.pre_r)
    sync.start([r1, r2, cells_local] + split_rows(class_local))
    mix(g_m.passes() + g_e.passes(), g_s.fars())
    sums = sync.wait()
    count = sums[2:3]
    count4 = wide(count, 4)
    norm_r = moments(sums[0:1], sums[1:2], count)
    class_count = join_rows(sums, 3, 2)

    def normed(ref, at, norm):
        return (ref[at, :] - norm[0]) * norm[1]

    spread_1 = Spread(v.h1)

    def make_h1(k):
        at = rows_at(k, 96)
        v.h1[t, at, :] = jax.nn.silu(gamma(0) * normed(v.pre_r, at, norm_r) + beta(0)).astype(BF)

    loop(6, make_h1)
    spread_1.start()
    mix(g_s.nears(), g_b0.fars())
    g_m.finish()
    spread_1.wait()

    def full_h(ref):
        return jnp.concatenate([ref[k] for k in range(SPLITS)], axis=1)

    def w_middle(tap):
        return v.w_m[rows_at(tap, 512), :]

    def middle_pair(p):
        both = jnp.concatenate([w_middle(2 * p), w_middle(2 * p + 1)], axis=1)
        value = dot(full_h(v.h1), both)
        v.pad[2 * p, EDGE : EDGE + CELLS, :] = value[:, :128]
        v.pad[2 * p + 1, EDGE : EDGE + CELLS, :] = value[:, 128:]

    loop(4, middle_pair)
    v.pad[8, EDGE : EDGE + CELLS, :] = dot(full_h(v.h1), w_middle(8))
    for at in range(0, CELLS, BLOCK):
        v.pre_m[at : at + BLOCK, :] = shift_sum(range(9), 4, at, lambda tap: tap)
    sync = Sync(v.sync_two)
    sync.start(list(masked_sums(v.pre_m)))
    mix(g_s.passes() + g_b0.nears(), g_b1.fars())
    sums = sync.wait()
    norm_m = moments(sums[0:1], sums[1:2], count)
    spread_2 = Spread(v.h2)

    def make_h2(k):
        at = rows_at(k, 96)
        v.h2[t, at, :] = jax.nn.silu(gamma(5) * normed(v.pre_m, at, norm_m) + beta(5)).astype(BF)

    loop(6, make_h2)
    spread_2.start()
    mix(g_b0.passes() + g_b1.nears(), g_u.fars(0))
    g_e.finish()
    g_s.finish()
    for k in range(0, 512, 256):
        v.pre_s[:, k : k + 256] = dot(whole_feat(), v.w_s[:, k : k + 256])
    s1, s2 = masked_sums(v.pre_s)
    spread_2.wait()
    for k in range(0, 512, 256):
        v.pre_e[:, k : k + 256] = dot(full_h(v.h2), v.w_e[:, k : k + 256])
    sync = Sync(v.sync_three)
    e1, e2 = masked_sums(v.pre_e)
    sync.start(split_rows(e1) + split_rows(e2) + split_rows(s1) + split_rows(s2))
    mix(g_b1.passes() + g_u.nears(0), g_u.fars(1))
    mix(g_c.nears() + g_ac.nears(), g_c.fars() + g_ac.fars())
    sums = sync.wait()
    norm_e = moments(join_rows(sums, 0, 4), join_rows(sums, 4, 4), count4)
    norm_s = moments(join_rows(sums, 8, 4), join_rows(sums, 12, 4), count4)

    def summed(at):
        return (
            gamma(6, 4) * normed(v.pre_e, at, norm_e)
            + beta(6, 4)
            + gamma(1, 4) * normed(v.pre_s, at, norm_s)
            + beta(1, 4)
        )

    def make_merged(k):
        at = rows_at(k, 48)
        v.joined[t, at, :] = jax.nn.silu(summed(at)).astype(BF)

    loop(12, make_merged)

    j_send, j_recv = take(3), take(SPLITS)

    def joined_copy(k, slot, device):
        return remote(
            v.joined.at[slot], v.joined.at[slot], j_send + k, j_recv + slot, {TENSOR: device}
        )

    joined_copy(0, t, t_x).start()
    joined_copy(1, t, t_core).start()

    pool_move = ToGroup(
        lambda owner, rows: v.pool_half.at[lax.rem(owner, 2), 0:rows, :],
        lambda slot, rows: v.pool_all.at[slot, 0:rows, :],
    )
    bin_row = lax.broadcasted_iota(jnp.int32, (BINS, 1), 0)

    def group_mask(group, shape=None):
        low, top = GROUP_ROWS[group]
        kept = jnp.where((bin_row >= low) & (bin_row < top), 1.0, 0.0)
        return kept if shape is None else jnp.broadcast_to(kept, shape)

    cells_in = wide(v.cells_in[...], 4)
    pooled = dot(v.pool[...], v.joined[t]) / cells_in
    v.pooled[...] = pooled.astype(BF)
    for k in range(2):
        v.pool_half[k] = v.pooled[:, k * 256 : k * 256 + 256]
    v.pool_all[me] = v.pool_half[lax.rem(me, 2)]
    g_b0.finish()
    g_b1.finish()
    part = jnp.zeros((BINS, 512), F32)
    for group in range(4):
        rows = (v.pooled[...].astype(F32) * group_mask(group)).astype(BF)
        part = part + dot(rows, v.w_b[group * 512 : group * 512 + 512, :])
    for k in range(SPLITS):
        v.part_b[k] = part[:, k * 128 : k * 128 + 128].astype(BF)
    v.recv_b[t] = v.part_b[t]
    ex = Exchange(TENSOR, SPLITS, lambda o: v.part_b.at[o], lambda s: v.recv_b.at[s])
    ex.start()
    mix(g_u.passes(0) + g_u.nears(1), g_u.fars(2))
    joined_copy(0, t_x, t_x).wait_recv()
    joined_copy(2, t_x, t_core).start()
    ex.wait()
    own_b = v.recv_b[0].astype(F32)
    for k in range(1, SPLITS):
        own_b = own_b + v.recv_b[k].astype(F32)
    v.all_b[me] = own_b.astype(BF)
    ex = Exchange(BATCH, OWNERS, lambda o: v.all_b.at[me], lambda s: v.all_b.at[s])
    ex.start()
    mix(g_u.passes(1) + g_u.nears(2), g_u.fars(3))
    ex.wait()
    all_b = [v.all_b[k].astype(F32) for k in range(OWNERS)]
    sum_b, square_b = all_b[0], all_b[0] * all_b[0]
    for k in range(1, OWNERS):
        sum_b = sum_b + all_b[k]
        square_b = square_b + all_b[k] * all_b[k]
    mean_b = jnp.zeros((BINS, 128), F32)
    scale_b = jnp.zeros((BINS, 128), F32)
    gamma_b = jnp.zeros((BINS, 128), F32)
    beta_b = jnp.zeros((BINS, 128), F32)
    count_b = jnp.zeros((BINS, 1), F32)
    for group, bins in enumerate(BIN_COUNTS):
        kept = group_mask(group)
        size = float(OWNERS * bins * bins)
        mean, scaling = moments(total(sum_b * kept), total(square_b * kept), size)
        mean_b = mean_b + kept * mean
        scale_b = scale_b + kept * scaling
        gamma_b = gamma_b + kept * gamma(10 + group)
        beta_b = beta_b + kept * beta(10 + group)
        count_b = count_b + kept / size
    spread_b = Spread(v.act_b)
    for k in range(OWNERS):
        out = gamma_b * ((all_b[k] - mean_b) * scale_b) + beta_b
        v.act_b[t, k * BINS : k * BINS + BINS, :] = jax.nn.silu(out).astype(BF)
    spread_b.start()
    mix(g_u.passes(2) + g_u.nears(3), g_u.fars(4))
    spread_b.wait()
    row_512 = lax.broadcasted_iota(jnp.int32, (OWNERS * BINS, 1), 0) & (BINS - 1)
    group_id = jnp.where(
        row_512 < 1, 0, jnp.where(row_512 < 5, 1, jnp.where(row_512 < 14, 2, jnp.where(row_512 < 50, 3, 9)))
    )

    def full_act():
        return jnp.concatenate([v.act_b[k] for k in range(SPLITS)], axis=1)

    v.zsum[...] = jnp.zeros((2, OWNERS * BINS, 128), F32)

    def own_branch(j, body):
        chunk = lax.rem(me + j, 8)
        pl.when(chunk >= MERGED)(lambda: body(chunk - MERGED, lax.div(me + j, 8)))

    def make_z(j):
        def body(group, side):
            kept = jnp.where(group_id == group, 1.0, 0.0)
            v.zsum[side] = v.zsum[side] + kept * dot(full_act(), v.w_own[rows_at(j, 512), :])

        own_branch(j, body)

    loop(9, make_z)
    for k in range(OWNERS):
        for side in range(2):
            v.z_send[k, side] = v.zsum[side, k * BINS : k * BINS + BINS, :].astype(BF)
    v.z_recv[me] = v.z_send[me]
    ex = Exchange(BATCH, OWNERS, lambda o: v.z_send.at[o], lambda s: v.z_recv.at[s])
    ex.start()
    mix(g_u.passes(3) + g_u.nears(4))
    v.act_t[...] = full_act().T
    joined_copy(1, t_core, t_core).wait_recv()
    joined_copy(2, t_diag, t_core).wait_recv()
    for k in range(SPLITS):
        v.joined_t[k] = v.joined[k].T
    mix(g_u.passes(4) + g_c.passes() + g_ac.passes())
    ex.wait()
    g_u.finish()

    def tap_z(tap):
        if tap == 0:
            return v.z_recv[0, 0].astype(F32)
        if tap == 8:
            return v.z_recv[7, 1].astype(F32)
        return v.z_recv[tap, 0].astype(F32) + v.z_recv[tap - 1, 1].astype(F32)

    for tap in range(9):
        z = tap_z(tap)
        high_z = z.astype(BF)
        v.z_cat[tap, :BINS, :] = high_z
        v.z_cat[tap, BINS:, :] = (z - high_z.astype(F32)).astype(BF)

    def full_joined():
        return jnp.concatenate([v.joined[k] for k in range(SPLITS)] + [v.pick_t[...]], axis=1)

    def w_tap(tap):
        return jnp.concatenate([v.w_u[rows_at(tap, 2048), :], v.z_cat[tap]], axis=0)

    def unite_pair(p):
        value = dot(full_joined(), jnp.concatenate([w_tap(2 * p), w_tap(2 * p + 1)], axis=1))
        v.pad[2 * p, EDGE : EDGE + CELLS, :] = value[:, :128]
        v.pad[2 * p + 1, EDGE : EDGE + CELLS, :] = value[:, 128:]

    loop(4, unite_pair)
    v.pad[8, EDGE : EDGE + CELLS, :] = dot(full_joined(), w_tap(8))
    for at in range(0, CELLS, BLOCK):
        v.pre_u[at : at + BLOCK, :] = shift_sum(range(9), 1, at, lambda tap: tap)
    sync = Sync(v.sync_five)
    sync.start(list(masked_sums(v.pre_u)))
    pool_move.start()
    mix(g_a.nears(), g_a.fars())
    for item in (g_c, g_ac):
        item.finish()
    for item in (g_gain, g_r, g_s, g_m, g_e, g_b0, g_b1, g_c, g_ac, g_u):
        item.drain()
    joined_copy(0, t, t_x).wait_send()
    joined_copy(1, t, t_core).wait_send()
    joined_copy(2, t_x, t_core).wait_send()
    w_ac = jnp.concatenate([v.w_ac[...], jnp.zeros((64, 256), F32)], axis=0).astype(BF)
    sums = sync.wait()
    norm_u = moments(sums[0:1], sums[1:2], count)

    def make_u(k):
        at = rows_at(k, 96)
        v.united[at, :] = jax.nn.silu(gamma(14) * normed(v.pre_u, at, norm_u) + beta(14)).astype(BF)

    loop(6, make_u)
    class Band:
        def __init__(self, at):
            self.at = at
            self.ex = Exchange(
                TENSOR,
                SPLITS,
                lambda o: v.logit_send.at[rows_at(o, 144), at],
                lambda s: v.logit_recv.at[s, :, at],
            )
            self.back = Spread(v.slope_in, at)

        def start(self, value):
            v.logit_send[:, self.at] = value.astype(BF)
            self.ex.start()
            v.logit_recv[t, :, self.at] = v.logit_send[rows_at(t, 144), self.at]

        def finish(self, factor):
            self.ex.wait()
            logits = v.logit_recv[0, :, self.at].astype(F32)
            for k in range(1, SPLITS):
                logits = logits + v.logit_recv[k, :, self.at].astype(F32)
            class_weight, loss_weight = class_weights()
            hot = jnp.where(wide(v.lab[rows_at(t, 144), :], 2) == lanes, 1.0, 0.0)
            cell_weight = factor * jnp.sum(hot * class_weight, axis=1, keepdims=True)
            value = jnp.where(lanes < float(NCLS), logits, -1e30)
            value = value - jnp.max(value, axis=1, keepdims=True)
            powers = jnp.exp(value)
            mass = jnp.sum(powers, axis=1, keepdims=True)
            loss_rows = total(fold(-cell_weight * hot * (value - jnp.log(mass))))
            grad = cell_weight * (powers / mass - hot) / loss_weight
            v.slope_in[t, :, self.at] = grad.astype(BF)
            self.back.start()
            return loss_rows[:, :128] + loss_rows[:, 128:]

        def grad(self):
            self.back.wait()
            return v.slope_in[:, :, self.at].reshape(CELLS, 256)

    def class_weights():
        total_valid = jnp.sum(class_count, axis=1, keepdims=True)
        weight = total_valid / (NCLS * class_count + total_valid)
        whole = jnp.sum(class_count * weight, axis=1, keepdims=True)
        return jnp.where(lanes < float(NCLS), weight, 0.0), whole

    main_head, aux_head = Band(slice(0, 256)), Band(slice(256, 512))
    main_head.start(dot(v.united[...], v.w_c[...]))
    mix(g_a.passes())
    o_misc[1:2, :] = main_head.finish(1.0)

    g_a.finish()
    g_a.drain()

    def unpack(chunk):
        for pair in range(5):
            even = v.w_a[rows_at(2 * pair * 8 + chunk, 64), :].astype(F32)
            if pair < 4:
                odd = v.w_a[rows_at((2 * pair + 1) * 8 + chunk, 64), :].astype(F32)
            else:
                odd = jnp.zeros((64, 128), F32)
            low = jnp.where(left_half, even, pltpu.roll(odd, 64, 1))
            top = jnp.where(left_half, pltpu.roll(even, 64, 1), odd)
            v.pad[pair, pl.ds(EDGE, 64, stride=2), :] = low
            v.pad[pair, pl.ds(EDGE + 1, 64, stride=2), :] = top
            both = v.pad[pair, EDGE : EDGE + 128, :]
            v.w_pair[rows_at(chunk, 128), pair * 128 : pair * 128 + 128] = both.astype(BF)

    loop(8, unpack)

    for pair in (0, 2):
        value = dot(whole_feat(), v.w_pair[:, pair * 128 : pair * 128 + 256])
        v.pad[pair, EDGE : EDGE + CELLS, :] = value[:, :128]
        v.pad[pair + 1, EDGE : EDGE + CELLS, :] = value[:, 128:]
    v.pad[4, EDGE : EDGE + CELLS, :] = dot(whole_feat(), v.w_pair[:, 512:640])

    left_wide = lax.broadcasted_iota(jnp.int32, (BLOCK, 128), 1) < 64
    for at in range(0, CELLS, BLOCK):
        even = shift_sum((0, 2, 4, 6, 8), 1, at, lambda tap: tap // 2)
        odd = shift_sum((1, 3, 5, 7), 1, at, lambda tap: tap // 2)
        v.pre_a[at : at + BLOCK, :] = jnp.where(left_wide, even + pltpu.roll(odd, 64, 1), 0.0)

    sync_a = Sync(v.sync_aux)
    sync_a.start(list(masked_sums(v.pre_a)))
    g_main = main_head.grad()
    v.d_f[...] = dot_nt(g_main, v.w_c[...])

    def slope(value):
        gate = jax.nn.sigmoid(value)
        return gate * (1.0 + value * (1.0 - gate))

    def through_silu(ref, pre, norm, row):
        def step(k, carry):
            at = rows_at(k, 96)
            unit = normed(pre, at, norm)
            value = ref[at, :] * slope(gamma(row) * unit + beta(row))
            ref[at, :] = value
            return (carry[0] + fold(value), carry[1] + fold(value * unit))

        zero = jnp.zeros((8, 128), F32)
        sums = lax.fori_loop(0, 6, step, (zero, zero))
        return [total(sums[0]), total(sums[1])]

    def back_norm(value, unit, mask, norm, gain, first, second, size):
        inner = value - mask * (first + unit * second) / size
        return gain * norm[1] * inner

    gain_grads = {}
    sync = Sync(v.sync_b1)
    sync.start(through_silu(v.d_f, v.pre_u, norm_u, 14))
    sums = sync_a.wait()
    norm_a = moments(sums[0:1], sums[1:2], count)

    def make_a(k):
        at = rows_at(k, 96)
        v.act_a[at, :] = jax.nn.silu(gamma(15) * normed(v.pre_a, at, norm_a) + beta(15)).astype(BF)

    loop(6, make_a)
    aux_head.start(dot(v.act_a[...], w_ac))

    class Scatter:
        def __init__(self, first, second, full, rows, out, base=0):
            self.full, self.rows, self.out, self.base = full, rows, out, base
            self.first, self.second = first, second
            self.near_s, self.near_r = take(HALF), take(HALF)
            self.far_s, self.far_r = take(HALF), take(HALF)
            self.block = min(rows, 64)

        def near(self, step):
            dest = far_peer(partner, step)
            return remote(
                self.full.at[rows_at(dest, self.rows), :],
                self.first.at[step],
                self.near_s + step,
                self.near_r + step,
                {BATCH: partner},
            )

        def far(self, step):
            return remote(
                self.first.at[step],
                self.second.at[step - 1],
                self.far_s + step,
                self.far_r + step,
                {BATCH: far_peer(me, step)},
            )

        def starts(self):
            return [lambda step=step: self.near(step).start() for step in (1, 2, 3, 0)]

        def middles(self):
            def go(step):
                self.near(step).wait_recv()
                base = far_peer(me, step) * (self.rows // self.block)

                def add(k):
                    at = rows_at(k, self.block)
                    value = self.full[rows_at(base + k, self.block), :].astype(F32)
                    value = value + self.first[step, at, :].astype(F32)
                    self.first[step, at, :] = value.astype(self.first.dtype)

                loop(self.rows // self.block, add)
                self.far(step).start()

            return [functools.partial(go, step) for step in range(1, HALF)]

        def end(self):
            self.near(0).wait_recv()
            for step in range(1, HALF):
                self.far(step).wait_recv()
            base = me * (self.rows // self.block)

            def add(k, carry):
                at = rows_at(k, self.block)
                value = self.full[rows_at(base + k, self.block), :].astype(F32)
                value = value + self.first[0, at, :].astype(F32)
                for step in range(1, HALF):
                    value = value + self.second[step - 1, at, :].astype(F32)
                if self.out is o_flat:
                    times = value.shape[1] // 128
                    start = self.base + k * self.block * times
                    for q in range(times):
                        where = pl.ds(start + q, self.block, stride=times if times > 1 else None)
                        self.out[where, :] = value[:, q * 128 : q * 128 + 128]
                else:
                    self.out[at, :] = value
                return carry + fold(value * value)

            squares = lax.fori_loop(
                0, self.rows // self.block, add, jnp.zeros((8, self.full.shape[1]), F32)
            )
            for step in (1, 2, 3, 0):
                self.near(step).wait_send()
                if step:
                    self.far(step).wait_send()
            return sum(split_rows(total(squares)))

    s_c = Scatter(v.first_c, v.second_c, v.w_c, 16, v.out_c)
    s_ac = Scatter(v.first_ac, v.second_ac, v.w_ac, 8, v.out_ac)
    s_a = Scatter(v.first_a, v.second_a, v.w_a, 576, v.out_a)
    s_s = Scatter(v.first_s, v.second_s, v.w_s, 128, o_flat, 128)
    s_e = Scatter(v.first_e, v.second_e, v.w_e, 64, o_flat, 1216)
    s_m = Scatter(v.first_m, v.second_m, v.w_m, 576, o_flat, 640)
    s_r = Scatter(v.first_r, v.second_r, v.w_r, 128, o_flat, 0)

    class ScatterUnite:
        def __init__(self):
            self.near_s, self.near_r = take(SLOTS * HALF), take(SLOTS * HALF)
            self.far_s, self.far_r = take(SLOTS * HALF), take(SLOTS * HALF)

        def near(self, step, slot, base):
            dest = far_peer(base, step)
            return remote(
                v.w_u.at[merged_rows(dest, slot), :],
                v.first_u.at[step, slot],
                self.near_s + step * SLOTS + slot,
                self.near_r + step * SLOTS + slot,
                {BATCH: partner},
            )

        def far(self, step, slot):
            return remote(
                v.first_u.at[step, slot],
                v.second_u.at[step - 1, slot],
                self.far_s + step * SLOTS + slot,
                self.far_r + step * SLOTS + slot,
                {BATCH: far_peer(me, step)},
            )

        def own_rows(self, owner, slot, k):
            block = owner * 9 + block_of(owner, slot)
            index = lax.div(block, 8) * MERGED + lax.rem(block, 8)
            return rows_at(index * 8 + k, 64)

        def starts(self, slot):
            def go(step):
                self.near(step, slot, partner).start()

            return [
                functools.partial(has, far_peer(partner, step), slot, functools.partial(go, step))
                for step in (1, 2, 3, 0)
            ]

        def middles(self, slot):
            def go(step):
                self.near(step, slot, me).wait_recv()
                owner = far_peer(me, step)

                def add(k):
                    at = rows_at(k, 64)
                    value = v.w_u[self.own_rows(owner, slot, k), :].astype(F32)
                    value = value + v.first_u[step, slot, at, :].astype(F32)
                    v.first_u[step, slot, at, :] = value.astype(BF)

                loop(8, add)
                self.far(step, slot).start()

            return [
                functools.partial(has, far_peer(me, step), slot, functools.partial(go, step))
                for step in range(1, HALF)
            ]

        def end(self):
            for slot in range(SLOTS):

                def go(slot=slot):
                    self.near(0, slot, me).wait_recv()
                    for step in range(1, HALF):
                        self.far(step, slot).wait_recv()
                    j = block_of(me, slot)

                    def add(k):
                        at = rows_at(k, 64)
                        value = v.w_u[self.own_rows(me, slot, k), :].astype(F32)
                        value = value + v.first_u[0, slot, at, :].astype(F32)
                        for step in range(1, HALF):
                            value = value + v.second_u[step - 1, slot, at, :].astype(F32)
                        o_u[rows_at(j * 8 + k, 64), :] = value

                    loop(8, add)

                has(me, slot, go)
                for step in (1, 2, 3, 0):
                    has(
                        far_peer(partner, step),
                        slot,
                        lambda step=step, slot=slot: self.near(step, slot, partner).wait_send(),
                    )
                    if step:
                        has(
                            far_peer(me, step),
                            slot,
                            lambda step=step, slot=slot: self.far(step, slot).wait_send(),
                        )

            def square(k, carry):
                value = o_u[rows_at(k, 64), :]
                return carry + fold(value * value)

            squares = lax.fori_loop(0, 72, square, jnp.zeros((8, 128), F32))
            return sum(split_rows(total(squares)))

    s_u = ScatterUnite()

    v.w_c[...] = dot_tn(v.united[...], g_main).astype(BF)
    mix(s_c.starts())
    sums = sync.wait()
    gain_grads[14] = (sums[1:2], sums[0:1])

    def spread_taps(ref, pre, norm, row, first, second):
        def step(k):
            at = rows_at(k, 96)
            value = back_norm(
                ref[at, :], normed(pre, at, norm), v.ins[at, :], norm, gamma(row), first, second, count
            )
            ref[at, :] = value.astype(BF).astype(F32)

        loop(6, step)
        v.grad_pad[EDGE : EDGE + CELLS, :] = ref[...]

    def back_tap(tap, spacing, at):
        start = EDGE + at - offset(tap, spacing)
        value = v.grad_pad[start : start + 96, :]
        right = tap % 3 - 1
        if right:
            value = value * col_mask(slice(at, at + 96), -right * spacing)
        return value

    def fill(cat, spacing):
        for tap in range(9):
            for at in range(0, CELLS, 96):
                cat[at : at + 96, tap * 128 : tap * 128 + 128] = back_tap(tap, spacing, at).astype(
                    BF
                )

    spread_taps(v.d_f, v.pre_u, norm_u, 14, sums[0:1], sums[1:2])
    fill(v.cat_u, 1)

    dz = dot(v.pick[...], v.cat_u[...])
    for tap in range(9):
        v.dz_send[tap] = dz[:, tap * 128 : tap * 128 + 128].astype(BF)
    v.dz_recv[me] = v.dz_send[pl.ds(me, 2)]
    ex_dz = Exchange(
        BATCH, OWNERS, lambda o: v.dz_send.at[pl.ds(o, 2)], lambda s: v.dz_recv.at[s]
    )
    ex_dz.start()

    def merged_back(c):
        weight = jnp.concatenate(
            [v.w_u[rows_at(tap * MERGED + c, 512), :] for tap in range(9)], axis=1
        )
        v.joined[c] = dot_nt(v.cat_u[...], weight).astype(BF)

    near_s, near_r, far_s, far_r = take(2), take(2), take(1), take(1)

    def dm_near(k, slot):
        return remote(
            v.joined.at[slot], v.dm_near.at[k], near_s + k, near_r + k, {TENSOR: t_core}
        )

    merged_back(t_diag)
    dm_near(1, t_diag).start()
    merged_back(t_core)
    dm_near(0, t_core).start()
    merged_back(t_x)
    merged_back(t)

    def unite_grad(c):
        for p in range(5):
            width = 256 if p < 4 else 128
            value = dot(v.joined_t[c], v.cat_u[:, p * 256 : p * 256 + width])
            v.w_u[rows_at(2 * p * MERGED + c, 512), :] = value[:, :128].astype(BF)
            if p < 4:
                v.w_u[rows_at((2 * p + 1) * MERGED + c, 512), :] = value[:, 128:].astype(BF)

    unite_grad(0)
    mix(s_u.starts(0))
    o_misc[1:2, :] = o_misc[1:2, :] + aux_head.finish(0.4)
    ex_dz.wait()

    d_act = v.d_sum.at[0 : OWNERS * BINS, :]
    d_act[...] = jnp.zeros((OWNERS * BINS, 512), F32)

    def branch_back(j):
        def body(group, side):
            kept = jnp.where(group_id == group, 1.0, 0.0)
            value = v.dz_recv[:, side].reshape(OWNERS * BINS, 128).astype(F32) * kept
            value = value.astype(BF)
            o_u[rows_at(j, 512), :] = dot(v.act_t[...], value)
            d_act[...] = d_act[...] + dot_nt(value, v.w_own[rows_at(j, 512), :])

        own_branch(j, body)

    loop(9, branch_back)
    for k in range(SPLITS):
        v.d_act_send[k] = d_act[:, k * 128 : k * 128 + 128].astype(BF)
    v.d_act_recv[t] = v.d_act_send[t]
    ex = Exchange(TENSOR, SPLITS, lambda o: v.d_act_send.at[o], lambda s: v.d_act_recv.at[s])
    ex.start()
    unite_grad(1)
    mix(s_u.starts(1))
    dm_near(1, t_x).wait_recv()

    def add_x(k):
        at = rows_at(k, 48)
        value = v.joined[t_x, at, :].astype(F32) + v.dm_near[1, at, :].astype(F32)
        v.joined[t_x, at, :] = value.astype(BF)

    loop(12, add_x)
    dm_far = remote(v.joined.at[t_x], v.dm_far, far_s, far_r, {TENSOR: t_x})
    dm_far.start()
    g_aux = aux_head.grad()
    v.d_f2[...] = dot_nt(g_aux, w_ac)
    sync_a = Sync(v.sync_b2)
    sync_a.start(through_silu(v.d_f2, v.pre_a, norm_a, 15))
    v.w_ac[...] = dot_tn(v.act_a[...], g_aux)[:64]
    mix(s_ac.starts())

    unite_grad(2)
    unite_grad(3)
    ex.wait()
    for k in range(OWNERS):
        at = slice(k * BINS, k * BINS + BINS)
        value = v.d_act_recv[0, at, :].astype(F32)
        for slot in range(1, SPLITS):
            value = value + v.d_act_recv[slot, at, :].astype(F32)
        v.d_img_send[k] = value.astype(BF)
    v.d_img_recv[me] = v.d_img_send[me]
    ex = Exchange(BATCH, OWNERS, lambda o: v.d_img_send.at[o], lambda s: v.d_img_recv.at[s])
    ex.start()
    mix(s_u.starts(2), s_u.middles(0))

    sums = sync_a.wait()
    gain_grads[15] = (sums[1:2], sums[0:1])
    spread_taps(v.d_f2, v.pre_a, norm_a, 15, sums[0:1], sums[1:2])
    for p in range(5):
        for at in range(0, CELLS, 96):
            value = back_tap(2 * p, 1, at)
            if p < 4:
                value = value + pltpu.roll(back_tap(2 * p + 1, 1, at), 64, 1)
            v.cat_a[at : at + 96, p * 128 : p * 128 + 128] = value.astype(BF)

    def aux_grad(c2):
        value2 = dot_tn(v.whole[c2], v.cat_a[...])
        for half in range(2):
            value = value2[half * 128 : half * 128 + 128]
            c = 2 * c2 + half
            for p in range(5):
                v.pad[p, EDGE : EDGE + 128, :] = value[:, p * 128 : p * 128 + 128]
                low = v.pad[p, pl.ds(EDGE, 64, stride=2), :]
                top = v.pad[p, pl.ds(EDGE + 1, 64, stride=2), :]
                even = jnp.where(left_half, low, pltpu.roll(top, 64, 1))
                v.w_a[rows_at(2 * p * 8 + c, 64), :] = even.astype(BF)
                if p < 4:
                    odd = jnp.where(left_half, pltpu.roll(low, 64, 1), top)
                    v.w_a[rows_at((2 * p + 1) * 8 + c, 64), :] = odd.astype(BF)

    loop(SPLITS, aux_grad)
    ex.wait()
    d_b = v.d_img_recv[0].astype(F32)
    for k in range(1, OWNERS):
        d_b = d_b + v.d_img_recv[k].astype(F32)
    unit_b = (v.all_b[me].astype(F32) - mean_b) * scale_b
    d_b = d_b * slope(gamma_b * unit_b + beta_b)
    sync = Sync(v.sync_b3)
    sync.start(
        [total(d_b * group_mask(g)) for g in range(4)]
        + [total(d_b * unit_b * group_mask(g)) for g in range(4)]
    )
    mix(s_u.starts(3), s_u.middles(1))
    sums = sync.wait()
    first_b = jnp.zeros((BINS, 128), F32)
    second_b = jnp.zeros((BINS, 128), F32)
    for group in range(4):
        kept = group_mask(group)
        gain_grads[10 + group] = (sums[4 + group : 5 + group], sums[group : group + 1])
        first_b = first_b + kept * sums[group : group + 1]
        second_b = second_b + kept * sums[4 + group : 5 + group]
    inner = d_b - (first_b + unit_b * second_b) * count_b
    v.d_bp[t] = (gamma_b * scale_b * inner).astype(BF)
    spread_d = Spread(v.d_bp)
    spread_d.start()
    mix(s_u.starts(4), s_u.middles(2))
    spread_d.wait()
    d_bp_move = ToGroup(
        lambda owner, rows: v.d_bp.at[:, 0:rows, :],
        lambda slot, rows: v.d_bp_all.at[slot, :, 0:rows, :],
    )
    d_bp_move.start()
    v.d_bp_all[me] = v.d_bp[...]
    d_bp = jnp.concatenate([v.d_bp[k] for k in range(SPLITS)], axis=1)
    d_pooled = jnp.zeros((BINS, 512), F32)
    for group in range(4):
        rows = (d_bp.astype(F32) * group_mask(group)).astype(BF)
        d_pooled = d_pooled + dot_nt(rows, v.w_b[group * 512 : group * 512 + 512, :])
    d_pooled = (d_pooled / cells_in).astype(BF)
    v.d_sum[...] = dot_tn(v.pool[...], d_pooled)
    dm_near(0, t).wait_recv()
    dm_far.wait_recv()

    def through_sum(k, carry):
        at = rows_at(k, 48)
        value = v.d_sum[at, :] + v.joined[t, at, :].astype(F32) + v.dm_near[0, at, :].astype(F32)
        value = (value + v.dm_far[at, :].astype(F32)) * slope(summed(at))
        v.d_sum[at, :] = value
        return (
            carry[0] + fold(value),
            carry[1] + fold(value * normed(v.pre_e, at, norm_e)),
            carry[2] + fold(value * normed(v.pre_s, at, norm_s)),
        )

    zero = jnp.zeros((8, 512), F32)
    three = [total(item) for item in lax.fori_loop(0, 12, through_sum, (zero, zero, zero))]
    sync = Sync(v.sync_b4)
    sync.start(split_rows(three[0]) + split_rows(three[1]) + split_rows(three[2]))
    mix(s_a.starts(), s_u.middles(3))
    sums = sync.wait()
    first_s = join_rows(sums, 0, 4)
    second_e, second_s = join_rows(sums, 4, 4), join_rows(sums, 8, 4)
    for k in range(4):
        gain_grads[6 + k] = (sums[4 + k : 5 + k], sums[k : k + 1])
        gain_grads[1 + k] = (sums[8 + k : 9 + k], sums[k : k + 1])

    def back_both(k):
        at = rows_at(k, 48)
        value, mask = v.d_sum[at, :], wide(v.ins[at, :], 4)
        v.d_e[at, :] = back_norm(
            value, normed(v.pre_e, at, norm_e), mask, norm_e, gamma(6, 4), first_s, second_e, count4
        ).astype(BF)
        v.d_s[at, :] = back_norm(
            value, normed(v.pre_s, at, norm_s), mask, norm_s, gamma(1, 4), first_s, second_s, count4
        ).astype(BF)

    loop(12, back_both)

    def back_hidden(grad, weight, index):
        value = dot_nt(grad, weight)
        for k in range(SPLITS):
            v.dh_send[k] = value[:, k * 128 : k * 128 + 128].astype(BF)
        v.dh_recv[index, t] = v.dh_send[t]
        ex = Exchange(
            TENSOR, SPLITS, lambda o: v.dh_send.at[o], lambda s: v.dh_recv.at[index, s]
        )
        ex.start()
        return ex

    def hidden_sum(index):
        def step(k):
            at = rows_at(k, 96)
            value = v.dh_recv[index, 0, at, :].astype(F32)
            for slot in range(1, SPLITS):
                value = value + v.dh_recv[index, slot, at, :].astype(F32)
            v.d_f[at, :] = value

        loop(6, step)

    ex = back_hidden(v.d_e[...], v.w_e[...], 0)
    def short_grad(c):
        v.w_s[rows_at(c, 256), :] = dot_tn(v.whole[c], v.d_s[...]).astype(BF)

    loop(SPLITS, short_grad)
    mix(s_s.starts(), s_u.middles(4))
    for k in range(SPLITS):
        v.w_e[k * 128 : k * 128 + 128, :] = dot_tn(v.h2[k], v.d_e[...]).astype(BF)
    ex.wait()
    hidden_sum(0)
    sync = Sync(v.sync_b5)
    sync.start(through_silu(v.d_f, v.pre_m, norm_m, 5))
    mix(s_e.starts())
    mix(s_c.middles())
    mix(s_ac.middles())
    mix(s_a.middles())
    sums = sync.wait()
    gain_grads[5] = (sums[1:2], sums[0:1])
    spread_taps(v.d_f, v.pre_m, norm_m, 5, sums[0:1], sums[1:2])
    fill(v.cat_u, 4)
    weight = jnp.concatenate([v.w_m[tap * 512 : tap * 512 + 512, :] for tap in range(9)], axis=1)
    ex = back_hidden(v.cat_u[...], weight, 1)

    def middle_grad(k):
        value = dot_tn(v.h1[k], v.cat_u[...])
        for tap in range(9):
            v.w_m[rows_at(tap * 4 + k, 128), :] = value[:, tap * 128 : tap * 128 + 128].astype(BF)

    loop(SPLITS, middle_grad)
    mix(s_m.starts())
    mix(s_s.middles())
    ex.wait()
    hidden_sum(1)
    sync = Sync(v.sync_b6)
    sync.start(through_silu(v.d_f, v.pre_r, norm_r, 0))

    mix(s_e.middles())
    sums = sync.wait()
    gain_grads[0] = (sums[1:2], sums[0:1])

    def back_reduce(k):
        at = rows_at(k, 96)
        v.d_low[at, :] = back_norm(
            v.d_f[at, :], normed(v.pre_r, at, norm_r), v.ins[at, :], norm_r, gamma(0), sums[0:1], sums[1:2], count
        ).astype(BF)

    loop(6, back_reduce)

    def reduce_grad(c):
        v.w_r[rows_at(c, 256), :] = dot_tn(v.whole[c], v.d_low[...]).astype(BF)

    loop(SPLITS, reduce_grad)
    mix(s_r.starts())
    mix(s_m.middles() + s_r.middles())
    pool_move.wait()
    d_bp_move.wait()
    own_group = jnp.where(group_id == lax.div(me, 2), 1.0, 0.0)
    d_rows = jnp.concatenate(
        [v.d_bp_all[:, k].reshape(OWNERS * BINS, 128) for k in range(SPLITS)], axis=1
    )
    d_rows = (d_rows.astype(F32) * own_group).astype(BF)
    branch_grad = dot_tn(v.pool_all[...].reshape(OWNERS * BINS, 256), d_rows)
    for k in range(4):
        o_flat[pl.ds(1472 + k, 256, stride=4), :] = branch_grad[:, k * 128 : k * 128 + 128]
    rest = (s_c, s_ac, s_a, s_e, s_s, s_m, s_r)
    squares = s_u.end() + sum(split_rows(total(branch_grad * branch_grad)))
    for item in rest:
        squares = squares + item.end()
    dm_near(1, t_diag).wait_send()
    dm_near(0, t_core).wait_send()
    dm_far.wait_send()

    v.gain_rows[...] = jnp.zeros((40, 128), F32)
    gammas = [gain_grads[row][0] for row in range(16)]
    betas = [pltpu.roll(gain_grads[row][1], 64, 1) for row in range(16)]
    o_shift[...] = gain_grads[14][1]
    for row in range(31):
        if row < 15:
            value = gammas[row]
        else:
            left = gammas[15] if row == 15 else betas[row - 16]
            value = jnp.where(lane < 64, left, betas[row - 15])
        v.gain_rows[row + 1 : row + 2, :] = value
    squares = squares + total(fold(v.gain_rows[...] * v.gain_rows[...])) / OWNERS

    sync = Sync(v.sync_end)
    sync.start([squares, o_misc[1:2, :]])

    tail = {}

    def put(where, value):
        tail[where] = value if where not in tail else tail[where] + value

    def class_tail(ref, count, base):
        for row in range(count):
            first, shift = divmod(base + NCLS * row, 128)
            for k in range(2):
                value = roll(ref[row : row + 1, k * 128 : k * 128 + 128], shift)
                put(first + k, jnp.where(lane >= shift, value, 0.0))
                if shift:
                    put(first + k + 1, jnp.where(lane < shift, value, 0.0))

    class_tail(v.out_c, 16, 0)
    class_tail(v.out_ac, 8, 76128)
    start = lax.rem(496 * me, 128)
    first = lax.div(496 * me, 128)
    own = [
        pltpu.roll(v.gain_rows[pl.ds(first + k, 1), :], lax.rem(16 - start + 128, 128), 1)
        for k in range(6)
    ]
    spot = lane - 16 + start
    for k in range(4):
        value = jnp.where(spot < 0, own[k], jnp.where(spot >= 128, own[k + 2], own[k + 1]))
        put(604 + k, jnp.where(lane >= 16, value, 0.0) if k == 0 else value)
    v.grad_pad[EDGE : EDGE + 576, :] = pltpu.roll(v.out_a[...], 96, 1)
    o_flat[7122:7706, :] = jnp.where(
        lane >= 96, v.grad_pad[EDGE : EDGE + 584, :], v.grad_pad[EDGE - 1 : EDGE + 583, :]
    )
    for row in range(608):
        if row in (18, 594):
            o_flat[7104 + row : 7105 + row, :] = o_flat[7104 + row : 7105 + row, :] + tail[row]
        elif row < 18 or row > 594:
            o_flat[7104 + row : 7105 + row, :] = tail[row]
    v.end_t[t] = sync.wait()
    spread_e = Spread(v.end_t)
    spread_e.start()
    spread_e.wait()
    ends = v.end_t[0]
    for k in range(1, SPLITS):
        ends = ends + v.end_t[k]
    o_misc[...] = ends
    o_misc[2:3, :] = jnp.broadcast_to(class_weights()[1], (1, 128))


def whole_step(sizes, labels, feat, flat):
    plan = scratch_plan()
    vmem = pl.BlockSpec(memory_space=pltpu.VMEM)
    anywhere = pl.BlockSpec(memory_space=pl.ANY)
    outs = [flat.shape, (1, 128), (8, 128)]
    return pl.pallas_call(
        functools.partial(step_kernel, tuple(plan)),
        out_shape=[jax.ShapeDtypeStruct(shape, F32) for shape in outs],
        in_specs=[pl.BlockSpec(memory_space=pltpu.SMEM), vmem, anywhere, anywhere],
        out_specs=[vmem] * len(outs),
        scratch_shapes=[pltpu.VMEM(shape, kind) for shape, kind in plan.values()]
        + [pltpu.SemaphoreType.DMA((SEMAPHORES,))],
        compiler_params=pltpu.CompilerParams(
            collective_id=0, has_side_effects=True, vmem_limit_bytes=63 * 1024 * 1024
        ),
        name="whole_step",
    )(sizes, labels, feat, flat)


def update_kernel(
    misc, grad, param, first, second, average,
    o_param, o_first, o_second, o_average, o_norm, o_loss, o_weight,
):
    norm = jnp.sqrt(jnp.sum(misc[0:1, :], axis=1, keepdims=True))
    o_norm[...] = norm
    o_loss[...] = jnp.sum(misc[1:2, :], axis=1, keepdims=True)
    o_weight[...] = misc[2:3, 0:1]
    clipped = grad[...] * jnp.minimum(1.0, 0.05 / (norm + 1e-06))
    new_first = 0.5 * first[...] + 0.5 * clipped
    new_second = 0.5 * second[...] + 0.5 * clipped * clipped
    lift = 1.0 / (1.0 - 0.5**STEP)
    old = param[...]
    ratio = (new_first * lift) / (jnp.sqrt(new_second * lift) + 1e-08)
    new = old - 0.01 * (ratio + 0.01 * old)
    o_param[...] = new
    o_first[...] = new_first
    o_second[...] = new_second
    o_average[...] = 0.999 * average[...] + 0.001 * new


def update(misc, grad, param, first, second, average):
    rows = grad.shape[0]
    block = pl.BlockSpec((1024, 128), lambda i: (i, 0))
    whole = pl.BlockSpec((8, 128), lambda i: (0, 0))
    one = pl.BlockSpec((1, 1), lambda i: (0, 0))
    big = jax.ShapeDtypeStruct((rows, 128), F32)
    return pl.pallas_call(
        update_kernel,
        grid=(pl.cdiv(rows, 1024),),
        out_shape=[big] * 4 + [jax.ShapeDtypeStruct((1, 1), F32)] * 3,
        in_specs=[whole] + [block] * 5,
        out_specs=[block] * 4 + [one] * 3,
        compiler_params=pltpu.CompilerParams(vmem_limit_bytes=60 * 1024 * 1024),
        name="update",
    )(misc, grad, param, first, second, average)


def fits(splits, owners):
    return splits == SPLITS and owners == OWNERS


def local_fast(features, labels, valid, sizes, params, first_moment, squared_mean, average):
    flat = params.reshape(-1, 128)
    marked = jnp.where(valid > 0, labels, -1).astype(F32).reshape(CELLS, 1)
    grad, shift_grad, misc = whole_step(
        sizes, jnp.broadcast_to(marked, (CELLS, 128)), features.reshape(CELLS, -1), flat
    )
    news = update(
        misc,
        grad,
        flat,
        first_moment.reshape(-1, 128),
        squared_mean.reshape(-1, 128),
        average.reshape(-1, 128),
    )
    new_params, new_first, new_second, new_average = [
        item.reshape(params.shape) for item in news[:4]
    ]
    return (
        new_params,
        new_first,
        new_second,
        new_average,
        new_params.astype(BF),
        news[4].reshape(()),
        news[5].reshape(()),
        news[6].reshape(()),
        shift_grad.reshape(128),
    )


def solution(mesh):
    chosen = local_fast if fits(mesh.shape["tensor"], mesh.shape["batch"]) else local
    return jax.shard_map(
        chosen,
        mesh=mesh,
        in_specs=(
            P("batch", None, None, "tensor"),
            P("batch", None, None),
            P("batch", None, None),
            P("batch", None),
            P("tensor", "batch"),
            P("tensor", "batch"),
            P("tensor", "batch"),
            P("tensor", "batch"),
        ),
        out_specs=(
            P("tensor", "batch"),
            P("tensor", "batch"),
            P("tensor", "batch"),
            P("tensor", "batch"),
            P("tensor", "batch"),
            P(),
            P(),
            P(),
            P("tensor"),
        ),
        check_vma=False,
    )
```

```python
import functools

import jax
import jax.numpy as jnp
from jax import lax
from jax.experimental import pallas as pl
from jax.experimental.pallas import tpu as pltpu
from jax.sharding import PartitionSpec as P

C_IN = 1024
MID = 512
C_OUT = 2048
PPM = 512
AUXW = 256
NCLS = 150
MAP = 24
STEP = 3


BIN_COUNTS = (1, 2, 3, 6)
BIN_STARTS = (0, 1, 5, 14)


def segment_shapes(splits):
    return [
        (C_IN, MID // splits),
        (C_IN, C_OUT // splits),
        (9, MID, MID // splits),
        (MID, C_OUT // splits),
        (4, C_OUT // splits, PPM),
        (9, C_OUT + 4 * PPM, PPM // splits),
        (PPM // splits, NCLS),
        (9, C_IN, AUXW // splits),
        (AUXW // splits, NCLS),
        (2, (2 * MID + 2 * C_OUT + 5 * PPM + AUXW) // splits),
    ]


def unflatten(rows, splits):
    split_parts = []
    start = 0
    for shape in segment_shapes(splits):
        count = 1
        for extent in shape:
            count = count * extent
        count = count // rows.shape[0]
        split_parts.append(rows[:, start : start + count].reshape(shape))
        start = start + count
    return split_parts


def gain_pieces(gains, splits):
    widths = [MID, C_OUT, MID, C_OUT, PPM, PPM, PPM, PPM, PPM, AUXW]
    split_parts = []
    start = 0
    for width in widths:
        step_width = width // splits
        split_parts.append(gains[:, start : start + step_width])
        start = start + step_width
    return split_parts


def shifted(field, down, right):
    image_height, width = (field.shape[1], field.shape[2])
    rows_pad, cols_pad = (abs(down), abs(right))
    padded = jnp.pad(field, ((0, 0), (rows_pad, rows_pad), (cols_pad, cols_pad), (0, 0)))
    return padded[
        :,
        rows_pad + down : rows_pad + down + image_height,
        cols_pad + right : cols_pad + right + width,
        :,
    ]


def conv_forward(field, kernel, spacing):
    total = jnp.zeros(field.shape[:-1] + (kernel.shape[2],), jnp.float32)
    for tap in range(9):
        moved = shifted(field, (tap // 3 - 1) * spacing, (tap % 3 - 1) * spacing)
        total = total + jnp.dot(moved, kernel[tap], preferred_element_type=jnp.float32)
    return total


def conv_input_back(grad, kernel, spacing):
    total = jnp.zeros(grad.shape[:-1] + (kernel.shape[1],), jnp.float32)
    for tap in range(9):
        product = jnp.dot(grad, kernel[tap].T, preferred_element_type=jnp.float32)
        total = total + shifted(product, -(tap // 3 - 1) * spacing, -(tap % 3 - 1) * spacing)
    return total


def conv_kernel_back(field, grad, spacing):
    return jnp.stack(
        [
            jnp.einsum(
                "ihwc,ihwd->cd",
                shifted(field, (tap // 3 - 1) * spacing, (tap % 3 - 1) * spacing),
                grad,
                preferred_element_type=jnp.float32,
            )
            for tap in range(9)
        ]
    )


def silu_slope(value):
    gate = jax.nn.sigmoid(value)
    return gate * (1.0 + value * (1.0 - gate))


def channel_sums(values):
    return values.reshape(-1, values.shape[-1]).sum(0)


def masked_norm_apply(items, extra):
    sends = []
    for value, mask, norm in items:
        sends = sends + [
            channel_sums(value * mask),
            channel_sums(value * value * mask),
            jnp.sum(mask) * jnp.ones((1,), jnp.float32),
        ]
    totals = lax.psum(tuple(sends + extra), "batch")
    results = []
    for index, (value, mask, norm) in enumerate(items):
        count = totals[3 * index + 2]
        mean = totals[3 * index] / count
        spread = totals[3 * index + 1] / count - mean * mean
        scaling = lax.rsqrt(spread + 1e-05)
        normed = (value - mean) * scaling
        results.append((norm[0] * normed + norm[1], normed, scaling, count, mask, norm[0]))
    return (results, totals[3 * len(items) :])


def norm_backward(items):
    sends = []
    for grad, kept in items:
        sends = sends + [channel_sums(grad), channel_sums(grad * kept[1])]
    totals = lax.psum(tuple(sends), "batch")
    results = []
    for index, (grad, kept) in enumerate(items):
        outcome, normed, scaling, count, mask, gamma = kept
        first_sum, second_sum = (totals[2 * index], totals[2 * index + 1])
        inner = grad - mask * (first_sum + normed * second_sum) / count
        results.append(gamma * scaling * inner)
    return (results, sends, totals)


def bin_tables(extent, bins, length):
    which = jnp.arange(bins, dtype=jnp.int32)[None, :, None]
    place = jnp.arange(length, dtype=jnp.int32)[None, None, :]
    edge = extent[:, None, None]
    lower = which * edge // bins
    upper = ((which + 1) * edge + bins - 1) // bins
    member = ((place >= lower) & (place < upper)).astype(jnp.float32)
    target = jnp.minimum(place * bins // edge, bins - 1)
    chosen = (target == which).astype(jnp.float32)
    return (member, chosen)


def spread_bins(merged, branch, tables, images):
    joined = [merged]
    for group, bins in enumerate(BIN_COUNTS):
        rows_in, cols_in, rows_pick, cols_pick, cell_count = tables[group]
        piece = branch[:, BIN_STARTS[group] : BIN_STARTS[group] + bins * bins].reshape(
            images, bins, bins, -1
        )
        joined.append(
            jnp.einsum(
                "ikh,ilw,iklc->ihwc",
                rows_pick.astype(jnp.bfloat16),
                cols_pick.astype(jnp.bfloat16),
                piece,
                preferred_element_type=jnp.float32,
            ).astype(jnp.bfloat16)
        )
    return jnp.concatenate(joined, axis=-1)


def pick_bins(d_joined, width, tables, images):
    branch_width = (d_joined.shape[-1] - width) // 4
    d_up = []
    for group, bins in enumerate(BIN_COUNTS):
        rows_in, cols_in, rows_pick, cols_pick, cell_count = tables[group]
        piece = d_joined[..., width + group * branch_width : width + (group + 1) * branch_width]
        d_up.append(
            jnp.einsum("ikh,ilw,ihwc->iklc", rows_pick, cols_pick, piece).reshape(
                images, bins * bins, -1
            )
        )
    return (d_joined[..., :width], jnp.concatenate(d_up, axis=1))


def gather_channels(field):
    return lax.all_gather(field, "tensor", axis=3, tiled=True)


def scatter_channels(field):
    return lax.psum_scatter(
        field.astype(jnp.bfloat16), "tensor", scatter_dimension=3, tiled=True
    ).astype(jnp.float32)


def local(features, labels, valid, sizes, params, first_moment, squared_mean, average):
    splits = lax.axis_size("tensor")
    owners = lax.axis_size("batch")
    images = features.shape[0]
    gathered = lax.all_gather(params.astype(jnp.bfloat16), "batch", axis=0, tiled=True)
    (
        w_reduce,
        w_short,
        w_middle,
        w_expand,
        w_branch,
        w_unite,
        w_classes,
        w_aux,
        w_aux_classes,
        gains,
    ) = unflatten(gathered, splits)
    norms = [(piece[0], piece[1]) for piece in gain_pieces(gains.astype(jnp.float32), splits)]
    rows_at = jnp.arange(MAP, dtype=jnp.int32)
    inside = (rows_at[None, :, None] < sizes[:, 0][:, None, None]) & (
        rows_at[None, None, :] < sizes[:, 1][:, None, None]
    )
    inside = inside.astype(jnp.float32)[..., None]
    counted = inside * valid.astype(jnp.float32)[..., None]
    labels_hot = (labels[..., None] == jnp.arange(NCLS, dtype=jnp.int32)).astype(jnp.float32)
    class_local = channel_sums(labels_hot * counted)
    whole = lax.all_gather(features, "tensor", axis=3, tiled=True)
    pre_reduce = jnp.dot(whole, w_reduce, preferred_element_type=jnp.float32)
    pre_short = jnp.dot(whole, w_short, preferred_element_type=jnp.float32)
    pre_aux = conv_forward(whole, w_aux, 1)
    leading_part, label_tally = masked_norm_apply(
        [
            (pre_reduce, inside, norms[0]),
            (pre_short, inside, norms[1]),
            (pre_aux, inside, norms[9]),
        ],
        [class_local],
    )
    class_pixel_counts = label_tally[0]
    hidden_one = jax.nn.silu(leading_part[0][0]).astype(jnp.bfloat16)
    aux_act = jax.nn.silu(leading_part[2][0]).astype(jnp.bfloat16)
    hidden_full = gather_channels(hidden_one)
    pre_middle = conv_forward(hidden_full, w_middle, 4)
    second, unused = masked_norm_apply([(pre_middle, inside, norms[2])], [])
    hidden_two = jax.nn.silu(second[0][0]).astype(jnp.bfloat16)
    hidden_two_full = gather_channels(hidden_two)
    pre_expand = jnp.dot(hidden_two_full, w_expand, preferred_element_type=jnp.float32)
    third, unused = masked_norm_apply([(pre_expand, inside, norms[3])], [])
    summed = third[0][0] + leading_part[1][0]
    merged = jax.nn.silu(summed).astype(jnp.bfloat16)
    tables = []
    pooled_list = []
    partial_list = []
    for group, bins in enumerate(BIN_COUNTS):
        rows_in, rows_pick = bin_tables(sizes[:, 0], bins, MAP)
        cols_in, cols_pick = bin_tables(sizes[:, 1], bins, MAP)
        cell_count = (
            jnp.sum(rows_in, axis=2)[:, :, None, None] * jnp.sum(cols_in, axis=2)[:, None, :, None]
        )
        tables.append((rows_in, cols_in, rows_pick, cols_pick, cell_count))
        pooled = (
            jnp.einsum(
                "ikh,ilw,ihwc->iklc",
                rows_in.astype(jnp.bfloat16),
                cols_in.astype(jnp.bfloat16),
                merged,
                preferred_element_type=jnp.float32,
            )
            / cell_count
        )
        pooled = pooled.astype(jnp.bfloat16).reshape(images, bins * bins, -1)
        pooled_list.append(pooled)
        partial_list.append(
            jnp.einsum("ipc,cd->ipd", pooled, w_branch[group], preferred_element_type=jnp.float32)
        )
    branch_pre = lax.psum_scatter(
        jnp.concatenate(partial_list, axis=1).astype(jnp.bfloat16),
        "tensor",
        scatter_dimension=2,
        tiled=True,
    ).astype(jnp.float32)
    branch_items = []
    for group, bins in enumerate(BIN_COUNTS):
        piece = branch_pre[:, BIN_STARTS[group] : BIN_STARTS[group] + bins * bins]
        branch_items.append(
            (piece, jnp.ones(piece.shape[:-1] + (1,), jnp.float32), norms[4 + group])
        )
    fourth, unused = masked_norm_apply(branch_items, [])
    branch_act = jnp.concatenate([jax.nn.silu(kept[0]) for kept in fourth], axis=1).astype(
        jnp.bfloat16
    )
    merged_full, branch_full = (
        lax.all_gather(merged, "tensor", axis=3, tiled=True),
        lax.all_gather(branch_act, "tensor", axis=2, tiled=True),
    )
    joined = spread_bins(merged_full, branch_full, tables, images)
    pre_unite = conv_forward(joined, w_unite, 1)
    fifth, unused = masked_norm_apply([(pre_unite, inside, norms[8])], [])
    united = jax.nn.silu(fifth[0][0]).astype(jnp.bfloat16)
    logit_main, logit_aux = (
        lax.psum_scatter(
            jnp.dot(united, w_classes, preferred_element_type=jnp.float32).astype(jnp.bfloat16),
            "tensor",
            scatter_dimension=1,
            tiled=True,
        ).astype(jnp.float32),
        lax.psum_scatter(
            jnp.dot(aux_act, w_aux_classes, preferred_element_type=jnp.float32).astype(
                jnp.bfloat16
            ),
            "tensor",
            scatter_dimension=1,
            tiled=True,
        ).astype(jnp.float32),
    )
    total_valid = jnp.sum(class_pixel_counts)
    class_weight = total_valid / (NCLS * class_pixel_counts + total_valid)
    loss_weight = jnp.sum(class_pixel_counts * class_weight)
    cell_weight = jnp.sum(labels_hot * class_weight, axis=-1, keepdims=True) * counted
    band_rows = labels.shape[1] // splits
    band_start = lax.axis_index("tensor") * band_rows
    hot_band = lax.dynamic_slice_in_dim(labels_hot, band_start, band_rows, 1)
    weight_band = lax.dynamic_slice_in_dim(cell_weight, band_start, band_rows, 1)
    log_main = jax.nn.log_softmax(logit_main, axis=-1)
    log_aux = jax.nn.log_softmax(logit_aux, axis=-1)
    loss_cells = -jnp.sum(hot_band * (log_main + 0.4 * log_aux), axis=-1, keepdims=True)
    loss_local = jnp.sum(weight_band * loss_cells)
    band_main = (weight_band * (jnp.exp(log_main) - hot_band) / loss_weight).astype(jnp.bfloat16)
    band_aux = (0.4 * weight_band * (jnp.exp(log_aux) - hot_band) / loss_weight).astype(
        jnp.bfloat16
    )
    grad_main, grad_aux = (
        lax.all_gather(band_main, "tensor", axis=1, tiled=True),
        lax.all_gather(band_aux, "tensor", axis=1, tiled=True),
    )
    reduced = {}

    def settle(index, value):
        reduced[index] = value

    settle(6, jnp.einsum("ihwc,ihwk->ck", united, grad_main, preferred_element_type=jnp.float32))
    settle(8, jnp.einsum("ihwc,ihwk->ck", aux_act, grad_aux, preferred_element_type=jnp.float32))
    d_united = jnp.dot(grad_main, w_classes.T, preferred_element_type=jnp.float32) * silu_slope(
        fifth[0][0]
    )
    d_aux = jnp.dot(grad_aux, w_aux_classes.T, preferred_element_type=jnp.float32) * silu_slope(
        leading_part[2][0]
    )
    back_one, sums_one, totals_one = norm_backward([(d_united, fifth[0]), (d_aux, leading_part[2])])
    unite_shift_grad = totals_one[0]
    d_unite_pre = back_one[0].astype(jnp.bfloat16)
    d_aux_pre = back_one[1].astype(jnp.bfloat16)
    settle(5, conv_kernel_back(joined, d_unite_pre, 1))
    d_merged, d_branch = pick_bins(conv_input_back(d_unite_pre, w_unite, 1), C_OUT, tables, images)
    d_merged, d_branch = (
        lax.psum_scatter(
            d_merged.astype(jnp.bfloat16), "tensor", scatter_dimension=3, tiled=True
        ).astype(jnp.float32),
        lax.psum_scatter(
            d_branch.astype(jnp.bfloat16), "tensor", scatter_dimension=2, tiled=True
        ).astype(jnp.float32),
    )
    settle(7, conv_kernel_back(whole, d_aux_pre, 1))
    branch_back = []
    for group, bins in enumerate(BIN_COUNTS):
        piece = d_branch[:, BIN_STARTS[group] : BIN_STARTS[group] + bins * bins]
        branch_back.append((piece * silu_slope(fourth[group][0]), fourth[group]))
    back_two, sums_two, unused = norm_backward(branch_back)
    d_branch_pre = jnp.concatenate(back_two, axis=1).astype(jnp.bfloat16)
    d_branch_full = lax.all_gather(d_branch_pre, "tensor", axis=2, tiled=True)
    branch_grads = []
    for group, bins in enumerate(BIN_COUNTS):
        rows_in, cols_in, rows_pick, cols_pick, cell_count = tables[group]
        piece = d_branch_full[:, BIN_STARTS[group] : BIN_STARTS[group] + bins * bins]
        branch_grads.append(
            jnp.einsum("ipc,ipd->cd", pooled_list[group], piece, preferred_element_type=jnp.float32)
        )
        d_pooled = jnp.dot(piece, w_branch[group].T, preferred_element_type=jnp.float32).reshape(
            images, bins, bins, -1
        )
        d_merged = d_merged + jnp.einsum(
            "ikh,ilw,iklc->ihwc", rows_in, cols_in, d_pooled / cell_count
        )
    settle(4, jnp.stack(branch_grads))
    d_summed = d_merged * silu_slope(summed)
    back_three, sums_three, unused = norm_backward(
        [(d_summed, third[0]), (d_summed, leading_part[1])]
    )
    d_expand_pre = back_three[0].astype(jnp.bfloat16)
    d_short_pre = back_three[1].astype(jnp.bfloat16)
    settle(
        3,
        jnp.einsum(
            "ihwc,ihwd->cd", hidden_two_full, d_expand_pre, preferred_element_type=jnp.float32
        ),
    )
    settle(1, jnp.einsum("ihwc,ihwd->cd", whole, d_short_pre, preferred_element_type=jnp.float32))
    d_two = scatter_channels(jnp.dot(d_expand_pre, w_expand.T, preferred_element_type=jnp.float32))
    back_four, sums_four, unused = norm_backward([(d_two * silu_slope(second[0][0]), second[0])])
    d_middle_pre = back_four[0].astype(jnp.bfloat16)
    settle(2, conv_kernel_back(hidden_full, d_middle_pre, 4))
    d_one = scatter_channels(conv_input_back(d_middle_pre, w_middle, 4))
    back_five, sums_five, unused = norm_backward(
        [(d_one * silu_slope(leading_part[0][0]), leading_part[0])]
    )
    settle(
        0,
        jnp.einsum(
            "ihwc,ihwd->cd",
            whole,
            back_five[0].astype(jnp.bfloat16),
            preferred_element_type=jnp.float32,
        ),
    )
    beta_grads = (
        [sums_five[0], sums_three[2], sums_four[0], sums_three[0]]
        + [sums_two[2 * g] for g in range(4)]
        + [sums_one[0], sums_one[2]]
    )
    gamma_grads = (
        [sums_five[1], sums_three[3], sums_four[1], sums_three[1]]
        + [sums_two[2 * g + 1] for g in range(4)]
        + [sums_one[1], sums_one[3]]
    )
    settle(9, jnp.stack([jnp.concatenate(gamma_grads), jnp.concatenate(beta_grads)]))
    ordered = [reduced[index] for index in range(10)]
    grad_share = lax.psum_scatter(
        jnp.concatenate([part.reshape(owners, -1) for part in ordered], axis=1),
        "batch",
        scatter_dimension=0,
        tiled=True,
    )
    square_all, loss_sum = lax.psum(
        (jnp.sum(grad_share * grad_share), loss_local), ("batch", "tensor")
    )
    grad_norm = jnp.sqrt(square_all)
    clipped = grad_share * jnp.minimum(1.0, 0.05 / (grad_norm + 1e-06))
    new_first = 0.5 * first_moment + 0.5 * clipped
    new_second = 0.5 * squared_mean + 0.5 * clipped * clipped
    keep = 1.0 - 0.5**STEP
    new_params = params - 0.01 * (
        new_first / keep / (jnp.sqrt(new_second / keep) + 1e-08) + 0.01 * params
    )
    new_average = 0.999 * average + 0.001 * new_params
    return (
        new_params,
        new_first,
        new_second,
        new_average,
        new_params.astype(jnp.bfloat16),
        grad_norm,
        loss_sum,
        loss_weight,
        unite_shift_grad,
    )


CELLS = MAP * MAP
EDGE = 104
BATCH = "batch"
TENSOR = "tensor"
GROUP_ROWS = ((0, 1), (1, 5), (5, 14), (14, 50))
BINS = 64
BF = jnp.bfloat16
F32 = jnp.float32
MESH = pl.DeviceIdType.MESH
HALF = 4
OWNERS = 8
SPLITS = 4
MERGED = 4
SLOTS = 5


def scratch_plan():
    plan = dict(
        w_r=((1024, 128), BF),
        w_s=((1024, 512), BF),
        w_m=((4608, 128), BF),
        w_e=((512, 512), BF),
        w_b=((2048, 512), BF),
        w_u=((18432, 128), BF),
        w_own=((4608, 128), BF),
        w_a=((4608, 128), BF),
        w_pair=((1024, 640), BF),
        w_c=((128, 256), BF),
        w_ac=((64, 256), F32),
        gain_in=((OWNERS, 8, 128), F32),
        gain_rows=((40, 128), F32),
        out_a=((576, 128), F32),
        out_c=((16, 256), F32),
        out_ac=((8, 256), F32),
        whole=((SPLITS, CELLS, 256), BF),
        whole_t=((SPLITS, 256, CELLS), BF),
        w_c_all=((SPLITS, 128, 256), BF),
        slope_main=((CELLS, 256), BF),
        ins=((CELLS, 128), F32),
        col=((CELLS, 128), F32),
        lab=((CELLS, 128), F32),
        table=((BINS, CELLS), F32),
        pool=((BINS, CELLS), BF),
        pick=((BINS, CELLS), BF),
        cells_in=((BINS, 128), F32),
        pad=((9, CELLS + 2 * EDGE, 128), F32),
        grad_pad=((CELLS + 2 * EDGE, 128), F32),
        pre_r=((CELLS, 128), F32),
        pre_s=((CELLS, 512), F32),
        pre_a=((CELLS, 128), F32),
        pre_m=((CELLS, 128), F32),
        pre_e=((CELLS, 512), F32),
        pre_u=((CELLS, 128), F32),
        act_a=((CELLS, 128), BF),
        h1=((SPLITS, CELLS, 128), BF),
        h2=((SPLITS, CELLS, 128), BF),
        joined=((SPLITS, CELLS, 512), BF),
        joined_t=((SPLITS, 512, CELLS), BF),
        pooled=((BINS, 512), BF),
        pool_half=((2, BINS, 256), BF),
        pool_all=((OWNERS, BINS, 256), BF),
        d_bp_all=((OWNERS, SPLITS, BINS, 128), BF),
        part_b=((SPLITS, BINS, 128), BF),
        recv_b=((SPLITS, BINS, 128), BF),
        all_b=((OWNERS, BINS, 128), BF),
        act_b=((SPLITS, OWNERS * BINS, 128), BF),
        pick_t=((CELLS, 128), BF),
        z_cat=((9, 128, 128), BF),
        act_t=((512, OWNERS * BINS), BF),
        zsum=((2, OWNERS * BINS, 128), F32),
        z_send=((OWNERS, 2, BINS, 128), BF),
        z_recv=((OWNERS, 2, BINS, 128), BF),
        united=((SPLITS, CELLS, 128), BF),
        logit_send=((CELLS, 512), BF),
        logit_recv=((SPLITS, 144, 512), BF),
        slope_in=((SPLITS, 144, 512), BF),
        d_f=((CELLS, 128), F32),
        d_f2=((CELLS, 128), F32),
        cat_u=((CELLS, 1152), BF),
        cat_a=((CELLS, 640), BF),
        dz_send=((9, BINS, 128), BF),
        dz_recv=((OWNERS, 2, BINS, 128), BF),
        d_act_send=((SPLITS, OWNERS * BINS, 128), BF),
        d_act_recv=((SPLITS, OWNERS * BINS, 128), BF),
        d_img_send=((OWNERS, BINS, 128), BF),
        d_img_recv=((OWNERS, BINS, 128), BF),
        d_bp=((SPLITS, BINS, 128), BF),
        dm_near=((2, CELLS, 512), BF),
        dm_far=((CELLS, 512), BF),
        d_sum=((CELLS, 512), F32),
        d_e=((CELLS, 512), BF),
        d_s=((CELLS, 512), BF),
        dh_send=((SPLITS, CELLS, 128), BF),
        dh_recv=((2, SPLITS, CELLS, 128), BF),
        d_low=((CELLS, 128), BF),
        end_t=((SPLITS, 8, 128), F32),
    )
    for name, rows in SYNCS.items():
        plan["sync_" + name] = ((OWNERS, rows, 128), F32)
    for name, (rows, lanes, kind) in PARTS.items():
        plan["first_" + name] = ((HALF, rows, lanes), kind)
        plan["second_" + name] = ((HALF - 1, rows, lanes), kind)
    plan["first_u"] = ((HALF, SLOTS, 512, 128), BF)
    plan["second_u"] = ((HALF - 1, SLOTS, 512, 128), BF)
    return plan


SYNCS = dict(one=8, two=8, three=16, five=8, aux=8, b1=8, b2=8, b3=8, b4=16, b5=8, b6=8, end=8)
PARTS = dict(
    r=(128, 128, BF),
    s=(128, 512, BF),
    m=(576, 128, BF),
    e=(64, 512, BF),
    a=(576, 128, BF),
    c=(16, 256, BF),
    ac=(8, 256, F32),
)
SEMAPHORES = 1100
LOADS = (0, 128, 640, 1216, 1472, 2496, 7104, 7712)
LOAD_ORDER = (0, 2, 3, 1, 4, 6, 5)


class Refs:
    pass


def fold(value):
    return value.reshape(-1, 8, value.shape[-1]).sum(0)


def total(value):
    return jnp.sum(value, axis=0, keepdims=True)


def wide(value, times):
    return jnp.concatenate([value] * times, axis=1)


def dot(left, right):
    return jnp.dot(left, right, preferred_element_type=F32)


def dot_nt(left, right):
    return lax.dot_general(left, right, (((1,), (1,)), ((), ())), preferred_element_type=F32)


def dot_tn(left, right):
    return lax.dot_general(left, right, (((0,), (0,)), ((), ())), preferred_element_type=F32)


def loop(count, body):
    def step(k, carry):
        body(k)
        return carry

    lax.fori_loop(0, count, step, 0)


def rows_at(k, block):
    return pl.ds(pl.multiple_of(k * block, block), block)


def step_kernel(names, *refs):
    (
        sizes, lab_in, feat, flat, o_flat, o_shift, o_misc,
    ) = refs[:7]
    v = Refs()
    for name, ref in zip(names, refs[7:]):
        setattr(v, name, ref)
    sems = refs[-1]
    o_u = o_flat.at[2496:7104, :]
    me = lax.axis_index(BATCH)
    t = lax.axis_index(TENSOR)
    partner = me + 1 - 2 * lax.rem(me, 2)
    t_core = t + 1 - 2 * lax.rem(t, 2)
    t_x = lax.rem(t + 2, SPLITS)
    t_diag = lax.rem(t_core + 2, SPLITS)
    taken = [0]

    def take(count):
        start = taken[0]
        taken[0] = start + count
        assert taken[0] <= SEMAPHORES
        return start

    def far_peer(base, step):
        return lax.rem(base + 2 * step, OWNERS)

    def remote(src, dst, send, recv, device):
        return pltpu.make_async_remote_copy(
            src_ref=src,
            dst_ref=dst,
            send_sem=sems.at[send],
            recv_sem=sems.at[recv],
            device_id=device,
            device_id_type=MESH,
        )

    def mix(*lists):
        for turn in range(max(len(items) for items in lists)):
            for items in lists:
                if turn < len(items):
                    items[turn]()

    load_at = take(len(LOADS))

    def load(index):
        at = pl.ds(LOADS[index], LOADS[index + 1] - LOADS[index])
        return pltpu.make_async_copy(flat.at[at, :], o_flat.at[at, :], sems.at[load_at + index])

    for index in LOAD_ORDER:
        load(index).start()
    v.pool_all[...] = jnp.zeros((OWNERS, BINS, 256), BF)
    v.d_bp_all[...] = jnp.zeros((OWNERS, SPLITS, BINS, 128), BF)
    barrier = pltpu.get_barrier_semaphore()
    for k in range(1, OWNERS):
        pl.semaphore_signal(
            barrier, inc=1, device_id={BATCH: lax.rem(me + k, OWNERS)}, device_id_type=MESH
        )
    for k in range(1, SPLITS):
        pl.semaphore_signal(
            barrier, inc=1, device_id={TENSOR: lax.rem(t + k, SPLITS)}, device_id_type=MESH
        )
    pl.semaphore_wait(barrier, OWNERS + SPLITS - 2)

    class Gather:
        def __init__(self, full, rows, skip=0, step=None, piece=None):
            self.full, self.rows, self.piece = full, rows, piece
            self.skip, self.part = skip, step or rows
            self.near_s, self.far_s, self.pass_s = take(1), take(HALF), take(HALF)
            self.recv, self.keep = take(OWNERS), take(1)

        def at(self, owner):
            if self.rows is None:
                return self.full.at[owner]
            start = pl.multiple_of(owner * self.rows + self.skip, self.part)
            return self.full.at[pl.ds(start, self.part), :]

        def source(self):
            return self.at(me) if self.piece is None else self.piece

        def local(self):
            return pltpu.make_async_copy(self.piece, self.at(me), sems.at[self.keep])

        def near(self):
            return remote(
                self.source(), self.at(me), self.near_s, self.recv + me, {BATCH: partner}
            )

        def far(self, step):
            return remote(
                self.source(),
                self.at(me),
                self.far_s + step,
                self.recv + me,
                {BATCH: far_peer(me, step)},
            )

        def passed(self, step, base):
            source = far_peer(base, step)
            return remote(
                self.at(source),
                self.at(source),
                self.pass_s + step,
                self.recv + source,
                {BATCH: partner},
            )

        def fars(self):
            def go(step):
                if step == 1 and self.piece is not None:
                    self.local().start()
                self.far(step).start()

            return [functools.partial(go, step) for step in range(1, HALF)]

        def nears(self):
            return [lambda: self.near().start()]

        def passes(self):
            def go(step):
                self.passed(step, me).wait_recv()
                self.passed(step, me).start()

            return [functools.partial(go, step) for step in range(1, HALF)]

        def finish(self):
            for step in range(HALF):
                self.passed(step, partner).wait_recv()
            if self.piece is not None:
                self.local().wait()
            self.near().wait_send()
            for step in range(1, HALF):
                self.far(step).wait_send()

        def drain(self):
            for step in range(1, HALF):
                self.passed(step, me).wait_send()

    g_gain = Gather(v.gain_in, None, piece=flat.at[7704:7712, :])
    g_r = Gather(v.w_r, 128)
    g_s = Gather(v.w_s, 128)
    g_a = Gather(v.w_a, 576)
    g_m = Gather(v.w_m, 576)
    g_e = Gather(v.w_e, 64)
    g_b0 = Gather(v.w_b, 256, 0, 128)
    g_b1 = Gather(v.w_b, 256, 128, 128)
    g_c = Gather(v.w_c, 16)
    g_ac = Gather(v.w_ac, 8)

    def block_of(owner, slot):
        return 8 if slot == SLOTS - 1 else lax.rem(slot - owner + 8, 8)

    def merged_rows(owner, slot):
        block = owner * 9 + block_of(owner, slot)
        index = lax.div(block, 8) * MERGED + lax.rem(block, 8)
        return pl.ds(pl.multiple_of(index * 512, 512), 512)

    def has(owner, slot, body):
        if slot == SLOTS - 1:
            pl.when(owner < MERGED)(body)
        else:
            body()

    class GatherUnite:
        def __init__(self):
            self.near_s, self.far_s, self.pass_s = (
                take(SLOTS),
                take(SLOTS * HALF),
                take(SLOTS * HALF),
            )
            self.recv, self.keep = take(SLOTS * OWNERS), take(SLOTS)

        def source(self, slot):
            return v.w_own.at[rows_at(block_of(me, slot), 512), :]

        def full(self, owner, slot):
            return v.w_u.at[merged_rows(owner, slot), :]

        def local(self, slot):
            return pltpu.make_async_copy(
                self.source(slot), self.full(me, slot), sems.at[self.keep + slot]
            )

        def near(self, slot):
            return remote(
                self.source(slot),
                self.full(me, slot),
                self.near_s + slot,
                self.recv + me * SLOTS + slot,
                {BATCH: partner},
            )

        def far(self, step, slot):
            return remote(
                self.source(slot),
                self.full(me, slot),
                self.far_s + step * SLOTS + slot,
                self.recv + me * SLOTS + slot,
                {BATCH: far_peer(me, step)},
            )

        def passed(self, step, slot, base):
            source = far_peer(base, step)
            return remote(
                self.full(source, slot),
                self.full(source, slot),
                self.pass_s + step * SLOTS + slot,
                self.recv + source * SLOTS + slot,
                {BATCH: partner},
            )

        def fars(self, slot):
            def go(step):
                if step == 1:
                    self.local(slot).start()
                self.far(step, slot).start()

            return [
                functools.partial(has, me, slot, functools.partial(go, step))
                for step in range(1, HALF)
            ]

        def nears(self, slot):
            return [lambda: has(me, slot, lambda: self.near(slot).start())]

        def passes(self, slot):
            def go(step):
                self.passed(step, slot, me).wait_recv()
                self.passed(step, slot, me).start()

            return [
                functools.partial(has, far_peer(me, step), slot, functools.partial(go, step))
                for step in range(1, HALF)
            ]

        def finish(self, slots):
            for slot in slots:
                for step in range(HALF):
                    has(
                        far_peer(partner, step),
                        slot,
                        lambda step=step, slot=slot: self.passed(step, slot, partner).wait_recv(),
                    )

                def end(slot=slot):
                    self.local(slot).wait()
                    self.near(slot).wait_send()
                    for step in range(1, HALF):
                        self.far(step, slot).wait_send()

                has(me, slot, end)

        def drain(self):
            for slot in range(SLOTS):
                for step in range(1, HALF):
                    has(
                        far_peer(me, step),
                        slot,
                        lambda step=step, slot=slot: self.passed(step, slot, me).wait_send(),
                    )

    g_u = GatherUnite()

    class Sync:
        def __init__(self, buf):
            self.buf = buf
            self.send, self.recv = take(OWNERS), take(OWNERS)

        def copy(self, k, slot):
            return remote(
                self.buf.at[slot],
                self.buf.at[slot],
                self.send + k,
                self.recv + slot,
                {BATCH: lax.rem(me + k, OWNERS)},
            )

        def start(self, rows):
            for index, row in enumerate(rows):
                self.buf[me, index : index + 1, :] = row
            for index in range(len(rows), self.buf.shape[1]):
                self.buf[me, index : index + 1, :] = jnp.zeros((1, 128), F32)
            for k in range(1, OWNERS):
                self.copy(k, me).start()

        def wait(self):
            for k in range(1, OWNERS):
                self.copy(k, lax.rem(me + k, OWNERS)).wait_recv()
            for k in range(1, OWNERS):
                self.copy(k, me).wait_send()
            value = self.buf[0]
            for slot in range(1, OWNERS):
                value = value + self.buf[slot]
            return value

    class ToGroup:
        def __init__(self, part, into):
            self.part, self.into = part, into
            self.send, self.recv = take(OWNERS), take(OWNERS)

        def each(self, k, owner, slot, act):
            for rows, fits_ in ((16, owner < 6), (BINS, owner >= 6)):

                def go(rows=rows):
                    act(
                        remote(
                            self.part(owner, rows),
                            self.into(slot, rows),
                            self.send + k,
                            self.recv + slot,
                            {BATCH: lax.rem(me + k, OWNERS)},
                        )
                    )

                pl.when(fits_)(go)

        def start(self):
            for k in range(1, OWNERS):
                self.each(k, lax.rem(me + k, OWNERS), me, lambda c: c.start())

        def wait(self):
            for k in range(1, OWNERS):
                self.each(k, me, lax.rem(me + k, OWNERS), lambda c: c.wait_recv())
            for k in range(1, OWNERS):
                self.each(k, lax.rem(me + k, OWNERS), me, lambda c: c.wait_send())

    class Spread:

        def __init__(self, buf, lanes_=None):
            self.buf, self.lanes = buf, lanes_
            self.send, self.recv = take(SPLITS), take(SPLITS)

        def view(self, slot):
            return self.buf.at[slot] if self.lanes is None else self.buf.at[slot, :, self.lanes]

        def copy(self, k, slot):
            return remote(
                self.view(slot),
                self.view(slot),
                self.send + k,
                self.recv + slot,
                {TENSOR: lax.rem(t + k, SPLITS)},
            )

        def start(self):
            for k in range(1, SPLITS):
                self.copy(k, t).start()

        def wait(self):
            for k in range(1, SPLITS):
                self.copy(k, lax.rem(t + k, SPLITS)).wait_recv()
            for k in range(1, SPLITS):
                self.copy(k, t).wait_send()

    class Exchange:

        def __init__(self, axis, count, part, into):
            self.axis, self.count, self.part, self.into = axis, count, part, into
            self.mine = me if axis == BATCH else t
            self.send, self.recv = take(count), take(count)

        def copy(self, k, slot):
            other = lax.rem(self.mine + k, self.count)
            return remote(
                self.part(other),
                self.into(slot),
                self.send + k,
                self.recv + slot,
                {self.axis: other},
            )

        def start(self):
            for k in range(1, self.count):
                self.copy(k, self.mine).start()

        def wait(self):
            for k in range(1, self.count):
                self.copy(k, lax.rem(self.mine + k, self.count)).wait_recv()
            for k in range(1, self.count):
                self.copy(k, self.mine).wait_send()

    feat_keep = take(1)
    feat_local = pltpu.make_async_copy(feat, v.whole.at[t], sems.at[feat_keep])
    feat_s, feat_r = take(3), take(SPLITS)

    def feat_copy(k, slot, device):
        source = feat if k < 2 else v.whole.at[slot]
        return remote(source, v.whole.at[slot], feat_s + k, feat_r + slot, {TENSOR: device})

    def wide_rows(into, rows, low):
        for k in range(4):
            value = o_flat[pl.ds(low + k, rows, stride=4), :]
            into[rows_at(me, rows), k * 128 : k * 128 + 128] = value.astype(BF)

    load(0).wait()
    v.w_r[rows_at(me, 128), :] = o_flat[0:128, :].astype(BF)
    mix(g_r.nears() + g_gain.nears(), g_r.fars() + g_gain.fars())
    feat_local.start()
    feat_copy(0, t, t_x).start()
    feat_copy(1, t, t_core).start()
    load(2).wait()
    v.w_m[rows_at(me, 576), :] = o_flat[640:1216, :].astype(BF)
    load(3).wait()
    wide_rows(v.w_e, 64, 1216)
    mix(g_m.nears() + g_e.nears(), g_m.fars() + g_e.fars())
    lane = lax.broadcasted_iota(jnp.int32, (1, 128), 1)

    def roll(value, shift):
        return pltpu.roll(value, shift % 128, 1) if shift % 128 else value

    high, across = sizes[0, 0], sizes[0, 1]
    place = lax.broadcasted_iota(jnp.int32, (CELLS, 128), 0).astype(F32)
    row_of = jnp.floor((place + 0.5) / MAP)
    col_of = place - MAP * row_of
    within = (row_of < high.astype(F32)) & (col_of < across.astype(F32))
    v.ins[...] = jnp.where(within, 1.0, 0.0)
    v.col[...] = col_of
    v.lab[...] = jnp.where(within, lab_in[...], -1.0)
    v.table[...] = jnp.zeros((BINS, CELLS), F32)
    lane_place = lax.broadcasted_iota(jnp.int32, (1, CELLS), 1).astype(F32)
    lane_row = jnp.floor((lane_place + 0.5) / MAP)
    lane_col = lane_place - MAP * lane_row

    def ranges(extent, bins, where):
        inside, chosen, counts = [], [], []
        for k in range(bins):
            low = lax.div(k * extent, bins)
            top = lax.div((k + 1) * extent + (bins - 1), bins)
            member = (where >= low.astype(F32)) & (where < top.astype(F32))
            inside.append(jnp.where(member, 1.0, 0.0))
            picked = where * bins >= (k * extent).astype(F32)
            if k < bins - 1:
                picked = picked & (where * bins < ((k + 1) * extent).astype(F32))
            chosen.append(jnp.where(picked, 1.0, 0.0))
            counts.append(top - low)
        return inside, chosen, counts

    picks = []
    v.cells_in[...] = jnp.ones((BINS, 128), F32)
    for group, bins in enumerate(BIN_COUNTS):
        r_in, r_pick, r_count = ranges(high, bins, lane_row)
        c_in, c_pick, c_count = ranges(across, bins, lane_col)
        for a in range(bins):
            for b in range(bins):
                spot = BIN_STARTS[group] + a * bins + b
                v.table[spot : spot + 1, :] = r_in[a] * c_in[b]
                v.cells_in[spot : spot + 1, :] = jnp.full(
                    (1, 128), (r_count[a] * c_count[b]).astype(F32)
                )
                picks.append((spot, r_pick[a] * c_pick[b]))
    v.pool[...] = v.table[...].astype(BF)
    for spot, value in picks:
        v.table[spot : spot + 1, :] = value
    v.pick[...] = v.table[...].astype(BF)
    v.pick_t[...] = jnp.concatenate([v.pick[...], v.pick[...]], axis=0).T
    zeros_edge = jnp.zeros((EDGE, 128), F32)
    for tap in range(9):
        v.pad[tap, 0:EDGE, :] = zeros_edge
        v.pad[tap, EDGE + CELLS :, :] = zeros_edge
    v.grad_pad[0:EDGE, :] = zeros_edge
    v.grad_pad[EDGE + CELLS :, :] = zeros_edge
    lanes = lax.broadcasted_iota(jnp.int32, (1, 256), 1).astype(F32)
    counts = jnp.zeros((8, 256), F32)
    for k in range(0, CELLS, 96):
        counts = counts + fold(
            jnp.where(wide(v.lab[k : k + 96, :], 2) == lanes, 1.0, 0.0)
        )
    class_local = total(counts)
    cells_local = jnp.full((1, 128), (high * across).astype(F32))
    left_half = lax.broadcasted_iota(jnp.int32, (64, 128), 1) < 64

    mix(g_r.passes() + g_gain.passes())
    feat_copy(0, t_x, t_x).wait_recv()
    feat_copy(2, t_x, t_core).start()
    load(1).wait()
    wide_rows(v.w_s, 128, 128)
    load(4).wait()
    wide_rows(v.w_b, 256, 1472)
    load(6).wait()
    before = pltpu.roll(o_flat[7122:7698, :], 32, 1)
    after = pltpu.roll(o_flat[7123:7699, :], 32, 1)
    v.w_a[rows_at(me, 576), :] = jnp.where(lane < 32, before, after).astype(BF)

    def class_rows(count, base, into):
        for row in range(count):
            first, shift = divmod(base + NCLS * row, 128)
            three = [
                roll(o_flat[7104 + first + k : 7105 + first + k, :], 128 - shift) for k in range(3)
            ]
            into[row : row + 1, :128] = jnp.where(lane < 128 - shift, three[0], three[1])
            high_half = jnp.where(lane < 128 - shift, three[1], three[2])
            into[row : row + 1, 128:] = jnp.where(lane < NCLS - 128, high_half, 0.0)

    class_rows(16, 0, v.out_c)
    class_rows(8, 76128, v.out_ac)
    v.w_c[rows_at(me, 16), :] = v.out_c[...].astype(BF)
    v.w_ac[rows_at(me, 8), :] = v.out_ac[...].astype(BF).astype(F32)
    load(5).wait()

    def own_rows(j):
        at = pl.ds(pl.multiple_of(2496 + 512 * j, 64), 512)
        v.w_own[rows_at(j, 512), :] = o_flat[at, :].astype(BF)

    loop(9, own_rows)
    for item in (g_gain, g_r):
        item.finish()
    feat_local.wait()
    feat_copy(1, t_core, t_core).wait_recv()
    feat_copy(2, t_diag, t_core).wait_recv()
    feat_copy(0, t, t_x).wait_send()
    feat_copy(1, t, t_core).wait_send()
    feat_copy(2, t_x, t_core).wait_send()
    gain_of = [None] * 33
    for owner in range(OWNERS):
        start = 496 * (owner % 4) - 16
        first, shift = start // 128, start % 128
        for k in range(4):
            value = v.gain_in[owner, 4 + k : 5 + k, :].astype(BF).astype(F32)
            if k == 0:
                value = jnp.where(lane < 16, 0.0, value)
            value = roll(value, shift)
            spot = 16 * (owner // 4) + first + k
            for where, part in (
                (spot, jnp.where(lane >= shift, value, 0.0)),
                (spot + 1, jnp.where(lane < shift, value, 0.0)),
            ):
                gain_of[where] = part if gain_of[where] is None else gain_of[where] + part

    def gamma(row, width=1):
        return jnp.concatenate([gain_of[row + k] for k in range(width)], axis=1)

    def beta(row, width=1):
        return gamma(16 + row, width)

    def whole_feat():
        return jnp.concatenate([v.whole[k] for k in range(SPLITS)], axis=1)

    v.pre_r[...] = dot(whole_feat(), v.w_r[...])
    def offset(tap, spacing):
        return ((tap // 3 - 1) * MAP + (tap % 3 - 1)) * spacing

    def col_mask(at, right):
        where = v.col[at, :] + float(right)
        return jnp.where((where >= 0.0) & (where < float(MAP)), 1.0, 0.0)

    BLOCK = 72

    def shift_sum(taps, spacing, at, slot_of):
        out = None
        for b in (-1, 0, 1):
            part = None
            for tap in taps:
                if tap % 3 - 1 != b:
                    continue
                start = EDGE + at + offset(tap, spacing)
                value = v.pad[slot_of(tap), start : start + BLOCK, :]
                part = value if part is None else part + value
            if part is None:
                continue
            if b:
                part = part * col_mask(slice(at, at + BLOCK), b * spacing)
            out = part if out is None else out + part
        return out

    def masked_sums(ref):
        width = ref.shape[1]

        def step(k, carry):
            at = rows_at(k, 96)
            value = ref[at, :]
            kept = value * (v.ins[at, :] if width == 128 else wide(v.ins[at, :], width // 128))
            return (carry[0] + fold(kept), carry[1] + fold(kept * value))

        zero = jnp.zeros((8, width), F32)
        sums = lax.fori_loop(0, 6, step, (zero, zero))
        return total(sums[0]), total(sums[1])

    def split_rows(value):
        return [value[:, k : k + 128] for k in range(0, value.shape[1], 128)]

    def join_rows(value, row, count):
        return jnp.concatenate([value[row + k : row + k + 1] for k in range(count)], axis=1)

    def moments(first, second, count):
        mean = first / count
        return mean, lax.rsqrt(second / count - mean * mean + 1e-05)

    sync = Sync(v.sync_one)
    r1, r2 = masked_sums(v.pre_r)
    sync.start([r1, r2, cells_local] + split_rows(class_local))
    mix(g_m.passes() + g_e.passes(), g_s.fars())
    sums = sync.wait()
    count = sums[2:3]
    count4 = wide(count, 4)
    norm_r = moments(sums[0:1], sums[1:2], count)
    class_count = join_rows(sums, 3, 2)

    def normed(ref, at, norm):
        return (ref[at, :] - norm[0]) * norm[1]

    spread_1 = Spread(v.h1)

    def make_h1(k):
        at = rows_at(k, 96)
        v.h1[t, at, :] = jax.nn.silu(gamma(0) * normed(v.pre_r, at, norm_r) + beta(0)).astype(BF)

    loop(6, make_h1)
    spread_1.start()
    mix(g_s.nears(), g_b0.fars())
    g_m.finish()
    spread_1.wait()

    def full_h(ref):
        return jnp.concatenate([ref[k] for k in range(SPLITS)], axis=1)

    def w_middle(tap):
        return v.w_m[rows_at(tap, 512), :]

    def middle_pair(p):
        both = jnp.concatenate([w_middle(2 * p), w_middle(2 * p + 1)], axis=1)
        value = dot(full_h(v.h1), both)
        v.pad[2 * p, EDGE : EDGE + CELLS, :] = value[:, :128]
        v.pad[2 * p + 1, EDGE : EDGE + CELLS, :] = value[:, 128:]

    loop(4, middle_pair)
    v.pad[8, EDGE : EDGE + CELLS, :] = dot(full_h(v.h1), w_middle(8))
    for at in range(0, CELLS, BLOCK):
        v.pre_m[at : at + BLOCK, :] = shift_sum(range(9), 4, at, lambda tap: tap)
    sync = Sync(v.sync_two)
    sync.start(list(masked_sums(v.pre_m)))
    mix(g_s.passes() + g_b0.nears(), g_b1.fars())
    sums = sync.wait()
    norm_m = moments(sums[0:1], sums[1:2], count)
    spread_2 = Spread(v.h2)

    def make_h2(k):
        at = rows_at(k, 96)
        v.h2[t, at, :] = jax.nn.silu(gamma(5) * normed(v.pre_m, at, norm_m) + beta(5)).astype(BF)

    loop(6, make_h2)
    spread_2.start()
    mix(g_b0.passes() + g_b1.nears(), g_u.fars(0))
    g_e.finish()
    g_s.finish()
    for k in range(0, 512, 256):
        v.pre_s[:, k : k + 256] = dot(whole_feat(), v.w_s[:, k : k + 256])
    s1, s2 = masked_sums(v.pre_s)
    spread_2.wait()
    for k in range(0, 512, 256):
        v.pre_e[:, k : k + 256] = dot(full_h(v.h2), v.w_e[:, k : k + 256])
    sync = Sync(v.sync_three)
    e1, e2 = masked_sums(v.pre_e)
    sync.start(split_rows(e1) + split_rows(e2) + split_rows(s1) + split_rows(s2))
    mix(g_b1.passes() + g_u.nears(0), g_u.fars(1))
    mix(g_c.nears() + g_ac.nears(), g_c.fars() + g_ac.fars())
    sums = sync.wait()
    norm_e = moments(join_rows(sums, 0, 4), join_rows(sums, 4, 4), count4)
    norm_s = moments(join_rows(sums, 8, 4), join_rows(sums, 12, 4), count4)

    def summed(at):
        return (
            gamma(6, 4) * normed(v.pre_e, at, norm_e)
            + beta(6, 4)
            + gamma(1, 4) * normed(v.pre_s, at, norm_s)
            + beta(1, 4)
        )

    def make_merged(k):
        at = rows_at(k, 48)
        v.joined[t, at, :] = jax.nn.silu(summed(at)).astype(BF)

    loop(12, make_merged)

    j_send, j_recv = take(3), take(SPLITS)

    def joined_copy(k, slot, device):
        return remote(
            v.joined.at[slot], v.joined.at[slot], j_send + k, j_recv + slot, {TENSOR: device}
        )

    joined_copy(0, t, t_x).start()
    joined_copy(1, t, t_core).start()

    pool_move = ToGroup(
        lambda owner, rows: v.pool_half.at[lax.rem(owner, 2), 0:rows, :],
        lambda slot, rows: v.pool_all.at[slot, 0:rows, :],
    )
    bin_row = lax.broadcasted_iota(jnp.int32, (BINS, 1), 0)

    def group_mask(group, shape=None):
        low, top = GROUP_ROWS[group]
        kept = jnp.where((bin_row >= low) & (bin_row < top), 1.0, 0.0)
        return kept if shape is None else jnp.broadcast_to(kept, shape)

    cells_in = wide(v.cells_in[...], 4)
    pooled = dot(v.pool[...], v.joined[t]) / cells_in
    v.pooled[...] = pooled.astype(BF)
    for k in range(2):
        v.pool_half[k] = v.pooled[:, k * 256 : k * 256 + 256]
    v.pool_all[me] = v.pool_half[lax.rem(me, 2)]
    g_b0.finish()
    g_b1.finish()
    part = jnp.zeros((BINS, 512), F32)
    for group in range(4):
        rows = (v.pooled[...].astype(F32) * group_mask(group)).astype(BF)
        part = part + dot(rows, v.w_b[group * 512 : group * 512 + 512, :])
    for k in range(SPLITS):
        v.part_b[k] = part[:, k * 128 : k * 128 + 128].astype(BF)
    v.recv_b[t] = v.part_b[t]
    ex = Exchange(TENSOR, SPLITS, lambda o: v.part_b.at[o], lambda s: v.recv_b.at[s])
    ex.start()
    mix(g_u.passes(0) + g_u.nears(1), g_u.fars(2))
    joined_copy(0, t_x, t_x).wait_recv()
    joined_copy(2, t_x, t_core).start()
    ex.wait()
    own_b = v.recv_b[0].astype(F32)
    for k in range(1, SPLITS):
        own_b = own_b + v.recv_b[k].astype(F32)
    v.all_b[me] = own_b.astype(BF)
    ex = Exchange(BATCH, OWNERS, lambda o: v.all_b.at[me], lambda s: v.all_b.at[s])
    ex.start()
    mix(g_u.passes(1) + g_u.nears(2), g_u.fars(4))
    ex.wait()
    all_b = [v.all_b[k].astype(F32) for k in range(OWNERS)]
    sum_b, square_b = all_b[0], all_b[0] * all_b[0]
    for k in range(1, OWNERS):
        sum_b = sum_b + all_b[k]
        square_b = square_b + all_b[k] * all_b[k]
    mean_b = jnp.zeros((BINS, 128), F32)
    scale_b = jnp.zeros((BINS, 128), F32)
    gamma_b = jnp.zeros((BINS, 128), F32)
    beta_b = jnp.zeros((BINS, 128), F32)
    count_b = jnp.zeros((BINS, 1), F32)
    for group, bins in enumerate(BIN_COUNTS):
        kept = group_mask(group)
        size = float(OWNERS * bins * bins)
        mean, scaling = moments(total(sum_b * kept), total(square_b * kept), size)
        mean_b = mean_b + kept * mean
        scale_b = scale_b + kept * scaling
        gamma_b = gamma_b + kept * gamma(10 + group)
        beta_b = beta_b + kept * beta(10 + group)
        count_b = count_b + kept / size
    spread_b = Spread(v.act_b)
    for k in range(OWNERS):
        out = gamma_b * ((all_b[k] - mean_b) * scale_b) + beta_b
        v.act_b[t, k * BINS : k * BINS + BINS, :] = jax.nn.silu(out).astype(BF)
    spread_b.start()
    mix(g_u.passes(2) + g_u.nears(4), g_u.fars(3))
    spread_b.wait()
    row_512 = lax.broadcasted_iota(jnp.int32, (OWNERS * BINS, 1), 0) & (BINS - 1)
    group_id = jnp.where(
        row_512 < 1, 0, jnp.where(row_512 < 5, 1, jnp.where(row_512 < 14, 2, jnp.where(row_512 < 50, 3, 9)))
    )

    def full_act():
        return jnp.concatenate([v.act_b[k] for k in range(SPLITS)], axis=1)

    v.zsum[...] = jnp.zeros((2, OWNERS * BINS, 128), F32)

    def own_branch(j, body):
        chunk = lax.rem(me + j, 8)
        pl.when(chunk >= MERGED)(lambda: body(chunk - MERGED, lax.div(me + j, 8)))

    def make_z(j):
        def body(group, side):
            kept = jnp.where(group_id == group, 1.0, 0.0)
            v.zsum[side] = v.zsum[side] + kept * dot(full_act(), v.w_own[rows_at(j, 512), :])

        own_branch(j, body)

    loop(9, make_z)
    for k in range(OWNERS):
        for side in range(2):
            v.z_send[k, side] = v.zsum[side, k * BINS : k * BINS + BINS, :].astype(BF)
    v.z_recv[me] = v.z_send[me]
    ex = Exchange(BATCH, OWNERS, lambda o: v.z_send.at[o], lambda s: v.z_recv.at[s])
    ex.start()
    mix(g_u.passes(4) + g_u.nears(3))
    v.act_t[...] = full_act().T
    joined_copy(1, t_core, t_core).wait_recv()
    joined_copy(2, t_diag, t_core).wait_recv()
    for k in range(SPLITS):
        v.joined_t[k] = v.joined[k].T
    mix(g_u.passes(3) + g_c.passes() + g_ac.passes())
    ex.wait()
    g_u.finish((0, 1, 2, 4))

    def tap_z(tap):
        if tap == 0:
            return v.z_recv[0, 0].astype(F32)
        if tap == 8:
            return v.z_recv[7, 1].astype(F32)
        return v.z_recv[tap, 0].astype(F32) + v.z_recv[tap - 1, 1].astype(F32)

    for tap in range(9):
        z = tap_z(tap)
        high_z = z.astype(BF)
        v.z_cat[tap, :BINS, :] = high_z
        v.z_cat[tap, BINS:, :] = (z - high_z.astype(F32)).astype(BF)

    def most_joined():
        return jnp.concatenate([v.joined[k] for k in range(3)], axis=1)

    def rest_joined():
        return jnp.concatenate([v.joined[3], v.pick_t[...]], axis=1)

    def most_weight(tap):
        return v.w_u[pl.ds(pl.multiple_of(tap * 2048, 512), 1536), :]

    def rest_weight(tap):
        last = v.w_u[pl.ds(pl.multiple_of(tap * 2048 + 1536, 512), 512), :]
        return jnp.concatenate([last, v.z_cat[tap]], axis=0)

    inner = slice(EDGE, EDGE + CELLS)

    def most_pair(p):
        both = jnp.concatenate([most_weight(2 * p), most_weight(2 * p + 1)], axis=1)
        value = dot(most_joined(), both)
        v.pad[2 * p, inner, :] = value[:, :128]
        v.pad[2 * p + 1, inner, :] = value[:, 128:]

    def rest_pair(p):
        both = jnp.concatenate([rest_weight(2 * p), rest_weight(2 * p + 1)], axis=1)
        value = dot(rest_joined(), both)
        v.pad[2 * p, inner, :] = v.pad[2 * p, inner, :] + value[:, :128]
        v.pad[2 * p + 1, inner, :] = v.pad[2 * p + 1, inner, :] + value[:, 128:]

    loop(4, most_pair)
    v.pad[8, inner, :] = dot(most_joined(), most_weight(8))
    g_u.finish((3,))
    loop(4, rest_pair)
    v.pad[8, inner, :] = v.pad[8, inner, :] + dot(rest_joined(), rest_weight(8))
    for at in range(0, CELLS, BLOCK):
        v.pre_u[at : at + BLOCK, :] = shift_sum(range(9), 1, at, lambda tap: tap)
    sync = Sync(v.sync_five)
    sync.start(list(masked_sums(v.pre_u)))
    pool_move.start()
    mix(g_a.nears(), g_a.fars())
    for item in (g_c, g_ac):
        item.finish()
    v.w_c_all[t] = v.w_c[...]
    spread_c = Spread(v.w_c_all)
    spread_c.start()
    for k in range(SPLITS):
        v.whole_t[k] = v.whole[k].T
    for item in (g_gain, g_r, g_s, g_m, g_e, g_b0, g_b1, g_c, g_ac, g_u):
        item.drain()
    joined_copy(0, t, t_x).wait_send()
    joined_copy(1, t, t_core).wait_send()
    joined_copy(2, t_x, t_core).wait_send()
    w_ac = jnp.concatenate([v.w_ac[...], jnp.zeros((64, 256), F32)], axis=0).astype(BF)
    sums = sync.wait()
    norm_u = moments(sums[0:1], sums[1:2], count)

    def make_u(k):
        at = rows_at(k, 96)
        v.united[t, at, :] = jax.nn.silu(gamma(14) * normed(v.pre_u, at, norm_u) + beta(14)).astype(BF)

    loop(6, make_u)
    spread_u = Spread(v.united)
    spread_u.start()
    class Band:
        def __init__(self, at):
            self.at = at
            self.ex = Exchange(
                TENSOR,
                SPLITS,
                lambda o: v.logit_send.at[rows_at(o, 144), at],
                lambda s: v.logit_recv.at[s, :, at],
            )
            self.back = Spread(v.slope_in, at)

        def start(self, value):
            v.logit_send[:, self.at] = value.astype(BF)
            self.ex.start()
            v.logit_recv[t, :, self.at] = v.logit_send[rows_at(t, 144), self.at]

        def finish(self, factor):
            self.ex.wait()
            logits = v.logit_recv[0, :, self.at].astype(F32)
            for k in range(1, SPLITS):
                logits = logits + v.logit_recv[k, :, self.at].astype(F32)
            loss_rows, grad = soft_loss(logits, rows_at(t, 144), factor)
            v.slope_in[t, :, self.at] = grad
            self.back.start()
            loss_rows = total(loss_rows)
            return loss_rows[:, :128] + loss_rows[:, 128:]

        def grad(self):
            self.back.wait()
            return v.slope_in[:, :, self.at].reshape(CELLS, 256)

    def class_weights():
        total_valid = jnp.sum(class_count, axis=1, keepdims=True)
        weight = total_valid / (NCLS * class_count + total_valid)
        whole = jnp.sum(class_count * weight, axis=1, keepdims=True)
        return jnp.where(lanes < float(NCLS), weight, 0.0), whole

    def soft_loss(logits, at, factor):
        class_weight, loss_weight = class_weights()
        hot = jnp.where(wide(v.lab[at, :], 2) == lanes, 1.0, 0.0)
        cell_weight = factor * jnp.sum(hot * class_weight, axis=1, keepdims=True)
        value = jnp.where(lanes < float(NCLS), logits, -1e30)
        value = value - jnp.max(value, axis=1, keepdims=True)
        powers = jnp.exp(value)
        mass = jnp.sum(powers, axis=1, keepdims=True)
        grad = cell_weight * (powers / mass - hot) / loss_weight
        return fold(-cell_weight * hot * (value - jnp.log(mass))), grad.astype(BF)

    aux_head = Band(slice(256, 512))
    mix(g_a.passes())
    spread_c.wait()

    g_a.finish()
    g_a.drain()

    def unpack(chunk):
        for pair in range(5):
            even = v.w_a[rows_at(2 * pair * 8 + chunk, 64), :].astype(F32)
            if pair < 4:
                odd = v.w_a[rows_at((2 * pair + 1) * 8 + chunk, 64), :].astype(F32)
            else:
                odd = jnp.zeros((64, 128), F32)
            low = jnp.where(left_half, even, pltpu.roll(odd, 64, 1))
            top = jnp.where(left_half, pltpu.roll(even, 64, 1), odd)
            v.pad[pair, pl.ds(EDGE, 64, stride=2), :] = low
            v.pad[pair, pl.ds(EDGE + 1, 64, stride=2), :] = top
            both = v.pad[pair, EDGE : EDGE + 128, :]
            v.w_pair[rows_at(chunk, 128), pair * 128 : pair * 128 + 128] = both.astype(BF)

    loop(8, unpack)

    for pair in (0, 2):
        value = dot(whole_feat(), v.w_pair[:, pair * 128 : pair * 128 + 256])
        v.pad[pair, EDGE : EDGE + CELLS, :] = value[:, :128]
        v.pad[pair + 1, EDGE : EDGE + CELLS, :] = value[:, 128:]
    v.pad[4, EDGE : EDGE + CELLS, :] = dot(whole_feat(), v.w_pair[:, 512:640])

    left_wide = lax.broadcasted_iota(jnp.int32, (BLOCK, 128), 1) < 64
    for at in range(0, CELLS, BLOCK):
        even = shift_sum((0, 2, 4, 6, 8), 1, at, lambda tap: tap // 2)
        odd = shift_sum((1, 3, 5, 7), 1, at, lambda tap: tap // 2)
        v.pre_a[at : at + BLOCK, :] = jnp.where(left_wide, even + pltpu.roll(odd, 64, 1), 0.0)

    sync_a = Sync(v.sync_aux)
    sync_a.start(list(masked_sums(v.pre_a)))
    spread_u.wait()
    weight_c = v.w_c_all[...].reshape(512, 256)

    def main_loss(k, carry):
        at = rows_at(k, 144)
        rows = jnp.concatenate([v.united[slot, at, :] for slot in range(SPLITS)], axis=1)
        loss_rows, grad = soft_loss(dot(rows, weight_c), at, 1.0)
        v.slope_main[at, :] = grad
        return carry + loss_rows

    loss_rows = total(lax.fori_loop(0, 4, main_loss, jnp.zeros((8, 256), F32)))
    o_misc[1:2, :] = (loss_rows[:, :128] + loss_rows[:, 128:]) / SPLITS
    g_main = v.slope_main[...]
    v.d_f[...] = dot_nt(g_main, v.w_c[...])

    def slope(value):
        gate = jax.nn.sigmoid(value)
        return gate * (1.0 + value * (1.0 - gate))

    def through_silu(ref, pre, norm, row):
        def step(k, carry):
            at = rows_at(k, 96)
            unit = normed(pre, at, norm)
            value = ref[at, :] * slope(gamma(row) * unit + beta(row))
            ref[at, :] = value
            return (carry[0] + fold(value), carry[1] + fold(value * unit))

        zero = jnp.zeros((8, 128), F32)
        sums = lax.fori_loop(0, 6, step, (zero, zero))
        return [total(sums[0]), total(sums[1])]

    def back_norm(value, unit, mask, norm, gain, first, second, size):
        inner = value - mask * (first + unit * second) / size
        return gain * norm[1] * inner

    gain_grads = {}
    sync = Sync(v.sync_b1)
    sync.start(through_silu(v.d_f, v.pre_u, norm_u, 14))
    sums = sync_a.wait()
    norm_a = moments(sums[0:1], sums[1:2], count)

    def make_a(k):
        at = rows_at(k, 96)
        v.act_a[at, :] = jax.nn.silu(gamma(15) * normed(v.pre_a, at, norm_a) + beta(15)).astype(BF)

    loop(6, make_a)
    aux_head.start(dot(v.act_a[...], w_ac))

    class Scatter:
        def __init__(self, first, second, full, rows, out, base=0):
            self.full, self.rows, self.out, self.base = full, rows, out, base
            self.first, self.second = first, second
            self.near_s, self.near_r = take(HALF), take(HALF)
            self.far_s, self.far_r = take(HALF), take(HALF)
            self.block = min(rows, 64)

        def near(self, step):
            dest = far_peer(partner, step)
            return remote(
                self.full.at[rows_at(dest, self.rows), :],
                self.first.at[step],
                self.near_s + step,
                self.near_r + step,
                {BATCH: partner},
            )

        def far(self, step):
            return remote(
                self.first.at[step],
                self.second.at[step - 1],
                self.far_s + step,
                self.far_r + step,
                {BATCH: far_peer(me, step)},
            )

        def starts(self):
            return [lambda step=step: self.near(step).start() for step in (1, 2, 3, 0)]

        def middles(self):
            def go(step):
                self.near(step).wait_recv()
                base = far_peer(me, step) * (self.rows // self.block)

                def add(k):
                    at = rows_at(k, self.block)
                    value = self.full[rows_at(base + k, self.block), :].astype(F32)
                    value = value + self.first[step, at, :].astype(F32)
                    self.first[step, at, :] = value.astype(self.first.dtype)

                loop(self.rows // self.block, add)
                self.far(step).start()

            return [functools.partial(go, step) for step in range(1, HALF)]

        def end(self):
            self.near(0).wait_recv()
            for step in range(1, HALF):
                self.far(step).wait_recv()
            base = me * (self.rows // self.block)

            def add(k, carry):
                at = rows_at(k, self.block)
                value = self.full[rows_at(base + k, self.block), :].astype(F32)
                value = value + self.first[0, at, :].astype(F32)
                for step in range(1, HALF):
                    value = value + self.second[step - 1, at, :].astype(F32)
                if self.out is o_flat:
                    times = value.shape[1] // 128
                    start = self.base + k * self.block * times
                    for q in range(times):
                        where = pl.ds(start + q, self.block, stride=times if times > 1 else None)
                        self.out[where, :] = value[:, q * 128 : q * 128 + 128]
                else:
                    self.out[at, :] = value
                return carry + fold(value * value)

            squares = lax.fori_loop(
                0, self.rows // self.block, add, jnp.zeros((8, self.full.shape[1]), F32)
            )
            for step in (1, 2, 3, 0):
                self.near(step).wait_send()
                if step:
                    self.far(step).wait_send()
            return sum(split_rows(total(squares)))

    s_c = Scatter(v.first_c, v.second_c, v.w_c, 16, v.out_c)
    s_ac = Scatter(v.first_ac, v.second_ac, v.w_ac, 8, v.out_ac)
    s_a = Scatter(v.first_a, v.second_a, v.w_a, 576, v.out_a)
    s_s = Scatter(v.first_s, v.second_s, v.w_s, 128, o_flat, 128)
    s_e = Scatter(v.first_e, v.second_e, v.w_e, 64, o_flat, 1216)
    s_m = Scatter(v.first_m, v.second_m, v.w_m, 576, o_flat, 640)
    s_r = Scatter(v.first_r, v.second_r, v.w_r, 128, o_flat, 0)

    class ScatterUnite:
        def __init__(self):
            self.near_s, self.near_r = take(SLOTS * HALF), take(SLOTS * HALF)
            self.far_s, self.far_r = take(SLOTS * HALF), take(SLOTS * HALF)

        def near(self, step, slot, base):
            dest = far_peer(base, step)
            return remote(
                v.w_u.at[merged_rows(dest, slot), :],
                v.first_u.at[step, slot],
                self.near_s + step * SLOTS + slot,
                self.near_r + step * SLOTS + slot,
                {BATCH: partner},
            )

        def far(self, step, slot):
            return remote(
                v.first_u.at[step, slot],
                v.second_u.at[step - 1, slot],
                self.far_s + step * SLOTS + slot,
                self.far_r + step * SLOTS + slot,
                {BATCH: far_peer(me, step)},
            )

        def own_rows(self, owner, slot, k):
            block = owner * 9 + block_of(owner, slot)
            index = lax.div(block, 8) * MERGED + lax.rem(block, 8)
            return rows_at(index * 8 + k, 64)

        def starts(self, slot):
            def go(step):
                self.near(step, slot, partner).start()

            return [
                functools.partial(has, far_peer(partner, step), slot, functools.partial(go, step))
                for step in (1, 2, 3, 0)
            ]

        def middles(self, slot):
            def go(step):
                self.near(step, slot, me).wait_recv()
                owner = far_peer(me, step)

                def add(k):
                    at = rows_at(k, 64)
                    value = v.w_u[self.own_rows(owner, slot, k), :].astype(F32)
                    value = value + v.first_u[step, slot, at, :].astype(F32)
                    v.first_u[step, slot, at, :] = value.astype(BF)

                loop(8, add)
                self.far(step, slot).start()

            return [
                functools.partial(has, far_peer(me, step), slot, functools.partial(go, step))
                for step in range(1, HALF)
            ]

        def end(self):
            for slot in range(SLOTS):

                def go(slot=slot):
                    self.near(0, slot, me).wait_recv()
                    for step in range(1, HALF):
                        self.far(step, slot).wait_recv()
                    j = block_of(me, slot)

                    def add(k):
                        at = rows_at(k, 64)
                        value = v.w_u[self.own_rows(me, slot, k), :].astype(F32)
                        value = value + v.first_u[0, slot, at, :].astype(F32)
                        for step in range(1, HALF):
                            value = value + v.second_u[step - 1, slot, at, :].astype(F32)
                        o_u[rows_at(j * 8 + k, 64), :] = value

                    loop(8, add)

                has(me, slot, go)
                for step in (1, 2, 3, 0):
                    has(
                        far_peer(partner, step),
                        slot,
                        lambda step=step, slot=slot: self.near(step, slot, partner).wait_send(),
                    )
                    if step:
                        has(
                            far_peer(me, step),
                            slot,
                            lambda step=step, slot=slot: self.far(step, slot).wait_send(),
                        )

            def square(k, carry):
                value = o_u[rows_at(k, 64), :]
                return carry + fold(value * value)

            squares = lax.fori_loop(0, 72, square, jnp.zeros((8, 128), F32))
            return sum(split_rows(total(squares)))

    s_u = ScatterUnite()

    v.w_c[...] = dot_tn(v.united[t], g_main).astype(BF)
    mix(s_c.starts())
    sums = sync.wait()
    gain_grads[14] = (sums[1:2], sums[0:1])

    def spread_taps(ref, pre, norm, row, first, second):
        def step(k):
            at = rows_at(k, 96)
            value = back_norm(
                ref[at, :], normed(pre, at, norm), v.ins[at, :], norm, gamma(row), first, second, count
            )
            ref[at, :] = value.astype(BF).astype(F32)

        loop(6, step)
        v.grad_pad[EDGE : EDGE + CELLS, :] = ref[...]

    def back_tap(tap, spacing, at):
        start = EDGE + at - offset(tap, spacing)
        value = v.grad_pad[start : start + 96, :]
        right = tap % 3 - 1
        if right:
            value = value * col_mask(slice(at, at + 96), -right * spacing)
        return value

    def fill(cat, spacing):
        for tap in range(9):
            for at in range(0, CELLS, 96):
                cat[at : at + 96, tap * 128 : tap * 128 + 128] = back_tap(tap, spacing, at).astype(
                    BF
                )

    spread_taps(v.d_f, v.pre_u, norm_u, 14, sums[0:1], sums[1:2])
    fill(v.cat_u, 1)

    dz = dot(v.pick[...], v.cat_u[...])
    for tap in range(9):
        v.dz_send[tap] = dz[:, tap * 128 : tap * 128 + 128].astype(BF)
    v.dz_recv[me] = v.dz_send[pl.ds(me, 2)]
    ex_dz = Exchange(
        BATCH, OWNERS, lambda o: v.dz_send.at[pl.ds(o, 2)], lambda s: v.dz_recv.at[s]
    )
    ex_dz.start()

    def merged_back(c):
        weight = jnp.concatenate(
            [v.w_u[rows_at(tap * MERGED + c, 512), :] for tap in range(9)], axis=1
        )
        v.joined[c] = dot_nt(v.cat_u[...], weight).astype(BF)

    near_s, near_r, far_s, far_r = take(2), take(2), take(1), take(1)

    def dm_near(k, slot):
        return remote(
            v.joined.at[slot], v.dm_near.at[k], near_s + k, near_r + k, {TENSOR: t_core}
        )

    merged_back(t_diag)
    dm_near(1, t_diag).start()
    merged_back(t_core)
    dm_near(0, t_core).start()
    ex_dz.wait()

    d_act = v.d_sum.at[0 : OWNERS * BINS, :]
    d_act[...] = jnp.zeros((OWNERS * BINS, 512), F32)

    def branch_back(j):
        def body(group, side):
            kept = jnp.where(group_id == group, 1.0, 0.0)
            value = v.dz_recv[:, side].reshape(OWNERS * BINS, 128).astype(F32) * kept
            value = value.astype(BF)
            o_u[rows_at(j, 512), :] = dot(v.act_t[...], value)
            d_act[...] = d_act[...] + dot_nt(value, v.w_own[rows_at(j, 512), :])

        own_branch(j, body)

    loop(9, branch_back)
    for k in range(SPLITS):
        v.d_act_send[k] = d_act[:, k * 128 : k * 128 + 128].astype(BF)
    v.d_act_recv[t] = v.d_act_send[t]
    ex = Exchange(TENSOR, SPLITS, lambda o: v.d_act_send.at[o], lambda s: v.d_act_recv.at[s])
    ex.start()
    merged_back(t_x)
    merged_back(t)
    ex.wait()
    for k in range(OWNERS):
        at = slice(k * BINS, k * BINS + BINS)
        value = v.d_act_recv[0, at, :].astype(F32)
        for slot in range(1, SPLITS):
            value = value + v.d_act_recv[slot, at, :].astype(F32)
        v.d_img_send[k] = value.astype(BF)
    v.d_img_recv[me] = v.d_img_send[me]
    ex = Exchange(BATCH, OWNERS, lambda o: v.d_img_send.at[o], lambda s: v.d_img_recv.at[s])
    ex.start()

    def unite_grad(c):
        for p in range(5):
            width = 256 if p < 4 else 128
            value = dot(v.joined_t[c], v.cat_u[:, p * 256 : p * 256 + width])
            v.w_u[rows_at(2 * p * MERGED + c, 512), :] = value[:, :128].astype(BF)
            if p < 4:
                v.w_u[rows_at((2 * p + 1) * MERGED + c, 512), :] = value[:, 128:].astype(BF)

    unite_grad(0)
    mix(s_u.starts(0))
    dm_near(1, t_x).wait_recv()

    def add_x(k):
        at = rows_at(k, 48)
        value = v.joined[t_x, at, :].astype(F32) + v.dm_near[1, at, :].astype(F32)
        v.joined[t_x, at, :] = value.astype(BF)

    loop(12, add_x)
    dm_far = remote(v.joined.at[t_x], v.dm_far, far_s, far_r, {TENSOR: t_x})
    dm_far.start()
    ex.wait()
    d_b = v.d_img_recv[0].astype(F32)
    for k in range(1, OWNERS):
        d_b = d_b + v.d_img_recv[k].astype(F32)
    unit_b = (v.all_b[me].astype(F32) - mean_b) * scale_b
    d_b = d_b * slope(gamma_b * unit_b + beta_b)
    sync = Sync(v.sync_b3)
    sync.start(
        [total(d_b * group_mask(g)) for g in range(4)]
        + [total(d_b * unit_b * group_mask(g)) for g in range(4)]
    )
    unite_grad(1)
    mix(s_u.starts(1))
    o_misc[1:2, :] = o_misc[1:2, :] + aux_head.finish(0.4)
    sums = sync.wait()
    first_b = jnp.zeros((BINS, 128), F32)
    second_b = jnp.zeros((BINS, 128), F32)
    for group in range(4):
        kept = group_mask(group)
        gain_grads[10 + group] = (sums[4 + group : 5 + group], sums[group : group + 1])
        first_b = first_b + kept * sums[group : group + 1]
        second_b = second_b + kept * sums[4 + group : 5 + group]
    inner = d_b - (first_b + unit_b * second_b) * count_b
    v.d_bp[t] = (gamma_b * scale_b * inner).astype(BF)
    spread_d = Spread(v.d_bp)
    spread_d.start()
    unite_grad(2)
    mix(s_u.starts(2), s_u.middles(0))
    spread_d.wait()
    d_bp_move = ToGroup(
        lambda owner, rows: v.d_bp.at[:, 0:rows, :],
        lambda slot, rows: v.d_bp_all.at[slot, :, 0:rows, :],
    )
    d_bp_move.start()
    v.d_bp_all[me] = v.d_bp[...]
    d_bp = jnp.concatenate([v.d_bp[k] for k in range(SPLITS)], axis=1)
    d_pooled = jnp.zeros((BINS, 512), F32)
    for group in range(4):
        rows = (d_bp.astype(F32) * group_mask(group)).astype(BF)
        d_pooled = d_pooled + dot_nt(rows, v.w_b[group * 512 : group * 512 + 512, :])
    d_pooled = (d_pooled / cells_in).astype(BF)
    v.d_sum[...] = dot_tn(v.pool[...], d_pooled)
    dm_near(0, t).wait_recv()
    dm_far.wait_recv()

    def through_sum(k, carry):
        at = rows_at(k, 48)
        value = v.d_sum[at, :] + v.joined[t, at, :].astype(F32) + v.dm_near[0, at, :].astype(F32)
        value = (value + v.dm_far[at, :].astype(F32)) * slope(summed(at))
        v.d_sum[at, :] = value
        return (
            carry[0] + fold(value),
            carry[1] + fold(value * normed(v.pre_e, at, norm_e)),
            carry[2] + fold(value * normed(v.pre_s, at, norm_s)),
        )

    zero = jnp.zeros((8, 512), F32)
    three = [total(item) for item in lax.fori_loop(0, 12, through_sum, (zero, zero, zero))]
    sync = Sync(v.sync_b4)
    sync.start(split_rows(three[0]) + split_rows(three[1]) + split_rows(three[2]))
    unite_grad(3)
    mix(s_u.starts(3), s_u.middles(1))
    g_aux = aux_head.grad()
    v.d_f2[...] = dot_nt(g_aux, w_ac)
    sync_a = Sync(v.sync_b2)
    sync_a.start(through_silu(v.d_f2, v.pre_a, norm_a, 15))
    v.w_ac[...] = dot_tn(v.act_a[...], g_aux)[:64]
    mix(s_ac.starts())
    sums = sync.wait()
    first_s = join_rows(sums, 0, 4)
    second_e, second_s = join_rows(sums, 4, 4), join_rows(sums, 8, 4)
    for k in range(4):
        gain_grads[6 + k] = (sums[4 + k : 5 + k], sums[k : k + 1])
        gain_grads[1 + k] = (sums[8 + k : 9 + k], sums[k : k + 1])

    def back_both(k):
        at = rows_at(k, 48)
        value, mask = v.d_sum[at, :], wide(v.ins[at, :], 4)
        v.d_e[at, :] = back_norm(
            value, normed(v.pre_e, at, norm_e), mask, norm_e, gamma(6, 4), first_s, second_e, count4
        ).astype(BF)
        v.d_s[at, :] = back_norm(
            value, normed(v.pre_s, at, norm_s), mask, norm_s, gamma(1, 4), first_s, second_s, count4
        ).astype(BF)

    loop(12, back_both)

    def back_hidden(grad, weight, index):
        value = dot_nt(grad, weight)
        for k in range(SPLITS):
            v.dh_send[k] = value[:, k * 128 : k * 128 + 128].astype(BF)
        v.dh_recv[index, t] = v.dh_send[t]
        ex = Exchange(
            TENSOR, SPLITS, lambda o: v.dh_send.at[o], lambda s: v.dh_recv.at[index, s]
        )
        ex.start()
        return ex

    def hidden_sum(index):
        def step(k):
            at = rows_at(k, 96)
            value = v.dh_recv[index, 0, at, :].astype(F32)
            for slot in range(1, SPLITS):
                value = value + v.dh_recv[index, slot, at, :].astype(F32)
            v.d_f[at, :] = value

        loop(6, step)

    ex = back_hidden(v.d_e[...], v.w_e[...], 0)
    mix(s_u.starts(4), s_u.middles(2))
    for k in range(SPLITS):
        v.w_e[k * 128 : k * 128 + 128, :] = dot_tn(v.h2[k], v.d_e[...]).astype(BF)
    mix(s_e.starts())
    sums = sync_a.wait()
    gain_grads[15] = (sums[1:2], sums[0:1])
    spread_taps(v.d_f2, v.pre_a, norm_a, 15, sums[0:1], sums[1:2])
    for p in range(5):
        for at in range(0, CELLS, 96):
            value = back_tap(2 * p, 1, at)
            if p < 4:
                value = value + pltpu.roll(back_tap(2 * p + 1, 1, at), 64, 1)
            v.cat_a[at : at + 96, p * 128 : p * 128 + 128] = value.astype(BF)

    ex.wait()
    hidden_sum(0)
    sync = Sync(v.sync_b5)
    sync.start(through_silu(v.d_f, v.pre_m, norm_m, 5))
    def aux_grad(c2):
        value2 = dot(v.whole_t[c2], v.cat_a[...])
        for half in range(2):
            value = value2[half * 128 : half * 128 + 128]
            c = 2 * c2 + half
            for p in range(5):
                v.pad[p, EDGE : EDGE + 128, :] = value[:, p * 128 : p * 128 + 128]
                low = v.pad[p, pl.ds(EDGE, 64, stride=2), :]
                top = v.pad[p, pl.ds(EDGE + 1, 64, stride=2), :]
                even = jnp.where(left_half, low, pltpu.roll(top, 64, 1))
                v.w_a[rows_at(2 * p * 8 + c, 64), :] = even.astype(BF)
                if p < 4:
                    odd = jnp.where(left_half, pltpu.roll(low, 64, 1), top)
                    v.w_a[rows_at((2 * p + 1) * 8 + c, 64), :] = odd.astype(BF)

    loop(SPLITS, aux_grad)
    mix(s_a.starts(), s_u.middles(3))
    mix(s_c.middles() + s_ac.middles())
    sums = sync.wait()
    gain_grads[5] = (sums[1:2], sums[0:1])
    spread_taps(v.d_f, v.pre_m, norm_m, 5, sums[0:1], sums[1:2])
    fill(v.cat_u, 4)
    weight = jnp.concatenate([v.w_m[tap * 512 : tap * 512 + 512, :] for tap in range(9)], axis=1)
    ex = back_hidden(v.cat_u[...], weight, 1)

    def middle_grad(k):
        value = dot_tn(v.h1[k], v.cat_u[...])
        for tap in range(9):
            v.w_m[rows_at(tap * 4 + k, 128), :] = value[:, tap * 128 : tap * 128 + 128].astype(BF)

    loop(SPLITS, middle_grad)
    mix(s_m.starts(), s_u.middles(4))
    ex.wait()
    hidden_sum(1)
    sync = Sync(v.sync_b6)
    sync.start(through_silu(v.d_f, v.pre_r, norm_r, 0))

    def short_grad(c):
        v.w_s[rows_at(c, 256), :] = dot(v.whole_t[c], v.d_s[...]).astype(BF)

    loop(SPLITS, short_grad)
    mix(s_s.starts(), s_e.middles() + s_a.middles())
    sums = sync.wait()
    gain_grads[0] = (sums[1:2], sums[0:1])

    def back_reduce(k):
        at = rows_at(k, 96)
        v.d_low[at, :] = back_norm(
            v.d_f[at, :], normed(v.pre_r, at, norm_r), v.ins[at, :], norm_r, gamma(0), sums[0:1], sums[1:2], count
        ).astype(BF)

    loop(6, back_reduce)

    def reduce_grad(c):
        v.w_r[rows_at(c, 256), :] = dot(v.whole_t[c], v.d_low[...]).astype(BF)

    loop(SPLITS, reduce_grad)
    mix(s_r.starts())
    mix(s_m.middles() + s_s.middles() + s_r.middles())
    pool_move.wait()
    d_bp_move.wait()
    own_group = jnp.where(group_id == lax.div(me, 2), 1.0, 0.0)
    d_rows = jnp.concatenate(
        [v.d_bp_all[:, k].reshape(OWNERS * BINS, 128) for k in range(SPLITS)], axis=1
    )
    d_rows = (d_rows.astype(F32) * own_group).astype(BF)
    branch_grad = dot_tn(v.pool_all[...].reshape(OWNERS * BINS, 256), d_rows)
    for k in range(4):
        o_flat[pl.ds(1472 + k, 256, stride=4), :] = branch_grad[:, k * 128 : k * 128 + 128]
    rest = (s_c, s_ac, s_a, s_e, s_s, s_m, s_r)
    squares = s_u.end() + sum(split_rows(total(branch_grad * branch_grad)))
    for item in rest:
        squares = squares + item.end()
    dm_near(1, t_diag).wait_send()
    dm_near(0, t_core).wait_send()
    dm_far.wait_send()

    v.gain_rows[...] = jnp.zeros((40, 128), F32)
    gammas = [gain_grads[row][0] for row in range(16)]
    betas = [pltpu.roll(gain_grads[row][1], 64, 1) for row in range(16)]
    o_shift[...] = gain_grads[14][1]
    for row in range(31):
        if row < 15:
            value = gammas[row]
        else:
            left = gammas[15] if row == 15 else betas[row - 16]
            value = jnp.where(lane < 64, left, betas[row - 15])
        v.gain_rows[row + 1 : row + 2, :] = value
    squares = squares + total(fold(v.gain_rows[...] * v.gain_rows[...])) / OWNERS

    sync = Sync(v.sync_end)
    sync.start([squares, o_misc[1:2, :]])

    tail = {}

    def put(where, value):
        tail[where] = value if where not in tail else tail[where] + value

    def class_tail(ref, count, base):
        for row in range(count):
            first, shift = divmod(base + NCLS * row, 128)
            for k in range(2):
                value = roll(ref[row : row + 1, k * 128 : k * 128 + 128], shift)
                put(first + k, jnp.where(lane >= shift, value, 0.0))
                if shift:
                    put(first + k + 1, jnp.where(lane < shift, value, 0.0))

    class_tail(v.out_c, 16, 0)
    class_tail(v.out_ac, 8, 76128)
    start = lax.rem(496 * me, 128)
    first = lax.div(496 * me, 128)
    own = [
        pltpu.roll(v.gain_rows[pl.ds(first + k, 1), :], lax.rem(16 - start + 128, 128), 1)
        for k in range(6)
    ]
    spot = lane - 16 + start
    for k in range(4):
        value = jnp.where(spot < 0, own[k], jnp.where(spot >= 128, own[k + 2], own[k + 1]))
        put(604 + k, jnp.where(lane >= 16, value, 0.0) if k == 0 else value)
    v.grad_pad[EDGE : EDGE + 576, :] = pltpu.roll(v.out_a[...], 96, 1)
    o_flat[7122:7706, :] = jnp.where(
        lane >= 96, v.grad_pad[EDGE : EDGE + 584, :], v.grad_pad[EDGE - 1 : EDGE + 583, :]
    )
    for row in range(608):
        if row in (18, 594):
            o_flat[7104 + row : 7105 + row, :] = o_flat[7104 + row : 7105 + row, :] + tail[row]
        elif row < 18 or row > 594:
            o_flat[7104 + row : 7105 + row, :] = tail[row]
    v.end_t[t] = sync.wait()
    spread_e = Spread(v.end_t)
    spread_e.start()
    spread_e.wait()
    ends = v.end_t[0]
    for k in range(1, SPLITS):
        ends = ends + v.end_t[k]
    o_misc[...] = ends
    o_misc[2:3, :] = jnp.broadcast_to(class_weights()[1], (1, 128))


def whole_step(sizes, labels, feat, flat):
    plan = scratch_plan()
    vmem = pl.BlockSpec(memory_space=pltpu.VMEM)
    anywhere = pl.BlockSpec(memory_space=pl.ANY)
    outs = [flat.shape, (1, 128), (8, 128)]
    return pl.pallas_call(
        functools.partial(step_kernel, tuple(plan)),
        out_shape=[jax.ShapeDtypeStruct(shape, F32) for shape in outs],
        in_specs=[pl.BlockSpec(memory_space=pltpu.SMEM), vmem, anywhere, anywhere],
        out_specs=[vmem] * len(outs),
        scratch_shapes=[pltpu.VMEM(shape, kind) for shape, kind in plan.values()]
        + [pltpu.SemaphoreType.DMA((SEMAPHORES,))],
        compiler_params=pltpu.CompilerParams(
            collective_id=0, has_side_effects=True, vmem_limit_bytes=63 * 1024 * 1024
        ),
        name="whole_step",
    )(sizes, labels, feat, flat)


def update_kernel(
    misc, grad, param, first, second, average,
    o_param, o_first, o_second, o_average, o_norm, o_loss, o_weight,
):
    norm = jnp.sqrt(jnp.sum(misc[0:1, :], axis=1, keepdims=True))
    o_norm[...] = norm
    o_loss[...] = jnp.sum(misc[1:2, :], axis=1, keepdims=True)
    o_weight[...] = misc[2:3, 0:1]
    clipped = grad[...] * jnp.minimum(1.0, 0.05 / (norm + 1e-06))
    new_first = 0.5 * first[...] + 0.5 * clipped
    new_second = 0.5 * second[...] + 0.5 * clipped * clipped
    lift = 1.0 / (1.0 - 0.5**STEP)
    old = param[...]
    ratio = (new_first * lift) / (jnp.sqrt(new_second * lift) + 1e-08)
    new = old - 0.01 * (ratio + 0.01 * old)
    o_param[...] = new
    o_first[...] = new_first
    o_second[...] = new_second
    o_average[...] = 0.999 * average[...] + 0.001 * new


def update(misc, grad, param, first, second, average):
    rows = grad.shape[0]
    block = pl.BlockSpec((1024, 128), lambda i: (i, 0))
    whole = pl.BlockSpec((8, 128), lambda i: (0, 0))
    one = pl.BlockSpec((1, 1), lambda i: (0, 0))
    big = jax.ShapeDtypeStruct((rows, 128), F32)
    return pl.pallas_call(
        update_kernel,
        grid=(pl.cdiv(rows, 1024),),
        out_shape=[big] * 4 + [jax.ShapeDtypeStruct((1, 1), F32)] * 3,
        in_specs=[whole] + [block] * 5,
        out_specs=[block] * 4 + [one] * 3,
        compiler_params=pltpu.CompilerParams(vmem_limit_bytes=60 * 1024 * 1024),
        name="update",
    )(misc, grad, param, first, second, average)


def fits(splits, owners):
    return splits == SPLITS and owners == OWNERS


def local_fast(features, labels, valid, sizes, params, first_moment, squared_mean, average):
    flat = params.reshape(-1, 128)
    marked = jnp.where(valid > 0, labels, -1).astype(F32).reshape(CELLS, 1)
    grad, shift_grad, misc = whole_step(
        sizes, jnp.broadcast_to(marked, (CELLS, 128)), features.reshape(CELLS, -1), flat
    )
    news = update(
        misc,
        grad,
        flat,
        first_moment.reshape(-1, 128),
        squared_mean.reshape(-1, 128),
        average.reshape(-1, 128),
    )
    new_params, new_first, new_second, new_average = [
        item.reshape(params.shape) for item in news[:4]
    ]
    return (
        new_params,
        new_first,
        new_second,
        new_average,
        new_params.astype(BF),
        news[4].reshape(()),
        news[5].reshape(()),
        news[6].reshape(()),
        shift_grad.reshape(128),
    )


def solution(mesh):
    chosen = local_fast if fits(mesh.shape["tensor"], mesh.shape["batch"]) else local
    return jax.shard_map(
        chosen,
        mesh=mesh,
        in_specs=(
            P("batch", None, None, "tensor"),
            P("batch", None, None),
            P("batch", None, None),
            P("batch", None),
            P("tensor", "batch"),
            P("tensor", "batch"),
            P("tensor", "batch"),
            P("tensor", "batch"),
        ),
        out_specs=(
            P("tensor", "batch"),
            P("tensor", "batch"),
            P("tensor", "batch"),
            P("tensor", "batch"),
            P("tensor", "batch"),
            P(),
            P(),
            P(),
            P("tensor"),
        ),
        check_vma=False,
    )
```

```python
import functools

import jax
import jax.numpy as jnp
from jax import lax
from jax.experimental import pallas as pl
from jax.experimental.pallas import tpu as pltpu
from jax.sharding import PartitionSpec as P

C_IN = 1024
MID = 512
C_OUT = 2048
PPM = 512
AUXW = 256
NCLS = 150
MAP = 24
STEP = 3


BIN_COUNTS = (1, 2, 3, 6)
BIN_STARTS = (0, 1, 5, 14)


def segment_shapes(splits):
    return [
        (C_IN, MID // splits),
        (C_IN, C_OUT // splits),
        (9, MID, MID // splits),
        (MID, C_OUT // splits),
        (4, C_OUT // splits, PPM),
        (9, C_OUT + 4 * PPM, PPM // splits),
        (PPM // splits, NCLS),
        (9, C_IN, AUXW // splits),
        (AUXW // splits, NCLS),
        (2, (2 * MID + 2 * C_OUT + 5 * PPM + AUXW) // splits),
    ]


def unflatten(rows, splits):
    split_parts = []
    start = 0
    for shape in segment_shapes(splits):
        count = 1
        for extent in shape:
            count = count * extent
        count = count // rows.shape[0]
        split_parts.append(rows[:, start : start + count].reshape(shape))
        start = start + count
    return split_parts


def gain_pieces(gains, splits):
    widths = [MID, C_OUT, MID, C_OUT, PPM, PPM, PPM, PPM, PPM, AUXW]
    split_parts = []
    start = 0
    for width in widths:
        step_width = width // splits
        split_parts.append(gains[:, start : start + step_width])
        start = start + step_width
    return split_parts


def shifted(field, down, right):
    image_height, width = (field.shape[1], field.shape[2])
    rows_pad, cols_pad = (abs(down), abs(right))
    padded = jnp.pad(field, ((0, 0), (rows_pad, rows_pad), (cols_pad, cols_pad), (0, 0)))
    return padded[
        :,
        rows_pad + down : rows_pad + down + image_height,
        cols_pad + right : cols_pad + right + width,
        :,
    ]


def conv_forward(field, kernel, spacing):
    total = jnp.zeros(field.shape[:-1] + (kernel.shape[2],), jnp.float32)
    for tap in range(9):
        moved = shifted(field, (tap // 3 - 1) * spacing, (tap % 3 - 1) * spacing)
        total = total + jnp.dot(moved, kernel[tap], preferred_element_type=jnp.float32)
    return total


def conv_input_back(grad, kernel, spacing):
    total = jnp.zeros(grad.shape[:-1] + (kernel.shape[1],), jnp.float32)
    for tap in range(9):
        product = jnp.dot(grad, kernel[tap].T, preferred_element_type=jnp.float32)
        total = total + shifted(product, -(tap // 3 - 1) * spacing, -(tap % 3 - 1) * spacing)
    return total


def conv_kernel_back(field, grad, spacing):
    return jnp.stack(
        [
            jnp.einsum(
                "ihwc,ihwd->cd",
                shifted(field, (tap // 3 - 1) * spacing, (tap % 3 - 1) * spacing),
                grad,
                preferred_element_type=jnp.float32,
            )
            for tap in range(9)
        ]
    )


def silu_slope(value):
    gate = jax.nn.sigmoid(value)
    return gate * (1.0 + value * (1.0 - gate))


def channel_sums(values):
    return values.reshape(-1, values.shape[-1]).sum(0)


def masked_norm_apply(items, extra):
    sends = []
    for value, mask, norm in items:
        sends = sends + [
            channel_sums(value * mask),
            channel_sums(value * value * mask),
            jnp.sum(mask) * jnp.ones((1,), jnp.float32),
        ]
    totals = lax.psum(tuple(sends + extra), "batch")
    results = []
    for index, (value, mask, norm) in enumerate(items):
        count = totals[3 * index + 2]
        mean = totals[3 * index] / count
        spread = totals[3 * index + 1] / count - mean * mean
        scaling = lax.rsqrt(spread + 1e-05)
        normed = (value - mean) * scaling
        results.append((norm[0] * normed + norm[1], normed, scaling, count, mask, norm[0]))
    return (results, totals[3 * len(items) :])


def norm_backward(items):
    sends = []
    for grad, kept in items:
        sends = sends + [channel_sums(grad), channel_sums(grad * kept[1])]
    totals = lax.psum(tuple(sends), "batch")
    results = []
    for index, (grad, kept) in enumerate(items):
        outcome, normed, scaling, count, mask, gamma = kept
        first_sum, second_sum = (totals[2 * index], totals[2 * index + 1])
        inner = grad - mask * (first_sum + normed * second_sum) / count
        results.append(gamma * scaling * inner)
    return (results, sends, totals)


def bin_tables(extent, bins, length):
    which = jnp.arange(bins, dtype=jnp.int32)[None, :, None]
    place = jnp.arange(length, dtype=jnp.int32)[None, None, :]
    edge = extent[:, None, None]
    lower = which * edge // bins
    upper = ((which + 1) * edge + bins - 1) // bins
    member = ((place >= lower) & (place < upper)).astype(jnp.float32)
    target = jnp.minimum(place * bins // edge, bins - 1)
    chosen = (target == which).astype(jnp.float32)
    return (member, chosen)


def spread_bins(merged, branch, tables, images):
    joined = [merged]
    for group, bins in enumerate(BIN_COUNTS):
        rows_in, cols_in, rows_pick, cols_pick, cell_count = tables[group]
        piece = branch[:, BIN_STARTS[group] : BIN_STARTS[group] + bins * bins].reshape(
            images, bins, bins, -1
        )
        joined.append(
            jnp.einsum(
                "ikh,ilw,iklc->ihwc",
                rows_pick.astype(jnp.bfloat16),
                cols_pick.astype(jnp.bfloat16),
                piece,
                preferred_element_type=jnp.float32,
            ).astype(jnp.bfloat16)
        )
    return jnp.concatenate(joined, axis=-1)


def pick_bins(d_joined, width, tables, images):
    branch_width = (d_joined.shape[-1] - width) // 4
    d_up = []
    for group, bins in enumerate(BIN_COUNTS):
        rows_in, cols_in, rows_pick, cols_pick, cell_count = tables[group]
        piece = d_joined[..., width + group * branch_width : width + (group + 1) * branch_width]
        d_up.append(
            jnp.einsum("ikh,ilw,ihwc->iklc", rows_pick, cols_pick, piece).reshape(
                images, bins * bins, -1
            )
        )
    return (d_joined[..., :width], jnp.concatenate(d_up, axis=1))


def gather_channels(field):
    return lax.all_gather(field, "tensor", axis=3, tiled=True)


def scatter_channels(field):
    return lax.psum_scatter(
        field.astype(jnp.bfloat16), "tensor", scatter_dimension=3, tiled=True
    ).astype(jnp.float32)


def local(features, labels, valid, sizes, params, first_moment, squared_mean, average):
    splits = lax.axis_size("tensor")
    owners = lax.axis_size("batch")
    images = features.shape[0]
    gathered = lax.all_gather(params.astype(jnp.bfloat16), "batch", axis=0, tiled=True)
    (
        w_reduce,
        w_short,
        w_middle,
        w_expand,
        w_branch,
        w_unite,
        w_classes,
        w_aux,
        w_aux_classes,
        gains,
    ) = unflatten(gathered, splits)
    norms = [(piece[0], piece[1]) for piece in gain_pieces(gains.astype(jnp.float32), splits)]
    rows_at = jnp.arange(MAP, dtype=jnp.int32)
    inside = (rows_at[None, :, None] < sizes[:, 0][:, None, None]) & (
        rows_at[None, None, :] < sizes[:, 1][:, None, None]
    )
    inside = inside.astype(jnp.float32)[..., None]
    counted = inside * valid.astype(jnp.float32)[..., None]
    labels_hot = (labels[..., None] == jnp.arange(NCLS, dtype=jnp.int32)).astype(jnp.float32)
    class_local = channel_sums(labels_hot * counted)
    whole = lax.all_gather(features, "tensor", axis=3, tiled=True)
    pre_reduce = jnp.dot(whole, w_reduce, preferred_element_type=jnp.float32)
    pre_short = jnp.dot(whole, w_short, preferred_element_type=jnp.float32)
    pre_aux = conv_forward(whole, w_aux, 1)
    leading_part, label_tally = masked_norm_apply(
        [
            (pre_reduce, inside, norms[0]),
            (pre_short, inside, norms[1]),
            (pre_aux, inside, norms[9]),
        ],
        [class_local],
    )
    class_pixel_counts = label_tally[0]
    hidden_one = jax.nn.silu(leading_part[0][0]).astype(jnp.bfloat16)
    aux_act = jax.nn.silu(leading_part[2][0]).astype(jnp.bfloat16)
    hidden_full = gather_channels(hidden_one)
    pre_middle = conv_forward(hidden_full, w_middle, 4)
    second, unused = masked_norm_apply([(pre_middle, inside, norms[2])], [])
    hidden_two = jax.nn.silu(second[0][0]).astype(jnp.bfloat16)
    hidden_two_full = gather_channels(hidden_two)
    pre_expand = jnp.dot(hidden_two_full, w_expand, preferred_element_type=jnp.float32)
    third, unused = masked_norm_apply([(pre_expand, inside, norms[3])], [])
    summed = third[0][0] + leading_part[1][0]
    merged = jax.nn.silu(summed).astype(jnp.bfloat16)
    tables = []
    pooled_list = []
    partial_list = []
    for group, bins in enumerate(BIN_COUNTS):
        rows_in, rows_pick = bin_tables(sizes[:, 0], bins, MAP)
        cols_in, cols_pick = bin_tables(sizes[:, 1], bins, MAP)
        cell_count = (
            jnp.sum(rows_in, axis=2)[:, :, None, None] * jnp.sum(cols_in, axis=2)[:, None, :, None]
        )
        tables.append((rows_in, cols_in, rows_pick, cols_pick, cell_count))
        pooled = (
            jnp.einsum(
                "ikh,ilw,ihwc->iklc",
                rows_in.astype(jnp.bfloat16),
                cols_in.astype(jnp.bfloat16),
                merged,
                preferred_element_type=jnp.float32,
            )
            / cell_count
        )
        pooled = pooled.astype(jnp.bfloat16).reshape(images, bins * bins, -1)
        pooled_list.append(pooled)
        partial_list.append(
            jnp.einsum("ipc,cd->ipd", pooled, w_branch[group], preferred_element_type=jnp.float32)
        )
    branch_pre = lax.psum_scatter(
        jnp.concatenate(partial_list, axis=1).astype(jnp.bfloat16),
        "tensor",
        scatter_dimension=2,
        tiled=True,
    ).astype(jnp.float32)
    branch_items = []
    for group, bins in enumerate(BIN_COUNTS):
        piece = branch_pre[:, BIN_STARTS[group] : BIN_STARTS[group] + bins * bins]
        branch_items.append(
            (piece, jnp.ones(piece.shape[:-1] + (1,), jnp.float32), norms[4 + group])
        )
    fourth, unused = masked_norm_apply(branch_items, [])
    branch_act = jnp.concatenate([jax.nn.silu(kept[0]) for kept in fourth], axis=1).astype(
        jnp.bfloat16
    )
    merged_full, branch_full = (
        lax.all_gather(merged, "tensor", axis=3, tiled=True),
        lax.all_gather(branch_act, "tensor", axis=2, tiled=True),
    )
    joined = spread_bins(merged_full, branch_full, tables, images)
    pre_unite = conv_forward(joined, w_unite, 1)
    fifth, unused = masked_norm_apply([(pre_unite, inside, norms[8])], [])
    united = jax.nn.silu(fifth[0][0]).astype(jnp.bfloat16)
    logit_main, logit_aux = (
        lax.psum_scatter(
            jnp.dot(united, w_classes, preferred_element_type=jnp.float32).astype(jnp.bfloat16),
            "tensor",
            scatter_dimension=1,
            tiled=True,
        ).astype(jnp.float32),
        lax.psum_scatter(
            jnp.dot(aux_act, w_aux_classes, preferred_element_type=jnp.float32).astype(
                jnp.bfloat16
            ),
            "tensor",
            scatter_dimension=1,
            tiled=True,
        ).astype(jnp.float32),
    )
    total_valid = jnp.sum(class_pixel_counts)
    class_weight = total_valid / (NCLS * class_pixel_counts + total_valid)
    loss_weight = jnp.sum(class_pixel_counts * class_weight)
    cell_weight = jnp.sum(labels_hot * class_weight, axis=-1, keepdims=True) * counted
    band_rows = labels.shape[1] // splits
    band_start = lax.axis_index("tensor") * band_rows
    hot_band = lax.dynamic_slice_in_dim(labels_hot, band_start, band_rows, 1)
    weight_band = lax.dynamic_slice_in_dim(cell_weight, band_start, band_rows, 1)
    log_main = jax.nn.log_softmax(logit_main, axis=-1)
    log_aux = jax.nn.log_softmax(logit_aux, axis=-1)
    loss_cells = -jnp.sum(hot_band * (log_main + 0.4 * log_aux), axis=-1, keepdims=True)
    loss_local = jnp.sum(weight_band * loss_cells)
    band_main = (weight_band * (jnp.exp(log_main) - hot_band) / loss_weight).astype(jnp.bfloat16)
    band_aux = (0.4 * weight_band * (jnp.exp(log_aux) - hot_band) / loss_weight).astype(
        jnp.bfloat16
    )
    grad_main, grad_aux = (
        lax.all_gather(band_main, "tensor", axis=1, tiled=True),
        lax.all_gather(band_aux, "tensor", axis=1, tiled=True),
    )
    reduced = {}

    def settle(index, value):
        reduced[index] = value

    settle(6, jnp.einsum("ihwc,ihwk->ck", united, grad_main, preferred_element_type=jnp.float32))
    settle(8, jnp.einsum("ihwc,ihwk->ck", aux_act, grad_aux, preferred_element_type=jnp.float32))
    d_united = jnp.dot(grad_main, w_classes.T, preferred_element_type=jnp.float32) * silu_slope(
        fifth[0][0]
    )
    d_aux = jnp.dot(grad_aux, w_aux_classes.T, preferred_element_type=jnp.float32) * silu_slope(
        leading_part[2][0]
    )
    back_one, sums_one, totals_one = norm_backward([(d_united, fifth[0]), (d_aux, leading_part[2])])
    unite_shift_grad = totals_one[0]
    d_unite_pre = back_one[0].astype(jnp.bfloat16)
    d_aux_pre = back_one[1].astype(jnp.bfloat16)
    settle(5, conv_kernel_back(joined, d_unite_pre, 1))
    d_merged, d_branch = pick_bins(conv_input_back(d_unite_pre, w_unite, 1), C_OUT, tables, images)
    d_merged, d_branch = (
        lax.psum_scatter(
            d_merged.astype(jnp.bfloat16), "tensor", scatter_dimension=3, tiled=True
        ).astype(jnp.float32),
        lax.psum_scatter(
            d_branch.astype(jnp.bfloat16), "tensor", scatter_dimension=2, tiled=True
        ).astype(jnp.float32),
    )
    settle(7, conv_kernel_back(whole, d_aux_pre, 1))
    branch_back = []
    for group, bins in enumerate(BIN_COUNTS):
        piece = d_branch[:, BIN_STARTS[group] : BIN_STARTS[group] + bins * bins]
        branch_back.append((piece * silu_slope(fourth[group][0]), fourth[group]))
    back_two, sums_two, unused = norm_backward(branch_back)
    d_branch_pre = jnp.concatenate(back_two, axis=1).astype(jnp.bfloat16)
    d_branch_full = lax.all_gather(d_branch_pre, "tensor", axis=2, tiled=True)
    branch_grads = []
    for group, bins in enumerate(BIN_COUNTS):
        rows_in, cols_in, rows_pick, cols_pick, cell_count = tables[group]
        piece = d_branch_full[:, BIN_STARTS[group] : BIN_STARTS[group] + bins * bins]
        branch_grads.append(
            jnp.einsum("ipc,ipd->cd", pooled_list[group], piece, preferred_element_type=jnp.float32)
        )
        d_pooled = jnp.dot(piece, w_branch[group].T, preferred_element_type=jnp.float32).reshape(
            images, bins, bins, -1
        )
        d_merged = d_merged + jnp.einsum(
            "ikh,ilw,iklc->ihwc", rows_in, cols_in, d_pooled / cell_count
        )
    settle(4, jnp.stack(branch_grads))
    d_summed = d_merged * silu_slope(summed)
    back_three, sums_three, unused = norm_backward(
        [(d_summed, third[0]), (d_summed, leading_part[1])]
    )
    d_expand_pre = back_three[0].astype(jnp.bfloat16)
    d_short_pre = back_three[1].astype(jnp.bfloat16)
    settle(
        3,
        jnp.einsum(
            "ihwc,ihwd->cd", hidden_two_full, d_expand_pre, preferred_element_type=jnp.float32
        ),
    )
    settle(1, jnp.einsum("ihwc,ihwd->cd", whole, d_short_pre, preferred_element_type=jnp.float32))
    d_two = scatter_channels(jnp.dot(d_expand_pre, w_expand.T, preferred_element_type=jnp.float32))
    back_four, sums_four, unused = norm_backward([(d_two * silu_slope(second[0][0]), second[0])])
    d_middle_pre = back_four[0].astype(jnp.bfloat16)
    settle(2, conv_kernel_back(hidden_full, d_middle_pre, 4))
    d_one = scatter_channels(conv_input_back(d_middle_pre, w_middle, 4))
    back_five, sums_five, unused = norm_backward(
        [(d_one * silu_slope(leading_part[0][0]), leading_part[0])]
    )
    settle(
        0,
        jnp.einsum(
            "ihwc,ihwd->cd",
            whole,
            back_five[0].astype(jnp.bfloat16),
            preferred_element_type=jnp.float32,
        ),
    )
    beta_grads = (
        [sums_five[0], sums_three[2], sums_four[0], sums_three[0]]
        + [sums_two[2 * g] for g in range(4)]
        + [sums_one[0], sums_one[2]]
    )
    gamma_grads = (
        [sums_five[1], sums_three[3], sums_four[1], sums_three[1]]
        + [sums_two[2 * g + 1] for g in range(4)]
        + [sums_one[1], sums_one[3]]
    )
    settle(9, jnp.stack([jnp.concatenate(gamma_grads), jnp.concatenate(beta_grads)]))
    ordered = [reduced[index] for index in range(10)]
    grad_share = lax.psum_scatter(
        jnp.concatenate([part.reshape(owners, -1) for part in ordered], axis=1),
        "batch",
        scatter_dimension=0,
        tiled=True,
    )
    square_all, loss_sum = lax.psum(
        (jnp.sum(grad_share * grad_share), loss_local), ("batch", "tensor")
    )
    grad_norm = jnp.sqrt(square_all)
    clipped = grad_share * jnp.minimum(1.0, 0.05 / (grad_norm + 1e-06))
    new_first = 0.5 * first_moment + 0.5 * clipped
    new_second = 0.5 * squared_mean + 0.5 * clipped * clipped
    keep = 1.0 - 0.5**STEP
    new_params = params - 0.01 * (
        new_first / keep / (jnp.sqrt(new_second / keep) + 1e-08) + 0.01 * params
    )
    new_average = 0.999 * average + 0.001 * new_params
    return (
        new_params,
        new_first,
        new_second,
        new_average,
        new_params.astype(jnp.bfloat16),
        grad_norm,
        loss_sum,
        loss_weight,
        unite_shift_grad,
    )


CELLS = MAP * MAP
EDGE = 104
BATCH = "batch"
TENSOR = "tensor"
GROUP_ROWS = ((0, 1), (1, 5), (5, 14), (14, 50))
BINS = 64
BF = jnp.bfloat16
F32 = jnp.float32
MESH = pl.DeviceIdType.MESH
HALF = 4
OWNERS = 8
SPLITS = 4
MERGED = 4
SLOTS = 5


def scratch_plan():
    plan = dict(
        w_r=((1024, 128), BF),
        w_s=((1024, 512), BF),
        w_m=((4608, 128), BF),
        w_e=((512, 512), BF),
        w_b=((2048, 512), BF),
        w_u=((18432, 128), BF),
        w_own=((4608, 128), BF),
        w_a=((4608, 128), BF),
        w_pair=((1024, 640), BF),
        w_c=((128, 256), BF),
        w_ac=((64, 256), F32),
        gain_in=((OWNERS, 8, 128), F32),
        gain_rows=((40, 128), F32),
        out_a=((576, 128), F32),
        out_c=((16, 256), F32),
        out_ac=((8, 256), F32),
        whole=((SPLITS, CELLS, 256), BF),
        whole_t=((SPLITS, 256, CELLS), BF),
        w_c_all=((SPLITS, 128, 256), BF),
        slope_main=((CELLS, 256), BF),
        ins=((CELLS, 128), F32),
        col=((CELLS, 128), F32),
        lab=((CELLS, 128), F32),
        table=((BINS, CELLS), F32),
        pool=((BINS, CELLS), BF),
        pick=((BINS, CELLS), BF),
        cells_in=((BINS, 128), F32),
        pad=((9, CELLS + 2 * EDGE, 128), F32),
        grad_pad=((CELLS + 2 * EDGE, 128), F32),
        pre_r=((CELLS, 128), F32),
        pre_s=((CELLS, 512), F32),
        pre_a=((CELLS, 128), F32),
        pre_m=((CELLS, 128), F32),
        pre_e=((CELLS, 512), F32),
        pre_u=((CELLS, 128), F32),
        act_a=((CELLS, 128), BF),
        h1=((SPLITS, CELLS, 128), BF),
        h2=((SPLITS, CELLS, 128), BF),
        joined=((SPLITS, CELLS, 512), BF),
        joined_t=((SPLITS, 512, CELLS), BF),
        pooled=((BINS, 512), BF),
        pool_half=((2, BINS, 256), BF),
        pool_all=((OWNERS, BINS, 256), BF),
        d_bp_all=((OWNERS, SPLITS, BINS, 128), BF),
        part_b=((SPLITS, BINS, 128), BF),
        recv_b=((SPLITS, BINS, 128), BF),
        all_b=((OWNERS, BINS, 128), BF),
        act_b=((SPLITS, OWNERS * BINS, 128), BF),
        pick_t=((CELLS, 128), BF),
        z_cat=((9, 128, 128), BF),
        act_t=((512, OWNERS * BINS), BF),
        zsum=((2, OWNERS * BINS, 128), F32),
        z_send=((OWNERS, 2, BINS, 128), BF),
        z_recv=((OWNERS, 2, BINS, 128), BF),
        united=((SPLITS, CELLS, 128), BF),
        logit_send=((CELLS, 512), BF),
        logit_recv=((SPLITS, 144, 512), BF),
        slope_in=((SPLITS, 144, 512), BF),
        d_f=((CELLS, 128), F32),
        d_f2=((CELLS, 128), F32),
        cat_u=((CELLS, 1152), BF),
        cat_a=((CELLS, 640), BF),
        dz_send=((9, BINS, 128), BF),
        dz_recv=((OWNERS, 2, BINS, 128), BF),
        d_act_send=((SPLITS, OWNERS * BINS, 128), BF),
        d_act_recv=((SPLITS, OWNERS * BINS, 128), BF),
        d_img_send=((OWNERS, BINS, 128), BF),
        d_img_recv=((OWNERS, BINS, 128), BF),
        d_bp=((SPLITS, BINS, 128), BF),
        dm_near=((2, CELLS, 512), BF),
        dm_far=((CELLS, 512), BF),
        d_sum=((CELLS, 512), F32),
        d_e=((CELLS, 512), BF),
        d_s=((CELLS, 512), BF),
        dh_send=((SPLITS, CELLS, 128), BF),
        dh_recv=((2, SPLITS, CELLS, 128), BF),
        d_low=((CELLS, 128), BF),
        end_t=((SPLITS, 8, 128), F32),
    )
    for name, rows in SYNCS.items():
        plan["sync_" + name] = ((OWNERS, rows, 128), F32)
    for name, (rows, lanes, kind) in PARTS.items():
        plan["first_" + name] = ((HALF, rows, lanes), kind)
        plan["second_" + name] = ((HALF - 1, rows, lanes), kind)
    plan["first_u"] = ((HALF, SLOTS, 512, 128), BF)
    plan["second_u"] = ((HALF - 1, SLOTS, 512, 128), BF)
    return plan


SYNCS = dict(one=8, two=8, three=16, five=8, aux=8, b1=8, b2=8, b3=8, b4=16, b5=8, b6=8, end=8)
PARTS = dict(
    r=(128, 128, BF),
    s=(128, 512, BF),
    m=(576, 128, BF),
    e=(64, 512, BF),
    a=(576, 128, BF),
    c=(16, 256, BF),
    ac=(8, 256, F32),
)
SEMAPHORES = 1100
LOADS = (0, 128, 640, 1216, 1472, 2496, 7104, 7712)
LOAD_ORDER = (0, 2, 3, 1, 4, 6, 5)


class Refs:
    pass


def fold(value):
    return value.reshape(-1, 8, value.shape[-1]).sum(0)


def total(value):
    return jnp.sum(value, axis=0, keepdims=True)


def wide(value, times):
    return jnp.concatenate([value] * times, axis=1)


def dot(left, right):
    return jnp.dot(left, right, preferred_element_type=F32)


def dot_nt(left, right):
    return lax.dot_general(left, right, (((1,), (1,)), ((), ())), preferred_element_type=F32)


def dot_tn(left, right):
    return lax.dot_general(left, right, (((0,), (0,)), ((), ())), preferred_element_type=F32)


def loop(count, body):
    def step(k, carry):
        body(k)
        return carry

    lax.fori_loop(0, count, step, 0)


def rows_at(k, block):
    return pl.ds(pl.multiple_of(k * block, block), block)


def step_kernel(names, *refs):
    (
        sizes, lab_in, feat, flat, o_flat, o_shift, o_misc,
    ) = refs[:7]
    v = Refs()
    for name, ref in zip(names, refs[7:]):
        setattr(v, name, ref)
    sems = refs[-1]
    o_u = o_flat.at[2496:7104, :]
    me = lax.axis_index(BATCH)
    t = lax.axis_index(TENSOR)
    partner = me + 1 - 2 * lax.rem(me, 2)
    t_core = t + 1 - 2 * lax.rem(t, 2)
    t_x = lax.rem(t + 2, SPLITS)
    t_diag = lax.rem(t_core + 2, SPLITS)
    taken = [0]

    def take(count):
        start = taken[0]
        taken[0] = start + count
        assert taken[0] <= SEMAPHORES
        return start

    def far_peer(base, step):
        return lax.rem(base + 2 * step, OWNERS)

    def remote(src, dst, send, recv, device):
        return pltpu.make_async_remote_copy(
            src_ref=src,
            dst_ref=dst,
            send_sem=sems.at[send],
            recv_sem=sems.at[recv],
            device_id=device,
            device_id_type=MESH,
        )

    def mix(*lists):
        for turn in range(max(len(items) for items in lists)):
            for items in lists:
                if turn < len(items):
                    items[turn]()

    load_at = take(len(LOADS))

    def load(index):
        at = pl.ds(LOADS[index], LOADS[index + 1] - LOADS[index])
        return pltpu.make_async_copy(flat.at[at, :], o_flat.at[at, :], sems.at[load_at + index])

    for index in LOAD_ORDER:
        load(index).start()
    v.pool_all[...] = jnp.zeros((OWNERS, BINS, 256), BF)
    v.d_bp_all[...] = jnp.zeros((OWNERS, SPLITS, BINS, 128), BF)
    barrier = pltpu.get_barrier_semaphore()
    for k in range(1, OWNERS):
        pl.semaphore_signal(
            barrier, inc=1, device_id={BATCH: lax.rem(me + k, OWNERS)}, device_id_type=MESH
        )
    for k in range(1, SPLITS):
        pl.semaphore_signal(
            barrier, inc=1, device_id={TENSOR: lax.rem(t + k, SPLITS)}, device_id_type=MESH
        )
    pl.semaphore_wait(barrier, OWNERS + SPLITS - 2)

    class Gather:
        def __init__(self, full, rows, skip=0, step=None, piece=None):
            self.full, self.rows, self.piece = full, rows, piece
            self.skip, self.part = skip, step or rows
            self.near_s, self.far_s, self.pass_s = take(1), take(HALF), take(HALF)
            self.recv, self.keep = take(OWNERS), take(1)

        def at(self, owner):
            if self.rows is None:
                return self.full.at[owner]
            start = pl.multiple_of(owner * self.rows + self.skip, self.part)
            return self.full.at[pl.ds(start, self.part), :]

        def source(self):
            return self.at(me) if self.piece is None else self.piece

        def local(self):
            return pltpu.make_async_copy(self.piece, self.at(me), sems.at[self.keep])

        def near(self):
            return remote(
                self.source(), self.at(me), self.near_s, self.recv + me, {BATCH: partner}
            )

        def far(self, step):
            return remote(
                self.source(),
                self.at(me),
                self.far_s + step,
                self.recv + me,
                {BATCH: far_peer(me, step)},
            )

        def passed(self, step, base):
            source = far_peer(base, step)
            return remote(
                self.at(source),
                self.at(source),
                self.pass_s + step,
                self.recv + source,
                {BATCH: partner},
            )

        def fars(self):
            def go(step):
                if step == 1 and self.piece is not None:
                    self.local().start()
                self.far(step).start()

            return [functools.partial(go, step) for step in range(1, HALF)]

        def nears(self):
            return [lambda: self.near().start()]

        def passes(self):
            def go(step):
                self.passed(step, me).wait_recv()
                self.passed(step, me).start()

            return [functools.partial(go, step) for step in range(1, HALF)]

        def finish(self):
            for step in range(HALF):
                self.passed(step, partner).wait_recv()
            if self.piece is not None:
                self.local().wait()
            self.near().wait_send()
            for step in range(1, HALF):
                self.far(step).wait_send()

        def drain(self):
            for step in range(1, HALF):
                self.passed(step, me).wait_send()

    g_gain = Gather(v.gain_in, None, piece=flat.at[7704:7712, :])
    g_r = Gather(v.w_r, 128)
    g_s = Gather(v.w_s, 128)
    g_a = Gather(v.w_a, 576)
    g_m = Gather(v.w_m, 576)
    g_e = Gather(v.w_e, 64)
    g_b0 = Gather(v.w_b, 256, 0, 128)
    g_b1 = Gather(v.w_b, 256, 128, 128)
    g_c = Gather(v.w_c, 16)
    g_ac = Gather(v.w_ac, 8)

    def block_of(owner, slot):
        return 8 if slot == SLOTS - 1 else lax.rem(slot - owner + 8, 8)

    def merged_rows(owner, slot):
        block = owner * 9 + block_of(owner, slot)
        index = lax.div(block, 8) * MERGED + lax.rem(block, 8)
        return pl.ds(pl.multiple_of(index * 512, 512), 512)

    def has(owner, slot, body):
        if slot == SLOTS - 1:
            pl.when(owner < MERGED)(body)
        else:
            body()

    class GatherUnite:
        def __init__(self):
            self.near_s, self.far_s, self.pass_s = (
                take(SLOTS),
                take(SLOTS * HALF),
                take(SLOTS * HALF),
            )
            self.recv, self.keep = take(SLOTS * OWNERS), take(SLOTS)

        def source(self, slot):
            return v.w_own.at[rows_at(block_of(me, slot), 512), :]

        def full(self, owner, slot):
            return v.w_u.at[merged_rows(owner, slot), :]

        def local(self, slot):
            return pltpu.make_async_copy(
                self.source(slot), self.full(me, slot), sems.at[self.keep + slot]
            )

        def near(self, slot):
            return remote(
                self.source(slot),
                self.full(me, slot),
                self.near_s + slot,
                self.recv + me * SLOTS + slot,
                {BATCH: partner},
            )

        def far(self, step, slot):
            return remote(
                self.source(slot),
                self.full(me, slot),
                self.far_s + step * SLOTS + slot,
                self.recv + me * SLOTS + slot,
                {BATCH: far_peer(me, step)},
            )

        def passed(self, step, slot, base):
            source = far_peer(base, step)
            return remote(
                self.full(source, slot),
                self.full(source, slot),
                self.pass_s + step * SLOTS + slot,
                self.recv + source * SLOTS + slot,
                {BATCH: partner},
            )

        def fars(self, slot):
            def go(step):
                if step == 1:
                    self.local(slot).start()
                self.far(step, slot).start()

            return [
                functools.partial(has, me, slot, functools.partial(go, step))
                for step in range(1, HALF)
            ]

        def nears(self, slot):
            return [lambda: has(me, slot, lambda: self.near(slot).start())]

        def passes(self, slot):
            def go(step):
                self.passed(step, slot, me).wait_recv()
                self.passed(step, slot, me).start()

            return [
                functools.partial(has, far_peer(me, step), slot, functools.partial(go, step))
                for step in range(1, HALF)
            ]

        def finish(self, slots):
            for slot in slots:
                for step in range(HALF):
                    has(
                        far_peer(partner, step),
                        slot,
                        lambda step=step, slot=slot: self.passed(step, slot, partner).wait_recv(),
                    )

                def end(slot=slot):
                    self.local(slot).wait()
                    self.near(slot).wait_send()
                    for step in range(1, HALF):
                        self.far(step, slot).wait_send()

                has(me, slot, end)

        def drain(self):
            for slot in range(SLOTS):
                for step in range(1, HALF):
                    has(
                        far_peer(me, step),
                        slot,
                        lambda step=step, slot=slot: self.passed(step, slot, me).wait_send(),
                    )

    g_u = GatherUnite()

    class Sync:
        def __init__(self, buf):
            self.buf = buf
            self.send, self.recv = take(OWNERS), take(OWNERS)

        def copy(self, k, slot):
            return remote(
                self.buf.at[slot],
                self.buf.at[slot],
                self.send + k,
                self.recv + slot,
                {BATCH: lax.rem(me + k, OWNERS)},
            )

        def start(self, rows):
            for index, row in enumerate(rows):
                self.buf[me, index : index + 1, :] = row
            for index in range(len(rows), self.buf.shape[1]):
                self.buf[me, index : index + 1, :] = jnp.zeros((1, 128), F32)
            for k in range(1, OWNERS):
                self.copy(k, me).start()

        def wait(self):
            for k in range(1, OWNERS):
                self.copy(k, lax.rem(me + k, OWNERS)).wait_recv()
            for k in range(1, OWNERS):
                self.copy(k, me).wait_send()
            value = self.buf[0]
            for slot in range(1, OWNERS):
                value = value + self.buf[slot]
            return value

    class ToGroup:
        def __init__(self, part, into):
            self.part, self.into = part, into
            self.send, self.recv = take(OWNERS), take(OWNERS)

        def each(self, k, owner, slot, act):
            for rows, fits_ in ((16, owner < 6), (BINS, owner >= 6)):

                def go(rows=rows):
                    act(
                        remote(
                            self.part(owner, rows),
                            self.into(slot, rows),
                            self.send + k,
                            self.recv + slot,
                            {BATCH: lax.rem(me + k, OWNERS)},
                        )
                    )

                pl.when(fits_)(go)

        def start(self):
            for k in range(1, OWNERS):
                self.each(k, lax.rem(me + k, OWNERS), me, lambda c: c.start())

        def wait(self):
            for k in range(1, OWNERS):
                self.each(k, me, lax.rem(me + k, OWNERS), lambda c: c.wait_recv())
            for k in range(1, OWNERS):
                self.each(k, lax.rem(me + k, OWNERS), me, lambda c: c.wait_send())

    class Spread:

        def __init__(self, buf, lanes_=None):
            self.buf, self.lanes = buf, lanes_
            self.send, self.recv = take(SPLITS), take(SPLITS)

        def view(self, slot):
            return self.buf.at[slot] if self.lanes is None else self.buf.at[slot, :, self.lanes]

        def copy(self, k, slot):
            return remote(
                self.view(slot),
                self.view(slot),
                self.send + k,
                self.recv + slot,
                {TENSOR: lax.rem(t + k, SPLITS)},
            )

        def start(self):
            for k in range(1, SPLITS):
                self.copy(k, t).start()

        def wait(self):
            for k in range(1, SPLITS):
                self.copy(k, lax.rem(t + k, SPLITS)).wait_recv()
            for k in range(1, SPLITS):
                self.copy(k, t).wait_send()

    class Exchange:

        def __init__(self, axis, count, part, into):
            self.axis, self.count, self.part, self.into = axis, count, part, into
            self.mine = me if axis == BATCH else t
            self.send, self.recv = take(count), take(count)

        def copy(self, k, slot):
            other = lax.rem(self.mine + k, self.count)
            return remote(
                self.part(other),
                self.into(slot),
                self.send + k,
                self.recv + slot,
                {self.axis: other},
            )

        def start(self):
            for k in range(1, self.count):
                self.copy(k, self.mine).start()

        def wait(self):
            for k in range(1, self.count):
                self.copy(k, lax.rem(self.mine + k, self.count)).wait_recv()
            for k in range(1, self.count):
                self.copy(k, self.mine).wait_send()

    feat_keep = take(1)
    feat_local = pltpu.make_async_copy(feat, v.whole.at[t], sems.at[feat_keep])
    feat_s, feat_r = take(3), take(SPLITS)

    def feat_copy(k, slot, device):
        source = feat if k < 2 else v.whole.at[slot]
        return remote(source, v.whole.at[slot], feat_s + k, feat_r + slot, {TENSOR: device})

    def wide_rows(into, rows, low):
        for k in range(4):
            value = o_flat[pl.ds(low + k, rows, stride=4), :]
            into[rows_at(me, rows), k * 128 : k * 128 + 128] = value.astype(BF)

    load(0).wait()
    v.w_r[rows_at(me, 128), :] = o_flat[0:128, :].astype(BF)
    mix(g_r.nears() + g_gain.nears(), g_r.fars() + g_gain.fars())
    feat_local.start()
    feat_copy(0, t, t_x).start()
    feat_copy(1, t, t_core).start()
    load(2).wait()
    v.w_m[rows_at(me, 576), :] = o_flat[640:1216, :].astype(BF)
    load(3).wait()
    wide_rows(v.w_e, 64, 1216)
    mix(g_m.nears() + g_e.nears(), g_m.fars() + g_e.fars())
    lane = lax.broadcasted_iota(jnp.int32, (1, 128), 1)

    def roll(value, shift):
        return pltpu.roll(value, shift % 128, 1) if shift % 128 else value

    high, across = sizes[0, 0], sizes[0, 1]
    place = lax.broadcasted_iota(jnp.int32, (CELLS, 128), 0).astype(F32)
    row_of = jnp.floor((place + 0.5) / MAP)
    col_of = place - MAP * row_of
    within = (row_of < high.astype(F32)) & (col_of < across.astype(F32))
    v.ins[...] = jnp.where(within, 1.0, 0.0)
    v.col[...] = col_of
    v.lab[...] = jnp.where(within, lab_in[...], -1.0)
    v.table[...] = jnp.zeros((BINS, CELLS), F32)
    lane_place = lax.broadcasted_iota(jnp.int32, (1, CELLS), 1).astype(F32)
    lane_row = jnp.floor((lane_place + 0.5) / MAP)
    lane_col = lane_place - MAP * lane_row

    def ranges(extent, bins, where):
        inside, chosen, counts = [], [], []
        for k in range(bins):
            low = lax.div(k * extent, bins)
            top = lax.div((k + 1) * extent + (bins - 1), bins)
            member = (where >= low.astype(F32)) & (where < top.astype(F32))
            inside.append(jnp.where(member, 1.0, 0.0))
            picked = where * bins >= (k * extent).astype(F32)
            if k < bins - 1:
                picked = picked & (where * bins < ((k + 1) * extent).astype(F32))
            chosen.append(jnp.where(picked, 1.0, 0.0))
            counts.append(top - low)
        return inside, chosen, counts

    picks = []
    v.cells_in[...] = jnp.ones((BINS, 128), F32)
    for group, bins in enumerate(BIN_COUNTS):
        r_in, r_pick, r_count = ranges(high, bins, lane_row)
        c_in, c_pick, c_count = ranges(across, bins, lane_col)
        for a in range(bins):
            for b in range(bins):
                spot = BIN_STARTS[group] + a * bins + b
                v.table[spot : spot + 1, :] = r_in[a] * c_in[b]
                v.cells_in[spot : spot + 1, :] = jnp.full(
                    (1, 128), (r_count[a] * c_count[b]).astype(F32)
                )
                picks.append((spot, r_pick[a] * c_pick[b]))
    v.pool[...] = v.table[...].astype(BF)
    for spot, value in picks:
        v.table[spot : spot + 1, :] = value
    v.pick[...] = v.table[...].astype(BF)
    v.pick_t[...] = jnp.concatenate([v.pick[...], v.pick[...]], axis=0).T
    zeros_edge = jnp.zeros((EDGE, 128), F32)
    for tap in range(9):
        v.pad[tap, 0:EDGE, :] = zeros_edge
        v.pad[tap, EDGE + CELLS :, :] = zeros_edge
    v.grad_pad[0:EDGE, :] = zeros_edge
    v.grad_pad[EDGE + CELLS :, :] = zeros_edge
    lanes = lax.broadcasted_iota(jnp.int32, (1, 256), 1).astype(F32)
    counts = jnp.zeros((8, 256), F32)
    for k in range(0, CELLS, 96):
        counts = counts + fold(
            jnp.where(wide(v.lab[k : k + 96, :], 2) == lanes, 1.0, 0.0)
        )
    class_local = total(counts)
    cells_local = jnp.full((1, 128), (high * across).astype(F32))
    left_half = lax.broadcasted_iota(jnp.int32, (64, 128), 1) < 64

    mix(g_r.passes() + g_gain.passes())
    feat_copy(0, t_x, t_x).wait_recv()
    feat_copy(2, t_x, t_core).start()
    load(1).wait()
    wide_rows(v.w_s, 128, 128)
    load(4).wait()
    wide_rows(v.w_b, 256, 1472)
    load(6).wait()
    before = pltpu.roll(o_flat[7122:7698, :], 32, 1)
    after = pltpu.roll(o_flat[7123:7699, :], 32, 1)
    v.w_a[rows_at(me, 576), :] = jnp.where(lane < 32, before, after).astype(BF)

    def class_rows(count, base, into):
        for row in range(count):
            first, shift = divmod(base + NCLS * row, 128)
            three = [
                roll(o_flat[7104 + first + k : 7105 + first + k, :], 128 - shift) for k in range(3)
            ]
            into[row : row + 1, :128] = jnp.where(lane < 128 - shift, three[0], three[1])
            high_half = jnp.where(lane < 128 - shift, three[1], three[2])
            into[row : row + 1, 128:] = jnp.where(lane < NCLS - 128, high_half, 0.0)

    class_rows(16, 0, v.out_c)
    class_rows(8, 76128, v.out_ac)
    v.w_c[rows_at(me, 16), :] = v.out_c[...].astype(BF)
    v.w_ac[rows_at(me, 8), :] = v.out_ac[...].astype(BF).astype(F32)
    load(5).wait()

    def own_rows(j):
        at = pl.ds(pl.multiple_of(2496 + 512 * j, 64), 512)
        v.w_own[rows_at(j, 512), :] = o_flat[at, :].astype(BF)

    loop(9, own_rows)
    for item in (g_gain, g_r):
        item.finish()
    feat_local.wait()
    feat_copy(1, t_core, t_core).wait_recv()
    feat_copy(2, t_diag, t_core).wait_recv()
    feat_copy(0, t, t_x).wait_send()
    feat_copy(1, t, t_core).wait_send()
    feat_copy(2, t_x, t_core).wait_send()
    gain_of = [None] * 33
    for owner in range(OWNERS):
        start = 496 * (owner % 4) - 16
        first, shift = start // 128, start % 128
        for k in range(4):
            value = v.gain_in[owner, 4 + k : 5 + k, :].astype(BF).astype(F32)
            if k == 0:
                value = jnp.where(lane < 16, 0.0, value)
            value = roll(value, shift)
            spot = 16 * (owner // 4) + first + k
            for where, part in (
                (spot, jnp.where(lane >= shift, value, 0.0)),
                (spot + 1, jnp.where(lane < shift, value, 0.0)),
            ):
                gain_of[where] = part if gain_of[where] is None else gain_of[where] + part

    def gamma(row, width=1):
        return jnp.concatenate([gain_of[row + k] for k in range(width)], axis=1)

    def beta(row, width=1):
        return gamma(16 + row, width)

    def whole_feat():
        return jnp.concatenate([v.whole[k] for k in range(SPLITS)], axis=1)

    v.pre_r[...] = dot(whole_feat(), v.w_r[...])
    def offset(tap, spacing):
        return ((tap // 3 - 1) * MAP + (tap % 3 - 1)) * spacing

    def col_mask(at, right):
        where = v.col[at, :] + float(right)
        return jnp.where((where >= 0.0) & (where < float(MAP)), 1.0, 0.0)

    BLOCK = 72

    def shift_sum(taps, spacing, at, slot_of):
        out = None
        for b in (-1, 0, 1):
            part = None
            for tap in taps:
                if tap % 3 - 1 != b:
                    continue
                start = EDGE + at + offset(tap, spacing)
                value = v.pad[slot_of(tap), start : start + BLOCK, :]
                part = value if part is None else part + value
            if part is None:
                continue
            if b:
                part = part * col_mask(slice(at, at + BLOCK), b * spacing)
            out = part if out is None else out + part
        return out

    def masked_sums(ref):
        width = ref.shape[1]

        def step(k, carry):
            at = rows_at(k, 96)
            value = ref[at, :]
            kept = value * (v.ins[at, :] if width == 128 else wide(v.ins[at, :], width // 128))
            return (carry[0] + fold(kept), carry[1] + fold(kept * value))

        zero = jnp.zeros((8, width), F32)
        sums = lax.fori_loop(0, 6, step, (zero, zero))
        return total(sums[0]), total(sums[1])

    def split_rows(value):
        return [value[:, k : k + 128] for k in range(0, value.shape[1], 128)]

    def join_rows(value, row, count):
        return jnp.concatenate([value[row + k : row + k + 1] for k in range(count)], axis=1)

    def moments(first, second, count):
        mean = first / count
        return mean, lax.rsqrt(second / count - mean * mean + 1e-05)

    sync = Sync(v.sync_one)
    r1, r2 = masked_sums(v.pre_r)
    sync.start([r1, r2, cells_local] + split_rows(class_local))
    mix(g_m.passes() + g_e.passes(), g_s.fars())
    sums = sync.wait()
    count = sums[2:3]
    count4 = wide(count, 4)
    norm_r = moments(sums[0:1], sums[1:2], count)
    class_count = join_rows(sums, 3, 2)

    def normed(ref, at, norm):
        return (ref[at, :] - norm[0]) * norm[1]

    spread_1 = Spread(v.h1)

    def make_h1(k):
        at = rows_at(k, 96)
        v.h1[t, at, :] = jax.nn.silu(gamma(0) * normed(v.pre_r, at, norm_r) + beta(0)).astype(BF)

    loop(6, make_h1)
    spread_1.start()
    mix(g_s.nears(), g_b0.fars())
    g_m.finish()
    spread_1.wait()

    def full_h(ref):
        return jnp.concatenate([ref[k] for k in range(SPLITS)], axis=1)

    def w_middle(tap):
        return v.w_m[rows_at(tap, 512), :]

    def middle_pair(p):
        both = jnp.concatenate([w_middle(2 * p), w_middle(2 * p + 1)], axis=1)
        value = dot(full_h(v.h1), both)
        v.pad[2 * p, EDGE : EDGE + CELLS, :] = value[:, :128]
        v.pad[2 * p + 1, EDGE : EDGE + CELLS, :] = value[:, 128:]

    loop(4, middle_pair)
    v.pad[8, EDGE : EDGE + CELLS, :] = dot(full_h(v.h1), w_middle(8))
    for at in range(0, CELLS, BLOCK):
        v.pre_m[at : at + BLOCK, :] = shift_sum(range(9), 4, at, lambda tap: tap)
    sync = Sync(v.sync_two)
    sync.start(list(masked_sums(v.pre_m)))
    mix(g_s.passes() + g_b0.nears(), g_b1.fars())
    sums = sync.wait()
    norm_m = moments(sums[0:1], sums[1:2], count)
    spread_2 = Spread(v.h2)

    def make_h2(k):
        at = rows_at(k, 96)
        v.h2[t, at, :] = jax.nn.silu(gamma(5) * normed(v.pre_m, at, norm_m) + beta(5)).astype(BF)

    loop(6, make_h2)
    spread_2.start()
    mix(g_b0.passes() + g_b1.nears(), g_u.fars(0))
    g_e.finish()
    g_s.finish()
    for k in range(0, 512, 256):
        v.pre_s[:, k : k + 256] = dot(whole_feat(), v.w_s[:, k : k + 256])
    s1, s2 = masked_sums(v.pre_s)
    spread_2.wait()
    for k in range(0, 512, 256):
        v.pre_e[:, k : k + 256] = dot(full_h(v.h2), v.w_e[:, k : k + 256])
    sync = Sync(v.sync_three)
    e1, e2 = masked_sums(v.pre_e)
    sync.start(split_rows(e1) + split_rows(e2) + split_rows(s1) + split_rows(s2))
    mix(g_b1.passes() + g_u.nears(0), g_u.fars(1))
    mix(g_c.nears() + g_ac.nears(), g_c.fars() + g_ac.fars())
    sums = sync.wait()
    norm_e = moments(join_rows(sums, 0, 4), join_rows(sums, 4, 4), count4)
    norm_s = moments(join_rows(sums, 8, 4), join_rows(sums, 12, 4), count4)

    def summed(at):
        return (
            gamma(6, 4) * normed(v.pre_e, at, norm_e)
            + beta(6, 4)
            + gamma(1, 4) * normed(v.pre_s, at, norm_s)
            + beta(1, 4)
        )

    def make_merged(k):
        at = rows_at(k, 48)
        v.joined[t, at, :] = jax.nn.silu(summed(at)).astype(BF)

    loop(12, make_merged)

    j_send, j_recv = take(3), take(SPLITS)

    def joined_copy(k, slot, device):
        return remote(
            v.joined.at[slot], v.joined.at[slot], j_send + k, j_recv + slot, {TENSOR: device}
        )

    joined_copy(0, t, t_x).start()
    joined_copy(1, t, t_core).start()

    pool_move = ToGroup(
        lambda owner, rows: v.pool_half.at[lax.rem(owner, 2), 0:rows, :],
        lambda slot, rows: v.pool_all.at[slot, 0:rows, :],
    )
    bin_row = lax.broadcasted_iota(jnp.int32, (BINS, 1), 0)

    def group_mask(group, shape=None):
        low, top = GROUP_ROWS[group]
        kept = jnp.where((bin_row >= low) & (bin_row < top), 1.0, 0.0)
        return kept if shape is None else jnp.broadcast_to(kept, shape)

    cells_in = wide(v.cells_in[...], 4)
    pooled = dot(v.pool[...], v.joined[t]) / cells_in
    v.pooled[...] = pooled.astype(BF)
    for k in range(2):
        v.pool_half[k] = v.pooled[:, k * 256 : k * 256 + 256]
    v.pool_all[me] = v.pool_half[lax.rem(me, 2)]
    g_b0.finish()
    g_b1.finish()
    part = jnp.zeros((BINS, 512), F32)
    for group in range(4):
        rows = (v.pooled[...].astype(F32) * group_mask(group)).astype(BF)
        part = part + dot(rows, v.w_b[group * 512 : group * 512 + 512, :])
    for k in range(SPLITS):
        v.part_b[k] = part[:, k * 128 : k * 128 + 128].astype(BF)
    v.recv_b[t] = v.part_b[t]
    ex = Exchange(TENSOR, SPLITS, lambda o: v.part_b.at[o], lambda s: v.recv_b.at[s])
    ex.start()
    mix(g_u.passes(0) + g_u.nears(1), g_u.fars(2))
    joined_copy(0, t_x, t_x).wait_recv()
    joined_copy(2, t_x, t_core).start()
    ex.wait()
    own_b = v.recv_b[0].astype(F32)
    for k in range(1, SPLITS):
        own_b = own_b + v.recv_b[k].astype(F32)
    v.all_b[me] = own_b.astype(BF)
    ex = Exchange(BATCH, OWNERS, lambda o: v.all_b.at[me], lambda s: v.all_b.at[s])
    ex.start()
    mix(g_u.passes(1) + g_u.nears(2), g_u.fars(4))
    ex.wait()
    all_b = [v.all_b[k].astype(F32) for k in range(OWNERS)]
    sum_b, square_b = all_b[0], all_b[0] * all_b[0]
    for k in range(1, OWNERS):
        sum_b = sum_b + all_b[k]
        square_b = square_b + all_b[k] * all_b[k]
    mean_b = jnp.zeros((BINS, 128), F32)
    scale_b = jnp.zeros((BINS, 128), F32)
    gamma_b = jnp.zeros((BINS, 128), F32)
    beta_b = jnp.zeros((BINS, 128), F32)
    count_b = jnp.zeros((BINS, 1), F32)
    for group, bins in enumerate(BIN_COUNTS):
        kept = group_mask(group)
        size = float(OWNERS * bins * bins)
        mean, scaling = moments(total(sum_b * kept), total(square_b * kept), size)
        mean_b = mean_b + kept * mean
        scale_b = scale_b + kept * scaling
        gamma_b = gamma_b + kept * gamma(10 + group)
        beta_b = beta_b + kept * beta(10 + group)
        count_b = count_b + kept / size
    spread_b = Spread(v.act_b)
    for k in range(OWNERS):
        out = gamma_b * ((all_b[k] - mean_b) * scale_b) + beta_b
        v.act_b[t, k * BINS : k * BINS + BINS, :] = jax.nn.silu(out).astype(BF)
    spread_b.start()
    mix(g_u.passes(2) + g_u.nears(4), g_u.fars(3))
    spread_b.wait()
    row_512 = lax.broadcasted_iota(jnp.int32, (OWNERS * BINS, 1), 0) & (BINS - 1)
    group_id = jnp.where(
        row_512 < 1, 0, jnp.where(row_512 < 5, 1, jnp.where(row_512 < 14, 2, jnp.where(row_512 < 50, 3, 9)))
    )

    def full_act():
        return jnp.concatenate([v.act_b[k] for k in range(SPLITS)], axis=1)

    v.zsum[...] = jnp.zeros((2, OWNERS * BINS, 128), F32)

    def own_branch(j, body):
        chunk = lax.rem(me + j, 8)
        pl.when(chunk >= MERGED)(lambda: body(chunk - MERGED, lax.div(me + j, 8)))

    def make_z(j):
        def body(group, side):
            kept = jnp.where(group_id == group, 1.0, 0.0)
            v.zsum[side] = v.zsum[side] + kept * dot(full_act(), v.w_own[rows_at(j, 512), :])

        own_branch(j, body)

    loop(9, make_z)
    for k in range(OWNERS):
        for side in range(2):
            v.z_send[k, side] = v.zsum[side, k * BINS : k * BINS + BINS, :].astype(BF)
    v.z_recv[me] = v.z_send[me]
    ex = Exchange(BATCH, OWNERS, lambda o: v.z_send.at[o], lambda s: v.z_recv.at[s])
    ex.start()
    mix(g_u.passes(4) + g_u.nears(3))
    v.act_t[...] = full_act().T
    joined_copy(1, t_core, t_core).wait_recv()
    joined_copy(2, t_diag, t_core).wait_recv()
    for k in range(SPLITS):
        v.joined_t[k] = v.joined[k].T
    mix(g_u.passes(3) + g_c.passes() + g_ac.passes())
    ex.wait()
    g_u.finish((0, 1, 2, 4))

    def tap_z(tap):
        if tap == 0:
            return v.z_recv[0, 0].astype(F32)
        if tap == 8:
            return v.z_recv[7, 1].astype(F32)
        return v.z_recv[tap, 0].astype(F32) + v.z_recv[tap - 1, 1].astype(F32)

    for tap in range(9):
        z = tap_z(tap)
        high_z = z.astype(BF)
        v.z_cat[tap, :BINS, :] = high_z
        v.z_cat[tap, BINS:, :] = (z - high_z.astype(F32)).astype(BF)

    def most_joined():
        return jnp.concatenate([v.joined[k] for k in range(3)], axis=1)

    def rest_joined():
        return jnp.concatenate([v.joined[3], v.pick_t[...]], axis=1)

    def most_weight(tap):
        return v.w_u[pl.ds(pl.multiple_of(tap * 2048, 512), 1536), :]

    def rest_weight(tap):
        last = v.w_u[pl.ds(pl.multiple_of(tap * 2048 + 1536, 512), 512), :]
        return jnp.concatenate([last, v.z_cat[tap]], axis=0)

    inner = slice(EDGE, EDGE + CELLS)

    def most_pair(p):
        both = jnp.concatenate([most_weight(2 * p), most_weight(2 * p + 1)], axis=1)
        value = dot(most_joined(), both)
        v.pad[2 * p, inner, :] = value[:, :128]
        v.pad[2 * p + 1, inner, :] = value[:, 128:]

    def rest_pair(p):
        both = jnp.concatenate([rest_weight(2 * p), rest_weight(2 * p + 1)], axis=1)
        value = dot(rest_joined(), both)
        v.pad[2 * p, inner, :] = v.pad[2 * p, inner, :] + value[:, :128]
        v.pad[2 * p + 1, inner, :] = v.pad[2 * p + 1, inner, :] + value[:, 128:]

    loop(4, most_pair)
    v.pad[8, inner, :] = dot(most_joined(), most_weight(8))
    g_u.finish((3,))
    loop(4, rest_pair)
    v.pad[8, inner, :] = v.pad[8, inner, :] + dot(rest_joined(), rest_weight(8))
    for at in range(0, CELLS, BLOCK):
        v.pre_u[at : at + BLOCK, :] = shift_sum(range(9), 1, at, lambda tap: tap)
    sync = Sync(v.sync_five)
    sync.start(list(masked_sums(v.pre_u)))
    pool_move.start()
    mix(g_a.nears(), g_a.fars())
    for item in (g_c, g_ac):
        item.finish()
    v.w_c_all[t] = v.w_c[...]
    spread_c = Spread(v.w_c_all)
    spread_c.start()
    for k in range(SPLITS):
        v.whole_t[k] = v.whole[k].T
    for item in (g_gain, g_r, g_s, g_m, g_e, g_b0, g_b1, g_c, g_ac, g_u):
        item.drain()
    joined_copy(0, t, t_x).wait_send()
    joined_copy(1, t, t_core).wait_send()
    joined_copy(2, t_x, t_core).wait_send()
    w_ac = jnp.concatenate([v.w_ac[...], jnp.zeros((64, 256), F32)], axis=0).astype(BF)
    sums = sync.wait()
    norm_u = moments(sums[0:1], sums[1:2], count)

    def make_u(k):
        at = rows_at(k, 96)
        v.united[t, at, :] = jax.nn.silu(gamma(14) * normed(v.pre_u, at, norm_u) + beta(14)).astype(BF)

    loop(6, make_u)
    spread_u = Spread(v.united)
    spread_u.start()
    class Band:
        def __init__(self, at):
            self.at = at
            self.ex = Exchange(
                TENSOR,
                SPLITS,
                lambda o: v.logit_send.at[rows_at(o, 144), at],
                lambda s: v.logit_recv.at[s, :, at],
            )
            self.back = Spread(v.slope_in, at)

        def start(self, value):
            v.logit_send[:, self.at] = value.astype(BF)
            self.ex.start()
            v.logit_recv[t, :, self.at] = v.logit_send[rows_at(t, 144), self.at]

        def finish(self, factor):
            self.ex.wait()
            logits = v.logit_recv[0, :, self.at].astype(F32)
            for k in range(1, SPLITS):
                logits = logits + v.logit_recv[k, :, self.at].astype(F32)
            loss_rows, grad = soft_loss(logits, rows_at(t, 144), factor)
            v.slope_in[t, :, self.at] = grad
            self.back.start()
            loss_rows = total(loss_rows)
            return loss_rows[:, :128] + loss_rows[:, 128:]

        def grad(self):
            self.back.wait()
            return v.slope_in[:, :, self.at].reshape(CELLS, 256)

    def class_weights():
        total_valid = jnp.sum(class_count, axis=1, keepdims=True)
        weight = total_valid / (NCLS * class_count + total_valid)
        whole = jnp.sum(class_count * weight, axis=1, keepdims=True)
        return jnp.where(lanes < float(NCLS), weight, 0.0), whole

    def soft_loss(logits, at, factor):
        class_weight, loss_weight = class_weights()
        hot = jnp.where(wide(v.lab[at, :], 2) == lanes, 1.0, 0.0)
        cell_weight = factor * jnp.sum(hot * class_weight, axis=1, keepdims=True)
        value = jnp.where(lanes < float(NCLS), logits, -1e30)
        value = value - jnp.max(value, axis=1, keepdims=True)
        powers = jnp.exp(value)
        mass = jnp.sum(powers, axis=1, keepdims=True)
        grad = cell_weight * (powers / mass - hot) / loss_weight
        return fold(-cell_weight * hot * (value - jnp.log(mass))), grad.astype(BF)

    aux_head = Band(slice(256, 512))
    mix(g_a.passes())
    spread_c.wait()

    g_a.finish()
    g_a.drain()

    def unpack(chunk):
        for pair in range(5):
            even = v.w_a[rows_at(2 * pair * 8 + chunk, 64), :].astype(F32)
            if pair < 4:
                odd = v.w_a[rows_at((2 * pair + 1) * 8 + chunk, 64), :].astype(F32)
            else:
                odd = jnp.zeros((64, 128), F32)
            low = jnp.where(left_half, even, pltpu.roll(odd, 64, 1))
            top = jnp.where(left_half, pltpu.roll(even, 64, 1), odd)
            v.pad[pair, pl.ds(EDGE, 64, stride=2), :] = low
            v.pad[pair, pl.ds(EDGE + 1, 64, stride=2), :] = top
            both = v.pad[pair, EDGE : EDGE + 128, :]
            v.w_pair[rows_at(chunk, 128), pair * 128 : pair * 128 + 128] = both.astype(BF)

    loop(8, unpack)

    for pair in (0, 2):
        value = dot(whole_feat(), v.w_pair[:, pair * 128 : pair * 128 + 256])
        v.pad[pair, EDGE : EDGE + CELLS, :] = value[:, :128]
        v.pad[pair + 1, EDGE : EDGE + CELLS, :] = value[:, 128:]
    v.pad[4, EDGE : EDGE + CELLS, :] = dot(whole_feat(), v.w_pair[:, 512:640])

    left_wide = lax.broadcasted_iota(jnp.int32, (BLOCK, 128), 1) < 64
    for at in range(0, CELLS, BLOCK):
        even = shift_sum((0, 2, 4, 6, 8), 1, at, lambda tap: tap // 2)
        odd = shift_sum((1, 3, 5, 7), 1, at, lambda tap: tap // 2)
        v.pre_a[at : at + BLOCK, :] = jnp.where(left_wide, even + pltpu.roll(odd, 64, 1), 0.0)

    sync_a = Sync(v.sync_aux)
    sync_a.start(list(masked_sums(v.pre_a)))
    spread_u.wait()
    weight_c = v.w_c_all[...].reshape(512, 256)

    def main_loss(k, carry):
        at = rows_at(k, 144)
        rows = jnp.concatenate([v.united[slot, at, :] for slot in range(SPLITS)], axis=1)
        loss_rows, grad = soft_loss(dot(rows, weight_c), at, 1.0)
        v.slope_main[at, :] = grad
        return carry + loss_rows

    loss_rows = total(lax.fori_loop(0, 4, main_loss, jnp.zeros((8, 256), F32)))
    o_misc[1:2, :] = (loss_rows[:, :128] + loss_rows[:, 128:]) / SPLITS
    g_main = v.slope_main[...]
    v.d_f[...] = dot_nt(g_main, v.w_c[...])

    def slope(value):
        gate = jax.nn.sigmoid(value)
        return gate * (1.0 + value * (1.0 - gate))

    def through_silu(ref, pre, norm, row):
        def step(k, carry):
            at = rows_at(k, 96)
            unit = normed(pre, at, norm)
            value = ref[at, :] * slope(gamma(row) * unit + beta(row))
            ref[at, :] = value
            return (carry[0] + fold(value), carry[1] + fold(value * unit))

        zero = jnp.zeros((8, 128), F32)
        sums = lax.fori_loop(0, 6, step, (zero, zero))
        return [total(sums[0]), total(sums[1])]

    def back_norm(value, unit, mask, norm, gain, first, second, size):
        inner = value - mask * (first + unit * second) / size
        return gain * norm[1] * inner

    gain_grads = {}
    sync = Sync(v.sync_b1)
    sync.start(through_silu(v.d_f, v.pre_u, norm_u, 14))
    sums = sync_a.wait()
    norm_a = moments(sums[0:1], sums[1:2], count)

    def make_a(k):
        at = rows_at(k, 96)
        v.act_a[at, :] = jax.nn.silu(gamma(15) * normed(v.pre_a, at, norm_a) + beta(15)).astype(BF)

    loop(6, make_a)
    aux_head.start(dot(v.act_a[...], w_ac))

    class Scatter:
        def __init__(self, first, second, full, rows, out, base=0):
            self.full, self.rows, self.out, self.base = full, rows, out, base
            self.first, self.second = first, second
            self.near_s, self.near_r = take(HALF), take(HALF)
            self.far_s, self.far_r = take(HALF), take(HALF)
            self.block = min(rows, 64)

        def near(self, step):
            dest = far_peer(partner, step)
            return remote(
                self.full.at[rows_at(dest, self.rows), :],
                self.first.at[step],
                self.near_s + step,
                self.near_r + step,
                {BATCH: partner},
            )

        def far(self, step):
            return remote(
                self.first.at[step],
                self.second.at[step - 1],
                self.far_s + step,
                self.far_r + step,
                {BATCH: far_peer(me, step)},
            )

        def starts(self):
            return [lambda step=step: self.near(step).start() for step in (1, 2, 3, 0)]

        def middles(self):
            def go(step):
                self.near(step).wait_recv()
                base = far_peer(me, step) * (self.rows // self.block)

                def add(k):
                    at = rows_at(k, self.block)
                    value = self.full[rows_at(base + k, self.block), :].astype(F32)
                    value = value + self.first[step, at, :].astype(F32)
                    self.first[step, at, :] = value.astype(self.first.dtype)

                loop(self.rows // self.block, add)
                self.far(step).start()

            return [functools.partial(go, step) for step in range(1, HALF)]

        def end(self):
            self.near(0).wait_recv()
            for step in range(1, HALF):
                self.far(step).wait_recv()
            base = me * (self.rows // self.block)

            def add(k, carry):
                at = rows_at(k, self.block)
                value = self.full[rows_at(base + k, self.block), :].astype(F32)
                value = value + self.first[0, at, :].astype(F32)
                for step in range(1, HALF):
                    value = value + self.second[step - 1, at, :].astype(F32)
                if self.out is o_flat:
                    times = value.shape[1] // 128
                    start = self.base + k * self.block * times
                    for q in range(times):
                        where = pl.ds(start + q, self.block, stride=times if times > 1 else None)
                        self.out[where, :] = value[:, q * 128 : q * 128 + 128]
                else:
                    self.out[at, :] = value
                return carry + fold(value * value)

            squares = lax.fori_loop(
                0, self.rows // self.block, add, jnp.zeros((8, self.full.shape[1]), F32)
            )
            for step in (1, 2, 3, 0):
                self.near(step).wait_send()
                if step:
                    self.far(step).wait_send()
            return sum(split_rows(total(squares)))

    s_c = Scatter(v.first_c, v.second_c, v.w_c, 16, v.out_c)
    s_ac = Scatter(v.first_ac, v.second_ac, v.w_ac, 8, v.out_ac)
    s_a = Scatter(v.first_a, v.second_a, v.w_a, 576, v.out_a)
    s_s = Scatter(v.first_s, v.second_s, v.w_s, 128, o_flat, 128)
    s_e = Scatter(v.first_e, v.second_e, v.w_e, 64, o_flat, 1216)
    s_m = Scatter(v.first_m, v.second_m, v.w_m, 576, o_flat, 640)
    s_r = Scatter(v.first_r, v.second_r, v.w_r, 128, o_flat, 0)

    class ScatterUnite:
        def __init__(self):
            self.near_s, self.near_r = take(SLOTS * HALF), take(SLOTS * HALF)
            self.far_s, self.far_r = take(SLOTS * HALF), take(SLOTS * HALF)

        def near(self, step, slot, base):
            dest = far_peer(base, step)
            return remote(
                v.w_u.at[merged_rows(dest, slot), :],
                v.first_u.at[step, slot],
                self.near_s + step * SLOTS + slot,
                self.near_r + step * SLOTS + slot,
                {BATCH: partner},
            )

        def far(self, step, slot):
            return remote(
                v.first_u.at[step, slot],
                v.second_u.at[step - 1, slot],
                self.far_s + step * SLOTS + slot,
                self.far_r + step * SLOTS + slot,
                {BATCH: far_peer(me, step)},
            )

        def own_rows(self, owner, slot, k):
            block = owner * 9 + block_of(owner, slot)
            index = lax.div(block, 8) * MERGED + lax.rem(block, 8)
            return rows_at(index * 8 + k, 64)

        def starts(self, slot):
            def go(step):
                self.near(step, slot, partner).start()

            return [
                functools.partial(has, far_peer(partner, step), slot, functools.partial(go, step))
                for step in (1, 2, 3, 0)
            ]

        def middles(self, slot):
            def go(step):
                self.near(step, slot, me).wait_recv()
                owner = far_peer(me, step)

                def add(k):
                    at = rows_at(k, 64)
                    value = v.w_u[self.own_rows(owner, slot, k), :].astype(F32)
                    value = value + v.first_u[step, slot, at, :].astype(F32)
                    v.first_u[step, slot, at, :] = value.astype(BF)

                loop(8, add)
                self.far(step, slot).start()

            return [
                functools.partial(has, far_peer(me, step), slot, functools.partial(go, step))
                for step in range(1, HALF)
            ]

        def end(self):
            for slot in range(SLOTS):

                def go(slot=slot):
                    self.near(0, slot, me).wait_recv()
                    for step in range(1, HALF):
                        self.far(step, slot).wait_recv()
                    j = block_of(me, slot)

                    def add(k):
                        at = rows_at(k, 64)
                        value = v.w_u[self.own_rows(me, slot, k), :].astype(F32)
                        value = value + v.first_u[0, slot, at, :].astype(F32)
                        for step in range(1, HALF):
                            value = value + v.second_u[step - 1, slot, at, :].astype(F32)
                        o_u[rows_at(j * 8 + k, 64), :] = value

                    loop(8, add)

                has(me, slot, go)
                for step in (1, 2, 3, 0):
                    has(
                        far_peer(partner, step),
                        slot,
                        lambda step=step, slot=slot: self.near(step, slot, partner).wait_send(),
                    )
                    if step:
                        has(
                            far_peer(me, step),
                            slot,
                            lambda step=step, slot=slot: self.far(step, slot).wait_send(),
                        )

            def square(k, carry):
                value = o_u[rows_at(k, 64), :]
                return carry + fold(value * value)

            squares = lax.fori_loop(0, 72, square, jnp.zeros((8, 128), F32))
            return sum(split_rows(total(squares)))

    s_u = ScatterUnite()

    v.w_c[...] = dot_tn(v.united[t], g_main).astype(BF)
    mix(s_c.starts())
    sums = sync.wait()
    gain_grads[14] = (sums[1:2], sums[0:1])

    def spread_taps(ref, pre, norm, row, first, second):
        def step(k):
            at = rows_at(k, 96)
            value = back_norm(
                ref[at, :], normed(pre, at, norm), v.ins[at, :], norm, gamma(row), first, second, count
            )
            ref[at, :] = value.astype(BF).astype(F32)

        loop(6, step)
        v.grad_pad[EDGE : EDGE + CELLS, :] = ref[...]

    def back_tap(tap, spacing, at):
        start = EDGE + at - offset(tap, spacing)
        value = v.grad_pad[start : start + 96, :]
        right = tap % 3 - 1
        if right:
            value = value * col_mask(slice(at, at + 96), -right * spacing)
        return value

    def fill(cat, spacing):
        for tap in range(9):
            for at in range(0, CELLS, 96):
                cat[at : at + 96, tap * 128 : tap * 128 + 128] = back_tap(tap, spacing, at).astype(
                    BF
                )

    spread_taps(v.d_f, v.pre_u, norm_u, 14, sums[0:1], sums[1:2])
    fill(v.cat_u, 1)

    dz = dot(v.pick[...], v.cat_u[...])
    for tap in range(9):
        v.dz_send[tap] = dz[:, tap * 128 : tap * 128 + 128].astype(BF)
    v.dz_recv[me] = v.dz_send[pl.ds(me, 2)]
    ex_dz = Exchange(
        BATCH, OWNERS, lambda o: v.dz_send.at[pl.ds(o, 2)], lambda s: v.dz_recv.at[s]
    )
    ex_dz.start()

    def merged_back(c):
        weight = jnp.concatenate(
            [v.w_u[rows_at(tap * MERGED + c, 512), :] for tap in range(9)], axis=1
        )
        v.joined[c] = dot_nt(v.cat_u[...], weight).astype(BF)

    near_s, near_r, far_s, far_r = take(2), take(2), take(1), take(1)

    def dm_near(k, slot):
        return remote(
            v.joined.at[slot], v.dm_near.at[k], near_s + k, near_r + k, {TENSOR: t_core}
        )

    merged_back(t_diag)
    dm_near(1, t_diag).start()
    merged_back(t_core)
    dm_near(0, t_core).start()
    merged_back(t_x)
    merged_back(t)

    def unite_grad(c):
        for p in range(5):
            width = 256 if p < 4 else 128
            value = dot(v.joined_t[c], v.cat_u[:, p * 256 : p * 256 + width])
            v.w_u[rows_at(2 * p * MERGED + c, 512), :] = value[:, :128].astype(BF)
            if p < 4:
                v.w_u[rows_at((2 * p + 1) * MERGED + c, 512), :] = value[:, 128:].astype(BF)

    unite_grad(0)
    mix(s_u.starts(0))
    o_misc[1:2, :] = o_misc[1:2, :] + aux_head.finish(0.4)
    ex_dz.wait()

    d_act = v.d_sum.at[0 : OWNERS * BINS, :]
    d_act[...] = jnp.zeros((OWNERS * BINS, 512), F32)

    def branch_back(j):
        def body(group, side):
            kept = jnp.where(group_id == group, 1.0, 0.0)
            value = v.dz_recv[:, side].reshape(OWNERS * BINS, 128).astype(F32) * kept
            value = value.astype(BF)
            o_u[rows_at(j, 512), :] = dot(v.act_t[...], value)
            d_act[...] = d_act[...] + dot_nt(value, v.w_own[rows_at(j, 512), :])

        own_branch(j, body)

    loop(9, branch_back)
    for k in range(SPLITS):
        v.d_act_send[k] = d_act[:, k * 128 : k * 128 + 128].astype(BF)
    v.d_act_recv[t] = v.d_act_send[t]
    ex = Exchange(TENSOR, SPLITS, lambda o: v.d_act_send.at[o], lambda s: v.d_act_recv.at[s])
    ex.start()
    unite_grad(1)
    mix(s_u.starts(1))
    dm_near(1, t_x).wait_recv()

    def add_x(k):
        at = rows_at(k, 48)
        value = v.joined[t_x, at, :].astype(F32) + v.dm_near[1, at, :].astype(F32)
        v.joined[t_x, at, :] = value.astype(BF)

    loop(12, add_x)
    dm_far = remote(v.joined.at[t_x], v.dm_far, far_s, far_r, {TENSOR: t_x})
    dm_far.start()
    g_aux = aux_head.grad()
    v.d_f2[...] = dot_nt(g_aux, w_ac)
    sync_a = Sync(v.sync_b2)
    sync_a.start(through_silu(v.d_f2, v.pre_a, norm_a, 15))
    v.w_ac[...] = dot_tn(v.act_a[...], g_aux)[:64]
    mix(s_ac.starts())

    unite_grad(2)
    unite_grad(3)
    ex.wait()
    for k in range(OWNERS):
        at = slice(k * BINS, k * BINS + BINS)
        value = v.d_act_recv[0, at, :].astype(F32)
        for slot in range(1, SPLITS):
            value = value + v.d_act_recv[slot, at, :].astype(F32)
        v.d_img_send[k] = value.astype(BF)
    v.d_img_recv[me] = v.d_img_send[me]
    ex = Exchange(BATCH, OWNERS, lambda o: v.d_img_send.at[o], lambda s: v.d_img_recv.at[s])
    ex.start()
    mix(s_u.starts(2), s_u.middles(0))

    sums = sync_a.wait()
    gain_grads[15] = (sums[1:2], sums[0:1])
    spread_taps(v.d_f2, v.pre_a, norm_a, 15, sums[0:1], sums[1:2])
    for p in range(5):
        for at in range(0, CELLS, 96):
            value = back_tap(2 * p, 1, at)
            if p < 4:
                value = value + pltpu.roll(back_tap(2 * p + 1, 1, at), 64, 1)
            v.cat_a[at : at + 96, p * 128 : p * 128 + 128] = value.astype(BF)

    def aux_grad(c2):
        value2 = dot(v.whole_t[c2], v.cat_a[...])
        for half in range(2):
            value = value2[half * 128 : half * 128 + 128]
            c = 2 * c2 + half
            for p in range(5):
                v.pad[p, EDGE : EDGE + 128, :] = value[:, p * 128 : p * 128 + 128]
                low = v.pad[p, pl.ds(EDGE, 64, stride=2), :]
                top = v.pad[p, pl.ds(EDGE + 1, 64, stride=2), :]
                even = jnp.where(left_half, low, pltpu.roll(top, 64, 1))
                v.w_a[rows_at(2 * p * 8 + c, 64), :] = even.astype(BF)
                if p < 4:
                    odd = jnp.where(left_half, pltpu.roll(low, 64, 1), top)
                    v.w_a[rows_at((2 * p + 1) * 8 + c, 64), :] = odd.astype(BF)

    loop(SPLITS, aux_grad)
    ex.wait()
    d_b = v.d_img_recv[0].astype(F32)
    for k in range(1, OWNERS):
        d_b = d_b + v.d_img_recv[k].astype(F32)
    unit_b = (v.all_b[me].astype(F32) - mean_b) * scale_b
    d_b = d_b * slope(gamma_b * unit_b + beta_b)
    sync = Sync(v.sync_b3)
    sync.start(
        [total(d_b * group_mask(g)) for g in range(4)]
        + [total(d_b * unit_b * group_mask(g)) for g in range(4)]
    )
    mix(s_u.starts(3), s_u.middles(1))
    sums = sync.wait()
    first_b = jnp.zeros((BINS, 128), F32)
    second_b = jnp.zeros((BINS, 128), F32)
    for group in range(4):
        kept = group_mask(group)
        gain_grads[10 + group] = (sums[4 + group : 5 + group], sums[group : group + 1])
        first_b = first_b + kept * sums[group : group + 1]
        second_b = second_b + kept * sums[4 + group : 5 + group]
    inner = d_b - (first_b + unit_b * second_b) * count_b
    v.d_bp[t] = (gamma_b * scale_b * inner).astype(BF)
    spread_d = Spread(v.d_bp)
    spread_d.start()
    mix(s_u.starts(4), s_u.middles(2))
    spread_d.wait()
    d_bp_move = ToGroup(
        lambda owner, rows: v.d_bp.at[:, 0:rows, :],
        lambda slot, rows: v.d_bp_all.at[slot, :, 0:rows, :],
    )
    d_bp_move.start()
    v.d_bp_all[me] = v.d_bp[...]
    d_bp = jnp.concatenate([v.d_bp[k] for k in range(SPLITS)], axis=1)
    d_pooled = jnp.zeros((BINS, 512), F32)
    for group in range(4):
        rows = (d_bp.astype(F32) * group_mask(group)).astype(BF)
        d_pooled = d_pooled + dot_nt(rows, v.w_b[group * 512 : group * 512 + 512, :])
    d_pooled = (d_pooled / cells_in).astype(BF)
    v.d_sum[...] = dot_tn(v.pool[...], d_pooled)
    dm_near(0, t).wait_recv()
    dm_far.wait_recv()

    def through_sum(k, carry):
        at = rows_at(k, 48)
        value = v.d_sum[at, :] + v.joined[t, at, :].astype(F32) + v.dm_near[0, at, :].astype(F32)
        value = (value + v.dm_far[at, :].astype(F32)) * slope(summed(at))
        v.d_sum[at, :] = value
        return (
            carry[0] + fold(value),
            carry[1] + fold(value * normed(v.pre_e, at, norm_e)),
            carry[2] + fold(value * normed(v.pre_s, at, norm_s)),
        )

    zero = jnp.zeros((8, 512), F32)
    three = [total(item) for item in lax.fori_loop(0, 12, through_sum, (zero, zero, zero))]
    sync = Sync(v.sync_b4)
    sync.start(split_rows(three[0]) + split_rows(three[1]) + split_rows(three[2]))
    mix(s_a.starts(), s_u.middles(3))
    sums = sync.wait()
    first_s = join_rows(sums, 0, 4)
    second_e, second_s = join_rows(sums, 4, 4), join_rows(sums, 8, 4)
    for k in range(4):
        gain_grads[6 + k] = (sums[4 + k : 5 + k], sums[k : k + 1])
        gain_grads[1 + k] = (sums[8 + k : 9 + k], sums[k : k + 1])

    def back_both(k):
        at = rows_at(k, 48)
        value, mask = v.d_sum[at, :], wide(v.ins[at, :], 4)
        v.d_e[at, :] = back_norm(
            value, normed(v.pre_e, at, norm_e), mask, norm_e, gamma(6, 4), first_s, second_e, count4
        ).astype(BF)
        v.d_s[at, :] = back_norm(
            value, normed(v.pre_s, at, norm_s), mask, norm_s, gamma(1, 4), first_s, second_s, count4
        ).astype(BF)

    loop(12, back_both)

    def back_hidden(grad, weight, index):
        value = dot_nt(grad, weight)
        for k in range(SPLITS):
            v.dh_send[k] = value[:, k * 128 : k * 128 + 128].astype(BF)
        v.dh_recv[index, t] = v.dh_send[t]
        ex = Exchange(
            TENSOR, SPLITS, lambda o: v.dh_send.at[o], lambda s: v.dh_recv.at[index, s]
        )
        ex.start()
        return ex

    def hidden_sum(index):
        def step(k):
            at = rows_at(k, 96)
            value = v.dh_recv[index, 0, at, :].astype(F32)
            for slot in range(1, SPLITS):
                value = value + v.dh_recv[index, slot, at, :].astype(F32)
            v.d_f[at, :] = value

        loop(6, step)

    ex = back_hidden(v.d_e[...], v.w_e[...], 0)
    def short_grad(c):
        v.w_s[rows_at(c, 256), :] = dot(v.whole_t[c], v.d_s[...]).astype(BF)

    loop(SPLITS, short_grad)
    mix(s_s.starts(), s_u.middles(4))
    for k in range(SPLITS):
        v.w_e[k * 128 : k * 128 + 128, :] = dot_tn(v.h2[k], v.d_e[...]).astype(BF)
    ex.wait()
    hidden_sum(0)
    sync = Sync(v.sync_b5)
    sync.start(through_silu(v.d_f, v.pre_m, norm_m, 5))
    mix(s_e.starts())
    mix(s_c.middles())
    mix(s_ac.middles())
    mix(s_a.middles())
    sums = sync.wait()
    gain_grads[5] = (sums[1:2], sums[0:1])
    spread_taps(v.d_f, v.pre_m, norm_m, 5, sums[0:1], sums[1:2])
    fill(v.cat_u, 4)
    weight = jnp.concatenate([v.w_m[tap * 512 : tap * 512 + 512, :] for tap in range(9)], axis=1)
    ex = back_hidden(v.cat_u[...], weight, 1)

    def middle_grad(k):
        value = dot_tn(v.h1[k], v.cat_u[...])
        for tap in range(9):
            v.w_m[rows_at(tap * 4 + k, 128), :] = value[:, tap * 128 : tap * 128 + 128].astype(BF)

    loop(SPLITS, middle_grad)
    mix(s_m.starts())
    mix(s_s.middles())
    ex.wait()
    hidden_sum(1)
    sync = Sync(v.sync_b6)
    sync.start(through_silu(v.d_f, v.pre_r, norm_r, 0))

    mix(s_e.middles())
    sums = sync.wait()
    gain_grads[0] = (sums[1:2], sums[0:1])

    def back_reduce(k):
        at = rows_at(k, 96)
        v.d_low[at, :] = back_norm(
            v.d_f[at, :], normed(v.pre_r, at, norm_r), v.ins[at, :], norm_r, gamma(0), sums[0:1], sums[1:2], count
        ).astype(BF)

    loop(6, back_reduce)

    def reduce_grad(c):
        v.w_r[rows_at(c, 256), :] = dot(v.whole_t[c], v.d_low[...]).astype(BF)

    loop(SPLITS, reduce_grad)
    mix(s_r.starts())
    mix(s_m.middles() + s_r.middles())
    pool_move.wait()
    d_bp_move.wait()
    own_group = jnp.where(group_id == lax.div(me, 2), 1.0, 0.0)
    d_rows = jnp.concatenate(
        [v.d_bp_all[:, k].reshape(OWNERS * BINS, 128) for k in range(SPLITS)], axis=1
    )
    d_rows = (d_rows.astype(F32) * own_group).astype(BF)
    branch_grad = dot_tn(v.pool_all[...].reshape(OWNERS * BINS, 256), d_rows)
    for k in range(4):
        o_flat[pl.ds(1472 + k, 256, stride=4), :] = branch_grad[:, k * 128 : k * 128 + 128]
    rest = (s_c, s_ac, s_a, s_e, s_s, s_m, s_r)
    squares = s_u.end() + sum(split_rows(total(branch_grad * branch_grad)))
    for item in rest:
        squares = squares + item.end()
    dm_near(1, t_diag).wait_send()
    dm_near(0, t_core).wait_send()
    dm_far.wait_send()

    v.gain_rows[...] = jnp.zeros((40, 128), F32)
    gammas = [gain_grads[row][0] for row in range(16)]
    betas = [pltpu.roll(gain_grads[row][1], 64, 1) for row in range(16)]
    o_shift[...] = gain_grads[14][1]
    for row in range(31):
        if row < 15:
            value = gammas[row]
        else:
            left = gammas[15] if row == 15 else betas[row - 16]
            value = jnp.where(lane < 64, left, betas[row - 15])
        v.gain_rows[row + 1 : row + 2, :] = value
    squares = squares + total(fold(v.gain_rows[...] * v.gain_rows[...])) / OWNERS

    sync = Sync(v.sync_end)
    sync.start([squares, o_misc[1:2, :]])

    tail = {}

    def put(where, value):
        tail[where] = value if where not in tail else tail[where] + value

    def class_tail(ref, count, base):
        for row in range(count):
            first, shift = divmod(base + NCLS * row, 128)
            for k in range(2):
                value = roll(ref[row : row + 1, k * 128 : k * 128 + 128], shift)
                put(first + k, jnp.where(lane >= shift, value, 0.0))
                if shift:
                    put(first + k + 1, jnp.where(lane < shift, value, 0.0))

    class_tail(v.out_c, 16, 0)
    class_tail(v.out_ac, 8, 76128)
    start = lax.rem(496 * me, 128)
    first = lax.div(496 * me, 128)
    own = [
        pltpu.roll(v.gain_rows[pl.ds(first + k, 1), :], lax.rem(16 - start + 128, 128), 1)
        for k in range(6)
    ]
    spot = lane - 16 + start
    for k in range(4):
        value = jnp.where(spot < 0, own[k], jnp.where(spot >= 128, own[k + 2], own[k + 1]))
        put(604 + k, jnp.where(lane >= 16, value, 0.0) if k == 0 else value)
    v.grad_pad[EDGE : EDGE + 576, :] = pltpu.roll(v.out_a[...], 96, 1)
    o_flat[7122:7706, :] = jnp.where(
        lane >= 96, v.grad_pad[EDGE : EDGE + 584, :], v.grad_pad[EDGE - 1 : EDGE + 583, :]
    )
    for row in range(608):
        if row in (18, 594):
            o_flat[7104 + row : 7105 + row, :] = o_flat[7104 + row : 7105 + row, :] + tail[row]
        elif row < 18 or row > 594:
            o_flat[7104 + row : 7105 + row, :] = tail[row]
    v.end_t[t] = sync.wait()
    spread_e = Spread(v.end_t)
    spread_e.start()
    spread_e.wait()
    ends = v.end_t[0]
    for k in range(1, SPLITS):
        ends = ends + v.end_t[k]
    o_misc[...] = ends
    o_misc[2:3, :] = jnp.broadcast_to(class_weights()[1], (1, 128))


def whole_step(sizes, labels, feat, flat):
    plan = scratch_plan()
    vmem = pl.BlockSpec(memory_space=pltpu.VMEM)
    anywhere = pl.BlockSpec(memory_space=pl.ANY)
    outs = [flat.shape, (1, 128), (8, 128)]
    return pl.pallas_call(
        functools.partial(step_kernel, tuple(plan)),
        out_shape=[jax.ShapeDtypeStruct(shape, F32) for shape in outs],
        in_specs=[pl.BlockSpec(memory_space=pltpu.SMEM), vmem, anywhere, anywhere],
        out_specs=[vmem] * len(outs),
        scratch_shapes=[pltpu.VMEM(shape, kind) for shape, kind in plan.values()]
        + [pltpu.SemaphoreType.DMA((SEMAPHORES,))],
        compiler_params=pltpu.CompilerParams(
            collective_id=0, has_side_effects=True, vmem_limit_bytes=63 * 1024 * 1024
        ),
        name="whole_step",
    )(sizes, labels, feat, flat)


def update_kernel(
    misc, grad, param, first, second, average,
    o_param, o_first, o_second, o_average, o_norm, o_loss, o_weight,
):
    norm = jnp.sqrt(jnp.sum(misc[0:1, :], axis=1, keepdims=True))
    o_norm[...] = norm
    o_loss[...] = jnp.sum(misc[1:2, :], axis=1, keepdims=True)
    o_weight[...] = misc[2:3, 0:1]
    clipped = grad[...] * jnp.minimum(1.0, 0.05 / (norm + 1e-06))
    new_first = 0.5 * first[...] + 0.5 * clipped
    new_second = 0.5 * second[...] + 0.5 * clipped * clipped
    lift = 1.0 / (1.0 - 0.5**STEP)
    old = param[...]
    ratio = (new_first * lift) / (jnp.sqrt(new_second * lift) + 1e-08)
    new = old - 0.01 * (ratio + 0.01 * old)
    o_param[...] = new
    o_first[...] = new_first
    o_second[...] = new_second
    o_average[...] = 0.999 * average[...] + 0.001 * new


def update(misc, grad, param, first, second, average):
    rows = grad.shape[0]
    block = pl.BlockSpec((1024, 128), lambda i: (i, 0))
    whole = pl.BlockSpec((8, 128), lambda i: (0, 0))
    one = pl.BlockSpec((1, 1), lambda i: (0, 0))
    big = jax.ShapeDtypeStruct((rows, 128), F32)
    return pl.pallas_call(
        update_kernel,
        grid=(pl.cdiv(rows, 1024),),
        out_shape=[big] * 4 + [jax.ShapeDtypeStruct((1, 1), F32)] * 3,
        in_specs=[whole] + [block] * 5,
        out_specs=[block] * 4 + [one] * 3,
        compiler_params=pltpu.CompilerParams(vmem_limit_bytes=60 * 1024 * 1024),
        name="update",
    )(misc, grad, param, first, second, average)


def fits(splits, owners):
    return splits == SPLITS and owners == OWNERS


def local_fast(features, labels, valid, sizes, params, first_moment, squared_mean, average):
    flat = params.reshape(-1, 128)
    marked = jnp.where(valid > 0, labels, -1).astype(F32).reshape(CELLS, 1)
    grad, shift_grad, misc = whole_step(
        sizes, jnp.broadcast_to(marked, (CELLS, 128)), features.reshape(CELLS, -1), flat
    )
    news = update(
        misc,
        grad,
        flat,
        first_moment.reshape(-1, 128),
        squared_mean.reshape(-1, 128),
        average.reshape(-1, 128),
    )
    new_params, new_first, new_second, new_average = [
        item.reshape(params.shape) for item in news[:4]
    ]
    return (
        new_params,
        new_first,
        new_second,
        new_average,
        new_params.astype(BF),
        news[4].reshape(()),
        news[5].reshape(()),
        news[6].reshape(()),
        shift_grad.reshape(128),
    )


def solution(mesh):
    chosen = local_fast if fits(mesh.shape["tensor"], mesh.shape["batch"]) else local
    return jax.shard_map(
        chosen,
        mesh=mesh,
        in_specs=(
            P("batch", None, None, "tensor"),
            P("batch", None, None),
            P("batch", None, None),
            P("batch", None),
            P("tensor", "batch"),
            P("tensor", "batch"),
            P("tensor", "batch"),
            P("tensor", "batch"),
        ),
        out_specs=(
            P("tensor", "batch"),
            P("tensor", "batch"),
            P("tensor", "batch"),
            P("tensor", "batch"),
            P("tensor", "batch"),
            P(),
            P(),
            P(),
            P("tensor"),
        ),
        check_vma=False,
    )
```

```python
import functools

import jax
import jax.numpy as jnp
from jax import lax
from jax.experimental import pallas as pl
from jax.experimental.pallas import tpu as pltpu
from jax.sharding import PartitionSpec as P

C_IN = 1024
MID = 512
C_OUT = 2048
PPM = 512
AUXW = 256
NCLS = 150
MAP = 24
STEP = 3


BIN_COUNTS = (1, 2, 3, 6)
BIN_STARTS = (0, 1, 5, 14)


def segment_shapes(splits):
    return [
        (C_IN, MID // splits),
        (C_IN, C_OUT // splits),
        (9, MID, MID // splits),
        (MID, C_OUT // splits),
        (4, C_OUT // splits, PPM),
        (9, C_OUT + 4 * PPM, PPM // splits),
        (PPM // splits, NCLS),
        (9, C_IN, AUXW // splits),
        (AUXW // splits, NCLS),
        (2, (2 * MID + 2 * C_OUT + 5 * PPM + AUXW) // splits),
    ]


def unflatten(rows, splits):
    split_parts = []
    start = 0
    for shape in segment_shapes(splits):
        count = 1
        for extent in shape:
            count = count * extent
        count = count // rows.shape[0]
        split_parts.append(rows[:, start : start + count].reshape(shape))
        start = start + count
    return split_parts


def gain_pieces(gains, splits):
    widths = [MID, C_OUT, MID, C_OUT, PPM, PPM, PPM, PPM, PPM, AUXW]
    split_parts = []
    start = 0
    for width in widths:
        step_width = width // splits
        split_parts.append(gains[:, start : start + step_width])
        start = start + step_width
    return split_parts


def shifted(field, down, right):
    image_height, width = (field.shape[1], field.shape[2])
    rows_pad, cols_pad = (abs(down), abs(right))
    padded = jnp.pad(field, ((0, 0), (rows_pad, rows_pad), (cols_pad, cols_pad), (0, 0)))
    return padded[
        :,
        rows_pad + down : rows_pad + down + image_height,
        cols_pad + right : cols_pad + right + width,
        :,
    ]


def conv_forward(field, kernel, spacing):
    total = jnp.zeros(field.shape[:-1] + (kernel.shape[2],), jnp.float32)
    for tap in range(9):
        moved = shifted(field, (tap // 3 - 1) * spacing, (tap % 3 - 1) * spacing)
        total = total + jnp.dot(moved, kernel[tap], preferred_element_type=jnp.float32)
    return total


def conv_input_back(grad, kernel, spacing):
    total = jnp.zeros(grad.shape[:-1] + (kernel.shape[1],), jnp.float32)
    for tap in range(9):
        product = jnp.dot(grad, kernel[tap].T, preferred_element_type=jnp.float32)
        total = total + shifted(product, -(tap // 3 - 1) * spacing, -(tap % 3 - 1) * spacing)
    return total


def conv_kernel_back(field, grad, spacing):
    return jnp.stack(
        [
            jnp.einsum(
                "ihwc,ihwd->cd",
                shifted(field, (tap // 3 - 1) * spacing, (tap % 3 - 1) * spacing),
                grad,
                preferred_element_type=jnp.float32,
            )
            for tap in range(9)
        ]
    )


def silu_slope(value):
    gate = jax.nn.sigmoid(value)
    return gate * (1.0 + value * (1.0 - gate))


def channel_sums(values):
    return values.reshape(-1, values.shape[-1]).sum(0)


def masked_norm_apply(items, extra):
    sends = []
    for value, mask, norm in items:
        sends = sends + [
            channel_sums(value * mask),
            channel_sums(value * value * mask),
            jnp.sum(mask) * jnp.ones((1,), jnp.float32),
        ]
    totals = lax.psum(tuple(sends + extra), "batch")
    results = []
    for index, (value, mask, norm) in enumerate(items):
        count = totals[3 * index + 2]
        mean = totals[3 * index] / count
        spread = totals[3 * index + 1] / count - mean * mean
        scaling = lax.rsqrt(spread + 1e-05)
        normed = (value - mean) * scaling
        results.append((norm[0] * normed + norm[1], normed, scaling, count, mask, norm[0]))
    return (results, totals[3 * len(items) :])


def norm_backward(items):
    sends = []
    for grad, kept in items:
        sends = sends + [channel_sums(grad), channel_sums(grad * kept[1])]
    totals = lax.psum(tuple(sends), "batch")
    results = []
    for index, (grad, kept) in enumerate(items):
        outcome, normed, scaling, count, mask, gamma = kept
        first_sum, second_sum = (totals[2 * index], totals[2 * index + 1])
        inner = grad - mask * (first_sum + normed * second_sum) / count
        results.append(gamma * scaling * inner)
    return (results, sends, totals)


def bin_tables(extent, bins, length):
    which = jnp.arange(bins, dtype=jnp.int32)[None, :, None]
    place = jnp.arange(length, dtype=jnp.int32)[None, None, :]
    edge = extent[:, None, None]
    lower = which * edge // bins
    upper = ((which + 1) * edge + bins - 1) // bins
    member = ((place >= lower) & (place < upper)).astype(jnp.float32)
    target = jnp.minimum(place * bins // edge, bins - 1)
    chosen = (target == which).astype(jnp.float32)
    return (member, chosen)


def spread_bins(merged, branch, tables, images):
    joined = [merged]
    for group, bins in enumerate(BIN_COUNTS):
        rows_in, cols_in, rows_pick, cols_pick, cell_count = tables[group]
        piece = branch[:, BIN_STARTS[group] : BIN_STARTS[group] + bins * bins].reshape(
            images, bins, bins, -1
        )
        joined.append(
            jnp.einsum(
                "ikh,ilw,iklc->ihwc",
                rows_pick.astype(jnp.bfloat16),
                cols_pick.astype(jnp.bfloat16),
                piece,
                preferred_element_type=jnp.float32,
            ).astype(jnp.bfloat16)
        )
    return jnp.concatenate(joined, axis=-1)


def pick_bins(d_joined, width, tables, images):
    branch_width = (d_joined.shape[-1] - width) // 4
    d_up = []
    for group, bins in enumerate(BIN_COUNTS):
        rows_in, cols_in, rows_pick, cols_pick, cell_count = tables[group]
        piece = d_joined[..., width + group * branch_width : width + (group + 1) * branch_width]
        d_up.append(
            jnp.einsum("ikh,ilw,ihwc->iklc", rows_pick, cols_pick, piece).reshape(
                images, bins * bins, -1
            )
        )
    return (d_joined[..., :width], jnp.concatenate(d_up, axis=1))


def gather_channels(field):
    return lax.all_gather(field, "tensor", axis=3, tiled=True)


def scatter_channels(field):
    return lax.psum_scatter(
        field.astype(jnp.bfloat16), "tensor", scatter_dimension=3, tiled=True
    ).astype(jnp.float32)


def local(features, labels, valid, sizes, params, first_moment, squared_mean, average):
    splits = lax.axis_size("tensor")
    owners = lax.axis_size("batch")
    images = features.shape[0]
    gathered = lax.all_gather(params.astype(jnp.bfloat16), "batch", axis=0, tiled=True)
    (
        w_reduce,
        w_short,
        w_middle,
        w_expand,
        w_branch,
        w_unite,
        w_classes,
        w_aux,
        w_aux_classes,
        gains,
    ) = unflatten(gathered, splits)
    norms = [(piece[0], piece[1]) for piece in gain_pieces(gains.astype(jnp.float32), splits)]
    rows_at = jnp.arange(MAP, dtype=jnp.int32)
    inside = (rows_at[None, :, None] < sizes[:, 0][:, None, None]) & (
        rows_at[None, None, :] < sizes[:, 1][:, None, None]
    )
    inside = inside.astype(jnp.float32)[..., None]
    counted = inside * valid.astype(jnp.float32)[..., None]
    labels_hot = (labels[..., None] == jnp.arange(NCLS, dtype=jnp.int32)).astype(jnp.float32)
    class_local = channel_sums(labels_hot * counted)
    whole = lax.all_gather(features, "tensor", axis=3, tiled=True)
    pre_reduce = jnp.dot(whole, w_reduce, preferred_element_type=jnp.float32)
    pre_short = jnp.dot(whole, w_short, preferred_element_type=jnp.float32)
    pre_aux = conv_forward(whole, w_aux, 1)
    leading_part, label_tally = masked_norm_apply(
        [
            (pre_reduce, inside, norms[0]),
            (pre_short, inside, norms[1]),
            (pre_aux, inside, norms[9]),
        ],
        [class_local],
    )
    class_pixel_counts = label_tally[0]
    hidden_one = jax.nn.silu(leading_part[0][0]).astype(jnp.bfloat16)
    aux_act = jax.nn.silu(leading_part[2][0]).astype(jnp.bfloat16)
    hidden_full = gather_channels(hidden_one)
    pre_middle = conv_forward(hidden_full, w_middle, 4)
    second, unused = masked_norm_apply([(pre_middle, inside, norms[2])], [])
    hidden_two = jax.nn.silu(second[0][0]).astype(jnp.bfloat16)
    hidden_two_full = gather_channels(hidden_two)
    pre_expand = jnp.dot(hidden_two_full, w_expand, preferred_element_type=jnp.float32)
    third, unused = masked_norm_apply([(pre_expand, inside, norms[3])], [])
    summed = third[0][0] + leading_part[1][0]
    merged = jax.nn.silu(summed).astype(jnp.bfloat16)
    tables = []
    pooled_list = []
    partial_list = []
    for group, bins in enumerate(BIN_COUNTS):
        rows_in, rows_pick = bin_tables(sizes[:, 0], bins, MAP)
        cols_in, cols_pick = bin_tables(sizes[:, 1], bins, MAP)
        cell_count = (
            jnp.sum(rows_in, axis=2)[:, :, None, None] * jnp.sum(cols_in, axis=2)[:, None, :, None]
        )
        tables.append((rows_in, cols_in, rows_pick, cols_pick, cell_count))
        pooled = (
            jnp.einsum(
                "ikh,ilw,ihwc->iklc",
                rows_in.astype(jnp.bfloat16),
                cols_in.astype(jnp.bfloat16),
                merged,
                preferred_element_type=jnp.float32,
            )
            / cell_count
        )
        pooled = pooled.astype(jnp.bfloat16).reshape(images, bins * bins, -1)
        pooled_list.append(pooled)
        partial_list.append(
            jnp.einsum("ipc,cd->ipd", pooled, w_branch[group], preferred_element_type=jnp.float32)
        )
    branch_pre = lax.psum_scatter(
        jnp.concatenate(partial_list, axis=1).astype(jnp.bfloat16),
        "tensor",
        scatter_dimension=2,
        tiled=True,
    ).astype(jnp.float32)
    branch_items = []
    for group, bins in enumerate(BIN_COUNTS):
        piece = branch_pre[:, BIN_STARTS[group] : BIN_STARTS[group] + bins * bins]
        branch_items.append(
            (piece, jnp.ones(piece.shape[:-1] + (1,), jnp.float32), norms[4 + group])
        )
    fourth, unused = masked_norm_apply(branch_items, [])
    branch_act = jnp.concatenate([jax.nn.silu(kept[0]) for kept in fourth], axis=1).astype(
        jnp.bfloat16
    )
    merged_full, branch_full = (
        lax.all_gather(merged, "tensor", axis=3, tiled=True),
        lax.all_gather(branch_act, "tensor", axis=2, tiled=True),
    )
    joined = spread_bins(merged_full, branch_full, tables, images)
    pre_unite = conv_forward(joined, w_unite, 1)
    fifth, unused = masked_norm_apply([(pre_unite, inside, norms[8])], [])
    united = jax.nn.silu(fifth[0][0]).astype(jnp.bfloat16)
    logit_main, logit_aux = (
        lax.psum_scatter(
            jnp.dot(united, w_classes, preferred_element_type=jnp.float32).astype(jnp.bfloat16),
            "tensor",
            scatter_dimension=1,
            tiled=True,
        ).astype(jnp.float32),
        lax.psum_scatter(
            jnp.dot(aux_act, w_aux_classes, preferred_element_type=jnp.float32).astype(
                jnp.bfloat16
            ),
            "tensor",
            scatter_dimension=1,
            tiled=True,
        ).astype(jnp.float32),
    )
    total_valid = jnp.sum(class_pixel_counts)
    class_weight = total_valid / (NCLS * class_pixel_counts + total_valid)
    loss_weight = jnp.sum(class_pixel_counts * class_weight)
    cell_weight = jnp.sum(labels_hot * class_weight, axis=-1, keepdims=True) * counted
    band_rows = labels.shape[1] // splits
    band_start = lax.axis_index("tensor") * band_rows
    hot_band = lax.dynamic_slice_in_dim(labels_hot, band_start, band_rows, 1)
    weight_band = lax.dynamic_slice_in_dim(cell_weight, band_start, band_rows, 1)
    log_main = jax.nn.log_softmax(logit_main, axis=-1)
    log_aux = jax.nn.log_softmax(logit_aux, axis=-1)
    loss_cells = -jnp.sum(hot_band * (log_main + 0.4 * log_aux), axis=-1, keepdims=True)
    loss_local = jnp.sum(weight_band * loss_cells)
    band_main = (weight_band * (jnp.exp(log_main) - hot_band) / loss_weight).astype(jnp.bfloat16)
    band_aux = (0.4 * weight_band * (jnp.exp(log_aux) - hot_band) / loss_weight).astype(
        jnp.bfloat16
    )
    grad_main, grad_aux = (
        lax.all_gather(band_main, "tensor", axis=1, tiled=True),
        lax.all_gather(band_aux, "tensor", axis=1, tiled=True),
    )
    reduced = {}

    def settle(index, value):
        reduced[index] = value

    settle(6, jnp.einsum("ihwc,ihwk->ck", united, grad_main, preferred_element_type=jnp.float32))
    settle(8, jnp.einsum("ihwc,ihwk->ck", aux_act, grad_aux, preferred_element_type=jnp.float32))
    d_united = jnp.dot(grad_main, w_classes.T, preferred_element_type=jnp.float32) * silu_slope(
        fifth[0][0]
    )
    d_aux = jnp.dot(grad_aux, w_aux_classes.T, preferred_element_type=jnp.float32) * silu_slope(
        leading_part[2][0]
    )
    back_one, sums_one, totals_one = norm_backward([(d_united, fifth[0]), (d_aux, leading_part[2])])
    unite_shift_grad = totals_one[0]
    d_unite_pre = back_one[0].astype(jnp.bfloat16)
    d_aux_pre = back_one[1].astype(jnp.bfloat16)
    settle(5, conv_kernel_back(joined, d_unite_pre, 1))
    d_merged, d_branch = pick_bins(conv_input_back(d_unite_pre, w_unite, 1), C_OUT, tables, images)
    d_merged, d_branch = (
        lax.psum_scatter(
            d_merged.astype(jnp.bfloat16), "tensor", scatter_dimension=3, tiled=True
        ).astype(jnp.float32),
        lax.psum_scatter(
            d_branch.astype(jnp.bfloat16), "tensor", scatter_dimension=2, tiled=True
        ).astype(jnp.float32),
    )
    settle(7, conv_kernel_back(whole, d_aux_pre, 1))
    branch_back = []
    for group, bins in enumerate(BIN_COUNTS):
        piece = d_branch[:, BIN_STARTS[group] : BIN_STARTS[group] + bins * bins]
        branch_back.append((piece * silu_slope(fourth[group][0]), fourth[group]))
    back_two, sums_two, unused = norm_backward(branch_back)
    d_branch_pre = jnp.concatenate(back_two, axis=1).astype(jnp.bfloat16)
    d_branch_full = lax.all_gather(d_branch_pre, "tensor", axis=2, tiled=True)
    branch_grads = []
    for group, bins in enumerate(BIN_COUNTS):
        rows_in, cols_in, rows_pick, cols_pick, cell_count = tables[group]
        piece = d_branch_full[:, BIN_STARTS[group] : BIN_STARTS[group] + bins * bins]
        branch_grads.append(
            jnp.einsum("ipc,ipd->cd", pooled_list[group], piece, preferred_element_type=jnp.float32)
        )
        d_pooled = jnp.dot(piece, w_branch[group].T, preferred_element_type=jnp.float32).reshape(
            images, bins, bins, -1
        )
        d_merged = d_merged + jnp.einsum(
            "ikh,ilw,iklc->ihwc", rows_in, cols_in, d_pooled / cell_count
        )
    settle(4, jnp.stack(branch_grads))
    d_summed = d_merged * silu_slope(summed)
    back_three, sums_three, unused = norm_backward(
        [(d_summed, third[0]), (d_summed, leading_part[1])]
    )
    d_expand_pre = back_three[0].astype(jnp.bfloat16)
    d_short_pre = back_three[1].astype(jnp.bfloat16)
    settle(
        3,
        jnp.einsum(
            "ihwc,ihwd->cd", hidden_two_full, d_expand_pre, preferred_element_type=jnp.float32
        ),
    )
    settle(1, jnp.einsum("ihwc,ihwd->cd", whole, d_short_pre, preferred_element_type=jnp.float32))
    d_two = scatter_channels(jnp.dot(d_expand_pre, w_expand.T, preferred_element_type=jnp.float32))
    back_four, sums_four, unused = norm_backward([(d_two * silu_slope(second[0][0]), second[0])])
    d_middle_pre = back_four[0].astype(jnp.bfloat16)
    settle(2, conv_kernel_back(hidden_full, d_middle_pre, 4))
    d_one = scatter_channels(conv_input_back(d_middle_pre, w_middle, 4))
    back_five, sums_five, unused = norm_backward(
        [(d_one * silu_slope(leading_part[0][0]), leading_part[0])]
    )
    settle(
        0,
        jnp.einsum(
            "ihwc,ihwd->cd",
            whole,
            back_five[0].astype(jnp.bfloat16),
            preferred_element_type=jnp.float32,
        ),
    )
    beta_grads = (
        [sums_five[0], sums_three[2], sums_four[0], sums_three[0]]
        + [sums_two[2 * g] for g in range(4)]
        + [sums_one[0], sums_one[2]]
    )
    gamma_grads = (
        [sums_five[1], sums_three[3], sums_four[1], sums_three[1]]
        + [sums_two[2 * g + 1] for g in range(4)]
        + [sums_one[1], sums_one[3]]
    )
    settle(9, jnp.stack([jnp.concatenate(gamma_grads), jnp.concatenate(beta_grads)]))
    ordered = [reduced[index] for index in range(10)]
    grad_share = lax.psum_scatter(
        jnp.concatenate([part.reshape(owners, -1) for part in ordered], axis=1),
        "batch",
        scatter_dimension=0,
        tiled=True,
    )
    square_all, loss_sum = lax.psum(
        (jnp.sum(grad_share * grad_share), loss_local), ("batch", "tensor")
    )
    grad_norm = jnp.sqrt(square_all)
    clipped = grad_share * jnp.minimum(1.0, 0.05 / (grad_norm + 1e-06))
    new_first = 0.5 * first_moment + 0.5 * clipped
    new_second = 0.5 * squared_mean + 0.5 * clipped * clipped
    keep = 1.0 - 0.5**STEP
    new_params = params - 0.01 * (
        new_first / keep / (jnp.sqrt(new_second / keep) + 1e-08) + 0.01 * params
    )
    new_average = 0.999 * average + 0.001 * new_params
    return (
        new_params,
        new_first,
        new_second,
        new_average,
        new_params.astype(jnp.bfloat16),
        grad_norm,
        loss_sum,
        loss_weight,
        unite_shift_grad,
    )


CELLS = MAP * MAP
EDGE = 104
BATCH = "batch"
TENSOR = "tensor"
GROUP_ROWS = ((0, 1), (1, 5), (5, 14), (14, 50))
BINS = 64
BF = jnp.bfloat16
F32 = jnp.float32
MESH = pl.DeviceIdType.MESH
HALF = 4
OWNERS = 8
SPLITS = 4
MERGED = 4
SLOTS = 5


def scratch_plan():
    plan = dict(
        w_r=((1024, 128), BF),
        w_s=((1024, 512), BF),
        w_m=((4608, 128), BF),
        w_e=((512, 512), BF),
        w_b=((2048, 512), BF),
        w_u=((18432, 128), BF),
        w_own=((4608, 128), BF),
        w_a=((4608, 128), BF),
        w_pair=((1024, 640), BF),
        w_c=((128, 256), BF),
        w_ac=((64, 256), F32),
        gain_in=((OWNERS, 8, 128), F32),
        gain_rows=((40, 128), F32),
        out_a=((576, 128), F32),
        out_c=((16, 256), F32),
        out_ac=((8, 256), F32),
        whole=((SPLITS, CELLS, 256), BF),
        whole_t=((SPLITS, 256, CELLS), BF),
        w_c_all=((SPLITS, 128, 256), BF),
        slope_main=((CELLS, 256), BF),
        ins=((CELLS, 128), F32),
        col=((CELLS, 128), F32),
        lab=((CELLS, 128), F32),
        table=((BINS, CELLS), F32),
        pool=((BINS, CELLS), BF),
        pick=((BINS, CELLS), BF),
        cells_in=((BINS, 128), F32),
        pad=((9, CELLS + 2 * EDGE, 128), F32),
        grad_pad=((CELLS + 2 * EDGE, 128), F32),
        pre_r=((CELLS, 128), F32),
        pre_s=((CELLS, 512), F32),
        pre_a=((CELLS, 128), F32),
        pre_m=((CELLS, 128), F32),
        pre_e=((CELLS, 512), F32),
        pre_u=((CELLS, 128), F32),
        act_a=((CELLS, 128), BF),
        h1=((SPLITS, CELLS, 128), BF),
        h2=((SPLITS, CELLS, 128), BF),
        joined=((SPLITS, CELLS, 512), BF),
        joined_t=((SPLITS, 512, CELLS), BF),
        pooled=((BINS, 512), BF),
        pool_half=((2, BINS, 256), BF),
        pool_all=((OWNERS, BINS, 256), BF),
        d_bp_all=((OWNERS, SPLITS, BINS, 128), BF),
        part_b=((SPLITS, BINS, 128), BF),
        recv_b=((SPLITS, BINS, 128), BF),
        all_b=((OWNERS, BINS, 128), BF),
        act_b=((SPLITS, OWNERS * BINS, 128), BF),
        pick_t=((CELLS, 128), BF),
        z_cat=((9, 128, 128), BF),
        act_t=((512, OWNERS * BINS), BF),
        zsum=((2, OWNERS * BINS, 128), F32),
        z_send=((OWNERS, 2, BINS, 128), BF),
        z_recv=((OWNERS, 2, BINS, 128), BF),
        united=((SPLITS, CELLS, 128), BF),
        logit_send=((CELLS, 512), BF),
        logit_recv=((SPLITS, 144, 512), BF),
        slope_in=((SPLITS, 144, 512), BF),
        d_f=((CELLS, 128), F32),
        d_f2=((CELLS, 128), F32),
        cat_u=((CELLS, 1152), BF),
        cat_a=((CELLS, 640), BF),
        dz_send=((9, BINS, 128), BF),
        dz_recv=((OWNERS, 2, BINS, 128), BF),
        d_act_send=((SPLITS, OWNERS * BINS, 128), BF),
        d_act_recv=((SPLITS, OWNERS * BINS, 128), BF),
        d_img_send=((OWNERS, BINS, 128), BF),
        d_img_recv=((OWNERS, BINS, 128), BF),
        d_bp=((SPLITS, BINS, 128), BF),
        dm_near=((2, CELLS, 512), BF),
        dm_far=((CELLS, 512), BF),
        d_sum=((CELLS, 512), F32),
        d_e=((CELLS, 512), BF),
        d_s=((CELLS, 512), BF),
        dh_send=((SPLITS, CELLS, 128), BF),
        dh_recv=((2, SPLITS, CELLS, 128), BF),
        d_low=((CELLS, 128), BF),
        end_t=((SPLITS, 8, 128), F32),
    )
    for name, rows in SYNCS.items():
        plan["sync_" + name] = ((OWNERS, rows, 128), F32)
    for name, (rows, lanes, kind) in PARTS.items():
        plan["first_" + name] = ((HALF, rows, lanes), kind)
        plan["second_" + name] = ((HALF - 1, rows, lanes), kind)
    plan["first_u"] = ((HALF, SLOTS, 512, 128), BF)
    plan["second_u"] = ((HALF - 1, SLOTS, 512, 128), BF)
    return plan


SYNCS = dict(one=8, two=8, three=16, five=8, aux=8, b1=8, b2=8, b3=8, b4=16, b5=8, b6=8, end=8)
PARTS = dict(
    r=(128, 128, BF),
    s=(128, 512, BF),
    m=(576, 128, BF),
    e=(64, 512, BF),
    a=(576, 128, BF),
    c=(16, 256, BF),
    ac=(8, 256, F32),
)
SEMAPHORES = 1100
LOADS = (0, 128, 640, 1216, 1472, 2496, 7104, 7712)
LOAD_ORDER = (0, 2, 3, 1, 4, 6, 5)


class Refs:
    pass


def fold(value):
    return value.reshape(-1, 8, value.shape[-1]).sum(0)


def total(value):
    return jnp.sum(value, axis=0, keepdims=True)


def wide(value, times):
    return jnp.concatenate([value] * times, axis=1)


def dot(left, right):
    return jnp.dot(left, right, preferred_element_type=F32)


def dot_nt(left, right):
    return lax.dot_general(left, right, (((1,), (1,)), ((), ())), preferred_element_type=F32)


def dot_tn(left, right):
    return lax.dot_general(left, right, (((0,), (0,)), ((), ())), preferred_element_type=F32)


def loop(count, body):
    def step(k, carry):
        body(k)
        return carry

    lax.fori_loop(0, count, step, 0)


def rows_at(k, block):
    return pl.ds(pl.multiple_of(k * block, block), block)


def step_kernel(names, *refs):
    (
        sizes, lab_in, feat, flat, o_flat, o_shift, o_misc,
    ) = refs[:7]
    v = Refs()
    for name, ref in zip(names, refs[7:]):
        setattr(v, name, ref)
    sems = refs[-1]
    o_u = o_flat.at[2496:7104, :]
    me = lax.axis_index(BATCH)
    t = lax.axis_index(TENSOR)
    partner = me + 1 - 2 * lax.rem(me, 2)
    t_core = t + 1 - 2 * lax.rem(t, 2)
    t_x = lax.rem(t + 2, SPLITS)
    t_diag = lax.rem(t_core + 2, SPLITS)
    taken = [0]

    def take(count):
        start = taken[0]
        taken[0] = start + count
        assert taken[0] <= SEMAPHORES
        return start

    def far_peer(base, step):
        return lax.rem(base + 2 * step, OWNERS)

    def remote(src, dst, send, recv, device):
        return pltpu.make_async_remote_copy(
            src_ref=src,
            dst_ref=dst,
            send_sem=sems.at[send],
            recv_sem=sems.at[recv],
            device_id=device,
            device_id_type=MESH,
        )

    def mix(*lists):
        for turn in range(max(len(items) for items in lists)):
            for items in lists:
                if turn < len(items):
                    items[turn]()

    load_at = take(len(LOADS))

    def load(index):
        at = pl.ds(LOADS[index], LOADS[index + 1] - LOADS[index])
        return pltpu.make_async_copy(flat.at[at, :], o_flat.at[at, :], sems.at[load_at + index])

    for index in LOAD_ORDER:
        load(index).start()
    v.pool_all[...] = jnp.zeros((OWNERS, BINS, 256), BF)
    v.d_bp_all[...] = jnp.zeros((OWNERS, SPLITS, BINS, 128), BF)
    barrier = pltpu.get_barrier_semaphore()
    for k in range(1, OWNERS):
        pl.semaphore_signal(
            barrier, inc=1, device_id={BATCH: lax.rem(me + k, OWNERS)}, device_id_type=MESH
        )
    for k in range(1, SPLITS):
        pl.semaphore_signal(
            barrier, inc=1, device_id={TENSOR: lax.rem(t + k, SPLITS)}, device_id_type=MESH
        )
    pl.semaphore_wait(barrier, OWNERS + SPLITS - 2)

    class Gather:
        def __init__(self, full, rows, skip=0, step=None, piece=None):
            self.full, self.rows, self.piece = full, rows, piece
            self.skip, self.part = skip, step or rows
            self.near_s, self.far_s, self.pass_s = take(1), take(HALF), take(HALF)
            self.recv, self.keep = take(OWNERS), take(1)

        def at(self, owner):
            if self.rows is None:
                return self.full.at[owner]
            start = pl.multiple_of(owner * self.rows + self.skip, self.part)
            return self.full.at[pl.ds(start, self.part), :]

        def source(self):
            return self.at(me) if self.piece is None else self.piece

        def local(self):
            return pltpu.make_async_copy(self.piece, self.at(me), sems.at[self.keep])

        def near(self):
            return remote(
                self.source(), self.at(me), self.near_s, self.recv + me, {BATCH: partner}
            )

        def far(self, step):
            return remote(
                self.source(),
                self.at(me),
                self.far_s + step,
                self.recv + me,
                {BATCH: far_peer(me, step)},
            )

        def passed(self, step, base):
            source = far_peer(base, step)
            return remote(
                self.at(source),
                self.at(source),
                self.pass_s + step,
                self.recv + source,
                {BATCH: partner},
            )

        def fars(self):
            def go(step):
                if step == 1 and self.piece is not None:
                    self.local().start()
                self.far(step).start()

            return [functools.partial(go, step) for step in range(1, HALF)]

        def nears(self):
            return [lambda: self.near().start()]

        def passes(self):
            def go(step):
                self.passed(step, me).wait_recv()
                self.passed(step, me).start()

            return [functools.partial(go, step) for step in range(1, HALF)]

        def finish(self):
            for step in range(HALF):
                self.passed(step, partner).wait_recv()
            if self.piece is not None:
                self.local().wait()
            self.near().wait_send()
            for step in range(1, HALF):
                self.far(step).wait_send()

        def drain(self):
            for step in range(1, HALF):
                self.passed(step, me).wait_send()

    g_gain = Gather(v.gain_in, None, piece=flat.at[7704:7712, :])
    g_r = Gather(v.w_r, 128)
    g_s = Gather(v.w_s, 128)
    g_a = Gather(v.w_a, 576)
    g_m = Gather(v.w_m, 576)
    g_e = Gather(v.w_e, 64)
    g_b0 = Gather(v.w_b, 256, 0, 128)
    g_b1 = Gather(v.w_b, 256, 128, 128)
    g_c = Gather(v.w_c, 16)
    g_ac = Gather(v.w_ac, 8)

    def block_of(owner, slot):
        return 8 if slot == SLOTS - 1 else lax.rem(slot - owner + 8, 8)

    def merged_rows(owner, slot):
        block = owner * 9 + block_of(owner, slot)
        index = lax.div(block, 8) * MERGED + lax.rem(block, 8)
        return pl.ds(pl.multiple_of(index * 512, 512), 512)

    def has(owner, slot, body):
        if slot == SLOTS - 1:
            pl.when(owner < MERGED)(body)
        else:
            body()

    class GatherUnite:
        def __init__(self):
            self.near_s, self.far_s, self.pass_s = (
                take(SLOTS),
                take(SLOTS * HALF),
                take(SLOTS * HALF),
            )
            self.recv, self.keep = take(SLOTS * OWNERS), take(SLOTS)

        def source(self, slot):
            return v.w_own.at[rows_at(block_of(me, slot), 512), :]

        def full(self, owner, slot):
            return v.w_u.at[merged_rows(owner, slot), :]

        def local(self, slot):
            return pltpu.make_async_copy(
                self.source(slot), self.full(me, slot), sems.at[self.keep + slot]
            )

        def near(self, slot):
            return remote(
                self.source(slot),
                self.full(me, slot),
                self.near_s + slot,
                self.recv + me * SLOTS + slot,
                {BATCH: partner},
            )

        def far(self, step, slot):
            return remote(
                self.source(slot),
                self.full(me, slot),
                self.far_s + step * SLOTS + slot,
                self.recv + me * SLOTS + slot,
                {BATCH: far_peer(me, step)},
            )

        def passed(self, step, slot, base):
            source = far_peer(base, step)
            return remote(
                self.full(source, slot),
                self.full(source, slot),
                self.pass_s + step * SLOTS + slot,
                self.recv + source * SLOTS + slot,
                {BATCH: partner},
            )

        def fars(self, slot):
            def go(step):
                if step == 1:
                    self.local(slot).start()
                self.far(step, slot).start()

            return [
                functools.partial(has, me, slot, functools.partial(go, step))
                for step in range(1, HALF)
            ]

        def nears(self, slot):
            return [lambda: has(me, slot, lambda: self.near(slot).start())]

        def passes(self, slot):
            def go(step):
                self.passed(step, slot, me).wait_recv()
                self.passed(step, slot, me).start()

            return [
                functools.partial(has, far_peer(me, step), slot, functools.partial(go, step))
                for step in range(1, HALF)
            ]

        def finish(self, slots):
            for slot in slots:
                for step in range(HALF):
                    has(
                        far_peer(partner, step),
                        slot,
                        lambda step=step, slot=slot: self.passed(step, slot, partner).wait_recv(),
                    )

                def end(slot=slot):
                    self.local(slot).wait()
                    self.near(slot).wait_send()
                    for step in range(1, HALF):
                        self.far(step, slot).wait_send()

                has(me, slot, end)

        def drain(self):
            for slot in range(SLOTS):
                for step in range(1, HALF):
                    has(
                        far_peer(me, step),
                        slot,
                        lambda step=step, slot=slot: self.passed(step, slot, me).wait_send(),
                    )

    g_u = GatherUnite()

    class Sync:
        def __init__(self, buf):
            self.buf = buf
            self.send, self.recv = take(OWNERS), take(OWNERS)

        def copy(self, k, slot):
            return remote(
                self.buf.at[slot],
                self.buf.at[slot],
                self.send + k,
                self.recv + slot,
                {BATCH: lax.rem(me + k, OWNERS)},
            )

        def start(self, rows):
            for index, row in enumerate(rows):
                self.buf[me, index : index + 1, :] = row
            for index in range(len(rows), self.buf.shape[1]):
                self.buf[me, index : index + 1, :] = jnp.zeros((1, 128), F32)
            for k in range(1, OWNERS):
                self.copy(k, me).start()

        def wait(self):
            for k in range(1, OWNERS):
                self.copy(k, lax.rem(me + k, OWNERS)).wait_recv()
            for k in range(1, OWNERS):
                self.copy(k, me).wait_send()
            value = self.buf[0]
            for slot in range(1, OWNERS):
                value = value + self.buf[slot]
            return value

    class ToGroup:
        def __init__(self, part, into):
            self.part, self.into = part, into
            self.send, self.recv = take(OWNERS), take(OWNERS)

        def each(self, k, owner, slot, act):
            for rows, fits_ in ((16, owner < 6), (BINS, owner >= 6)):

                def go(rows=rows):
                    act(
                        remote(
                            self.part(owner, rows),
                            self.into(slot, rows),
                            self.send + k,
                            self.recv + slot,
                            {BATCH: lax.rem(me + k, OWNERS)},
                        )
                    )

                pl.when(fits_)(go)

        def start(self):
            for k in range(1, OWNERS):
                self.each(k, lax.rem(me + k, OWNERS), me, lambda c: c.start())

        def wait(self):
            for k in range(1, OWNERS):
                self.each(k, me, lax.rem(me + k, OWNERS), lambda c: c.wait_recv())
            for k in range(1, OWNERS):
                self.each(k, lax.rem(me + k, OWNERS), me, lambda c: c.wait_send())

    class Spread:

        def __init__(self, buf, lanes_=None):
            self.buf, self.lanes = buf, lanes_
            self.send, self.recv = take(SPLITS), take(SPLITS)

        def view(self, slot):
            return self.buf.at[slot] if self.lanes is None else self.buf.at[slot, :, self.lanes]

        def copy(self, k, slot):
            return remote(
                self.view(slot),
                self.view(slot),
                self.send + k,
                self.recv + slot,
                {TENSOR: lax.rem(t + k, SPLITS)},
            )

        def start(self):
            for k in range(1, SPLITS):
                self.copy(k, t).start()

        def wait(self):
            for k in range(1, SPLITS):
                self.copy(k, lax.rem(t + k, SPLITS)).wait_recv()
            for k in range(1, SPLITS):
                self.copy(k, t).wait_send()

    class Exchange:

        def __init__(self, axis, count, part, into):
            self.axis, self.count, self.part, self.into = axis, count, part, into
            self.mine = me if axis == BATCH else t
            self.send, self.recv = take(count), take(count)

        def copy(self, k, slot):
            other = lax.rem(self.mine + k, self.count)
            return remote(
                self.part(other),
                self.into(slot),
                self.send + k,
                self.recv + slot,
                {self.axis: other},
            )

        def start(self):
            for k in range(1, self.count):
                self.copy(k, self.mine).start()

        def wait(self):
            for k in range(1, self.count):
                self.copy(k, lax.rem(self.mine + k, self.count)).wait_recv()
            for k in range(1, self.count):
                self.copy(k, self.mine).wait_send()

    feat_keep = take(1)
    feat_local = pltpu.make_async_copy(feat, v.whole.at[t], sems.at[feat_keep])
    feat_s, feat_r = take(3), take(SPLITS)

    def feat_copy(k, slot, device):
        source = feat if k < 2 else v.whole.at[slot]
        return remote(source, v.whole.at[slot], feat_s + k, feat_r + slot, {TENSOR: device})

    def wide_rows(into, rows, low):
        for k in range(4):
            value = o_flat[pl.ds(low + k, rows, stride=4), :]
            into[rows_at(me, rows), k * 128 : k * 128 + 128] = value.astype(BF)

    load(0).wait()
    v.w_r[rows_at(me, 128), :] = o_flat[0:128, :].astype(BF)
    mix(g_r.nears() + g_gain.nears(), g_r.fars() + g_gain.fars())
    feat_local.start()
    feat_copy(0, t, t_x).start()
    feat_copy(1, t, t_core).start()
    load(2).wait()
    v.w_m[rows_at(me, 576), :] = o_flat[640:1216, :].astype(BF)
    load(3).wait()
    wide_rows(v.w_e, 64, 1216)
    mix(g_m.nears() + g_e.nears(), g_m.fars() + g_e.fars())
    lane = lax.broadcasted_iota(jnp.int32, (1, 128), 1)

    def roll(value, shift):
        return pltpu.roll(value, shift % 128, 1) if shift % 128 else value

    high, across = sizes[0, 0], sizes[0, 1]
    place = lax.broadcasted_iota(jnp.int32, (CELLS, 128), 0).astype(F32)
    row_of = jnp.floor((place + 0.5) / MAP)
    col_of = place - MAP * row_of
    within = (row_of < high.astype(F32)) & (col_of < across.astype(F32))
    v.ins[...] = jnp.where(within, 1.0, 0.0)
    v.col[...] = col_of
    v.lab[...] = jnp.where(within, lab_in[...], -1.0)
    v.table[...] = jnp.zeros((BINS, CELLS), F32)
    lane_place = lax.broadcasted_iota(jnp.int32, (1, CELLS), 1).astype(F32)
    lane_row = jnp.floor((lane_place + 0.5) / MAP)
    lane_col = lane_place - MAP * lane_row

    def ranges(extent, bins, where):
        inside, chosen, counts = [], [], []
        for k in range(bins):
            low = lax.div(k * extent, bins)
            top = lax.div((k + 1) * extent + (bins - 1), bins)
            member = (where >= low.astype(F32)) & (where < top.astype(F32))
            inside.append(jnp.where(member, 1.0, 0.0))
            picked = where * bins >= (k * extent).astype(F32)
            if k < bins - 1:
                picked = picked & (where * bins < ((k + 1) * extent).astype(F32))
            chosen.append(jnp.where(picked, 1.0, 0.0))
            counts.append(top - low)
        return inside, chosen, counts

    picks = []
    v.cells_in[...] = jnp.ones((BINS, 128), F32)
    for group, bins in enumerate(BIN_COUNTS):
        r_in, r_pick, r_count = ranges(high, bins, lane_row)
        c_in, c_pick, c_count = ranges(across, bins, lane_col)
        for a in range(bins):
            for b in range(bins):
                spot = BIN_STARTS[group] + a * bins + b
                v.table[spot : spot + 1, :] = r_in[a] * c_in[b]
                v.cells_in[spot : spot + 1, :] = jnp.full(
                    (1, 128), (r_count[a] * c_count[b]).astype(F32)
                )
                picks.append((spot, r_pick[a] * c_pick[b]))
    v.pool[...] = v.table[...].astype(BF)
    for spot, value in picks:
        v.table[spot : spot + 1, :] = value
    v.pick[...] = v.table[...].astype(BF)
    v.pick_t[...] = jnp.concatenate([v.pick[...], v.pick[...]], axis=0).T
    zeros_edge = jnp.zeros((EDGE, 128), F32)
    for tap in range(9):
        v.pad[tap, 0:EDGE, :] = zeros_edge
        v.pad[tap, EDGE + CELLS :, :] = zeros_edge
    v.grad_pad[0:EDGE, :] = zeros_edge
    v.grad_pad[EDGE + CELLS :, :] = zeros_edge
    lanes = lax.broadcasted_iota(jnp.int32, (1, 256), 1).astype(F32)
    counts = jnp.zeros((8, 256), F32)
    for k in range(0, CELLS, 96):
        counts = counts + fold(
            jnp.where(wide(v.lab[k : k + 96, :], 2) == lanes, 1.0, 0.0)
        )
    class_local = total(counts)
    cells_local = jnp.full((1, 128), (high * across).astype(F32))
    left_half = lax.broadcasted_iota(jnp.int32, (64, 128), 1) < 64

    mix(g_r.passes() + g_gain.passes())
    feat_copy(0, t_x, t_x).wait_recv()
    feat_copy(2, t_x, t_core).start()
    load(1).wait()
    wide_rows(v.w_s, 128, 128)
    load(4).wait()
    wide_rows(v.w_b, 256, 1472)
    load(6).wait()
    before = pltpu.roll(o_flat[7122:7698, :], 32, 1)
    after = pltpu.roll(o_flat[7123:7699, :], 32, 1)
    v.w_a[rows_at(me, 576), :] = jnp.where(lane < 32, before, after).astype(BF)

    def class_rows(count, base, into):
        for row in range(count):
            first, shift = divmod(base + NCLS * row, 128)
            three = [
                roll(o_flat[7104 + first + k : 7105 + first + k, :], 128 - shift) for k in range(3)
            ]
            into[row : row + 1, :128] = jnp.where(lane < 128 - shift, three[0], three[1])
            high_half = jnp.where(lane < 128 - shift, three[1], three[2])
            into[row : row + 1, 128:] = jnp.where(lane < NCLS - 128, high_half, 0.0)

    class_rows(16, 0, v.out_c)
    class_rows(8, 76128, v.out_ac)
    v.w_c[rows_at(me, 16), :] = v.out_c[...].astype(BF)
    v.w_ac[rows_at(me, 8), :] = v.out_ac[...].astype(BF).astype(F32)
    load(5).wait()

    def own_rows(j):
        at = pl.ds(pl.multiple_of(2496 + 512 * j, 64), 512)
        v.w_own[rows_at(j, 512), :] = o_flat[at, :].astype(BF)

    loop(9, own_rows)
    for item in (g_gain, g_r):
        item.finish()
    feat_local.wait()
    feat_copy(1, t_core, t_core).wait_recv()
    feat_copy(2, t_diag, t_core).wait_recv()
    feat_copy(0, t, t_x).wait_send()
    feat_copy(1, t, t_core).wait_send()
    feat_copy(2, t_x, t_core).wait_send()
    gain_of = [None] * 33
    for owner in range(OWNERS):
        start = 496 * (owner % 4) - 16
        first, shift = start // 128, start % 128
        for k in range(4):
            value = v.gain_in[owner, 4 + k : 5 + k, :].astype(BF).astype(F32)
            if k == 0:
                value = jnp.where(lane < 16, 0.0, value)
            value = roll(value, shift)
            spot = 16 * (owner // 4) + first + k
            for where, part in (
                (spot, jnp.where(lane >= shift, value, 0.0)),
                (spot + 1, jnp.where(lane < shift, value, 0.0)),
            ):
                gain_of[where] = part if gain_of[where] is None else gain_of[where] + part

    def gamma(row, width=1):
        return jnp.concatenate([gain_of[row + k] for k in range(width)], axis=1)

    def beta(row, width=1):
        return gamma(16 + row, width)

    def whole_feat():
        return jnp.concatenate([v.whole[k] for k in range(SPLITS)], axis=1)

    v.pre_r[...] = dot(whole_feat(), v.w_r[...])
    def offset(tap, spacing):
        return ((tap // 3 - 1) * MAP + (tap % 3 - 1)) * spacing

    def col_mask(at, right):
        where = v.col[at, :] + float(right)
        return jnp.where((where >= 0.0) & (where < float(MAP)), 1.0, 0.0)

    BLOCK = 72

    def shift_sum(taps, spacing, at, slot_of):
        out = None
        for b in (-1, 0, 1):
            part = None
            for tap in taps:
                if tap % 3 - 1 != b:
                    continue
                start = EDGE + at + offset(tap, spacing)
                value = v.pad[slot_of(tap), start : start + BLOCK, :]
                part = value if part is None else part + value
            if part is None:
                continue
            if b:
                part = part * col_mask(slice(at, at + BLOCK), b * spacing)
            out = part if out is None else out + part
        return out

    def masked_sums(ref):
        width = ref.shape[1]

        def step(k, carry):
            at = rows_at(k, 96)
            value = ref[at, :]
            kept = value * (v.ins[at, :] if width == 128 else wide(v.ins[at, :], width // 128))
            return (carry[0] + fold(kept), carry[1] + fold(kept * value))

        zero = jnp.zeros((8, width), F32)
        sums = lax.fori_loop(0, 6, step, (zero, zero))
        return total(sums[0]), total(sums[1])

    def split_rows(value):
        return [value[:, k : k + 128] for k in range(0, value.shape[1], 128)]

    def join_rows(value, row, count):
        return jnp.concatenate([value[row + k : row + k + 1] for k in range(count)], axis=1)

    def moments(first, second, count):
        mean = first / count
        return mean, lax.rsqrt(second / count - mean * mean + 1e-05)

    sync = Sync(v.sync_one)
    r1, r2 = masked_sums(v.pre_r)
    sync.start([r1, r2, cells_local] + split_rows(class_local))
    mix(g_m.passes() + g_e.passes(), g_s.fars())
    sums = sync.wait()
    count = sums[2:3]
    count4 = wide(count, 4)
    norm_r = moments(sums[0:1], sums[1:2], count)
    class_count = join_rows(sums, 3, 2)

    def normed(ref, at, norm):
        return (ref[at, :] - norm[0]) * norm[1]

    spread_1 = Spread(v.h1)

    def make_h1(k):
        at = rows_at(k, 96)
        v.h1[t, at, :] = jax.nn.silu(gamma(0) * normed(v.pre_r, at, norm_r) + beta(0)).astype(BF)

    loop(6, make_h1)
    spread_1.start()
    mix(g_s.nears(), g_b0.fars() + g_u.fars(0))
    g_m.finish()
    spread_1.wait()

    def full_h(ref):
        return jnp.concatenate([ref[k] for k in range(SPLITS)], axis=1)

    def w_middle(tap):
        return v.w_m[rows_at(tap, 512), :]

    def middle_pair(p):
        both = jnp.concatenate([w_middle(2 * p), w_middle(2 * p + 1)], axis=1)
        value = dot(full_h(v.h1), both)
        v.pad[2 * p, EDGE : EDGE + CELLS, :] = value[:, :128]
        v.pad[2 * p + 1, EDGE : EDGE + CELLS, :] = value[:, 128:]

    loop(4, middle_pair)
    v.pad[8, EDGE : EDGE + CELLS, :] = dot(full_h(v.h1), w_middle(8))
    for at in range(0, CELLS, BLOCK):
        v.pre_m[at : at + BLOCK, :] = shift_sum(range(9), 4, at, lambda tap: tap)
    sync = Sync(v.sync_two)
    sync.start(list(masked_sums(v.pre_m)))
    mix(g_s.passes() + g_b0.nears(), g_b1.fars())
    sums = sync.wait()
    norm_m = moments(sums[0:1], sums[1:2], count)
    spread_2 = Spread(v.h2)

    def make_h2(k):
        at = rows_at(k, 96)
        v.h2[t, at, :] = jax.nn.silu(gamma(5) * normed(v.pre_m, at, norm_m) + beta(5)).astype(BF)

    loop(6, make_h2)
    spread_2.start()
    mix(g_b0.passes() + g_b1.nears(), g_u.fars(1))
    g_e.finish()
    g_s.finish()
    for k in range(0, 512, 256):
        v.pre_s[:, k : k + 256] = dot(whole_feat(), v.w_s[:, k : k + 256])
    s1, s2 = masked_sums(v.pre_s)
    spread_2.wait()
    for k in range(0, 512, 256):
        v.pre_e[:, k : k + 256] = dot(full_h(v.h2), v.w_e[:, k : k + 256])
    sync = Sync(v.sync_three)
    e1, e2 = masked_sums(v.pre_e)
    sync.start(split_rows(e1) + split_rows(e2) + split_rows(s1) + split_rows(s2))
    mix(g_b1.passes() + g_u.nears(0), g_u.fars(2))
    mix(g_c.nears() + g_ac.nears(), g_c.fars() + g_ac.fars())
    sums = sync.wait()
    norm_e = moments(join_rows(sums, 0, 4), join_rows(sums, 4, 4), count4)
    norm_s = moments(join_rows(sums, 8, 4), join_rows(sums, 12, 4), count4)

    def summed(at):
        return (
            gamma(6, 4) * normed(v.pre_e, at, norm_e)
            + beta(6, 4)
            + gamma(1, 4) * normed(v.pre_s, at, norm_s)
            + beta(1, 4)
        )

    def make_merged(k):
        at = rows_at(k, 48)
        v.joined[t, at, :] = jax.nn.silu(summed(at)).astype(BF)

    loop(12, make_merged)

    j_send, j_recv = take(3), take(SPLITS)

    def joined_copy(k, slot, device):
        return remote(
            v.joined.at[slot], v.joined.at[slot], j_send + k, j_recv + slot, {TENSOR: device}
        )

    joined_copy(0, t, t_x).start()
    joined_copy(1, t, t_core).start()

    pool_move = ToGroup(
        lambda owner, rows: v.pool_half.at[lax.rem(owner, 2), 0:rows, :],
        lambda slot, rows: v.pool_all.at[slot, 0:rows, :],
    )
    bin_row = lax.broadcasted_iota(jnp.int32, (BINS, 1), 0)

    def group_mask(group, shape=None):
        low, top = GROUP_ROWS[group]
        kept = jnp.where((bin_row >= low) & (bin_row < top), 1.0, 0.0)
        return kept if shape is None else jnp.broadcast_to(kept, shape)

    cells_in = wide(v.cells_in[...], 4)
    pooled = dot(v.pool[...], v.joined[t]) / cells_in
    v.pooled[...] = pooled.astype(BF)
    for k in range(2):
        v.pool_half[k] = v.pooled[:, k * 256 : k * 256 + 256]
    v.pool_all[me] = v.pool_half[lax.rem(me, 2)]
    g_b0.finish()
    g_b1.finish()
    part = jnp.zeros((BINS, 512), F32)
    for group in range(4):
        rows = (v.pooled[...].astype(F32) * group_mask(group)).astype(BF)
        part = part + dot(rows, v.w_b[group * 512 : group * 512 + 512, :])
    for k in range(SPLITS):
        v.part_b[k] = part[:, k * 128 : k * 128 + 128].astype(BF)
    v.recv_b[t] = v.part_b[t]
    ex = Exchange(TENSOR, SPLITS, lambda o: v.part_b.at[o], lambda s: v.recv_b.at[s])
    ex.start()
    mix(g_u.passes(0) + g_u.nears(1), g_u.fars(4))
    joined_copy(0, t_x, t_x).wait_recv()
    joined_copy(2, t_x, t_core).start()
    ex.wait()
    own_b = v.recv_b[0].astype(F32)
    for k in range(1, SPLITS):
        own_b = own_b + v.recv_b[k].astype(F32)
    v.all_b[me] = own_b.astype(BF)
    ex = Exchange(BATCH, OWNERS, lambda o: v.all_b.at[me], lambda s: v.all_b.at[s])
    ex.start()
    mix(g_u.passes(1) + g_u.nears(2), g_u.fars(3))
    ex.wait()
    all_b = [v.all_b[k].astype(F32) for k in range(OWNERS)]
    sum_b, square_b = all_b[0], all_b[0] * all_b[0]
    for k in range(1, OWNERS):
        sum_b = sum_b + all_b[k]
        square_b = square_b + all_b[k] * all_b[k]
    mean_b = jnp.zeros((BINS, 128), F32)
    scale_b = jnp.zeros((BINS, 128), F32)
    gamma_b = jnp.zeros((BINS, 128), F32)
    beta_b = jnp.zeros((BINS, 128), F32)
    count_b = jnp.zeros((BINS, 1), F32)
    for group, bins in enumerate(BIN_COUNTS):
        kept = group_mask(group)
        size = float(OWNERS * bins * bins)
        mean, scaling = moments(total(sum_b * kept), total(square_b * kept), size)
        mean_b = mean_b + kept * mean
        scale_b = scale_b + kept * scaling
        gamma_b = gamma_b + kept * gamma(10 + group)
        beta_b = beta_b + kept * beta(10 + group)
        count_b = count_b + kept / size
    spread_b = Spread(v.act_b)
    for k in range(OWNERS):
        out = gamma_b * ((all_b[k] - mean_b) * scale_b) + beta_b
        v.act_b[t, k * BINS : k * BINS + BINS, :] = jax.nn.silu(out).astype(BF)
    spread_b.start()
    mix(g_u.passes(2) + g_u.nears(4) + g_u.nears(3))
    spread_b.wait()
    row_512 = lax.broadcasted_iota(jnp.int32, (OWNERS * BINS, 1), 0) & (BINS - 1)
    group_id = jnp.where(
        row_512 < 1, 0, jnp.where(row_512 < 5, 1, jnp.where(row_512 < 14, 2, jnp.where(row_512 < 50, 3, 9)))
    )

    def full_act():
        return jnp.concatenate([v.act_b[k] for k in range(SPLITS)], axis=1)

    v.zsum[...] = jnp.zeros((2, OWNERS * BINS, 128), F32)

    def own_branch(j, body):
        chunk = lax.rem(me + j, 8)
        pl.when(chunk >= MERGED)(lambda: body(chunk - MERGED, lax.div(me + j, 8)))

    def make_z(j):
        def body(group, side):
            kept = jnp.where(group_id == group, 1.0, 0.0)
            v.zsum[side] = v.zsum[side] + kept * dot(full_act(), v.w_own[rows_at(j, 512), :])

        own_branch(j, body)

    loop(9, make_z)
    for k in range(OWNERS):
        for side in range(2):
            v.z_send[k, side] = v.zsum[side, k * BINS : k * BINS + BINS, :].astype(BF)
    v.z_recv[me] = v.z_send[me]
    ex = Exchange(BATCH, OWNERS, lambda o: v.z_send.at[o], lambda s: v.z_recv.at[s])
    ex.start()
    mix(g_u.passes(4) + g_u.passes(3))
    v.act_t[...] = full_act().T
    joined_copy(1, t_core, t_core).wait_recv()
    joined_copy(2, t_diag, t_core).wait_recv()
    for k in range(SPLITS):
        v.joined_t[k] = v.joined[k].T
    mix(g_c.passes() + g_ac.passes())
    ex.wait()
    g_u.finish((0, 1, 2, 4))

    def tap_z(tap):
        if tap == 0:
            return v.z_recv[0, 0].astype(F32)
        if tap == 8:
            return v.z_recv[7, 1].astype(F32)
        return v.z_recv[tap, 0].astype(F32) + v.z_recv[tap - 1, 1].astype(F32)

    for tap in range(9):
        z = tap_z(tap)
        high_z = z.astype(BF)
        v.z_cat[tap, :BINS, :] = high_z
        v.z_cat[tap, BINS:, :] = (z - high_z.astype(F32)).astype(BF)

    def most_joined():
        return jnp.concatenate([v.joined[k] for k in range(3)], axis=1)

    def rest_joined():
        return jnp.concatenate([v.joined[3], v.pick_t[...]], axis=1)

    def most_weight(tap):
        return v.w_u[pl.ds(pl.multiple_of(tap * 2048, 512), 1536), :]

    def rest_weight(tap):
        last = v.w_u[pl.ds(pl.multiple_of(tap * 2048 + 1536, 512), 512), :]
        return jnp.concatenate([last, v.z_cat[tap]], axis=0)

    inner = slice(EDGE, EDGE + CELLS)

    def most_pair(p):
        both = jnp.concatenate([most_weight(2 * p), most_weight(2 * p + 1)], axis=1)
        value = dot(most_joined(), both)
        v.pad[2 * p, inner, :] = value[:, :128]
        v.pad[2 * p + 1, inner, :] = value[:, 128:]

    def rest_pair(p):
        both = jnp.concatenate([rest_weight(2 * p), rest_weight(2 * p + 1)], axis=1)
        value = dot(rest_joined(), both)
        v.pad[2 * p, inner, :] = v.pad[2 * p, inner, :] + value[:, :128]
        v.pad[2 * p + 1, inner, :] = v.pad[2 * p + 1, inner, :] + value[:, 128:]

    loop(4, most_pair)
    v.pad[8, inner, :] = dot(most_joined(), most_weight(8))
    g_u.finish((3,))
    loop(4, rest_pair)
    v.pad[8, inner, :] = v.pad[8, inner, :] + dot(rest_joined(), rest_weight(8))
    for at in range(0, CELLS, BLOCK):
        v.pre_u[at : at + BLOCK, :] = shift_sum(range(9), 1, at, lambda tap: tap)
    sync = Sync(v.sync_five)
    sync.start(list(masked_sums(v.pre_u)))
    pool_move.start()
    mix(g_a.nears(), g_a.fars())
    for item in (g_c, g_ac):
        item.finish()
    v.w_c_all[t] = v.w_c[...]
    spread_c = Spread(v.w_c_all)
    spread_c.start()
    for k in range(SPLITS):
        v.whole_t[k] = v.whole[k].T
    for item in (g_gain, g_r, g_s, g_m, g_e, g_b0, g_b1, g_c, g_ac, g_u):
        item.drain()
    joined_copy(0, t, t_x).wait_send()
    joined_copy(1, t, t_core).wait_send()
    joined_copy(2, t_x, t_core).wait_send()
    w_ac = jnp.concatenate([v.w_ac[...], jnp.zeros((64, 256), F32)], axis=0).astype(BF)
    sums = sync.wait()
    norm_u = moments(sums[0:1], sums[1:2], count)

    def make_u(k):
        at = rows_at(k, 96)
        v.united[t, at, :] = jax.nn.silu(gamma(14) * normed(v.pre_u, at, norm_u) + beta(14)).astype(BF)

    loop(6, make_u)
    spread_u = Spread(v.united)
    spread_u.start()
    class Band:
        def __init__(self, at):
            self.at = at
            self.ex = Exchange(
                TENSOR,
                SPLITS,
                lambda o: v.logit_send.at[rows_at(o, 144), at],
                lambda s: v.logit_recv.at[s, :, at],
            )
            self.back = Spread(v.slope_in, at)

        def start(self, value):
            v.logit_send[:, self.at] = value.astype(BF)
            self.ex.start()
            v.logit_recv[t, :, self.at] = v.logit_send[rows_at(t, 144), self.at]

        def finish(self, factor):
            self.ex.wait()
            logits = v.logit_recv[0, :, self.at].astype(F32)
            for k in range(1, SPLITS):
                logits = logits + v.logit_recv[k, :, self.at].astype(F32)
            loss_rows, grad = soft_loss(logits, rows_at(t, 144), factor)
            v.slope_in[t, :, self.at] = grad
            self.back.start()
            loss_rows = total(loss_rows)
            return loss_rows[:, :128] + loss_rows[:, 128:]

        def grad(self):
            self.back.wait()
            return v.slope_in[:, :, self.at].reshape(CELLS, 256)

    def class_weights():
        total_valid = jnp.sum(class_count, axis=1, keepdims=True)
        weight = total_valid / (NCLS * class_count + total_valid)
        whole = jnp.sum(class_count * weight, axis=1, keepdims=True)
        return jnp.where(lanes < float(NCLS), weight, 0.0), whole

    def soft_loss(logits, at, factor):
        class_weight, loss_weight = class_weights()
        hot = jnp.where(wide(v.lab[at, :], 2) == lanes, 1.0, 0.0)
        cell_weight = factor * jnp.sum(hot * class_weight, axis=1, keepdims=True)
        value = jnp.where(lanes < float(NCLS), logits, -1e30)
        value = value - jnp.max(value, axis=1, keepdims=True)
        powers = jnp.exp(value)
        mass = jnp.sum(powers, axis=1, keepdims=True)
        grad = cell_weight * (powers / mass - hot) / loss_weight
        return fold(-cell_weight * hot * (value - jnp.log(mass))), grad.astype(BF)

    aux_head = Band(slice(256, 512))
    mix(g_a.passes())
    spread_c.wait()

    g_a.finish()
    g_a.drain()

    def unpack(chunk):
        for pair in range(5):
            even = v.w_a[rows_at(2 * pair * 8 + chunk, 64), :].astype(F32)
            if pair < 4:
                odd = v.w_a[rows_at((2 * pair + 1) * 8 + chunk, 64), :].astype(F32)
            else:
                odd = jnp.zeros((64, 128), F32)
            low = jnp.where(left_half, even, pltpu.roll(odd, 64, 1))
            top = jnp.where(left_half, pltpu.roll(even, 64, 1), odd)
            v.pad[pair, pl.ds(EDGE, 64, stride=2), :] = low
            v.pad[pair, pl.ds(EDGE + 1, 64, stride=2), :] = top
            both = v.pad[pair, EDGE : EDGE + 128, :]
            v.w_pair[rows_at(chunk, 128), pair * 128 : pair * 128 + 128] = both.astype(BF)

    loop(8, unpack)

    for pair in (0, 2):
        value = dot(whole_feat(), v.w_pair[:, pair * 128 : pair * 128 + 256])
        v.pad[pair, EDGE : EDGE + CELLS, :] = value[:, :128]
        v.pad[pair + 1, EDGE : EDGE + CELLS, :] = value[:, 128:]
    v.pad[4, EDGE : EDGE + CELLS, :] = dot(whole_feat(), v.w_pair[:, 512:640])

    left_wide = lax.broadcasted_iota(jnp.int32, (BLOCK, 128), 1) < 64
    for at in range(0, CELLS, BLOCK):
        even = shift_sum((0, 2, 4, 6, 8), 1, at, lambda tap: tap // 2)
        odd = shift_sum((1, 3, 5, 7), 1, at, lambda tap: tap // 2)
        v.pre_a[at : at + BLOCK, :] = jnp.where(left_wide, even + pltpu.roll(odd, 64, 1), 0.0)

    sync_a = Sync(v.sync_aux)
    sync_a.start(list(masked_sums(v.pre_a)))
    spread_u.wait()
    weight_c = v.w_c_all[...].reshape(512, 256)

    def main_loss(k, carry):
        at = rows_at(k, 144)
        rows = jnp.concatenate([v.united[slot, at, :] for slot in range(SPLITS)], axis=1)
        loss_rows, grad = soft_loss(dot(rows, weight_c), at, 1.0)
        v.slope_main[at, :] = grad
        return carry + loss_rows

    loss_rows = total(lax.fori_loop(0, 4, main_loss, jnp.zeros((8, 256), F32)))
    o_misc[1:2, :] = (loss_rows[:, :128] + loss_rows[:, 128:]) / SPLITS
    g_main = v.slope_main[...]
    v.d_f[...] = dot_nt(g_main, v.w_c[...])

    def slope(value):
        gate = jax.nn.sigmoid(value)
        return gate * (1.0 + value * (1.0 - gate))

    def through_silu(ref, pre, norm, row):
        def step(k, carry):
            at = rows_at(k, 96)
            unit = normed(pre, at, norm)
            value = ref[at, :] * slope(gamma(row) * unit + beta(row))
            ref[at, :] = value
            return (carry[0] + fold(value), carry[1] + fold(value * unit))

        zero = jnp.zeros((8, 128), F32)
        sums = lax.fori_loop(0, 6, step, (zero, zero))
        return [total(sums[0]), total(sums[1])]

    def back_norm(value, unit, mask, norm, gain, first, second, size):
        inner = value - mask * (first + unit * second) / size
        return gain * norm[1] * inner

    gain_grads = {}
    sync = Sync(v.sync_b1)
    sync.start(through_silu(v.d_f, v.pre_u, norm_u, 14))
    sums = sync_a.wait()
    norm_a = moments(sums[0:1], sums[1:2], count)

    def make_a(k):
        at = rows_at(k, 96)
        v.act_a[at, :] = jax.nn.silu(gamma(15) * normed(v.pre_a, at, norm_a) + beta(15)).astype(BF)

    loop(6, make_a)
    aux_head.start(dot(v.act_a[...], w_ac))

    class Scatter:
        def __init__(self, first, second, full, rows, out, base=0):
            self.full, self.rows, self.out, self.base = full, rows, out, base
            self.first, self.second = first, second
            self.near_s, self.near_r = take(HALF), take(HALF)
            self.far_s, self.far_r = take(HALF), take(HALF)
            self.block = min(rows, 64)

        def near(self, step):
            dest = far_peer(partner, step)
            return remote(
                self.full.at[rows_at(dest, self.rows), :],
                self.first.at[step],
                self.near_s + step,
                self.near_r + step,
                {BATCH: partner},
            )

        def far(self, step):
            return remote(
                self.first.at[step],
                self.second.at[step - 1],
                self.far_s + step,
                self.far_r + step,
                {BATCH: far_peer(me, step)},
            )

        def starts(self):
            return [lambda step=step: self.near(step).start() for step in (1, 2, 3, 0)]

        def middles(self):
            def go(step):
                self.near(step).wait_recv()
                base = far_peer(me, step) * (self.rows // self.block)

                def add(k):
                    at = rows_at(k, self.block)
                    value = self.full[rows_at(base + k, self.block), :].astype(F32)
                    value = value + self.first[step, at, :].astype(F32)
                    self.first[step, at, :] = value.astype(self.first.dtype)

                loop(self.rows // self.block, add)
                self.far(step).start()

            return [functools.partial(go, step) for step in range(1, HALF)]

        def end(self):
            self.near(0).wait_recv()
            for step in range(1, HALF):
                self.far(step).wait_recv()
            base = me * (self.rows // self.block)

            def add(k, carry):
                at = rows_at(k, self.block)
                value = self.full[rows_at(base + k, self.block), :].astype(F32)
                value = value + self.first[0, at, :].astype(F32)
                for step in range(1, HALF):
                    value = value + self.second[step - 1, at, :].astype(F32)
                if self.out is o_flat:
                    times = value.shape[1] // 128
                    start = self.base + k * self.block * times
                    for q in range(times):
                        where = pl.ds(start + q, self.block, stride=times if times > 1 else None)
                        self.out[where, :] = value[:, q * 128 : q * 128 + 128]
                else:
                    self.out[at, :] = value
                return carry + fold(value * value)

            squares = lax.fori_loop(
                0, self.rows // self.block, add, jnp.zeros((8, self.full.shape[1]), F32)
            )
            for step in (1, 2, 3, 0):
                self.near(step).wait_send()
                if step:
                    self.far(step).wait_send()
            return sum(split_rows(total(squares)))

    s_c = Scatter(v.first_c, v.second_c, v.w_c, 16, v.out_c)
    s_ac = Scatter(v.first_ac, v.second_ac, v.w_ac, 8, v.out_ac)
    s_a = Scatter(v.first_a, v.second_a, v.w_a, 576, v.out_a)
    s_s = Scatter(v.first_s, v.second_s, v.w_s, 128, o_flat, 128)
    s_e = Scatter(v.first_e, v.second_e, v.w_e, 64, o_flat, 1216)
    s_m = Scatter(v.first_m, v.second_m, v.w_m, 576, o_flat, 640)
    s_r = Scatter(v.first_r, v.second_r, v.w_r, 128, o_flat, 0)

    class ScatterUnite:
        def __init__(self):
            self.near_s, self.near_r = take(SLOTS * HALF), take(SLOTS * HALF)
            self.far_s, self.far_r = take(SLOTS * HALF), take(SLOTS * HALF)

        def near(self, step, slot, base):
            dest = far_peer(base, step)
            return remote(
                v.w_u.at[merged_rows(dest, slot), :],
                v.first_u.at[step, slot],
                self.near_s + step * SLOTS + slot,
                self.near_r + step * SLOTS + slot,
                {BATCH: partner},
            )

        def far(self, step, slot):
            return remote(
                v.first_u.at[step, slot],
                v.second_u.at[step - 1, slot],
                self.far_s + step * SLOTS + slot,
                self.far_r + step * SLOTS + slot,
                {BATCH: far_peer(me, step)},
            )

        def own_rows(self, owner, slot, k):
            block = owner * 9 + block_of(owner, slot)
            index = lax.div(block, 8) * MERGED + lax.rem(block, 8)
            return rows_at(index * 8 + k, 64)

        def starts(self, slot):
            def go(step):
                self.near(step, slot, partner).start()

            return [
                functools.partial(has, far_peer(partner, step), slot, functools.partial(go, step))
                for step in (1, 2, 3, 0)
            ]

        def middles(self, slot):
            def go(step):
                self.near(step, slot, me).wait_recv()
                owner = far_peer(me, step)

                def add(k):
                    at = rows_at(k, 64)
                    value = v.w_u[self.own_rows(owner, slot, k), :].astype(F32)
                    value = value + v.first_u[step, slot, at, :].astype(F32)
                    v.first_u[step, slot, at, :] = value.astype(BF)

                loop(8, add)
                self.far(step, slot).start()

            return [
                functools.partial(has, far_peer(me, step), slot, functools.partial(go, step))
                for step in range(1, HALF)
            ]

        def end(self):
            for slot in range(SLOTS):

                def go(slot=slot):
                    self.near(0, slot, me).wait_recv()
                    for step in range(1, HALF):
                        self.far(step, slot).wait_recv()
                    j = block_of(me, slot)

                    def add(k):
                        at = rows_at(k, 64)
                        value = v.w_u[self.own_rows(me, slot, k), :].astype(F32)
                        value = value + v.first_u[0, slot, at, :].astype(F32)
                        for step in range(1, HALF):
                            value = value + v.second_u[step - 1, slot, at, :].astype(F32)
                        o_u[rows_at(j * 8 + k, 64), :] = value

                    loop(8, add)

                has(me, slot, go)
                for step in (1, 2, 3, 0):
                    has(
                        far_peer(partner, step),
                        slot,
                        lambda step=step, slot=slot: self.near(step, slot, partner).wait_send(),
                    )
                    if step:
                        has(
                            far_peer(me, step),
                            slot,
                            lambda step=step, slot=slot: self.far(step, slot).wait_send(),
                        )

            def square(k, carry):
                value = o_u[rows_at(k, 64), :]
                return carry + fold(value * value)

            squares = lax.fori_loop(0, 72, square, jnp.zeros((8, 128), F32))
            return sum(split_rows(total(squares)))

    s_u = ScatterUnite()

    v.w_c[...] = dot_tn(v.united[t], g_main).astype(BF)
    mix(s_c.starts())
    sums = sync.wait()
    gain_grads[14] = (sums[1:2], sums[0:1])

    def spread_taps(ref, pre, norm, row, first, second):
        def step(k):
            at = rows_at(k, 96)
            value = back_norm(
                ref[at, :], normed(pre, at, norm), v.ins[at, :], norm, gamma(row), first, second, count
            )
            ref[at, :] = value.astype(BF).astype(F32)

        loop(6, step)
        v.grad_pad[EDGE : EDGE + CELLS, :] = ref[...]

    def back_tap(tap, spacing, at):
        start = EDGE + at - offset(tap, spacing)
        value = v.grad_pad[start : start + 96, :]
        right = tap % 3 - 1
        if right:
            value = value * col_mask(slice(at, at + 96), -right * spacing)
        return value

    def fill(cat, spacing):
        for tap in range(9):
            for at in range(0, CELLS, 96):
                cat[at : at + 96, tap * 128 : tap * 128 + 128] = back_tap(tap, spacing, at).astype(
                    BF
                )

    spread_taps(v.d_f, v.pre_u, norm_u, 14, sums[0:1], sums[1:2])
    fill(v.cat_u, 1)

    dz = dot(v.pick[...], v.cat_u[...])
    for tap in range(9):
        v.dz_send[tap] = dz[:, tap * 128 : tap * 128 + 128].astype(BF)
    v.dz_recv[me] = v.dz_send[pl.ds(me, 2)]
    ex_dz = Exchange(
        BATCH, OWNERS, lambda o: v.dz_send.at[pl.ds(o, 2)], lambda s: v.dz_recv.at[s]
    )
    ex_dz.start()

    def merged_back(c):
        weight = jnp.concatenate(
            [v.w_u[rows_at(tap * MERGED + c, 512), :] for tap in range(9)], axis=1
        )
        v.joined[c] = dot_nt(v.cat_u[...], weight).astype(BF)

    near_s, near_r, far_s, far_r = take(2), take(2), take(1), take(1)

    def dm_near(k, slot):
        return remote(
            v.joined.at[slot], v.dm_near.at[k], near_s + k, near_r + k, {TENSOR: t_core}
        )

    merged_back(t_diag)
    dm_near(1, t_diag).start()
    merged_back(t_core)
    dm_near(0, t_core).start()
    merged_back(t_x)
    merged_back(t)

    def unite_grad(c):
        for p in range(5):
            width = 256 if p < 4 else 128
            value = dot(v.joined_t[c], v.cat_u[:, p * 256 : p * 256 + width])
            v.w_u[rows_at(2 * p * MERGED + c, 512), :] = value[:, :128].astype(BF)
            if p < 4:
                v.w_u[rows_at((2 * p + 1) * MERGED + c, 512), :] = value[:, 128:].astype(BF)

    unite_grad(0)
    mix(s_u.starts(0))
    o_misc[1:2, :] = o_misc[1:2, :] + aux_head.finish(0.4)
    ex_dz.wait()

    d_act = v.d_sum.at[0 : OWNERS * BINS, :]
    d_act[...] = jnp.zeros((OWNERS * BINS, 512), F32)

    def branch_back(j):
        def body(group, side):
            kept = jnp.where(group_id == group, 1.0, 0.0)
            value = v.dz_recv[:, side].reshape(OWNERS * BINS, 128).astype(F32) * kept
            value = value.astype(BF)
            o_u[rows_at(j, 512), :] = dot(v.act_t[...], value)
            d_act[...] = d_act[...] + dot_nt(value, v.w_own[rows_at(j, 512), :])

        own_branch(j, body)

    loop(9, branch_back)
    for k in range(SPLITS):
        v.d_act_send[k] = d_act[:, k * 128 : k * 128 + 128].astype(BF)
    v.d_act_recv[t] = v.d_act_send[t]
    ex = Exchange(TENSOR, SPLITS, lambda o: v.d_act_send.at[o], lambda s: v.d_act_recv.at[s])
    ex.start()
    unite_grad(1)
    mix(s_u.starts(1))
    dm_near(1, t_x).wait_recv()

    def add_x(k):
        at = rows_at(k, 48)
        value = v.joined[t_x, at, :].astype(F32) + v.dm_near[1, at, :].astype(F32)
        v.joined[t_x, at, :] = value.astype(BF)

    loop(12, add_x)
    dm_far = remote(v.joined.at[t_x], v.dm_far, far_s, far_r, {TENSOR: t_x})
    dm_far.start()
    g_aux = aux_head.grad()
    v.d_f2[...] = dot_nt(g_aux, w_ac)
    sync_a = Sync(v.sync_b2)
    sync_a.start(through_silu(v.d_f2, v.pre_a, norm_a, 15))
    v.w_ac[...] = dot_tn(v.act_a[...], g_aux)[:64]
    mix(s_ac.starts())

    unite_grad(2)
    unite_grad(3)
    ex.wait()
    for k in range(OWNERS):
        at = slice(k * BINS, k * BINS + BINS)
        value = v.d_act_recv[0, at, :].astype(F32)
        for slot in range(1, SPLITS):
            value = value + v.d_act_recv[slot, at, :].astype(F32)
        v.d_img_send[k] = value.astype(BF)
    v.d_img_recv[me] = v.d_img_send[me]
    ex = Exchange(BATCH, OWNERS, lambda o: v.d_img_send.at[o], lambda s: v.d_img_recv.at[s])
    ex.start()
    mix(s_u.starts(2), s_u.middles(0))

    sums = sync_a.wait()
    gain_grads[15] = (sums[1:2], sums[0:1])
    spread_taps(v.d_f2, v.pre_a, norm_a, 15, sums[0:1], sums[1:2])
    for p in range(5):
        for at in range(0, CELLS, 96):
            value = back_tap(2 * p, 1, at)
            if p < 4:
                value = value + pltpu.roll(back_tap(2 * p + 1, 1, at), 64, 1)
            v.cat_a[at : at + 96, p * 128 : p * 128 + 128] = value.astype(BF)

    def aux_grad(c2):
        value2 = dot(v.whole_t[c2], v.cat_a[...])
        for half in range(2):
            value = value2[half * 128 : half * 128 + 128]
            c = 2 * c2 + half
            for p in range(5):
                v.pad[p, EDGE : EDGE + 128, :] = value[:, p * 128 : p * 128 + 128]
                low = v.pad[p, pl.ds(EDGE, 64, stride=2), :]
                top = v.pad[p, pl.ds(EDGE + 1, 64, stride=2), :]
                even = jnp.where(left_half, low, pltpu.roll(top, 64, 1))
                v.w_a[rows_at(2 * p * 8 + c, 64), :] = even.astype(BF)
                if p < 4:
                    odd = jnp.where(left_half, pltpu.roll(low, 64, 1), top)
                    v.w_a[rows_at((2 * p + 1) * 8 + c, 64), :] = odd.astype(BF)

    loop(SPLITS, aux_grad)
    ex.wait()
    d_b = v.d_img_recv[0].astype(F32)
    for k in range(1, OWNERS):
        d_b = d_b + v.d_img_recv[k].astype(F32)
    unit_b = (v.all_b[me].astype(F32) - mean_b) * scale_b
    d_b = d_b * slope(gamma_b * unit_b + beta_b)
    sync = Sync(v.sync_b3)
    sync.start(
        [total(d_b * group_mask(g)) for g in range(4)]
        + [total(d_b * unit_b * group_mask(g)) for g in range(4)]
    )
    mix(s_u.starts(3), s_u.middles(1))
    sums = sync.wait()
    first_b = jnp.zeros((BINS, 128), F32)
    second_b = jnp.zeros((BINS, 128), F32)
    for group in range(4):
        kept = group_mask(group)
        gain_grads[10 + group] = (sums[4 + group : 5 + group], sums[group : group + 1])
        first_b = first_b + kept * sums[group : group + 1]
        second_b = second_b + kept * sums[4 + group : 5 + group]
    inner = d_b - (first_b + unit_b * second_b) * count_b
    v.d_bp[t] = (gamma_b * scale_b * inner).astype(BF)
    spread_d = Spread(v.d_bp)
    spread_d.start()
    mix(s_u.starts(4), s_u.middles(2))
    spread_d.wait()
    d_bp_move = ToGroup(
        lambda owner, rows: v.d_bp.at[:, 0:rows, :],
        lambda slot, rows: v.d_bp_all.at[slot, :, 0:rows, :],
    )
    d_bp_move.start()
    v.d_bp_all[me] = v.d_bp[...]
    d_bp = jnp.concatenate([v.d_bp[k] for k in range(SPLITS)], axis=1)
    d_pooled = jnp.zeros((BINS, 512), F32)
    for group in range(4):
        rows = (d_bp.astype(F32) * group_mask(group)).astype(BF)
        d_pooled = d_pooled + dot_nt(rows, v.w_b[group * 512 : group * 512 + 512, :])
    d_pooled = (d_pooled / cells_in).astype(BF)
    v.d_sum[...] = dot_tn(v.pool[...], d_pooled)
    dm_near(0, t).wait_recv()
    dm_far.wait_recv()

    def through_sum(k, carry):
        at = rows_at(k, 48)
        value = v.d_sum[at, :] + v.joined[t, at, :].astype(F32) + v.dm_near[0, at, :].astype(F32)
        value = (value + v.dm_far[at, :].astype(F32)) * slope(summed(at))
        v.d_sum[at, :] = value
        return (
            carry[0] + fold(value),
            carry[1] + fold(value * normed(v.pre_e, at, norm_e)),
            carry[2] + fold(value * normed(v.pre_s, at, norm_s)),
        )

    zero = jnp.zeros((8, 512), F32)
    three = [total(item) for item in lax.fori_loop(0, 12, through_sum, (zero, zero, zero))]
    sync = Sync(v.sync_b4)
    sync.start(split_rows(three[0]) + split_rows(three[1]) + split_rows(three[2]))
    mix(s_a.starts(), s_u.middles(3))
    sums = sync.wait()
    first_s = join_rows(sums, 0, 4)
    second_e, second_s = join_rows(sums, 4, 4), join_rows(sums, 8, 4)
    for k in range(4):
        gain_grads[6 + k] = (sums[4 + k : 5 + k], sums[k : k + 1])
        gain_grads[1 + k] = (sums[8 + k : 9 + k], sums[k : k + 1])

    def back_both(k):
        at = rows_at(k, 48)
        value, mask = v.d_sum[at, :], wide(v.ins[at, :], 4)
        v.d_e[at, :] = back_norm(
            value, normed(v.pre_e, at, norm_e), mask, norm_e, gamma(6, 4), first_s, second_e, count4
        ).astype(BF)
        v.d_s[at, :] = back_norm(
            value, normed(v.pre_s, at, norm_s), mask, norm_s, gamma(1, 4), first_s, second_s, count4
        ).astype(BF)

    loop(12, back_both)

    def back_hidden(grad, weight, index):
        value = dot_nt(grad, weight)
        for k in range(SPLITS):
            v.dh_send[k] = value[:, k * 128 : k * 128 + 128].astype(BF)
        v.dh_recv[index, t] = v.dh_send[t]
        ex = Exchange(
            TENSOR, SPLITS, lambda o: v.dh_send.at[o], lambda s: v.dh_recv.at[index, s]
        )
        ex.start()
        return ex

    def hidden_sum(index):
        def step(k):
            at = rows_at(k, 96)
            value = v.dh_recv[index, 0, at, :].astype(F32)
            for slot in range(1, SPLITS):
                value = value + v.dh_recv[index, slot, at, :].astype(F32)
            v.d_f[at, :] = value

        loop(6, step)

    ex = back_hidden(v.d_e[...], v.w_e[...], 0)
    def short_grad(c):
        v.w_s[rows_at(c, 256), :] = dot(v.whole_t[c], v.d_s[...]).astype(BF)

    loop(SPLITS, short_grad)
    mix(s_s.starts(), s_u.middles(4))
    for k in range(SPLITS):
        v.w_e[k * 128 : k * 128 + 128, :] = dot_tn(v.h2[k], v.d_e[...]).astype(BF)
    ex.wait()
    hidden_sum(0)
    sync = Sync(v.sync_b5)
    sync.start(through_silu(v.d_f, v.pre_m, norm_m, 5))
    mix(s_e.starts())
    mix(s_c.middles())
    mix(s_ac.middles())
    mix(s_a.middles())
    sums = sync.wait()
    gain_grads[5] = (sums[1:2], sums[0:1])
    spread_taps(v.d_f, v.pre_m, norm_m, 5, sums[0:1], sums[1:2])
    fill(v.cat_u, 4)
    weight = jnp.concatenate([v.w_m[tap * 512 : tap * 512 + 512, :] for tap in range(9)], axis=1)
    ex = back_hidden(v.cat_u[...], weight, 1)

    def middle_grad(k):
        value = dot_tn(v.h1[k], v.cat_u[...])
        for tap in range(9):
            v.w_m[rows_at(tap * 4 + k, 128), :] = value[:, tap * 128 : tap * 128 + 128].astype(BF)

    loop(SPLITS, middle_grad)
    mix(s_m.starts())
    mix(s_s.middles())
    ex.wait()
    hidden_sum(1)
    sync = Sync(v.sync_b6)
    sync.start(through_silu(v.d_f, v.pre_r, norm_r, 0))

    mix(s_e.middles())
    squares = s_u.end()
    pool_move.wait()
    d_bp_move.wait()
    own_group = jnp.where(group_id == lax.div(me, 2), 1.0, 0.0)
    d_rows = jnp.concatenate(
        [v.d_bp_all[:, k].reshape(OWNERS * BINS, 128) for k in range(SPLITS)], axis=1
    )
    d_rows = (d_rows.astype(F32) * own_group).astype(BF)
    branch_grad = dot_tn(v.pool_all[...].reshape(OWNERS * BINS, 256), d_rows)
    for k in range(4):
        o_flat[pl.ds(1472 + k, 256, stride=4), :] = branch_grad[:, k * 128 : k * 128 + 128]
    squares = squares + sum(split_rows(total(branch_grad * branch_grad)))
    sums = sync.wait()
    mix(s_m.middles())
    gain_grads[0] = (sums[1:2], sums[0:1])

    def back_reduce(k):
        at = rows_at(k, 96)
        v.d_low[at, :] = back_norm(
            v.d_f[at, :], normed(v.pre_r, at, norm_r), v.ins[at, :], norm_r, gamma(0), sums[0:1], sums[1:2], count
        ).astype(BF)

    loop(6, back_reduce)

    def reduce_grad(c):
        v.w_r[rows_at(c, 256), :] = dot(v.whole_t[c], v.d_low[...]).astype(BF)

    loop(SPLITS, reduce_grad)
    mix(s_r.starts())
    for item in (s_c, s_ac, s_a, s_s, s_e):
        squares = squares + item.end()
    mix(s_r.middles())
    for item in (s_m, s_r):
        squares = squares + item.end()
    dm_near(1, t_diag).wait_send()
    dm_near(0, t_core).wait_send()
    dm_far.wait_send()

    v.gain_rows[...] = jnp.zeros((40, 128), F32)
    gammas = [gain_grads[row][0] for row in range(16)]
    betas = [pltpu.roll(gain_grads[row][1], 64, 1) for row in range(16)]
    o_shift[...] = gain_grads[14][1]
    for row in range(31):
        if row < 15:
            value = gammas[row]
        else:
            left = gammas[15] if row == 15 else betas[row - 16]
            value = jnp.where(lane < 64, left, betas[row - 15])
        v.gain_rows[row + 1 : row + 2, :] = value
    squares = squares + total(fold(v.gain_rows[...] * v.gain_rows[...])) / OWNERS

    sync = Sync(v.sync_end)
    sync.start([squares, o_misc[1:2, :]])

    tail = {}

    def put(where, value):
        tail[where] = value if where not in tail else tail[where] + value

    def class_tail(ref, count, base):
        for row in range(count):
            first, shift = divmod(base + NCLS * row, 128)
            for k in range(2):
                value = roll(ref[row : row + 1, k * 128 : k * 128 + 128], shift)
                put(first + k, jnp.where(lane >= shift, value, 0.0))
                if shift:
                    put(first + k + 1, jnp.where(lane < shift, value, 0.0))

    class_tail(v.out_c, 16, 0)
    class_tail(v.out_ac, 8, 76128)
    start = lax.rem(496 * me, 128)
    first = lax.div(496 * me, 128)
    own = [
        pltpu.roll(v.gain_rows[pl.ds(first + k, 1), :], lax.rem(16 - start + 128, 128), 1)
        for k in range(6)
    ]
    spot = lane - 16 + start
    for k in range(4):
        value = jnp.where(spot < 0, own[k], jnp.where(spot >= 128, own[k + 2], own[k + 1]))
        put(604 + k, jnp.where(lane >= 16, value, 0.0) if k == 0 else value)
    v.grad_pad[EDGE : EDGE + 576, :] = pltpu.roll(v.out_a[...], 96, 1)
    o_flat[7122:7706, :] = jnp.where(
        lane >= 96, v.grad_pad[EDGE : EDGE + 584, :], v.grad_pad[EDGE - 1 : EDGE + 583, :]
    )
    for row in range(608):
        if row in (18, 594):
            o_flat[7104 + row : 7105 + row, :] = o_flat[7104 + row : 7105 + row, :] + tail[row]
        elif row < 18 or row > 594:
            o_flat[7104 + row : 7105 + row, :] = tail[row]
    v.end_t[t] = sync.wait()
    spread_e = Spread(v.end_t)
    spread_e.start()
    spread_e.wait()
    ends = v.end_t[0]
    for k in range(1, SPLITS):
        ends = ends + v.end_t[k]
    o_misc[...] = ends
    o_misc[2:3, :] = jnp.broadcast_to(class_weights()[1], (1, 128))


def whole_step(sizes, labels, feat, flat):
    plan = scratch_plan()
    vmem = pl.BlockSpec(memory_space=pltpu.VMEM)
    anywhere = pl.BlockSpec(memory_space=pl.ANY)
    outs = [flat.shape, (1, 128), (8, 128)]
    return pl.pallas_call(
        functools.partial(step_kernel, tuple(plan)),
        out_shape=[jax.ShapeDtypeStruct(shape, F32) for shape in outs],
        in_specs=[pl.BlockSpec(memory_space=pltpu.SMEM), vmem, anywhere, anywhere],
        out_specs=[vmem] * len(outs),
        scratch_shapes=[pltpu.VMEM(shape, kind) for shape, kind in plan.values()]
        + [pltpu.SemaphoreType.DMA((SEMAPHORES,))],
        compiler_params=pltpu.CompilerParams(
            collective_id=0, has_side_effects=True, vmem_limit_bytes=63 * 1024 * 1024
        ),
        name="whole_step",
    )(sizes, labels, feat, flat)


def update_kernel(
    misc, grad, param, first, second, average,
    o_param, o_first, o_second, o_average, o_norm, o_loss, o_weight,
):
    norm = jnp.sqrt(jnp.sum(misc[0:1, :], axis=1, keepdims=True))
    o_norm[...] = norm
    o_loss[...] = jnp.sum(misc[1:2, :], axis=1, keepdims=True)
    o_weight[...] = misc[2:3, 0:1]
    clipped = grad[...] * jnp.minimum(1.0, 0.05 / (norm + 1e-06))
    new_first = 0.5 * first[...] + 0.5 * clipped
    new_second = 0.5 * second[...] + 0.5 * clipped * clipped
    lift = 1.0 / (1.0 - 0.5**STEP)
    old = param[...]
    ratio = (new_first * lift) / (jnp.sqrt(new_second * lift) + 1e-08)
    new = old - 0.01 * (ratio + 0.01 * old)
    o_param[...] = new
    o_first[...] = new_first
    o_second[...] = new_second
    o_average[...] = 0.999 * average[...] + 0.001 * new


def update(misc, grad, param, first, second, average):
    rows = grad.shape[0]
    block = pl.BlockSpec((1024, 128), lambda i: (i, 0))
    whole = pl.BlockSpec((8, 128), lambda i: (0, 0))
    one = pl.BlockSpec((1, 1), lambda i: (0, 0))
    big = jax.ShapeDtypeStruct((rows, 128), F32)
    return pl.pallas_call(
        update_kernel,
        grid=(pl.cdiv(rows, 1024),),
        out_shape=[big] * 4 + [jax.ShapeDtypeStruct((1, 1), F32)] * 3,
        in_specs=[whole] + [block] * 5,
        out_specs=[block] * 4 + [one] * 3,
        compiler_params=pltpu.CompilerParams(vmem_limit_bytes=60 * 1024 * 1024),
        name="update",
    )(misc, grad, param, first, second, average)


def fits(splits, owners):
    return splits == SPLITS and owners == OWNERS


def local_fast(features, labels, valid, sizes, params, first_moment, squared_mean, average):
    flat = params.reshape(-1, 128)
    marked = jnp.where(valid > 0, labels, -1).astype(F32).reshape(CELLS, 1)
    grad, shift_grad, misc = whole_step(
        sizes, jnp.broadcast_to(marked, (CELLS, 128)), features.reshape(CELLS, -1), flat
    )
    news = update(
        misc,
        grad,
        flat,
        first_moment.reshape(-1, 128),
        squared_mean.reshape(-1, 128),
        average.reshape(-1, 128),
    )
    new_params, new_first, new_second, new_average = [
        item.reshape(params.shape) for item in news[:4]
    ]
    return (
        new_params,
        new_first,
        new_second,
        new_average,
        new_params.astype(BF),
        news[4].reshape(()),
        news[5].reshape(()),
        news[6].reshape(()),
        shift_grad.reshape(128),
    )


def solution(mesh):
    chosen = local_fast if fits(mesh.shape["tensor"], mesh.shape["batch"]) else local
    return jax.shard_map(
        chosen,
        mesh=mesh,
        in_specs=(
            P("batch", None, None, "tensor"),
            P("batch", None, None),
            P("batch", None, None),
            P("batch", None),
            P("tensor", "batch"),
            P("tensor", "batch"),
            P("tensor", "batch"),
            P("tensor", "batch"),
        ),
        out_specs=(
            P("tensor", "batch"),
            P("tensor", "batch"),
            P("tensor", "batch"),
            P("tensor", "batch"),
            P("tensor", "batch"),
            P(),
            P(),
            P(),
            P("tensor"),
        ),
        check_vma=False,
    )
```
